32 devices in a mesh: dp: 8 (over z, y), rep: 4 (over x, core).
Axes of the slice: x: 2, y: 2, z: 4, core: 2. Of those that a mesh axis runs over, the one named last changes fastest.
Arguments:
- incoming_activations: bfloat16 [16384, 768], P(('dp', 'rep')), may hold values from -6 to 6
- caption_final_place: int32 [1024], P(('dp', 'rep')), may hold values from 2 to 15
- paired_picture: int32 [1024], P(('dp', 'rep')), may hold values from 0 to 383, as said below
- caption_weight: float32 [1024], P(('dp', 'rep')), may hold values from 0.5 to 12, as said below
- locked_picture_features: bfloat16 [384, 768], P(('dp', 'rep')), may hold values from -6 to 6
- softmax_heat: float32 [1], replicated, may hold values from 0.012 to 0.025
- premix_scaling_factor: float32 [768], replicated, may hold values from 0.5 to 1.5
- premix_shift_term: float32 [768], replicated, may hold values from -1.75 to 1.75
- stacked_mixing_matrix: bfloat16 [768, 2304], replicated, may hold values from -0.21875 to 0.21875
- asking_reading_offsets: float32 [1536], replicated, may hold values from -1.75 to 1.75
- mixing_result_matrix: bfloat16 [768, 768], replicated, may hold values from -0.625 to 0.625
- mixing_result_offset: float32 [768], replicated, may hold values from -1.75 to 1.75
- premlp_scaling_factor: float32 [768], replicated, may hold values from 0.5 to 1.5
- premlp_shift_term: float32 [768], replicated, may hold values from -1.75 to 1.75
- widening_matrix: bfloat16 [768, 3072], replicated, may hold values from -0.21875 to 0.21875
- widening_offset: float32 [3072], replicated, may hold values from -1.75 to 1.75
- narrowing_matrix: bfloat16 [3072, 768], replicated, may hold values from -0.15625 to 0.15625
- narrowing_offset: float32 [768], replicated, may hold values from -1.75 to 1.75
- caption_mapping_matrix: bfloat16 [768, 768], replicated, may hold values from -0.21875 to 0.21875
- picture_mapping_matrix: bfloat16 [768, 768], replicated, may hold values from -0.21875 to 0.21875
Outputs:
- loss: float32 [1], replicated
- token_gradient: float32 [16384, 768], P(('dp', 'rep'))
- first_gain_gradient: float32 [768], replicated
- first_bias_gradient: float32 [768], replicated
- joint_weight_gradient: float32 [768, 2304], P('dp', 'rep')
- joint_bias_gradient: float32 [1536], replicated
- output_weight_gradient: float32 [768, 768], P('dp', 'rep')
- output_bias_gradient: float32 [768], replicated
- second_gain_gradient: float32 [768], replicated
- second_bias_gradient: float32 [768], replicated
- up_weight_gradient: float32 [768, 3072], P('dp', 'rep')
- up_bias_gradient: float32 [3072], replicated
- down_weight_gradient: float32 [3072, 768], P('dp', 'rep')
- down_bias_gradient: float32 [768], replicated
- text_head_gradient: float32 [768, 768], P('dp', 'rep')
The draws below stay inside these ranges and needn't reach their ends.
Inputs may be any that keep to these rules, and one draw needn't show every extreme that they name: `paired_picture`: the 32 captions of one device name only the 12 images of the same device; every image is named by 1 to 5 captions, and on every device some image by exactly 5. `caption_weight`: positive weights.
All inputs are finite; a program needn't handle non-finite values.
Results may differ from the reference program's by a relative error of at most 0.0109.
Values may be sent and summed in bfloat16 or wider, within the bound.
No kernel may reach another device: no remote copies, remote signals or barrier semaphores. Data moves between devices by JAX's collectives and lax.ppermute only.
A program may use at most 128 MiB of HBM per device.

```python
import math
import jax
import jax.numpy as jnp
from jax import lax

D = 768
HEADS = 12
HEAD = 64
FF = 3072
E = 768
EV = 768
SEQ = 16
CAP_DEV = 32
IMG_DEV = 12
CAPTIONS = 1024
IMAGES = 384
TOKENS = 16384


def one_block(key):
    first, second, third = jax.random.split(key, 3)
    chosen_full = jax.random.randint(first, (), 0, IMG_DEV)
    slot_image = jnp.arange(4 * IMG_DEV, dtype=jnp.int32) // 4
    ranks = jax.random.permutation(second, 4 * IMG_DEV).astype(jnp.int32)
    forced = -1 - jnp.arange(4 * IMG_DEV, dtype=jnp.int32) % 4
    ranks = jnp.where(slot_image == chosen_full, forced, ranks)
    order = jnp.argsort(ranks, stable=True)
    extra = slot_image[order[:CAP_DEV - IMG_DEV]]
    images = jnp.concatenate([jnp.arange(IMG_DEV, dtype=jnp.int32), extra])
    shuffle = jax.random.permutation(third, CAP_DEV)
    return images[shuffle]


def draw_paired_picture(key, part):
    key = jax.random.fold_in(key, 7)
    blocks = IMAGES // IMG_DEV
    keys = jax.random.split(key, blocks)
    local = jax.vmap(one_block)(keys)
    offsets = (jnp.arange(blocks, dtype=jnp.int32) * IMG_DEV)[:, None]
    return (local + offsets).reshape(-1).astype(jnp.int32)


def rising_weights(key, top, low_end, high_end):
    place = jnp.arange(CAPTIONS, dtype=jnp.float32) / jnp.float32(CAPTIONS - 1)
    base = jnp.exp(place * jnp.log(jnp.float32(top)))
    rough = jax.random.uniform(key, (CAPTIONS,), jnp.float32, low_end, high_end)
    return base * rough


def draw_caption_weight(key, part):
    key = jax.random.fold_in(key, 11)
    return rising_weights(key, 5.0, 0.7, 1.3).astype(jnp.float32)


def set_ends(result, key, low, top_value):
    index_at = [jax.random.randint(jax.random.fold_in(key, axis), (), 0, length) for axis, length in enumerate(result.shape)]
    longest = result.shape.index(max(result.shape))
    beside = index_at[:longest] + [(index_at[longest] + 1) % result.shape[longest]] + index_at[longest + 1:]
    return result.at[tuple(index_at)].set(low).at[tuple(beside)].set(top_value)


def block_scale(stream_key, shape, shards, low, top_value):
    def one(position, parts):
        heights = jax.random.uniform(jax.random.fold_in(jax.random.fold_in(stream_key, 6), position), (parts,), jnp.float32, low / len(shards), top_value / len(shards))
        return jnp.repeat(jnp.exp(heights), shape[position] // parts).reshape((-1,) + (1,) * (len(shape) - position - 1))

    level = one(*shards[0])
    for cut in shards[1:]:
        level = level * one(*cut)
    return level


def bell_draw(rng, extent, deviation, most, cuts=(), held_as=jnp.bfloat16):
    level = block_scale(rng, extent, cuts, -0.22, 0.18) if cuts else 1.0
    result = jax.random.normal(rng, extent, jnp.float32) * deviation * level
    return jnp.minimum(jnp.maximum(result, -most), most).astype(held_as)


def setup_inputs(seed: int = 0) -> dict:
    arg_keys = jax.random.split(jax.random.key(seed), 21)
    return {
        "incoming_activations": bell_draw(arg_keys[0], (TOKENS, D), 1.0, 6.0, ((0, 32),)),
        "caption_final_place": set_ends(jax.random.randint(arg_keys[1], (CAPTIONS,), 2, SEQ), jax.random.fold_in(arg_keys[1], 1), 2, SEQ - 1).astype(jnp.int32),
        "paired_picture": draw_paired_picture(jax.random.fold_in(arg_keys[20], 71), 0),
        "caption_weight": draw_caption_weight(jax.random.fold_in(arg_keys[20], 71), 0),
        "locked_picture_features": bell_draw(arg_keys[4], (IMAGES, EV), 1.0, 6.0, ((0, 32),)),
        "softmax_heat": jnp.clip(jnp.exp(jax.random.uniform(arg_keys[5], (1,), jnp.float32, math.log(0.012), math.log(0.025))), 0.012, 0.025),
        "premix_scaling_factor": jnp.clip(1.0 + 0.1 * jax.random.normal(arg_keys[6], (D,), jnp.float32), 0.5, 1.5),
        "premix_shift_term": bell_draw(arg_keys[7], (D,), 0.3, 1.75, (), jnp.float32),
        "stacked_mixing_matrix": bell_draw(arg_keys[8], (D, 3 * D), D ** -0.5, 0.21875),
        "asking_reading_offsets": bell_draw(arg_keys[9], (2 * D,), 0.3, 1.75, (), jnp.float32),
        "mixing_result_matrix": bell_draw(arg_keys[10], (D, D), (D // 8) ** -0.5, 0.625),
        "mixing_result_offset": bell_draw(arg_keys[11], (D,), 0.3, 1.75, (), jnp.float32),
        "premlp_scaling_factor": jnp.clip(1.0 + 0.1 * jax.random.normal(arg_keys[12], (D,), jnp.float32), 0.5, 1.5),
        "premlp_shift_term": bell_draw(arg_keys[13], (D,), 0.3, 1.75, (), jnp.float32),
        "widening_matrix": bell_draw(arg_keys[14], (D, FF), D ** -0.5, 0.21875),
        "widening_offset": bell_draw(arg_keys[15], (FF,), 0.3, 1.75, (), jnp.float32),
        "narrowing_matrix": bell_draw(arg_keys[16], (FF, D), (FF // 2) ** -0.5, 0.15625),
        "narrowing_offset": bell_draw(arg_keys[17], (D,), 0.3, 1.75, (), jnp.float32),
        "caption_mapping_matrix": bell_draw(arg_keys[18], (D, E), D ** -0.5, 0.21875),
        "picture_mapping_matrix": bell_draw(arg_keys[19], (EV, E), EV ** -0.5, 0.21875),
    }


epsilon = 1e-06
highest = lax.Precision.HIGHEST

@jax.custom_vjp
def low(v):
    return lax.optimization_barrier(v.astype(jnp.bfloat16)).astype(jnp.float32)

@jax.custom_vjp
def low_back(v):
    return v

def low_keep(v):
    return (low(v), None)

def low_pass(kept, grad):
    return (grad,)

def back_keep(v):
    return (v, None)

def back_low(kept, grad):
    return (low(grad),)
low.defvjp(low_keep, low_pass)
low_back.defvjp(back_keep, back_low)

def layer_norm(values, gain, bias):
    average = lax.optimization_barrier(jnp.mean(values, axis=-1, keepdims=True))
    centred = values - average
    spread = lax.optimization_barrier(jnp.mean(centred * centred, axis=-1, keepdims=True))
    return centred * lax.rsqrt(spread + epsilon) * gain + bias

def log_total(values, axis):
    top = lax.optimization_barrier(jnp.max(values, axis=axis, keepdims=True))
    return jnp.log(lax.optimization_barrier(jnp.sum(jnp.exp(values - top), axis=axis))) + jnp.squeeze(top, axis=axis)

def block(rows, positions, params):
    premix_scaling_factor, premix_shift_term, stacked_mixing_matrix, asking_reading_offsets, mixing_result_matrix, mixing_result_offset, premlp_scaling_factor, premlp_shift_term, widening_matrix, widening_offset, narrowing_matrix, narrowing_offset, caption_mapping_matrix = params
    count = positions.shape[0]
    normed = low(layer_norm(rows, premix_scaling_factor, premix_shift_term))
    bias_full = jnp.concatenate([asking_reading_offsets[:D], jnp.zeros((D,), jnp.float32), asking_reading_offsets[D:]])
    project = low_back(low(jnp.dot(normed, stacked_mixing_matrix, precision=highest) + bias_full))
    query = project[:, :D].reshape(count, SEQ, HEADS, HEAD)
    keys = project[:, D:2 * D].reshape(count, SEQ, HEADS, HEAD)
    values = project[:, 2 * D:].reshape(count, SEQ, HEADS, HEAD)
    scores = low_back(jnp.einsum('cqhe,ckhe->chqk', query, keys, precision=highest) * HEAD ** (-0.5))
    valid = jnp.arange(SEQ, dtype=jnp.int32)[None, :] <= positions[:, None]
    masked = jnp.where(valid[:, None, None, :], scores, -1e+30)
    attention = low(jax.nn.softmax(masked, axis=-1))
    context = jnp.einsum('chqk,ckhe->cqhe', attention, values, precision=highest).reshape(count * SEQ, D)
    context = low_back(low(context))
    attended = low_back(jnp.dot(context, mixing_result_matrix, precision=highest) + mixing_result_offset)
    middle = rows + attended
    second = low(layer_norm(middle, premlp_scaling_factor, premlp_shift_term))
    upper = low_back(jnp.dot(second, widening_matrix, precision=highest) + widening_offset)
    active = low(jax.nn.gelu(upper, approximate=True))
    branch = low_back(jnp.dot(active, narrowing_matrix, precision=highest) + narrowing_offset)
    final = middle + branch
    pool_weight = valid.astype(jnp.float32) / (positions[:, None] + 1).astype(jnp.float32)
    pooled = low(lax.optimization_barrier(jnp.sum(final.reshape(count, SEQ, D) * pool_weight[:, :, None], axis=1)))
    text = low_back(jnp.dot(pooled, caption_mapping_matrix, precision=highest))
    return low(text * lax.rsqrt(lax.optimization_barrier(jnp.sum(text * text, axis=1, keepdims=True)) + epsilon))

def reference(incoming_activations, caption_final_place, paired_picture, caption_weight, locked_picture_features, softmax_heat, premix_scaling_factor, premix_shift_term, stacked_mixing_matrix, asking_reading_offsets, mixing_result_matrix, mixing_result_offset, premlp_scaling_factor, premlp_shift_term, widening_matrix, widening_offset, narrowing_matrix, narrowing_offset, caption_mapping_matrix, picture_mapping_matrix):
    params = tuple((item.astype(jnp.float32) for item in (premix_scaling_factor, premix_shift_term, stacked_mixing_matrix, asking_reading_offsets, mixing_result_matrix, mixing_result_offset, premlp_scaling_factor, premlp_shift_term, widening_matrix, widening_offset, narrowing_matrix, narrowing_offset, caption_mapping_matrix)))
    rows = incoming_activations.astype(jnp.float32)
    feats_full = locked_picture_features.astype(jnp.float32)
    image_map = picture_mapping_matrix.astype(jnp.float32)
    weights_row = caption_weight.astype(jnp.float32)
    onehot = (paired_picture[:, None] == jnp.arange(IMAGES, dtype=jnp.int32)[None, :]).astype(jnp.float32)
    counts = lax.optimization_barrier(jnp.sum(onehot, axis=0))
    inverse = lax.optimization_barrier(jnp.sum(onehot / counts[None, :], axis=1))
    group = math.gcd(CAPTIONS, 256)
    batches = CAPTIONS // group
    partition_sum = softmax_heat[0]

    def objective(inputs, weights):
        picture = jnp.dot(feats_full, image_map, precision=highest)
        picture = low(picture * lax.rsqrt(lax.optimization_barrier(jnp.sum(picture * picture, axis=1, keepdims=True)) + epsilon))

        def one_group(pair):
            return block(pair[0], pair[1], weights)
        embed = lax.map(jax.checkpoint(one_group), (inputs.reshape(batches, group * SEQ, D), caption_final_place.reshape(batches, group)))
        embed = embed.reshape(CAPTIONS, E)
        raw = low_back(jnp.dot(embed, picture.T, precision=highest))
        scores = raw / partition_sum
        positive = lax.optimization_barrier(jnp.sum(scores * onehot, axis=1))
        return jnp.sum(weights_row * (log_total(scores, 1) - positive)) + jnp.sum(log_total(scores, 0)) - jnp.sum(weights_row * positive * inverse)
    total, pullback = jax.vjp(objective, rows, params)
    token_gradient, gradients = pullback(jnp.ones_like(total))
    loss = (total / CAPTIONS).reshape(1)
    return (loss, token_gradient, gradients[0], gradients[1], gradients[2], gradients[3], gradients[4], gradients[5], gradients[6], gradients[7], gradients[8], gradients[9], gradients[10], gradients[11], gradients[12])
```

```python
import jax
import jax.numpy as jnp
from jax import lax
from jax.sharding import PartitionSpec as P

D = 768
HEADS = 12
HEAD = 64
SEQ = 16
BF = jnp.bfloat16
F32 = jnp.float32

epsilon = 1e-06
negative = -1e30


def dot(a, b, dims):
    return lax.dot_general(a, b, (dims, ((), ())), preferred_element_type=F32)


def nn(a, b):
    return dot(a, b, ((1,), (0,)))


def nt(a, b):
    return dot(a, b, ((1,), (1,)))


def tn(a, b):
    return dot(a, b, ((0,), (0,)))


def swap(value, axis, bit):
    size = lax.axis_size(axis)
    return lax.ppermute(value, axis, [(i, i ^ (1 << bit)) for i in range(size)])


def my_bit(axis, bit):
    return (lax.axis_index(axis) >> bit) & 1


def bit_count(axis):
    return lax.axis_size(axis).bit_length() - 1


def pick(value, axis, index):
    return lax.dynamic_index_in_dim(value, index, axis, keepdims=False)


def column_step(total, bit):
    rows, blocks, wide = total.shape
    view = total.reshape(rows, blocks // 2, 2, wide)
    mine = my_bit("rep", bit)
    got = swap(pick(view, 2, 1 - mine), "rep", bit)
    return (pick(view, 2, mine).astype(F32) + got.astype(F32)).astype(BF)


def row_step(total, bit):
    view = total.reshape((total.shape[0] // 2, 2) + total.shape[1:])
    mine = my_bit("dp", bit)
    got = swap(pick(view, 1, 1 - mine), "dp", bit)
    return (pick(view, 1, mine).astype(F32) + got.astype(F32)).astype(BF)


def weight_sum(left, right, columns_first):
    rep, dp = lax.axis_size("rep"), lax.axis_size("dp")
    tokens, rows = left.shape
    wide = right.shape[1] // rep
    view = right.reshape(tokens, rep // 2, 2, wide)
    core = my_bit("rep", 0)
    away = pick(view, 2, 1 - core).reshape(tokens, -1)
    here = pick(view, 2, core).reshape(tokens, -1)
    got = swap(tn(left, away).astype(BF), "rep", 0)
    total = (tn(left, here) + got.astype(F32)).astype(BF)

    def columns(total):
        for bit in range(1, bit_count("rep")):
            total = column_step(total.reshape(total.shape[0], -1, wide), bit)
        return total.reshape(total.shape[0], -1)

    def rows_(total):
        total = total.reshape(dp, -1, total.shape[1])
        for bit in range(bit_count("dp")):
            total = row_step(total, bit)
        return total.reshape(-1, total.shape[-1])

    total = rows_(columns(total)) if columns_first else columns(rows_(total))
    return total.astype(F32)


def spread_rows(value):
    for axis in ("dp", "rep"):
        for bit in range(bit_count(axis)):
            value = jnp.concatenate([value, swap(value, axis, bit)], axis=0)
    return value


def spread_blocks(value):
    for bit in range(bit_count("dp")):
        view = value.reshape(value.shape[0], -1, 2, value.shape[-1])
        mine = my_bit("dp", bit)
        got = swap(pick(view, 2, 1 - mine), "dp", bit)
        value = jnp.concatenate([pick(view, 2, mine), got], axis=0)
    value = value.reshape(value.shape[0], -1)
    for bit in range(bit_count("rep")):
        value = jnp.concatenate([value, swap(value, "rep", bit)], axis=0)
    return value


def norm_parts(values):
    average = jnp.mean(values, axis=-1, keepdims=True)
    centred = values - average
    inverse = lax.rsqrt(jnp.mean(centred * centred, axis=-1, keepdims=True) + epsilon)
    return centred * inverse, inverse


def norm_back(unit, inverse, gain, back):
    inner = back * gain
    part = inverse * (
        inner
        - jnp.mean(inner, axis=-1, keepdims=True)
        - unit * jnp.mean(inner * unit, axis=-1, keepdims=True)
    )
    return part, jnp.sum(back * unit, axis=0), jnp.sum(back, axis=0)


def local(
    incoming_activations,
    caption_final_place,
    paired_picture,
    caption_weight,
    locked_picture_features,
    softmax_heat,
    premix_scaling_factor,
    premix_shift_term,
    stacked_mixing_matrix,
    asking_reading_offsets,
    mixing_result_matrix,
    mixing_result_offset,
    premlp_scaling_factor,
    premlp_shift_term,
    widening_matrix,
    widening_offset,
    narrowing_matrix,
    narrowing_offset,
    caption_mapping_matrix,
    picture_mapping_matrix,
):
    both = ("dp", "rep")
    devices = lax.axis_size(both)
    dp = lax.axis_size("dp")
    rep = lax.axis_size("rep")
    captions = caption_final_place.shape[0]
    grouped = 8
    blocks = captions // grouped
    span = grouped * SEQ
    scale = HEAD ** (-0.5)
    heat = softmax_heat[0]
    features = lax.all_gather(locked_picture_features, both, axis=0, tiled=True)

    rows = incoming_activations.astype(F32)
    unit1, inverse1 = norm_parts(rows)
    normed = (unit1 * premix_scaling_factor + premix_shift_term).astype(BF)
    bias_full = jnp.concatenate(
        [asking_reading_offsets[:D], jnp.zeros((D,), F32), asking_reading_offsets[D:]]
    )
    project = (nn(normed, stacked_mixing_matrix) + bias_full).astype(BF)
    shaped = project.reshape(blocks, span, 3, HEADS, HEAD)
    query = shaped[:, :, 0]
    keys = shaped[:, :, 1]
    values = shaped[:, :, 2]
    token_caption = jnp.arange(span, dtype=jnp.int32) // SEQ
    token_place = jnp.arange(span, dtype=jnp.int32) % SEQ
    limits = jnp.repeat(caption_final_place.reshape(blocks, grouped), SEQ, axis=1)
    allowed = (token_caption[:, None] == token_caption[None, :])[None, :, :] & (
        token_place[None, None, :] <= limits[:, None, :]
    )
    scores = jnp.einsum("nqhe,nkhe->nhqk", query, keys, preferred_element_type=F32) * scale
    attention = jax.nn.softmax(jnp.where(allowed[:, None, :, :], scores, negative), axis=-1)
    attention_low = attention.astype(BF)
    context = jnp.einsum("nhqk,nkhe->nqhe", attention_low, values, preferred_element_type=F32)
    context_low = context.reshape(captions * SEQ, D).astype(BF)
    middle = rows + (nn(context_low, mixing_result_matrix) + mixing_result_offset)
    unit2, inverse2 = norm_parts(middle)
    second = (unit2 * premlp_scaling_factor + premlp_shift_term).astype(BF)
    upper = nn(second, widening_matrix) + widening_offset
    active, gelu_back = jax.vjp(lambda v: jax.nn.gelu(v, approximate=True), upper)
    place = jnp.arange(SEQ, dtype=jnp.int32)
    inside = (place[None, :] <= caption_final_place[:, None]).astype(F32)
    share = 1.0 / (caption_final_place + 1).astype(F32)
    pool_weight = inside * share[:, None]
    active_mean = (
        jnp.sum(active.astype(BF).astype(F32).reshape(captions, SEQ, -1) * inside[:, :, None], axis=1)
        * share[:, None]
    )
    active_high = active_mean.astype(BF)
    active_rest = (active_mean - active_high.astype(F32)).astype(BF)
    branch = nn(active_high, narrowing_matrix) + nn(active_rest, narrowing_matrix) + narrowing_offset
    pooled = (
        jnp.sum(middle.reshape(captions, SEQ, D) * pool_weight[:, :, None], axis=1) + branch
    ).astype(BF)
    left_low = spread_blocks(
        jnp.concatenate([active_high.reshape(captions, dp, -1), pooled.reshape(captions, dp, -1)], axis=2)
    )
    text = nn(pooled, caption_mapping_matrix)
    text_scale = lax.rsqrt(jnp.sum(text * text, axis=1, keepdims=True) + epsilon)
    embed = (text * text_scale).astype(BF)

    picture = nn(features, picture_mapping_matrix)
    picture = (
        picture * lax.rsqrt(jnp.sum(picture * picture, axis=1, keepdims=True) + epsilon)
    ).astype(BF)
    image_total = picture.shape[0]
    score = nt(embed, picture) / heat
    top = jnp.max(score, axis=1, keepdims=True)
    row_logsum = jnp.log(jnp.sum(jnp.exp(score - top), axis=1, keepdims=True)) + top
    match = paired_picture[:, None] == jnp.arange(image_total, dtype=jnp.int32)[None, :]
    positive = jnp.sum(jnp.where(match, score, 0.0), axis=1)
    counts = jnp.sum(match.astype(F32), axis=0)
    inverse_count = 1.0 / jnp.sum(jnp.where(match, counts[None, :], 0.0), axis=1)
    local_total = jnp.sum(caption_weight * (row_logsum[:, 0] - positive - positive * inverse_count))
    column_top = jnp.max(score, axis=0)
    column_sum = jnp.sum(jnp.exp(score - column_top[None, :]), axis=0)
    stats = jnp.concatenate(
        [column_top, column_sum, jnp.full((128,), local_total)]
    )[None]
    stats = lax.all_gather(stats, both, axis=0, tiled=True)
    tops = stats[:, :image_total]
    column_top = jnp.max(tops, axis=0)
    column_logsum = (
        jnp.log(
            jnp.sum(jnp.exp(tops - column_top[None, :]) * stats[:, image_total : 2 * image_total], axis=0)
        )
        + column_top
    )
    total = jnp.sum(stats[:, 2 * image_total]) + jnp.sum(column_logsum)
    loss = (total / (captions * devices)).reshape(1)

    weight = caption_weight[:, None]
    slope = (
        weight * jnp.exp(score - row_logsum)
        + jnp.exp(score - column_logsum[None, :])
        - jnp.where(match, weight * (1.0 + inverse_count[:, None]), 0.0)
    )
    slope_low = (slope / heat).astype(BF)
    embed_back = nn(slope_low, picture)
    text_dot = jnp.sum(text * embed_back, axis=1, keepdims=True)
    text_back = (
        text_scale * embed_back - text * (text_scale * text_scale * text_scale) * text_dot
    ).astype(BF)
    all_back = spread_rows(text_back)

    pooled_back = nt(text_back, caption_mapping_matrix)
    final_back = (pooled_back[:, None, :] * pool_weight[:, :, None]).reshape(captions * SEQ, D)
    branch_row = (pooled_back * share[:, None]).astype(BF)
    down_bias_back = jnp.sum(branch_row.astype(F32) * (caption_final_place + 1).astype(F32)[:, None], axis=0)
    active_back = nt(branch_row, narrowing_matrix)
    active_back = (active_back[:, None, :] * inside[:, :, None]).reshape(captions * SEQ, -1)
    upper_back = gelu_back(active_back)[0].astype(BF)
    up_bias_back = jnp.sum(upper_back, axis=0, dtype=F32)
    up_block = weight_sum(second, upper_back, True)
    second_back = nt(upper_back, widening_matrix)
    middle_part, second_gain_back, second_bias_back = norm_back(
        unit2, inverse2, premlp_scaling_factor, second_back
    )
    middle_back = final_back + middle_part
    attended_back = middle_back.astype(BF)
    output_bias_back = jnp.sum(attended_back, axis=0, dtype=F32)
    context_back = nt(attended_back, mixing_result_matrix).astype(BF)
    context_back = context_back.reshape(blocks, span, HEADS, HEAD)
    attention_back = jnp.einsum("nqhe,nkhe->nhqk", context_back, values, preferred_element_type=F32)
    values_back = jnp.einsum("nhqk,nqhe->nkhe", attention_low, context_back, preferred_element_type=F32)
    score_back = attention * (
        attention_back - jnp.sum(attention * attention_back, axis=-1, keepdims=True)
    )
    score_low = score_back.astype(BF) * jnp.asarray(scale, BF)
    query_back = jnp.einsum("nhqk,nkhe->nqhe", score_low, keys, preferred_element_type=F32)
    keys_back = jnp.einsum("nhqk,nqhe->nkhe", score_low, query, preferred_element_type=F32)
    project_back = (
        jnp.stack([query_back, keys_back, values_back], axis=2)
        .reshape(captions * SEQ, 3 * D)
        .astype(BF)
    )
    output_block = weight_sum(context_low, attended_back, False)
    joint_block = weight_sum(normed, project_back, False)
    column_total = jnp.sum(project_back, axis=0, dtype=F32)
    joint_bias_back = jnp.concatenate([column_total[:D], column_total[2 * D :]])
    normed_back = nt(project_back, stacked_mixing_matrix)
    rows_part, first_gain_back, first_bias_back = norm_back(
        unit1, inverse1, premix_scaling_factor, normed_back
    )
    token_back = middle_back + rows_part

    place_rep = lax.axis_index("rep")
    wide = D // rep
    back_here = lax.dynamic_slice_in_dim(all_back, place_rep * wide, wide, 1)
    map_here = lax.dynamic_slice_in_dim(caption_mapping_matrix, place_rep * wide, wide, 0)
    pooled_all = nt(all_back, map_here).astype(BF)
    hidden = active_high.shape[1] // dp
    down_block = tn(left_low[:, :hidden], pooled_all)
    head_block = tn(left_low[:, hidden:], back_here)

    vectors = lax.psum(
        (
            first_gain_back,
            first_bias_back,
            joint_bias_back,
            output_bias_back,
            second_gain_back,
            second_bias_back,
            up_bias_back,
            down_bias_back,
        ),
        both,
    )
    return (
        loss,
        token_back,
        vectors[0],
        vectors[1],
        joint_block,
        vectors[2],
        output_block,
        vectors[3],
        vectors[4],
        vectors[5],
        up_block,
        vectors[6],
        down_block,
        vectors[7],
        head_block,
    )


def solution(mesh):
    spread = P(("dp", "rep"), None)
    line = P(("dp", "rep"))
    block = P("dp", "rep")
    in_specs = (spread, line, line, line, spread) + (P(),) * 15
    out_specs = (
        P(),
        spread,
        P(),
        P(),
        block,
        P(),
        block,
        P(),
        P(),
        P(),
        block,
        P(),
        block,
        P(),
        block,
    )
    return jax.shard_map(local, mesh=mesh, in_specs=in_specs, out_specs=out_specs, check_vma=False)
```

```python
import functools

import jax
import jax.numpy as jnp
from jax import lax
from jax.experimental import pallas as pl
from jax.experimental.pallas import tpu as pltpu
from jax.sharding import PartitionSpec as P

D = 768
HEADS = 12
HEAD = 64
SEQ = 16
FF = 3072
GROUP = 128
PAIRS = HEADS // 2
SLOT = 16
BF = jnp.bfloat16
F32 = jnp.float32

epsilon = 1e-06
negative = -1e30
scale = HEAD ** (-0.5)
LIMIT = 58 * 1024 * 1024

GAIN1, SHIFT1, JOINT, OUT, GAIN2, SHIFT2, WIDE, NARROW = 0, 768, 1536, 3840, 4608, 5376, 6144, 9216
VECTORS = 9984

any_space = pl.BlockSpec(memory_space=pl.ANY)
vmem = pl.BlockSpec(memory_space=pltpu.VMEM)
smem = pl.BlockSpec(memory_space=pltpu.SMEM)


def dot(a, b, dims):
    return lax.dot_general(a, b, (dims, ((), ())), preferred_element_type=F32)


def nn(a, b):
    return dot(a, b, ((1,), (0,)))


def nt(a, b):
    return dot(a, b, ((1,), (1,)))


def tn(a, b):
    return dot(a, b, ((0,), (0,)))


def cost(flops, steps, moved):
    return pl.CostEstimate(flops=flops, transcendentals=steps, bytes_accessed=moved)


def shape(*dims, dtype=F32):
    return jax.ShapeDtypeStruct(dims, dtype)


def iota(dims, axis):
    return lax.broadcasted_iota(jnp.int32, dims, axis)


def norm_parts(values):
    average = jnp.mean(values, axis=-1, keepdims=True)
    centred = values - average
    inverse = lax.rsqrt(jnp.mean(centred * centred, axis=-1, keepdims=True) + epsilon)
    return centred * inverse, inverse


def norm_back(unit, inverse, gain, back):
    inner = back * gain
    part = inverse * (
        inner
        - jnp.mean(inner, axis=-1, keepdims=True)
        - unit * jnp.mean(inner * unit, axis=-1, keepdims=True)
    )
    return part, jnp.sum(back * unit, axis=0, keepdims=True), jnp.sum(back, axis=0, keepdims=True)


def split(value):
    high = value.astype(BF)
    return high, (value - high.astype(F32)).astype(BF)


def two(value):
    return jnp.concatenate(split(value), axis=0)


class Copies:
    def __init__(self, sems):
        self.sems = sems
        self.used = 0

    def start(self, source, target):
        copy = pltpu.make_async_copy(source, target, self.sems.at[self.used])
        self.used += 1
        copy.start()
        return copy


def token_limits(place):
    captions = place.shape[1]
    tokens = captions * SEQ
    owner = (iota((tokens, captions), 0) // SEQ == iota((tokens, captions), 1)).astype(F32)
    column = jnp.sum(owner * place, axis=1, keepdims=True)
    line = nt(place.astype(BF), owner.astype(BF))
    return line, column


def pool_mask(line, captions):
    dims = (captions, captions * SEQ)
    token = iota(dims, 1)
    inside = (token % SEQ).astype(F32) <= line
    return jnp.where((token // SEQ == iota(dims, 0)) & inside, 1.0, 0.0)


def spread_mask(column, captions):
    dims = (captions * SEQ, captions)
    token = iota(dims, 0)
    inside = (token % SEQ).astype(F32) <= column
    return jnp.where((token // SEQ == iota(dims, 1)) & inside, 1.0, 0.0)


def head_masks():
    lane = iota((1, 2 * HEAD), 1)
    even = (lane < HEAD).astype(F32)
    return even.astype(BF), (1.0 - even).astype(BF)


def caption_masks():
    lane = iota((SEQ, GROUP), 1) // SEQ
    return [lane == c for c in range(GROUP // SEQ)]


def compact(full, picks):
    out = full[:SEQ]
    for c in range(1, len(picks)):
        out = jnp.where(picks[c], full[c * SEQ : (c + 1) * SEQ], out)
    return out


def expand(low, lows):
    return jnp.concatenate([low * mask for mask in lows], axis=0)


def both_heads(value, masks):
    return jnp.concatenate([value * masks[0], value * masks[1]], axis=0)


def store_permuted(ref, value, dp, blocks):
    rows = value.shape[0] // blocks
    bits = blocks.bit_length() - 1
    if rows % SLOT:
        ref[...] = value
        return
    for b in range(blocks):
        k = jnp.bitwise_xor(dp, b)
        place = 0
        for bit in range(bits):
            place = place + ((k >> bit) & 1) * (1 << (bits - 1 - bit))
        ref[pl.ds(pl.multiple_of(place * rows, SLOT), rows), :] = value[b * rows : (b + 1) * rows]


def forward_kernel(
    blocks,
    dp_ref,
    place_ref,
    vec_ref,
    x_hbm,
    wj_hbm,
    wo_hbm,
    wu_hbm,
    wn_hbm,
    wm_hbm,
    project_hbm,
    slope_hbm,
    normed_hbm,
    context_hbm,
    second_hbm,
    middle_hbm,
    att_hbm,
    mean_ref,
    pooled_ref,
    text_ref,
    scale_ref,
    embed_ref,
    x_ref,
    wj,
    wo,
    wu,
    wn,
    wm,
    project,
    slope,
    normed_t,
    context_t,
    second_t,
    middle,
    att,
    normed,
    context,
    second,
    branch,
    sems,
):
    copies = Copies(sems)
    get = [
        copies.start(a, b)
        for a, b in (
            (x_hbm, x_ref),
            (wj_hbm, wj),
            (wo_hbm, wo),
            (wu_hbm, wu),
            (wn_hbm, wn),
            (wm_hbm, wm),
        )
    ]
    put = []
    dp = dp_ref[0]
    captions = place_ref.shape[1]
    line, column = token_limits(place_ref[...])
    pool = pool_mask(line, captions)
    share = 1.0 / jnp.sum(pool, axis=1, keepdims=True)

    get[0].wait()
    rows = x_ref[...].astype(F32)
    unit, _ = norm_parts(rows)
    value = (unit * vec_ref[:, GAIN1 : GAIN1 + D] + vec_ref[:, SHIFT1 : SHIFT1 + D]).astype(BF)
    normed[...] = value
    get[1].wait()

    def project_step(i, carry):
        at = pl.multiple_of(i * 768, 128)
        bias = vec_ref[:, pl.ds(pl.multiple_of(JOINT + i * 768, 128), 768)]
        project[:, pl.ds(at, 768)] = (nn(normed[...], wj[:, pl.ds(at, 768)]) + bias).astype(BF)
        return carry

    lax.fori_loop(0, 3, project_step, 0)
    put.append(copies.start(project, project_hbm))
    store_permuted(normed_t, normed[...].T, dp, blocks)
    put.append(copies.start(normed_t, normed_hbm))

    masks = head_masks()
    picks = caption_masks()
    lows = [pick.astype(F32).astype(BF) for pick in picks]
    key_place = iota((SEQ, GROUP), 0).astype(F32)
    groups = x_ref.shape[0] // GROUP

    def attend(h, carry):
        at = pl.multiple_of(h * 2 * HEAD, 128)
        for g in range(groups):
            here = slice(g * GROUP, (g + 1) * GROUP)
            query = project[here, pl.ds(at, 128)]
            keys = both_heads(project[here, pl.ds(pl.multiple_of(D + at, 128), 128)], masks)
            values = both_heads(project[here, pl.ds(pl.multiple_of(2 * D + at, 128), 128)], masks)
            scores = nt(keys, query)
            allowed = key_place <= line[:, here]
            parts = []
            for e in range(2):
                score = compact(scores[e * GROUP : (e + 1) * GROUP], picks) * scale
                score = jnp.where(allowed, score, negative)
                score = jnp.exp(score - jnp.max(score, axis=0, keepdims=True))
                weight = score / jnp.sum(score, axis=0, keepdims=True)
                att[2 * h + e, :, here] = weight
                parts.append(expand(weight.astype(BF), lows))
            context[here, pl.ds(at, 128)] = tn(jnp.concatenate(parts, axis=0), values).astype(BF)
        return carry

    lax.fori_loop(0, PAIRS, attend, 0)
    put.append(copies.start(att, att_hbm))
    get[2].wait()
    middle[...] = x_ref[...].astype(F32) + (nn(context[...], wo[...]) + vec_ref[:, OUT : OUT + D])
    put.append(copies.start(middle, middle_hbm))
    store_permuted(context_t, context[...].T, dp, blocks)
    put.append(copies.start(context_t, context_hbm))
    unit, _ = norm_parts(middle[...])
    second[...] = (
        unit * vec_ref[:, GAIN2 : GAIN2 + D] + vec_ref[:, SHIFT2 : SHIFT2 + D]
    ).astype(BF)
    store_permuted(second_t, second[...].T, dp, blocks)
    put.append(copies.start(second_t, second_hbm))
    get[3].wait()
    get[4].wait()
    branch[...] = jnp.zeros_like(branch)
    pool_low = pool.astype(BF)
    c0 = 0.7978845608028654
    c1 = c0 * 0.044715
    step = 512

    def widen(i, carry):
        at = pl.multiple_of(i * step, 128)
        upper = nn(second[...], wu[:, pl.ds(at, step)]) + vec_ref[
            :, pl.ds(pl.multiple_of(WIDE + i * step, 128), step)
        ]
        square = upper * upper
        bend = jnp.tanh(upper * (c0 + c1 * square))
        half = 0.5 + 0.5 * bend
        active = (upper * half).astype(BF)
        slope[:, pl.ds(at, step)] = (
            half + (0.5 * upper) * (1.0 - bend * bend) * (c0 + 3.0 * c1 * square)
        ).astype(BF)
        parts = two(nn(pool_low, active) * share)
        mean_ref[:, pl.ds(at, step)] = parts[:captions]
        branch[...] += nn(parts, wn[pl.ds(at, step), :])
        return carry

    lax.fori_loop(0, FF // step, widen, 0)
    put.append(copies.start(slope, slope_hbm))
    inside = jnp.where((iota((captions * SEQ, 1), 0) % SEQ).astype(F32) <= column, 1.0, 0.0)
    weight = inside / (column + 1.0)
    pooled = jnp.sum((middle[...] * weight).reshape(captions, SEQ, D), axis=1)
    pooled = (
        pooled + (branch[:captions] + branch[captions:] + vec_ref[:, NARROW : NARROW + D])
    ).astype(BF)
    pooled_ref[...] = pooled
    get[5].wait()
    text = nn(pooled, wm[...])
    factor = lax.rsqrt(jnp.sum(text * text, axis=1, keepdims=True) + epsilon)
    text_ref[...] = text
    scale_ref[...] = factor
    embed_ref[...] = (text * factor).astype(BF)
    for copy in put:
        copy.wait()


def forward(blocks, dp, place, vectors, x, wj, wo, wu, wn, wm):
    tokens = x.shape[0]
    captions = place.shape[1]
    big = [
        ((tokens, 3 * D), BF),
        ((tokens, FF), BF),
        ((D, tokens), BF),
        ((D, tokens), BF),
        ((D, tokens), BF),
        ((tokens, D), F32),
        ((HEADS, SEQ, tokens), F32),
    ]
    small = [
        ((captions, FF), BF),
        ((captions, D), BF),
        ((captions, D), F32),
        ((captions, 1), F32),
        ((captions, D), BF),
    ]
    scratch = (
        [((tokens, D), BF)]
        + [(w.shape, BF) for w in (wj, wo, wu, wn, wm)]
        + big
        + [((tokens, D), BF)] * 3
        + [((2 * captions, D), F32)]
    )
    return pl.pallas_call(
        functools.partial(forward_kernel, blocks),
        out_shape=[shape(*s, dtype=t) for s, t in big + small],
        in_specs=[smem, vmem, vmem] + [any_space] * 6,
        out_specs=[any_space] * len(big) + [vmem] * len(small),
        scratch_shapes=[pltpu.VMEM(s, t) for s, t in scratch] + [pltpu.SemaphoreType.DMA((13,))],
        compiler_params=pltpu.CompilerParams(vmem_limit_bytes=LIMIT),
        cost_estimate=cost(10 * tokens * D * FF, 2 * tokens * FF, 40 * D * FF),
        name="text_forward",
    )(dp, place, vectors, x, wj, wo, wu, wn, wm)


def match_of(paired, columns, images):
    column = iota((1, columns), 1)
    valid = column % SLOT < images
    name = jnp.where(valid, (column // SLOT) * images + column % SLOT, -1)
    return paired == name, valid


def contrast_kernel(
    images,
    heat_ref,
    features_ref,
    wp_ref,
    embed_ref,
    paired_ref,
    weight_ref,
    picture_ref,
    score_ref,
    row_ref,
    inverse_ref,
    stats_ref,
):
    picture = nn(features_ref[...], wp_ref[...])
    picture = (
        picture * lax.rsqrt(jnp.sum(picture * picture, axis=1, keepdims=True) + epsilon)
    ).astype(BF)
    picture_ref[...] = picture
    score = nt(embed_ref[...], picture) / heat_ref[0]
    match, valid = match_of(paired_ref[...], score.shape[1], images)
    score = jnp.where(valid, score, negative)
    score_ref[...] = score
    top = jnp.max(score, axis=1, keepdims=True)
    row = jnp.log(jnp.sum(jnp.exp(score - top), axis=1, keepdims=True)) + top
    row_ref[...] = row
    positive = jnp.sum(jnp.where(match, score, 0.0), axis=1, keepdims=True)
    hits = jnp.where(match, 1.0, 0.0)
    counts = jnp.sum(hits, axis=0, keepdims=True)
    inverse = 1.0 / jnp.sum(hits * counts, axis=1, keepdims=True)
    inverse_ref[...] = inverse
    total = jnp.sum(weight_ref[...] * (row - positive - positive * inverse))
    best = jnp.max(score, axis=0, keepdims=True)
    mass = jnp.sum(jnp.exp(score - best), axis=0, keepdims=True)
    line = iota(stats_ref.shape, 0)
    stats_ref[...] = jnp.where(line == 0, best, jnp.where(line == 1, mass, total))


def contrast(images, heat, features, wp, embed, paired, weight):
    captions = embed.shape[0]
    columns = features.shape[0]
    return pl.pallas_call(
        functools.partial(contrast_kernel, images),
        out_shape=[
            shape(columns, D, dtype=BF),
            shape(captions, columns),
            shape(captions, 1),
            shape(captions, 1),
            shape(8, columns),
        ],
        in_specs=[smem] + [vmem] * 5,
        out_specs=[vmem] * 5,
        compiler_params=pltpu.CompilerParams(vmem_limit_bytes=LIMIT),
        cost_estimate=cost(4 * columns * D * D, columns * captions, 8 * columns * D),
        name="contrast",
    )(heat, features, wp, embed, paired, weight)


def quarters(rep, away):
    core = rep & 1
    out = []
    for xrel in range(2):
        for yrel in range(2):
            block = jnp.bitwise_xor(rep, 2 * xrel + away)
            x_first = 1 - core if away == 0 else core
            out.append((jnp.where(x_first == 1, 2 * xrel + yrel, 2 * yrel + xrel), block, yrel))
    return out


def head_back_kernel(
    images,
    rep_ref,
    heat_ref,
    place_ref,
    stats_ref,
    score_ref,
    row_ref,
    inverse_ref,
    weight_ref,
    paired_ref,
    picture_ref,
    text_ref,
    scale_ref,
    wm_hbm,
    wn_hbm,
    slope_hbm,
    second_hbm,
    back_hbm,
    away_hbm,
    here_hbm,
    text_back_ref,
    pooled_ref,
    loss_ref,
    down_bias_ref,
    up_bias_ref,
    wm,
    wn,
    slope,
    second_t,
    back,
    away,
    here,
    sems,
):
    copies = Copies(sems)
    get = [
        copies.start(a, b)
        for a, b in ((wm_hbm, wm), (wn_hbm, wn), (slope_hbm, slope), (second_hbm, second_t))
    ]
    put = []
    rep = rep_ref[0]
    heat = heat_ref[0]
    captions = place_ref.shape[1]
    line, column = token_limits(place_ref[...])
    pool = pool_mask(line, captions)
    count = jnp.sum(pool, axis=1, keepdims=True)
    owner = spread_mask(column, captions).astype(BF)
    owner = jnp.concatenate([owner, owner], axis=1)

    score = score_ref[...]
    match, valid = match_of(paired_ref[...], score.shape[1], images)
    column_log = jnp.log(stats_ref[1:2]) + stats_ref[0:1]
    loss_ref[...] = stats_ref[2:3, :1] + jnp.sum(
        jnp.where(valid, column_log, 0.0), axis=1, keepdims=True
    )
    weight = weight_ref[...]
    graded = (
        weight * jnp.exp(score - row_ref[...])
        + jnp.exp(score - column_log)
        - jnp.where(match, weight * (1.0 + inverse_ref[...]), 0.0)
    )
    graded = jnp.where(valid, graded / heat, 0.0).astype(BF)
    embed_back = nn(graded, picture_ref[...])
    text = text_ref[...]
    factor = scale_ref[...]
    text_dot = jnp.sum(text * embed_back, axis=1, keepdims=True)
    text_back = (factor * embed_back - text * (factor * factor * factor) * text_dot).astype(BF)
    text_back_ref[...] = text_back
    get[0].wait()
    pooled_back = nt(text_back, wm[...])
    pooled_ref[...] = pooled_back
    branch = (pooled_back / count).astype(BF)
    down_bias_ref[...] = jnp.sum(branch.astype(F32) * count, axis=0, keepdims=True)
    get[1].wait()
    get[2].wait()
    ones = jnp.ones((SLOT, back.shape[0]), BF)
    step = 512

    def widen(i, carry):
        at = pl.multiple_of(i * step, 128)
        part = nn(owner, two(nt(branch, wn[pl.ds(at, step), :])))
        part = (part * slope[:, pl.ds(at, step)].astype(F32)).astype(BF)
        back[:, pl.ds(at, step)] = part
        up_bias_ref[:, pl.ds(at, step)] = nn(ones, part)[:1]
        return carry

    lax.fori_loop(0, FF // step, widen, 0)
    put.append(copies.start(back, back_hbm))
    get[3].wait()
    half = second_t.shape[0] // 2
    wide = FF // 4
    for turn, (target, target_hbm) in enumerate(((away, away_hbm), (here, here_hbm))):
        for place, block, yrel in quarters(rep, 1 - turn):
            part = nn(
                second_t[yrel * half : (yrel + 1) * half],
                back[:, pl.ds(pl.multiple_of(block * wide, 128), wide)],
            )
            target[place] = part.astype(BF)
        put.append(copies.start(target, target_hbm))
    for copy in put:
        copy.wait()


def head_back(images, rep, heat, place, stats, score, row, inverse, weight, paired, picture, text,
              factor, wm, wn, slope, second_t):
    captions = text.shape[0]
    tokens = slope.shape[0]
    piece = (4, D // 2, FF // 4)
    return pl.pallas_call(
        functools.partial(head_back_kernel, images),
        out_shape=[
            shape(tokens, FF, dtype=BF),
            shape(*piece, dtype=BF),
            shape(*piece, dtype=BF),
            shape(captions, D, dtype=BF),
            shape(captions, D),
            shape(1, 1),
            shape(1, D),
            shape(1, FF),
        ],
        in_specs=[smem] * 2 + [vmem] * 10 + [any_space] * 4,
        out_specs=[any_space] * 3 + [vmem] * 5,
        scratch_shapes=[
            pltpu.VMEM(wm.shape, BF),
            pltpu.VMEM(wn.shape, BF),
            pltpu.VMEM(slope.shape, BF),
            pltpu.VMEM(second_t.shape, BF),
            pltpu.VMEM(slope.shape, BF),
            pltpu.VMEM(piece, BF),
            pltpu.VMEM(piece, BF),
            pltpu.SemaphoreType.DMA((7,)),
        ],
        compiler_params=pltpu.CompilerParams(vmem_limit_bytes=LIMIT),
        cost_estimate=cost(6 * tokens * D * FF, captions * FF, 24 * D * FF),
        name="head_back",
    )(rep, heat, place, stats, score, row, inverse, weight, paired, picture, text, factor, wm, wn,
      slope, second_t)


def middle_back_kernel(
    place_ref,
    vec_ref,
    pooled_ref,
    back_hbm,
    wu_hbm,
    middle_hbm,
    wo_hbm,
    middle_back_hbm,
    attended_ref,
    context_back_ref,
    gain_ref,
    shift_ref,
    bias_ref,
    back,
    wu,
    middle,
    wo,
    middle_back,
    sems,
):
    copies = Copies(sems)
    get = [
        copies.start(a, b)
        for a, b in ((back_hbm, back), (wu_hbm, wu), (middle_hbm, middle), (wo_hbm, wo))
    ]
    captions = place_ref.shape[1]
    line, column = token_limits(place_ref[...])
    count = jnp.sum(pool_mask(line, captions), axis=1, keepdims=True)
    owner = spread_mask(column, captions).astype(BF)
    owner = jnp.concatenate([owner, owner], axis=1)
    final = nn(owner, two(pooled_ref[...] / count))
    get[2].wait()
    unit, inverse = norm_parts(middle[...])
    get[0].wait()
    get[1].wait()
    second_back = nt(back[...], wu[...])
    part, gain_ref[...], shift_ref[...] = norm_back(
        unit, inverse, vec_ref[:, GAIN2 : GAIN2 + D], second_back
    )
    total = final + part
    middle_back[...] = total
    put = copies.start(middle_back, middle_back_hbm)
    attended = total.astype(BF)
    attended_ref[...] = attended
    bias_ref[...] = nn(jnp.ones((SLOT, attended.shape[0]), BF), attended)[:1]
    get[3].wait()
    context_back_ref[...] = nt(attended, wo[...]).astype(BF)
    put.wait()


def middle_back(place, vectors, pooled, back, wu, middle, wo):
    tokens = back.shape[0]
    return pl.pallas_call(
        middle_back_kernel,
        out_shape=[
            shape(tokens, D),
            shape(tokens, D, dtype=BF),
            shape(tokens, D, dtype=BF),
            shape(1, D),
            shape(1, D),
            shape(1, D),
        ],
        in_specs=[vmem] * 3 + [any_space] * 4,
        out_specs=[any_space] + [vmem] * 5,
        scratch_shapes=[
            pltpu.VMEM(back.shape, BF),
            pltpu.VMEM(wu.shape, BF),
            pltpu.VMEM(middle.shape, F32),
            pltpu.VMEM(wo.shape, BF),
            pltpu.VMEM((tokens, D), F32),
            pltpu.SemaphoreType.DMA((5,)),
        ],
        compiler_params=pltpu.CompilerParams(vmem_limit_bytes=LIMIT),
        cost_estimate=cost(4 * tokens * D * FF, 0, 12 * D * FF),
        name="middle_back",
    )(place, vectors, pooled, back, wu, middle, wo)


def attention_back_kernel(
    rep_ref,
    project_hbm,
    att_hbm,
    context_back_ref,
    attended_ref,
    normed_hbm,
    context_hbm,
    after_hbm,
    back_hbm,
    away_hbm,
    here_hbm,
    bias_ref,
    project,
    att,
    normed_t,
    context_t,
    back,
    away,
    here,
    chosen,
    sems,
):
    copies = Copies(sems)
    get = [
        copies.start(a, b)
        for a, b in (
            (project_hbm, project),
            (att_hbm, att),
            (normed_hbm, normed_t),
            (context_hbm, context_t),
        )
    ]
    put = []
    rep = rep_ref[0]
    masks = head_masks()
    picks = caption_masks()
    lows = [pick.astype(F32).astype(BF) for pick in picks]
    low_scale = jnp.asarray(scale, BF)
    first = iota((GROUP, 2 * HEAD), 1) < HEAD
    tokens = project.shape[0]
    ones = jnp.ones((SLOT, tokens), BF)
    get[0].wait()
    get[1].wait()

    def attend(h, carry):
        at = pl.multiple_of(h * 2 * HEAD, 128)
        at_k = pl.multiple_of(D + at, 128)
        at_v = pl.multiple_of(2 * D + at, 128)
        for g in range(tokens // GROUP):
            span = slice(g * GROUP, (g + 1) * GROUP)
            query = project[span, pl.ds(at, 128)]
            keys = both_heads(project[span, pl.ds(at_k, 128)], masks)
            values = both_heads(project[span, pl.ds(at_v, 128)], masks)
            upper = context_back_ref[span, pl.ds(at, 128)]
            full = nt(values, upper)
            weights, grads = [], []
            for e in range(2):
                weight = att[2 * h + e, :, span]
                part = compact(full[e * GROUP : (e + 1) * GROUP], picks)
                grad = weight * (part - jnp.sum(weight * part, axis=0, keepdims=True))
                weights.append(expand(weight.astype(BF), lows))
                grads.append(expand(grad.astype(BF) * low_scale, lows))
            weights = jnp.concatenate(weights, axis=0)
            grads = jnp.concatenate(grads, axis=0)
            back[span, pl.ds(at, 128)] = tn(grads, keys).astype(BF)
            wide = nn(grads, query)
            back[span, pl.ds(at_k, 128)] = jnp.where(first, wide[:GROUP], wide[GROUP:]).astype(BF)
            wide = nn(weights, upper)
            back[span, pl.ds(at_v, 128)] = jnp.where(first, wide[:GROUP], wide[GROUP:]).astype(BF)
        return carry

    lax.fori_loop(0, PAIRS, attend, 0)
    put.append(copies.start(back, back_hbm))
    joint = 3 * D // 4
    out = D // 4
    for r in range(4):

        @pl.when(rep == r)
        def _():
            for i, k in enumerate((1, 3, 0, 2)):
                b = r ^ k
                chosen[i, :, :joint] = back[:, b * joint : (b + 1) * joint]
                chosen[i, :, joint:] = attended_ref[:, b * out : (b + 1) * out]

    get[2].wait()
    get[3].wait()
    half = D // 2
    for turn, (target, target_hbm) in enumerate(((away, away_hbm), (here, here_hbm))):
        for i, (place, _, yrel) in enumerate(quarters(rep, 1 - turn)):
            block = 2 * turn + i // 2
            lines = slice(yrel * half, (yrel + 1) * half)
            target[place, :, :joint] = nn(normed_t[lines], chosen[block, :, :joint]).astype(BF)
            target[place, :, joint:] = nn(context_t[lines], chosen[block, :, joint:]).astype(BF)
        put.append(copies.start(target, target_hbm))
    for i in range(3):
        lanes = slice(i * D, (i + 1) * D)
        bias_ref[:, lanes] = nn(ones, back[:, lanes])[:1]
    for copy in put:
        copy.wait()


def attention_back(rep, project, att, context_back, attended, normed_t, context_t, after):
    tokens = project.shape[0]
    piece = (4, D // 2, D)
    return pl.pallas_call(
        attention_back_kernel,
        out_shape=[
            shape(tokens, 3 * D, dtype=BF),
            shape(*piece, dtype=BF),
            shape(*piece, dtype=BF),
            shape(1, 3 * D),
        ],
        in_specs=[smem, any_space, any_space, vmem, vmem, any_space, any_space, any_space],
        out_specs=[any_space] * 3 + [vmem],
        scratch_shapes=[
            pltpu.VMEM(project.shape, BF),
            pltpu.VMEM(att.shape, F32),
            pltpu.VMEM(normed_t.shape, BF),
            pltpu.VMEM(context_t.shape, BF),
            pltpu.VMEM(project.shape, BF),
            pltpu.VMEM(piece, BF),
            pltpu.VMEM(piece, BF),
            pltpu.VMEM((4, tokens, D), BF),
            pltpu.SemaphoreType.DMA((7,)),
        ],
        compiler_params=pltpu.CompilerParams(vmem_limit_bytes=LIMIT),
        cost_estimate=cost(10 * tokens * D * FF, 0, 24 * D * FF),
        name="attention_back",
    )(rep, project, att, context_back, attended, normed_t, context_t, after)


def token_back_kernel(
    vec_ref, x_ref, middle_ref, back_ref, wj_ref, after_ref, token_ref, gain_ref, shift_ref
):
    unit, inverse = norm_parts(x_ref[...].astype(F32))
    part, gain_ref[...], shift_ref[...] = norm_back(
        unit, inverse, vec_ref[:, GAIN1 : GAIN1 + D], nt(back_ref[...], wj_ref[...])
    )
    token_ref[...] = middle_ref[...] + part


def token_back(vectors, x, middle, back, wj, after):
    return pl.pallas_call(
        token_back_kernel,
        out_shape=[shape(x.shape[0], D), shape(1, D), shape(1, D)],
        in_specs=[vmem] * 5 + [any_space],
        out_specs=[vmem] * 3,
        compiler_params=pltpu.CompilerParams(vmem_limit_bytes=LIMIT),
        cost_estimate=cost(2 * x.shape[0] * D * FF, 0, 8 * D * FF),
        name="token_back",
    )(vectors, x, middle, back, wj, after)


def both_pairs(partner):
    dp, rep = lax.axis_size("dp"), lax.axis_size("rep")
    pairs = []
    for i in range(dp):
        for j in range(rep):
            a, b = partner(i, j)
            pairs.append((i * rep + j, a * rep + b))
    return pairs


def exchange(value, partner):
    return lax.ppermute(value, ("dp", "rep"), both_pairs(partner))


def first_turn(i, j):
    return (i, j ^ 2) if j & 1 == 0 else (i ^ 1, j)


def second_turn(i, j):
    return (i ^ 1, j) if j & 1 == 0 else (i, j ^ 2)


def added(a, b):
    return (a.astype(F32) + b.astype(F32)).astype(BF)


def core_turn(away, here):
    got = exchange(away, lambda i, j: (i, j ^ 1))
    return added(here[:2], got[:2]), added(here[2:], got[2:])


def half_turn(keep, send, partner):
    got = exchange(send, partner)
    half = keep.shape[0] // 2
    return added(keep[:half], got[:half]), added(keep[half:], got[half:])


def wide_turns(keep, send):
    keep, send = half_turn(keep, send, first_turn)
    return keep[0], send[0]


def last_turns(keep, send):
    dp = lax.axis_size("dp")
    if dp == 2:
        return keep.astype(F32) + exchange(send, second_turn).astype(F32)
    keep, send = half_turn(keep, send, second_turn)
    bits = dp.bit_length() - 1
    for bit in range(1, bits - 1):
        keep, send = half_turn(keep, send, lambda i, j: (i ^ (1 << bit), j))
    got = exchange(send, lambda i, j: (i ^ (1 << (bits - 1)), j))
    return keep.astype(F32) + got.astype(F32)


def relative_rows(value, blocks):
    rows = value.shape[0] // blocks
    if rows % SLOT == 0:
        return value
    bits = blocks.bit_length() - 1
    place = jnp.arange(blocks, dtype=jnp.int32)
    source = jnp.zeros_like(place)
    for bit in range(bits):
        source = source + ((place >> (bits - 1 - bit)) & 1) * (1 << bit)
    source = source ^ lax.axis_index("dp")
    return value.reshape(blocks, rows, -1)[source].reshape(value.shape)


def combine(stats):
    dp, rep = lax.axis_size("dp"), lax.axis_size("rep")
    turns = [(0, 1 << b) for b in range(rep.bit_length() - 1)]
    turns += [(1 << b, 0) for b in range(dp.bit_length() - 1)]
    for a, b in turns:
        got = exchange(stats, lambda i, j: (i ^ a, j ^ b))
        best = jnp.maximum(stats[0:1], got[0:1])
        mass = stats[1:2] * jnp.exp(stats[0:1] - best) + got[1:2] * jnp.exp(got[0:1] - best)
        line = lax.broadcasted_iota(jnp.int32, stats.shape, 0)
        stats = jnp.where(line == 0, best, jnp.where(line == 1, mass, stats + got))
    return stats


def local(
    incoming_activations,
    caption_final_place,
    paired_picture,
    caption_weight,
    locked_picture_features,
    softmax_heat,
    premix_scaling_factor,
    premix_shift_term,
    stacked_mixing_matrix,
    asking_reading_offsets,
    mixing_result_matrix,
    mixing_result_offset,
    premlp_scaling_factor,
    premlp_shift_term,
    widening_matrix,
    widening_offset,
    narrowing_matrix,
    narrowing_offset,
    caption_mapping_matrix,
    picture_mapping_matrix,
):
    both = ("dp", "rep")
    devices = lax.axis_size(both)
    blocks = lax.axis_size("dp")
    parts = lax.axis_size("rep")
    captions = caption_final_place.shape[0]
    images = locked_picture_features.shape[0]
    features = lax.all_gather(
        jnp.pad(locked_picture_features, ((0, SLOT - images), (0, 0))), both, axis=0, tiled=True
    )
    dp = lax.axis_index("dp").astype(jnp.int32).reshape(1)
    rep = lax.axis_index("rep").astype(jnp.int32).reshape(1)
    place = caption_final_place.astype(F32).reshape(1, captions)
    paired = paired_picture.reshape(captions, 1)
    weight = caption_weight.reshape(captions, 1)
    vectors = jnp.concatenate(
        [
            premix_scaling_factor,
            premix_shift_term,
            asking_reading_offsets[:D],
            jnp.zeros((D,), F32),
            asking_reading_offsets[D:],
            mixing_result_offset,
            premlp_scaling_factor,
            premlp_shift_term,
            widening_offset,
            narrowing_offset,
        ]
    ).reshape(1, VECTORS)

    (
        project,
        slope,
        normed_t,
        context_t,
        second_t,
        middle,
        att,
        mean,
        pooled,
        text,
        factor,
        embed,
    ) = forward(
        blocks,
        dp,
        place,
        vectors,
        incoming_activations,
        stacked_mixing_matrix,
        mixing_result_matrix,
        widening_matrix,
        narrowing_matrix,
        caption_mapping_matrix,
    )
    normed_t, context_t, second_t = (
        relative_rows(v, blocks) for v in (normed_t, context_t, second_t)
    )
    picture, score, row, inverse, stats = contrast(
        images, softmax_heat, features, picture_mapping_matrix, embed, paired, weight
    )
    stats = combine(stats)
    hidden, wide = FF // blocks, D // blocks
    fill = -(hidden + wide) % 128
    left = jnp.concatenate(
        [
            mean.reshape(captions, blocks, hidden).transpose(1, 0, 2),
            pooled.reshape(captions, blocks, wide).transpose(1, 0, 2),
            jnp.zeros((blocks, captions, fill), BF),
        ],
        axis=2,
    )
    left = lax.all_to_all(left, "dp", 0, 0, tiled=True)
    left = lax.all_gather(left, "rep", axis=1, tiled=True)
    left = left.reshape(devices * captions, hidden + wide + fill)

    back, away, here, text_back, pooled_back, loss, down_bias, up_bias = head_back(
        images,
        rep,
        softmax_heat,
        place,
        stats,
        score,
        row,
        inverse,
        weight,
        paired,
        picture,
        text,
        factor,
        caption_mapping_matrix,
        narrowing_matrix,
        slope,
        second_t,
    )
    loss = (loss / (captions * devices)).reshape(1)
    all_back = lax.all_gather(text_back, both, axis=0, tiled=True)
    up = core_turn(away, here)
    total, attended, context_back, gain2, shift2, out_bias = middle_back(
        place, vectors, pooled_back, back, widening_matrix, middle, mixing_result_matrix
    )
    project_back, away, here, joint_bias = attention_back(
        rep, project, att, context_back, attended, normed_t, context_t, up[0]
    )
    up = wide_turns(*up)
    mix = core_turn(away, here)
    joint = 3 * D // parts
    token, gain1, shift1 = token_back(
        vectors, incoming_activations, total, project_back, stacked_mixing_matrix, up[0]
    )
    up_block = last_turns(*up)
    mixed = last_turns(*wide_turns(*mix))

    here_rep = lax.axis_index("rep")
    part = D // parts
    back_here = lax.dynamic_slice_in_dim(all_back, here_rep * part, part, 1)
    map_here = lax.dynamic_slice_in_dim(caption_mapping_matrix, here_rep * part, part, 0)
    pooled_all = nt(all_back, map_here).astype(BF)
    down_block = tn(left[:, :hidden], pooled_all)
    head_block = tn(left[:, hidden : hidden + wide], back_here)

    sums = lax.psum(
        jnp.concatenate(
            [
                gain1,
                shift1,
                joint_bias,
                out_bias,
                gain2,
                shift2,
                up_bias,
                down_bias,
                jnp.zeros((1, -VECTORS % 1024), F32),
            ],
            axis=1,
        ).reshape(-1, 128),
        both,
    ).reshape(-1)
    return (
        loss,
        token,
        sums[GAIN1 : GAIN1 + D],
        sums[SHIFT1 : SHIFT1 + D],
        mixed[:, :joint],
        jnp.concatenate([sums[JOINT : JOINT + D], sums[JOINT + 2 * D : JOINT + 3 * D]]),
        mixed[:, joint:],
        sums[OUT : OUT + D],
        sums[GAIN2 : GAIN2 + D],
        sums[SHIFT2 : SHIFT2 + D],
        up_block,
        sums[WIDE : WIDE + FF],
        down_block,
        sums[NARROW : NARROW + D],
        head_block,
    )


def solution(mesh):
    spread = P(("dp", "rep"), None)
    line = P(("dp", "rep"))
    block = P("dp", "rep")
    in_specs = (spread, line, line, line, spread) + (P(),) * 15
    out_specs = (
        P(),
        spread,
        P(),
        P(),
        block,
        P(),
        block,
        P(),
        P(),
        P(),
        block,
        P(),
        block,
        P(),
        block,
    )
    return jax.shard_map(local, mesh=mesh, in_specs=in_specs, out_specs=out_specs, check_vma=False)
```

```python
import functools

import jax
import jax.numpy as jnp
from jax import lax
from jax.experimental import pallas as pl
from jax.experimental.pallas import tpu as pltpu
from jax.sharding import PartitionSpec as P

D = 768
HEADS = 12
HEAD = 64
SEQ = 16
FF = 3072
GROUP = 128
PAIRS = HEADS // 2
SLOT = 16
BF = jnp.bfloat16
F32 = jnp.float32

epsilon = 1e-06
negative = -1e30
scale = HEAD ** (-0.5)
LIMIT = 58 * 1024 * 1024

GAIN1, SHIFT1, JOINT, OUT, GAIN2, SHIFT2, WIDE, NARROW = 0, 768, 1536, 3840, 4608, 5376, 6144, 9216
VECTORS = 9984
LINES = VECTORS // 128

any_space = pl.BlockSpec(memory_space=pl.ANY)
vmem = pl.BlockSpec(memory_space=pltpu.VMEM)
smem = pl.BlockSpec(memory_space=pltpu.SMEM)


def dot(a, b, dims):
    return lax.dot_general(a, b, (dims, ((), ())), preferred_element_type=F32)


def nn(a, b):
    return dot(a, b, ((1,), (0,)))


def nt(a, b):
    return dot(a, b, ((1,), (1,)))


def tn(a, b):
    return dot(a, b, ((0,), (0,)))


def cost(flops, steps, moved):
    return pl.CostEstimate(flops=flops, transcendentals=steps, bytes_accessed=moved)


def shape(*dims, dtype=F32):
    return jax.ShapeDtypeStruct(dims, dtype)


def iota(dims, axis):
    return lax.broadcasted_iota(jnp.int32, dims, axis)


def norm_parts(values):
    average = jnp.mean(values, axis=-1, keepdims=True)
    centred = values - average
    inverse = lax.rsqrt(jnp.mean(centred * centred, axis=-1, keepdims=True) + epsilon)
    return centred * inverse, inverse


def norm_back(unit, inverse, gain, back):
    inner = back * gain
    part = inverse * (
        inner
        - jnp.mean(inner, axis=-1, keepdims=True)
        - unit * jnp.mean(inner * unit, axis=-1, keepdims=True)
    )
    return part, jnp.sum(back * unit, axis=0, keepdims=True), jnp.sum(back, axis=0, keepdims=True)


def split(value):
    high = value.astype(BF)
    return high, (value - high.astype(F32)).astype(BF)


def two(value):
    return jnp.concatenate(split(value), axis=0)


class Copies:
    def __init__(self, sems):
        self.sems = sems
        self.used = 0

    def start(self, source, target):
        copy = pltpu.make_async_copy(source, target, self.sems.at[self.used])
        self.used += 1
        copy.start()
        return copy


def as_row(ref):
    return ref[...].reshape(1, ref.shape[0])


def as_column(ref):
    size = ref.shape[0]
    same = iota((size, size), 0) == iota((size, size), 1)
    row = as_row(ref)
    return jnp.sum(jnp.where(same, row, jnp.zeros_like(row)), axis=1, keepdims=True)


def token_limits(ref):
    place = as_row(ref).astype(F32)
    captions = place.shape[1]
    tokens = captions * SEQ
    owner = (iota((tokens, captions), 0) // SEQ == iota((tokens, captions), 1)).astype(F32)
    column = jnp.sum(owner * place, axis=1, keepdims=True)
    line = nt(place.astype(BF), owner.astype(BF))
    return line, column


def pool_mask(line, captions):
    dims = (captions, captions * SEQ)
    token = iota(dims, 1)
    inside = (token % SEQ).astype(F32) <= line
    return jnp.where((token // SEQ == iota(dims, 0)) & inside, 1.0, 0.0)


def spread_mask(column, captions):
    dims = (captions * SEQ, captions)
    token = iota(dims, 0)
    inside = (token % SEQ).astype(F32) <= column
    return jnp.where((token // SEQ == iota(dims, 1)) & inside, 1.0, 0.0)


def head_masks():
    lane = iota((1, 2 * HEAD), 1)
    even = (lane < HEAD).astype(F32)
    return even.astype(BF), (1.0 - even).astype(BF)


def caption_masks():
    lane = iota((SEQ, GROUP), 1) // SEQ
    return [lane == c for c in range(GROUP // SEQ)]


def compact(full, picks):
    out = full[:SEQ]
    for c in range(1, len(picks)):
        out = jnp.where(picks[c], full[c * SEQ : (c + 1) * SEQ], out)
    return out


def expand(low, lows):
    return jnp.concatenate([low * mask for mask in lows], axis=0)


def both_heads(value, masks):
    return jnp.concatenate([value * masks[0], value * masks[1]], axis=0)


def store_permuted(ref, value, dp, blocks):
    rows = value.shape[0] // blocks
    bits = blocks.bit_length() - 1
    if rows % SLOT:
        ref[...] = value
        return
    for b in range(blocks):
        k = jnp.bitwise_xor(dp, b)
        place = 0
        for bit in range(bits):
            place = place + ((k >> bit) & 1) * (1 << (bits - 1 - bit))
        ref[pl.ds(pl.multiple_of(place * rows, SLOT), rows), :] = value[b * rows : (b + 1) * rows]


def forward_kernel(
    blocks,
    dp_ref,
    place_ref,
    gain1_ref,
    shift1_ref,
    joint_ref,
    out_ref,
    gain2_ref,
    shift2_ref,
    wide_ref,
    narrow_ref,
    x_hbm,
    wj_hbm,
    wo_hbm,
    wu_hbm,
    wn_hbm,
    wm_hbm,
    project_hbm,
    slope_hbm,
    normed_hbm,
    context_hbm,
    second_hbm,
    middle_hbm,
    att_hbm,
    mean_ref,
    pooled_ref,
    text_ref,
    scale_ref,
    embed_ref,
    x_ref,
    wj,
    wo,
    wu,
    wn,
    wm,
    project,
    slope,
    normed_t,
    context_t,
    second_t,
    middle,
    att,
    normed,
    context,
    second,
    branch,
    wide,
    sems,
):
    copies = Copies(sems)
    get = [
        copies.start(a, b)
        for a, b in (
            (x_hbm, x_ref),
            (wj_hbm, wj),
            (wo_hbm, wo),
            (wu_hbm, wu),
            (wn_hbm, wn),
            (wm_hbm, wm),
        )
    ]
    put = []
    dp = dp_ref[0]
    captions = place_ref.shape[0]
    line, column = token_limits(place_ref)
    pool = pool_mask(line, captions)
    share = 1.0 / jnp.sum(pool, axis=1, keepdims=True)

    get[0].wait()
    rows = x_ref[...].astype(F32)
    unit, _ = norm_parts(rows)
    value = (unit * as_row(gain1_ref) + as_row(shift1_ref)).astype(BF)
    normed[...] = value
    get[1].wait()

    joint = as_row(joint_ref)

    def project_step(i, carry):
        at = pl.multiple_of(i * 768, 128)
        bias = jnp.where(i == 0, joint[:, :D], jnp.where(i == 2, joint[:, D:], 0.0))
        project[:, pl.ds(at, 768)] = (nn(normed[...], wj[:, pl.ds(at, 768)]) + bias).astype(BF)
        return carry

    lax.fori_loop(0, 3, project_step, 0)
    put.append(copies.start(project, project_hbm))
    store_permuted(normed_t, normed[...].T, dp, blocks)
    put.append(copies.start(normed_t, normed_hbm))

    masks = head_masks()
    picks = caption_masks()
    lows = [pick.astype(F32).astype(BF) for pick in picks]
    key_place = iota((SEQ, GROUP), 0).astype(F32)
    groups = x_ref.shape[0] // GROUP

    def attend(h, carry):
        at = pl.multiple_of(h * 2 * HEAD, 128)
        for g in range(groups):
            here = slice(g * GROUP, (g + 1) * GROUP)
            query = project[here, pl.ds(at, 128)]
            keys = both_heads(project[here, pl.ds(pl.multiple_of(D + at, 128), 128)], masks)
            values = both_heads(project[here, pl.ds(pl.multiple_of(2 * D + at, 128), 128)], masks)
            scores = nt(keys, query)
            allowed = key_place <= line[:, here]
            parts = []
            for e in range(2):
                score = compact(scores[e * GROUP : (e + 1) * GROUP], picks) * scale
                score = jnp.where(allowed, score, negative)
                score = jnp.exp(score - jnp.max(score, axis=0, keepdims=True))
                weight = score / jnp.sum(score, axis=0, keepdims=True)
                att[2 * h + e, :, here] = weight
                parts.append(expand(weight.astype(BF), lows))
            context[here, pl.ds(at, 128)] = tn(jnp.concatenate(parts, axis=0), values).astype(BF)
        return carry

    lax.fori_loop(0, PAIRS, attend, 0)
    put.append(copies.start(att, att_hbm))
    get[2].wait()
    middle[...] = x_ref[...].astype(F32) + (nn(context[...], wo[...]) + as_row(out_ref))
    put.append(copies.start(middle, middle_hbm))
    store_permuted(context_t, context[...].T, dp, blocks)
    put.append(copies.start(context_t, context_hbm))
    unit, _ = norm_parts(middle[...])
    second[...] = (
        unit * as_row(gain2_ref) + as_row(shift2_ref)
    ).astype(BF)
    store_permuted(second_t, second[...].T, dp, blocks)
    put.append(copies.start(second_t, second_hbm))
    get[3].wait()
    get[4].wait()
    branch[...] = jnp.zeros_like(branch)
    wide[...] = as_row(wide_ref)
    pool_low = pool.astype(BF)
    c0 = 0.7978845608028654
    c1 = c0 * 0.044715
    step = 512

    def widen(i, carry):
        at = pl.multiple_of(i * step, 128)
        upper = nn(second[...], wu[:, pl.ds(at, step)]) + wide[
            :, pl.ds(at, step)
        ]
        square = upper * upper
        bend = jnp.tanh(upper * (c0 + c1 * square))
        half = 0.5 + 0.5 * bend
        active = (upper * half).astype(BF)
        slope[:, pl.ds(at, step)] = (
            half + (0.5 * upper) * (1.0 - bend * bend) * (c0 + 3.0 * c1 * square)
        ).astype(BF)
        parts = two(nn(pool_low, active) * share)
        mean_ref[:, pl.ds(at, step)] = parts[:captions]
        branch[...] += nn(parts, wn[pl.ds(at, step), :])
        return carry

    lax.fori_loop(0, FF // step, widen, 0)
    put.append(copies.start(slope, slope_hbm))
    inside = jnp.where((iota((captions * SEQ, 1), 0) % SEQ).astype(F32) <= column, 1.0, 0.0)
    weight = inside / (column + 1.0)
    pooled = jnp.sum((middle[...] * weight).reshape(captions, SEQ, D), axis=1)
    pooled = (
        pooled + (branch[:captions] + branch[captions:] + as_row(narrow_ref))
    ).astype(BF)
    pooled_ref[...] = pooled
    get[5].wait()
    text = nn(pooled, wm[...])
    factor = lax.rsqrt(jnp.sum(text * text, axis=1, keepdims=True) + epsilon)
    text_ref[...] = text
    scale_ref[...] = factor
    embed_ref[...] = (text * factor).astype(BF)
    for copy in put:
        copy.wait()


def forward(blocks, dp, place, vectors, x, wj, wo, wu, wn, wm):
    tokens = x.shape[0]
    captions = place.shape[0]
    big = [
        ((tokens, 3 * D), BF),
        ((tokens, FF), BF),
        ((D, tokens), BF),
        ((D, tokens), BF),
        ((D, tokens), BF),
        ((tokens, D), F32),
        ((HEADS, SEQ, tokens), F32),
    ]
    small = [
        ((captions, FF), BF),
        ((captions, D), BF),
        ((captions, D), F32),
        ((captions, 1), F32),
        ((captions, D), BF),
    ]
    scratch = (
        [((tokens, D), BF)]
        + [(w.shape, BF) for w in (wj, wo, wu, wn, wm)]
        + big
        + [((tokens, D), BF)] * 3
        + [((2 * captions, D), F32), ((1, FF), F32)]
    )
    return pl.pallas_call(
        functools.partial(forward_kernel, blocks),
        out_shape=[shape(*s, dtype=t) for s, t in big + small],
        in_specs=[smem] + [vmem] * 9 + [any_space] * 6,
        out_specs=[any_space] * len(big) + [vmem] * len(small),
        scratch_shapes=[pltpu.VMEM(s, t) for s, t in scratch] + [pltpu.SemaphoreType.DMA((13,))],
        compiler_params=pltpu.CompilerParams(vmem_limit_bytes=LIMIT),
        cost_estimate=cost(10 * tokens * D * FF, 2 * tokens * FF, 40 * D * FF),
        name="text_forward",
    )(dp, place, *vectors, x, wj, wo, wu, wn, wm)


def match_of(paired, columns, images):
    column = iota((1, columns), 1)
    valid = column % SLOT < images
    name = jnp.where(valid, (column // SLOT) * images + column % SLOT, -1)
    return paired == name, valid


def contrast_kernel(
    images,
    heat_ref,
    features_ref,
    wp_ref,
    embed_ref,
    paired_ref,
    weight_ref,
    picture_ref,
    score_ref,
    row_ref,
    inverse_ref,
    stats_ref,
):
    picture = nn(features_ref[...], wp_ref[...])
    picture = (
        picture * lax.rsqrt(jnp.sum(picture * picture, axis=1, keepdims=True) + epsilon)
    ).astype(BF)
    picture_ref[...] = picture
    score = nt(embed_ref[...], picture) / heat_ref[0]
    match, valid = match_of(as_column(paired_ref), score.shape[1], images)
    score = jnp.where(valid, score, negative)
    score_ref[...] = score
    top = jnp.max(score, axis=1, keepdims=True)
    row = jnp.log(jnp.sum(jnp.exp(score - top), axis=1, keepdims=True)) + top
    row_ref[...] = row
    positive = jnp.sum(jnp.where(match, score, 0.0), axis=1, keepdims=True)
    hits = jnp.where(match, 1.0, 0.0)
    counts = jnp.sum(hits, axis=0, keepdims=True)
    inverse = 1.0 / jnp.sum(hits * counts, axis=1, keepdims=True)
    inverse_ref[...] = inverse
    total = jnp.sum(as_column(weight_ref) * (row - positive - positive * inverse))
    best = jnp.max(score, axis=0, keepdims=True)
    mass = jnp.sum(jnp.exp(score - best), axis=0, keepdims=True)
    mass = jnp.where(iota(mass.shape, 1) == images, total, mass)
    wide = best.shape[1] // 4
    rows = [v[:, i * wide : (i + 1) * wide] for v in (best, mass) for i in range(4)]
    stats_ref[...] = jnp.broadcast_to(jnp.concatenate(rows, axis=0)[None], stats_ref.shape)


def contrast(images, devices, heat, features, wp, embed, paired, weight):
    captions = embed.shape[0]
    columns = features.shape[0]
    return pl.pallas_call(
        functools.partial(contrast_kernel, images),
        out_shape=[
            shape(columns, D, dtype=BF),
            shape(captions, columns),
            shape(captions, 1),
            shape(captions, 1),
            shape(devices, 8, columns // 4),
        ],
        in_specs=[smem] + [vmem] * 5,
        out_specs=[vmem] * 5,
        compiler_params=pltpu.CompilerParams(vmem_limit_bytes=LIMIT),
        cost_estimate=cost(4 * columns * D * D, columns * captions, 8 * columns * D),
        name="contrast",
    )(heat, features, wp, embed, paired, weight)


def quarters(rep, away):
    core = rep & 1
    out = []
    for xrel in range(2):
        for yrel in range(2):
            block = jnp.bitwise_xor(rep, 2 * xrel + away)
            x_first = 1 - core if away == 0 else core
            out.append((jnp.where(x_first == 1, 2 * xrel + yrel, 2 * yrel + xrel), block, yrel))
    return out


def head_back_kernel(
    images,
    rep_ref,
    heat_ref,
    place_ref,
    stats_ref,
    score_ref,
    row_ref,
    inverse_ref,
    weight_ref,
    paired_ref,
    picture_ref,
    text_ref,
    scale_ref,
    mean_ref,
    pooled_low_ref,
    wm_hbm,
    wn_hbm,
    slope_hbm,
    second_hbm,
    back_hbm,
    away_hbm,
    here_hbm,
    outbox_ref,
    pooled_ref,
    loss_ref,
    down_bias_ref,
    up_bias_ref,
    wm,
    wn,
    slope,
    second_t,
    back,
    away,
    here,
    sems,
):
    copies = Copies(sems)
    get = [
        copies.start(a, b)
        for a, b in ((wm_hbm, wm), (wn_hbm, wn), (slope_hbm, slope), (second_hbm, second_t))
    ]
    put = []
    rep = rep_ref[0]
    heat = heat_ref[0]
    captions = place_ref.shape[0]
    line, column = token_limits(place_ref)
    pool = pool_mask(line, captions)
    count = jnp.sum(pool, axis=1, keepdims=True)
    owner = spread_mask(column, captions).astype(BF)
    owner = jnp.concatenate([owner, owner], axis=1)

    score = score_ref[...]
    match, valid = match_of(as_column(paired_ref), score.shape[1], images)
    best = jnp.max(stats_ref[:, :4], axis=0)
    mass = stats_ref[:, 4:] * jnp.exp(stats_ref[:, :4] - best[None])
    column_log = jnp.log(jnp.sum(mass, axis=0)) + best
    column_log = jnp.concatenate([column_log[i : i + 1] for i in range(4)], axis=1)
    total = jnp.sum(stats_ref[:, 4:5, images : images + 1], axis=0)
    loss_ref[...] = total + jnp.sum(
        jnp.where(valid, column_log, 0.0), axis=1, keepdims=True
    )
    weight = as_column(weight_ref)
    graded = (
        weight * jnp.exp(score - row_ref[...])
        + jnp.exp(score - column_log)
        - jnp.where(match, weight * (1.0 + inverse_ref[...]), 0.0)
    )
    graded = jnp.where(valid, graded / heat, 0.0).astype(BF)
    embed_back = nn(graded, picture_ref[...])
    text = text_ref[...]
    factor = scale_ref[...]
    text_dot = jnp.sum(text * embed_back, axis=1, keepdims=True)
    text_back = (factor * embed_back - text * (factor * factor * factor) * text_dot).astype(BF)
    rows_all = mean_ref.shape[1]
    blocks = outbox_ref.shape[0]
    hidden, wide = rows_all // blocks, D // blocks
    for b in range(blocks):
        outbox_ref[b, :, :hidden] = mean_ref[:, b * hidden : (b + 1) * hidden]
        outbox_ref[b, :, hidden : hidden + wide] = pooled_low_ref[:, b * wide : (b + 1) * wide]
        outbox_ref[b, :, outbox_ref.shape[2] - D :] = text_back
    get[0].wait()
    pooled_back = nt(text_back, wm[...])
    pooled_ref[...] = pooled_back
    branch = (pooled_back / count).astype(BF)
    down_bias_ref[...] = jnp.sum(branch.astype(F32) * count, axis=0, keepdims=True)
    get[1].wait()
    get[2].wait()
    ones = jnp.ones((SLOT, back.shape[0]), BF)
    step = 512

    def widen(i, carry):
        at = pl.multiple_of(i * step, 128)
        part = nn(owner, two(nt(branch, wn[pl.ds(at, step), :])))
        part = (part * slope[:, pl.ds(at, step)].astype(F32)).astype(BF)
        back[:, pl.ds(at, step)] = part
        up_bias_ref[:, pl.ds(at, step)] = nn(ones, part)[:1]
        return carry

    lax.fori_loop(0, FF // step, widen, 0)
    put.append(copies.start(back, back_hbm))
    get[3].wait()
    half = second_t.shape[0] // 2
    wide = FF // 4
    for turn, (target, target_hbm) in enumerate(((away, away_hbm), (here, here_hbm))):
        for place, block, yrel in quarters(rep, 1 - turn):
            part = nn(
                second_t[yrel * half : (yrel + 1) * half],
                back[:, pl.ds(pl.multiple_of(block * wide, 128), wide)],
            )
            target[place] = part.astype(BF)
        put.append(copies.start(target, target_hbm))
    for copy in put:
        copy.wait()


def box_width(blocks):
    used = (FF + D) // blocks
    return used + -used % 128 + D


def head_back(images, blocks, rep, heat, place, stats, score, row, inverse, weight, paired, picture,
              text, factor, mean, pooled, wm, wn, slope, second_t):
    captions = text.shape[0]
    tokens = slope.shape[0]
    piece = (4, D // 2, FF // 4)
    return pl.pallas_call(
        functools.partial(head_back_kernel, images),
        out_shape=[
            shape(tokens, FF, dtype=BF),
            shape(*piece, dtype=BF),
            shape(*piece, dtype=BF),
            shape(blocks, captions, box_width(blocks), dtype=BF),
            shape(captions, D),
            shape(1, 1),
            shape(1, D),
            shape(1, FF),
        ],
        in_specs=[smem] * 2 + [vmem] * 12 + [any_space] * 4,
        out_specs=[any_space] * 3 + [vmem] * 5,
        scratch_shapes=[
            pltpu.VMEM(wm.shape, BF),
            pltpu.VMEM(wn.shape, BF),
            pltpu.VMEM(slope.shape, BF),
            pltpu.VMEM(second_t.shape, BF),
            pltpu.VMEM(slope.shape, BF),
            pltpu.VMEM(piece, BF),
            pltpu.VMEM(piece, BF),
            pltpu.SemaphoreType.DMA((7,)),
        ],
        compiler_params=pltpu.CompilerParams(vmem_limit_bytes=LIMIT),
        cost_estimate=cost(6 * tokens * D * FF, captions * FF, 24 * D * FF),
        name="head_back",
    )(rep, heat, place, stats, score, row, inverse, weight, paired, picture, text, factor, mean,
      pooled, wm, wn, slope, second_t)


def middle_back_kernel(
    place_ref,
    gain2_ref,
    pooled_ref,
    back_hbm,
    wu_hbm,
    middle_hbm,
    wo_hbm,
    after_hbm,
    middle_back_hbm,
    attended_ref,
    context_back_ref,
    gain_ref,
    shift_ref,
    bias_ref,
    back,
    wu,
    middle,
    wo,
    middle_back,
    sems,
):
    copies = Copies(sems)
    get = [
        copies.start(a, b)
        for a, b in ((back_hbm, back), (wu_hbm, wu), (middle_hbm, middle), (wo_hbm, wo))
    ]
    captions = place_ref.shape[0]
    line, column = token_limits(place_ref)
    count = jnp.sum(pool_mask(line, captions), axis=1, keepdims=True)
    owner = spread_mask(column, captions).astype(BF)
    owner = jnp.concatenate([owner, owner], axis=1)
    final = nn(owner, two(pooled_ref[...] / count))
    get[2].wait()
    unit, inverse = norm_parts(middle[...])
    get[0].wait()
    get[1].wait()
    second_back = nt(back[...], wu[...])
    part, gain_ref[...], shift_ref[...] = norm_back(
        unit, inverse, as_row(gain2_ref), second_back
    )
    total = final + part
    middle_back[...] = total
    put = copies.start(middle_back, middle_back_hbm)
    attended = total.astype(BF)
    attended_ref[...] = attended
    bias_ref[...] = nn(jnp.ones((SLOT, attended.shape[0]), BF), attended)[:1]
    get[3].wait()
    context_back_ref[...] = nt(attended, wo[...]).astype(BF)
    put.wait()


def middle_back(place, gain, pooled, back, wu, middle, wo, after):
    tokens = back.shape[0]
    return pl.pallas_call(
        middle_back_kernel,
        out_shape=[
            shape(tokens, D),
            shape(tokens, D, dtype=BF),
            shape(tokens, D, dtype=BF),
            shape(1, D),
            shape(1, D),
            shape(1, D),
        ],
        in_specs=[vmem] * 3 + [any_space] * 5,
        out_specs=[any_space] + [vmem] * 5,
        scratch_shapes=[
            pltpu.VMEM(back.shape, BF),
            pltpu.VMEM(wu.shape, BF),
            pltpu.VMEM(middle.shape, F32),
            pltpu.VMEM(wo.shape, BF),
            pltpu.VMEM((tokens, D), F32),
            pltpu.SemaphoreType.DMA((5,)),
        ],
        compiler_params=pltpu.CompilerParams(vmem_limit_bytes=LIMIT),
        cost_estimate=cost(4 * tokens * D * FF, 0, 12 * D * FF),
        name="middle_back",
    )(place, gain, pooled, back, wu, middle, wo, after)


def attention_back_kernel(
    rep_ref,
    project_hbm,
    att_hbm,
    context_back_ref,
    attended_ref,
    normed_hbm,
    context_hbm,
    after_hbm,
    also_hbm,
    back_hbm,
    away_hbm,
    here_hbm,
    bias_ref,
    project,
    att,
    normed_t,
    context_t,
    back,
    away,
    here,
    chosen,
    sems,
):
    copies = Copies(sems)
    get = [
        copies.start(a, b)
        for a, b in (
            (project_hbm, project),
            (att_hbm, att),
            (normed_hbm, normed_t),
            (context_hbm, context_t),
        )
    ]
    put = []
    rep = rep_ref[0]
    masks = head_masks()
    picks = caption_masks()
    lows = [pick.astype(F32).astype(BF) for pick in picks]
    low_scale = jnp.asarray(scale, BF)
    first = iota((GROUP, 2 * HEAD), 1) < HEAD
    tokens = project.shape[0]
    ones = jnp.ones((SLOT, tokens), BF)
    get[0].wait()
    get[1].wait()

    def attend(h, carry):
        at = pl.multiple_of(h * 2 * HEAD, 128)
        at_k = pl.multiple_of(D + at, 128)
        at_v = pl.multiple_of(2 * D + at, 128)
        for g in range(tokens // GROUP):
            span = slice(g * GROUP, (g + 1) * GROUP)
            query = project[span, pl.ds(at, 128)]
            keys = both_heads(project[span, pl.ds(at_k, 128)], masks)
            values = both_heads(project[span, pl.ds(at_v, 128)], masks)
            upper = context_back_ref[span, pl.ds(at, 128)]
            full = nt(values, upper)
            weights, grads = [], []
            for e in range(2):
                weight = att[2 * h + e, :, span]
                part = compact(full[e * GROUP : (e + 1) * GROUP], picks)
                grad = weight * (part - jnp.sum(weight * part, axis=0, keepdims=True))
                weights.append(expand(weight.astype(BF), lows))
                grads.append(expand(grad.astype(BF) * low_scale, lows))
            weights = jnp.concatenate(weights, axis=0)
            grads = jnp.concatenate(grads, axis=0)
            back[span, pl.ds(at, 128)] = tn(grads, keys).astype(BF)
            wide = nn(grads, query)
            back[span, pl.ds(at_k, 128)] = jnp.where(first, wide[:GROUP], wide[GROUP:]).astype(BF)
            wide = nn(weights, upper)
            back[span, pl.ds(at_v, 128)] = jnp.where(first, wide[:GROUP], wide[GROUP:]).astype(BF)
        return carry

    lax.fori_loop(0, PAIRS, attend, 0)
    put.append(copies.start(back, back_hbm))
    joint = 3 * D // 4
    out = D // 4
    for r in range(4):

        @pl.when(rep == r)
        def _():
            for i, k in enumerate((1, 3, 0, 2)):
                b = r ^ k
                chosen[i, :, :joint] = back[:, b * joint : (b + 1) * joint]
                chosen[i, :, joint:] = attended_ref[:, b * out : (b + 1) * out]

    get[2].wait()
    get[3].wait()
    half = D // 2
    for turn, (target, target_hbm) in enumerate(((away, away_hbm), (here, here_hbm))):
        for i, (place, _, yrel) in enumerate(quarters(rep, 1 - turn)):
            block = 2 * turn + i // 2
            lines = slice(yrel * half, (yrel + 1) * half)
            target[place, :, :joint] = nn(normed_t[lines], chosen[block, :, :joint]).astype(BF)
            target[place, :, joint:] = nn(context_t[lines], chosen[block, :, joint:]).astype(BF)
        put.append(copies.start(target, target_hbm))
    for i in range(3):
        lanes = slice(i * D, (i + 1) * D)
        bias_ref[:, lanes] = nn(ones, back[:, lanes])[:1]
    for copy in put:
        copy.wait()


def attention_back(rep, project, att, context_back, attended, normed_t, context_t, after, also):
    tokens = project.shape[0]
    piece = (4, D // 2, D)
    return pl.pallas_call(
        attention_back_kernel,
        out_shape=[
            shape(tokens, 3 * D, dtype=BF),
            shape(*piece, dtype=BF),
            shape(*piece, dtype=BF),
            shape(1, 3 * D),
        ],
        in_specs=[smem, any_space, any_space, vmem, vmem] + [any_space] * 4,
        out_specs=[any_space] * 3 + [vmem],
        scratch_shapes=[
            pltpu.VMEM(project.shape, BF),
            pltpu.VMEM(att.shape, F32),
            pltpu.VMEM(normed_t.shape, BF),
            pltpu.VMEM(context_t.shape, BF),
            pltpu.VMEM(project.shape, BF),
            pltpu.VMEM(piece, BF),
            pltpu.VMEM(piece, BF),
            pltpu.VMEM((4, tokens, D), BF),
            pltpu.SemaphoreType.DMA((7,)),
        ],
        compiler_params=pltpu.CompilerParams(vmem_limit_bytes=LIMIT),
        cost_estimate=cost(10 * tokens * D * FF, 0, 24 * D * FF),
        name="attention_back",
    )(rep, project, att, context_back, attended, normed_t, context_t, after, also)


def token_back_kernel(
    gain1_ref,
    x_ref,
    middle_ref,
    back_ref,
    wj_ref,
    joint_ref,
    out_ref,
    gain2_ref,
    shift2_ref,
    wide_ref,
    narrow_ref,
    after_ref,
    token_ref,
    sums_ref,
):
    unit, inverse = norm_parts(x_ref[...].astype(F32))
    part, gain1, shift1 = norm_back(
        unit, inverse, as_row(gain1_ref), nt(back_ref[...], wj_ref[...])
    )
    token_ref[...] = middle_ref[...] + part
    per = -(-LINES // sums_ref.shape[0])
    line = 0
    rest = (joint_ref, out_ref, gain2_ref, shift2_ref, wide_ref, narrow_ref)
    for value in [gain1, shift1] + [ref[...] for ref in rest]:
        for i in range(value.shape[1] // 128):
            sums_ref[line // per, line % per : line % per + 1] = value[:, i * 128 : (i + 1) * 128]
            line += 1


def token_back(devices, gain, x, middle, back, wj, sums, after):
    return pl.pallas_call(
        token_back_kernel,
        out_shape=[shape(x.shape[0], D), shape(devices, 8, 128)],
        in_specs=[vmem] * 11 + [any_space],
        out_specs=[vmem] * 2,
        compiler_params=pltpu.CompilerParams(vmem_limit_bytes=LIMIT),
        cost_estimate=cost(2 * x.shape[0] * D * FF, 0, 8 * D * FF),
        name="token_back",
    )(gain, x, middle, back, wj, *sums, after)


def low_rank_kernel(
    hidden, rep_ref, own_ref, near_ref, wm_ref, after_ref, down_ref, head_ref, other_ref, box, back
):
    rows = own_ref.shape[0]
    box[:rows] = own_ref[...]
    box[rows:] = near_ref[...]
    part = down_ref.shape[0]
    start = box.shape[1] - D
    rep = rep_ref[0]
    for r in range(D // part):

        @pl.when(rep == r)
        def _():
            for i, b in enumerate((r, r ^ 2)):
                back[i] = box[:, start + b * part : start + (b + 1) * part]

    wide = head_ref.shape[1]
    for i in range(2):
        block = jnp.bitwise_xor(rep, 2 * i)
        here = wm_ref[pl.ds(pl.multiple_of(block * part, SLOT), part), :]
        pooled = nt(box[:, start:], here).astype(BF)
        down = tn(pooled, box[:, :hidden])
        head = tn(back[i], box[:, hidden : hidden + wide])
        if i == 0:
            down_ref[...] = down
            head_ref[...] = head
        else:
            other_ref[:, :hidden] = down.astype(BF)
            other_ref[:, hidden:] = head.astype(BF)


def low_rank(blocks, parts, rep, own, near, wm, after):
    rows = own.shape[0] + near.shape[0]
    hidden, wide, part = FF // blocks, D // blocks, D // parts
    return pl.pallas_call(
        functools.partial(low_rank_kernel, hidden),
        out_shape=[shape(part, hidden), shape(part, wide), shape(part, hidden + wide, dtype=BF)],
        in_specs=[smem] + [vmem] * 3 + [any_space],
        out_specs=[vmem] * 3,
        scratch_shapes=[pltpu.VMEM((rows, own.shape[1]), BF), pltpu.VMEM((2, rows, part), BF)],
        compiler_params=pltpu.CompilerParams(vmem_limit_bytes=LIMIT),
        cost_estimate=cost(8 * rows * D * D, 0, 4 * rows * own.shape[1]),
        name="low_rank",
    )(rep, own, near, wm, after)


def finish_kernel(
    mix_ref,
    mix_got_ref,
    up_ref,
    up_got_ref,
    sums_ref,
    loss_ref,
    down_ref,
    head_ref,
    other_ref,
    joint_ref,
    out_ref,
    up_block_ref,
    down_block_ref,
    head_block_ref,
    loss_out_ref,
    *vector_refs,
):
    total = mix_ref[...].astype(F32) + mix_got_ref[...].astype(F32)
    wide = joint_ref.shape[1]
    joint_ref[...] = total[:, :wide]
    out_ref[...] = total[:, wide:]
    up_block_ref[...] = up_ref[...].astype(F32) + up_got_ref[...].astype(F32)
    hidden = down_ref.shape[1]
    down_block_ref[...] = down_ref[...] + other_ref[:, :hidden].astype(F32)
    head_block_ref[...] = (head_ref[...] + other_ref[:, hidden:].astype(F32)).T
    loss_out_ref[...] = loss_ref[...].reshape(1)
    per = -(-LINES // sums_ref.shape[0])
    starts = (GAIN1, SHIFT1, JOINT, OUT, GAIN2, SHIFT2, WIDE, NARROW)
    for start, ref in zip(starts, vector_refs):
        for i in range(ref.shape[0] // 128):
            line = start // 128 + i
            if start == JOINT and i >= D // 128:
                line += D // 128
            ref[pl.ds(i * 128, 128)] = sums_ref[line // per, line % per]


def finish(mix, up, sums, loss, low, joint):
    rows = mix[0].shape[0]
    sizes = (D, D, 2 * D, D, D, D, FF, D)
    return pl.pallas_call(
        finish_kernel,
        out_shape=[
            shape(rows, joint),
            shape(rows, D - joint),
            shape(rows, D),
            shape(*low[0].shape),
            shape(*low[1].shape[::-1]),
            shape(1),
        ]
        + [shape(n) for n in sizes],
        in_specs=[vmem] * 9,
        out_specs=[vmem] * 14,
        compiler_params=pltpu.CompilerParams(vmem_limit_bytes=LIMIT),
        name="finish",
    )(*mix, *up, sums, loss, *low)


def both_pairs(partner):
    dp, rep = lax.axis_size("dp"), lax.axis_size("rep")
    pairs = []
    for i in range(dp):
        for j in range(rep):
            a, b = partner(i, j)
            pairs.append((i * rep + j, a * rep + b))
    return pairs


def exchange(value, partner):
    return lax.ppermute(value, ("dp", "rep"), both_pairs(partner))


def first_turn(i, j):
    return (i, j ^ 2) if j & 1 == 0 else (i ^ 1, j)


def second_turn(i, j):
    return (i ^ 1, j) if j & 1 == 0 else (i, j ^ 2)


def added(a, b):
    return (a.astype(F32) + b.astype(F32)).astype(BF)


def core_turn(away, here):
    got = exchange(away, lambda i, j: (i, j ^ 1))
    return added(here[:2], got[:2]), added(here[2:], got[2:])


def half_turn(keep, send, partner):
    got = exchange(send, partner)
    half = keep.shape[0] // 2
    return added(keep[:half], got[:half]), added(keep[half:], got[half:])


def wide_turns(keep, send):
    keep, send = half_turn(keep, send, first_turn)
    return keep[0], send[0]


def last_turns(keep, send):
    dp = lax.axis_size("dp")
    if dp == 2:
        return keep, exchange(send, second_turn)
    keep, send = half_turn(keep, send, second_turn)
    bits = dp.bit_length() - 1
    for bit in range(1, bits - 1):
        keep, send = half_turn(keep, send, lambda i, j: (i ^ (1 << bit), j))
    return keep, exchange(send, lambda i, j: (i ^ (1 << (bits - 1)), j))


def relative_rows(value, blocks):
    rows = value.shape[0] // blocks
    if rows % SLOT == 0:
        return value
    bits = blocks.bit_length() - 1
    place = jnp.arange(blocks, dtype=jnp.int32)
    source = jnp.zeros_like(place)
    for bit in range(bits):
        source = source + ((place >> (bits - 1 - bit)) & 1) * (1 << bit)
    source = source ^ lax.axis_index("dp")
    return value.reshape(blocks, rows, -1)[source].reshape(value.shape)


def to_all(value):
    return lax.all_to_all(value, ("dp", "rep"), 0, 0, tiled=True)


def local(
    incoming_activations,
    caption_final_place,
    paired_picture,
    caption_weight,
    locked_picture_features,
    softmax_heat,
    premix_scaling_factor,
    premix_shift_term,
    stacked_mixing_matrix,
    asking_reading_offsets,
    mixing_result_matrix,
    mixing_result_offset,
    premlp_scaling_factor,
    premlp_shift_term,
    widening_matrix,
    widening_offset,
    narrowing_matrix,
    narrowing_offset,
    caption_mapping_matrix,
    picture_mapping_matrix,
):
    both = ("dp", "rep")
    devices = lax.axis_size(both)
    blocks = lax.axis_size("dp")
    parts = lax.axis_size("rep")
    captions = caption_final_place.shape[0]
    images = locked_picture_features.shape[0]
    features = jnp.pad(locked_picture_features, ((0, SLOT - images), (0, 0)))
    features = to_all(jnp.broadcast_to(features[None], (devices,) + features.shape)).reshape(-1, D)
    dp = lax.axis_index("dp").astype(jnp.int32).reshape(1)
    rep = lax.axis_index("rep").astype(jnp.int32).reshape(1)
    vectors = (
        premix_scaling_factor,
        premix_shift_term,
        asking_reading_offsets,
        mixing_result_offset,
        premlp_scaling_factor,
        premlp_shift_term,
        widening_offset,
        narrowing_offset,
    )

    (
        project,
        slope,
        normed_t,
        context_t,
        second_t,
        middle,
        att,
        mean,
        pooled,
        text,
        factor,
        embed,
    ) = forward(
        blocks,
        dp,
        caption_final_place,
        vectors,
        incoming_activations,
        stacked_mixing_matrix,
        mixing_result_matrix,
        widening_matrix,
        narrowing_matrix,
        caption_mapping_matrix,
    )
    normed_t, context_t, second_t = (
        relative_rows(v, blocks) for v in (normed_t, context_t, second_t)
    )
    picture, score, row, inverse, stats = contrast(
        images,
        devices,
        softmax_heat,
        features,
        picture_mapping_matrix,
        embed,
        paired_picture,
        caption_weight,
    )
    stats = to_all(stats)
    back, away, here, box, pooled_back, loss, down_bias, up_bias = head_back(
        images,
        blocks,
        rep,
        softmax_heat,
        caption_final_place,
        stats,
        score,
        row,
        inverse,
        caption_weight,
        paired_picture,
        picture,
        text,
        factor,
        mean,
        pooled,
        caption_mapping_matrix,
        narrowing_matrix,
        slope,
        second_t,
    )
    loss = loss / (captions * devices)
    up = core_turn(away, here)
    box = lax.all_to_all(box, "dp", 0, 0, tiled=True).reshape(blocks * captions, -1)
    total, attended, context_back, gain2, shift2, out_bias = middle_back(
        caption_final_place,
        premlp_scaling_factor,
        pooled_back,
        back,
        widening_matrix,
        middle,
        mixing_result_matrix,
        box,
    )
    near = exchange(box, lambda i, j: (i, j ^ 1))
    project_back, away, here, joint_bias = attention_back(
        rep, project, att, context_back, attended, normed_t, context_t, up[0], near
    )
    up = wide_turns(*up)
    mix = core_turn(away, here)
    joint = 3 * D // parts
    token, sums = token_back(
        devices,
        premix_scaling_factor,
        incoming_activations,
        total,
        project_back,
        stacked_mixing_matrix,
        (joint_bias, out_bias, gain2, shift2, up_bias, down_bias),
        up[0],
    )
    low = low_rank(blocks, parts, rep, box, near, caption_mapping_matrix, token)
    low = (low[0], low[1], exchange(low[2], lambda i, j: (i, j ^ 2)))
    sums = jnp.sum(to_all(sums), axis=0)
    sums = to_all(jnp.broadcast_to(sums[None], (devices,) + sums.shape))
    up = last_turns(*up)
    mix = last_turns(*wide_turns(*mix))
    joint_block, out_block, up_block, down_block, head_block, loss, *grads = finish(
        mix, up, sums, loss, low, joint
    )
    return (
        loss,
        token,
        grads[0],
        grads[1],
        joint_block,
        grads[2],
        out_block,
        grads[3],
        grads[4],
        grads[5],
        up_block,
        grads[6],
        down_block.T,
        grads[7],
        head_block,
    )


def solution(mesh):
    spread = P(("dp", "rep"), None)
    line = P(("dp", "rep"))
    block = P("dp", "rep")
    in_specs = (spread, line, line, line, spread) + (P(),) * 15
    out_specs = (
        P(),
        spread,
        P(),
        P(),
        block,
        P(),
        block,
        P(),
        P(),
        P(),
        block,
        P(),
        block,
        P(),
        block,
    )
    return jax.shard_map(local, mesh=mesh, in_specs=in_specs, out_specs=out_specs, check_vma=False)
```

```python
import functools

import jax
import jax.numpy as jnp
from jax import lax
from jax.experimental import pallas as pl
from jax.experimental.pallas import tpu as pltpu
from jax.sharding import PartitionSpec as P

D = 768
HEADS = 12
HEAD = 64
SEQ = 16
FF = 3072
GROUP = 128
PAIRS = HEADS // 2
SLOT = 16
BF = jnp.bfloat16
F32 = jnp.float32

epsilon = 1e-06
negative = -1e30
scale = HEAD ** (-0.5)
LIMIT = 58 * 1024 * 1024

GAIN1, SHIFT1, JOINT, OUT, GAIN2, SHIFT2, WIDE, NARROW = 0, 768, 1536, 3840, 4608, 5376, 6144, 9216
VECTORS = 9984
LINES = VECTORS // 128

any_space = pl.BlockSpec(memory_space=pl.ANY)
vmem = pl.BlockSpec(memory_space=pltpu.VMEM)
smem = pl.BlockSpec(memory_space=pltpu.SMEM)


def dot(a, b, dims):
    return lax.dot_general(a, b, (dims, ((), ())), preferred_element_type=F32)


def nn(a, b):
    return dot(a, b, ((1,), (0,)))


def nt(a, b):
    return dot(a, b, ((1,), (1,)))


def tn(a, b):
    return dot(a, b, ((0,), (0,)))


def cost(flops, steps, moved):
    return pl.CostEstimate(flops=flops, transcendentals=steps, bytes_accessed=moved)


def shape(*dims, dtype=F32):
    return jax.ShapeDtypeStruct(dims, dtype)


def iota(dims, axis):
    return lax.broadcasted_iota(jnp.int32, dims, axis)


def norm_parts(values):
    average = jnp.mean(values, axis=-1, keepdims=True)
    centred = values - average
    inverse = lax.rsqrt(jnp.mean(centred * centred, axis=-1, keepdims=True) + epsilon)
    return centred * inverse, inverse


def norm_back(unit, inverse, gain, back):
    inner = back * gain
    part = inverse * (
        inner
        - jnp.mean(inner, axis=-1, keepdims=True)
        - unit * jnp.mean(inner * unit, axis=-1, keepdims=True)
    )
    return part, jnp.sum(back * unit, axis=0, keepdims=True), jnp.sum(back, axis=0, keepdims=True)


def split(value):
    high = value.astype(BF)
    return high, (value - high.astype(F32)).astype(BF)


def two(value):
    return jnp.concatenate(split(value), axis=0)


class Copies:
    def __init__(self, sems):
        self.sems = sems
        self.used = 0

    def start(self, source, target):
        copy = pltpu.make_async_copy(source, target, self.sems.at[self.used])
        self.used += 1
        copy.start()
        return copy


def as_row(ref):
    return ref[...].reshape(1, ref.shape[0])


def as_column(ref):
    size = ref.shape[0]
    same = iota((size, size), 0) == iota((size, size), 1)
    row = as_row(ref)
    return jnp.sum(jnp.where(same, row, jnp.zeros_like(row)), axis=1, keepdims=True)


def token_limits(ref):
    place = as_row(ref).astype(F32)
    captions = place.shape[1]
    tokens = captions * SEQ
    owner = (iota((tokens, captions), 0) // SEQ == iota((tokens, captions), 1)).astype(F32)
    column = jnp.sum(owner * place, axis=1, keepdims=True)
    line = nt(place.astype(BF), owner.astype(BF))
    return line, column


def pool_mask(line, captions):
    dims = (captions, captions * SEQ)
    token = iota(dims, 1)
    inside = (token % SEQ).astype(F32) <= line
    return jnp.where((token // SEQ == iota(dims, 0)) & inside, 1.0, 0.0)


def spread_mask(column, captions):
    dims = (captions * SEQ, captions)
    token = iota(dims, 0)
    inside = (token % SEQ).astype(F32) <= column
    return jnp.where((token // SEQ == iota(dims, 1)) & inside, 1.0, 0.0)


def head_masks():
    lane = iota((1, 2 * HEAD), 1)
    even = (lane < HEAD).astype(F32)
    return even.astype(BF), (1.0 - even).astype(BF)


def caption_masks():
    lane = iota((SEQ, GROUP), 1) // SEQ
    return [lane == c for c in range(GROUP // SEQ)]


def compact(full, picks):
    out = full[:SEQ]
    for c in range(1, len(picks)):
        out = jnp.where(picks[c], full[c * SEQ : (c + 1) * SEQ], out)
    return out


def expand(low, lows):
    return jnp.concatenate([low * mask for mask in lows], axis=0)


def both_heads(value, masks):
    return jnp.concatenate([value * masks[0], value * masks[1]], axis=0)


def store_permuted(ref, value, dp, blocks):
    rows = value.shape[0] // blocks
    bits = blocks.bit_length() - 1
    if rows % SLOT:
        ref[...] = value
        return
    for b in range(blocks):
        k = jnp.bitwise_xor(dp, b)
        place = 0
        for bit in range(bits):
            place = place + ((k >> bit) & 1) * (1 << (bits - 1 - bit))
        ref[pl.ds(pl.multiple_of(place * rows, SLOT), rows), :] = value[b * rows : (b + 1) * rows]


def box_width(blocks):
    used = (FF + D) // blocks
    return used + -used % 128


def forward_kernel(
    blocks,
    dp_ref,
    place_ref,
    gain1_ref,
    shift1_ref,
    joint_ref,
    out_ref,
    gain2_ref,
    shift2_ref,
    wide_ref,
    narrow_ref,
    x_hbm,
    wj_hbm,
    wo_hbm,
    wu_hbm,
    wn_hbm,
    wm_hbm,
    project_hbm,
    slope_hbm,
    normed_hbm,
    context_hbm,
    second_hbm,
    middle_hbm,
    att_hbm,
    box_ref,
    text_ref,
    scale_ref,
    embed_ref,
    x_ref,
    wj,
    wo,
    wu,
    wn,
    wm,
    project,
    slope,
    normed_t,
    context_t,
    second_t,
    middle,
    att,
    normed,
    context,
    second,
    branch,
    wide,
    mean,
    sems,
):
    copies = Copies(sems)
    get = [
        copies.start(a, b)
        for a, b in (
            (x_hbm, x_ref),
            (wj_hbm, wj),
            (wo_hbm, wo),
            (wu_hbm, wu),
            (wn_hbm, wn),
            (wm_hbm, wm),
        )
    ]
    put = []
    dp = dp_ref[0]
    captions = place_ref.shape[0]
    line, column = token_limits(place_ref)
    pool = pool_mask(line, captions)
    share = 1.0 / jnp.sum(pool, axis=1, keepdims=True)

    get[0].wait()
    rows = x_ref[...].astype(F32)
    unit, _ = norm_parts(rows)
    value = (unit * as_row(gain1_ref) + as_row(shift1_ref)).astype(BF)
    normed[...] = value
    get[1].wait()

    joint = as_row(joint_ref)

    def project_step(i, carry):
        at = pl.multiple_of(i * 768, 128)
        bias = jnp.where(i == 0, joint[:, :D], jnp.where(i == 2, joint[:, D:], 0.0))
        project[:, pl.ds(at, 768)] = (nn(normed[...], wj[:, pl.ds(at, 768)]) + bias).astype(BF)
        return carry

    lax.fori_loop(0, 3, project_step, 0)
    put.append(copies.start(project, project_hbm))
    store_permuted(normed_t, normed[...].T, dp, blocks)
    put.append(copies.start(normed_t, normed_hbm))

    masks = head_masks()
    picks = caption_masks()
    lows = [pick.astype(F32).astype(BF) for pick in picks]
    key_place = iota((SEQ, GROUP), 0).astype(F32)
    groups = x_ref.shape[0] // GROUP

    def attend(h, carry):
        at = pl.multiple_of(h * 2 * HEAD, 128)
        for g in range(groups):
            here = slice(g * GROUP, (g + 1) * GROUP)
            query = project[here, pl.ds(at, 128)]
            keys = both_heads(project[here, pl.ds(pl.multiple_of(D + at, 128), 128)], masks)
            values = both_heads(project[here, pl.ds(pl.multiple_of(2 * D + at, 128), 128)], masks)
            scores = nt(keys, query)
            allowed = key_place <= line[:, here]
            parts = []
            for e in range(2):
                score = compact(scores[e * GROUP : (e + 1) * GROUP], picks) * scale
                score = jnp.where(allowed, score, negative)
                score = jnp.exp(score - jnp.max(score, axis=0, keepdims=True))
                weight = score / jnp.sum(score, axis=0, keepdims=True)
                att[2 * h + e, :, here] = weight
                parts.append(expand(weight.astype(BF), lows))
            context[here, pl.ds(at, 128)] = tn(jnp.concatenate(parts, axis=0), values).astype(BF)
        return carry

    lax.fori_loop(0, PAIRS, attend, 0)
    put.append(copies.start(att, att_hbm))
    get[2].wait()
    middle[...] = x_ref[...].astype(F32) + (nn(context[...], wo[...]) + as_row(out_ref))
    put.append(copies.start(middle, middle_hbm))
    store_permuted(context_t, context[...].T, dp, blocks)
    put.append(copies.start(context_t, context_hbm))
    unit, _ = norm_parts(middle[...])
    second[...] = (
        unit * as_row(gain2_ref) + as_row(shift2_ref)
    ).astype(BF)
    store_permuted(second_t, second[...].T, dp, blocks)
    put.append(copies.start(second_t, second_hbm))
    get[3].wait()
    get[4].wait()
    branch[...] = jnp.zeros_like(branch)
    wide[...] = as_row(wide_ref)
    pool_low = pool.astype(BF)
    c0 = 0.7978845608028654
    c1 = c0 * 0.044715
    step = 512

    def widen(i, carry):
        at = pl.multiple_of(i * step, 128)
        upper = nn(second[...], wu[:, pl.ds(at, step)]) + wide[
            :, pl.ds(at, step)
        ]
        square = upper * upper
        bend = jnp.tanh(upper * (c0 + c1 * square))
        half = 0.5 + 0.5 * bend
        active = (upper * half).astype(BF)
        slope[:, pl.ds(at, step)] = (
            half + (0.5 * upper) * (1.0 - bend * bend) * (c0 + 3.0 * c1 * square)
        ).astype(BF)
        parts = two(nn(pool_low, active) * share)
        mean[:, pl.ds(at, step)] = parts[:captions]
        branch[...] += nn(parts, wn[pl.ds(at, step), :])
        return carry

    lax.fori_loop(0, FF // step, widen, 0)
    put.append(copies.start(slope, slope_hbm))
    inside = jnp.where((iota((captions * SEQ, 1), 0) % SEQ).astype(F32) <= column, 1.0, 0.0)
    weight = inside / (column + 1.0)
    pooled = jnp.sum((middle[...] * weight).reshape(captions, SEQ, D), axis=1)
    pooled = (
        pooled + (branch[:captions] + branch[captions:] + as_row(narrow_ref))
    ).astype(BF)
    hidden, part = FF // blocks, D // blocks
    for b in range(blocks):
        box_ref[b, :, :hidden] = mean[:, b * hidden : (b + 1) * hidden]
        box_ref[b, :, hidden : hidden + part] = pooled[:, b * part : (b + 1) * part]
    get[5].wait()
    text = nn(pooled, wm[...])
    factor = lax.rsqrt(jnp.sum(text * text, axis=1, keepdims=True) + epsilon)
    text_ref[...] = text
    scale_ref[...] = factor
    embed_ref[...] = (text * factor).astype(BF)
    for copy in put:
        copy.wait()


def forward(blocks, dp, place, vectors, x, wj, wo, wu, wn, wm):
    tokens = x.shape[0]
    captions = place.shape[0]
    big = [
        ((tokens, 3 * D), BF),
        ((tokens, FF), BF),
        ((D, tokens), BF),
        ((D, tokens), BF),
        ((D, tokens), BF),
        ((tokens, D), F32),
        ((HEADS, SEQ, tokens), F32),
    ]
    small = [
        ((blocks, captions, box_width(blocks)), BF),
        ((captions, D), F32),
        ((captions, 1), F32),
        ((captions, D), BF),
    ]
    scratch = (
        [((tokens, D), BF)]
        + [(w.shape, BF) for w in (wj, wo, wu, wn, wm)]
        + big
        + [((tokens, D), BF)] * 3
        + [((2 * captions, D), F32), ((1, FF), F32), ((captions, FF), BF)]
    )
    return pl.pallas_call(
        functools.partial(forward_kernel, blocks),
        out_shape=[shape(*s, dtype=t) for s, t in big + small],
        in_specs=[smem] + [vmem] * 9 + [any_space] * 6,
        out_specs=[any_space] * len(big) + [vmem] * len(small),
        scratch_shapes=[pltpu.VMEM(s, t) for s, t in scratch] + [pltpu.SemaphoreType.DMA((13,))],
        compiler_params=pltpu.CompilerParams(vmem_limit_bytes=LIMIT),
        cost_estimate=cost(10 * tokens * D * FF, 2 * tokens * FF, 40 * D * FF),
        name="text_forward",
    )(dp, place, *vectors, x, wj, wo, wu, wn, wm)


def match_of(paired, columns, images):
    column = iota((1, columns), 1)
    valid = column % SLOT < images
    name = jnp.where(valid, (column // SLOT) * images + column % SLOT, -1)
    return paired == name, valid


def contrast_kernel(
    images,
    heat_ref,
    features_ref,
    wp_ref,
    embed_ref,
    paired_ref,
    weight_ref,
    picture_ref,
    score_ref,
    row_ref,
    inverse_ref,
    stats_ref,
):
    picture = nn(features_ref[...], wp_ref[...])
    picture = (
        picture * lax.rsqrt(jnp.sum(picture * picture, axis=1, keepdims=True) + epsilon)
    ).astype(BF)
    picture_ref[...] = picture
    score = nt(embed_ref[...], picture) / heat_ref[0]
    match, valid = match_of(as_column(paired_ref), score.shape[1], images)
    score = jnp.where(valid, score, negative)
    score_ref[...] = score
    top = jnp.max(score, axis=1, keepdims=True)
    row = jnp.log(jnp.sum(jnp.exp(score - top), axis=1, keepdims=True)) + top
    row_ref[...] = row
    positive = jnp.sum(jnp.where(match, score, 0.0), axis=1, keepdims=True)
    hits = jnp.where(match, 1.0, 0.0)
    counts = jnp.sum(hits, axis=0, keepdims=True)
    inverse = 1.0 / jnp.sum(hits * counts, axis=1, keepdims=True)
    inverse_ref[...] = inverse
    total = jnp.sum(as_column(weight_ref) * (row - positive - positive * inverse))
    best = jnp.max(score, axis=0, keepdims=True)
    mass = jnp.sum(jnp.exp(score - best), axis=0, keepdims=True)
    mass = jnp.where(iota(mass.shape, 1) == images, total, mass)
    wide = best.shape[1] // 4
    rows = [v[:, i * wide : (i + 1) * wide] for v in (best, mass) for i in range(4)]
    stats_ref[...] = jnp.broadcast_to(jnp.concatenate(rows, axis=0)[None], stats_ref.shape)


def contrast(images, devices, heat, features, wp, embed, paired, weight):
    captions = embed.shape[0]
    columns = features.shape[0]
    return pl.pallas_call(
        functools.partial(contrast_kernel, images),
        out_shape=[
            shape(columns, D, dtype=BF),
            shape(captions, columns),
            shape(captions, 1),
            shape(captions, 1),
            shape(devices, 8, columns // 4),
        ],
        in_specs=[smem] + [vmem] * 5,
        out_specs=[vmem] * 5,
        compiler_params=pltpu.CompilerParams(vmem_limit_bytes=LIMIT),
        cost_estimate=cost(4 * columns * D * D, columns * captions, 8 * columns * D),
        name="contrast",
    )(heat, features, wp, embed, paired, weight)


def quarters(rep, away):
    core = rep & 1
    out = []
    for xrel in range(2):
        for yrel in range(2):
            block = jnp.bitwise_xor(rep, 2 * xrel + away)
            x_first = 1 - core if away == 0 else core
            out.append((jnp.where(x_first == 1, 2 * xrel + yrel, 2 * yrel + xrel), block, yrel))
    return out


def head_back_kernel(
    images,
    rep_ref,
    heat_ref,
    place_ref,
    stats_ref,
    score_ref,
    row_ref,
    inverse_ref,
    weight_ref,
    paired_ref,
    picture_ref,
    text_ref,
    scale_ref,
    wm_hbm,
    wn_hbm,
    slope_hbm,
    second_hbm,
    back_hbm,
    away_hbm,
    here_hbm,
    text_back_ref,
    pooled_ref,
    loss_ref,
    down_bias_ref,
    up_bias_ref,
    wm,
    wn,
    slope,
    second_t,
    back,
    away,
    here,
    sems,
):
    copies = Copies(sems)
    get = [
        copies.start(a, b)
        for a, b in ((wm_hbm, wm), (wn_hbm, wn), (slope_hbm, slope), (second_hbm, second_t))
    ]
    put = []
    rep = rep_ref[0]
    heat = heat_ref[0]
    captions = place_ref.shape[0]
    line, column = token_limits(place_ref)
    pool = pool_mask(line, captions)
    count = jnp.sum(pool, axis=1, keepdims=True)
    owner = spread_mask(column, captions).astype(BF)
    owner = jnp.concatenate([owner, owner], axis=1)

    score = score_ref[...]
    match, valid = match_of(as_column(paired_ref), score.shape[1], images)
    best = jnp.max(stats_ref[:, :4], axis=0)
    mass = stats_ref[:, 4:] * jnp.exp(stats_ref[:, :4] - best[None])
    column_log = jnp.log(jnp.sum(mass, axis=0)) + best
    column_log = jnp.concatenate([column_log[i : i + 1] for i in range(4)], axis=1)
    total = jnp.sum(stats_ref[:, 4:5, images : images + 1], axis=0)
    loss_ref[...] = total + jnp.sum(
        jnp.where(valid, column_log, 0.0), axis=1, keepdims=True
    )
    weight = as_column(weight_ref)
    graded = (
        weight * jnp.exp(score - row_ref[...])
        + jnp.exp(score - column_log)
        - jnp.where(match, weight * (1.0 + inverse_ref[...]), 0.0)
    )
    graded = jnp.where(valid, graded / heat, 0.0).astype(BF)
    embed_back = nn(graded, picture_ref[...])
    text = text_ref[...]
    factor = scale_ref[...]
    text_dot = jnp.sum(text * embed_back, axis=1, keepdims=True)
    text_back = (factor * embed_back - text * (factor * factor * factor) * text_dot).astype(BF)
    text_back_ref[...] = text_back
    get[0].wait()
    pooled_back = nt(text_back, wm[...])
    pooled_ref[...] = pooled_back
    branch = (pooled_back / count).astype(BF)
    down_bias_ref[...] = jnp.sum(branch.astype(F32) * count, axis=0, keepdims=True)
    get[1].wait()
    get[2].wait()
    ones = jnp.ones((SLOT, back.shape[0]), BF)
    step = 512

    def widen(i, carry):
        at = pl.multiple_of(i * step, 128)
        part = nn(owner, two(nt(branch, wn[pl.ds(at, step), :])))
        part = (part * slope[:, pl.ds(at, step)].astype(F32)).astype(BF)
        back[:, pl.ds(at, step)] = part
        up_bias_ref[:, pl.ds(at, step)] = nn(ones, part)[:1]
        return carry

    lax.fori_loop(0, FF // step, widen, 0)
    put.append(copies.start(back, back_hbm))
    get[3].wait()
    half = second_t.shape[0] // 2
    wide = FF // 4
    for turn, (target, target_hbm) in enumerate(((away, away_hbm), (here, here_hbm))):
        for place, block, yrel in quarters(rep, 1 - turn):
            part = nn(
                second_t[yrel * half : (yrel + 1) * half],
                back[:, pl.ds(pl.multiple_of(block * wide, 128), wide)],
            )
            target[place] = part.astype(BF)
        put.append(copies.start(target, target_hbm))
    for copy in put:
        copy.wait()


def head_back(images, rep, heat, place, stats, score, row, inverse, weight, paired, picture, text,
              factor, wm, wn, slope, second_t):
    captions = text.shape[0]
    tokens = slope.shape[0]
    piece = (4, D // 2, FF // 4)
    return pl.pallas_call(
        functools.partial(head_back_kernel, images),
        out_shape=[
            shape(tokens, FF, dtype=BF),
            shape(*piece, dtype=BF),
            shape(*piece, dtype=BF),
            shape(captions, D, dtype=BF),
            shape(captions, D),
            shape(1, 1),
            shape(1, D),
            shape(1, FF),
        ],
        in_specs=[smem] * 2 + [vmem] * 10 + [any_space] * 4,
        out_specs=[any_space] * 3 + [vmem] * 5,
        scratch_shapes=[
            pltpu.VMEM(wm.shape, BF),
            pltpu.VMEM(wn.shape, BF),
            pltpu.VMEM(slope.shape, BF),
            pltpu.VMEM(second_t.shape, BF),
            pltpu.VMEM(slope.shape, BF),
            pltpu.VMEM(piece, BF),
            pltpu.VMEM(piece, BF),
            pltpu.SemaphoreType.DMA((7,)),
        ],
        compiler_params=pltpu.CompilerParams(vmem_limit_bytes=LIMIT),
        cost_estimate=cost(6 * tokens * D * FF, captions * FF, 24 * D * FF),
        name="head_back",
    )(rep, heat, place, stats, score, row, inverse, weight, paired, picture, text, factor, wm, wn,
      slope, second_t)


def middle_back_kernel(
    place_ref,
    gain2_ref,
    pooled_ref,
    back_hbm,
    wu_hbm,
    middle_hbm,
    wo_hbm,
    middle_back_hbm,
    attended_ref,
    context_back_ref,
    gain_ref,
    shift_ref,
    bias_ref,
    back,
    wu,
    middle,
    wo,
    middle_back,
    sems,
):
    copies = Copies(sems)
    get = [
        copies.start(a, b)
        for a, b in ((back_hbm, back), (wu_hbm, wu), (middle_hbm, middle), (wo_hbm, wo))
    ]
    captions = place_ref.shape[0]
    line, column = token_limits(place_ref)
    count = jnp.sum(pool_mask(line, captions), axis=1, keepdims=True)
    owner = spread_mask(column, captions).astype(BF)
    owner = jnp.concatenate([owner, owner], axis=1)
    final = nn(owner, two(pooled_ref[...] / count))
    get[2].wait()
    unit, inverse = norm_parts(middle[...])
    get[0].wait()
    get[1].wait()
    second_back = nt(back[...], wu[...])
    part, gain_ref[...], shift_ref[...] = norm_back(
        unit, inverse, as_row(gain2_ref), second_back
    )
    total = final + part
    middle_back[...] = total
    put = copies.start(middle_back, middle_back_hbm)
    attended = total.astype(BF)
    attended_ref[...] = attended
    bias_ref[...] = nn(jnp.ones((SLOT, attended.shape[0]), BF), attended)[:1]
    get[3].wait()
    context_back_ref[...] = nt(attended, wo[...]).astype(BF)
    put.wait()


def middle_back(place, gain, pooled, back, wu, middle, wo):
    tokens = back.shape[0]
    return pl.pallas_call(
        middle_back_kernel,
        out_shape=[
            shape(tokens, D),
            shape(tokens, D, dtype=BF),
            shape(tokens, D, dtype=BF),
            shape(1, D),
            shape(1, D),
            shape(1, D),
        ],
        in_specs=[vmem] * 3 + [any_space] * 4,
        out_specs=[any_space] + [vmem] * 5,
        scratch_shapes=[
            pltpu.VMEM(back.shape, BF),
            pltpu.VMEM(wu.shape, BF),
            pltpu.VMEM(middle.shape, F32),
            pltpu.VMEM(wo.shape, BF),
            pltpu.VMEM((tokens, D), F32),
            pltpu.SemaphoreType.DMA((5,)),
        ],
        compiler_params=pltpu.CompilerParams(vmem_limit_bytes=LIMIT),
        cost_estimate=cost(4 * tokens * D * FF, 0, 12 * D * FF),
        name="middle_back",
    )(place, gain, pooled, back, wu, middle, wo)


def attention_back_kernel(
    rep_ref,
    project_hbm,
    att_hbm,
    context_back_ref,
    attended_ref,
    normed_hbm,
    context_hbm,
    back_hbm,
    away_hbm,
    here_hbm,
    bias_ref,
    project,
    att,
    normed_t,
    context_t,
    back,
    away,
    here,
    chosen,
    sems,
):
    copies = Copies(sems)
    get = [
        copies.start(a, b)
        for a, b in (
            (project_hbm, project),
            (att_hbm, att),
            (normed_hbm, normed_t),
            (context_hbm, context_t),
        )
    ]
    put = []
    rep = rep_ref[0]
    masks = head_masks()
    picks = caption_masks()
    lows = [pick.astype(F32).astype(BF) for pick in picks]
    low_scale = jnp.asarray(scale, BF)
    first = iota((GROUP, 2 * HEAD), 1) < HEAD
    tokens = project.shape[0]
    ones = jnp.ones((SLOT, tokens), BF)
    get[0].wait()
    get[1].wait()

    def attend(h, carry):
        at = pl.multiple_of(h * 2 * HEAD, 128)
        at_k = pl.multiple_of(D + at, 128)
        at_v = pl.multiple_of(2 * D + at, 128)
        for g in range(tokens // GROUP):
            span = slice(g * GROUP, (g + 1) * GROUP)
            query = project[span, pl.ds(at, 128)]
            keys = both_heads(project[span, pl.ds(at_k, 128)], masks)
            values = both_heads(project[span, pl.ds(at_v, 128)], masks)
            upper = context_back_ref[span, pl.ds(at, 128)]
            full = nt(values, upper)
            weights, grads = [], []
            for e in range(2):
                weight = att[2 * h + e, :, span]
                part = compact(full[e * GROUP : (e + 1) * GROUP], picks)
                grad = weight * (part - jnp.sum(weight * part, axis=0, keepdims=True))
                weights.append(expand(weight.astype(BF), lows))
                grads.append(expand(grad.astype(BF) * low_scale, lows))
            weights = jnp.concatenate(weights, axis=0)
            grads = jnp.concatenate(grads, axis=0)
            back[span, pl.ds(at, 128)] = tn(grads, keys).astype(BF)
            wide = nn(grads, query)
            back[span, pl.ds(at_k, 128)] = jnp.where(first, wide[:GROUP], wide[GROUP:]).astype(BF)
            wide = nn(weights, upper)
            back[span, pl.ds(at_v, 128)] = jnp.where(first, wide[:GROUP], wide[GROUP:]).astype(BF)
        return carry

    lax.fori_loop(0, PAIRS, attend, 0)
    put.append(copies.start(back, back_hbm))
    joint = 3 * D // 4
    out = D // 4
    for r in range(4):

        @pl.when(rep == r)
        def _():
            for i, k in enumerate((1, 3, 0, 2)):
                b = r ^ k
                chosen[i, :, :joint] = back[:, b * joint : (b + 1) * joint]
                chosen[i, :, joint:] = attended_ref[:, b * out : (b + 1) * out]

    get[2].wait()
    get[3].wait()
    half = D // 2
    for turn, (target, target_hbm) in enumerate(((away, away_hbm), (here, here_hbm))):
        for i, (place, _, yrel) in enumerate(quarters(rep, 1 - turn)):
            block = 2 * turn + i // 2
            lines = slice(yrel * half, (yrel + 1) * half)
            target[place, :, :joint] = nn(normed_t[lines], chosen[block, :, :joint]).astype(BF)
            target[place, :, joint:] = nn(context_t[lines], chosen[block, :, joint:]).astype(BF)
        put.append(copies.start(target, target_hbm))
    for i in range(3):
        lanes = slice(i * D, (i + 1) * D)
        bias_ref[:, lanes] = nn(ones, back[:, lanes])[:1]
    for copy in put:
        copy.wait()


def attention_back(rep, project, att, context_back, attended, normed_t, context_t):
    tokens = project.shape[0]
    piece = (4, D // 2, D)
    return pl.pallas_call(
        attention_back_kernel,
        out_shape=[
            shape(tokens, 3 * D, dtype=BF),
            shape(*piece, dtype=BF),
            shape(*piece, dtype=BF),
            shape(1, 3 * D),
        ],
        in_specs=[smem, any_space, any_space, vmem, vmem, any_space, any_space],
        out_specs=[any_space] * 3 + [vmem],
        scratch_shapes=[
            pltpu.VMEM(project.shape, BF),
            pltpu.VMEM(att.shape, F32),
            pltpu.VMEM(normed_t.shape, BF),
            pltpu.VMEM(context_t.shape, BF),
            pltpu.VMEM(project.shape, BF),
            pltpu.VMEM(piece, BF),
            pltpu.VMEM(piece, BF),
            pltpu.VMEM((4, tokens, D), BF),
            pltpu.SemaphoreType.DMA((7,)),
        ],
        compiler_params=pltpu.CompilerParams(vmem_limit_bytes=LIMIT),
        cost_estimate=cost(10 * tokens * D * FF, 0, 24 * D * FF),
        name="attention_back",
    )(rep, project, att, context_back, attended, normed_t, context_t)


def token_back_kernel(
    gain1_ref,
    x_ref,
    middle_ref,
    back_ref,
    wj_ref,
    joint_ref,
    out_ref,
    gain2_ref,
    shift2_ref,
    wide_ref,
    narrow_ref,
    token_ref,
    sums_ref,
):
    unit, inverse = norm_parts(x_ref[...].astype(F32))
    part, gain1, shift1 = norm_back(
        unit, inverse, as_row(gain1_ref), nt(back_ref[...], wj_ref[...])
    )
    token_ref[...] = middle_ref[...] + part
    per = -(-LINES // sums_ref.shape[0])
    line = 0
    rest = (joint_ref, out_ref, gain2_ref, shift2_ref, wide_ref, narrow_ref)
    for value in [gain1, shift1] + [ref[...] for ref in rest]:
        for i in range(value.shape[1] // 128):
            sums_ref[line // per, line % per : line % per + 1] = value[:, i * 128 : (i + 1) * 128]
            line += 1


def token_back(devices, gain, x, middle, back, wj, sums):
    return pl.pallas_call(
        token_back_kernel,
        out_shape=[shape(x.shape[0], D), shape(devices, 8, 128)],
        in_specs=[vmem] * 11,
        out_specs=[vmem] * 2,
        compiler_params=pltpu.CompilerParams(vmem_limit_bytes=LIMIT),
        cost_estimate=cost(2 * x.shape[0] * D * FF, 0, 8 * D * FF),
        name="token_back",
    )(gain, x, middle, back, wj, *sums)


def low_rank_kernel(
    hidden,
    masks,
    dp_ref,
    rep_ref,
    left_ref,
    left_near_ref,
    text_ref,
    text_near_ref,
    wm_ref,
    down_ref,
    head_ref,
    other_ref,
    left,
    text,
    back,
):
    rows = text_ref.shape[0]
    text[:rows] = text_ref[...]
    text[rows:] = text_near_ref[...]
    some = rows // len(masks)
    dp = dp_ref[0]
    for i, mask in enumerate(masks):
        source = pl.ds(pl.multiple_of(jnp.bitwise_xor(dp, mask) * some, SLOT), some)
        left[i * some : (i + 1) * some] = left_ref[source]
        left[rows + i * some : rows + (i + 1) * some] = left_near_ref[source]
    part = down_ref.shape[0]
    rep = rep_ref[0]
    for r in range(D // part):

        @pl.when(rep == r)
        def _():
            for i, b in enumerate((r, r ^ 2)):
                back[i] = text[:, b * part : (b + 1) * part]

    wide = head_ref.shape[1]
    for i in range(2):
        block = jnp.bitwise_xor(rep, 2 * i)
        here = wm_ref[pl.ds(pl.multiple_of(block * part, SLOT), part), :]
        pooled = nt(text[...], here).astype(BF)
        down = tn(pooled, left[:, :hidden])
        head = tn(back[i], left[:, hidden : hidden + wide])
        if i == 0:
            down_ref[...] = down
            head_ref[...] = head
        else:
            other_ref[:, :hidden] = down.astype(BF)
            other_ref[:, hidden:] = head.astype(BF)


def low_rank(blocks, parts, masks, dp, rep, left, left_near, text, text_near, wm):
    rows = 2 * text.shape[0]
    hidden, wide, part = FF // blocks, D // blocks, D // parts
    return pl.pallas_call(
        functools.partial(low_rank_kernel, hidden, masks),
        out_shape=[shape(part, hidden), shape(part, wide), shape(part, hidden + wide, dtype=BF)],
        in_specs=[smem] * 2 + [vmem] * 5,
        out_specs=[vmem] * 3,
        scratch_shapes=[
            pltpu.VMEM((rows, left.shape[1]), BF),
            pltpu.VMEM((rows, D), BF),
            pltpu.VMEM((2, rows, part), BF),
        ],
        compiler_params=pltpu.CompilerParams(vmem_limit_bytes=LIMIT),
        cost_estimate=cost(8 * rows * D * D, 0, 4 * rows * D),
        name="low_rank",
    )(dp, rep, left, left_near, text, text_near, wm)


def finish_kernel(
    mix_ref,
    mix_got_ref,
    up_ref,
    up_got_ref,
    sums_ref,
    loss_ref,
    down_ref,
    head_ref,
    other_ref,
    joint_ref,
    out_ref,
    up_block_ref,
    down_block_ref,
    head_block_ref,
    loss_out_ref,
    *vector_refs,
):
    total = mix_ref[...].astype(F32) + mix_got_ref[...].astype(F32)
    wide = joint_ref.shape[1]
    joint_ref[...] = total[:, :wide]
    out_ref[...] = total[:, wide:]
    up_block_ref[...] = up_ref[...].astype(F32) + up_got_ref[...].astype(F32)
    hidden = down_ref.shape[1]
    down_block_ref[...] = down_ref[...] + other_ref[:, :hidden].astype(F32)
    head_block_ref[...] = (head_ref[...] + other_ref[:, hidden:].astype(F32)).T
    loss_out_ref[...] = loss_ref[...].reshape(1)
    per = -(-LINES // sums_ref.shape[0])
    starts = (GAIN1, SHIFT1, JOINT, OUT, GAIN2, SHIFT2, WIDE, NARROW)
    for start, ref in zip(starts, vector_refs):
        for i in range(ref.shape[0] // 128):
            line = start // 128 + i
            if start == JOINT and i >= D // 128:
                line += D // 128
            ref[pl.ds(i * 128, 128)] = sums_ref[line // per, line % per]


def finish(mix, up, sums, loss, low, joint):
    rows = mix[0].shape[0]
    sizes = (D, D, 2 * D, D, D, D, FF, D)
    return pl.pallas_call(
        finish_kernel,
        out_shape=[
            shape(rows, joint),
            shape(rows, D - joint),
            shape(rows, D),
            shape(*low[0].shape),
            shape(*low[1].shape[::-1]),
            shape(1),
        ]
        + [shape(n) for n in sizes],
        in_specs=[vmem] * 9,
        out_specs=[vmem] * 14,
        compiler_params=pltpu.CompilerParams(vmem_limit_bytes=LIMIT),
        name="finish",
    )(*mix, *up, sums, loss, *low)


def both_pairs(partner):
    dp, rep = lax.axis_size("dp"), lax.axis_size("rep")
    pairs = []
    for i in range(dp):
        for j in range(rep):
            a, b = partner(i, j)
            pairs.append((i * rep + j, a * rep + b))
    return pairs


def exchange(value, partner):
    return lax.ppermute(value, ("dp", "rep"), both_pairs(partner))


def first_turn(i, j):
    return (i, j ^ 2) if j & 1 == 0 else (i ^ 1, j)


def second_turn(i, j):
    return (i ^ 1, j) if j & 1 == 0 else (i, j ^ 2)


def added(a, b):
    return (a.astype(F32) + b.astype(F32)).astype(BF)


def halved(here, got):
    half = here.shape[0] // 2
    return added(here[:half], got[:half]), added(here[half:], got[half:])


def core_turn(i, j):
    return i, j ^ 1


def across(i, j):
    return i, j ^ 2


def row_turn(bit):
    return lambda i, j: (i ^ (1 << bit), j)


def next_turn(keep, got, turns, i):
    if i >= len(turns):
        return keep, got
    keep, send = halved(keep, got)
    return keep, exchange(send, turns[i])


order = lax.optimization_barrier


def dp_groups():
    bits = list(range(1, lax.axis_size("dp").bit_length() - 1))
    return [bits[i : i + 2] for i in range(0, len(bits), 2)] + [[0]]


def group_masks(group):
    out = [0]
    for bit in group:
        out += [m | 1 << bit for m in out]
    return out


def gather_masks():
    masks = [0]
    for group in dp_groups():
        masks = [m ^ c for c in group_masks(group) for m in masks]
    return masks


def round_of(value, group):
    return [value] + [
        exchange(value, lambda i, j: (i ^ mask, j)) for mask in group_masks(group)[1:]
    ]


def relative_rows(value, blocks):
    rows = value.shape[0] // blocks
    if rows % SLOT == 0:
        return value
    bits = blocks.bit_length() - 1
    place = jnp.arange(blocks, dtype=jnp.int32)
    source = jnp.zeros_like(place)
    for bit in range(bits):
        source = source + ((place >> (bits - 1 - bit)) & 1) * (1 << bit)
    source = source ^ lax.axis_index("dp")
    return value.reshape(blocks, rows, -1)[source].reshape(value.shape)


def to_all(value):
    return lax.all_to_all(value, ("dp", "rep"), 0, 0, tiled=True)


def local(
    incoming_activations,
    caption_final_place,
    paired_picture,
    caption_weight,
    locked_picture_features,
    softmax_heat,
    premix_scaling_factor,
    premix_shift_term,
    stacked_mixing_matrix,
    asking_reading_offsets,
    mixing_result_matrix,
    mixing_result_offset,
    premlp_scaling_factor,
    premlp_shift_term,
    widening_matrix,
    widening_offset,
    narrowing_matrix,
    narrowing_offset,
    caption_mapping_matrix,
    picture_mapping_matrix,
):
    both = ("dp", "rep")
    devices = lax.axis_size(both)
    blocks = lax.axis_size("dp")
    parts = lax.axis_size("rep")
    captions = caption_final_place.shape[0]
    images = locked_picture_features.shape[0]
    features = jnp.pad(locked_picture_features, ((0, SLOT - images), (0, 0)))
    features = to_all(jnp.broadcast_to(features[None], (devices,) + features.shape)).reshape(-1, D)
    dp = lax.axis_index("dp").astype(jnp.int32).reshape(1)
    rep = lax.axis_index("rep").astype(jnp.int32).reshape(1)
    vectors = (
        premix_scaling_factor,
        premix_shift_term,
        asking_reading_offsets,
        mixing_result_offset,
        premlp_scaling_factor,
        premlp_shift_term,
        widening_offset,
        narrowing_offset,
    )

    (
        project,
        slope,
        normed_t,
        context_t,
        second_t,
        middle,
        att,
        box,
        text,
        factor,
        embed,
    ) = forward(
        blocks,
        dp,
        caption_final_place,
        vectors,
        incoming_activations,
        stacked_mixing_matrix,
        mixing_result_matrix,
        widening_matrix,
        narrowing_matrix,
        caption_mapping_matrix,
    )
    normed_t, context_t, second_t = (
        relative_rows(v, blocks) for v in (normed_t, context_t, second_t)
    )
    picture, score, row, inverse, stats = contrast(
        images,
        devices,
        softmax_heat,
        features,
        picture_mapping_matrix,
        embed,
        paired_picture,
        caption_weight,
    )
    stats, box = order((stats, box))
    stats = to_all(stats)
    left = lax.all_to_all(box, "dp", 0, 0, tiled=True).reshape(blocks * captions, -1)
    back, away, here, text_back, pooled_back, loss, down_bias, up_bias = head_back(
        images,
        rep,
        softmax_heat,
        caption_final_place,
        stats,
        score,
        row,
        inverse,
        caption_weight,
        paired_picture,
        picture,
        text,
        factor,
        caption_mapping_matrix,
        narrowing_matrix,
        slope,
        second_t,
    )
    loss = loss / (captions * devices)
    back, away, text_back, left = order((back, away, text_back, left))
    got = exchange(away, core_turn)
    left_near = exchange(left, core_turn)
    groups = dp_groups()
    pieces = round_of(text_back, groups[0])
    total, attended, context_back, gain2, shift2, out_bias = middle_back(
        caption_final_place,
        premlp_scaling_factor,
        pooled_back,
        back,
        widening_matrix,
        middle,
        mixing_result_matrix,
    )
    context_back, got, left_near, pieces = order((context_back, got, left_near, pieces))
    keep, send = halved(here, got)
    got = exchange(send, first_turn)
    for group in groups[1:]:
        pieces = round_of(jnp.concatenate(pieces), group)
    project_back, away, here, joint_bias = attention_back(
        rep, project, att, context_back, attended, normed_t, context_t
    )
    project_back, away, got, pieces = order((project_back, away, got, pieces))
    keep, send = halved(keep, got)
    up, send = keep[0], send[0]
    got_up = exchange(send, second_turn)
    got = exchange(away, core_turn)
    text_back = jnp.concatenate(pieces)
    text_near = exchange(text_back, core_turn)
    joint = 3 * D // parts
    token, sums = token_back(
        devices,
        premix_scaling_factor,
        incoming_activations,
        total,
        project_back,
        stacked_mixing_matrix,
        (joint_bias, out_bias, gain2, shift2, up_bias, down_bias),
    )
    sums, got_up, got, text_near = order((sums, got_up, got, text_near))
    keep, send = halved(here, got)
    got = exchange(send, first_turn)
    turns = [second_turn] + [row_turn(bit) for bit in range(1, blocks.bit_length() - 1)]
    up, got_up = next_turn(up, got_up, turns, 1)
    sums = to_all(sums)
    *low, other = low_rank(
        blocks,
        parts,
        gather_masks(),
        dp,
        rep,
        left,
        left_near,
        text_back,
        text_near,
        caption_mapping_matrix,
    )
    other = exchange(other, across)
    other, got, got_up, sums = order((other, got, got_up, sums))
    keep, send = halved(keep, got)
    mix = keep[0]
    got = exchange(send[0], second_turn)
    sums = jnp.sum(sums, axis=0)
    sums = to_all(jnp.broadcast_to(sums[None], (devices,) + sums.shape))
    for i in range(2, len(turns)):
        up, got_up = next_turn(up, got_up, turns, i)
    for i in range(1, len(turns)):
        mix, got = next_turn(mix, got, turns, i)
    joint_block, out_block, up_block, down_block, head_block, loss, *grads = finish(
        (mix, got), (up, got_up), sums, loss, (*low, other), joint
    )
    return (
        loss,
        token,
        grads[0],
        grads[1],
        joint_block,
        grads[2],
        out_block,
        grads[3],
        grads[4],
        grads[5],
        up_block,
        grads[6],
        down_block.T,
        grads[7],
        head_block,
    )


def solution(mesh):
    spread = P(("dp", "rep"), None)
    line = P(("dp", "rep"))
    block = P("dp", "rep")
    in_specs = (spread, line, line, line, spread) + (P(),) * 15
    out_specs = (
        P(),
        spread,
        P(),
        P(),
        block,
        P(),
        block,
        P(),
        P(),
        P(),
        block,
        P(),
        block,
        P(),
        block,
    )
    return jax.shard_map(local, mesh=mesh, in_specs=in_specs, out_specs=out_specs, check_vma=False)
```

```python
import functools

import jax
import jax.numpy as jnp
from jax import lax
from jax.experimental import pallas as pl
from jax.experimental.pallas import tpu as pltpu
from jax.sharding import PartitionSpec as P

D = 768
HEADS = 12
HEAD = 64
SEQ = 16
FF = 3072
GROUP = 128
PAIRS = HEADS // 2
SLOT = 16
BF = jnp.bfloat16
F32 = jnp.float32

epsilon = 1e-06
negative = -1e30
scale = HEAD ** (-0.5)
LIMIT = 16 * 1024 * 1024

GAIN1, SHIFT1, JOINT, OUT, GAIN2, SHIFT2, WIDE, NARROW = 0, 768, 1536, 3840, 4608, 5376, 6144, 9216
VECTORS = 9984
LINES = VECTORS // 128
ALL_LINES = LINES + -LINES % 8

vmem = pl.BlockSpec(memory_space=pltpu.VMEM)
smem = pl.BlockSpec(memory_space=pltpu.SMEM)


def dot(a, b, dims):
    return lax.dot_general(a, b, (dims, ((), ())), preferred_element_type=F32)


def nn(a, b):
    return dot(a, b, ((1,), (0,)))


def nt(a, b):
    return dot(a, b, ((1,), (1,)))


def tn(a, b):
    return dot(a, b, ((0,), (0,)))


def cost(flops, steps, moved):
    return pl.CostEstimate(flops=flops, transcendentals=steps, bytes_accessed=moved)


def shape(*dims, dtype=F32):
    return jax.ShapeDtypeStruct(dims, dtype)


def kept(*dims, dtype=BF):
    return pltpu.VMEM(dims, dtype)


def near(*values):
    return [pltpu.with_memory_space_constraint(v, pltpu.VMEM) for v in values]


def kernel_call(name, body, results, small, operands, scratch=(), estimate=None, limit=LIMIT):
    return pl.pallas_call(
        body,
        out_shape=results,
        in_specs=[smem] * len(small) + [vmem] * len(operands),
        out_specs=[vmem] * len(results),
        scratch_shapes=[pltpu.VMEM(s, t) for s, t in scratch],
        compiler_params=pltpu.CompilerParams(vmem_limit_bytes=limit),
        cost_estimate=estimate,
        name=name,
    )(*small, *operands)


def iota(dims, axis):
    return lax.broadcasted_iota(jnp.int32, dims, axis)


def norm_parts(values):
    average = jnp.mean(values, axis=-1, keepdims=True)
    centred = values - average
    inverse = lax.rsqrt(jnp.mean(centred * centred, axis=-1, keepdims=True) + epsilon)
    return centred * inverse, inverse


def norm_back(unit, inverse, gain, back):
    inner = back * gain
    part = inverse * (
        inner
        - jnp.mean(inner, axis=-1, keepdims=True)
        - unit * jnp.mean(inner * unit, axis=-1, keepdims=True)
    )
    return part, jnp.sum(back * unit, axis=0, keepdims=True), jnp.sum(back, axis=0, keepdims=True)


def split(value):
    high = value.astype(BF)
    return high, (value - high.astype(F32)).astype(BF)


def two(value):
    return jnp.concatenate(split(value), axis=0)


def as_row(ref):
    return ref[...].reshape(1, ref.shape[0])


def as_column(ref):
    size = ref.shape[0]
    same = iota((size, size), 0) == iota((size, size), 1)
    row = as_row(ref)
    return jnp.sum(jnp.where(same, row, jnp.zeros_like(row)), axis=1, keepdims=True)


def token_limits(ref):
    place = as_row(ref).astype(F32)
    captions = place.shape[1]
    tokens = captions * SEQ
    owner = (iota((tokens, captions), 0) // SEQ == iota((tokens, captions), 1)).astype(F32)
    column = jnp.sum(owner * place, axis=1, keepdims=True)
    line = nt(place.astype(BF), owner.astype(BF))
    return line, column


def pool_mask(line, captions):
    dims = (captions, captions * SEQ)
    token = iota(dims, 1)
    inside = (token % SEQ).astype(F32) <= line
    return jnp.where((token // SEQ == iota(dims, 0)) & inside, 1.0, 0.0)


def spread_mask(column, captions):
    dims = (captions * SEQ, captions)
    token = iota(dims, 0)
    inside = (token % SEQ).astype(F32) <= column
    return jnp.where((token // SEQ == iota(dims, 1)) & inside, 1.0, 0.0)


def head_masks():
    lane = iota((1, 2 * HEAD), 1)
    even = (lane < HEAD).astype(F32)
    return even.astype(BF), (1.0 - even).astype(BF)


def caption_masks():
    lane = iota((SEQ, GROUP), 1) // SEQ
    return [lane == c for c in range(GROUP // SEQ)]


def compact(full, picks):
    out = full[:SEQ]
    for c in range(1, len(picks)):
        out = jnp.where(picks[c], full[c * SEQ : (c + 1) * SEQ], out)
    return out


def expand(low, lows):
    return jnp.concatenate([low * mask for mask in lows], axis=0)


def both_heads(value, masks):
    return jnp.concatenate([value * masks[0], value * masks[1]], axis=0)


def store_permuted(ref, value, dp, blocks):
    rows = value.shape[0] // blocks
    bits = blocks.bit_length() - 1
    if rows % SLOT:
        ref[...] = value
        return
    for b in range(blocks):
        k = jnp.bitwise_xor(dp, b)
        place = 0
        for bit in range(bits):
            place = place + ((k >> bit) & 1) * (1 << (bits - 1 - bit))
        ref[pl.ds(pl.multiple_of(place * rows, SLOT), rows), :] = value[b * rows : (b + 1) * rows]


def box_width(blocks):
    used = (FF + D) // blocks
    return used + -used % 128


def project_kernel(
    blocks, dp_ref, gain_ref, shift_ref, joint_ref, x_ref, wj_ref, project_ref, normed_ref, normed
):
    unit, _ = norm_parts(x_ref[...].astype(F32))
    normed[...] = (unit * as_row(gain_ref) + as_row(shift_ref)).astype(BF)
    joint = as_row(joint_ref)
    for i, bias in enumerate((joint[:, :D], 0.0, joint[:, D:])):
        lanes = slice(i * D, (i + 1) * D)
        project_ref[:, lanes] = (nn(normed[...], wj_ref[:, lanes]) + bias).astype(BF)
    store_permuted(normed_ref, normed[...].T, dp_ref[0], blocks)


def project_tokens(blocks, dp, gain, shift, joint, x, wj):
    tokens = x.shape[0]
    return kernel_call(
        "project_tokens",
        functools.partial(project_kernel, blocks),
        [kept(tokens, 3 * D), kept(D, tokens)],
        (dp,),
        (gain, shift, joint, *near(x, wj)),
        [((tokens, D), BF)],
        cost(6 * tokens * D * D, 0, 8 * D * D),
    )


def attend_kernel(
    blocks,
    dp_ref,
    place_ref,
    out_ref,
    x_ref,
    project_ref,
    wo_ref,
    att_ref,
    context_t_ref,
    middle_ref,
    context,
):
    line, _ = token_limits(place_ref)
    masks = head_masks()
    picks = caption_masks()
    lows = [pick.astype(F32).astype(BF) for pick in picks]
    key_place = iota((SEQ, GROUP), 0).astype(F32)

    def attend(h, carry):
        at = pl.multiple_of(h * 2 * HEAD, 128)
        for g in range(x_ref.shape[0] // GROUP):
            here = slice(g * GROUP, (g + 1) * GROUP)
            query = project_ref[here, pl.ds(at, 128)]
            keys = both_heads(project_ref[here, pl.ds(pl.multiple_of(D + at, 128), 128)], masks)
            values = both_heads(
                project_ref[here, pl.ds(pl.multiple_of(2 * D + at, 128), 128)], masks
            )
            scores = nt(keys, query)
            allowed = key_place <= line[:, here]
            parts = []
            for e in range(2):
                score = compact(scores[e * GROUP : (e + 1) * GROUP], picks) * scale
                score = jnp.where(allowed, score, negative)
                score = jnp.exp(score - jnp.max(score, axis=0, keepdims=True))
                weight = score / jnp.sum(score, axis=0, keepdims=True)
                att_ref[2 * h + e, :, here] = weight
                parts.append(expand(weight.astype(BF), lows))
            context[here, pl.ds(at, 128)] = tn(jnp.concatenate(parts, axis=0), values).astype(BF)
        return carry

    lax.fori_loop(0, PAIRS, attend, 0)
    middle_ref[...] = x_ref[...].astype(F32) + (nn(context[...], wo_ref[...]) + as_row(out_ref))
    store_permuted(context_t_ref, context[...].T, dp_ref[0], blocks)


def attend_tokens(blocks, dp, place, out, x, project, wo):
    tokens = x.shape[0]
    return kernel_call(
        "attend_tokens",
        functools.partial(attend_kernel, blocks),
        [kept(HEADS, SEQ, tokens, dtype=F32), kept(D, tokens), kept(tokens, D, dtype=F32)],
        (dp,),
        (place, out, *near(x, project, wo)),
        [((tokens, D), BF)],
        cost(8 * tokens * D * D, 0, 8 * D * D),
    )


def widen_kernel(
    blocks,
    dp_ref,
    place_ref,
    gain_ref,
    shift_ref,
    wide_ref,
    narrow_ref,
    middle_ref,
    wu_ref,
    wn_ref,
    wm_ref,
    second_t_ref,
    slope_ref,
    box_ref,
    text_ref,
    scale_ref,
    embed_ref,
    second,
    branch,
    wide,
    mean,
):
    captions = place_ref.shape[0]
    line, column = token_limits(place_ref)
    pool = pool_mask(line, captions)
    share = 1.0 / jnp.sum(pool, axis=1, keepdims=True)
    unit, _ = norm_parts(middle_ref[...])
    second[...] = (unit * as_row(gain_ref) + as_row(shift_ref)).astype(BF)
    store_permuted(second_t_ref, second[...].T, dp_ref[0], blocks)
    branch[...] = jnp.zeros_like(branch)
    wide[...] = as_row(wide_ref)
    pool_low = pool.astype(BF)
    c0 = 0.7978845608028654
    c1 = c0 * 0.044715
    step = 512

    def widen(i, carry):
        at = pl.multiple_of(i * step, 128)
        upper = nn(second[...], wu_ref[:, pl.ds(at, step)]) + wide[:, pl.ds(at, step)]
        square = upper * upper
        bend = jnp.tanh(upper * (c0 + c1 * square))
        half = 0.5 + 0.5 * bend
        active = (upper * half).astype(BF)
        slope_ref[:, pl.ds(at, step)] = (
            half + (0.5 * upper) * (1.0 - bend * bend) * (c0 + 3.0 * c1 * square)
        ).astype(BF)
        parts = two(nn(pool_low, active) * share)
        mean[:, pl.ds(at, step)] = parts[:captions]
        branch[...] += nn(parts, wn_ref[pl.ds(at, step), :])
        return carry

    lax.fori_loop(0, FF // step, widen, 0)
    inside = jnp.where((iota((captions * SEQ, 1), 0) % SEQ).astype(F32) <= column, 1.0, 0.0)
    weight = inside / (column + 1.0)
    pooled = jnp.sum((middle_ref[...] * weight).reshape(captions, SEQ, D), axis=1)
    pooled = (pooled + (branch[:captions] + branch[captions:] + as_row(narrow_ref))).astype(BF)
    hidden, part = FF // blocks, D // blocks
    for b in range(blocks):
        box_ref[b, :, :hidden] = mean[:, b * hidden : (b + 1) * hidden]
        box_ref[b, :, hidden : hidden + part] = pooled[:, b * part : (b + 1) * part]
    text = nn(pooled, wm_ref[...])
    factor = lax.rsqrt(jnp.sum(text * text, axis=1, keepdims=True) + epsilon)
    text_ref[...] = text
    scale_ref[...] = factor
    embed_ref[...] = (text * factor).astype(BF)


def widen_tokens(blocks, dp, place, gain, shift, wide, narrow, middle, wu, wn, wm):
    tokens = middle.shape[0]
    captions = place.shape[0]
    return kernel_call(
        "widen_tokens",
        functools.partial(widen_kernel, blocks),
        [
            kept(D, tokens),
            kept(tokens, FF),
            shape(blocks, captions, box_width(blocks), dtype=BF),
            kept(captions, D, dtype=F32),
            kept(captions, 1, dtype=F32),
            kept(captions, D),
        ],
        (dp,),
        (place, gain, shift, wide, narrow, *near(middle, wu, wn, wm)),
        [
            ((tokens, D), BF),
            ((2 * captions, D), F32),
            ((1, FF), F32),
            ((captions, FF), BF),
        ],
        cost(3 * tokens * D * FF, tokens * FF, 8 * D * FF),
    )


def match_of(paired, columns, images):
    column = iota((1, columns), 1)
    valid = column % SLOT < images
    name = jnp.where(valid, (column // SLOT) * images + column % SLOT, -1)
    return paired == name, valid


def contrast_kernel(
    images,
    parts,
    bits,
    dp_ref,
    rep_ref,
    heat_ref,
    own_ref,
    near_ref,
    wp_ref,
    embed_ref,
    paired_ref,
    weight_ref,
    picture_ref,
    score_ref,
    row_ref,
    inverse_ref,
    stats_ref,
    features,
):
    half = own_ref.shape[0] // SLOT
    for far, ref in enumerate((own_ref, near_ref)):

        def place(i, carry, far=far, ref=ref):
            p = i + far * half
            index = {"dp": dp_ref[0], "rep": rep_ref[0]}
            for n, (axis, bit) in enumerate(bits):
                index[axis] = jnp.bitwise_xor(index[axis], ((p >> n) & 1) << bit)
            to = pl.ds(pl.multiple_of((index["dp"] * parts + index["rep"]) * SLOT, SLOT), SLOT)
            features[to, :] = ref[pl.ds(pl.multiple_of(i * SLOT, SLOT), SLOT), :]
            return carry

        lax.fori_loop(0, half, place, 0, unroll=4)
    picture = nn(features[...], wp_ref[...])
    picture = (
        picture * lax.rsqrt(jnp.sum(picture * picture, axis=1, keepdims=True) + epsilon)
    ).astype(BF)
    picture_ref[...] = picture
    score = nt(embed_ref[...], picture) / heat_ref[0]
    match, valid = match_of(as_column(paired_ref), score.shape[1], images)
    score = jnp.where(valid, score, negative)
    score_ref[...] = score
    top = jnp.max(score, axis=1, keepdims=True)
    row = jnp.log(jnp.sum(jnp.exp(score - top), axis=1, keepdims=True)) + top
    row_ref[...] = row
    positive = jnp.sum(jnp.where(match, score, 0.0), axis=1, keepdims=True)
    hits = jnp.where(match, 1.0, 0.0)
    counts = jnp.sum(hits, axis=0, keepdims=True)
    inverse = 1.0 / jnp.sum(hits * counts, axis=1, keepdims=True)
    inverse_ref[...] = inverse
    total = jnp.sum(as_column(weight_ref) * (row - positive - positive * inverse))
    best = jnp.max(score, axis=0, keepdims=True)
    mass = jnp.sum(jnp.exp(score - best), axis=0, keepdims=True)
    mass = jnp.where(iota(mass.shape, 1) == images, total, mass)
    wide = best.shape[1] // 4
    rows = [v[:, i * wide : (i + 1) * wide] for v in (best, mass) for i in range(4)]
    stats_ref[...] = jnp.concatenate(rows, axis=0)


def contrast(images, parts, bits, dp, rep, heat, own, far, wp, embed, paired, weight):
    captions = embed.shape[0]
    columns = 2 * own.shape[0]
    return kernel_call(
        "contrast",
        functools.partial(contrast_kernel, images, parts, bits),
        [
            kept(columns, D),
            kept(captions, columns, dtype=F32),
            kept(captions, 1, dtype=F32),
            kept(captions, 1, dtype=F32),
            shape(8, columns // 4),
        ],
        (dp, rep, heat),
        (*near(own, far, wp, embed), paired, weight),
        [((columns, D), BF)],
        cost(4 * columns * D * D, columns * captions, 8 * columns * D),
        2 * LIMIT,
    )


def merged(refs):
    best = functools.reduce(jnp.maximum, [ref[:4] for ref in refs])
    mass = sum(ref[4:] * jnp.exp(ref[:4] - best) for ref in refs)
    return best, mass


def merge_kernel(*refs):
    *given, out_ref = refs
    best, mass = merged(given)
    out_ref[...] = jnp.concatenate([best, mass], axis=0)


def merge(stats):
    return kernel_call("merge", merge_kernel, [shape(*stats[0].shape)], (), stats)[0]


def quarters(rep, away):
    core = rep & 1
    out = []
    for xrel in range(2):
        for yrel in range(2):
            block = jnp.bitwise_xor(rep, 2 * xrel + away)
            x_first = 1 - core if away == 0 else core
            out.append((jnp.where(x_first == 1, 2 * xrel + yrel, 2 * yrel + xrel), block, yrel))
    return out


def head_back_kernel(
    images,
    count_stats,
    rep_ref,
    heat_ref,
    place_ref,
    score_ref,
    row_ref,
    inverse_ref,
    weight_ref,
    paired_ref,
    picture_ref,
    text_ref,
    scale_ref,
    wm_ref,
    wn_ref,
    slope_ref,
    second_t_ref,
    *refs,
):
    stats = refs[:count_stats]
    (
        back_ref,
        away_ref,
        here_ref,
        text_back_ref,
        pooled_ref,
        loss_ref,
        down_bias_ref,
        up_bias_ref,
    ) = refs[count_stats:]
    rep = rep_ref[0]
    heat = heat_ref[0]
    captions = place_ref.shape[0]
    line, column = token_limits(place_ref)
    count = jnp.sum(pool_mask(line, captions), axis=1, keepdims=True)
    owner = spread_mask(column, captions).astype(BF)
    owner = jnp.concatenate([owner, owner], axis=1)

    score = score_ref[...]
    match, valid = match_of(as_column(paired_ref), score.shape[1], images)
    best, mass = merged(stats)
    column_log = jnp.log(mass) + best
    column_log = jnp.concatenate([column_log[i : i + 1] for i in range(4)], axis=1)
    loss_ref[...] = mass[:1, images : images + 1] + jnp.sum(
        jnp.where(valid, column_log, 0.0), axis=1, keepdims=True
    )
    weight = as_column(weight_ref)
    graded = (
        weight * jnp.exp(score - row_ref[...])
        + jnp.exp(score - column_log)
        - jnp.where(match, weight * (1.0 + inverse_ref[...]), 0.0)
    )
    graded = jnp.where(valid, graded / heat, 0.0).astype(BF)
    embed_back = nn(graded, picture_ref[...])
    text = text_ref[...]
    factor = scale_ref[...]
    text_dot = jnp.sum(text * embed_back, axis=1, keepdims=True)
    text_back = (factor * embed_back - text * (factor * factor * factor) * text_dot).astype(BF)
    text_back_ref[...] = text_back
    pooled_back = nt(text_back, wm_ref[...])
    pooled_ref[...] = pooled_back
    branch = (pooled_back / count).astype(BF)
    down_bias_ref[...] = jnp.sum(branch.astype(F32) * count, axis=0, keepdims=True)
    ones = jnp.ones((SLOT, back_ref.shape[0]), BF)
    step = 512

    def widen(i, carry):
        at = pl.multiple_of(i * step, 128)
        part = nn(owner, two(nt(branch, wn_ref[pl.ds(at, step), :])))
        part = (part * slope_ref[:, pl.ds(at, step)].astype(F32)).astype(BF)
        back_ref[:, pl.ds(at, step)] = part
        up_bias_ref[:, pl.ds(at, step)] = nn(ones, part)[:1]
        return carry

    lax.fori_loop(0, FF // step, widen, 0)
    half = second_t_ref.shape[0] // 2
    wide = FF // 4
    for turn, target in enumerate((away_ref, here_ref)):
        for place, block, yrel in quarters(rep, 1 - turn):
            part = nn(
                second_t_ref[yrel * half : (yrel + 1) * half],
                back_ref[:, pl.ds(pl.multiple_of(block * wide, 128), wide)],
            )
            target[place] = part.astype(BF)


def head_back(images, rep, heat, place, stats, score, row, inverse, weight, paired, picture, text,
              factor, wm, wn, slope, second_t):
    captions = text.shape[0]
    tokens = slope.shape[0]
    piece = (4, D // 2, FF // 4)
    return kernel_call(
        "head_back",
        functools.partial(head_back_kernel, images, len(stats)),
        [
            kept(tokens, FF),
            kept(*piece),
            kept(*piece),
            shape(captions, D, dtype=BF),
            kept(captions, D, dtype=F32),
            shape(1, 1),
            shape(1, D),
            shape(1, FF),
        ],
        (rep, heat),
        (
            place,
            *near(score, row, inverse),
            weight,
            paired,
            *near(picture, text, factor, wm, wn, slope, second_t),
            *stats,
        ),
        (),
        cost(6 * tokens * D * FF, captions * FF, 24 * D * FF),
    )


def middle_back_kernel(
    place_ref,
    gain_ref,
    pooled_ref,
    back_ref,
    wu_ref,
    middle_ref,
    wo_ref,
    total_ref,
    attended_ref,
    context_back_ref,
    gain_back_ref,
    shift_back_ref,
    bias_ref,
):
    captions = place_ref.shape[0]
    line, column = token_limits(place_ref)
    count = jnp.sum(pool_mask(line, captions), axis=1, keepdims=True)
    owner = spread_mask(column, captions).astype(BF)
    owner = jnp.concatenate([owner, owner], axis=1)
    second_back = nt(back_ref[...], wu_ref[...])
    unit, inverse = norm_parts(middle_ref[...])
    part, gain_back_ref[...], shift_back_ref[...] = norm_back(
        unit, inverse, as_row(gain_ref), second_back
    )
    total = nn(owner, two(pooled_ref[...] / count)) + part
    total_ref[...] = total
    attended = total.astype(BF)
    attended_ref[...] = attended
    bias_ref[...] = nn(jnp.ones((SLOT, attended.shape[0]), BF), attended)[:1]
    context_back_ref[...] = nt(attended, wo_ref[...]).astype(BF)


def middle_back(place, gain, pooled, back, wu, middle, wo):
    tokens = back.shape[0]
    return kernel_call(
        "middle_back",
        middle_back_kernel,
        [
            kept(tokens, D, dtype=F32),
            kept(tokens, D),
            kept(tokens, D),
            shape(1, D),
            shape(1, D),
            shape(1, D),
        ],
        (),
        (place, gain, *near(pooled, back, wu, middle, wo)),
        (),
        cost(4 * tokens * D * FF, 0, 12 * D * FF),
        2 * LIMIT,
    )


def attention_back_kernel(project_ref, att_ref, context_back_ref, back_ref, bias_ref):
    masks = head_masks()
    picks = caption_masks()
    lows = [pick.astype(F32).astype(BF) for pick in picks]
    low_scale = jnp.asarray(scale, BF)
    first = iota((GROUP, 2 * HEAD), 1) < HEAD
    tokens = project_ref.shape[0]

    def attend(h, carry):
        at = pl.multiple_of(h * 2 * HEAD, 128)
        at_k = pl.multiple_of(D + at, 128)
        at_v = pl.multiple_of(2 * D + at, 128)
        for g in range(tokens // GROUP):
            span = slice(g * GROUP, (g + 1) * GROUP)
            query = project_ref[span, pl.ds(at, 128)]
            keys = both_heads(project_ref[span, pl.ds(at_k, 128)], masks)
            values = both_heads(project_ref[span, pl.ds(at_v, 128)], masks)
            upper = context_back_ref[span, pl.ds(at, 128)]
            full = nt(values, upper)
            weights, grads = [], []
            for e in range(2):
                weight = att_ref[2 * h + e, :, span]
                part = compact(full[e * GROUP : (e + 1) * GROUP], picks)
                grad = weight * (part - jnp.sum(weight * part, axis=0, keepdims=True))
                weights.append(expand(weight.astype(BF), lows))
                grads.append(expand(grad.astype(BF) * low_scale, lows))
            weights = jnp.concatenate(weights, axis=0)
            grads = jnp.concatenate(grads, axis=0)
            back_ref[span, pl.ds(at, 128)] = tn(grads, keys).astype(BF)
            wide = nn(grads, query)
            back_ref[span, pl.ds(at_k, 128)] = jnp.where(first, wide[:GROUP], wide[GROUP:]).astype(
                BF
            )
            wide = nn(weights, upper)
            back_ref[span, pl.ds(at_v, 128)] = jnp.where(first, wide[:GROUP], wide[GROUP:]).astype(
                BF
            )
        return carry

    lax.fori_loop(0, PAIRS, attend, 0)
    ones = jnp.ones((SLOT, tokens), BF)
    for i in range(3):
        lanes = slice(i * D, (i + 1) * D)
        bias_ref[:, lanes] = nn(ones, back_ref[:, lanes])[:1]


def attention_back(project, att, context_back):
    tokens = project.shape[0]
    return kernel_call(
        "attention_back",
        attention_back_kernel,
        [kept(tokens, 3 * D), shape(1, 3 * D)],
        (),
        near(project, att, context_back),
        (),
        cost(5 * tokens * D * FF, 0, 12 * D * FF),
    )


def joint_gradient_kernel(
    rep_ref, back_ref, attended_ref, normed_t_ref, context_t_ref, away_ref, here_ref, chosen
):
    rep = rep_ref[0]
    joint = 3 * D // 4
    out = D // 4
    for r in range(4):

        @pl.when(rep == r)
        def _():
            for i, k in enumerate((1, 3, 0, 2)):
                b = r ^ k
                chosen[i, :, :joint] = back_ref[:, b * joint : (b + 1) * joint]
                chosen[i, :, joint:] = attended_ref[:, b * out : (b + 1) * out]

    half = D // 2
    for turn, target in enumerate((away_ref, here_ref)):
        for i, (place, _, yrel) in enumerate(quarters(rep, 1 - turn)):
            block = 2 * turn + i // 2
            lines = slice(yrel * half, (yrel + 1) * half)
            target[place, :, :joint] = nn(normed_t_ref[lines], chosen[block, :, :joint]).astype(BF)
            target[place, :, joint:] = nn(context_t_ref[lines], chosen[block, :, joint:]).astype(BF)


def joint_gradient(rep, back, attended, normed_t, context_t):
    tokens = back.shape[0]
    piece = (4, D // 2, D)
    return kernel_call(
        "joint_gradient",
        joint_gradient_kernel,
        [kept(*piece), kept(*piece)],
        (rep,),
        near(back, attended, normed_t, context_t),
        [((4, tokens, D), BF)],
        cost(3 * tokens * D * FF, 0, 12 * D * FF),
    )


def token_back_kernel(
    gain_ref,
    x_ref,
    middle_ref,
    back_ref,
    wj_ref,
    joint_ref,
    out_ref,
    gain2_ref,
    shift2_ref,
    wide_ref,
    narrow_ref,
    token_ref,
    sums_ref,
):
    unit, inverse = norm_parts(x_ref[...].astype(F32))
    part, gain1, shift1 = norm_back(unit, inverse, as_row(gain_ref), nt(back_ref[...], wj_ref[...]))
    token_ref[...] = middle_ref[...] + part
    line = 0
    rest = (joint_ref, out_ref, gain2_ref, shift2_ref, wide_ref, narrow_ref)
    for value in [gain1, shift1] + [ref[...] for ref in rest]:
        for i in range(value.shape[1] // 128):
            sums_ref[line : line + 1] = value[:, i * 128 : (i + 1) * 128]
            line += 1
    sums_ref[line:] = jnp.zeros((sums_ref.shape[0] - line, 128), F32)


def token_back(gain, x, middle, back, wj, sums):
    return kernel_call(
        "token_back",
        token_back_kernel,
        [shape(x.shape[0], D), shape(ALL_LINES, 128)],
        (),
        (gain, *near(x, middle, back, wj), *sums),
        (),
        cost(2 * x.shape[0] * D * FF, 0, 8 * D * FF),
        2 * LIMIT,
    )


def low_rank_kernel(
    hidden,
    masks,
    dp_ref,
    rep_ref,
    left_ref,
    left_near_ref,
    text_ref,
    text_near_ref,
    wm_ref,
    down_ref,
    head_ref,
    other_ref,
    left,
    text,
    back,
):
    rows = text_ref.shape[0]
    text[:rows] = text_ref[...]
    text[rows:] = text_near_ref[...]
    some = rows // len(masks)
    dp = dp_ref[0]
    for i, mask in enumerate(masks):
        source = pl.ds(pl.multiple_of(jnp.bitwise_xor(dp, mask) * some, SLOT), some)
        left[i * some : (i + 1) * some] = left_ref[source]
        left[rows + i * some : rows + (i + 1) * some] = left_near_ref[source]
    part = down_ref.shape[0]
    rep = rep_ref[0]
    for r in range(D // part):

        @pl.when(rep == r)
        def _():
            for i, b in enumerate((r, r ^ 2)):
                back[i] = text[:, b * part : (b + 1) * part]

    wide = head_ref.shape[1]
    for i in range(2):
        block = jnp.bitwise_xor(rep, 2 * i)
        here = wm_ref[pl.ds(pl.multiple_of(block * part, SLOT), part), :]
        pooled = nt(text[...], here).astype(BF)
        down = tn(pooled, left[:, :hidden])
        head = tn(back[i], left[:, hidden : hidden + wide])
        if i == 0:
            down_ref[...] = down
            head_ref[...] = head
        else:
            other_ref[:, :hidden] = down.astype(BF)
            other_ref[:, hidden:] = head.astype(BF)


def low_rank(blocks, parts, masks, dp, rep, left, left_near, text, text_near, wm):
    rows = 2 * text.shape[0]
    hidden, wide, part = FF // blocks, D // blocks, D // parts
    return kernel_call(
        "low_rank",
        functools.partial(low_rank_kernel, hidden, masks),
        [shape(part, hidden), shape(part, wide), shape(part, hidden + wide, dtype=BF)],
        (dp, rep),
        (left, left_near, text, text_near, wm),
        [((rows, left.shape[1]), BF), ((rows, D), BF), ((2, rows, part), BF)],
        cost(8 * rows * D * D, 0, 4 * rows * D),
    )


def finish_kernel(
    mix_ref,
    mix_got_ref,
    up_ref,
    up_got_ref,
    sums_ref,
    sums_got_ref,
    loss_ref,
    down_ref,
    head_ref,
    other_ref,
    joint_ref,
    out_ref,
    up_block_ref,
    down_block_ref,
    head_block_ref,
    loss_out_ref,
    *vector_refs,
):
    total = mix_ref[...].astype(F32) + mix_got_ref[...].astype(F32)
    wide = joint_ref.shape[1]
    joint_ref[...] = total[:, :wide]
    out_ref[...] = total[:, wide:]
    up_block_ref[...] = up_ref[...].astype(F32) + up_got_ref[...].astype(F32)
    hidden = down_ref.shape[1]
    down_block_ref[...] = down_ref[...] + other_ref[:, :hidden].astype(F32)
    head_block_ref[...] = (head_ref[...] + other_ref[:, hidden:].astype(F32)).T
    loss_out_ref[...] = loss_ref[...].reshape(1)
    starts = (GAIN1, SHIFT1, JOINT, OUT, GAIN2, SHIFT2, WIDE, NARROW)
    for start, ref in zip(starts, vector_refs):
        for i in range(ref.shape[0] // 128):
            line = start // 128 + i
            if start == JOINT and i >= D // 128:
                line += D // 128
            ref[pl.ds(i * 128, 128)] = sums_ref[line] + sums_got_ref[line]


def finish(mix, up, sums, loss, low, joint):
    rows = mix[0].shape[0]
    sizes = (D, D, 2 * D, D, D, D, FF, D)
    return kernel_call(
        "finish",
        finish_kernel,
        [
            shape(rows, joint),
            shape(rows, D - joint),
            shape(rows, D),
            shape(*low[0].shape),
            shape(*low[1].shape[::-1]),
            shape(1),
        ]
        + [shape(n) for n in sizes],
        (),
        (*mix, *up, *sums, loss, *low),
    )


def both_pairs(partner):
    dp, rep = lax.axis_size("dp"), lax.axis_size("rep")
    pairs = []
    for i in range(dp):
        for j in range(rep):
            a, b = partner(i, j)
            pairs.append((i * rep + j, a * rep + b))
    return pairs


def exchange(value, partner):
    return lax.ppermute(value, ("dp", "rep"), both_pairs(partner))


def first_turn(i, j):
    return (i, j ^ 2) if j & 1 == 0 else (i ^ 1, j)


def second_turn(i, j):
    return (i ^ 1, j) if j & 1 == 0 else (i, j ^ 2)


def added(a, b):
    return (a.astype(F32) + b.astype(F32)).astype(BF)


def halved(here, got):
    half = here.shape[0] // 2
    return added(here[:half], got[:half]), added(here[half:], got[half:])


def core_turn(i, j):
    return i, j ^ 1


def across(i, j):
    return i, j ^ 2


def row_turn(bit):
    return lambda i, j: (i ^ (1 << bit), j)


def next_turn(keep, got, turns, i):
    if i >= len(turns):
        return keep, got
    keep, send = halved(keep, got)
    return keep, exchange(send, turns[i])


order = lax.optimization_barrier


def dp_groups():
    bits = [("dp", b) for b in range(1, lax.axis_size("dp").bit_length() - 1)]
    return [bits[i : i + 2] for i in range(0, len(bits), 2)] + [[("dp", 0)]]


def all_groups():
    bits = [("rep", b) for b in range(1, lax.axis_size("rep").bit_length() - 1)]
    groups = dp_groups()
    return groups[:-1] + [groups[-1] + bits, [("rep", 0)]]


def group_masks(group):
    out = [(0, 0)]
    for axis, bit in group:
        out += [(a | 1 << bit, b) if axis == "dp" else (a, b | 1 << bit) for a, b in out]
    return out


def gather_masks():
    masks = [0]
    for group in dp_groups():
        masks = [m ^ c for c, _ in group_masks(group) for m in masks]
    return masks


def round_of(value, group):
    return [value] + [
        exchange(value, lambda i, j: (i ^ a, j ^ b)) for a, b in group_masks(group)[1:]
    ]


def relative_rows(value, blocks):
    rows = value.shape[0] // blocks
    if rows % SLOT == 0:
        return value
    bits = blocks.bit_length() - 1
    place = jnp.arange(blocks, dtype=jnp.int32)
    source = jnp.zeros_like(place)
    for bit in range(bits):
        source = source + ((place >> (bits - 1 - bit)) & 1) * (1 << bit)
    source = source ^ lax.axis_index("dp")
    return value.reshape(blocks, rows, -1)[source].reshape(value.shape)


def local(
    incoming_activations,
    caption_final_place,
    paired_picture,
    caption_weight,
    locked_picture_features,
    softmax_heat,
    premix_scaling_factor,
    premix_shift_term,
    stacked_mixing_matrix,
    asking_reading_offsets,
    mixing_result_matrix,
    mixing_result_offset,
    premlp_scaling_factor,
    premlp_shift_term,
    widening_matrix,
    widening_offset,
    narrowing_matrix,
    narrowing_offset,
    caption_mapping_matrix,
    picture_mapping_matrix,
):
    both = ("dp", "rep")
    devices = lax.axis_size(both)
    blocks = lax.axis_size("dp")
    parts = lax.axis_size("rep")
    captions = caption_final_place.shape[0]
    images = locked_picture_features.shape[0]
    dp = lax.axis_index("dp").astype(jnp.int32).reshape(1)
    rep = lax.axis_index("rep").astype(jnp.int32).reshape(1)
    groups = all_groups()
    pieces = round_of(jnp.pad(locked_picture_features, ((0, SLOT - images), (0, 0))), groups[0])
    project, normed_t = project_tokens(
        blocks,
        dp,
        premix_scaling_factor,
        premix_shift_term,
        asking_reading_offsets,
        incoming_activations,
        stacked_mixing_matrix,
    )
    project, pieces = order((project, pieces))
    for group in groups[1:-1]:
        pieces = round_of(jnp.concatenate(pieces), group)
    att, context_t, middle = attend_tokens(
        blocks,
        dp,
        caption_final_place,
        mixing_result_offset,
        incoming_activations,
        project,
        mixing_result_matrix,
    )
    middle, pieces = order((middle, pieces))
    own, far = round_of(jnp.concatenate(pieces), groups[-1])
    second_t, slope, box, text, factor, embed = widen_tokens(
        blocks,
        dp,
        caption_final_place,
        premlp_scaling_factor,
        premlp_shift_term,
        widening_offset,
        narrowing_offset,
        middle,
        widening_matrix,
        narrowing_matrix,
        caption_mapping_matrix,
    )
    normed_t, context_t, second_t = (
        relative_rows(v, blocks) for v in (normed_t, context_t, second_t)
    )
    embed, far = order((embed, far))
    picture, score, row, inverse, stats = contrast(
        images,
        parts,
        sum(groups, []),
        dp,
        rep,
        softmax_heat,
        own,
        far,
        picture_mapping_matrix,
        embed,
        paired_picture,
        caption_weight,
    )
    stats, box = order((stats, box))
    groups = dp_groups()
    stats = round_of(stats, [("rep", 0), ("rep", 1)] + groups[-1])
    left = lax.all_to_all(box, "dp", 0, 0, tiled=True).reshape(blocks * captions, -1)
    stats, left = order((stats, left))
    for group in groups[:-1]:
        stats = round_of(merge(stats), group)
    back, away, here, text_back, pooled_back, loss, down_bias, up_bias = head_back(
        images,
        rep,
        softmax_heat,
        caption_final_place,
        stats,
        score,
        row,
        inverse,
        caption_weight,
        paired_picture,
        picture,
        text,
        factor,
        caption_mapping_matrix,
        narrowing_matrix,
        slope,
        second_t,
    )
    loss = loss / (captions * devices)
    back, away, text_back, left = order((back, away, text_back, left))
    got = exchange(away, core_turn)
    left_near = exchange(left, core_turn)
    pieces = round_of(text_back, groups[0])
    total, attended, context_back, gain2, shift2, out_bias = middle_back(
        caption_final_place,
        premlp_scaling_factor,
        pooled_back,
        back,
        widening_matrix,
        middle,
        mixing_result_matrix,
    )
    context_back, got, left_near, pieces = order((context_back, got, left_near, pieces))
    keep, send = halved(here, got)
    got = exchange(send, first_turn)
    for group in groups[1:]:
        pieces = round_of(jnp.concatenate(pieces), group)
    project_back, joint_bias = attention_back(project, att, context_back)
    away, here = joint_gradient(rep, project_back, attended, normed_t, context_t)
    project_back, away, got, pieces = order((project_back, away, got, pieces))
    keep, send = halved(keep, got)
    up, send = keep[0], send[0]
    got_up = exchange(send, second_turn)
    got = exchange(away, core_turn)
    text_back = jnp.concatenate(pieces)
    text_near = exchange(text_back, core_turn)
    joint = 3 * D // parts
    token, sums = token_back(
        premix_scaling_factor,
        incoming_activations,
        total,
        project_back,
        stacked_mixing_matrix,
        (joint_bias, out_bias, gain2, shift2, up_bias, down_bias),
    )
    sums, got_up, got, text_near = order((sums, got_up, got, text_near))
    turns = [first_turn, second_turn]
    turns += [row_turn(bit) for bit in range(1, blocks.bit_length() - 1)]
    keep, send = halved(here, got)
    got = exchange(send, first_turn)
    vectors = round_of(sums, [("rep", 0), ("rep", 1)])
    up, got_up = next_turn(up, got_up, turns, 2)
    *low, other = low_rank(
        blocks,
        parts,
        gather_masks(),
        dp,
        rep,
        left,
        left_near,
        text_back,
        text_near,
        caption_mapping_matrix,
    )
    other = exchange(other, across)
    got, got_up, vectors = order((got, got_up, vectors))
    keep, send = halved(keep, got)
    mix = keep[0]
    got = exchange(send[0], second_turn)
    vectors = round_of(sum(vectors), [("dp", 0)])
    up, got_up = next_turn(up, got_up, turns, 3)
    for i in range(2, len(turns)):
        got, got_up, vectors = order((got, got_up, vectors))
        mix, got = next_turn(mix, got, turns, i)
        vectors = round_of(sum(vectors), [("dp", i - 1)])
        up, got_up = next_turn(up, got_up, turns, i + 2)
    joint_block, out_block, up_block, down_block, head_block, loss, *grads = finish(
        (mix, got), (up, got_up), vectors, loss, (*low, other), joint
    )
    return (
        loss,
        token,
        grads[0],
        grads[1],
        joint_block,
        grads[2],
        out_block,
        grads[3],
        grads[4],
        grads[5],
        up_block,
        grads[6],
        down_block.T,
        grads[7],
        head_block,
    )


def solution(mesh):
    spread = P(("dp", "rep"), None)
    line = P(("dp", "rep"))
    block = P("dp", "rep")
    in_specs = (spread, line, line, line, spread) + (P(),) * 15
    out_specs = (
        P(),
        spread,
        P(),
        P(),
        block,
        P(),
        block,
        P(),
        P(),
        P(),
        block,
        P(),
        block,
        P(),
        block,
    )
    return jax.shard_map(local, mesh=mesh, in_specs=in_specs, out_specs=out_specs, check_vma=False)
```

```python
import functools

import jax
import jax.numpy as jnp
from jax import lax
from jax.experimental import pallas as pl
from jax.experimental.pallas import tpu as pltpu
from jax.sharding import PartitionSpec as P

D = 768
HEADS = 12
HEAD = 64
SEQ = 16
FF = 3072
GROUP = 128
PAIRS = HEADS // 2
SLOT = 16
BF = jnp.bfloat16
F32 = jnp.float32

epsilon = 1e-06
negative = -1e30
scale = HEAD ** (-0.5)
LIMIT = 16 * 1024 * 1024

GAIN1, SHIFT1, JOINT, OUT, GAIN2, SHIFT2, WIDE, NARROW = 0, 768, 1536, 3840, 4608, 5376, 6144, 9216
VECTORS = 9984
LINES = VECTORS // 128
ALL_LINES = LINES + -LINES % 8

vmem = pl.BlockSpec(memory_space=pltpu.VMEM)
smem = pl.BlockSpec(memory_space=pltpu.SMEM)


def dot(a, b, dims):
    return lax.dot_general(a, b, (dims, ((), ())), preferred_element_type=F32)


def nn(a, b):
    return dot(a, b, ((1,), (0,)))


def nt(a, b):
    return dot(a, b, ((1,), (1,)))


def tn(a, b):
    return dot(a, b, ((0,), (0,)))


def cost(flops, steps, moved):
    return pl.CostEstimate(flops=flops, transcendentals=steps, bytes_accessed=moved)


def shape(*dims, dtype=F32):
    return jax.ShapeDtypeStruct(dims, dtype)


def kept(*dims, dtype=BF):
    return pltpu.VMEM(dims, dtype)


def near(*values):
    return [pltpu.with_memory_space_constraint(v, pltpu.VMEM) for v in values]


def kernel_call(name, body, results, small, operands, scratch=(), estimate=None, limit=LIMIT):
    return pl.pallas_call(
        body,
        out_shape=results,
        in_specs=[smem] * len(small) + [vmem] * len(operands),
        out_specs=[vmem] * len(results),
        scratch_shapes=[pltpu.VMEM(s, t) for s, t in scratch],
        compiler_params=pltpu.CompilerParams(vmem_limit_bytes=limit),
        cost_estimate=estimate,
        name=name,
    )(*small, *operands)


def iota(dims, axis):
    return lax.broadcasted_iota(jnp.int32, dims, axis)


def norm_parts(values):
    average = jnp.mean(values, axis=-1, keepdims=True)
    centred = values - average
    inverse = lax.rsqrt(jnp.mean(centred * centred, axis=-1, keepdims=True) + epsilon)
    return centred * inverse, inverse


def norm_back(unit, inverse, gain, back):
    inner = back * gain
    part = inverse * (
        inner
        - jnp.mean(inner, axis=-1, keepdims=True)
        - unit * jnp.mean(inner * unit, axis=-1, keepdims=True)
    )
    return part, jnp.sum(back * unit, axis=0, keepdims=True), jnp.sum(back, axis=0, keepdims=True)


def split(value):
    high = value.astype(BF)
    return high, (value - high.astype(F32)).astype(BF)


def two(value):
    return jnp.concatenate(split(value), axis=0)


def as_row(ref):
    return ref[...].reshape(1, ref.shape[0])


def as_column(ref):
    size = ref.shape[0]
    same = iota((size, size), 0) == iota((size, size), 1)
    row = as_row(ref)
    return jnp.sum(jnp.where(same, row, jnp.zeros_like(row)), axis=1, keepdims=True)


def token_limits(ref):
    place = as_row(ref).astype(F32)
    captions = place.shape[1]
    tokens = captions * SEQ
    owner = (iota((tokens, captions), 0) // SEQ == iota((tokens, captions), 1)).astype(F32)
    column = jnp.sum(owner * place, axis=1, keepdims=True)
    line = nt(place.astype(BF), owner.astype(BF))
    return line, column


def pool_mask(line, captions):
    dims = (captions, captions * SEQ)
    token = iota(dims, 1)
    inside = (token % SEQ).astype(F32) <= line
    return jnp.where((token // SEQ == iota(dims, 0)) & inside, 1.0, 0.0)


def spread_mask(column, captions):
    dims = (captions * SEQ, captions)
    token = iota(dims, 0)
    inside = (token % SEQ).astype(F32) <= column
    return jnp.where((token // SEQ == iota(dims, 1)) & inside, 1.0, 0.0)


def head_masks():
    lane = iota((1, 2 * HEAD), 1)
    even = (lane < HEAD).astype(F32)
    return even.astype(BF), (1.0 - even).astype(BF)


def caption_masks():
    lane = iota((SEQ, GROUP), 1) // SEQ
    return [lane == c for c in range(GROUP // SEQ)]


def compact(full, picks):
    out = full[:SEQ]
    for c in range(1, len(picks)):
        out = jnp.where(picks[c], full[c * SEQ : (c + 1) * SEQ], out)
    return out


def expand(low, lows):
    return jnp.concatenate([low * mask for mask in lows], axis=0)


def both_heads(value, masks):
    return jnp.concatenate([value * masks[0], value * masks[1]], axis=0)


def store_permuted(ref, value, dp, blocks):
    rows = value.shape[0] // blocks
    bits = blocks.bit_length() - 1
    if rows % SLOT:
        ref[...] = value
        return
    for b in range(blocks):
        k = jnp.bitwise_xor(dp, b)
        place = 0
        for bit in range(bits):
            place = place + ((k >> bit) & 1) * (1 << (bits - 1 - bit))
        ref[pl.ds(pl.multiple_of(place * rows, SLOT), rows), :] = value[b * rows : (b + 1) * rows]


def box_width(blocks):
    used = (FF + D) // blocks
    return used + -used % 128


def project_kernel(
    blocks, gain_ref, shift_ref, joint_ref, x_ref, wj_ref, project_ref, normed_ref, normed
):
    unit, _ = norm_parts(x_ref[...].astype(F32))
    normed[...] = (unit * as_row(gain_ref) + as_row(shift_ref)).astype(BF)
    joint = as_row(joint_ref)
    for i, bias in enumerate((joint[:, :D], 0.0, joint[:, D:])):
        lanes = slice(i * D, (i + 1) * D)
        project_ref[:, lanes] = (nn(normed[...], wj_ref[:, lanes]) + bias).astype(BF)
    store_permuted(normed_ref, normed[...].T, lax.axis_index("dp"), blocks)


def project_tokens(blocks, gain, shift, joint, x, wj):
    tokens = x.shape[0]
    return kernel_call(
        "project_tokens",
        functools.partial(project_kernel, blocks),
        [kept(tokens, 3 * D), kept(D, tokens)],
        (),
        (gain, shift, joint, *near(x, wj)),
        [((tokens, D), BF)],
        cost(6 * tokens * D * D, 0, 8 * D * D),
    )


def attend_kernel(
    blocks,
    place_ref,
    out_ref,
    x_ref,
    project_ref,
    wo_ref,
    att_ref,
    context_t_ref,
    middle_ref,
    context,
):
    line, _ = token_limits(place_ref)
    masks = head_masks()
    picks = caption_masks()
    lows = [pick.astype(F32).astype(BF) for pick in picks]
    key_place = iota((SEQ, GROUP), 0).astype(F32)

    def attend(h, carry):
        at = pl.multiple_of(h * 2 * HEAD, 128)
        for g in range(x_ref.shape[0] // GROUP):
            here = slice(g * GROUP, (g + 1) * GROUP)
            query = project_ref[here, pl.ds(at, 128)]
            keys = both_heads(project_ref[here, pl.ds(pl.multiple_of(D + at, 128), 128)], masks)
            values = both_heads(
                project_ref[here, pl.ds(pl.multiple_of(2 * D + at, 128), 128)], masks
            )
            scores = nt(keys, query)
            allowed = key_place <= line[:, here]
            parts = []
            for e in range(2):
                score = compact(scores[e * GROUP : (e + 1) * GROUP], picks) * scale
                score = jnp.where(allowed, score, negative)
                score = jnp.exp(score - jnp.max(score, axis=0, keepdims=True))
                weight = score / jnp.sum(score, axis=0, keepdims=True)
                att_ref[2 * h + e, :, here] = weight
                parts.append(expand(weight.astype(BF), lows))
            context[here, pl.ds(at, 128)] = tn(jnp.concatenate(parts, axis=0), values).astype(BF)
        return carry

    lax.fori_loop(0, PAIRS, attend, 0)
    middle_ref[...] = x_ref[...].astype(F32) + (nn(context[...], wo_ref[...]) + as_row(out_ref))
    store_permuted(context_t_ref, context[...].T, lax.axis_index("dp"), blocks)


def attend_tokens(blocks, place, out, x, project, wo):
    tokens = x.shape[0]
    return kernel_call(
        "attend_tokens",
        functools.partial(attend_kernel, blocks),
        [kept(HEADS, SEQ, tokens, dtype=F32), kept(D, tokens), kept(tokens, D, dtype=F32)],
        (),
        (place, out, *near(x, project, wo)),
        [((tokens, D), BF)],
        cost(8 * tokens * D * D, 0, 8 * D * D),
    )


def widen_kernel(
    blocks,
    place_ref,
    gain_ref,
    shift_ref,
    wide_ref,
    narrow_ref,
    middle_ref,
    wu_ref,
    wn_ref,
    wm_ref,
    second_t_ref,
    slope_ref,
    box_ref,
    text_ref,
    scale_ref,
    embed_ref,
    second,
    branch,
    wide,
    mean,
):
    captions = place_ref.shape[0]
    line, column = token_limits(place_ref)
    pool = pool_mask(line, captions)
    share = 1.0 / jnp.sum(pool, axis=1, keepdims=True)
    unit, _ = norm_parts(middle_ref[...])
    second[...] = (unit * as_row(gain_ref) + as_row(shift_ref)).astype(BF)
    store_permuted(second_t_ref, second[...].T, lax.axis_index("dp"), blocks)
    branch[...] = jnp.zeros_like(branch)
    wide[...] = as_row(wide_ref)
    pool_low = pool.astype(BF)
    c0 = 0.7978845608028654
    c1 = c0 * 0.044715
    step = 512

    def widen(i, carry):
        at = pl.multiple_of(i * step, 128)
        upper = nn(second[...], wu_ref[:, pl.ds(at, step)]) + wide[:, pl.ds(at, step)]
        square = upper * upper
        bend = jnp.tanh(upper * (c0 + c1 * square))
        half = 0.5 + 0.5 * bend
        active = (upper * half).astype(BF)
        slope_ref[:, pl.ds(at, step)] = (
            half + (0.5 * upper) * (1.0 - bend * bend) * (c0 + 3.0 * c1 * square)
        ).astype(BF)
        parts = two(nn(pool_low, active) * share)
        mean[:, pl.ds(at, step)] = parts[:captions]
        branch[...] += nn(parts, wn_ref[pl.ds(at, step), :])
        return carry

    lax.fori_loop(0, FF // step, widen, 0)
    inside = jnp.where((iota((captions * SEQ, 1), 0) % SEQ).astype(F32) <= column, 1.0, 0.0)
    weight = inside / (column + 1.0)
    pooled = jnp.sum((middle_ref[...] * weight).reshape(captions, SEQ, D), axis=1)
    pooled = (pooled + (branch[:captions] + branch[captions:] + as_row(narrow_ref))).astype(BF)
    hidden, part = FF // blocks, D // blocks
    for b in range(blocks):
        box_ref[b, :, :hidden] = mean[:, b * hidden : (b + 1) * hidden]
        box_ref[b, :, hidden : hidden + part] = pooled[:, b * part : (b + 1) * part]
    text = nn(pooled, wm_ref[...])
    factor = lax.rsqrt(jnp.sum(text * text, axis=1, keepdims=True) + epsilon)
    text_ref[...] = text
    scale_ref[...] = factor
    embed_ref[...] = (text * factor).astype(BF)


def widen_tokens(blocks, place, gain, shift, wide, narrow, middle, wu, wn, wm):
    tokens = middle.shape[0]
    captions = place.shape[0]
    return kernel_call(
        "widen_tokens",
        functools.partial(widen_kernel, blocks),
        [
            kept(D, tokens),
            kept(tokens, FF),
            kept(blocks, captions, box_width(blocks)),
            kept(captions, D, dtype=F32),
            kept(captions, 1, dtype=F32),
            kept(captions, D),
        ],
        (),
        (place, gain, shift, wide, narrow, *near(middle, wu, wn, wm)),
        [
            ((tokens, D), BF),
            ((2 * captions, D), F32),
            ((1, FF), F32),
            ((captions, FF), BF),
        ],
        cost(3 * tokens * D * FF, tokens * FF, 8 * D * FF),
    )


def match_of(paired, columns, images):
    column = iota((1, columns), 1)
    valid = column % SLOT < images
    name = jnp.where(valid, (column // SLOT) * images + column % SLOT, -1)
    return paired == name, valid


def contrast_kernel(
    images,
    parts,
    bits,
    heat_ref,
    own_ref,
    near_ref,
    wp_ref,
    embed_ref,
    paired_ref,
    weight_ref,
    picture_ref,
    score_ref,
    row_ref,
    inverse_ref,
    stats_ref,
    features,
):
    half = own_ref.shape[0] // SLOT
    for far, ref in enumerate((own_ref, near_ref)):

        def place(i, carry, far=far, ref=ref):
            p = i + far * half
            index = {axis: lax.axis_index(axis) for axis in ("dp", "rep")}
            for n, (axis, bit) in enumerate(bits):
                index[axis] = jnp.bitwise_xor(index[axis], ((p >> n) & 1) << bit)
            to = pl.ds(pl.multiple_of((index["dp"] * parts + index["rep"]) * SLOT, SLOT), SLOT)
            features[to, :] = ref[pl.ds(pl.multiple_of(i * SLOT, SLOT), SLOT), :]
            return carry

        lax.fori_loop(0, half, place, 0, unroll=4)
    picture = nn(features[...], wp_ref[...])
    picture = (
        picture * lax.rsqrt(jnp.sum(picture * picture, axis=1, keepdims=True) + epsilon)
    ).astype(BF)
    picture_ref[...] = picture
    score = nt(embed_ref[...], picture) / heat_ref[0]
    match, valid = match_of(as_column(paired_ref), score.shape[1], images)
    score = jnp.where(valid, score, negative)
    score_ref[...] = score
    top = jnp.max(score, axis=1, keepdims=True)
    row = jnp.log(jnp.sum(jnp.exp(score - top), axis=1, keepdims=True)) + top
    row_ref[...] = row
    positive = jnp.sum(jnp.where(match, score, 0.0), axis=1, keepdims=True)
    hits = jnp.where(match, 1.0, 0.0)
    counts = jnp.sum(hits, axis=0, keepdims=True)
    inverse = 1.0 / jnp.sum(hits * counts, axis=1, keepdims=True)
    inverse_ref[...] = inverse
    total = jnp.sum(as_column(weight_ref) * (row - positive - positive * inverse))
    best = jnp.max(score, axis=0, keepdims=True)
    mass = jnp.sum(jnp.exp(score - best), axis=0, keepdims=True)
    mass = jnp.where(iota(mass.shape, 1) == images, total, mass)
    wide = best.shape[1] // 4
    rows = [v[:, i * wide : (i + 1) * wide] for v in (best, mass) for i in range(4)]
    stats_ref[...] = jnp.concatenate(rows, axis=0)


def contrast(images, parts, bits, heat, own, far, wp, embed, paired, weight):
    captions = embed.shape[0]
    columns = 2 * own.shape[0]
    return kernel_call(
        "contrast",
        functools.partial(contrast_kernel, images, parts, bits),
        [
            kept(columns, D),
            kept(captions, columns, dtype=F32),
            kept(captions, 1, dtype=F32),
            kept(captions, 1, dtype=F32),
            shape(8, columns // 4),
        ],
        (heat,),
        (*near(own, far, wp, embed), paired, weight),
        [((columns, D), BF)],
        cost(4 * columns * D * D, columns * captions, 8 * columns * D),
        max(LIMIT, columns * 8192),
    )


def merged(refs):
    best = functools.reduce(jnp.maximum, [ref[:4] for ref in refs])
    mass = sum(ref[4:] * jnp.exp(ref[:4] - best) for ref in refs)
    return best, mass


def merge_kernel(*refs):
    *given, out_ref = refs
    best, mass = merged(given)
    out_ref[...] = jnp.concatenate([best, mass], axis=0)


def merge(stats):
    return kernel_call("merge", merge_kernel, [shape(*stats[0].shape)], (), stats)[0]


def quarters(rep, away):
    core = rep & 1
    out = []
    for xrel in range(2):
        for yrel in range(2):
            block = jnp.bitwise_xor(rep, 2 * xrel + away)
            x_first = 1 - core if away == 0 else core
            out.append((jnp.where(x_first == 1, 2 * xrel + yrel, 2 * yrel + xrel), block, yrel))
    return out


def head_back_kernel(
    images,
    count_stats,
    rounds,
    heat_ref,
    place_ref,
    score_ref,
    row_ref,
    inverse_ref,
    weight_ref,
    paired_ref,
    picture_ref,
    text_ref,
    scale_ref,
    wm_ref,
    wn_ref,
    slope_ref,
    second_t_ref,
    box_ref,
    *refs,
):
    first = 1 << rounds[0]
    pieces = refs[len(refs) - first :]
    stats = refs[:count_stats]
    (
        back_ref,
        away_ref,
        here_ref,
        pooled_ref,
        loss_ref,
        down_bias_ref,
        up_bias_ref,
    ) = refs[count_stats : len(refs) - first]
    rep = lax.axis_index("rep")
    heat = heat_ref[0]
    captions = place_ref.shape[0]
    line, column = token_limits(place_ref)
    count = jnp.sum(pool_mask(line, captions), axis=1, keepdims=True)
    owner = spread_mask(column, captions).astype(BF)
    owner = jnp.concatenate([owner, owner], axis=1)

    score = score_ref[...]
    match, valid = match_of(as_column(paired_ref), score.shape[1], images)
    best, mass = merged(stats)
    column_log = jnp.log(mass) + best
    column_log = jnp.concatenate([column_log[i : i + 1] for i in range(4)], axis=1)
    loss_ref[...] = mass[:1, images : images + 1] + jnp.sum(
        jnp.where(valid, column_log, 0.0), axis=1, keepdims=True
    )
    weight = as_column(weight_ref)
    graded = (
        weight * jnp.exp(score - row_ref[...])
        + jnp.exp(score - column_log)
        - jnp.where(match, weight * (1.0 + inverse_ref[...]), 0.0)
    )
    graded = jnp.where(valid, graded / heat, 0.0).astype(BF)
    embed_back = nn(graded, picture_ref[...])
    text = text_ref[...]
    factor = scale_ref[...]
    text_dot = jnp.sum(text * embed_back, axis=1, keepdims=True)
    text_back = (factor * embed_back - text * (factor * factor * factor) * text_dot).astype(BF)
    blocks, _, wide = box_ref.shape
    masks = gather_masks(rounds, blocks)
    for c, piece_ref in enumerate(pieces):
        for i in range(blocks // first):
            block = jnp.bitwise_xor(lax.axis_index("dp"), masks[i * first + c])
            piece_ref[:, i * wide : (i + 1) * wide] = box_ref[block]
        piece_ref[:, (blocks // first) * wide :] = text_back
    pooled_back = nt(text_back, wm_ref[...])
    pooled_ref[...] = pooled_back
    branch = (pooled_back / count).astype(BF)
    down_bias_ref[...] = jnp.sum(branch.astype(F32) * count, axis=0, keepdims=True)
    ones = jnp.ones((SLOT, back_ref.shape[0]), BF)
    step = 512

    def widen(i, carry):
        at = pl.multiple_of(i * step, 128)
        part = nn(owner, two(nt(branch, wn_ref[pl.ds(at, step), :])))
        part = (part * slope_ref[:, pl.ds(at, step)].astype(F32)).astype(BF)
        back_ref[:, pl.ds(at, step)] = part
        up_bias_ref[:, pl.ds(at, step)] = nn(ones, part)[:1]
        return carry

    lax.fori_loop(0, FF // step, widen, 0)
    half = second_t_ref.shape[0] // 2
    wide = FF // 4
    for turn, target in enumerate((away_ref, here_ref)):
        for place, block, yrel in quarters(rep, 1 - turn):
            part = nn(
                second_t_ref[yrel * half : (yrel + 1) * half],
                back_ref[:, pl.ds(pl.multiple_of(block * wide, 128), wide)],
            )
            target[place] = part.astype(BF)


def head_back(images, rounds, heat, place, stats, score, row, inverse, weight, paired, picture, text,
              factor, wm, wn, slope, second_t, box):
    captions = text.shape[0]
    tokens = slope.shape[0]
    piece = (4, D // 2, FF // 4)
    return kernel_call(
        "head_back",
        functools.partial(head_back_kernel, images, len(stats), rounds),
        [
            kept(tokens, FF),
            kept(*piece),
            kept(*piece),
            kept(captions, D, dtype=F32),
            shape(1, 1),
            shape(1, D),
            shape(1, FF),
        ]
        + [shape(captions, (box.shape[0] >> rounds[0]) * box.shape[2] + D, dtype=BF)] * (1 << rounds[0]),
        (heat,),
        (
            place,
            *near(score, row, inverse),
            weight,
            paired,
            *near(picture, text, factor, wm, wn, slope, second_t, box),
            *stats,
        ),
        (),
        cost(6 * tokens * D * FF, captions * FF, 24 * D * FF),
    )


def middle_back_kernel(
    place_ref,
    gain_ref,
    pooled_ref,
    back_ref,
    wu_ref,
    middle_ref,
    wo_ref,
    total_ref,
    attended_ref,
    context_back_ref,
    gain_back_ref,
    shift_back_ref,
    bias_ref,
):
    captions = place_ref.shape[0]
    line, column = token_limits(place_ref)
    count = jnp.sum(pool_mask(line, captions), axis=1, keepdims=True)
    owner = spread_mask(column, captions).astype(BF)
    owner = jnp.concatenate([owner, owner], axis=1)
    second_back = nt(back_ref[...], wu_ref[...])
    unit, inverse = norm_parts(middle_ref[...])
    part, gain_back_ref[...], shift_back_ref[...] = norm_back(
        unit, inverse, as_row(gain_ref), second_back
    )
    total = nn(owner, two(pooled_ref[...] / count)) + part
    total_ref[...] = total
    attended = total.astype(BF)
    attended_ref[...] = attended
    bias_ref[...] = nn(jnp.ones((SLOT, attended.shape[0]), BF), attended)[:1]
    context_back_ref[...] = nt(attended, wo_ref[...]).astype(BF)


def middle_back(place, gain, pooled, back, wu, middle, wo):
    tokens = back.shape[0]
    return kernel_call(
        "middle_back",
        middle_back_kernel,
        [
            kept(tokens, D, dtype=F32),
            kept(tokens, D),
            kept(tokens, D),
            shape(1, D),
            shape(1, D),
            shape(1, D),
        ],
        (),
        (place, gain, *near(pooled, back, wu, middle, wo)),
        (),
        cost(4 * tokens * D * FF, 0, 12 * D * FF),
    )


def attention_back_kernel(project_ref, att_ref, context_back_ref, back_ref, bias_ref):
    masks = head_masks()
    picks = caption_masks()
    lows = [pick.astype(F32).astype(BF) for pick in picks]
    low_scale = jnp.asarray(scale, BF)
    first = iota((GROUP, 2 * HEAD), 1) < HEAD
    tokens = project_ref.shape[0]

    def attend(h, carry):
        at = pl.multiple_of(h * 2 * HEAD, 128)
        at_k = pl.multiple_of(D + at, 128)
        at_v = pl.multiple_of(2 * D + at, 128)
        for g in range(tokens // GROUP):
            span = slice(g * GROUP, (g + 1) * GROUP)
            query = project_ref[span, pl.ds(at, 128)]
            keys = both_heads(project_ref[span, pl.ds(at_k, 128)], masks)
            values = both_heads(project_ref[span, pl.ds(at_v, 128)], masks)
            upper = context_back_ref[span, pl.ds(at, 128)]
            full = nt(values, upper)
            weights, grads = [], []
            for e in range(2):
                weight = att_ref[2 * h + e, :, span]
                part = compact(full[e * GROUP : (e + 1) * GROUP], picks)
                grad = weight * (part - jnp.sum(weight * part, axis=0, keepdims=True))
                weights.append(expand(weight.astype(BF), lows))
                grads.append(expand(grad.astype(BF) * low_scale, lows))
            weights = jnp.concatenate(weights, axis=0)
            grads = jnp.concatenate(grads, axis=0)
            back_ref[span, pl.ds(at, 128)] = tn(grads, keys).astype(BF)
            wide = nn(grads, query)
            back_ref[span, pl.ds(at_k, 128)] = jnp.where(first, wide[:GROUP], wide[GROUP:]).astype(
                BF
            )
            wide = nn(weights, upper)
            back_ref[span, pl.ds(at_v, 128)] = jnp.where(first, wide[:GROUP], wide[GROUP:]).astype(
                BF
            )
        return carry

    lax.fori_loop(0, PAIRS, attend, 0)
    ones = jnp.ones((SLOT, tokens), BF)
    for i in range(3):
        lanes = slice(i * D, (i + 1) * D)
        bias_ref[:, lanes] = nn(ones, back_ref[:, lanes])[:1]


def attention_back(project, att, context_back):
    tokens = project.shape[0]
    return kernel_call(
        "attention_back",
        attention_back_kernel,
        [kept(tokens, 3 * D), shape(1, 3 * D)],
        (),
        near(project, att, context_back),
        (),
        cost(5 * tokens * D * FF, 0, 12 * D * FF),
    )


def joint_gradient_kernel(
    back_ref, attended_ref, normed_t_ref, context_t_ref, away_ref, here_ref, chosen
):
    rep = lax.axis_index("rep")
    joint = 3 * D // 4
    out = D // 4
    for r in range(4):

        @pl.when(rep == r)
        def _():
            for i, k in enumerate((1, 3, 0, 2)):
                b = r ^ k
                chosen[i, :, :joint] = back_ref[:, b * joint : (b + 1) * joint]
                chosen[i, :, joint:] = attended_ref[:, b * out : (b + 1) * out]

    half = D // 2
    for turn, target in enumerate((away_ref, here_ref)):
        for i, (place, _, yrel) in enumerate(quarters(rep, 1 - turn)):
            block = 2 * turn + i // 2
            lines = slice(yrel * half, (yrel + 1) * half)
            target[place, :, :joint] = nn(normed_t_ref[lines], chosen[block, :, :joint]).astype(BF)
            target[place, :, joint:] = nn(context_t_ref[lines], chosen[block, :, joint:]).astype(BF)


def joint_gradient(back, attended, normed_t, context_t):
    tokens = back.shape[0]
    piece = (4, D // 2, D)
    return kernel_call(
        "joint_gradient",
        joint_gradient_kernel,
        [kept(*piece), kept(*piece)],
        (),
        near(back, attended, normed_t, context_t),
        [((4, tokens, D), BF)],
        cost(3 * tokens * D * FF, 0, 12 * D * FF),
    )


def token_back_kernel(
    gain_ref,
    x_ref,
    middle_ref,
    back_ref,
    wj_ref,
    joint_ref,
    out_ref,
    gain2_ref,
    shift2_ref,
    wide_ref,
    narrow_ref,
    token_ref,
    sums_ref,
):
    unit, inverse = norm_parts(x_ref[...].astype(F32))
    part, gain1, shift1 = norm_back(unit, inverse, as_row(gain_ref), nt(back_ref[...], wj_ref[...]))
    token_ref[...] = middle_ref[...] + part
    line = 0
    rest = (joint_ref, out_ref, gain2_ref, shift2_ref, wide_ref, narrow_ref)
    for value in [gain1, shift1] + [ref[...] for ref in rest]:
        for i in range(value.shape[1] // 128):
            sums_ref[line : line + 1] = value[:, i * 128 : (i + 1) * 128]
            line += 1
    sums_ref[line:] = jnp.zeros((sums_ref.shape[0] - line, 128), F32)


def token_back(gain, x, middle, back, wj, sums):
    return kernel_call(
        "token_back",
        token_back_kernel,
        [shape(x.shape[0], D), shape(ALL_LINES, 128)],
        (),
        (gain, *near(x, middle, back, wj), *sums),
        (),
        cost(2 * x.shape[0] * D * FF, 0, 8 * D * FF),
    )


def low_rank_kernel(
    hidden, own_ref, near_ref, wm_ref, down_ref, head_ref, other_ref, box, back
):
    rows = own_ref.shape[0]
    box[:rows] = own_ref[...]
    box[rows:] = near_ref[...]
    part = down_ref.shape[0]
    start = box.shape[1] - D
    rep = lax.axis_index("rep")
    for r in range(D // part):

        @pl.when(rep == r)
        def _():
            for i, b in enumerate((r, r ^ 2)):
                back[i] = box[:, start + b * part : start + (b + 1) * part]

    wide = head_ref.shape[1]
    for i in range(2):
        block = jnp.bitwise_xor(rep, 2 * i)
        here = wm_ref[pl.ds(pl.multiple_of(block * part, SLOT), part), :]
        pooled = nt(box[:, start:], here).astype(BF)
        down = tn(pooled, box[:, :hidden])
        head = tn(back[i], box[:, hidden : hidden + wide])
        if i == 0:
            down_ref[...] = down
            head_ref[...] = head
        else:
            other_ref[:, :hidden] = down.astype(BF)
            other_ref[:, hidden:] = head.astype(BF)


def low_rank(blocks, parts, own, far, wm):
    rows = 2 * own.shape[0]
    hidden, wide, part = FF // blocks, D // blocks, D // parts
    return kernel_call(
        "low_rank",
        functools.partial(low_rank_kernel, hidden),
        [shape(part, hidden), shape(part, wide), shape(part, hidden + wide, dtype=BF)],
        (),
        near(own, far, wm),
        [((rows, own.shape[1]), BF), ((2, rows, part), BF)],
        cost(8 * rows * D * D, 0, 4 * rows * D),
    )


def finish_kernel(
    mix_ref,
    mix_got_ref,
    up_ref,
    up_got_ref,
    sums_ref,
    sums_got_ref,
    loss_ref,
    down_ref,
    head_ref,
    other_ref,
    joint_ref,
    out_ref,
    up_block_ref,
    down_block_ref,
    head_block_ref,
    loss_out_ref,
    *vector_refs,
):
    total = mix_ref[...].astype(F32) + mix_got_ref[...].astype(F32)
    wide = joint_ref.shape[1]
    joint_ref[...] = total[:, :wide]
    out_ref[...] = total[:, wide:]
    up_block_ref[...] = up_ref[...].astype(F32) + up_got_ref[...].astype(F32)
    hidden = down_ref.shape[1]
    down_block_ref[...] = down_ref[...] + other_ref[:, :hidden].astype(F32)
    head_block_ref[...] = (head_ref[...] + other_ref[:, hidden:].astype(F32)).T
    loss_out_ref[...] = loss_ref[...].reshape(1)
    starts = (GAIN1, SHIFT1, JOINT, OUT, GAIN2, SHIFT2, WIDE, NARROW)
    for start, ref in zip(starts, vector_refs):
        for i in range(ref.shape[0] // 128):
            line = start // 128 + i
            if start == JOINT and i >= D // 128:
                line += D // 128
            ref[pl.ds(i * 128, 128)] = sums_ref[line] + sums_got_ref[line]


def finish(mix, up, sums, loss, low, joint):
    rows = mix[0].shape[0]
    sizes = (D, D, 2 * D, D, D, D, FF, D)
    return kernel_call(
        "finish",
        finish_kernel,
        [
            shape(rows, joint),
            shape(rows, D - joint),
            shape(rows, D),
            shape(*low[0].shape),
            shape(*low[1].shape[::-1]),
            shape(1),
        ]
        + [shape(n) for n in sizes],
        (),
        (*mix, *up, *sums, loss, *low),
    )


def both_pairs(partner):
    dp, rep = lax.axis_size("dp"), lax.axis_size("rep")
    pairs = []
    for i in range(dp):
        for j in range(rep):
            a, b = partner(i, j)
            pairs.append((i * rep + j, a * rep + b))
    return pairs


def exchange(value, partner):
    return lax.ppermute(value, ("dp", "rep"), both_pairs(partner))


def first_turn(i, j):
    return (i, j ^ 2) if j & 1 == 0 else (i ^ 1, j)


def second_turn(i, j):
    return (i ^ 1, j) if j & 1 == 0 else (i, j ^ 2)


def added(a, b):
    return (a.astype(F32) + b.astype(F32)).astype(BF)


def halved(here, got):
    half = here.shape[0] // 2
    return added(here[:half], got[:half]), added(here[half:], got[half:])


def core_turn(i, j):
    return i, j ^ 1


def across(i, j):
    return i, j ^ 2


def row_turn(bit):
    return lambda i, j: (i ^ (1 << bit), j)


def next_turn(keep, got, turns, i):
    if i >= len(turns):
        return keep, got
    keep, send = halved(keep, got)
    return keep, exchange(send, turns[i])


order = lax.optimization_barrier


def dp_groups():
    bits = [("dp", b) for b in range(1, lax.axis_size("dp").bit_length() - 1)]
    return [bits[i : i + 2] for i in range(0, len(bits), 2)] + [[("dp", 0)]]


def all_groups():
    bits = [("rep", b) for b in range(1, lax.axis_size("rep").bit_length() - 1)]
    groups = dp_groups()
    return groups[:-1] + [groups[-1] + bits, [("rep", 0)]]


def group_masks(group):
    out = [(0, 0)]
    for axis, bit in group:
        out += [(a | 1 << bit, b) if axis == "dp" else (a, b | 1 << bit) for a, b in out]
    return out


def gather_masks(rounds, blocks):
    bits = list(range(1, blocks.bit_length() - 1)) + [0]
    masks, used = [0], 0
    for count in rounds:
        for bit in bits[used : used + count]:
            masks = masks + [m | 1 << bit for m in masks]
        used += count
    return masks


def split_round(value, wide, group):
    blocks = (value.shape[1] - D) // wide
    turns = group_masks(group)
    text = value[:, blocks * wide :]
    pieces = []
    for c, (a, b) in enumerate(turns):
        chosen = [value[:, i * wide : (i + 1) * wide] for i in range(c, blocks, len(turns))]
        piece = jnp.concatenate(chosen + [text], axis=1)
        pieces.append(piece if c == 0 else exchange(piece, lambda i, j: (i ^ a, j ^ b)))
    return jnp.concatenate(pieces)


def round_of(value, group):
    return [value] + [
        exchange(value, lambda i, j: (i ^ a, j ^ b)) for a, b in group_masks(group)[1:]
    ]


def relative_rows(value, blocks):
    rows = value.shape[0] // blocks
    if rows % SLOT == 0:
        return value
    bits = blocks.bit_length() - 1
    place = jnp.arange(blocks, dtype=jnp.int32)
    source = jnp.zeros_like(place)
    for bit in range(bits):
        source = source + ((place >> (bits - 1 - bit)) & 1) * (1 << bit)
    source = source ^ lax.axis_index("dp")
    return value.reshape(blocks, rows, -1)[source].reshape(value.shape)


def local(
    incoming_activations,
    caption_final_place,
    paired_picture,
    caption_weight,
    locked_picture_features,
    softmax_heat,
    premix_scaling_factor,
    premix_shift_term,
    stacked_mixing_matrix,
    asking_reading_offsets,
    mixing_result_matrix,
    mixing_result_offset,
    premlp_scaling_factor,
    premlp_shift_term,
    widening_matrix,
    widening_offset,
    narrowing_matrix,
    narrowing_offset,
    caption_mapping_matrix,
    picture_mapping_matrix,
):
    both = ("dp", "rep")
    devices = lax.axis_size(both)
    blocks = lax.axis_size("dp")
    parts = lax.axis_size("rep")
    captions = caption_final_place.shape[0]
    images = locked_picture_features.shape[0]
    groups = all_groups()
    pieces = round_of(jnp.pad(locked_picture_features, ((0, SLOT - images), (0, 0))), groups[0])
    project, normed_t = project_tokens(
        blocks,
        premix_scaling_factor,
        premix_shift_term,
        asking_reading_offsets,
        incoming_activations,
        stacked_mixing_matrix,
    )
    project, pieces = order((project, pieces))
    for group in groups[1:-1]:
        pieces = round_of(jnp.concatenate(pieces), group)
    att, context_t, middle = attend_tokens(
        blocks,
        caption_final_place,
        mixing_result_offset,
        incoming_activations,
        project,
        mixing_result_matrix,
    )
    middle, pieces = order((middle, pieces))
    own, far = round_of(jnp.concatenate(pieces), groups[-1])
    second_t, slope, box, text, factor, embed = widen_tokens(
        blocks,
        caption_final_place,
        premlp_scaling_factor,
        premlp_shift_term,
        widening_offset,
        narrowing_offset,
        middle,
        widening_matrix,
        narrowing_matrix,
        caption_mapping_matrix,
    )
    normed_t, context_t, second_t = (
        relative_rows(v, blocks) for v in (normed_t, context_t, second_t)
    )
    embed, far = order((embed, far))
    picture, score, row, inverse, stats = contrast(
        images,
        parts,
        sum(groups, []),
        softmax_heat,
        own,
        far,
        picture_mapping_matrix,
        embed,
        paired_picture,
        caption_weight,
    )
    groups = dp_groups()
    stats = round_of(stats, [("rep", 0), ("rep", 1)] + groups[-1])
    for group in groups[:-1]:
        stats = round_of(merge(stats), group)
    back, away, here, pooled_back, loss, down_bias, up_bias, *pieces = head_back(
        images,
        [len(group) for group in groups],
        softmax_heat,
        caption_final_place,
        stats,
        score,
        row,
        inverse,
        caption_weight,
        paired_picture,
        picture,
        text,
        factor,
        caption_mapping_matrix,
        narrowing_matrix,
        slope,
        second_t,
        box,
    )
    loss = loss / (captions * devices)
    got = exchange(away, core_turn)
    pieces = pieces[:1] + [
        exchange(piece, lambda i, j: (i ^ a, j ^ b))
        for piece, (a, b) in zip(pieces[1:], group_masks(groups[0])[1:])
    ]
    total, attended, context_back, gain2, shift2, out_bias = middle_back(
        caption_final_place,
        premlp_scaling_factor,
        pooled_back,
        back,
        widening_matrix,
        middle,
        mixing_result_matrix,
    )
    context_back, got, pieces = order((context_back, got, pieces))
    keep, send = halved(here, got)
    got = exchange(send, first_turn)
    factors = jnp.concatenate(pieces)
    for group in groups[1:]:
        factors = split_round(factors, box.shape[2], group)
    project_back, joint_bias = attention_back(project, att, context_back)
    away, here = joint_gradient(project_back, attended, normed_t, context_t)
    project_back, away, got, factors = order((project_back, away, got, factors))
    keep, send = halved(keep, got)
    up, send = keep[0], send[0]
    got_up = exchange(send, second_turn)
    got = exchange(away, core_turn)
    far = exchange(factors, core_turn)
    joint = 3 * D // parts
    token, sums = token_back(
        premix_scaling_factor,
        incoming_activations,
        total,
        project_back,
        stacked_mixing_matrix,
        (joint_bias, out_bias, gain2, shift2, up_bias, down_bias),
    )
    sums, got_up, got, far = order((sums, got_up, got, far))
    turns = [first_turn, second_turn]
    turns += [row_turn(bit) for bit in range(1, blocks.bit_length() - 1)]
    keep, send = halved(here, got)
    got = exchange(send, first_turn)
    vectors = round_of(sums, [("rep", 0), ("rep", 1)])
    up, got_up = next_turn(up, got_up, turns, 2)
    *low, other = low_rank(blocks, parts, factors, far, caption_mapping_matrix)
    other = exchange(other, across)
    got, got_up, vectors = order((got, got_up, vectors))
    keep, send = halved(keep, got)
    mix = keep[0]
    got = exchange(send[0], second_turn)
    vectors = round_of(sum(vectors), [("dp", 0)])
    up, got_up = next_turn(up, got_up, turns, 3)
    for i in range(2, len(turns)):
        got, got_up, vectors = order((got, got_up, vectors))
        mix, got = next_turn(mix, got, turns, i)
        vectors = round_of(sum(vectors), [("dp", i - 1)])
        up, got_up = next_turn(up, got_up, turns, i + 2)
    joint_block, out_block, up_block, down_block, head_block, loss, *grads = finish(
        (mix, got), (up, got_up), vectors, loss, (*low, other), joint
    )
    return (
        loss,
        token,
        grads[0],
        grads[1],
        joint_block,
        grads[2],
        out_block,
        grads[3],
        grads[4],
        grads[5],
        up_block,
        grads[6],
        down_block.T,
        grads[7],
        head_block,
    )


def solution(mesh):
    spread = P(("dp", "rep"), None)
    line = P(("dp", "rep"))
    block = P("dp", "rep")
    in_specs = (spread, line, line, line, spread) + (P(),) * 15
    out_specs = (
        P(),
        spread,
        P(),
        P(),
        block,
        P(),
        block,
        P(),
        P(),
        P(),
        block,
        P(),
        block,
        P(),
        block,
    )
    return jax.shard_map(local, mesh=mesh, in_specs=in_specs, out_specs=out_specs, check_vma=False)
```

```python
import functools

import jax
import jax.numpy as jnp
from jax import lax
from jax.experimental import pallas as pl
from jax.experimental.pallas import tpu as pltpu
from jax.sharding import PartitionSpec as P

D = 768
HEADS = 12
HEAD = 64
SEQ = 16
FF = 3072
GROUP = 128
PAIRS = HEADS // 2
SLOT = 16
BF = jnp.bfloat16
F32 = jnp.float32

epsilon = 1e-06
negative = -1e30
scale = HEAD ** (-0.5)
LIMIT = 16 * 1024 * 1024

GAIN1, SHIFT1, JOINT, OUT, GAIN2, SHIFT2, WIDE, NARROW = 0, 768, 1536, 3840, 4608, 5376, 6144, 9216
VECTORS = 9984
LINES = VECTORS // 128
ALL_LINES = LINES + -LINES % 8

vmem = pl.BlockSpec(memory_space=pltpu.VMEM)
smem = pl.BlockSpec(memory_space=pltpu.SMEM)


def dot(a, b, dims):
    return lax.dot_general(a, b, (dims, ((), ())), preferred_element_type=F32)


def nn(a, b):
    return dot(a, b, ((1,), (0,)))


def nt(a, b):
    return dot(a, b, ((1,), (1,)))


def tn(a, b):
    return dot(a, b, ((0,), (0,)))


def cost(flops, steps, moved):
    return pl.CostEstimate(flops=flops, transcendentals=steps, bytes_accessed=moved)


def shape(*dims, dtype=F32):
    return jax.ShapeDtypeStruct(dims, dtype)


def kept(*dims, dtype=BF):
    return pltpu.VMEM(dims, dtype)


def near(*values):
    return [pltpu.with_memory_space_constraint(v, pltpu.VMEM) for v in values]


def kernel_call(name, body, results, small, operands, scratch=(), estimate=None, limit=LIMIT):
    return pl.pallas_call(
        body,
        out_shape=results,
        in_specs=[smem] * len(small) + [vmem] * len(operands),
        out_specs=[vmem] * len(results),
        scratch_shapes=[pltpu.VMEM(s, t) for s, t in scratch],
        compiler_params=pltpu.CompilerParams(vmem_limit_bytes=limit),
        cost_estimate=estimate,
        name=name,
    )(*small, *operands)


def iota(dims, axis):
    return lax.broadcasted_iota(jnp.int32, dims, axis)


def norm_parts(values):
    average = jnp.mean(values, axis=-1, keepdims=True)
    centred = values - average
    inverse = lax.rsqrt(jnp.mean(centred * centred, axis=-1, keepdims=True) + epsilon)
    return centred * inverse, inverse


def norm_back(unit, inverse, gain, back):
    inner = back * gain
    part = inverse * (
        inner
        - jnp.mean(inner, axis=-1, keepdims=True)
        - unit * jnp.mean(inner * unit, axis=-1, keepdims=True)
    )
    return part, jnp.sum(back * unit, axis=0, keepdims=True), jnp.sum(back, axis=0, keepdims=True)


def split(value):
    high = value.astype(BF)
    return high, (value - high.astype(F32)).astype(BF)


def two(value):
    return jnp.concatenate(split(value), axis=0)


def as_row(ref):
    return ref[...].reshape(1, ref.shape[0])


def as_column(ref):
    size = ref.shape[0]
    same = iota((size, size), 0) == iota((size, size), 1)
    row = as_row(ref)
    return jnp.sum(jnp.where(same, row, jnp.zeros_like(row)), axis=1, keepdims=True)


def token_limits(ref):
    place = as_row(ref).astype(F32)
    captions = place.shape[1]
    tokens = captions * SEQ
    owner = (iota((tokens, captions), 0) // SEQ == iota((tokens, captions), 1)).astype(F32)
    column = jnp.sum(owner * place, axis=1, keepdims=True)
    line = nt(place.astype(BF), owner.astype(BF))
    return line, column


def pool_mask(line, captions):
    dims = (captions, captions * SEQ)
    token = iota(dims, 1)
    inside = (token % SEQ).astype(F32) <= line
    return jnp.where((token // SEQ == iota(dims, 0)) & inside, 1.0, 0.0)


def spread_mask(column, captions):
    dims = (captions * SEQ, captions)
    token = iota(dims, 0)
    inside = (token % SEQ).astype(F32) <= column
    return jnp.where((token // SEQ == iota(dims, 1)) & inside, 1.0, 0.0)


def head_masks():
    lane = iota((1, 2 * HEAD), 1)
    even = (lane < HEAD).astype(F32)
    return even.astype(BF), (1.0 - even).astype(BF)


def caption_masks():
    lane = iota((SEQ, GROUP), 1) // SEQ
    return [lane == c for c in range(GROUP // SEQ)]


def compact(full, picks):
    out = full[:SEQ]
    for c in range(1, len(picks)):
        out = jnp.where(picks[c], full[c * SEQ : (c + 1) * SEQ], out)
    return out


def expand(low, lows):
    return jnp.concatenate([low * mask for mask in lows], axis=0)


def both_heads(value, masks):
    return jnp.concatenate([value * masks[0], value * masks[1]], axis=0)


def store_permuted(ref, value, dp, blocks):
    rows = value.shape[0] // blocks
    bits = blocks.bit_length() - 1
    if rows % SLOT:
        ref[...] = value
        return
    for b in range(blocks):
        k = jnp.bitwise_xor(dp, b)
        place = 0
        for bit in range(bits):
            place = place + ((k >> bit) & 1) * (1 << (bits - 1 - bit))
        ref[pl.ds(pl.multiple_of(place * rows, SLOT), rows), :] = value[b * rows : (b + 1) * rows]


def box_width(blocks):
    used = (FF + D) // blocks
    return used + -used % 128


def project_kernel(
    blocks, gain_ref, shift_ref, joint_ref, x_ref, wj_ref, project_ref, normed_ref, normed
):
    unit, _ = norm_parts(x_ref[...].astype(F32))
    normed[...] = (unit * as_row(gain_ref) + as_row(shift_ref)).astype(BF)
    joint = as_row(joint_ref)
    for i, bias in enumerate((joint[:, :D], 0.0, joint[:, D:])):
        lanes = slice(i * D, (i + 1) * D)
        project_ref[:, lanes] = (nn(normed[...], wj_ref[:, lanes]) + bias).astype(BF)
    store_permuted(normed_ref, normed[...].T, lax.axis_index("dp"), blocks)


def project_tokens(blocks, gain, shift, joint, x, wj):
    tokens = x.shape[0]
    return kernel_call(
        "project_tokens",
        functools.partial(project_kernel, blocks),
        [kept(tokens, 3 * D), kept(D, tokens)],
        (),
        (gain, shift, joint, *near(x, wj)),
        [((tokens, D), BF)],
        cost(6 * tokens * D * D, 0, 8 * D * D),
    )


def attend_kernel(
    blocks,
    place_ref,
    out_ref,
    x_ref,
    project_ref,
    wo_ref,
    att_ref,
    context_t_ref,
    middle_ref,
    context,
):
    line, _ = token_limits(place_ref)
    masks = head_masks()
    picks = caption_masks()
    lows = [pick.astype(F32).astype(BF) for pick in picks]
    key_place = iota((SEQ, GROUP), 0).astype(F32)

    def attend(h, carry):
        at = pl.multiple_of(h * 2 * HEAD, 128)
        for g in range(x_ref.shape[0] // GROUP):
            here = slice(g * GROUP, (g + 1) * GROUP)
            query = project_ref[here, pl.ds(at, 128)]
            keys = both_heads(project_ref[here, pl.ds(pl.multiple_of(D + at, 128), 128)], masks)
            values = both_heads(
                project_ref[here, pl.ds(pl.multiple_of(2 * D + at, 128), 128)], masks
            )
            scores = nt(keys, query)
            allowed = key_place <= line[:, here]
            parts = []
            for e in range(2):
                score = compact(scores[e * GROUP : (e + 1) * GROUP], picks) * scale
                score = jnp.where(allowed, score, negative)
                score = jnp.exp(score - jnp.max(score, axis=0, keepdims=True))
                weight = score / jnp.sum(score, axis=0, keepdims=True)
                att_ref[2 * h + e, :, here] = weight
                parts.append(expand(weight.astype(BF), lows))
            context[here, pl.ds(at, 128)] = tn(jnp.concatenate(parts, axis=0), values).astype(BF)
        return carry

    lax.fori_loop(0, PAIRS, attend, 0)
    middle_ref[...] = x_ref[...].astype(F32) + (nn(context[...], wo_ref[...]) + as_row(out_ref))
    store_permuted(context_t_ref, context[...].T, lax.axis_index("dp"), blocks)


def attend_tokens(blocks, place, out, x, project, wo):
    tokens = x.shape[0]
    return kernel_call(
        "attend_tokens",
        functools.partial(attend_kernel, blocks),
        [kept(HEADS, SEQ, tokens, dtype=F32), kept(D, tokens), kept(tokens, D, dtype=F32)],
        (),
        (place, out, *near(x, project, wo)),
        [((tokens, D), BF)],
        cost(8 * tokens * D * D, 0, 8 * D * D),
    )


def widen_kernel(
    blocks,
    place_ref,
    gain_ref,
    shift_ref,
    wide_ref,
    narrow_ref,
    middle_ref,
    wu_ref,
    wn_ref,
    wm_ref,
    second_t_ref,
    slope_ref,
    box_ref,
    text_ref,
    scale_ref,
    embed_ref,
    second,
    branch,
    wide,
    mean,
):
    captions = place_ref.shape[0]
    line, column = token_limits(place_ref)
    pool = pool_mask(line, captions)
    share = 1.0 / jnp.sum(pool, axis=1, keepdims=True)
    unit, _ = norm_parts(middle_ref[...])
    second[...] = (unit * as_row(gain_ref) + as_row(shift_ref)).astype(BF)
    store_permuted(second_t_ref, second[...].T, lax.axis_index("dp"), blocks)
    branch[...] = jnp.zeros_like(branch)
    wide[...] = as_row(wide_ref)
    pool_low = pool.astype(BF)
    c0 = 0.7978845608028654
    c1 = c0 * 0.044715
    step = 512

    def widen(i, carry):
        at = pl.multiple_of(i * step, 128)
        upper = nn(second[...], wu_ref[:, pl.ds(at, step)]) + wide[:, pl.ds(at, step)]
        square = upper * upper
        bend = jnp.tanh(upper * (c0 + c1 * square))
        half = 0.5 + 0.5 * bend
        active = (upper * half).astype(BF)
        slope_ref[:, pl.ds(at, step)] = (
            half + (0.5 * upper) * (1.0 - bend * bend) * (c0 + 3.0 * c1 * square)
        ).astype(BF)
        parts = two(nn(pool_low, active) * share)
        mean[:, pl.ds(at, step)] = parts[:captions]
        branch[...] += nn(parts, wn_ref[pl.ds(at, step), :])
        return carry

    lax.fori_loop(0, FF // step, widen, 0)
    inside = jnp.where((iota((captions * SEQ, 1), 0) % SEQ).astype(F32) <= column, 1.0, 0.0)
    weight = inside / (column + 1.0)
    pooled = jnp.sum((middle_ref[...] * weight).reshape(captions, SEQ, D), axis=1)
    pooled = (pooled + (branch[:captions] + branch[captions:] + as_row(narrow_ref))).astype(BF)
    hidden, part = FF // blocks, D // blocks
    for b in range(blocks):
        box_ref[b, :, :hidden] = mean[:, b * hidden : (b + 1) * hidden]
        box_ref[b, :, hidden : hidden + part] = pooled[:, b * part : (b + 1) * part]
    text = nn(pooled, wm_ref[...])
    factor = lax.rsqrt(jnp.sum(text * text, axis=1, keepdims=True) + epsilon)
    text_ref[...] = text
    scale_ref[...] = factor
    embed_ref[...] = (text * factor).astype(BF)


def widen_tokens(blocks, place, gain, shift, wide, narrow, middle, wu, wn, wm):
    tokens = middle.shape[0]
    captions = place.shape[0]
    return kernel_call(
        "widen_tokens",
        functools.partial(widen_kernel, blocks),
        [
            kept(D, tokens),
            kept(tokens, FF),
            kept(blocks, captions, box_width(blocks)),
            kept(captions, D, dtype=F32),
            kept(captions, 1, dtype=F32),
            kept(captions, D),
        ],
        (),
        (place, gain, shift, wide, narrow, *near(middle, wu, wn, wm)),
        [
            ((tokens, D), BF),
            ((2 * captions, D), F32),
            ((1, FF), F32),
            ((captions, FF), BF),
        ],
        cost(3 * tokens * D * FF, tokens * FF, 8 * D * FF),
    )


def match_of(paired, columns, images):
    column = iota((1, columns), 1)
    valid = column % SLOT < images
    name = jnp.where(valid, (column // SLOT) * images + column % SLOT, -1)
    return paired == name, valid


def contrast_kernel(
    images,
    parts,
    bits,
    heat_ref,
    own_ref,
    near_ref,
    wp_ref,
    embed_ref,
    paired_ref,
    weight_ref,
    picture_ref,
    score_ref,
    row_ref,
    inverse_ref,
    stats_ref,
    features,
):
    half = own_ref.shape[0] // SLOT
    for far, ref in enumerate((own_ref, near_ref)):

        def place(i, carry, far=far, ref=ref):
            p = i + far * half
            index = {axis: lax.axis_index(axis) for axis in ("dp", "rep")}
            for n, (axis, bit) in enumerate(bits):
                index[axis] = jnp.bitwise_xor(index[axis], ((p >> n) & 1) << bit)
            to = pl.ds(pl.multiple_of((index["dp"] * parts + index["rep"]) * SLOT, SLOT), SLOT)
            features[to, :] = ref[pl.ds(pl.multiple_of(i * SLOT, SLOT), SLOT), :]
            return carry

        lax.fori_loop(0, half, place, 0, unroll=4)
    picture = nn(features[...], wp_ref[...])
    picture = (
        picture * lax.rsqrt(jnp.sum(picture * picture, axis=1, keepdims=True) + epsilon)
    ).astype(BF)
    picture_ref[...] = picture
    score = nt(embed_ref[...], picture) / heat_ref[0]
    match, valid = match_of(as_column(paired_ref), score.shape[1], images)
    score = jnp.where(valid, score, negative)
    score_ref[...] = score
    top = jnp.max(score, axis=1, keepdims=True)
    row = jnp.log(jnp.sum(jnp.exp(score - top), axis=1, keepdims=True)) + top
    row_ref[...] = row
    positive = jnp.sum(jnp.where(match, score, 0.0), axis=1, keepdims=True)
    hits = jnp.where(match, 1.0, 0.0)
    counts = jnp.sum(hits, axis=0, keepdims=True)
    inverse = 1.0 / jnp.sum(hits * counts, axis=1, keepdims=True)
    inverse_ref[...] = inverse
    total = jnp.sum(as_column(weight_ref) * (row - positive - positive * inverse))
    best = jnp.max(score, axis=0, keepdims=True)
    mass = jnp.sum(jnp.exp(score - best), axis=0, keepdims=True)
    mass = jnp.where(iota(mass.shape, 1) == images, total, mass)
    wide = best.shape[1] // 4
    rows = [v[:, i * wide : (i + 1) * wide] for v in (best, mass) for i in range(4)]
    stats_ref[...] = jnp.concatenate(rows, axis=0)


def contrast(images, parts, bits, heat, own, far, wp, embed, paired, weight):
    captions = embed.shape[0]
    columns = 2 * own.shape[0]
    return kernel_call(
        "contrast",
        functools.partial(contrast_kernel, images, parts, bits),
        [
            kept(columns, D),
            kept(captions, columns, dtype=F32),
            kept(captions, 1, dtype=F32),
            kept(captions, 1, dtype=F32),
            shape(8, columns // 4),
        ],
        (heat,),
        (*near(own, far, wp, embed), paired, weight),
        [((columns, D), BF)],
        cost(4 * columns * D * D, columns * captions, 8 * columns * D),
        max(LIMIT, columns * 8192),
    )


def merged(refs):
    best = functools.reduce(jnp.maximum, [ref[:4] for ref in refs])
    mass = sum(ref[4:] * jnp.exp(ref[:4] - best) for ref in refs)
    return best, mass


def merge_kernel(*refs):
    *given, out_ref = refs
    best, mass = merged(given)
    out_ref[...] = jnp.concatenate([best, mass], axis=0)


def merge(stats):
    return kernel_call("merge", merge_kernel, [shape(*stats[0].shape)], (), stats)[0]


def quarters(rep, away):
    core = rep & 1
    out = []
    for xrel in range(2):
        for yrel in range(2):
            block = jnp.bitwise_xor(rep, 2 * xrel + away)
            x_first = 1 - core if away == 0 else core
            out.append((jnp.where(x_first == 1, 2 * xrel + yrel, 2 * yrel + xrel), block, yrel))
    return out


def head_back_kernel(
    images,
    count_stats,
    rounds,
    heat_ref,
    place_ref,
    score_ref,
    row_ref,
    inverse_ref,
    weight_ref,
    paired_ref,
    picture_ref,
    text_ref,
    scale_ref,
    wm_ref,
    wn_ref,
    slope_ref,
    second_t_ref,
    box_ref,
    *refs,
):
    first = 1 << rounds[0]
    pieces = refs[len(refs) - first :]
    stats = refs[:count_stats]
    (
        back_ref,
        away_ref,
        here_ref,
        pooled_ref,
        loss_ref,
        down_bias_ref,
        up_bias_ref,
    ) = refs[count_stats : len(refs) - first]
    rep = lax.axis_index("rep")
    heat = heat_ref[0]
    captions = place_ref.shape[0]
    line, column = token_limits(place_ref)
    count = jnp.sum(pool_mask(line, captions), axis=1, keepdims=True)
    owner = spread_mask(column, captions).astype(BF)
    owner = jnp.concatenate([owner, owner], axis=1)

    score = score_ref[...]
    match, valid = match_of(as_column(paired_ref), score.shape[1], images)
    best, mass = merged(stats)
    column_log = jnp.log(mass) + best
    column_log = jnp.concatenate([column_log[i : i + 1] for i in range(4)], axis=1)
    loss_ref[...] = mass[:1, images : images + 1] + jnp.sum(
        jnp.where(valid, column_log, 0.0), axis=1, keepdims=True
    )
    weight = as_column(weight_ref)
    graded = (
        weight * jnp.exp(score - row_ref[...])
        + jnp.exp(score - column_log)
        - jnp.where(match, weight * (1.0 + inverse_ref[...]), 0.0)
    )
    graded = jnp.where(valid, graded / heat, 0.0).astype(BF)
    embed_back = nn(graded, picture_ref[...])
    text = text_ref[...]
    factor = scale_ref[...]
    text_dot = jnp.sum(text * embed_back, axis=1, keepdims=True)
    text_back = (factor * embed_back - text * (factor * factor * factor) * text_dot).astype(BF)
    blocks, _, wide = box_ref.shape
    masks = gather_masks(rounds, blocks)
    for c, piece_ref in enumerate(pieces):
        for i in range(blocks // first):
            block = jnp.bitwise_xor(lax.axis_index("dp"), masks[i * first + c])
            piece_ref[:, i * wide : (i + 1) * wide] = box_ref[block]
        piece_ref[:, (blocks // first) * wide :] = text_back
    pooled_back = nt(text_back, wm_ref[...])
    pooled_ref[...] = pooled_back
    branch = (pooled_back / count).astype(BF)
    down_bias_ref[...] = jnp.sum(branch.astype(F32) * count, axis=0, keepdims=True)
    ones = jnp.ones((SLOT, back_ref.shape[0]), BF)
    step = 512

    def widen(i, carry):
        at = pl.multiple_of(i * step, 128)
        part = nn(owner, two(nt(branch, wn_ref[pl.ds(at, step), :])))
        part = (part * slope_ref[:, pl.ds(at, step)].astype(F32)).astype(BF)
        back_ref[:, pl.ds(at, step)] = part
        up_bias_ref[:, pl.ds(at, step)] = nn(ones, part)[:1]
        return carry

    lax.fori_loop(0, FF // step, widen, 0)
    half = second_t_ref.shape[0] // 2
    wide = FF // 4
    for turn, target in enumerate((away_ref, here_ref)):
        for place, block, yrel in quarters(rep, 1 - turn):
            part = nn(
                second_t_ref[yrel * half : (yrel + 1) * half],
                back_ref[:, pl.ds(pl.multiple_of(block * wide, 128), wide)],
            )
            target[place] = part.astype(BF)


def head_back(images, rounds, heat, place, stats, score, row, inverse, weight, paired, picture, text,
              factor, wm, wn, slope, second_t, box):
    captions = text.shape[0]
    tokens = slope.shape[0]
    piece = (4, D // 2, FF // 4)
    return kernel_call(
        "head_back",
        functools.partial(head_back_kernel, images, len(stats), rounds),
        [
            kept(tokens, FF),
            kept(*piece),
            kept(*piece),
            kept(captions, D, dtype=F32),
            shape(1, 1),
            shape(1, D),
            shape(1, FF),
        ]
        + [shape(captions, (box.shape[0] >> rounds[0]) * box.shape[2] + D, dtype=BF)] * (1 << rounds[0]),
        (heat,),
        (
            place,
            *near(score, row, inverse),
            weight,
            paired,
            *near(picture, text, factor, wm, wn, slope, second_t, box),
            *stats,
        ),
        (),
        cost(6 * tokens * D * FF, captions * FF, 24 * D * FF),
    )


def middle_back_kernel(
    place_ref,
    gain_ref,
    pooled_ref,
    back_ref,
    wu_ref,
    middle_ref,
    wo_ref,
    total_ref,
    attended_ref,
    context_back_ref,
    gain_back_ref,
    shift_back_ref,
    bias_ref,
):
    captions = place_ref.shape[0]
    line, column = token_limits(place_ref)
    count = jnp.sum(pool_mask(line, captions), axis=1, keepdims=True)
    owner = spread_mask(column, captions).astype(BF)
    owner = jnp.concatenate([owner, owner], axis=1)
    second_back = nt(back_ref[...], wu_ref[...])
    unit, inverse = norm_parts(middle_ref[...])
    part, gain_back_ref[...], shift_back_ref[...] = norm_back(
        unit, inverse, as_row(gain_ref), second_back
    )
    total = nn(owner, two(pooled_ref[...] / count)) + part
    total_ref[...] = total
    attended = total.astype(BF)
    attended_ref[...] = attended
    bias_ref[...] = nn(jnp.ones((SLOT, attended.shape[0]), BF), attended)[:1]
    context_back_ref[...] = nt(attended, wo_ref[...]).astype(BF)


def middle_back(place, gain, pooled, back, wu, middle, wo):
    tokens = back.shape[0]
    return kernel_call(
        "middle_back",
        middle_back_kernel,
        [
            kept(tokens, D, dtype=F32),
            kept(tokens, D),
            kept(tokens, D),
            shape(1, D),
            shape(1, D),
            shape(1, D),
        ],
        (),
        (place, gain, *near(pooled, back, wu, middle, wo)),
        (),
        cost(4 * tokens * D * FF, 0, 12 * D * FF),
    )


def attention_back_kernel(project_ref, att_ref, context_back_ref, back_ref, bias_ref):
    masks = head_masks()
    picks = caption_masks()
    lows = [pick.astype(F32).astype(BF) for pick in picks]
    low_scale = jnp.asarray(scale, BF)
    first = iota((GROUP, 2 * HEAD), 1) < HEAD
    tokens = project_ref.shape[0]

    def attend(h, carry):
        at = pl.multiple_of(h * 2 * HEAD, 128)
        at_k = pl.multiple_of(D + at, 128)
        at_v = pl.multiple_of(2 * D + at, 128)
        for g in range(tokens // GROUP):
            span = slice(g * GROUP, (g + 1) * GROUP)
            query = project_ref[span, pl.ds(at, 128)]
            keys = both_heads(project_ref[span, pl.ds(at_k, 128)], masks)
            values = both_heads(project_ref[span, pl.ds(at_v, 128)], masks)
            upper = context_back_ref[span, pl.ds(at, 128)]
            full = nt(values, upper)
            weights, grads = [], []
            for e in range(2):
                weight = att_ref[2 * h + e, :, span]
                part = compact(full[e * GROUP : (e + 1) * GROUP], picks)
                grad = weight * (part - jnp.sum(weight * part, axis=0, keepdims=True))
                weights.append(expand(weight.astype(BF), lows))
                grads.append(expand(grad.astype(BF) * low_scale, lows))
            weights = jnp.concatenate(weights, axis=0)
            grads = jnp.concatenate(grads, axis=0)
            back_ref[span, pl.ds(at, 128)] = tn(grads, keys).astype(BF)
            wide = nn(grads, query)
            back_ref[span, pl.ds(at_k, 128)] = jnp.where(first, wide[:GROUP], wide[GROUP:]).astype(
                BF
            )
            wide = nn(weights, upper)
            back_ref[span, pl.ds(at_v, 128)] = jnp.where(first, wide[:GROUP], wide[GROUP:]).astype(
                BF
            )
        return carry

    lax.fori_loop(0, PAIRS, attend, 0)
    ones = jnp.ones((SLOT, tokens), BF)
    for i in range(3):
        lanes = slice(i * D, (i + 1) * D)
        bias_ref[:, lanes] = nn(ones, back_ref[:, lanes])[:1]


def attention_back(project, att, context_back):
    tokens = project.shape[0]
    return kernel_call(
        "attention_back",
        attention_back_kernel,
        [kept(tokens, 3 * D), shape(1, 3 * D)],
        (),
        near(project, att, context_back),
        (),
        cost(5 * tokens * D * FF, 0, 12 * D * FF),
    )


def left_columns_kernel(back_ref, normed_t_ref, away_ref, here_ref, chosen):
    rep = lax.axis_index("rep")
    joint = 3 * D // 4
    some = chosen.shape[2]
    for r in range(4):

        @pl.when(rep == r)
        def _():
            for i, k in enumerate((1, 3, 0, 2)):
                b = r ^ k
                chosen[i] = back_ref[:, b * joint : b * joint + some]

    half = D // 2
    for turn, target in enumerate((away_ref, here_ref)):
        for i, (place, _, yrel) in enumerate(quarters(rep, 1 - turn)):
            lines = slice(yrel * half, (yrel + 1) * half)
            target[place] = nn(normed_t_ref[lines], chosen[2 * turn + i // 2]).astype(BF)


def right_columns_kernel(
    back_ref, attended_ref, normed_t_ref, context_t_ref, away_ref, here_ref, chosen
):
    rep = lax.axis_index("rep")
    joint = 3 * D // 4
    out = D // 4
    some = chosen.shape[2] - out
    for r in range(4):

        @pl.when(rep == r)
        def _():
            for i, k in enumerate((1, 3, 0, 2)):
                b = r ^ k
                chosen[i, :, :some] = back_ref[:, (b + 1) * joint - some : (b + 1) * joint]
                chosen[i, :, some:] = attended_ref[:, b * out : (b + 1) * out]

    half = D // 2
    for turn, target in enumerate((away_ref, here_ref)):
        for i, (place, _, yrel) in enumerate(quarters(rep, 1 - turn)):
            block = 2 * turn + i // 2
            lines = slice(yrel * half, (yrel + 1) * half)
            target[place, :, :some] = nn(normed_t_ref[lines], chosen[block, :, :some]).astype(BF)
            target[place, :, some:] = nn(context_t_ref[lines], chosen[block, :, some:]).astype(BF)


def columns_gradient(name, body, operands):
    tokens = operands[0].shape[0]
    piece = (4, D // 2, D // 2)
    return kernel_call(
        name,
        body,
        [kept(*piece), kept(*piece)],
        (),
        near(*operands),
        [((4, tokens, D // 2), BF)],
        cost(2 * tokens * D * FF, 0, 6 * D * FF),
    )


def token_back_kernel(
    gain_ref,
    x_ref,
    middle_ref,
    back_ref,
    wj_ref,
    joint_ref,
    out_ref,
    gain2_ref,
    shift2_ref,
    wide_ref,
    narrow_ref,
    token_ref,
    sums_ref,
):
    unit, inverse = norm_parts(x_ref[...].astype(F32))
    part, gain1, shift1 = norm_back(unit, inverse, as_row(gain_ref), nt(back_ref[...], wj_ref[...]))
    token_ref[...] = middle_ref[...] + part
    line = 0
    rest = (joint_ref, out_ref, gain2_ref, shift2_ref, wide_ref, narrow_ref)
    for value in [gain1, shift1] + [ref[...] for ref in rest]:
        for i in range(value.shape[1] // 128):
            sums_ref[line : line + 1] = value[:, i * 128 : (i + 1) * 128]
            line += 1
    sums_ref[line:] = jnp.zeros((sums_ref.shape[0] - line, 128), F32)


def token_back(gain, x, middle, back, wj, sums):
    return kernel_call(
        "token_back",
        token_back_kernel,
        [shape(x.shape[0], D), shape(ALL_LINES, 128)],
        (),
        (gain, *near(x, middle, back, wj), *sums),
        (),
        cost(2 * x.shape[0] * D * FF, 0, 8 * D * FF),
    )


def low_rank_kernel(
    hidden, own_ref, near_ref, wm_ref, down_ref, head_ref, other_ref, box, back
):
    rows = own_ref.shape[0]
    box[:rows] = own_ref[...]
    box[rows:] = near_ref[...]
    part = down_ref.shape[0]
    start = box.shape[1] - D
    rep = lax.axis_index("rep")
    for r in range(D // part):

        @pl.when(rep == r)
        def _():
            for i, b in enumerate((r, r ^ 2)):
                back[i] = box[:, start + b * part : start + (b + 1) * part]

    wide = head_ref.shape[1]
    for i in range(2):
        block = jnp.bitwise_xor(rep, 2 * i)
        here = wm_ref[pl.ds(pl.multiple_of(block * part, SLOT), part), :]
        pooled = nt(box[:, start:], here).astype(BF)
        down = tn(pooled, box[:, :hidden])
        head = tn(back[i], box[:, hidden : hidden + wide])
        if i == 0:
            down_ref[...] = down
            head_ref[...] = head
        else:
            other_ref[:, :hidden] = down.astype(BF)
            other_ref[:, hidden:] = head.astype(BF)


def low_rank(blocks, parts, own, far, wm):
    rows = 2 * own.shape[0]
    hidden, wide, part = FF // blocks, D // blocks, D // parts
    return kernel_call(
        "low_rank",
        functools.partial(low_rank_kernel, hidden),
        [shape(part, hidden), shape(part, wide), shape(part, hidden + wide, dtype=BF)],
        (),
        near(own, far, wm),
        [((rows, own.shape[1]), BF), ((2, rows, part), BF)],
        cost(8 * rows * D * D, 0, 4 * rows * D),
    )


def finish_kernel(groups, *refs):
    up, first, second, lines = (
        [refs[sum(groups[:i]) + n] for n in range(groups[i])] for i in range(4)
    )
    loss_ref, down_ref, head_ref, other_ref = refs[sum(groups) : sum(groups) + 4]
    (
        joint_ref,
        out_ref,
        up_block_ref,
        down_block_ref,
        head_block_ref,
        loss_out_ref,
        *vector_refs,
    ) = refs[sum(groups) + 4 :]

    def total(terms):
        return sum(ref[...].astype(F32) for ref in terms)

    up_block_ref[...] = total(up)
    one, two_ = total(first), total(second)
    some = one.shape[1]
    rest = joint_ref.shape[1] - some
    joint_ref[:, :some] = one
    joint_ref[:, some:] = two_[:, :rest]
    out_ref[...] = two_[:, rest:]
    hidden = down_ref.shape[1]
    down_block_ref[...] = down_ref[...] + other_ref[:, :hidden].astype(F32)
    head_block_ref[...] = (head_ref[...] + other_ref[:, hidden:].astype(F32)).T
    loss_out_ref[...] = loss_ref[...].reshape(1)
    vectors = total(lines)
    starts = (GAIN1, SHIFT1, JOINT, OUT, GAIN2, SHIFT2, WIDE, NARROW)
    for start, ref in zip(starts, vector_refs):
        for i in range(ref.shape[0] // 128):
            line = start // 128 + i
            if start == JOINT and i >= D // 128:
                line += D // 128
            ref[pl.ds(i * 128, 128)] = vectors[line]


def finish(up, first, second, vectors, loss, low, joint):
    rows = up[0].shape[0]
    sizes = (D, D, 2 * D, D, D, D, FF, D)
    return kernel_call(
        "finish",
        functools.partial(finish_kernel, [len(v) for v in (up, first, second, vectors)]),
        [
            shape(rows, joint),
            shape(rows, D - joint),
            shape(rows, D),
            shape(*low[0].shape),
            shape(*low[1].shape[::-1]),
            shape(1),
        ]
        + [shape(n) for n in sizes],
        (),
        (*up, *first, *second, *vectors, loss, *low),
    )


def both_pairs(partner):
    dp, rep = lax.axis_size("dp"), lax.axis_size("rep")
    pairs = []
    for i in range(dp):
        for j in range(rep):
            a, b = partner(i, j)
            pairs.append((i * rep + j, a * rep + b))
    return pairs


def exchange(value, partner):
    return lax.ppermute(value, ("dp", "rep"), both_pairs(partner))


def first_turn(i, j):
    return (i, j ^ 2) if j & 1 == 0 else (i ^ 1, j)


def second_turn(i, j):
    return (i ^ 1, j) if j & 1 == 0 else (i, j ^ 2)


def added(a, b):
    return (a.astype(F32) + b.astype(F32)).astype(BF)


def halved(here, got):
    half = here.shape[0] // 2
    return added(here[:half], got[:half]), added(here[half:], got[half:])


def parted(here, got, count):
    rows = here.shape[0] // count
    return [added(here[i * rows : (i + 1) * rows], got[i * rows : (i + 1) * rows]) for i in range(count)]


def core_turn(i, j):
    return i, j ^ 1


def across(i, j):
    return i, j ^ 2


def group_round(keep, got, group):
    masks = group_masks(group)
    bits = len(group)
    parts = parted(keep, got, len(masks))
    place = [sum(((c >> n) & 1) << (bits - 1 - n) for n in range(bits)) for c in range(len(masks))]
    return [parts[0]] + [
        exchange(parts[place[c]], lambda i, j: (i ^ masks[c][0], j)) for c in range(1, len(masks))
    ]


def row_rounds(keep, got, groups):
    terms = [keep, got]
    for group in groups:
        if len(terms) > 2:
            terms = [terms[0], sum(v.astype(F32) for v in terms[1:])]
        terms = group_round(*terms, group)
    return terms


order = lax.optimization_barrier


def dp_groups():
    bits = [("dp", b) for b in range(1, lax.axis_size("dp").bit_length() - 1)]
    return [bits[i : i + 2] for i in range(0, len(bits), 2)] + [[("dp", 0)]]


def all_groups():
    bits = [("rep", b) for b in range(1, lax.axis_size("rep").bit_length() - 1)]
    groups = dp_groups()
    return groups[:-1] + [groups[-1] + bits, [("rep", 0)]]


def group_masks(group):
    out = [(0, 0)]
    for axis, bit in group:
        out += [(a | 1 << bit, b) if axis == "dp" else (a, b | 1 << bit) for a, b in out]
    return out


def gather_masks(rounds, blocks):
    bits = list(range(blocks.bit_length() - 1))
    masks, used = [0], 0
    for count in rounds:
        for bit in bits[used : used + count]:
            masks = masks + [m | 1 << bit for m in masks]
        used += count
    return masks


def split_round(value, wide, group):
    blocks = (value.shape[1] - D) // wide
    turns = group_masks(group)
    text = value[:, blocks * wide :]
    pieces = []
    for c, (a, b) in enumerate(turns):
        chosen = [value[:, i * wide : (i + 1) * wide] for i in range(c, blocks, len(turns))]
        piece = jnp.concatenate(chosen + [text], axis=1)
        pieces.append(piece if c == 0 else exchange(piece, lambda i, j: (i ^ a, j ^ b)))
    return jnp.concatenate(pieces)


def round_of(value, group):
    return [value] + [
        exchange(value, lambda i, j: (i ^ a, j ^ b)) for a, b in group_masks(group)[1:]
    ]


def relative_rows(value, blocks):
    rows = value.shape[0] // blocks
    if rows % SLOT == 0:
        return value
    bits = blocks.bit_length() - 1
    place = jnp.arange(blocks, dtype=jnp.int32)
    source = jnp.zeros_like(place)
    for bit in range(bits):
        source = source + ((place >> (bits - 1 - bit)) & 1) * (1 << bit)
    source = source ^ lax.axis_index("dp")
    return value.reshape(blocks, rows, -1)[source].reshape(value.shape)


def local(
    incoming_activations,
    caption_final_place,
    paired_picture,
    caption_weight,
    locked_picture_features,
    softmax_heat,
    premix_scaling_factor,
    premix_shift_term,
    stacked_mixing_matrix,
    asking_reading_offsets,
    mixing_result_matrix,
    mixing_result_offset,
    premlp_scaling_factor,
    premlp_shift_term,
    widening_matrix,
    widening_offset,
    narrowing_matrix,
    narrowing_offset,
    caption_mapping_matrix,
    picture_mapping_matrix,
):
    both = ("dp", "rep")
    devices = lax.axis_size(both)
    blocks = lax.axis_size("dp")
    parts = lax.axis_size("rep")
    captions = caption_final_place.shape[0]
    images = locked_picture_features.shape[0]
    groups = all_groups()
    pieces = round_of(jnp.pad(locked_picture_features, ((0, SLOT - images), (0, 0))), groups[0])
    project, normed_t = project_tokens(
        blocks,
        premix_scaling_factor,
        premix_shift_term,
        asking_reading_offsets,
        incoming_activations,
        stacked_mixing_matrix,
    )
    project, pieces = order((project, pieces))
    for group in groups[1:-1]:
        pieces = round_of(jnp.concatenate(pieces), group)
    att, context_t, middle = attend_tokens(
        blocks,
        caption_final_place,
        mixing_result_offset,
        incoming_activations,
        project,
        mixing_result_matrix,
    )
    middle, pieces = order((middle, pieces))
    own, far = round_of(jnp.concatenate(pieces), groups[-1])
    second_t, slope, box, text, factor, embed = widen_tokens(
        blocks,
        caption_final_place,
        premlp_scaling_factor,
        premlp_shift_term,
        widening_offset,
        narrowing_offset,
        middle,
        widening_matrix,
        narrowing_matrix,
        caption_mapping_matrix,
    )
    normed_t, context_t, second_t = (
        relative_rows(v, blocks) for v in (normed_t, context_t, second_t)
    )
    embed, far = order((embed, far))
    picture, score, row, inverse, stats = contrast(
        images,
        parts,
        sum(groups, []),
        softmax_heat,
        own,
        far,
        picture_mapping_matrix,
        embed,
        paired_picture,
        caption_weight,
    )
    groups = dp_groups()
    factor_groups = groups[-1:] + groups[:-1]
    high = groups[:-1]
    stats = round_of(stats, [("rep", 0), ("rep", 1)] + groups[-1])
    for group in groups[:-1]:
        stats = round_of(merge(stats), group)
    back, away, here, pooled_back, loss, down_bias, up_bias, *pieces = head_back(
        images,
        [len(group) for group in factor_groups],
        softmax_heat,
        caption_final_place,
        stats,
        score,
        row,
        inverse,
        caption_weight,
        paired_picture,
        picture,
        text,
        factor,
        caption_mapping_matrix,
        narrowing_matrix,
        slope,
        second_t,
        box,
    )
    loss = loss / (captions * devices)
    got = exchange(away, core_turn)
    pieces = pieces[:1] + [
        exchange(piece, lambda i, j: (i ^ a, j ^ b))
        for piece, (a, b) in zip(pieces[1:], group_masks(factor_groups[0])[1:])
    ]
    total, attended, context_back, gain2, shift2, out_bias = middle_back(
        caption_final_place,
        premlp_scaling_factor,
        pooled_back,
        back,
        widening_matrix,
        middle,
        mixing_result_matrix,
    )
    context_back, got, pieces = order((context_back, got, pieces))
    up, send = halved(here, got)
    got_up = exchange(send, first_turn)
    factors = jnp.concatenate(pieces)
    for group in factor_groups[1:]:
        factors = split_round(factors, box.shape[2], group)
    project_back, joint_bias = attention_back(project, att, context_back)
    away, here = columns_gradient("left_columns", left_columns_kernel, (project_back, normed_t))
    got = exchange(away, core_turn)
    project_back, away = order((project_back, away))
    away2, here2 = columns_gradient(
        "right_columns", right_columns_kernel, (project_back, attended, normed_t, context_t)
    )
    project_back, away2, got, got_up = order((project_back, away2, got, got_up))
    up, send = halved(up, got_up)
    got_up = exchange(send[0], second_turn)
    first, send = halved(here, got)
    got = exchange(send, first_turn)
    got2 = exchange(away2, core_turn)
    joint = 3 * D // parts
    token, sums = token_back(
        premix_scaling_factor,
        incoming_activations,
        total,
        project_back,
        stacked_mixing_matrix,
        (joint_bias, out_bias, gain2, shift2, up_bias, down_bias),
    )
    sums, got2 = order((sums, got2))
    second, send = halved(here2, got2)
    got2 = exchange(send, first_turn)
    vectors = round_of(sums, [("rep", 0), ("rep", 1)])
    send, got_up = order((send, got_up))
    up = row_rounds(up[0], got_up, high)
    send, got = order((send, got))
    first, send = halved(first, got)
    got = exchange(send[0], second_turn)
    send, vectors = order((send, vectors))
    vectors = round_of(sum(vectors), groups[-1])
    send, factors = order((send, factors))
    far = exchange(factors, core_turn)
    send, got2 = order((send, got2))
    second, send = halved(second, got2)
    got2 = exchange(send[0], second_turn)
    send, far = order((send, far))
    *low, other = low_rank(blocks, parts, factors, far, caption_mapping_matrix)
    other, vectors = order((other, vectors))
    other = exchange(other, across)
    for group in high:
        vectors = round_of(sum(vectors), group)
    first = row_rounds(first[0], got, high)
    second = row_rounds(second[0], got2, high)
    joint_block, out_block, up_block, down_block, head_block, loss, *grads = finish(
        up, first, second, vectors, loss, (*low, other), joint
    )
    return (
        loss,
        token,
        grads[0],
        grads[1],
        joint_block,
        grads[2],
        out_block,
        grads[3],
        grads[4],
        grads[5],
        up_block,
        grads[6],
        down_block.T,
        grads[7],
        head_block,
    )


def solution(mesh):
    spread = P(("dp", "rep"), None)
    line = P(("dp", "rep"))
    block = P("dp", "rep")
    in_specs = (spread, line, line, line, spread) + (P(),) * 15
    out_specs = (
        P(),
        spread,
        P(),
        P(),
        block,
        P(),
        block,
        P(),
        P(),
        P(),
        block,
        P(),
        block,
        P(),
        block,
    )
    return jax.shard_map(local, mesh=mesh, in_specs=in_specs, out_specs=out_specs, check_vma=False)
```

```python
import functools

import jax
import jax.numpy as jnp
from jax import lax
from jax.experimental import pallas as pl
from jax.experimental.pallas import tpu as pltpu
from jax.sharding import PartitionSpec as P

D = 768
HEADS = 12
HEAD = 64
SEQ = 16
FF = 3072
GROUP = 128
PAIRS = HEADS // 2
SLOT = 16
BF = jnp.bfloat16
F32 = jnp.float32

epsilon = 1e-06
negative = -1e30
scale = HEAD ** (-0.5)
LIMIT = 16 * 1024 * 1024

GAIN1, SHIFT1, JOINT, OUT, GAIN2, SHIFT2, WIDE, NARROW = 0, 768, 1536, 3840, 4608, 5376, 6144, 9216
VECTORS = 9984
LINES = VECTORS // 128
ALL_LINES = LINES + -LINES % 8

vmem = pl.BlockSpec(memory_space=pltpu.VMEM)
smem = pl.BlockSpec(memory_space=pltpu.SMEM)


def dot(a, b, dims):
    return lax.dot_general(a, b, (dims, ((), ())), preferred_element_type=F32)


def nn(a, b):
    return dot(a, b, ((1,), (0,)))


def nt(a, b):
    return dot(a, b, ((1,), (1,)))


def tn(a, b):
    return dot(a, b, ((0,), (0,)))


def cost(flops, steps, moved):
    return pl.CostEstimate(flops=flops, transcendentals=steps, bytes_accessed=moved)


def shape(*dims, dtype=F32):
    return jax.ShapeDtypeStruct(dims, dtype)


def kept(*dims, dtype=BF):
    return pltpu.VMEM(dims, dtype)


def near(*values):
    return [pltpu.with_memory_space_constraint(v, pltpu.VMEM) for v in values]


def kernel_call(name, body, results, small, operands, scratch=(), estimate=None, limit=LIMIT):
    return pl.pallas_call(
        body,
        out_shape=results,
        in_specs=[smem] * len(small) + [vmem] * len(operands),
        out_specs=[vmem] * len(results),
        scratch_shapes=[pltpu.VMEM(s, t) for s, t in scratch],
        compiler_params=pltpu.CompilerParams(vmem_limit_bytes=limit),
        cost_estimate=estimate,
        name=name,
    )(*small, *operands)


def iota(dims, axis):
    return lax.broadcasted_iota(jnp.int32, dims, axis)


def norm_parts(values):
    average = jnp.mean(values, axis=-1, keepdims=True)
    centred = values - average
    inverse = lax.rsqrt(jnp.mean(centred * centred, axis=-1, keepdims=True) + epsilon)
    return centred * inverse, inverse


def norm_back(unit, inverse, gain, back):
    inner = back * gain
    part = inverse * (
        inner
        - jnp.mean(inner, axis=-1, keepdims=True)
        - unit * jnp.mean(inner * unit, axis=-1, keepdims=True)
    )
    return part, jnp.sum(back * unit, axis=0, keepdims=True), jnp.sum(back, axis=0, keepdims=True)


def split(value):
    high = value.astype(BF)
    return high, (value - high.astype(F32)).astype(BF)


def two(value):
    return jnp.concatenate(split(value), axis=0)


def as_row(ref):
    return ref[...].reshape(1, ref.shape[0])


def as_column(ref):
    size = ref.shape[0]
    same = iota((size, size), 0) == iota((size, size), 1)
    row = as_row(ref)
    return jnp.sum(jnp.where(same, row, jnp.zeros_like(row)), axis=1, keepdims=True)


def token_limits(ref):
    place = as_row(ref).astype(F32)
    captions = place.shape[1]
    tokens = captions * SEQ
    owner = (iota((tokens, captions), 0) // SEQ == iota((tokens, captions), 1)).astype(F32)
    column = jnp.sum(owner * place, axis=1, keepdims=True)
    line = nt(place.astype(BF), owner.astype(BF))
    return line, column


def pool_mask(line, captions):
    dims = (captions, captions * SEQ)
    token = iota(dims, 1)
    inside = (token % SEQ).astype(F32) <= line
    return jnp.where((token // SEQ == iota(dims, 0)) & inside, 1.0, 0.0)


def spread_mask(column, captions):
    dims = (captions * SEQ, captions)
    token = iota(dims, 0)
    inside = (token % SEQ).astype(F32) <= column
    return jnp.where((token // SEQ == iota(dims, 1)) & inside, 1.0, 0.0)


def head_masks():
    lane = iota((1, 2 * HEAD), 1)
    even = (lane < HEAD).astype(F32)
    return even.astype(BF), (1.0 - even).astype(BF)


def caption_masks():
    lane = iota((SEQ, GROUP), 1) // SEQ
    return [lane == c for c in range(GROUP // SEQ)]


def compact(full, picks):
    out = full[:SEQ]
    for c in range(1, len(picks)):
        out = jnp.where(picks[c], full[c * SEQ : (c + 1) * SEQ], out)
    return out


def expand(low, lows):
    return jnp.concatenate([low * mask for mask in lows], axis=0)


def both_heads(value, masks):
    return jnp.concatenate([value * masks[0], value * masks[1]], axis=0)


def store_permuted(ref, value, dp, blocks):
    rows = value.shape[0] // blocks
    bits = blocks.bit_length() - 1
    if rows % SLOT:
        ref[...] = value
        return
    for b in range(blocks):
        k = jnp.bitwise_xor(dp, b)
        place = 0
        for bit in range(bits):
            place = place + ((k >> bit) & 1) * (1 << (bits - 1 - bit))
        ref[pl.ds(pl.multiple_of(place * rows, SLOT), rows), :] = value[b * rows : (b + 1) * rows]


def box_width(blocks):
    used = (FF + D) // blocks
    return used + -used % 128


def project_kernel(
    blocks, gain_ref, shift_ref, joint_ref, x_ref, wj_ref, project_ref, normed_ref, normed
):
    unit, _ = norm_parts(x_ref[...].astype(F32))
    normed[...] = (unit * as_row(gain_ref) + as_row(shift_ref)).astype(BF)
    joint = as_row(joint_ref)
    for i, bias in enumerate((joint[:, :D], 0.0, joint[:, D:])):
        lanes = slice(i * D, (i + 1) * D)
        project_ref[:, lanes] = (nn(normed[...], wj_ref[:, lanes]) + bias).astype(BF)
    store_permuted(normed_ref, normed[...].T, lax.axis_index("dp"), blocks)


def project_tokens(blocks, gain, shift, joint, x, wj):
    tokens = x.shape[0]
    return kernel_call(
        "project_tokens",
        functools.partial(project_kernel, blocks),
        [kept(tokens, 3 * D), kept(D, tokens)],
        (),
        (gain, shift, joint, *near(x, wj)),
        [((tokens, D), BF)],
        cost(6 * tokens * D * D, 0, 8 * D * D),
    )


def attend_kernel(
    blocks,
    place_ref,
    out_ref,
    x_ref,
    project_ref,
    wo_ref,
    att_ref,
    context_t_ref,
    middle_ref,
    context,
):
    line, _ = token_limits(place_ref)
    masks = head_masks()
    picks = caption_masks()
    lows = [pick.astype(F32).astype(BF) for pick in picks]
    key_place = iota((SEQ, GROUP), 0).astype(F32)

    def attend(h, carry):
        at = pl.multiple_of(h * 2 * HEAD, 128)
        for g in range(x_ref.shape[0] // GROUP):
            here = slice(g * GROUP, (g + 1) * GROUP)
            query = project_ref[here, pl.ds(at, 128)]
            keys = both_heads(project_ref[here, pl.ds(pl.multiple_of(D + at, 128), 128)], masks)
            values = both_heads(
                project_ref[here, pl.ds(pl.multiple_of(2 * D + at, 128), 128)], masks
            )
            scores = nt(keys, query)
            allowed = key_place <= line[:, here]
            parts = []
            for e in range(2):
                score = compact(scores[e * GROUP : (e + 1) * GROUP], picks) * scale
                score = jnp.where(allowed, score, negative)
                score = jnp.exp(score - jnp.max(score, axis=0, keepdims=True))
                weight = score / jnp.sum(score, axis=0, keepdims=True)
                att_ref[2 * h + e, :, here] = weight
                parts.append(expand(weight.astype(BF), lows))
            context[here, pl.ds(at, 128)] = tn(jnp.concatenate(parts, axis=0), values).astype(BF)
        return carry

    lax.fori_loop(0, PAIRS, attend, 0)
    middle_ref[...] = x_ref[...].astype(F32) + (nn(context[...], wo_ref[...]) + as_row(out_ref))
    store_permuted(context_t_ref, context[...].T, lax.axis_index("dp"), blocks)


def attend_tokens(blocks, place, out, x, project, wo):
    tokens = x.shape[0]
    return kernel_call(
        "attend_tokens",
        functools.partial(attend_kernel, blocks),
        [kept(HEADS, SEQ, tokens, dtype=F32), kept(D, tokens), kept(tokens, D, dtype=F32)],
        (),
        (place, out, *near(x, project, wo)),
        [((tokens, D), BF)],
        cost(8 * tokens * D * D, 0, 8 * D * D),
    )


def widen_kernel(
    blocks,
    place_ref,
    gain_ref,
    shift_ref,
    wide_ref,
    narrow_ref,
    middle_ref,
    wu_ref,
    wn_ref,
    wm_ref,
    second_t_ref,
    slope_ref,
    box_ref,
    text_ref,
    scale_ref,
    embed_ref,
    second,
    branch,
    wide,
    mean,
):
    captions = place_ref.shape[0]
    line, column = token_limits(place_ref)
    pool = pool_mask(line, captions)
    share = 1.0 / jnp.sum(pool, axis=1, keepdims=True)
    unit, _ = norm_parts(middle_ref[...])
    second[...] = (unit * as_row(gain_ref) + as_row(shift_ref)).astype(BF)
    store_permuted(second_t_ref, second[...].T, lax.axis_index("dp"), blocks)
    branch[...] = jnp.zeros_like(branch)
    wide[...] = as_row(wide_ref)
    pool_low = pool.astype(BF)
    c0 = 0.7978845608028654
    c1 = c0 * 0.044715
    step = 512

    def widen(i, carry):
        at = pl.multiple_of(i * step, 128)
        upper = nn(second[...], wu_ref[:, pl.ds(at, step)]) + wide[:, pl.ds(at, step)]
        square = upper * upper
        bend = jnp.tanh(upper * (c0 + c1 * square))
        half = 0.5 + 0.5 * bend
        active = (upper * half).astype(BF)
        slope_ref[:, pl.ds(at, step)] = (
            half + (0.5 * upper) * (1.0 - bend * bend) * (c0 + 3.0 * c1 * square)
        ).astype(BF)
        parts = two(nn(pool_low, active) * share)
        mean[:, pl.ds(at, step)] = parts[:captions]
        branch[...] += nn(parts, wn_ref[pl.ds(at, step), :])
        return carry

    lax.fori_loop(0, FF // step, widen, 0)
    inside = jnp.where((iota((captions * SEQ, 1), 0) % SEQ).astype(F32) <= column, 1.0, 0.0)
    weight = inside / (column + 1.0)
    pooled = jnp.sum((middle_ref[...] * weight).reshape(captions, SEQ, D), axis=1)
    pooled = (pooled + (branch[:captions] + branch[captions:] + as_row(narrow_ref))).astype(BF)
    hidden, part = FF // blocks, D // blocks
    for b in range(blocks):
        box_ref[b, :, :hidden] = mean[:, b * hidden : (b + 1) * hidden]
        box_ref[b, :, hidden : hidden + part] = pooled[:, b * part : (b + 1) * part]
    text = nn(pooled, wm_ref[...])
    factor = lax.rsqrt(jnp.sum(text * text, axis=1, keepdims=True) + epsilon)
    text_ref[...] = text
    scale_ref[...] = factor
    embed_ref[...] = (text * factor).astype(BF)


def widen_tokens(blocks, place, gain, shift, wide, narrow, middle, wu, wn, wm):
    tokens = middle.shape[0]
    captions = place.shape[0]
    return kernel_call(
        "widen_tokens",
        functools.partial(widen_kernel, blocks),
        [
            kept(D, tokens),
            kept(tokens, FF),
            kept(blocks, captions, box_width(blocks)),
            kept(captions, D, dtype=F32),
            kept(captions, 1, dtype=F32),
            kept(captions, D),
        ],
        (),
        (place, gain, shift, wide, narrow, *near(middle, wu, wn, wm)),
        [
            ((tokens, D), BF),
            ((2 * captions, D), F32),
            ((1, FF), F32),
            ((captions, FF), BF),
        ],
        cost(3 * tokens * D * FF, tokens * FF, 8 * D * FF),
    )


def match_of(paired, columns, images):
    column = iota((1, columns), 1)
    valid = column % SLOT < images
    name = jnp.where(valid, (column // SLOT) * images + column % SLOT, -1)
    return paired == name, valid


def contrast_kernel(
    images,
    parts,
    bits,
    heat_ref,
    own_ref,
    near_ref,
    wp_ref,
    embed_ref,
    paired_ref,
    weight_ref,
    picture_ref,
    score_ref,
    row_ref,
    inverse_ref,
    stats_ref,
    features,
):
    half = own_ref.shape[0] // SLOT
    for far, ref in enumerate((own_ref, near_ref)):

        def place(i, carry, far=far, ref=ref):
            p = i + far * half
            index = {axis: lax.axis_index(axis) for axis in ("dp", "rep")}
            for n, (axis, bit) in enumerate(bits):
                index[axis] = jnp.bitwise_xor(index[axis], ((p >> n) & 1) << bit)
            to = pl.ds(pl.multiple_of((index["dp"] * parts + index["rep"]) * SLOT, SLOT), SLOT)
            features[to, :] = ref[pl.ds(pl.multiple_of(i * SLOT, SLOT), SLOT), :]
            return carry

        lax.fori_loop(0, half, place, 0, unroll=4)
    picture = nn(features[...], wp_ref[...])
    picture = (
        picture * lax.rsqrt(jnp.sum(picture * picture, axis=1, keepdims=True) + epsilon)
    ).astype(BF)
    picture_ref[...] = picture
    score = nt(embed_ref[...], picture) / heat_ref[0]
    match, valid = match_of(as_column(paired_ref), score.shape[1], images)
    score = jnp.where(valid, score, negative)
    score_ref[...] = score
    top = jnp.max(score, axis=1, keepdims=True)
    row = jnp.log(jnp.sum(jnp.exp(score - top), axis=1, keepdims=True)) + top
    row_ref[...] = row
    positive = jnp.sum(jnp.where(match, score, 0.0), axis=1, keepdims=True)
    hits = jnp.where(match, 1.0, 0.0)
    counts = jnp.sum(hits, axis=0, keepdims=True)
    inverse = 1.0 / jnp.sum(hits * counts, axis=1, keepdims=True)
    inverse_ref[...] = inverse
    total = jnp.sum(as_column(weight_ref) * (row - positive - positive * inverse))
    best = jnp.max(score, axis=0, keepdims=True)
    mass = jnp.sum(jnp.exp(score - best), axis=0, keepdims=True)
    mass = jnp.where(iota(mass.shape, 1) == images, total, mass)
    wide = best.shape[1] // 4
    rows = [v[:, i * wide : (i + 1) * wide] for v in (best, mass) for i in range(4)]
    stats_ref[...] = jnp.concatenate(rows, axis=0)


def contrast(images, parts, bits, heat, own, far, wp, embed, paired, weight):
    captions = embed.shape[0]
    columns = 2 * own.shape[0]
    return kernel_call(
        "contrast",
        functools.partial(contrast_kernel, images, parts, bits),
        [
            kept(columns, D),
            kept(captions, columns, dtype=F32),
            kept(captions, 1, dtype=F32),
            kept(captions, 1, dtype=F32),
            shape(8, columns // 4),
        ],
        (heat,),
        (*near(own, far, wp, embed), paired, weight),
        [((columns, D), BF)],
        cost(4 * columns * D * D, columns * captions, 8 * columns * D),
        max(LIMIT, columns * 8192),
    )


def merged(refs):
    best = functools.reduce(jnp.maximum, [ref[:4] for ref in refs])
    mass = sum(ref[4:] * jnp.exp(ref[:4] - best) for ref in refs)
    return best, mass


def merge_kernel(*refs):
    *given, out_ref = refs
    best, mass = merged(given)
    out_ref[...] = jnp.concatenate([best, mass], axis=0)


def merge(stats):
    return kernel_call("merge", merge_kernel, [shape(*stats[0].shape)], (), stats)[0]


def quarters(rep, away):
    core = rep & 1
    out = []
    for xrel in range(2):
        for yrel in range(2):
            block = jnp.bitwise_xor(rep, 2 * xrel + away)
            x_first = 1 - core if away == 0 else core
            out.append((jnp.where(x_first == 1, 2 * xrel + yrel, 2 * yrel + xrel), block, yrel))
    return out


def head_back_kernel(
    images,
    count_stats,
    rounds,
    heat_ref,
    place_ref,
    score_ref,
    row_ref,
    inverse_ref,
    weight_ref,
    paired_ref,
    picture_ref,
    text_ref,
    scale_ref,
    wm_ref,
    wn_ref,
    slope_ref,
    second_t_ref,
    box_ref,
    *refs,
):
    first = 1 << rounds[0]
    pieces = refs[len(refs) - first :]
    stats = refs[:count_stats]
    (
        back_ref,
        away_ref,
        here_ref,
        pooled_ref,
        loss_ref,
        down_bias_ref,
        up_bias_ref,
    ) = refs[count_stats : len(refs) - first]
    rep = lax.axis_index("rep")
    heat = heat_ref[0]
    captions = place_ref.shape[0]
    line, column = token_limits(place_ref)
    count = jnp.sum(pool_mask(line, captions), axis=1, keepdims=True)
    owner = spread_mask(column, captions).astype(BF)
    owner = jnp.concatenate([owner, owner], axis=1)

    score = score_ref[...]
    match, valid = match_of(as_column(paired_ref), score.shape[1], images)
    best, mass = merged(stats)
    column_log = jnp.log(mass) + best
    column_log = jnp.concatenate([column_log[i : i + 1] for i in range(4)], axis=1)
    loss_ref[...] = mass[:1, images : images + 1] + jnp.sum(
        jnp.where(valid, column_log, 0.0), axis=1, keepdims=True
    )
    weight = as_column(weight_ref)
    graded = (
        weight * jnp.exp(score - row_ref[...])
        + jnp.exp(score - column_log)
        - jnp.where(match, weight * (1.0 + inverse_ref[...]), 0.0)
    )
    graded = jnp.where(valid, graded / heat, 0.0).astype(BF)
    embed_back = nn(graded, picture_ref[...])
    text = text_ref[...]
    factor = scale_ref[...]
    text_dot = jnp.sum(text * embed_back, axis=1, keepdims=True)
    text_back = (factor * embed_back - text * (factor * factor * factor) * text_dot).astype(BF)
    blocks, _, wide = box_ref.shape
    masks = gather_masks(rounds, blocks)
    for c, piece_ref in enumerate(pieces):
        for i in range(blocks // first):
            block = jnp.bitwise_xor(lax.axis_index("dp"), masks[i * first + c])
            piece_ref[:, i * wide : (i + 1) * wide] = box_ref[block]
        piece_ref[:, (blocks // first) * wide :] = text_back
    pooled_back = nt(text_back, wm_ref[...])
    pooled_ref[...] = pooled_back
    branch = (pooled_back / count).astype(BF)
    down_bias_ref[...] = jnp.sum(branch.astype(F32) * count, axis=0, keepdims=True)
    ones = jnp.ones((SLOT, back_ref.shape[0]), BF)
    step = 512

    def widen(i, carry):
        at = pl.multiple_of(i * step, 128)
        part = nn(owner, two(nt(branch, wn_ref[pl.ds(at, step), :])))
        part = (part * slope_ref[:, pl.ds(at, step)].astype(F32)).astype(BF)
        back_ref[:, pl.ds(at, step)] = part
        up_bias_ref[:, pl.ds(at, step)] = nn(ones, part)[:1]
        return carry

    lax.fori_loop(0, FF // step, widen, 0)
    half = second_t_ref.shape[0] // 2
    wide = FF // 4
    for turn, target in enumerate((away_ref, here_ref)):
        for place, block, yrel in quarters(rep, 1 - turn):
            part = nn(
                second_t_ref[yrel * half : (yrel + 1) * half],
                back_ref[:, pl.ds(pl.multiple_of(block * wide, 128), wide)],
            )
            target[place] = part.astype(BF)


def head_back(images, rounds, heat, place, stats, score, row, inverse, weight, paired, picture, text,
              factor, wm, wn, slope, second_t, box):
    captions = text.shape[0]
    tokens = slope.shape[0]
    piece = (4, D // 2, FF // 4)
    return kernel_call(
        "head_back",
        functools.partial(head_back_kernel, images, len(stats), rounds),
        [
            kept(tokens, FF),
            kept(*piece),
            kept(*piece),
            kept(captions, D, dtype=F32),
            shape(1, 1),
            shape(1, D),
            shape(1, FF),
        ]
        + [shape(captions, (box.shape[0] >> rounds[0]) * box.shape[2] + D, dtype=BF)] * (1 << rounds[0]),
        (heat,),
        (
            place,
            *near(score, row, inverse),
            weight,
            paired,
            *near(picture, text, factor, wm, wn, slope, second_t, box),
            *stats,
        ),
        (),
        cost(6 * tokens * D * FF, captions * FF, 24 * D * FF),
    )


def middle_back_kernel(
    place_ref,
    gain_ref,
    pooled_ref,
    back_ref,
    wu_ref,
    middle_ref,
    wo_ref,
    total_ref,
    attended_ref,
    context_back_ref,
    gain_back_ref,
    shift_back_ref,
    bias_ref,
):
    captions = place_ref.shape[0]
    line, column = token_limits(place_ref)
    count = jnp.sum(pool_mask(line, captions), axis=1, keepdims=True)
    owner = spread_mask(column, captions).astype(BF)
    owner = jnp.concatenate([owner, owner], axis=1)
    second_back = nt(back_ref[...], wu_ref[...])
    unit, inverse = norm_parts(middle_ref[...])
    part, gain_back_ref[...], shift_back_ref[...] = norm_back(
        unit, inverse, as_row(gain_ref), second_back
    )
    total = nn(owner, two(pooled_ref[...] / count)) + part
    total_ref[...] = total
    attended = total.astype(BF)
    attended_ref[...] = attended
    bias_ref[...] = nn(jnp.ones((SLOT, attended.shape[0]), BF), attended)[:1]
    context_back_ref[...] = nt(attended, wo_ref[...]).astype(BF)


def middle_back(place, gain, pooled, back, wu, middle, wo):
    tokens = back.shape[0]
    return kernel_call(
        "middle_back",
        middle_back_kernel,
        [
            kept(tokens, D, dtype=F32),
            kept(tokens, D),
            kept(tokens, D),
            shape(1, D),
            shape(1, D),
            shape(1, D),
        ],
        (),
        (place, gain, *near(pooled, back, wu, middle, wo)),
        (),
        cost(4 * tokens * D * FF, 0, 12 * D * FF),
    )


def attention_back_kernel(project_ref, att_ref, context_back_ref, back_ref, bias_ref):
    masks = head_masks()
    picks = caption_masks()
    lows = [pick.astype(F32).astype(BF) for pick in picks]
    low_scale = jnp.asarray(scale, BF)
    first = iota((GROUP, 2 * HEAD), 1) < HEAD
    tokens = project_ref.shape[0]

    def attend(h, carry):
        at = pl.multiple_of(h * 2 * HEAD, 128)
        at_k = pl.multiple_of(D + at, 128)
        at_v = pl.multiple_of(2 * D + at, 128)
        for g in range(tokens // GROUP):
            span = slice(g * GROUP, (g + 1) * GROUP)
            query = project_ref[span, pl.ds(at, 128)]
            keys = both_heads(project_ref[span, pl.ds(at_k, 128)], masks)
            values = both_heads(project_ref[span, pl.ds(at_v, 128)], masks)
            upper = context_back_ref[span, pl.ds(at, 128)]
            full = nt(values, upper)
            weights, grads = [], []
            for e in range(2):
                weight = att_ref[2 * h + e, :, span]
                part = compact(full[e * GROUP : (e + 1) * GROUP], picks)
                grad = weight * (part - jnp.sum(weight * part, axis=0, keepdims=True))
                weights.append(expand(weight.astype(BF), lows))
                grads.append(expand(grad.astype(BF) * low_scale, lows))
            weights = jnp.concatenate(weights, axis=0)
            grads = jnp.concatenate(grads, axis=0)
            back_ref[span, pl.ds(at, 128)] = tn(grads, keys).astype(BF)
            wide = nn(grads, query)
            back_ref[span, pl.ds(at_k, 128)] = jnp.where(first, wide[:GROUP], wide[GROUP:]).astype(
                BF
            )
            wide = nn(weights, upper)
            back_ref[span, pl.ds(at_v, 128)] = jnp.where(first, wide[:GROUP], wide[GROUP:]).astype(
                BF
            )
        return carry

    lax.fori_loop(0, PAIRS, attend, 0)
    ones = jnp.ones((SLOT, tokens), BF)
    for i in range(3):
        lanes = slice(i * D, (i + 1) * D)
        bias_ref[:, lanes] = nn(ones, back_ref[:, lanes])[:1]


def attention_back(project, att, context_back):
    tokens = project.shape[0]
    return kernel_call(
        "attention_back",
        attention_back_kernel,
        [kept(tokens, 3 * D), shape(1, 3 * D)],
        (),
        near(project, att, context_back),
        (),
        cost(5 * tokens * D * FF, 0, 12 * D * FF),
    )


def left_columns_kernel(back_ref, normed_t_ref, away_ref, here_ref, chosen):
    rep = lax.axis_index("rep")
    joint = 3 * D // 4
    some = chosen.shape[2]
    for r in range(4):

        @pl.when(rep == r)
        def _():
            for i, k in enumerate((1, 3, 0, 2)):
                b = r ^ k
                chosen[i] = back_ref[:, b * joint : b * joint + some]

    half = D // 2
    for turn, target in enumerate((away_ref, here_ref)):
        for i, (place, _, yrel) in enumerate(quarters(rep, 1 - turn)):
            lines = slice(yrel * half, (yrel + 1) * half)
            target[place] = nn(normed_t_ref[lines], chosen[2 * turn + i // 2]).astype(BF)


def right_columns_kernel(
    back_ref, attended_ref, normed_t_ref, context_t_ref, away_ref, here_ref, chosen
):
    rep = lax.axis_index("rep")
    joint = 3 * D // 4
    out = D // 4
    some = chosen.shape[2] - out
    for r in range(4):

        @pl.when(rep == r)
        def _():
            for i, k in enumerate((1, 3, 0, 2)):
                b = r ^ k
                chosen[i, :, :some] = back_ref[:, (b + 1) * joint - some : (b + 1) * joint]
                chosen[i, :, some:] = attended_ref[:, b * out : (b + 1) * out]

    half = D // 2
    for turn, target in enumerate((away_ref, here_ref)):
        for i, (place, _, yrel) in enumerate(quarters(rep, 1 - turn)):
            block = 2 * turn + i // 2
            lines = slice(yrel * half, (yrel + 1) * half)
            target[place, :, :some] = nn(normed_t_ref[lines], chosen[block, :, :some]).astype(BF)
            target[place, :, some:] = nn(context_t_ref[lines], chosen[block, :, some:]).astype(BF)


def columns_gradient(name, body, operands):
    tokens = operands[0].shape[0]
    piece = (4, D // 2, D // 2)
    return kernel_call(
        name,
        body,
        [kept(*piece), kept(*piece)],
        (),
        near(*operands),
        [((4, tokens, D // 2), BF)],
        cost(2 * tokens * D * FF, 0, 6 * D * FF),
    )


def token_back_kernel(
    gain_ref,
    x_ref,
    middle_ref,
    back_ref,
    wj_ref,
    joint_ref,
    out_ref,
    gain2_ref,
    shift2_ref,
    wide_ref,
    narrow_ref,
    token_ref,
    sums_ref,
):
    unit, inverse = norm_parts(x_ref[...].astype(F32))
    part, gain1, shift1 = norm_back(unit, inverse, as_row(gain_ref), nt(back_ref[...], wj_ref[...]))
    token_ref[...] = middle_ref[...] + part
    line = 0
    rest = (joint_ref, out_ref, gain2_ref, shift2_ref, wide_ref, narrow_ref)
    for value in [gain1, shift1] + [ref[...] for ref in rest]:
        for i in range(value.shape[1] // 128):
            sums_ref[line : line + 1] = value[:, i * 128 : (i + 1) * 128]
            line += 1
    sums_ref[line:] = jnp.zeros((sums_ref.shape[0] - line, 128), F32)


def token_back(gain, x, middle, back, wj, sums):
    return kernel_call(
        "token_back",
        token_back_kernel,
        [shape(x.shape[0], D), shape(ALL_LINES, 128)],
        (),
        (gain, *near(x, middle, back, wj), *sums),
        (),
        cost(2 * x.shape[0] * D * FF, 0, 8 * D * FF),
    )


def low_rank_kernel(
    hidden, own_ref, near_ref, wm_ref, down_ref, head_ref, other_ref, box, back
):
    rows = own_ref.shape[0]
    box[:rows] = own_ref[...]
    box[rows:] = near_ref[...]
    part = down_ref.shape[0]
    start = box.shape[1] - D
    rep = lax.axis_index("rep")
    for r in range(D // part):

        @pl.when(rep == r)
        def _():
            for i, b in enumerate((r, r ^ 2)):
                back[i] = box[:, start + b * part : start + (b + 1) * part]

    wide = head_ref.shape[1]
    for i in range(2):
        block = jnp.bitwise_xor(rep, 2 * i)
        here = wm_ref[pl.ds(pl.multiple_of(block * part, SLOT), part), :]
        pooled = nt(box[:, start:], here).astype(BF)
        down = tn(pooled, box[:, :hidden])
        head = tn(back[i], box[:, hidden : hidden + wide])
        if i == 0:
            down_ref[...] = down
            head_ref[...] = head
        else:
            other_ref[:, :hidden] = down.astype(BF)
            other_ref[:, hidden:] = head.astype(BF)


def low_rank(blocks, parts, own, far, wm):
    rows = 2 * own.shape[0]
    hidden, wide, part = FF // blocks, D // blocks, D // parts
    return kernel_call(
        "low_rank",
        functools.partial(low_rank_kernel, hidden),
        [shape(part, hidden), shape(part, wide), shape(part, hidden + wide, dtype=BF)],
        (),
        near(own, far, wm),
        [((rows, own.shape[1]), BF), ((2, rows, part), BF)],
        cost(8 * rows * D * D, 0, 4 * rows * D),
    )


def finish_kernel(groups, *refs):
    up, first, second, lines = (
        [refs[sum(groups[:i]) + n] for n in range(groups[i])] for i in range(4)
    )
    loss_ref, down_ref, head_ref, other_ref = refs[sum(groups) : sum(groups) + 4]
    (
        joint_ref,
        out_ref,
        up_block_ref,
        down_block_ref,
        head_block_ref,
        loss_out_ref,
        *vector_refs,
    ) = refs[sum(groups) + 4 :]

    def total(terms):
        return sum(ref[...].astype(F32) for ref in terms)

    up_block_ref[...] = total(up)
    one, two_ = total(first), total(second)
    some = one.shape[1]
    rest = joint_ref.shape[1] - some
    joint_ref[:, :some] = one
    joint_ref[:, some:] = two_[:, :rest]
    out_ref[...] = two_[:, rest:]
    hidden = down_ref.shape[1]
    down_block_ref[...] = down_ref[...] + other_ref[:, :hidden].astype(F32)
    head_block_ref[...] = (head_ref[...] + other_ref[:, hidden:].astype(F32)).T
    loss_out_ref[...] = loss_ref[...].reshape(1)
    vectors = total(lines)
    starts = (GAIN1, SHIFT1, JOINT, OUT, GAIN2, SHIFT2, WIDE, NARROW)
    for start, ref in zip(starts, vector_refs):
        for i in range(ref.shape[0] // 128):
            line = start // 128 + i
            if start == JOINT and i >= D // 128:
                line += D // 128
            ref[pl.ds(i * 128, 128)] = vectors[line]


def finish(up, first, second, vectors, loss, low, joint):
    rows = up[0].shape[0]
    sizes = (D, D, 2 * D, D, D, D, FF, D)
    return kernel_call(
        "finish",
        functools.partial(finish_kernel, [len(v) for v in (up, first, second, vectors)]),
        [
            shape(rows, joint),
            shape(rows, D - joint),
            shape(rows, D),
            shape(*low[0].shape),
            shape(*low[1].shape[::-1]),
            shape(1),
        ]
        + [shape(n) for n in sizes],
        (),
        (*up, *first, *second, *vectors, loss, *low),
    )


def both_pairs(partner):
    dp, rep = lax.axis_size("dp"), lax.axis_size("rep")
    pairs = []
    for i in range(dp):
        for j in range(rep):
            a, b = partner(i, j)
            pairs.append((i * rep + j, a * rep + b))
    return pairs


def exchange(value, partner):
    return lax.ppermute(value, ("dp", "rep"), both_pairs(partner))


def first_turn(i, j):
    return (i, j ^ 2) if j & 1 == 0 else (i ^ 1, j)


def second_turn(i, j):
    return (i ^ 1, j) if j & 1 == 0 else (i, j ^ 2)


def added(a, b):
    return (a.astype(F32) + b.astype(F32)).astype(BF)


def halved(here, got):
    half = here.shape[0] // 2
    return added(here[:half], got[:half]), added(here[half:], got[half:])


def parted(here, got, count):
    rows = here.shape[0] // count
    return [added(here[i * rows : (i + 1) * rows], got[i * rows : (i + 1) * rows]) for i in range(count)]


def core_turn(i, j):
    return i, j ^ 1


def across(i, j):
    return i, j ^ 2


def group_round(keep, got, group):
    masks = group_masks(group)
    bits = len(group)
    parts = parted(keep, got, len(masks))
    place = [sum(((c >> n) & 1) << (bits - 1 - n) for n in range(bits)) for c in range(len(masks))]
    return [parts[0]] + [
        exchange(parts[place[c]], lambda i, j: (i ^ masks[c][0], j)) for c in range(1, len(masks))
    ]


def row_rounds(keep, got, groups):
    terms = [keep, got]
    for group in groups:
        if len(terms) > 2:
            terms = [terms[0], sum(v.astype(F32) for v in terms[1:])]
        terms = group_round(*terms, group)
    return terms


order = lax.optimization_barrier


def dp_groups():
    bits = [("dp", b) for b in range(1, lax.axis_size("dp").bit_length() - 1)]
    return [bits[i : i + 2] for i in range(0, len(bits), 2)] + [[("dp", 0)]]


def all_groups():
    bits = [("rep", b) for b in range(1, lax.axis_size("rep").bit_length() - 1)]
    groups = dp_groups()
    return groups[:-1] + [groups[-1] + bits, [("rep", 0)]]


def group_masks(group):
    out = [(0, 0)]
    for axis, bit in group:
        out += [(a | 1 << bit, b) if axis == "dp" else (a, b | 1 << bit) for a, b in out]
    return out


def gather_masks(rounds, blocks):
    bits = list(range(blocks.bit_length() - 1))
    masks, used = [0], 0
    for count in rounds:
        for bit in bits[used : used + count]:
            masks = masks + [m | 1 << bit for m in masks]
        used += count
    return masks


def split_round(value, wide, group):
    blocks = (value.shape[1] - D) // wide
    turns = group_masks(group)
    text = value[:, blocks * wide :]
    pieces = []
    for c, (a, b) in enumerate(turns):
        chosen = [value[:, i * wide : (i + 1) * wide] for i in range(c, blocks, len(turns))]
        piece = jnp.concatenate(chosen + [text], axis=1)
        pieces.append(piece if c == 0 else exchange(piece, lambda i, j: (i ^ a, j ^ b)))
    return pieces


def round_of(value, group):
    return [value] + [
        exchange(value, lambda i, j: (i ^ a, j ^ b)) for a, b in group_masks(group)[1:]
    ]


def relative_rows(value, blocks):
    rows = value.shape[0] // blocks
    if rows % SLOT == 0:
        return value
    bits = blocks.bit_length() - 1
    place = jnp.arange(blocks, dtype=jnp.int32)
    source = jnp.zeros_like(place)
    for bit in range(bits):
        source = source + ((place >> (bits - 1 - bit)) & 1) * (1 << bit)
    source = source ^ lax.axis_index("dp")
    return value.reshape(blocks, rows, -1)[source].reshape(value.shape)


def local(
    incoming_activations,
    caption_final_place,
    paired_picture,
    caption_weight,
    locked_picture_features,
    softmax_heat,
    premix_scaling_factor,
    premix_shift_term,
    stacked_mixing_matrix,
    asking_reading_offsets,
    mixing_result_matrix,
    mixing_result_offset,
    premlp_scaling_factor,
    premlp_shift_term,
    widening_matrix,
    widening_offset,
    narrowing_matrix,
    narrowing_offset,
    caption_mapping_matrix,
    picture_mapping_matrix,
):
    both = ("dp", "rep")
    devices = lax.axis_size(both)
    blocks = lax.axis_size("dp")
    parts = lax.axis_size("rep")
    captions = caption_final_place.shape[0]
    images = locked_picture_features.shape[0]
    groups = all_groups()
    pieces = round_of(jnp.pad(locked_picture_features, ((0, SLOT - images), (0, 0))), groups[0])
    project, normed_t = project_tokens(
        blocks,
        premix_scaling_factor,
        premix_shift_term,
        asking_reading_offsets,
        incoming_activations,
        stacked_mixing_matrix,
    )
    project, pieces = order((project, pieces))
    for group in groups[1:-1]:
        pieces = round_of(jnp.concatenate(pieces), group)
    att, context_t, middle = attend_tokens(
        blocks,
        caption_final_place,
        mixing_result_offset,
        incoming_activations,
        project,
        mixing_result_matrix,
    )
    middle, pieces = order((middle, pieces))
    own, far = round_of(jnp.concatenate(pieces), groups[-1])
    second_t, slope, box, text, factor, embed = widen_tokens(
        blocks,
        caption_final_place,
        premlp_scaling_factor,
        premlp_shift_term,
        widening_offset,
        narrowing_offset,
        middle,
        widening_matrix,
        narrowing_matrix,
        caption_mapping_matrix,
    )
    normed_t, context_t, second_t = (
        relative_rows(v, blocks) for v in (normed_t, context_t, second_t)
    )
    embed, far = order((embed, far))
    picture, score, row, inverse, stats = contrast(
        images,
        parts,
        sum(groups, []),
        softmax_heat,
        own,
        far,
        picture_mapping_matrix,
        embed,
        paired_picture,
        caption_weight,
    )
    groups = dp_groups()
    factor_groups = groups[-1:] + groups[:-1]
    high = groups[:-1]
    stats = round_of(stats, [("rep", 0), ("rep", 1)] + groups[-1])
    for group in groups[:-1]:
        stats = round_of(merge(stats), group)
    back, away, here, pooled_back, loss, down_bias, up_bias, *pieces = head_back(
        images,
        [len(group) for group in factor_groups],
        softmax_heat,
        caption_final_place,
        stats,
        score,
        row,
        inverse,
        caption_weight,
        paired_picture,
        picture,
        text,
        factor,
        caption_mapping_matrix,
        narrowing_matrix,
        slope,
        second_t,
        box,
    )
    loss = loss / (captions * devices)
    got = exchange(away, core_turn)
    pieces = pieces[:1] + [
        exchange(piece, lambda i, j: (i ^ a, j ^ b))
        for piece, (a, b) in zip(pieces[1:], group_masks(factor_groups[0])[1:])
    ]
    total, attended, context_back, gain2, shift2, out_bias = middle_back(
        caption_final_place,
        premlp_scaling_factor,
        pooled_back,
        back,
        widening_matrix,
        middle,
        mixing_result_matrix,
    )
    context_back, got, pieces = order((context_back, got, pieces))
    up, send = halved(here, got)
    got_up = exchange(send, first_turn)
    for group in factor_groups[1:]:
        pieces = split_round(jnp.concatenate(pieces), box.shape[2], group)
    project_back, joint_bias = attention_back(project, att, context_back)
    away, here = columns_gradient("left_columns", left_columns_kernel, (project_back, normed_t))
    got = exchange(away, core_turn)
    project_back, away = order((project_back, away))
    joint = 3 * D // parts
    token, sums = token_back(
        premix_scaling_factor,
        incoming_activations,
        total,
        project_back,
        stacked_mixing_matrix,
        (joint_bias, out_bias, gain2, shift2, up_bias, down_bias),
    )
    project_back, sums, got, got_up = order((project_back, sums, got, got_up))
    up, send = halved(up, got_up)
    got_up = exchange(send[0], second_turn)
    first, send = halved(here, got)
    got = exchange(send, first_turn)
    lines = round_of(sums, [("rep", 0)])
    away, here = columns_gradient(
        "right_columns", right_columns_kernel, (project_back, attended, normed_t, context_t)
    )
    away, lines = order((away, lines))
    got2 = exchange(away, core_turn)
    lines = round_of(sum(lines), [("rep", 1)])
    single = [[bit] for group in high for bit in group]
    got_up, got, got2, lines, pieces = order((got_up, got, got2, lines, pieces))
    second, send = halved(here, got2)
    got2 = exchange(send, first_turn)
    first, send = halved(first, got)
    got = exchange(send[0], second_turn)
    up, got_up = group_round(up[0], got_up, single[0])
    lines = round_of(sum(lines), groups[-1])
    got_up, got, got2, lines = order((got_up, got, got2, lines))
    second, send = halved(second, got2)
    got2 = exchange(send[0], second_turn)
    first = row_rounds(first[0], got, high)
    for group in single[1:]:
        up, got_up = group_round(up, got_up, group)
    lines = round_of(sum(lines), single[0])
    factors = jnp.concatenate(pieces)
    far = exchange(factors, core_turn)
    got2, lines, far = order((got2, lines, far))
    second = row_rounds(second[0], got2, high)
    for group in single[1:]:
        lines = round_of(sum(lines), group)
    *low, other = low_rank(blocks, parts, factors, far, caption_mapping_matrix)
    other = exchange(other, across)
    vectors = lines
    up = [up, got_up]
    joint_block, out_block, up_block, down_block, head_block, loss, *grads = finish(
        up, first, second, vectors, loss, (*low, other), joint
    )
    return (
        loss,
        token,
        grads[0],
        grads[1],
        joint_block,
        grads[2],
        out_block,
        grads[3],
        grads[4],
        grads[5],
        up_block,
        grads[6],
        down_block.T,
        grads[7],
        head_block,
    )


def solution(mesh):
    spread = P(("dp", "rep"), None)
    line = P(("dp", "rep"))
    block = P("dp", "rep")
    in_specs = (spread, line, line, line, spread) + (P(),) * 15
    out_specs = (
        P(),
        spread,
        P(),
        P(),
        block,
        P(),
        block,
        P(),
        P(),
        P(),
        block,
        P(),
        block,
        P(),
        block,
    )
    return jax.shard_map(local, mesh=mesh, in_specs=in_specs, out_specs=out_specs, check_vma=False)
```

```python
import functools

import jax
import jax.numpy as jnp
from jax import lax
from jax.experimental import pallas as pl
from jax.experimental.pallas import tpu as pltpu
from jax.sharding import PartitionSpec as P

D = 768
HEADS = 12
HEAD = 64
SEQ = 16
FF = 3072
GROUP = 128
PAIRS = HEADS // 2
SLOT = 16
BF = jnp.bfloat16
F32 = jnp.float32

epsilon = 1e-06
negative = -1e30
scale = HEAD ** (-0.5)
LIMIT = 16 * 1024 * 1024

GAIN1, SHIFT1, JOINT, OUT, GAIN2, SHIFT2, WIDE, NARROW = 0, 768, 1536, 3840, 4608, 5376, 6144, 9216
VECTORS = 9984
LINES = VECTORS // 128
ALL_LINES = LINES + -LINES % 8

vmem = pl.BlockSpec(memory_space=pltpu.VMEM)
smem = pl.BlockSpec(memory_space=pltpu.SMEM)


def dot(a, b, dims):
    return lax.dot_general(a, b, (dims, ((), ())), preferred_element_type=F32)


def nn(a, b):
    return dot(a, b, ((1,), (0,)))


def nt(a, b):
    return dot(a, b, ((1,), (1,)))


def tn(a, b):
    return dot(a, b, ((0,), (0,)))


def cost(flops):
    return pl.CostEstimate(flops=flops, transcendentals=0, bytes_accessed=0)


def shape(*dims, dtype=F32):
    return jax.ShapeDtypeStruct(dims, dtype)


def kept(*dims, dtype=BF):
    return pltpu.VMEM(dims, dtype)


def near(*values):
    return [pltpu.with_memory_space_constraint(v, pltpu.VMEM) for v in values]


def kernel_call(name, body, results, small, operands, scratch=(), estimate=None, limit=LIMIT):
    return pl.pallas_call(
        body,
        out_shape=results,
        in_specs=[smem] * len(small) + [vmem] * len(operands),
        out_specs=[vmem] * len(results),
        scratch_shapes=[pltpu.VMEM(s, t) for s, t in scratch],
        compiler_params=pltpu.CompilerParams(vmem_limit_bytes=limit),
        cost_estimate=estimate,
        name=name,
    )(*small, *operands)


def iota(dims, axis):
    return lax.broadcasted_iota(jnp.int32, dims, axis)


def norm_parts(values):
    average = jnp.mean(values, axis=-1, keepdims=True)
    centred = values - average
    inverse = lax.rsqrt(jnp.mean(centred * centred, axis=-1, keepdims=True) + epsilon)
    return centred * inverse, inverse


def norm_back(unit, inverse, gain, back):
    inner = back * gain
    part = inverse * (
        inner
        - jnp.mean(inner, axis=-1, keepdims=True)
        - unit * jnp.mean(inner * unit, axis=-1, keepdims=True)
    )
    return part, jnp.sum(back * unit, axis=0, keepdims=True), jnp.sum(back, axis=0, keepdims=True)


def split(value):
    high = value.astype(BF)
    return high, (value - high.astype(F32)).astype(BF)


def two(value):
    return jnp.concatenate(split(value), axis=0)


def as_row(ref):
    return ref[...].reshape(1, ref.shape[0])


def as_column(ref):
    size = ref.shape[0]
    same = iota((size, size), 0) == iota((size, size), 1)
    row = as_row(ref)
    return jnp.sum(jnp.where(same, row, jnp.zeros_like(row)), axis=1, keepdims=True)


def token_limits(ref):
    place = as_row(ref).astype(F32)
    captions = place.shape[1]
    tokens = captions * SEQ
    owner = (iota((tokens, captions), 0) // SEQ == iota((tokens, captions), 1)).astype(F32)
    column = jnp.sum(owner * place, axis=1, keepdims=True)
    line = nt(place.astype(BF), owner.astype(BF))
    return line, column


def pool_mask(line, captions):
    dims = (captions, captions * SEQ)
    token = iota(dims, 1)
    inside = (token % SEQ).astype(F32) <= line
    return jnp.where((token // SEQ == iota(dims, 0)) & inside, 1.0, 0.0)


def spread_mask(column, captions):
    dims = (captions * SEQ, captions)
    token = iota(dims, 0)
    inside = (token % SEQ).astype(F32) <= column
    return jnp.where((token // SEQ == iota(dims, 1)) & inside, 1.0, 0.0)


def head_masks():
    lane = iota((1, 2 * HEAD), 1)
    even = (lane < HEAD).astype(F32)
    return even.astype(BF), (1.0 - even).astype(BF)


def caption_masks():
    lane = iota((SEQ, GROUP), 1) // SEQ
    return [lane == c for c in range(GROUP // SEQ)]


def compact(full, picks):
    out = full[:SEQ]
    for c in range(1, len(picks)):
        out = jnp.where(picks[c], full[c * SEQ : (c + 1) * SEQ], out)
    return out


def expand(low, lows):
    return jnp.concatenate([low * mask for mask in lows], axis=0)


def both_heads(value, masks):
    return jnp.concatenate([value * masks[0], value * masks[1]], axis=0)


def store_permuted(ref, value, dp, blocks):
    rows = value.shape[0] // blocks
    bits = blocks.bit_length() - 1
    if rows % SLOT:
        ref[...] = value
        return
    for b in range(blocks):
        k = jnp.bitwise_xor(dp, b)
        place = 0
        for bit in range(bits):
            place = place + ((k >> bit) & 1) * (1 << (bits - 1 - bit))
        ref[pl.ds(pl.multiple_of(place * rows, SLOT), rows), :] = value[b * rows : (b + 1) * rows]


def box_width(blocks):
    used = (FF + D) // blocks
    return used + -used % 128


def project_kernel(
    blocks, gain_ref, shift_ref, joint_ref, x_ref, wj_ref, project_ref, normed_ref, normed
):
    unit, _ = norm_parts(x_ref[...].astype(F32))
    normed[...] = (unit * as_row(gain_ref) + as_row(shift_ref)).astype(BF)
    joint = as_row(joint_ref)
    for i, bias in enumerate((joint[:, :D], 0.0, joint[:, D:])):
        lanes = slice(i * D, (i + 1) * D)
        project_ref[:, lanes] = (nn(normed[...], wj_ref[:, lanes]) + bias).astype(BF)
    store_permuted(normed_ref, normed[...].T, lax.axis_index("dp"), blocks)


def project_tokens(blocks, gain, shift, joint, x, wj):
    tokens = x.shape[0]
    return kernel_call(
        "project_tokens",
        functools.partial(project_kernel, blocks),
        [kept(tokens, 3 * D), kept(D, tokens)],
        (),
        (gain, shift, joint, *near(x, wj)),
        [((tokens, D), BF)],
        cost(6 * tokens * D * D),
    )


def attend_kernel(
    blocks,
    place_ref,
    out_ref,
    x_ref,
    project_ref,
    wo_ref,
    att_ref,
    context_t_ref,
    middle_ref,
    context,
):
    line, _ = token_limits(place_ref)
    masks = head_masks()
    picks = caption_masks()
    lows = [pick.astype(F32).astype(BF) for pick in picks]
    key_place = iota((SEQ, GROUP), 0).astype(F32)

    def attend(h, carry):
        at = pl.multiple_of(h * 2 * HEAD, 128)
        for g in range(x_ref.shape[0] // GROUP):
            here = slice(g * GROUP, (g + 1) * GROUP)
            query = project_ref[here, pl.ds(at, 128)]
            keys = both_heads(project_ref[here, pl.ds(pl.multiple_of(D + at, 128), 128)], masks)
            values = both_heads(
                project_ref[here, pl.ds(pl.multiple_of(2 * D + at, 128), 128)], masks
            )
            scores = nt(keys, query)
            allowed = key_place <= line[:, here]
            parts = []
            for e in range(2):
                score = compact(scores[e * GROUP : (e + 1) * GROUP], picks) * scale
                score = jnp.where(allowed, score, negative)
                score = jnp.exp(score - jnp.max(score, axis=0, keepdims=True))
                weight = score / jnp.sum(score, axis=0, keepdims=True)
                att_ref[2 * h + e, :, here] = weight
                parts.append(expand(weight.astype(BF), lows))
            context[here, pl.ds(at, 128)] = tn(jnp.concatenate(parts, axis=0), values).astype(BF)
        return carry

    lax.fori_loop(0, PAIRS, attend, 0)
    middle_ref[...] = x_ref[...].astype(F32) + (nn(context[...], wo_ref[...]) + as_row(out_ref))
    store_permuted(context_t_ref, context[...].T, lax.axis_index("dp"), blocks)


def attend_tokens(blocks, place, out, x, project, wo):
    tokens = x.shape[0]
    return kernel_call(
        "attend_tokens",
        functools.partial(attend_kernel, blocks),
        [kept(HEADS, SEQ, tokens, dtype=F32), kept(D, tokens), kept(tokens, D, dtype=F32)],
        (),
        (place, out, *near(x, project, wo)),
        [((tokens, D), BF)],
        cost(4 * tokens * D * D),
    )


def widen_kernel(
    blocks,
    place_ref,
    gain_ref,
    shift_ref,
    wide_ref,
    narrow_ref,
    middle_ref,
    wu_ref,
    wn_ref,
    wm_ref,
    second_t_ref,
    slope_ref,
    box_ref,
    text_ref,
    scale_ref,
    embed_ref,
    second,
    branch,
    wide,
    mean,
):
    captions = place_ref.shape[0]
    line, column = token_limits(place_ref)
    pool = pool_mask(line, captions)
    share = 1.0 / jnp.sum(pool, axis=1, keepdims=True)
    unit, _ = norm_parts(middle_ref[...])
    second[...] = (unit * as_row(gain_ref) + as_row(shift_ref)).astype(BF)
    store_permuted(second_t_ref, second[...].T, lax.axis_index("dp"), blocks)
    branch[...] = jnp.zeros_like(branch)
    wide[...] = as_row(wide_ref)
    pool_low = pool.astype(BF)
    c0 = 0.7978845608028654
    c1 = c0 * 0.044715
    step = 512

    def widen(i, carry):
        at = pl.multiple_of(i * step, 128)
        upper = nn(second[...], wu_ref[:, pl.ds(at, step)]) + wide[:, pl.ds(at, step)]
        square = upper * upper
        bend = jnp.tanh(upper * (c0 + c1 * square))
        half = 0.5 + 0.5 * bend
        active = upper * half
        slope_ref[:, pl.ds(at, step)] = (
            half * (1.0 + (upper - active) * (2.0 * c0 + 6.0 * c1 * square))
        ).astype(BF)
        parts = two(nn(pool_low, active.astype(BF)) * share)
        mean[:, pl.ds(at, step)] = parts[:captions]
        branch[...] += nn(parts, wn_ref[pl.ds(at, step), :])
        return carry

    lax.fori_loop(0, FF // step, widen, 0)
    inside = jnp.where((iota((captions * SEQ, 1), 0) % SEQ).astype(F32) <= column, 1.0, 0.0)
    weight = inside / (column + 1.0)
    pooled = jnp.sum((middle_ref[...] * weight).reshape(captions, SEQ, D), axis=1)
    pooled = (pooled + (branch[:captions] + branch[captions:] + as_row(narrow_ref))).astype(BF)
    hidden, part = FF // blocks, D // blocks
    for b in range(blocks):
        box_ref[b, :, :hidden] = mean[:, b * hidden : (b + 1) * hidden]
        box_ref[b, :, hidden : hidden + part] = pooled[:, b * part : (b + 1) * part]
    text = nn(pooled, wm_ref[...])
    factor = lax.rsqrt(jnp.sum(text * text, axis=1, keepdims=True) + epsilon)
    text_ref[...] = text
    scale_ref[...] = factor
    embed_ref[...] = (text * factor).astype(BF)


def widen_tokens(blocks, place, gain, shift, wide, narrow, middle, wu, wn, wm):
    tokens = middle.shape[0]
    captions = place.shape[0]
    return kernel_call(
        "widen_tokens",
        functools.partial(widen_kernel, blocks),
        [
            kept(D, tokens),
            kept(tokens, FF),
            kept(blocks, captions, box_width(blocks)),
            kept(captions, D, dtype=F32),
            kept(captions, 1, dtype=F32),
            kept(captions, D),
        ],
        (),
        (place, gain, shift, wide, narrow, *near(middle, wu, wn, wm)),
        [
            ((tokens, D), BF),
            ((2 * captions, D), F32),
            ((1, FF), F32),
            ((captions, FF), BF),
        ],
        cost(2 * tokens * D * FF),
    )


def match_of(paired, columns, images):
    column = iota((1, columns), 1)
    valid = column % SLOT < images
    name = jnp.where(valid, (column // SLOT) * images + column % SLOT, -1)
    return paired == name, valid


def contrast_kernel(
    images,
    parts,
    bits,
    heat_ref,
    own_ref,
    near_ref,
    wp_ref,
    embed_ref,
    paired_ref,
    weight_ref,
    picture_ref,
    score_ref,
    row_ref,
    inverse_ref,
    stats_ref,
    features,
):
    half = own_ref.shape[0] // SLOT
    for far, ref in enumerate((own_ref, near_ref)):

        def place(i, carry, far=far, ref=ref):
            p = i + far * half
            index = {axis: lax.axis_index(axis) for axis in ("dp", "rep")}
            for n, (axis, bit) in enumerate(bits):
                index[axis] = jnp.bitwise_xor(index[axis], ((p >> n) & 1) << bit)
            to = pl.ds(pl.multiple_of((index["dp"] * parts + index["rep"]) * SLOT, SLOT), SLOT)
            features[to, :] = ref[pl.ds(pl.multiple_of(i * SLOT, SLOT), SLOT), :]
            return carry

        lax.fori_loop(0, half, place, 0, unroll=4)
    picture = nn(features[...], wp_ref[...])
    picture = (
        picture * lax.rsqrt(jnp.sum(picture * picture, axis=1, keepdims=True) + epsilon)
    ).astype(BF)
    picture_ref[...] = picture
    score = nt(embed_ref[...], picture) / heat_ref[0]
    match, valid = match_of(as_column(paired_ref), score.shape[1], images)
    score = jnp.where(valid, score, negative)
    score_ref[...] = score
    top = jnp.max(score, axis=1, keepdims=True)
    row = jnp.log(jnp.sum(jnp.exp(score - top), axis=1, keepdims=True)) + top
    row_ref[...] = row
    positive = jnp.sum(jnp.where(match, score, 0.0), axis=1, keepdims=True)
    hits = jnp.where(match, 1.0, 0.0)
    counts = jnp.sum(hits, axis=0, keepdims=True)
    inverse = 1.0 / jnp.sum(hits * counts, axis=1, keepdims=True)
    inverse_ref[...] = inverse
    total = jnp.sum(as_column(weight_ref) * (row - positive - positive * inverse))
    best = jnp.max(score, axis=0, keepdims=True)
    mass = jnp.sum(jnp.exp(score - best), axis=0, keepdims=True)
    mass = jnp.where(iota(mass.shape, 1) == images, total, mass)
    wide = best.shape[1] // 4
    rows = [v[:, i * wide : (i + 1) * wide] for v in (best, mass) for i in range(4)]
    stats_ref[...] = jnp.concatenate(rows, axis=0)


def contrast(images, parts, bits, heat, own, far, wp, embed, paired, weight):
    captions = embed.shape[0]
    columns = 2 * own.shape[0]
    return kernel_call(
        "contrast",
        functools.partial(contrast_kernel, images, parts, bits),
        [
            kept(columns, D),
            kept(captions, columns, dtype=F32),
            kept(captions, 1, dtype=F32),
            kept(captions, 1, dtype=F32),
            shape(8, columns // 4),
        ],
        (heat,),
        (*near(own, far, wp, embed), paired, weight),
        [((columns, D), BF)],
        cost(2 * columns * D * D),
        max(LIMIT, columns * 8192),
    )


def merged(refs):
    best = functools.reduce(jnp.maximum, [ref[:4] for ref in refs])
    mass = sum(ref[4:] * jnp.exp(ref[:4] - best) for ref in refs)
    return best, mass


def merge_kernel(*refs):
    *given, out_ref = refs
    best, mass = merged(given)
    out_ref[...] = jnp.concatenate([best, mass], axis=0)


def merge(stats):
    return kernel_call("merge", merge_kernel, [shape(*stats[0].shape)], (), stats)[0]


def quarters(rep, away):
    core = rep & 1
    out = []
    for xrel in range(2):
        for yrel in range(2):
            block = jnp.bitwise_xor(rep, 2 * xrel + away)
            x_first = 1 - core if away == 0 else core
            out.append((jnp.where(x_first == 1, 2 * xrel + yrel, 2 * yrel + xrel), block, yrel))
    return out


def head_back_kernel(
    images,
    count_stats,
    rounds,
    heat_ref,
    place_ref,
    score_ref,
    row_ref,
    inverse_ref,
    weight_ref,
    paired_ref,
    picture_ref,
    text_ref,
    scale_ref,
    wm_ref,
    wn_ref,
    slope_ref,
    second_t_ref,
    box_ref,
    *refs,
):
    first = 1 << rounds[0]
    pieces = refs[len(refs) - first :]
    stats = refs[:count_stats]
    (
        back_ref,
        away_ref,
        here_ref,
        pooled_ref,
        loss_ref,
        down_bias_ref,
        up_bias_ref,
    ) = refs[count_stats : len(refs) - first]
    rep = lax.axis_index("rep")
    heat = heat_ref[0]
    captions = place_ref.shape[0]
    line, column = token_limits(place_ref)
    count = jnp.sum(pool_mask(line, captions), axis=1, keepdims=True)
    owner = spread_mask(column, captions).astype(BF)
    owner = jnp.concatenate([owner, owner], axis=1)

    score = score_ref[...]
    match, valid = match_of(as_column(paired_ref), score.shape[1], images)
    best, mass = merged(stats)
    column_log = jnp.log(mass) + best
    column_log = jnp.concatenate([column_log[i : i + 1] for i in range(4)], axis=1)
    loss_ref[...] = mass[:1, images : images + 1] + jnp.sum(
        jnp.where(valid, column_log, 0.0), axis=1, keepdims=True
    )
    weight = as_column(weight_ref)
    graded = (
        weight * jnp.exp(score - row_ref[...])
        + jnp.exp(score - column_log)
        - jnp.where(match, weight * (1.0 + inverse_ref[...]), 0.0)
    )
    graded = jnp.where(valid, graded / heat, 0.0).astype(BF)
    embed_back = nn(graded, picture_ref[...])
    text = text_ref[...]
    factor = scale_ref[...]
    text_dot = jnp.sum(text * embed_back, axis=1, keepdims=True)
    text_back = (factor * embed_back - text * (factor * factor * factor) * text_dot).astype(BF)
    blocks, _, wide = box_ref.shape
    masks = gather_masks(rounds, blocks)
    for c, piece_ref in enumerate(pieces):
        for i in range(blocks // first):
            block = jnp.bitwise_xor(lax.axis_index("dp"), masks[i * first + c])
            piece_ref[:, i * wide : (i + 1) * wide] = box_ref[block]
        piece_ref[:, (blocks // first) * wide :] = text_back
    pooled_back = nt(text_back, wm_ref[...])
    pooled_ref[...] = pooled_back
    branch = (pooled_back / count).astype(BF)
    down_bias_ref[...] = jnp.sum(branch.astype(F32) * count, axis=0, keepdims=True)
    ones = jnp.ones((SLOT, back_ref.shape[0]), BF)
    step = 512

    def widen(i, carry):
        at = pl.multiple_of(i * step, 128)
        part = nn(owner, two(nt(branch, wn_ref[pl.ds(at, step), :])))
        part = (part * slope_ref[:, pl.ds(at, step)].astype(F32)).astype(BF)
        back_ref[:, pl.ds(at, step)] = part
        up_bias_ref[:, pl.ds(at, step)] = nn(ones, part)[:1]
        return carry

    lax.fori_loop(0, FF // step, widen, 0)
    half = second_t_ref.shape[0] // 2
    wide = FF // 4
    for turn, target in enumerate((away_ref, here_ref)):
        for place, block, yrel in quarters(rep, 1 - turn):
            part = nn(
                second_t_ref[yrel * half : (yrel + 1) * half],
                back_ref[:, pl.ds(pl.multiple_of(block * wide, 128), wide)],
            )
            target[place] = part.astype(BF)


def head_back(images, rounds, heat, place, stats, score, row, inverse, weight, paired, picture, text,
              factor, wm, wn, slope, second_t, box):
    captions = text.shape[0]
    tokens = slope.shape[0]
    piece = (4, D // 2, FF // 4)
    return kernel_call(
        "head_back",
        functools.partial(head_back_kernel, images, len(stats), rounds),
        [
            kept(tokens, FF),
            kept(*piece),
            kept(*piece),
            kept(captions, D, dtype=F32),
            shape(1, 1),
            shape(1, D),
            shape(1, FF),
        ]
        + [shape(captions, (box.shape[0] >> rounds[0]) * box.shape[2] + D, dtype=BF)] * (1 << rounds[0]),
        (heat,),
        (
            place,
            *near(score, row, inverse),
            weight,
            paired,
            *near(picture, text, factor, wm, wn, slope, second_t, box),
            *stats,
        ),
        (),
        cost(2 * tokens * D * FF),
    )


def middle_back_kernel(
    place_ref,
    gain_ref,
    pooled_ref,
    back_ref,
    wu_ref,
    middle_ref,
    wo_ref,
    total_ref,
    attended_ref,
    context_back_ref,
    gain_back_ref,
    shift_back_ref,
    bias_ref,
):
    captions = place_ref.shape[0]
    line, column = token_limits(place_ref)
    count = jnp.sum(pool_mask(line, captions), axis=1, keepdims=True)
    owner = spread_mask(column, captions).astype(BF)
    owner = jnp.concatenate([owner, owner], axis=1)
    second_back = nt(back_ref[...], wu_ref[...])
    unit, inverse = norm_parts(middle_ref[...])
    part, gain_back_ref[...], shift_back_ref[...] = norm_back(
        unit, inverse, as_row(gain_ref), second_back
    )
    total = nn(owner, two(pooled_ref[...] / count)) + part
    total_ref[...] = total
    attended = total.astype(BF)
    attended_ref[...] = attended
    bias_ref[...] = nn(jnp.ones((SLOT, attended.shape[0]), BF), attended)[:1]
    context_back_ref[...] = nt(attended, wo_ref[...]).astype(BF)


def middle_back(place, gain, pooled, back, wu, middle, wo):
    tokens = back.shape[0]
    return kernel_call(
        "middle_back",
        middle_back_kernel,
        [
            kept(tokens, D, dtype=F32),
            kept(tokens, D),
            kept(tokens, D),
            shape(1, D),
            shape(1, D),
            shape(1, D),
        ],
        (),
        (place, gain, *near(pooled, back, wu, middle, wo)),
        (),
        cost(2 * tokens * D * (FF + D)),
    )


def attention_back_kernel(project_ref, att_ref, context_back_ref, back_ref, bias_ref):
    masks = head_masks()
    picks = caption_masks()
    lows = [pick.astype(F32).astype(BF) for pick in picks]
    low_scale = jnp.asarray(scale, BF)
    first = iota((GROUP, 2 * HEAD), 1) < HEAD
    tokens = project_ref.shape[0]

    def attend(h, carry):
        at = pl.multiple_of(h * 2 * HEAD, 128)
        at_k = pl.multiple_of(D + at, 128)
        at_v = pl.multiple_of(2 * D + at, 128)
        for g in range(tokens // GROUP):
            span = slice(g * GROUP, (g + 1) * GROUP)
            query = project_ref[span, pl.ds(at, 128)]
            keys = both_heads(project_ref[span, pl.ds(at_k, 128)], masks)
            values = both_heads(project_ref[span, pl.ds(at_v, 128)], masks)
            upper = context_back_ref[span, pl.ds(at, 128)]
            full = nt(values, upper)
            weights, grads = [], []
            for e in range(2):
                weight = att_ref[2 * h + e, :, span]
                part = compact(full[e * GROUP : (e + 1) * GROUP], picks)
                grad = weight * (part - jnp.sum(weight * part, axis=0, keepdims=True))
                weights.append(expand(weight.astype(BF), lows))
                grads.append(expand(grad.astype(BF) * low_scale, lows))
            weights = jnp.concatenate(weights, axis=0)
            grads = jnp.concatenate(grads, axis=0)
            back_ref[span, pl.ds(at, 128)] = tn(grads, keys).astype(BF)
            wide = nn(grads, query)
            back_ref[span, pl.ds(at_k, 128)] = jnp.where(first, wide[:GROUP], wide[GROUP:]).astype(
                BF
            )
            wide = nn(weights, upper)
            back_ref[span, pl.ds(at_v, 128)] = jnp.where(first, wide[:GROUP], wide[GROUP:]).astype(
                BF
            )
        return carry

    lax.fori_loop(0, PAIRS, attend, 0)
    ones = jnp.ones((SLOT, tokens), BF)
    for i in range(3):
        lanes = slice(i * D, (i + 1) * D)
        bias_ref[:, lanes] = nn(ones, back_ref[:, lanes])[:1]


def attention_back(project, att, context_back):
    tokens = project.shape[0]
    return kernel_call(
        "attention_back",
        attention_back_kernel,
        [kept(tokens, 3 * D), shape(1, 3 * D)],
        (),
        near(project, att, context_back),
        (),
        cost(3 * tokens * D * D),
    )


def left_columns_kernel(back_ref, normed_t_ref, away_ref, here_ref, chosen):
    rep = lax.axis_index("rep")
    joint = 3 * D // 4
    some = chosen.shape[2]
    for r in range(4):

        @pl.when(rep == r)
        def _():
            for i, k in enumerate((1, 3, 0, 2)):
                b = r ^ k
                chosen[i] = back_ref[:, b * joint : b * joint + some]

    half = D // 2
    for turn, target in enumerate((away_ref, here_ref)):
        for i, (place, _, yrel) in enumerate(quarters(rep, 1 - turn)):
            lines = slice(yrel * half, (yrel + 1) * half)
            target[place] = nn(normed_t_ref[lines], chosen[2 * turn + i // 2]).astype(BF)


def right_columns_kernel(
    back_ref, attended_ref, normed_t_ref, context_t_ref, away_ref, here_ref, chosen
):
    rep = lax.axis_index("rep")
    joint = 3 * D // 4
    out = D // 4
    some = chosen.shape[2] - out
    for r in range(4):

        @pl.when(rep == r)
        def _():
            for i, k in enumerate((1, 3, 0, 2)):
                b = r ^ k
                chosen[i, :, :some] = back_ref[:, (b + 1) * joint - some : (b + 1) * joint]
                chosen[i, :, some:] = attended_ref[:, b * out : (b + 1) * out]

    half = D // 2
    for turn, target in enumerate((away_ref, here_ref)):
        for i, (place, _, yrel) in enumerate(quarters(rep, 1 - turn)):
            block = 2 * turn + i // 2
            lines = slice(yrel * half, (yrel + 1) * half)
            target[place, :, :some] = nn(normed_t_ref[lines], chosen[block, :, :some]).astype(BF)
            target[place, :, some:] = nn(context_t_ref[lines], chosen[block, :, some:]).astype(BF)


def columns_gradient(name, body, operands):
    tokens = operands[0].shape[0]
    piece = (4, D // 2, D // 2)
    return kernel_call(
        name,
        body,
        [kept(*piece), kept(*piece)],
        (),
        near(*operands),
        [((4, tokens, D // 2), BF)],
        cost(tokens * D * FF),
    )


def token_back_kernel(
    gain_ref,
    x_ref,
    middle_ref,
    back_ref,
    wj_ref,
    joint_ref,
    out_ref,
    gain2_ref,
    shift2_ref,
    wide_ref,
    narrow_ref,
    token_ref,
    sums_ref,
):
    unit, inverse = norm_parts(x_ref[...].astype(F32))
    part, gain1, shift1 = norm_back(unit, inverse, as_row(gain_ref), nt(back_ref[...], wj_ref[...]))
    token_ref[...] = middle_ref[...] + part
    line = 0
    rest = (joint_ref, out_ref, gain2_ref, shift2_ref, wide_ref, narrow_ref)
    for value in [gain1, shift1] + [ref[...] for ref in rest]:
        for i in range(value.shape[1] // 128):
            sums_ref[line : line + 1] = value[:, i * 128 : (i + 1) * 128]
            line += 1
    sums_ref[line:] = jnp.zeros((sums_ref.shape[0] - line, 128), F32)


def token_back(gain, x, middle, back, wj, sums):
    return kernel_call(
        "token_back",
        token_back_kernel,
        [shape(x.shape[0], D), shape(ALL_LINES, 128)],
        (),
        (gain, *near(x, middle, back, wj), *sums),
        (),
        cost(6 * x.shape[0] * D * D),
    )


def low_rank_kernel(
    hidden, own_ref, near_ref, wm_ref, down_ref, head_ref, other_ref, box, back
):
    rows = own_ref.shape[0]
    box[:rows] = own_ref[...]
    box[rows:] = near_ref[...]
    part = down_ref.shape[0]
    start = box.shape[1] - D
    rep = lax.axis_index("rep")
    for r in range(D // part):

        @pl.when(rep == r)
        def _():
            for i, b in enumerate((r, r ^ 2)):
                back[i] = box[:, start + b * part : start + (b + 1) * part]

    wide = head_ref.shape[1]
    for i in range(2):
        block = jnp.bitwise_xor(rep, 2 * i)
        here = wm_ref[pl.ds(pl.multiple_of(block * part, SLOT), part), :]
        pooled = nt(box[:, start:], here).astype(BF)
        down = tn(pooled, box[:, :hidden])
        head = tn(back[i], box[:, hidden : hidden + wide])
        if i == 0:
            down_ref[...] = down
            head_ref[...] = head
        else:
            other_ref[:, :hidden] = down.astype(BF)
            other_ref[:, hidden:] = head.astype(BF)


def low_rank(blocks, parts, own, far, wm):
    rows = 2 * own.shape[0]
    hidden, wide, part = FF // blocks, D // blocks, D // parts
    return kernel_call(
        "low_rank",
        functools.partial(low_rank_kernel, hidden),
        [shape(part, hidden), shape(part, wide), shape(part, hidden + wide, dtype=BF)],
        (),
        near(own, far, wm),
        [((rows, own.shape[1]), BF), ((2, rows, part), BF)],
        cost(2 * rows * D * D),
    )


def finish_kernel(groups, *refs):
    up, first, second, lines = (
        [refs[sum(groups[:i]) + n] for n in range(groups[i])] for i in range(4)
    )
    loss_ref, down_ref, head_ref, other_ref = refs[sum(groups) : sum(groups) + 4]
    (
        joint_ref,
        out_ref,
        up_block_ref,
        down_block_ref,
        head_block_ref,
        loss_out_ref,
        *vector_refs,
    ) = refs[sum(groups) + 4 :]

    def total(terms):
        return sum(ref[...].astype(F32) for ref in terms)

    up_block_ref[...] = total(up)
    one, two_ = total(first), total(second)
    some = one.shape[1]
    rest = joint_ref.shape[1] - some
    joint_ref[:, :some] = one
    joint_ref[:, some:] = two_[:, :rest]
    out_ref[...] = two_[:, rest:]
    hidden = down_ref.shape[1]
    down_block_ref[...] = down_ref[...] + other_ref[:, :hidden].astype(F32)
    head_block_ref[...] = (head_ref[...] + other_ref[:, hidden:].astype(F32)).T
    loss_out_ref[...] = loss_ref[...].reshape(1)
    vectors = total(lines)
    starts = (GAIN1, SHIFT1, JOINT, OUT, GAIN2, SHIFT2, WIDE, NARROW)
    for start, ref in zip(starts, vector_refs):
        for i in range(ref.shape[0] // 128):
            line = start // 128 + i
            if start == JOINT and i >= D // 128:
                line += D // 128
            ref[pl.ds(i * 128, 128)] = vectors[line]


def finish(up, first, second, vectors, loss, low, joint):
    rows = up[0].shape[0]
    sizes = (D, D, 2 * D, D, D, D, FF, D)
    return kernel_call(
        "finish",
        functools.partial(finish_kernel, [len(v) for v in (up, first, second, vectors)]),
        [
            shape(rows, joint),
            shape(rows, D - joint),
            shape(rows, D),
            shape(*low[0].shape),
            shape(*low[1].shape[::-1]),
            shape(1),
        ]
        + [shape(n) for n in sizes],
        (),
        (*up, *first, *second, *vectors, loss, *low),
    )


def both_pairs(partner):
    dp, rep = lax.axis_size("dp"), lax.axis_size("rep")
    pairs = []
    for i in range(dp):
        for j in range(rep):
            a, b = partner(i, j)
            pairs.append((i * rep + j, a * rep + b))
    return pairs


def exchange(value, partner):
    return lax.ppermute(value, ("dp", "rep"), both_pairs(partner))


def first_turn(i, j):
    return (i, j ^ 2) if j & 1 == 0 else (i ^ 1, j)


def second_turn(i, j):
    return (i ^ 1, j) if j & 1 == 0 else (i, j ^ 2)


def added(a, b):
    return (a.astype(F32) + b.astype(F32)).astype(BF)


def halved(here, got):
    half = here.shape[0] // 2
    return added(here[:half], got[:half]), added(here[half:], got[half:])


def parted(here, got, count):
    rows = here.shape[0] // count
    return [added(here[i * rows : (i + 1) * rows], got[i * rows : (i + 1) * rows]) for i in range(count)]


def core_turn(i, j):
    return i, j ^ 1


def across(i, j):
    return i, j ^ 2


def group_round(keep, got, group):
    masks = group_masks(group)
    bits = len(group)
    parts = parted(keep, got, len(masks))
    place = [sum(((c >> n) & 1) << (bits - 1 - n) for n in range(bits)) for c in range(len(masks))]
    return [parts[0]] + [
        exchange(parts[place[c]], lambda i, j: (i ^ masks[c][0], j)) for c in range(1, len(masks))
    ]


def row_rounds(keep, got, groups):
    terms = [keep, got]
    for group in groups:
        if len(terms) > 2:
            terms = [terms[0], sum(v.astype(F32) for v in terms[1:])]
        terms = group_round(*terms, group)
    return terms


order = lax.optimization_barrier


def dp_groups():
    bits = [("dp", b) for b in range(1, lax.axis_size("dp").bit_length() - 1)]
    return [bits[i : i + 2] for i in range(0, len(bits), 2)] + [[("dp", 0)]]


def all_groups():
    bits = [("rep", b) for b in range(1, lax.axis_size("rep").bit_length() - 1)]
    groups = dp_groups()
    return groups[:-1] + [groups[-1] + bits, [("rep", 0)]]


def group_masks(group):
    out = [(0, 0)]
    for axis, bit in group:
        out += [(a | 1 << bit, b) if axis == "dp" else (a, b | 1 << bit) for a, b in out]
    return out


def gather_masks(rounds, blocks):
    bits = [0] + list(range(blocks.bit_length() - 2, 0, -1))
    masks, used = [0], 0
    for count in rounds:
        for bit in bits[used : used + count]:
            masks = masks + [m | 1 << bit for m in masks]
        used += count
    return masks


def split_round(value, wide, group):
    blocks = (value.shape[1] - D) // wide
    turns = group_masks(group)
    text = value[:, blocks * wide :]
    pieces = []
    for c, (a, b) in enumerate(turns):
        chosen = [value[:, i * wide : (i + 1) * wide] for i in range(c, blocks, len(turns))]
        piece = jnp.concatenate(chosen + [text], axis=1)
        pieces.append(piece if c == 0 else exchange(piece, lambda i, j: (i ^ a, j ^ b)))
    return pieces


def round_of(value, group):
    return [value] + [
        exchange(value, lambda i, j: (i ^ a, j ^ b)) for a, b in group_masks(group)[1:]
    ]


def relative_rows(value, blocks):
    rows = value.shape[0] // blocks
    if rows % SLOT == 0:
        return value
    bits = blocks.bit_length() - 1
    place = jnp.arange(blocks, dtype=jnp.int32)
    source = jnp.zeros_like(place)
    for bit in range(bits):
        source = source + ((place >> (bits - 1 - bit)) & 1) * (1 << bit)
    source = source ^ lax.axis_index("dp")
    return value.reshape(blocks, rows, -1)[source].reshape(value.shape)


def local(
    incoming_activations,
    caption_final_place,
    paired_picture,
    caption_weight,
    locked_picture_features,
    softmax_heat,
    premix_scaling_factor,
    premix_shift_term,
    stacked_mixing_matrix,
    asking_reading_offsets,
    mixing_result_matrix,
    mixing_result_offset,
    premlp_scaling_factor,
    premlp_shift_term,
    widening_matrix,
    widening_offset,
    narrowing_matrix,
    narrowing_offset,
    caption_mapping_matrix,
    picture_mapping_matrix,
):
    both = ("dp", "rep")
    devices = lax.axis_size(both)
    blocks = lax.axis_size("dp")
    parts = lax.axis_size("rep")
    captions = caption_final_place.shape[0]
    images = locked_picture_features.shape[0]
    groups = all_groups()
    pieces = round_of(jnp.pad(locked_picture_features, ((0, SLOT - images), (0, 0))), groups[0])
    project, normed_t = project_tokens(
        blocks,
        premix_scaling_factor,
        premix_shift_term,
        asking_reading_offsets,
        incoming_activations,
        stacked_mixing_matrix,
    )
    project, pieces = order((project, pieces))
    for group in groups[1:-1]:
        pieces = round_of(jnp.concatenate(pieces), group)
    att, context_t, middle = attend_tokens(
        blocks,
        caption_final_place,
        mixing_result_offset,
        incoming_activations,
        project,
        mixing_result_matrix,
    )
    middle, pieces = order((middle, pieces))
    own, far = round_of(jnp.concatenate(pieces), groups[-1])
    second_t, slope, box, text, factor, embed = widen_tokens(
        blocks,
        caption_final_place,
        premlp_scaling_factor,
        premlp_shift_term,
        widening_offset,
        narrowing_offset,
        middle,
        widening_matrix,
        narrowing_matrix,
        caption_mapping_matrix,
    )
    normed_t, context_t, second_t = (
        relative_rows(v, blocks) for v in (normed_t, context_t, second_t)
    )
    embed, far = order((embed, far))
    picture, score, row, inverse, stats = contrast(
        images,
        parts,
        sum(groups, []),
        softmax_heat,
        own,
        far,
        picture_mapping_matrix,
        embed,
        paired_picture,
        caption_weight,
    )
    groups = dp_groups()
    high = [[bit] for group in groups[:-1] for bit in group]
    factor_groups = groups[-1:] + high[::-1]
    stats = round_of(stats, [("rep", 0)])
    stats = round_of(merge(stats), [("rep", 1)] + groups[-1])
    for group in groups[:-1]:
        stats = round_of(merge(stats), group)
    back, away, here, pooled_back, loss, down_bias, up_bias, *pieces = head_back(
        images,
        [len(group) for group in factor_groups],
        softmax_heat,
        caption_final_place,
        stats,
        score,
        row,
        inverse,
        caption_weight,
        paired_picture,
        picture,
        text,
        factor,
        caption_mapping_matrix,
        narrowing_matrix,
        slope,
        second_t,
        box,
    )
    loss = loss / (captions * devices)
    got = exchange(away, core_turn)
    pieces = pieces[:1] + [
        exchange(piece, lambda i, j: (i ^ a, j ^ b))
        for piece, (a, b) in zip(pieces[1:], group_masks(factor_groups[0])[1:])
    ]
    total, attended, context_back, gain2, shift2, out_bias = middle_back(
        caption_final_place,
        premlp_scaling_factor,
        pooled_back,
        back,
        widening_matrix,
        middle,
        mixing_result_matrix,
    )
    context_back, got, pieces = order((context_back, got, pieces))
    up, send = halved(here, got)
    got_up = exchange(send, first_turn)
    pieces = split_round(jnp.concatenate(pieces), box.shape[2], factor_groups[1])
    project_back, joint_bias = attention_back(project, att, context_back)
    project_back, pieces = order((project_back, pieces))
    for group in factor_groups[2:]:
        pieces = split_round(jnp.concatenate(pieces), box.shape[2], group)
    away, here = columns_gradient("left_columns", left_columns_kernel, (project_back, normed_t))
    got = exchange(away, core_turn)
    project_back, away = order((project_back, away))
    joint = 3 * D // parts
    token, sums = token_back(
        premix_scaling_factor,
        incoming_activations,
        total,
        project_back,
        stacked_mixing_matrix,
        (joint_bias, out_bias, gain2, shift2, up_bias, down_bias),
    )
    project_back, sums, got, got_up = order((project_back, sums, got, got_up))
    up, send = halved(up, got_up)
    got_up = exchange(send[0], second_turn)
    first, send = halved(here, got)
    got = exchange(send, first_turn)
    lines = round_of(sums, [("rep", 0)])
    away, here = columns_gradient(
        "right_columns", right_columns_kernel, (project_back, attended, normed_t, context_t)
    )
    away, lines, pieces = order((away, lines, pieces))
    got2 = exchange(away, core_turn)
    lines = round_of(sum(lines), [("rep", 1)])
    factors = jnp.concatenate(pieces)
    far = exchange(factors, core_turn)
    got_up, got, got2, lines, far = order((got_up, got, got2, lines, far))
    second, send = halved(here, got2)
    got2 = exchange(send, first_turn)
    first, send = halved(first, got)
    got = exchange(send[0], second_turn)
    up, got_up = group_round(up[0], got_up, high[0])
    lines = round_of(sum(lines), groups[-1])
    *low, other = low_rank(blocks, parts, factors, far, caption_mapping_matrix)
    other = exchange(other, across)
    got_up, got, got2, lines, other = order((got_up, got, got2, lines, other))
    second, send = halved(second, got2)
    got2 = exchange(send[0], second_turn)
    first, got = group_round(first[0], got, high[0])
    lines = round_of(sum(lines), high[0])
    for group in high[1:2]:
        up, got_up = group_round(up, got_up, group)
    second = second[0]
    for i, group in enumerate(high):
        got, got2, lines = order((got, got2, lines))
        second, got2 = group_round(second, got2, group)
        if i + 1 < len(high):
            first, got = group_round(first, got, high[i + 1])
            lines = round_of(sum(lines), high[i + 1])
    for group in high[2:]:
        up, got_up = group_round(up, got_up, group)
    first, second, up, vectors = [first, got], [second, got2], [up, got_up], lines
    joint_block, out_block, up_block, down_block, head_block, loss, *grads = finish(
        up, first, second, vectors, loss, (*low, other), joint
    )
    return (
        loss,
        token,
        grads[0],
        grads[1],
        joint_block,
        grads[2],
        out_block,
        grads[3],
        grads[4],
        grads[5],
        up_block,
        grads[6],
        down_block.T,
        grads[7],
        head_block,
    )


def solution(mesh):
    spread = P(("dp", "rep"), None)
    line = P(("dp", "rep"))
    block = P("dp", "rep")
    in_specs = (spread, line, line, line, spread) + (P(),) * 15
    out_specs = (
        P(),
        spread,
        P(),
        P(),
        block,
        P(),
        block,
        P(),
        P(),
        P(),
        block,
        P(),
        block,
        P(),
        block,
    )
    return jax.shard_map(local, mesh=mesh, in_specs=in_specs, out_specs=out_specs, check_vma=False)
```

```python
import functools

import jax
import jax.numpy as jnp
from jax import lax
from jax.experimental import pallas as pl
from jax.experimental.pallas import tpu as pltpu
from jax.sharding import PartitionSpec as P

D = 768
HEADS = 12
HEAD = 64
SEQ = 16
FF = 3072
GROUP = 128
PAIRS = HEADS // 2
SLOT = 16
BF = jnp.bfloat16
F32 = jnp.float32

epsilon = 1e-06
negative = -1e30
scale = HEAD ** (-0.5)
LIMIT = 16 * 1024 * 1024

GAIN1, SHIFT1, JOINT, OUT, GAIN2, SHIFT2, WIDE, NARROW = 0, 768, 1536, 3840, 4608, 5376, 6144, 9216
VECTORS = 9984
LINES = VECTORS // 128
ALL_LINES = LINES + -LINES % 8

vmem = pl.BlockSpec(memory_space=pltpu.VMEM)
smem = pl.BlockSpec(memory_space=pltpu.SMEM)


def dot(a, b, dims):
    return lax.dot_general(a, b, (dims, ((), ())), preferred_element_type=F32)


def nn(a, b):
    return dot(a, b, ((1,), (0,)))


def nt(a, b):
    return dot(a, b, ((1,), (1,)))


def tn(a, b):
    return dot(a, b, ((0,), (0,)))


def cost(flops):
    return pl.CostEstimate(flops=flops, transcendentals=0, bytes_accessed=0)


def shape(*dims, dtype=F32):
    return jax.ShapeDtypeStruct(dims, dtype)


def kept(*dims, dtype=BF):
    return pltpu.VMEM(dims, dtype)


def near(*values):
    return [pltpu.with_memory_space_constraint(v, pltpu.VMEM) for v in values]


def kernel_call(name, body, results, small, operands, scratch=(), estimate=None, limit=LIMIT):
    return pl.pallas_call(
        body,
        out_shape=results,
        in_specs=[smem] * len(small) + [vmem] * len(operands),
        out_specs=[vmem] * len(results),
        scratch_shapes=[pltpu.VMEM(s, t) for s, t in scratch],
        compiler_params=pltpu.CompilerParams(vmem_limit_bytes=limit),
        cost_estimate=estimate,
        name=name,
    )(*small, *operands)


def iota(dims, axis):
    return lax.broadcasted_iota(jnp.int32, dims, axis)


def norm_parts(values):
    average = jnp.mean(values, axis=-1, keepdims=True)
    centred = values - average
    inverse = lax.rsqrt(jnp.mean(centred * centred, axis=-1, keepdims=True) + epsilon)
    return centred * inverse, inverse


def norm_back(unit, inverse, gain, back):
    inner = back * gain
    part = inverse * (
        inner
        - jnp.mean(inner, axis=-1, keepdims=True)
        - unit * jnp.mean(inner * unit, axis=-1, keepdims=True)
    )
    return part, jnp.sum(back * unit, axis=0, keepdims=True), jnp.sum(back, axis=0, keepdims=True)


def split(value):
    high = value.astype(BF)
    return high, (value - high.astype(F32)).astype(BF)


def two(value):
    return jnp.concatenate(split(value), axis=0)


def as_row(ref):
    return ref[...].reshape(1, ref.shape[0])


def as_column(ref):
    size = ref.shape[0]
    same = iota((size, size), 0) == iota((size, size), 1)
    row = as_row(ref)
    return jnp.sum(jnp.where(same, row, jnp.zeros_like(row)), axis=1, keepdims=True)


def token_limits(ref):
    place = as_row(ref).astype(F32)
    captions = place.shape[1]
    tokens = captions * SEQ
    owner = (iota((tokens, captions), 0) // SEQ == iota((tokens, captions), 1)).astype(F32)
    column = jnp.sum(owner * place, axis=1, keepdims=True)
    line = nt(place.astype(BF), owner.astype(BF))
    return line, column


def pool_mask(line, captions):
    dims = (captions, captions * SEQ)
    token = iota(dims, 1)
    inside = (token % SEQ).astype(F32) <= line
    return jnp.where((token // SEQ == iota(dims, 0)) & inside, 1.0, 0.0)


def spread_mask(column, captions):
    dims = (captions * SEQ, captions)
    token = iota(dims, 0)
    inside = (token % SEQ).astype(F32) <= column
    return jnp.where((token // SEQ == iota(dims, 1)) & inside, 1.0, 0.0)


def head_masks():
    lane = iota((1, 2 * HEAD), 1)
    even = (lane < HEAD).astype(F32)
    return even.astype(BF), (1.0 - even).astype(BF)


def caption_masks():
    lane = iota((SEQ, GROUP), 1) // SEQ
    return [lane == c for c in range(GROUP // SEQ)]


def compact(full, picks):
    out = full[:SEQ]
    for c in range(1, len(picks)):
        out = jnp.where(picks[c], full[c * SEQ : (c + 1) * SEQ], out)
    return out


def expand(low, lows):
    return jnp.concatenate([low * mask for mask in lows], axis=0)


def both_heads(value, masks):
    return jnp.concatenate([value * masks[0], value * masks[1]], axis=0)


def store_permuted(ref, value, dp, blocks):
    rows = value.shape[0] // blocks
    bits = blocks.bit_length() - 1
    if rows % SLOT:
        ref[...] = value
        return
    for b in range(blocks):
        k = jnp.bitwise_xor(dp, b)
        place = 0
        for bit in range(bits):
            place = place + ((k >> bit) & 1) * (1 << (bits - 1 - bit))
        ref[pl.ds(pl.multiple_of(place * rows, SLOT), rows), :] = value[b * rows : (b + 1) * rows]


def box_width(blocks):
    used = (FF + D) // blocks
    return used + -used % 128


def project_kernel(
    blocks, gain_ref, shift_ref, joint_ref, x_ref, wj_ref, project_ref, normed_ref, normed
):
    unit, _ = norm_parts(x_ref[...].astype(F32))
    normed[...] = (unit * as_row(gain_ref) + as_row(shift_ref)).astype(BF)
    joint = as_row(joint_ref)
    for i, bias in enumerate((joint[:, :D], 0.0, joint[:, D:])):
        lanes = slice(i * D, (i + 1) * D)
        project_ref[:, lanes] = (nn(normed[...], wj_ref[:, lanes]) + bias).astype(BF)
    store_permuted(normed_ref, normed[...].T, lax.axis_index("dp"), blocks)


def project_tokens(blocks, gain, shift, joint, x, wj):
    tokens = x.shape[0]
    return kernel_call(
        "project_tokens",
        functools.partial(project_kernel, blocks),
        [kept(tokens, 3 * D), kept(D, tokens)],
        (),
        (gain, shift, joint, *near(x, wj)),
        [((tokens, D), BF)],
        cost(6 * tokens * D * D),
    )


def attend_kernel(
    blocks,
    place_ref,
    out_ref,
    x_ref,
    project_ref,
    wo_ref,
    att_ref,
    context_t_ref,
    middle_ref,
    context,
):
    line, _ = token_limits(place_ref)
    masks = head_masks()
    picks = caption_masks()
    lows = [pick.astype(F32).astype(BF) for pick in picks]
    key_place = iota((SEQ, GROUP), 0).astype(F32)

    def attend(h, carry):
        at = pl.multiple_of(h * 2 * HEAD, 128)
        for g in range(x_ref.shape[0] // GROUP):
            here = slice(g * GROUP, (g + 1) * GROUP)
            query = project_ref[here, pl.ds(at, 128)]
            keys = both_heads(project_ref[here, pl.ds(pl.multiple_of(D + at, 128), 128)], masks)
            values = both_heads(
                project_ref[here, pl.ds(pl.multiple_of(2 * D + at, 128), 128)], masks
            )
            scores = nt(keys, query)
            allowed = key_place <= line[:, here]
            parts = []
            for e in range(2):
                score = compact(scores[e * GROUP : (e + 1) * GROUP], picks) * scale
                score = jnp.where(allowed, score, negative)
                score = jnp.exp(score - jnp.max(score, axis=0, keepdims=True))
                weight = score / jnp.sum(score, axis=0, keepdims=True)
                att_ref[2 * h + e, :, here] = weight
                parts.append(expand(weight.astype(BF), lows))
            context[here, pl.ds(at, 128)] = tn(jnp.concatenate(parts, axis=0), values).astype(BF)
        return carry

    lax.fori_loop(0, PAIRS, attend, 0)
    middle_ref[...] = x_ref[...].astype(F32) + (nn(context[...], wo_ref[...]) + as_row(out_ref))
    store_permuted(context_t_ref, context[...].T, lax.axis_index("dp"), blocks)


def attend_tokens(blocks, place, out, x, project, wo):
    tokens = x.shape[0]
    return kernel_call(
        "attend_tokens",
        functools.partial(attend_kernel, blocks),
        [kept(HEADS, SEQ, tokens, dtype=F32), kept(D, tokens), kept(tokens, D, dtype=F32)],
        (),
        (place, out, *near(x, project, wo)),
        [((tokens, D), BF)],
        cost(4 * tokens * D * D),
    )


def widen_kernel(
    blocks,
    place_ref,
    gain_ref,
    shift_ref,
    wide_ref,
    narrow_ref,
    middle_ref,
    wu_ref,
    wn_ref,
    wm_ref,
    second_t_ref,
    slope_ref,
    box_ref,
    text_ref,
    scale_ref,
    embed_ref,
    second,
    branch,
    wide,
    mean,
):
    captions = place_ref.shape[0]
    line, column = token_limits(place_ref)
    pool = pool_mask(line, captions)
    share = 1.0 / jnp.sum(pool, axis=1, keepdims=True)
    unit, _ = norm_parts(middle_ref[...])
    second[...] = (unit * as_row(gain_ref) + as_row(shift_ref)).astype(BF)
    store_permuted(second_t_ref, second[...].T, lax.axis_index("dp"), blocks)
    branch[...] = jnp.zeros_like(branch)
    wide[...] = as_row(wide_ref)
    pool_low = pool.astype(BF)
    c0 = 0.7978845608028654
    c1 = c0 * 0.044715
    step = 512

    def widen(i, carry):
        at = pl.multiple_of(i * step, 128)
        upper = nn(second[...], wu_ref[:, pl.ds(at, step)]) + wide[:, pl.ds(at, step)]
        square = upper * upper
        bend = jnp.tanh(upper * (c0 + c1 * square))
        half = 0.5 + 0.5 * bend
        active = upper * half
        slope_ref[:, pl.ds(at, step)] = (
            half * (1.0 + (upper - active) * (2.0 * c0 + 6.0 * c1 * square))
        ).astype(BF)
        parts = two(nn(pool_low, active.astype(BF)) * share)
        mean[:, pl.ds(at, step)] = parts[:captions]
        branch[...] += nn(parts, wn_ref[pl.ds(at, step), :])
        return carry

    lax.fori_loop(0, FF // step, widen, 0)
    inside = jnp.where((iota((captions * SEQ, 1), 0) % SEQ).astype(F32) <= column, 1.0, 0.0)
    weight = inside / (column + 1.0)
    pooled = jnp.sum((middle_ref[...] * weight).reshape(captions, SEQ, D), axis=1)
    pooled = (pooled + (branch[:captions] + branch[captions:] + as_row(narrow_ref))).astype(BF)
    hidden, part = FF // blocks, D // blocks
    for b in range(blocks):
        box_ref[b, :, :hidden] = mean[:, b * hidden : (b + 1) * hidden]
        box_ref[b, :, hidden : hidden + part] = pooled[:, b * part : (b + 1) * part]
    text = nn(pooled, wm_ref[...])
    factor = lax.rsqrt(jnp.sum(text * text, axis=1, keepdims=True) + epsilon)
    text_ref[...] = text
    scale_ref[...] = factor
    embed_ref[...] = (text * factor).astype(BF)


def widen_tokens(blocks, place, gain, shift, wide, narrow, middle, wu, wn, wm):
    tokens = middle.shape[0]
    captions = place.shape[0]
    return kernel_call(
        "widen_tokens",
        functools.partial(widen_kernel, blocks),
        [
            kept(D, tokens),
            kept(tokens, FF),
            kept(blocks, captions, box_width(blocks)),
            kept(captions, D, dtype=F32),
            kept(captions, 1, dtype=F32),
            kept(captions, D),
        ],
        (),
        (place, gain, shift, wide, narrow, *near(middle, wu, wn, wm)),
        [
            ((tokens, D), BF),
            ((2 * captions, D), F32),
            ((1, FF), F32),
            ((captions, FF), BF),
        ],
        cost(2 * tokens * D * FF),
    )


def match_of(paired, columns, images):
    column = iota((1, columns), 1)
    valid = column % SLOT < images
    name = jnp.where(valid, (column // SLOT) * images + column % SLOT, -1)
    return paired == name, valid


def contrast_kernel(
    images,
    parts,
    bits,
    heat_ref,
    own_ref,
    near_ref,
    wp_ref,
    embed_ref,
    paired_ref,
    weight_ref,
    picture_ref,
    score_ref,
    row_ref,
    inverse_ref,
    stats_ref,
    features,
):
    half = own_ref.shape[0] // SLOT
    for far, ref in enumerate((own_ref, near_ref)):

        def place(i, carry, far=far, ref=ref):
            p = i + far * half
            index = {axis: lax.axis_index(axis) for axis in ("dp", "rep")}
            for n, (axis, bit) in enumerate(bits):
                index[axis] = jnp.bitwise_xor(index[axis], ((p >> n) & 1) << bit)
            to = pl.ds(pl.multiple_of((index["dp"] * parts + index["rep"]) * SLOT, SLOT), SLOT)
            features[to, :] = ref[pl.ds(pl.multiple_of(i * SLOT, SLOT), SLOT), :]
            return carry

        lax.fori_loop(0, half, place, 0, unroll=4)
    picture = nn(features[...], wp_ref[...])
    picture = (
        picture * lax.rsqrt(jnp.sum(picture * picture, axis=1, keepdims=True) + epsilon)
    ).astype(BF)
    picture_ref[...] = picture
    score = nt(embed_ref[...], picture) / heat_ref[0]
    match, valid = match_of(as_column(paired_ref), score.shape[1], images)
    score = jnp.where(valid, score, negative)
    score_ref[...] = score
    top = jnp.max(score, axis=1, keepdims=True)
    row = jnp.log(jnp.sum(jnp.exp(score - top), axis=1, keepdims=True)) + top
    row_ref[...] = row
    positive = jnp.sum(jnp.where(match, score, 0.0), axis=1, keepdims=True)
    hits = jnp.where(match, 1.0, 0.0)
    counts = jnp.sum(hits, axis=0, keepdims=True)
    inverse = 1.0 / jnp.sum(hits * counts, axis=1, keepdims=True)
    inverse_ref[...] = inverse
    total = jnp.sum(as_column(weight_ref) * (row - positive - positive * inverse))
    best = jnp.max(score, axis=0, keepdims=True)
    mass = jnp.sum(jnp.exp(score - best), axis=0, keepdims=True)
    mass = jnp.where(iota(mass.shape, 1) == images, total, mass)
    wide = best.shape[1] // 4
    rows = [v[:, i * wide : (i + 1) * wide] for v in (best, mass) for i in range(4)]
    stats_ref[...] = jnp.concatenate(rows, axis=0)


def contrast(images, parts, bits, heat, own, far, wp, embed, paired, weight):
    captions = embed.shape[0]
    columns = 2 * own.shape[0]
    return kernel_call(
        "contrast",
        functools.partial(contrast_kernel, images, parts, bits),
        [
            kept(columns, D),
            kept(captions, columns, dtype=F32),
            kept(captions, 1, dtype=F32),
            kept(captions, 1, dtype=F32),
            shape(8, columns // 4),
        ],
        (heat,),
        (*near(own, far, wp, embed), paired, weight),
        [((columns, D), BF)],
        cost(2 * columns * D * D),
        max(LIMIT, columns * 8192),
    )


def merged(refs):
    best = functools.reduce(jnp.maximum, [ref[:4] for ref in refs])
    mass = sum(ref[4:] * jnp.exp(ref[:4] - best) for ref in refs)
    return best, mass


def merge_kernel(*refs):
    *given, out_ref = refs
    best, mass = merged(given)
    out_ref[...] = jnp.concatenate([best, mass], axis=0)


def merge(stats):
    return kernel_call("merge", merge_kernel, [shape(*stats[0].shape)], (), stats)[0]


def quarters(rep, away, flip=0):
    core = rep & 1
    out = []
    for xrel in range(2):
        for yrel in range(2):
            block = jnp.bitwise_xor(rep, 2 * xrel + away)
            x_first = 1 - core if away == flip else core
            out.append((jnp.where(x_first == 1, 2 * xrel + yrel, 2 * yrel + xrel), block, yrel))
    return out


def head_back_kernel(
    images,
    count_stats,
    rounds,
    heat_ref,
    place_ref,
    score_ref,
    row_ref,
    inverse_ref,
    weight_ref,
    paired_ref,
    picture_ref,
    text_ref,
    scale_ref,
    wm_ref,
    wn_ref,
    slope_ref,
    second_t_ref,
    box_ref,
    *refs,
):
    first = 1 << rounds[0]
    pieces = refs[len(refs) - first :]
    stats = refs[:count_stats]
    (
        back_ref,
        away_ref,
        here_ref,
        pooled_ref,
        loss_ref,
        down_bias_ref,
        up_bias_ref,
    ) = refs[count_stats : len(refs) - first]
    rep = lax.axis_index("rep")
    heat = heat_ref[0]
    captions = place_ref.shape[0]
    line, column = token_limits(place_ref)
    count = jnp.sum(pool_mask(line, captions), axis=1, keepdims=True)
    owner = spread_mask(column, captions).astype(BF)
    owner = jnp.concatenate([owner, owner], axis=1)

    score = score_ref[...]
    match, valid = match_of(as_column(paired_ref), score.shape[1], images)
    best, mass = merged(stats)
    column_log = jnp.log(mass) + best
    column_log = jnp.concatenate([column_log[i : i + 1] for i in range(4)], axis=1)
    loss_ref[...] = mass[:1, images : images + 1] + jnp.sum(
        jnp.where(valid, column_log, 0.0), axis=1, keepdims=True
    )
    weight = as_column(weight_ref)
    graded = (
        weight * jnp.exp(score - row_ref[...])
        + jnp.exp(score - column_log)
        - jnp.where(match, weight * (1.0 + inverse_ref[...]), 0.0)
    )
    graded = jnp.where(valid, graded / heat, 0.0).astype(BF)
    embed_back = nn(graded, picture_ref[...])
    text = text_ref[...]
    factor = scale_ref[...]
    text_dot = jnp.sum(text * embed_back, axis=1, keepdims=True)
    text_back = (factor * embed_back - text * (factor * factor * factor) * text_dot).astype(BF)
    blocks, _, wide = box_ref.shape
    masks = gather_masks(rounds, blocks)
    for c, piece_ref in enumerate(pieces):
        for i in range(blocks // first):
            block = jnp.bitwise_xor(lax.axis_index("dp"), masks[i * first + c])
            piece_ref[:, i * wide : (i + 1) * wide] = box_ref[block]
        piece_ref[:, (blocks // first) * wide :] = text_back
    pooled_back = nt(text_back, wm_ref[...])
    pooled_ref[...] = pooled_back
    branch = (pooled_back / count).astype(BF)
    down_bias_ref[...] = jnp.sum(branch.astype(F32) * count, axis=0, keepdims=True)
    ones = jnp.ones((SLOT, back_ref.shape[0]), BF)
    step = 512

    def widen(i, carry):
        at = pl.multiple_of(i * step, 128)
        part = nn(owner, two(nt(branch, wn_ref[pl.ds(at, step), :])))
        part = (part * slope_ref[:, pl.ds(at, step)].astype(F32)).astype(BF)
        back_ref[:, pl.ds(at, step)] = part
        up_bias_ref[:, pl.ds(at, step)] = nn(ones, part)[:1]
        return carry

    lax.fori_loop(0, FF // step, widen, 0)
    half = second_t_ref.shape[0] // 2
    wide = FF // 4
    for turn, target in enumerate((away_ref, here_ref)):
        for place, block, yrel in quarters(rep, 1 - turn):
            part = nn(
                second_t_ref[yrel * half : (yrel + 1) * half],
                back_ref[:, pl.ds(pl.multiple_of(block * wide, 128), wide)],
            )
            for h in range(2):
                target[place, h] = part[:, h * (wide // 2) : (h + 1) * (wide // 2)].astype(BF)


def head_back(images, rounds, heat, place, stats, score, row, inverse, weight, paired, picture, text,
              factor, wm, wn, slope, second_t, box):
    captions = text.shape[0]
    tokens = slope.shape[0]
    piece = (4, 2, D // 2, FF // 8)
    return kernel_call(
        "head_back",
        functools.partial(head_back_kernel, images, len(stats), rounds),
        [
            kept(tokens, FF),
            kept(*piece),
            kept(*piece),
            kept(captions, D, dtype=F32),
            shape(1, 1),
            shape(1, D),
            shape(1, FF),
        ]
        + [shape(captions, (box.shape[0] >> rounds[0]) * box.shape[2] + D, dtype=BF)] * (1 << rounds[0]),
        (heat,),
        (
            place,
            *near(score, row, inverse),
            weight,
            paired,
            *near(picture, text, factor, wm, wn, slope, second_t, box),
            *stats,
        ),
        (),
        cost(2 * tokens * D * FF),
    )


def middle_back_kernel(
    place_ref,
    gain_ref,
    pooled_ref,
    back_ref,
    wu_ref,
    middle_ref,
    wo_ref,
    total_ref,
    attended_ref,
    context_back_ref,
    gain_back_ref,
    shift_back_ref,
    bias_ref,
):
    captions = place_ref.shape[0]
    line, column = token_limits(place_ref)
    count = jnp.sum(pool_mask(line, captions), axis=1, keepdims=True)
    owner = spread_mask(column, captions).astype(BF)
    owner = jnp.concatenate([owner, owner], axis=1)
    second_back = nt(back_ref[...], wu_ref[...])
    unit, inverse = norm_parts(middle_ref[...])
    part, gain_back_ref[...], shift_back_ref[...] = norm_back(
        unit, inverse, as_row(gain_ref), second_back
    )
    total = nn(owner, two(pooled_ref[...] / count)) + part
    total_ref[...] = total
    attended = total.astype(BF)
    attended_ref[...] = attended
    bias_ref[...] = nn(jnp.ones((SLOT, attended.shape[0]), BF), attended)[:1]
    context_back_ref[...] = nt(attended, wo_ref[...]).astype(BF)


def middle_back(place, gain, pooled, back, wu, middle, wo):
    tokens = back.shape[0]
    return kernel_call(
        "middle_back",
        middle_back_kernel,
        [
            kept(tokens, D, dtype=F32),
            kept(tokens, D),
            kept(tokens, D),
            shape(1, D),
            shape(1, D),
            shape(1, D),
        ],
        (),
        (place, gain, *near(pooled, back, wu, middle, wo)),
        (),
        cost(2 * tokens * D * (FF + D)),
    )


def attention_back_kernel(project_ref, att_ref, context_back_ref, back_ref, bias_ref):
    masks = head_masks()
    picks = caption_masks()
    lows = [pick.astype(F32).astype(BF) for pick in picks]
    low_scale = jnp.asarray(scale, BF)
    first = iota((GROUP, 2 * HEAD), 1) < HEAD
    tokens = project_ref.shape[0]

    def attend(h, carry):
        at = pl.multiple_of(h * 2 * HEAD, 128)
        at_k = pl.multiple_of(D + at, 128)
        at_v = pl.multiple_of(2 * D + at, 128)
        for g in range(tokens // GROUP):
            span = slice(g * GROUP, (g + 1) * GROUP)
            query = project_ref[span, pl.ds(at, 128)]
            keys = both_heads(project_ref[span, pl.ds(at_k, 128)], masks)
            values = both_heads(project_ref[span, pl.ds(at_v, 128)], masks)
            upper = context_back_ref[span, pl.ds(at, 128)]
            full = nt(values, upper)
            weights, grads = [], []
            for e in range(2):
                weight = att_ref[2 * h + e, :, span]
                part = compact(full[e * GROUP : (e + 1) * GROUP], picks)
                grad = weight * (part - jnp.sum(weight * part, axis=0, keepdims=True))
                weights.append(expand(weight.astype(BF), lows))
                grads.append(expand(grad.astype(BF) * low_scale, lows))
            weights = jnp.concatenate(weights, axis=0)
            grads = jnp.concatenate(grads, axis=0)
            back_ref[span, pl.ds(at, 128)] = tn(grads, keys).astype(BF)
            wide = nn(grads, query)
            back_ref[span, pl.ds(at_k, 128)] = jnp.where(first, wide[:GROUP], wide[GROUP:]).astype(
                BF
            )
            wide = nn(weights, upper)
            back_ref[span, pl.ds(at_v, 128)] = jnp.where(first, wide[:GROUP], wide[GROUP:]).astype(
                BF
            )
        return carry

    lax.fori_loop(0, PAIRS, attend, 0)
    ones = jnp.ones((SLOT, tokens), BF)
    for i in range(3):
        lanes = slice(i * D, (i + 1) * D)
        bias_ref[:, lanes] = nn(ones, back_ref[:, lanes])[:1]


def attention_back(project, att, context_back):
    tokens = project.shape[0]
    return kernel_call(
        "attention_back",
        attention_back_kernel,
        [kept(tokens, 3 * D), shape(1, 3 * D)],
        (),
        near(project, att, context_back),
        (),
        cost(3 * tokens * D * D),
    )


def left_columns_kernel(back_ref, normed_t_ref, away_ref, here_ref, chosen):
    rep = lax.axis_index("rep")
    joint = 3 * D // 4
    some = chosen.shape[2]
    for r in range(4):

        @pl.when(rep == r)
        def _():
            for i, k in enumerate((1, 3, 0, 2)):
                b = r ^ k
                chosen[i] = back_ref[:, b * joint : b * joint + some]

    half = D // 2
    for turn, target in enumerate((away_ref, here_ref)):
        for i, (place, _, yrel) in enumerate(quarters(rep, 1 - turn, 1)):
            lines = slice(yrel * half, (yrel + 1) * half)
            target[place] = nn(normed_t_ref[lines], chosen[2 * turn + i // 2]).astype(BF)


def right_columns_kernel(
    back_ref, attended_ref, normed_t_ref, context_t_ref, away_ref, here_ref, chosen
):
    rep = lax.axis_index("rep")
    joint = 3 * D // 4
    out = D // 4
    some = chosen.shape[2] - out
    for r in range(4):

        @pl.when(rep == r)
        def _():
            for i, k in enumerate((1, 3, 0, 2)):
                b = r ^ k
                chosen[i, :, :some] = back_ref[:, (b + 1) * joint - some : (b + 1) * joint]
                chosen[i, :, some:] = attended_ref[:, b * out : (b + 1) * out]

    half = D // 2
    for turn, target in enumerate((away_ref, here_ref)):
        for i, (place, _, yrel) in enumerate(quarters(rep, 1 - turn)):
            block = 2 * turn + i // 2
            lines = slice(yrel * half, (yrel + 1) * half)
            target[place, :, :some] = nn(normed_t_ref[lines], chosen[block, :, :some]).astype(BF)
            target[place, :, some:] = nn(context_t_ref[lines], chosen[block, :, some:]).astype(BF)


def columns_gradient(name, body, operands):
    tokens = operands[0].shape[0]
    piece = (4, D // 2, D // 2)
    return kernel_call(
        name,
        body,
        [kept(*piece), kept(*piece)],
        (),
        near(*operands),
        [((4, tokens, D // 2), BF)],
        cost(tokens * D * FF),
    )


def token_back_kernel(
    gain_ref,
    x_ref,
    middle_ref,
    back_ref,
    wj_ref,
    joint_ref,
    out_ref,
    gain2_ref,
    shift2_ref,
    wide_ref,
    narrow_ref,
    token_ref,
    sums_ref,
):
    unit, inverse = norm_parts(x_ref[...].astype(F32))
    part, gain1, shift1 = norm_back(unit, inverse, as_row(gain_ref), nt(back_ref[...], wj_ref[...]))
    token_ref[...] = middle_ref[...] + part
    line = 0
    rest = (joint_ref, out_ref, gain2_ref, shift2_ref, wide_ref, narrow_ref)
    for value in [gain1, shift1] + [ref[...] for ref in rest]:
        for i in range(value.shape[1] // 128):
            sums_ref[line : line + 1] = value[:, i * 128 : (i + 1) * 128]
            line += 1
    sums_ref[line:] = jnp.zeros((sums_ref.shape[0] - line, 128), F32)


def token_back(gain, x, middle, back, wj, sums):
    return kernel_call(
        "token_back",
        token_back_kernel,
        [shape(x.shape[0], D), shape(ALL_LINES, 128)],
        (),
        (gain, *near(x, middle, back, wj), *sums),
        (),
        cost(6 * x.shape[0] * D * D),
    )


def low_rank_kernel(
    hidden, own_ref, near_ref, wm_ref, down_ref, head_ref, other_ref, box, back
):
    rows = own_ref.shape[0]
    box[:rows] = own_ref[...]
    box[rows:] = near_ref[...]
    part = down_ref.shape[0]
    start = box.shape[1] - D
    rep = lax.axis_index("rep")
    for r in range(D // part):

        @pl.when(rep == r)
        def _():
            for i, b in enumerate((r, r ^ 2)):
                back[i] = box[:, start + b * part : start + (b + 1) * part]

    wide = head_ref.shape[1]
    for i in range(2):
        block = jnp.bitwise_xor(rep, 2 * i)
        here = wm_ref[pl.ds(pl.multiple_of(block * part, SLOT), part), :]
        pooled = nt(box[:, start:], here).astype(BF)
        down = tn(pooled, box[:, :hidden])
        head = tn(back[i], box[:, hidden : hidden + wide])
        if i == 0:
            down_ref[...] = down
            head_ref[...] = head
        else:
            other_ref[:, :hidden] = down.astype(BF)
            other_ref[:, hidden:] = head.astype(BF)


def low_rank(blocks, parts, own, far, wm):
    rows = 2 * own.shape[0]
    hidden, wide, part = FF // blocks, D // blocks, D // parts
    return kernel_call(
        "low_rank",
        functools.partial(low_rank_kernel, hidden),
        [shape(part, hidden), shape(part, wide), shape(part, hidden + wide, dtype=BF)],
        (),
        near(own, far, wm),
        [((rows, own.shape[1]), BF), ((2, rows, part), BF)],
        cost(2 * rows * D * D),
    )


def finish_kernel(groups, *refs):
    up, first, second, lines = (
        [refs[sum(groups[:i]) + n] for n in range(groups[i])] for i in range(4)
    )
    loss_ref, down_ref, head_ref, other_ref = refs[sum(groups) : sum(groups) + 4]
    (
        joint_ref,
        out_ref,
        up_block_ref,
        down_block_ref,
        head_block_ref,
        loss_out_ref,
        *vector_refs,
    ) = refs[sum(groups) + 4 :]

    def total(terms):
        return sum(ref[...].astype(F32) for ref in terms)

    up_sum = total(up)
    for h in range(2):
        lanes = slice(h * up_sum.shape[2], (h + 1) * up_sum.shape[2])
        up_block_ref[:, lanes] = up_sum[h]
    one, two_ = total(first), total(second)
    some = one.shape[1]
    rest = joint_ref.shape[1] - some
    joint_ref[:, :some] = one
    joint_ref[:, some:] = two_[:, :rest]
    out_ref[...] = two_[:, rest:]
    hidden = down_ref.shape[1]
    down_block_ref[...] = down_ref[...] + other_ref[:, :hidden].astype(F32)
    head_block_ref[...] = (head_ref[...] + other_ref[:, hidden:].astype(F32)).T
    loss_out_ref[...] = loss_ref[...].reshape(1)
    vectors = total(lines)
    starts = (GAIN1, SHIFT1, JOINT, OUT, GAIN2, SHIFT2, WIDE, NARROW)
    for start, ref in zip(starts, vector_refs):
        for i in range(ref.shape[0] // 128):
            line = start // 128 + i
            if start == JOINT and i >= D // 128:
                line += D // 128
            ref[pl.ds(i * 128, 128)] = vectors[line]


def finish(up, first, second, vectors, loss, low, joint):
    rows = up[0].shape[1]
    sizes = (D, D, 2 * D, D, D, D, FF, D)
    return kernel_call(
        "finish",
        functools.partial(finish_kernel, [len(v) for v in (up, first, second, vectors)]),
        [
            shape(rows, joint),
            shape(rows, D - joint),
            shape(rows, D),
            shape(*low[0].shape),
            shape(*low[1].shape[::-1]),
            shape(1),
        ]
        + [shape(n) for n in sizes],
        (),
        (*up, *first, *second, *vectors, loss, *low),
    )


def both_pairs(partner):
    dp, rep = lax.axis_size("dp"), lax.axis_size("rep")
    pairs = []
    for i in range(dp):
        for j in range(rep):
            a, b = partner(i, j)
            pairs.append((i * rep + j, a * rep + b))
    return pairs


def exchange(value, partner):
    return lax.ppermute(value, ("dp", "rep"), both_pairs(partner))


def first_turn(i, j):
    return (i, j ^ 2) if j & 1 == 0 else (i ^ 1, j)


def second_turn(i, j):
    return (i ^ 1, j) if j & 1 == 0 else (i, j ^ 2)


def added(a, b):
    return (a.astype(F32) + b.astype(F32)).astype(BF)


def halved(here, got):
    half = here.shape[0] // 2
    return added(here[:half], got[:half]), added(here[half:], got[half:])


def parted(here, got, count):
    rows = here.shape[-2] // count
    parts = [slice(i * rows, (i + 1) * rows) for i in range(count)]
    return [added(here[..., p, :], got[..., p, :]) for p in parts]


def core_turn(i, j):
    return i, j ^ 1


def across(i, j):
    return i, j ^ 2


def group_round(keep, got, group):
    masks = group_masks(group)
    bits = len(group)
    parts = parted(keep, got, len(masks))
    place = [sum(((c >> n) & 1) << (bits - 1 - n) for n in range(bits)) for c in range(len(masks))]
    return [parts[0]] + [
        exchange(parts[place[c]], lambda i, j: (i ^ masks[c][0], j)) for c in range(1, len(masks))
    ]


def row_rounds(keep, got, groups):
    terms = [keep, got]
    for group in groups:
        if len(terms) > 2:
            terms = [terms[0], sum(v.astype(F32) for v in terms[1:])]
        terms = group_round(*terms, group)
    return terms


order = lax.optimization_barrier


def dp_groups():
    bits = [("dp", b) for b in range(1, lax.axis_size("dp").bit_length() - 1)]
    return [bits[i : i + 2] for i in range(0, len(bits), 2)] + [[("dp", 0)]]


def all_groups():
    bits = [("rep", b) for b in range(1, lax.axis_size("rep").bit_length() - 1)]
    groups = dp_groups()
    return groups[:-1] + [groups[-1] + bits, [("rep", 0)]]


def group_masks(group):
    out = [(0, 0)]
    for axis, bit in group:
        out += [(a | 1 << bit, b) if axis == "dp" else (a, b | 1 << bit) for a, b in out]
    return out


def gather_masks(rounds, blocks):
    bits = [0] + list(range(blocks.bit_length() - 2, 0, -1))
    masks, used = [0], 0
    for count in rounds:
        for bit in bits[used : used + count]:
            masks = masks + [m | 1 << bit for m in masks]
        used += count
    return masks


def split_round(value, wide, group):
    blocks = (value.shape[1] - D) // wide
    turns = group_masks(group)
    text = value[:, blocks * wide :]
    pieces = []
    for c, (a, b) in enumerate(turns):
        chosen = [value[:, i * wide : (i + 1) * wide] for i in range(c, blocks, len(turns))]
        piece = jnp.concatenate(chosen + [text], axis=1)
        pieces.append(piece if c == 0 else exchange(piece, lambda i, j: (i ^ a, j ^ b)))
    return pieces


def round_of(value, group):
    return [value] + [
        exchange(value, lambda i, j: (i ^ a, j ^ b)) for a, b in group_masks(group)[1:]
    ]


def relative_rows(value, blocks):
    rows = value.shape[0] // blocks
    if rows % SLOT == 0:
        return value
    bits = blocks.bit_length() - 1
    place = jnp.arange(blocks, dtype=jnp.int32)
    source = jnp.zeros_like(place)
    for bit in range(bits):
        source = source + ((place >> (bits - 1 - bit)) & 1) * (1 << bit)
    source = source ^ lax.axis_index("dp")
    return value.reshape(blocks, rows, -1)[source].reshape(value.shape)


def local(
    incoming_activations,
    caption_final_place,
    paired_picture,
    caption_weight,
    locked_picture_features,
    softmax_heat,
    premix_scaling_factor,
    premix_shift_term,
    stacked_mixing_matrix,
    asking_reading_offsets,
    mixing_result_matrix,
    mixing_result_offset,
    premlp_scaling_factor,
    premlp_shift_term,
    widening_matrix,
    widening_offset,
    narrowing_matrix,
    narrowing_offset,
    caption_mapping_matrix,
    picture_mapping_matrix,
):
    both = ("dp", "rep")
    devices = lax.axis_size(both)
    blocks = lax.axis_size("dp")
    parts = lax.axis_size("rep")
    captions = caption_final_place.shape[0]
    images = locked_picture_features.shape[0]
    groups = all_groups()
    pieces = round_of(jnp.pad(locked_picture_features, ((0, SLOT - images), (0, 0))), groups[0])
    project, normed_t = project_tokens(
        blocks,
        premix_scaling_factor,
        premix_shift_term,
        asking_reading_offsets,
        incoming_activations,
        stacked_mixing_matrix,
    )
    project, pieces = order((project, pieces))
    for group in groups[1:-1]:
        pieces = round_of(jnp.concatenate(pieces), group)
    att, context_t, middle = attend_tokens(
        blocks,
        caption_final_place,
        mixing_result_offset,
        incoming_activations,
        project,
        mixing_result_matrix,
    )
    middle, pieces = order((middle, pieces))
    own, far = round_of(jnp.concatenate(pieces), groups[-1])
    second_t, slope, box, text, factor, embed = widen_tokens(
        blocks,
        caption_final_place,
        premlp_scaling_factor,
        premlp_shift_term,
        widening_offset,
        narrowing_offset,
        middle,
        widening_matrix,
        narrowing_matrix,
        caption_mapping_matrix,
    )
    normed_t, context_t, second_t = (
        relative_rows(v, blocks) for v in (normed_t, context_t, second_t)
    )
    embed, far = order((embed, far))
    picture, score, row, inverse, stats = contrast(
        images,
        parts,
        sum(groups, []),
        softmax_heat,
        own,
        far,
        picture_mapping_matrix,
        embed,
        paired_picture,
        caption_weight,
    )
    groups = dp_groups()
    high = [[bit] for group in groups[:-1] for bit in group]
    factor_groups = groups[-1:] + high[::-1]
    stats = round_of(stats, [("rep", 0)])
    stats = round_of(merge(stats), [("rep", 1)] + groups[-1])
    for group in groups[:-1]:
        stats = round_of(merge(stats), group)
    back, away, here, pooled_back, loss, down_bias, up_bias, *pieces = head_back(
        images,
        [len(group) for group in factor_groups],
        softmax_heat,
        caption_final_place,
        stats,
        score,
        row,
        inverse,
        caption_weight,
        paired_picture,
        picture,
        text,
        factor,
        caption_mapping_matrix,
        narrowing_matrix,
        slope,
        second_t,
        box,
    )
    loss = loss / (captions * devices)
    got = exchange(away, core_turn)
    pieces = pieces[:1] + [
        exchange(piece, lambda i, j: (i ^ a, j ^ b))
        for piece, (a, b) in zip(pieces[1:], group_masks(factor_groups[0])[1:])
    ]
    total, attended, context_back, gain2, shift2, out_bias = middle_back(
        caption_final_place,
        premlp_scaling_factor,
        pooled_back,
        back,
        widening_matrix,
        middle,
        mixing_result_matrix,
    )
    context_back, got, pieces = order((context_back, got, pieces))
    up, send = halved(here, got)
    got_up = exchange(send, first_turn)
    pieces = split_round(jnp.concatenate(pieces), box.shape[2], factor_groups[1])
    project_back, joint_bias = attention_back(project, att, context_back)
    away, here = columns_gradient("left_columns", left_columns_kernel, (project_back, normed_t))
    got = exchange(away, core_turn)
    project_back, away = order((project_back, away))
    away, here2 = columns_gradient(
        "right_columns", right_columns_kernel, (project_back, attended, normed_t, context_t)
    )
    project_back, away, got, got_up, pieces = order((project_back, away, got, got_up, pieces))
    up, up_send = halved(up, got_up)
    first, send = halved(here, got)
    got = exchange(jnp.concatenate([up_send[0], send]), second_turn)
    got2 = exchange(away, core_turn)
    for group in factor_groups[2:]:
        pieces = split_round(jnp.concatenate(pieces), box.shape[2], group)
    joint = 3 * D // parts
    token, sums = token_back(
        premix_scaling_factor,
        incoming_activations,
        total,
        project_back,
        stacked_mixing_matrix,
        (joint_bias, out_bias, gain2, shift2, up_bias, down_bias),
    )
    sums, got2 = order((sums, got2))
    lines = round_of(sums, [("rep", 0)])
    second, send2 = halved(here2, got2)
    got, send2, lines, pieces = order((got, send2, lines, pieces))
    up, got_up = group_round(up[0], got[:2], high[0])
    first, send = halved(first, got[2:])
    got2 = exchange(jnp.concatenate([send2, send]), first_turn)
    lines = round_of(sum(lines), [("rep", 1)])
    factors = jnp.concatenate(pieces)
    far = exchange(factors, core_turn)
    got_up, got2, lines, far = order((got_up, got2, lines, far))
    second, send = halved(second, got2[:2])
    second, first, got = second[0], first[0], got2[2]
    got2 = exchange(send[0], second_turn)
    first, got = group_round(first, got, high[0])
    for group in high[1:]:
        up, got_up = group_round(up, got_up, group)
    lines = round_of(sum(lines), groups[-1])
    *low, other = low_rank(blocks, parts, factors, far, caption_mapping_matrix)
    other = exchange(other, across)
    for i, group in enumerate(high):
        if i:
            got_up, got2 = order((got_up, got2))
        got, got2, lines = order((got, got2, lines))
        second, got2 = group_round(second, got2, group)
        if i + 1 < len(high):
            first, got = group_round(first, got, high[i + 1])
        lines = round_of(sum(lines), group)
    first, second, up, vectors = [first, got], [second, got2], [up, got_up], lines
    joint_block, out_block, up_block, down_block, head_block, loss, *grads = finish(
        up, first, second, vectors, loss, (*low, other), joint
    )
    return (
        loss,
        token,
        grads[0],
        grads[1],
        joint_block,
        grads[2],
        out_block,
        grads[3],
        grads[4],
        grads[5],
        up_block,
        grads[6],
        down_block.T,
        grads[7],
        head_block,
    )


def solution(mesh):
    spread = P(("dp", "rep"), None)
    line = P(("dp", "rep"))
    block = P("dp", "rep")
    in_specs = (spread, line, line, line, spread) + (P(),) * 15
    out_specs = (
        P(),
        spread,
        P(),
        P(),
        block,
        P(),
        block,
        P(),
        P(),
        P(),
        block,
        P(),
        block,
        P(),
        block,
    )
    return jax.shard_map(local, mesh=mesh, in_specs=in_specs, out_specs=out_specs, check_vma=False)
```

```python
import functools

import jax
import jax.numpy as jnp
from jax import lax
from jax.experimental import pallas as pl
from jax.experimental.pallas import tpu as pltpu
from jax.sharding import PartitionSpec as P

D = 768
HEADS = 12
HEAD = 64
SEQ = 16
FF = 3072
GROUP = 128
PAIRS = HEADS // 2
SLOT = 16
BF = jnp.bfloat16
F32 = jnp.float32

epsilon = 1e-06
negative = -1e30
scale = HEAD ** (-0.5)
LIMIT = 16 * 1024 * 1024

GAIN1, SHIFT1, JOINT, OUT, GAIN2, SHIFT2, WIDE, NARROW = 0, 768, 1536, 3840, 4608, 5376, 6144, 9216
VECTORS = 9984
LINES = VECTORS // 128
ALL_LINES = LINES + -LINES % 8

vmem = pl.BlockSpec(memory_space=pltpu.VMEM)
smem = pl.BlockSpec(memory_space=pltpu.SMEM)


def dot(a, b, dims):
    return lax.dot_general(a, b, (dims, ((), ())), preferred_element_type=F32)


def nn(a, b):
    return dot(a, b, ((1,), (0,)))


def nt(a, b):
    return dot(a, b, ((1,), (1,)))


def tn(a, b):
    return dot(a, b, ((0,), (0,)))


def cost(flops):
    return pl.CostEstimate(flops=flops, transcendentals=0, bytes_accessed=0)


def shape(*dims, dtype=F32):
    return jax.ShapeDtypeStruct(dims, dtype)


def kept(*dims, dtype=BF):
    return pltpu.VMEM(dims, dtype)


def near(*values):
    return [pltpu.with_memory_space_constraint(v, pltpu.VMEM) for v in values]


def kernel_call(name, body, results, small, operands, scratch=(), estimate=None, limit=LIMIT):
    return pl.pallas_call(
        body,
        out_shape=results,
        in_specs=[smem] * len(small) + [vmem] * len(operands),
        out_specs=[vmem] * len(results),
        scratch_shapes=[pltpu.VMEM(s, t) for s, t in scratch],
        compiler_params=pltpu.CompilerParams(vmem_limit_bytes=limit),
        cost_estimate=estimate,
        name=name,
    )(*small, *operands)


def iota(dims, axis):
    return lax.broadcasted_iota(jnp.int32, dims, axis)


def norm_parts(values):
    average = jnp.mean(values, axis=-1, keepdims=True)
    centred = values - average
    inverse = lax.rsqrt(jnp.mean(centred * centred, axis=-1, keepdims=True) + epsilon)
    return centred * inverse, inverse


def norm_back(unit, inverse, gain, back):
    inner = back * gain
    part = inverse * (
        inner
        - jnp.mean(inner, axis=-1, keepdims=True)
        - unit * jnp.mean(inner * unit, axis=-1, keepdims=True)
    )
    return part, jnp.sum(back * unit, axis=0, keepdims=True), jnp.sum(back, axis=0, keepdims=True)


def split(value):
    high = value.astype(BF)
    return high, (value - high.astype(F32)).astype(BF)


def two(value):
    return jnp.concatenate(split(value), axis=0)


def as_row(ref):
    return ref[...].reshape(1, ref.shape[0])


def as_column(ref):
    size = ref.shape[0]
    same = iota((size, size), 0) == iota((size, size), 1)
    row = as_row(ref)
    return jnp.sum(jnp.where(same, row, jnp.zeros_like(row)), axis=1, keepdims=True)


def token_limits(ref):
    place = as_row(ref).astype(F32)
    captions = place.shape[1]
    tokens = captions * SEQ
    owner = (iota((tokens, captions), 0) // SEQ == iota((tokens, captions), 1)).astype(F32)
    column = jnp.sum(owner * place, axis=1, keepdims=True)
    line = nt(place.astype(BF), owner.astype(BF))
    return line, column


def pool_mask(line, captions):
    dims = (captions, captions * SEQ)
    token = iota(dims, 1)
    inside = (token % SEQ).astype(F32) <= line
    return jnp.where((token // SEQ == iota(dims, 0)) & inside, 1.0, 0.0)


def spread_mask(column, captions):
    dims = (captions * SEQ, captions)
    token = iota(dims, 0)
    inside = (token % SEQ).astype(F32) <= column
    return jnp.where((token // SEQ == iota(dims, 1)) & inside, 1.0, 0.0)


def head_masks():
    lane = iota((1, 2 * HEAD), 1)
    even = (lane < HEAD).astype(F32)
    return even.astype(BF), (1.0 - even).astype(BF)


def caption_masks():
    lane = iota((SEQ, GROUP), 1) // SEQ
    return [lane == c for c in range(GROUP // SEQ)]


def compact(full, picks):
    out = full[:SEQ]
    for c in range(1, len(picks)):
        out = jnp.where(picks[c], full[c * SEQ : (c + 1) * SEQ], out)
    return out


def expand(low, lows):
    return jnp.concatenate([low * mask for mask in lows], axis=0)


def both_heads(value, masks):
    return jnp.concatenate([value * masks[0], value * masks[1]], axis=0)


def store_permuted(ref, value, dp, blocks):
    rows = value.shape[0] // blocks
    bits = blocks.bit_length() - 1
    if rows % SLOT:
        ref[...] = value
        return
    for b in range(blocks):
        k = jnp.bitwise_xor(dp, b)
        place = 0
        for bit in range(bits):
            place = place + ((k >> bit) & 1) * (1 << (bits - 1 - bit))
        ref[pl.ds(pl.multiple_of(place * rows, SLOT), rows), :] = value[b * rows : (b + 1) * rows]


def box_width(blocks):
    used = (FF + D) // blocks
    return used + -used % 128


def project_kernel(
    blocks, gain_ref, shift_ref, joint_ref, x_ref, wj_ref, project_ref, normed_ref, normed
):
    unit, _ = norm_parts(x_ref[...].astype(F32))
    normed[...] = (unit * as_row(gain_ref) + as_row(shift_ref)).astype(BF)
    joint = as_row(joint_ref)
    for i, bias in enumerate((joint[:, :D], 0.0, joint[:, D:])):
        lanes = slice(i * D, (i + 1) * D)
        project_ref[:, lanes] = (nn(normed[...], wj_ref[:, lanes]) + bias).astype(BF)
    store_permuted(normed_ref, normed[...].T, lax.axis_index("dp"), blocks)


def project_tokens(blocks, gain, shift, joint, x, wj):
    tokens = x.shape[0]
    return kernel_call(
        "project_tokens",
        functools.partial(project_kernel, blocks),
        [kept(tokens, 3 * D), kept(D, tokens)],
        (),
        (gain, shift, joint, *near(x, wj)),
        [((tokens, D), BF)],
        cost(6 * tokens * D * D),
    )


def attend_kernel(
    blocks,
    place_ref,
    out_ref,
    x_ref,
    project_ref,
    wo_ref,
    att_ref,
    context_t_ref,
    middle_ref,
    context,
):
    line, _ = token_limits(place_ref)
    masks = head_masks()
    picks = caption_masks()
    lows = [pick.astype(F32).astype(BF) for pick in picks]
    key_place = iota((SEQ, GROUP), 0).astype(F32)

    def attend(h, carry):
        at = pl.multiple_of(h * 2 * HEAD, 128)
        for g in range(x_ref.shape[0] // GROUP):
            here = slice(g * GROUP, (g + 1) * GROUP)
            query = project_ref[here, pl.ds(at, 128)]
            keys = both_heads(project_ref[here, pl.ds(pl.multiple_of(D + at, 128), 128)], masks)
            values = both_heads(
                project_ref[here, pl.ds(pl.multiple_of(2 * D + at, 128), 128)], masks
            )
            scores = nt(keys, query)
            allowed = key_place <= line[:, here]
            parts = []
            for e in range(2):
                score = compact(scores[e * GROUP : (e + 1) * GROUP], picks) * scale
                score = jnp.where(allowed, score, negative)
                score = jnp.exp(score - jnp.max(score, axis=0, keepdims=True))
                weight = score / jnp.sum(score, axis=0, keepdims=True)
                att_ref[2 * h + e, :, here] = weight
                parts.append(expand(weight.astype(BF), lows))
            context[here, pl.ds(at, 128)] = tn(jnp.concatenate(parts, axis=0), values).astype(BF)
        return carry

    lax.fori_loop(0, PAIRS, attend, 0)
    middle_ref[...] = x_ref[...].astype(F32) + (nn(context[...], wo_ref[...]) + as_row(out_ref))
    store_permuted(context_t_ref, context[...].T, lax.axis_index("dp"), blocks)


def attend_tokens(blocks, place, out, x, project, wo):
    tokens = x.shape[0]
    return kernel_call(
        "attend_tokens",
        functools.partial(attend_kernel, blocks),
        [kept(HEADS, SEQ, tokens, dtype=F32), kept(D, tokens), kept(tokens, D, dtype=F32)],
        (),
        (place, out, *near(x, project, wo)),
        [((tokens, D), BF)],
        cost(4 * tokens * D * D),
    )


def widen_kernel(
    blocks,
    place_ref,
    gain_ref,
    shift_ref,
    wide_ref,
    narrow_ref,
    middle_ref,
    wu_ref,
    wn_ref,
    wm_ref,
    second_t_ref,
    slope_ref,
    box_ref,
    text_ref,
    scale_ref,
    embed_ref,
    second,
    branch,
    wide,
    mean,
):
    captions = place_ref.shape[0]
    line, column = token_limits(place_ref)
    pool = pool_mask(line, captions)
    share = 1.0 / jnp.sum(pool, axis=1, keepdims=True)
    unit, _ = norm_parts(middle_ref[...])
    second[...] = (unit * as_row(gain_ref) + as_row(shift_ref)).astype(BF)
    store_permuted(second_t_ref, second[...].T, lax.axis_index("dp"), blocks)
    branch[...] = jnp.zeros_like(branch)
    wide[...] = as_row(wide_ref)
    pool_low = pool.astype(BF)
    c0 = 0.7978845608028654
    c1 = c0 * 0.044715
    step = 512

    def widen(i, carry):
        at = pl.multiple_of(i * step, 128)
        upper = nn(second[...], wu_ref[:, pl.ds(at, step)]) + wide[:, pl.ds(at, step)]
        square = upper * upper
        bend = jnp.tanh(upper * (c0 + c1 * square))
        half = 0.5 + 0.5 * bend
        active = upper * half
        slope_ref[:, pl.ds(at, step)] = (
            half * (1.0 + (upper - active) * (2.0 * c0 + 6.0 * c1 * square))
        ).astype(BF)
        parts = two(nn(pool_low, active.astype(BF)) * share)
        mean[:, pl.ds(at, step)] = parts[:captions]
        branch[...] += nn(parts, wn_ref[pl.ds(at, step), :])
        return carry

    lax.fori_loop(0, FF // step, widen, 0)
    inside = jnp.where((iota((captions * SEQ, 1), 0) % SEQ).astype(F32) <= column, 1.0, 0.0)
    weight = inside / (column + 1.0)
    pooled = jnp.sum((middle_ref[...] * weight).reshape(captions, SEQ, D), axis=1)
    pooled = (pooled + (branch[:captions] + branch[captions:] + as_row(narrow_ref))).astype(BF)
    hidden, part = FF // blocks, D // blocks
    for b in range(blocks):
        box_ref[b, :, :hidden] = mean[:, b * hidden : (b + 1) * hidden]
        box_ref[b, :, hidden : hidden + part] = pooled[:, b * part : (b + 1) * part]
    text = nn(pooled, wm_ref[...])
    factor = lax.rsqrt(jnp.sum(text * text, axis=1, keepdims=True) + epsilon)
    text_ref[...] = text
    scale_ref[...] = factor
    embed_ref[...] = (text * factor).astype(BF)


def widen_tokens(blocks, place, gain, shift, wide, narrow, middle, wu, wn, wm):
    tokens = middle.shape[0]
    captions = place.shape[0]
    return kernel_call(
        "widen_tokens",
        functools.partial(widen_kernel, blocks),
        [
            kept(D, tokens),
            kept(tokens, FF),
            kept(blocks, captions, box_width(blocks)),
            kept(captions, D, dtype=F32),
            kept(captions, 1, dtype=F32),
            kept(captions, D),
        ],
        (),
        (place, gain, shift, wide, narrow, *near(middle, wu, wn, wm)),
        [
            ((tokens, D), BF),
            ((2 * captions, D), F32),
            ((1, FF), F32),
            ((captions, FF), BF),
        ],
        cost(2 * tokens * D * FF),
    )


def match_of(paired, columns, images):
    column = iota((1, columns), 1)
    valid = column % SLOT < images
    name = jnp.where(valid, (column // SLOT) * images + column % SLOT, -1)
    return paired == name, valid


def contrast_kernel(
    images,
    parts,
    bits,
    heat_ref,
    own_ref,
    near_ref,
    wp_ref,
    embed_ref,
    paired_ref,
    weight_ref,
    picture_ref,
    score_ref,
    row_ref,
    inverse_ref,
    stats_ref,
    features,
):
    half = own_ref.shape[0] // SLOT
    for far, ref in enumerate((own_ref, near_ref)):

        def place(i, carry, far=far, ref=ref):
            p = i + far * half
            index = {axis: lax.axis_index(axis) for axis in ("dp", "rep")}
            for n, (axis, bit) in enumerate(bits):
                index[axis] = jnp.bitwise_xor(index[axis], ((p >> n) & 1) << bit)
            to = pl.ds(pl.multiple_of((index["dp"] * parts + index["rep"]) * SLOT, SLOT), SLOT)
            features[to, :] = ref[pl.ds(pl.multiple_of(i * SLOT, SLOT), SLOT), :]
            return carry

        lax.fori_loop(0, half, place, 0, unroll=4)
    picture = nn(features[...], wp_ref[...])
    picture = (
        picture * lax.rsqrt(jnp.sum(picture * picture, axis=1, keepdims=True) + epsilon)
    ).astype(BF)
    picture_ref[...] = picture
    score = nt(embed_ref[...], picture) / heat_ref[0]
    match, valid = match_of(as_column(paired_ref), score.shape[1], images)
    score = jnp.where(valid, score, negative)
    score_ref[...] = score
    top = jnp.max(score, axis=1, keepdims=True)
    row = jnp.log(jnp.sum(jnp.exp(score - top), axis=1, keepdims=True)) + top
    row_ref[...] = row
    positive = jnp.sum(jnp.where(match, score, 0.0), axis=1, keepdims=True)
    hits = jnp.where(match, 1.0, 0.0)
    counts = jnp.sum(hits, axis=0, keepdims=True)
    inverse = 1.0 / jnp.sum(hits * counts, axis=1, keepdims=True)
    inverse_ref[...] = inverse
    total = jnp.sum(as_column(weight_ref) * (row - positive - positive * inverse))
    best = jnp.max(score, axis=0, keepdims=True)
    mass = jnp.sum(jnp.exp(score - best), axis=0, keepdims=True)
    mass = jnp.where(iota(mass.shape, 1) == images, total, mass)
    wide = best.shape[1] // 4
    rows = [v[:, i * wide : (i + 1) * wide] for v in (best, mass) for i in range(4)]
    stats_ref[...] = jnp.concatenate(rows, axis=0)


def contrast(images, parts, bits, heat, own, far, wp, embed, paired, weight):
    captions = embed.shape[0]
    columns = 2 * own.shape[0]
    return kernel_call(
        "contrast",
        functools.partial(contrast_kernel, images, parts, bits),
        [
            kept(columns, D),
            kept(captions, columns, dtype=F32),
            kept(captions, 1, dtype=F32),
            kept(captions, 1, dtype=F32),
            shape(8, columns // 4),
        ],
        (heat,),
        (*near(own, far, wp, embed), paired, weight),
        [((columns, D), BF)],
        cost(2 * columns * D * D),
        max(LIMIT, columns * 8192),
    )


def merged(refs):
    best = functools.reduce(jnp.maximum, [ref[:4] for ref in refs])
    mass = sum(ref[4:] * jnp.exp(ref[:4] - best) for ref in refs)
    return best, mass


def merge_kernel(*refs):
    *given, out_ref = refs
    best, mass = merged(given)
    out_ref[...] = jnp.concatenate([best, mass], axis=0)


def merge(stats):
    return kernel_call("merge", merge_kernel, [shape(*stats[0].shape)], (), stats)[0]


def quarters(rep, away, flip=0):
    core = rep & 1
    out = []
    for xrel in range(2):
        for yrel in range(2):
            block = jnp.bitwise_xor(rep, 2 * xrel + away)
            x_first = 1 - core if away == flip else core
            out.append((jnp.where(x_first == 1, 2 * xrel + yrel, 2 * yrel + xrel), block, yrel))
    return out


def head_back_kernel(
    images,
    count_stats,
    rounds,
    heat_ref,
    place_ref,
    score_ref,
    row_ref,
    inverse_ref,
    weight_ref,
    paired_ref,
    picture_ref,
    text_ref,
    scale_ref,
    wm_ref,
    wn_ref,
    slope_ref,
    second_t_ref,
    box_ref,
    *refs,
):
    first = 1 << rounds[0]
    pieces = refs[len(refs) - first :]
    stats = refs[:count_stats]
    (
        back_ref,
        away_ref,
        here_ref,
        pooled_ref,
        loss_ref,
        down_bias_ref,
        up_bias_ref,
    ) = refs[count_stats : len(refs) - first]
    rep = lax.axis_index("rep")
    heat = heat_ref[0]
    captions = place_ref.shape[0]
    line, column = token_limits(place_ref)
    count = jnp.sum(pool_mask(line, captions), axis=1, keepdims=True)
    owner = spread_mask(column, captions).astype(BF)
    owner = jnp.concatenate([owner, owner], axis=1)

    score = score_ref[...]
    match, valid = match_of(as_column(paired_ref), score.shape[1], images)
    best, mass = merged(stats)
    column_log = jnp.log(mass) + best
    column_log = jnp.concatenate([column_log[i : i + 1] for i in range(4)], axis=1)
    loss_ref[...] = mass[:1, images : images + 1] + jnp.sum(
        jnp.where(valid, column_log, 0.0), axis=1, keepdims=True
    )
    weight = as_column(weight_ref)
    graded = (
        weight * jnp.exp(score - row_ref[...])
        + jnp.exp(score - column_log)
        - jnp.where(match, weight * (1.0 + inverse_ref[...]), 0.0)
    )
    graded = jnp.where(valid, graded / heat, 0.0).astype(BF)
    embed_back = nn(graded, picture_ref[...])
    text = text_ref[...]
    factor = scale_ref[...]
    text_dot = jnp.sum(text * embed_back, axis=1, keepdims=True)
    text_back = (factor * embed_back - text * (factor * factor * factor) * text_dot).astype(BF)
    blocks, _, wide = box_ref.shape
    masks = gather_masks(rounds, blocks)
    for c, piece_ref in enumerate(pieces):
        for i in range(blocks // first):
            block = jnp.bitwise_xor(lax.axis_index("dp"), masks[i * first + c])
            piece_ref[:, i * wide : (i + 1) * wide] = box_ref[block]
        piece_ref[:, (blocks // first) * wide :] = text_back
    pooled_back = nt(text_back, wm_ref[...])
    pooled_ref[...] = pooled_back
    branch = (pooled_back / count).astype(BF)
    down_bias_ref[...] = jnp.sum(branch.astype(F32) * count, axis=0, keepdims=True)
    ones = jnp.ones((SLOT, back_ref.shape[0]), BF)
    step = 512

    def widen(i, carry):
        at = pl.multiple_of(i * step, 128)
        part = nn(owner, two(nt(branch, wn_ref[pl.ds(at, step), :])))
        part = (part * slope_ref[:, pl.ds(at, step)].astype(F32)).astype(BF)
        back_ref[:, pl.ds(at, step)] = part
        up_bias_ref[:, pl.ds(at, step)] = nn(ones, part)[:1]
        return carry

    lax.fori_loop(0, FF // step, widen, 0)
    half = second_t_ref.shape[0] // 2
    wide = FF // 4
    for turn, target in enumerate((away_ref, here_ref)):
        for place, block, yrel in quarters(rep, 1 - turn):
            part = nn(
                second_t_ref[yrel * half : (yrel + 1) * half],
                back_ref[:, pl.ds(pl.multiple_of(block * wide, 128), wide)],
            )
            for h in range(2):
                target[place, h] = part[:, h * (wide // 2) : (h + 1) * (wide // 2)].astype(BF)


def head_back(images, rounds, heat, place, stats, score, row, inverse, weight, paired, picture, text,
              factor, wm, wn, slope, second_t, box):
    captions = text.shape[0]
    tokens = slope.shape[0]
    piece = (4, 2, D // 2, FF // 8)
    return kernel_call(
        "head_back",
        functools.partial(head_back_kernel, images, len(stats), rounds),
        [
            kept(tokens, FF),
            kept(*piece),
            kept(*piece),
            kept(captions, D, dtype=F32),
            shape(1, 1),
            shape(1, D),
            shape(1, FF),
        ]
        + [shape(captions, (box.shape[0] >> rounds[0]) * box.shape[2] + D, dtype=BF)] * (1 << rounds[0]),
        (heat,),
        (
            place,
            *near(score, row, inverse),
            weight,
            paired,
            *near(picture, text, factor, wm, wn, slope, second_t, box),
            *stats,
        ),
        (),
        cost(2 * tokens * D * FF),
    )


def middle_back_kernel(
    place_ref,
    gain_ref,
    pooled_ref,
    back_ref,
    wu_ref,
    middle_ref,
    wo_ref,
    total_ref,
    attended_ref,
    context_back_ref,
    gain_back_ref,
    shift_back_ref,
    bias_ref,
):
    captions = place_ref.shape[0]
    line, column = token_limits(place_ref)
    count = jnp.sum(pool_mask(line, captions), axis=1, keepdims=True)
    owner = spread_mask(column, captions).astype(BF)
    owner = jnp.concatenate([owner, owner], axis=1)
    second_back = nt(back_ref[...], wu_ref[...])
    unit, inverse = norm_parts(middle_ref[...])
    part, gain_back_ref[...], shift_back_ref[...] = norm_back(
        unit, inverse, as_row(gain_ref), second_back
    )
    total = nn(owner, two(pooled_ref[...] / count)) + part
    total_ref[...] = total
    attended = total.astype(BF)
    attended_ref[...] = attended
    bias_ref[...] = nn(jnp.ones((SLOT, attended.shape[0]), BF), attended)[:1]
    context_back_ref[...] = nt(attended, wo_ref[...]).astype(BF)


def middle_back(place, gain, pooled, back, wu, middle, wo):
    tokens = back.shape[0]
    return kernel_call(
        "middle_back",
        middle_back_kernel,
        [
            kept(tokens, D, dtype=F32),
            kept(tokens, D),
            kept(tokens, D),
            shape(1, D),
            shape(1, D),
            shape(1, D),
        ],
        (),
        (place, gain, *near(pooled, back, wu, middle, wo)),
        (),
        cost(2 * tokens * D * (FF + D)),
    )


def attention_back_kernel(project_ref, att_ref, context_back_ref, back_ref, bias_ref):
    masks = head_masks()
    picks = caption_masks()
    lows = [pick.astype(F32).astype(BF) for pick in picks]
    low_scale = jnp.asarray(scale, BF)
    first = iota((GROUP, 2 * HEAD), 1) < HEAD
    tokens = project_ref.shape[0]

    def attend(h, carry):
        at = pl.multiple_of(h * 2 * HEAD, 128)
        at_k = pl.multiple_of(D + at, 128)
        at_v = pl.multiple_of(2 * D + at, 128)
        for g in range(tokens // GROUP):
            span = slice(g * GROUP, (g + 1) * GROUP)
            query = project_ref[span, pl.ds(at, 128)]
            keys = both_heads(project_ref[span, pl.ds(at_k, 128)], masks)
            values = both_heads(project_ref[span, pl.ds(at_v, 128)], masks)
            upper = context_back_ref[span, pl.ds(at, 128)]
            full = nt(values, upper)
            weights, grads = [], []
            for e in range(2):
                weight = att_ref[2 * h + e, :, span]
                part = compact(full[e * GROUP : (e + 1) * GROUP], picks)
                grad = weight * (part - jnp.sum(weight * part, axis=0, keepdims=True))
                weights.append(expand(weight.astype(BF), lows))
                grads.append(expand(grad.astype(BF) * low_scale, lows))
            weights = jnp.concatenate(weights, axis=0)
            grads = jnp.concatenate(grads, axis=0)
            back_ref[span, pl.ds(at, 128)] = tn(grads, keys).astype(BF)
            wide = nn(grads, query)
            back_ref[span, pl.ds(at_k, 128)] = jnp.where(first, wide[:GROUP], wide[GROUP:]).astype(
                BF
            )
            wide = nn(weights, upper)
            back_ref[span, pl.ds(at_v, 128)] = jnp.where(first, wide[:GROUP], wide[GROUP:]).astype(
                BF
            )
        return carry

    lax.fori_loop(0, PAIRS, attend, 0)
    ones = jnp.ones((SLOT, tokens), BF)
    for i in range(3):
        lanes = slice(i * D, (i + 1) * D)
        bias_ref[:, lanes] = nn(ones, back_ref[:, lanes])[:1]


def attention_back(project, att, context_back):
    tokens = project.shape[0]
    return kernel_call(
        "attention_back",
        attention_back_kernel,
        [kept(tokens, 3 * D), shape(1, 3 * D)],
        (),
        near(project, att, context_back),
        (),
        cost(3 * tokens * D * D),
    )


def left_columns_kernel(back_ref, normed_t_ref, away_ref, here_ref, chosen):
    rep = lax.axis_index("rep")
    joint = 3 * D // 4
    some = chosen.shape[2]
    for r in range(4):

        @pl.when(rep == r)
        def _():
            for i, k in enumerate((1, 3, 0, 2)):
                b = r ^ k
                chosen[i] = back_ref[:, b * joint : b * joint + some]

    half = D // 2
    for turn, target in enumerate((away_ref, here_ref)):
        for i, (place, _, yrel) in enumerate(quarters(rep, 1 - turn, 1)):
            lines = slice(yrel * half, (yrel + 1) * half)
            target[place] = nn(normed_t_ref[lines], chosen[2 * turn + i // 2]).astype(BF)


def right_columns_kernel(
    back_ref, attended_ref, normed_t_ref, context_t_ref, away_ref, here_ref, chosen
):
    rep = lax.axis_index("rep")
    joint = 3 * D // 4
    out = D // 4
    some = chosen.shape[2] - out
    for r in range(4):

        @pl.when(rep == r)
        def _():
            for i, k in enumerate((1, 3, 0, 2)):
                b = r ^ k
                chosen[i, :, :some] = back_ref[:, (b + 1) * joint - some : (b + 1) * joint]
                chosen[i, :, some:] = attended_ref[:, b * out : (b + 1) * out]

    half = D // 2
    for turn, target in enumerate((away_ref, here_ref)):
        for i, (place, _, yrel) in enumerate(quarters(rep, 1 - turn)):
            block = 2 * turn + i // 2
            lines = slice(yrel * half, (yrel + 1) * half)
            target[place, :, :some] = nn(normed_t_ref[lines], chosen[block, :, :some]).astype(BF)
            target[place, :, some:] = nn(context_t_ref[lines], chosen[block, :, some:]).astype(BF)


def columns_gradient(name, body, operands):
    tokens = operands[0].shape[0]
    piece = (4, D // 2, D // 2)
    return kernel_call(
        name,
        body,
        [kept(*piece), kept(*piece)],
        (),
        near(*operands),
        [((4, tokens, D // 2), BF)],
        cost(tokens * D * FF),
    )


def token_back_kernel(
    gain_ref,
    x_ref,
    middle_ref,
    back_ref,
    wj_ref,
    joint_ref,
    out_ref,
    gain2_ref,
    shift2_ref,
    wide_ref,
    narrow_ref,
    token_ref,
    sums_ref,
):
    unit, inverse = norm_parts(x_ref[...].astype(F32))
    part, gain1, shift1 = norm_back(unit, inverse, as_row(gain_ref), nt(back_ref[...], wj_ref[...]))
    token_ref[...] = middle_ref[...] + part
    line = 0
    rest = (joint_ref, out_ref, gain2_ref, shift2_ref, wide_ref, narrow_ref)
    for value in [gain1, shift1] + [ref[...] for ref in rest]:
        for i in range(value.shape[1] // 128):
            sums_ref[line : line + 1] = value[:, i * 128 : (i + 1) * 128]
            line += 1
    sums_ref[line:] = jnp.zeros((sums_ref.shape[0] - line, 128), F32)


def token_back(gain, x, middle, back, wj, sums):
    return kernel_call(
        "token_back",
        token_back_kernel,
        [shape(x.shape[0], D), shape(ALL_LINES, 128)],
        (),
        (gain, *near(x, middle, back, wj), *sums),
        (),
        cost(6 * x.shape[0] * D * D),
    )


def low_rank_kernel(
    hidden, own_ref, near_ref, wm_ref, down_ref, head_ref, other_ref, box, back
):
    rows = own_ref.shape[0]
    box[:rows] = own_ref[...]
    box[rows:] = near_ref[...]
    part = down_ref.shape[0]
    start = box.shape[1] - D
    rep = lax.axis_index("rep")
    for r in range(D // part):

        @pl.when(rep == r)
        def _():
            for i, b in enumerate((r, r ^ 2)):
                back[i] = box[:, start + b * part : start + (b + 1) * part]

    wide = head_ref.shape[1]
    for i in range(2):
        block = jnp.bitwise_xor(rep, 2 * i)
        here = wm_ref[pl.ds(pl.multiple_of(block * part, SLOT), part), :]
        pooled = nt(box[:, start:], here).astype(BF)
        down = tn(pooled, box[:, :hidden])
        head = tn(back[i], box[:, hidden : hidden + wide])
        if i == 0:
            down_ref[...] = down
            head_ref[...] = head
        else:
            other_ref[:, :hidden] = down.astype(BF)
            other_ref[:, hidden:] = head.astype(BF)


def low_rank(blocks, parts, own, far, wm):
    rows = 2 * own.shape[0]
    hidden, wide, part = FF // blocks, D // blocks, D // parts
    return kernel_call(
        "low_rank",
        functools.partial(low_rank_kernel, hidden),
        [shape(part, hidden), shape(part, wide), shape(part, hidden + wide, dtype=BF)],
        (),
        near(own, far, wm),
        [((rows, own.shape[1]), BF), ((2, rows, part), BF)],
        cost(2 * rows * D * D),
    )


def finish_kernel(groups, *refs):
    up, first, second, lines = (
        [refs[sum(groups[:i]) + n] for n in range(groups[i])] for i in range(4)
    )
    loss_ref, down_ref, head_ref, other_ref = refs[sum(groups) : sum(groups) + 4]
    (
        joint_ref,
        out_ref,
        up_block_ref,
        down_block_ref,
        head_block_ref,
        loss_out_ref,
        *vector_refs,
    ) = refs[sum(groups) + 4 :]

    def total(terms):
        return sum(ref[...].astype(F32) for ref in terms)

    up_sum = total(up)
    for h in range(2):
        lanes = slice(h * up_sum.shape[2], (h + 1) * up_sum.shape[2])
        up_block_ref[:, lanes] = up_sum[h]
    one, two_ = total(first), total(second)
    some = one.shape[1]
    rest = joint_ref.shape[1] - some
    joint_ref[:, :some] = one
    joint_ref[:, some:] = two_[:, :rest]
    out_ref[...] = two_[:, rest:]
    hidden = down_ref.shape[1]
    down_block_ref[...] = down_ref[...] + other_ref[:, :hidden].astype(F32)
    head_block_ref[...] = (head_ref[...] + other_ref[:, hidden:].astype(F32)).T
    loss_out_ref[...] = loss_ref[...].reshape(1)
    vectors = total(lines)
    starts = (GAIN1, SHIFT1, JOINT, OUT, GAIN2, SHIFT2, WIDE, NARROW)
    for start, ref in zip(starts, vector_refs):
        for i in range(ref.shape[0] // 128):
            line = start // 128 + i
            if start == JOINT and i >= D // 128:
                line += D // 128
            ref[pl.ds(i * 128, 128)] = vectors[line]


def finish(up, first, second, vectors, loss, low, joint):
    rows = up[0].shape[1]
    sizes = (D, D, 2 * D, D, D, D, FF, D)
    return kernel_call(
        "finish",
        functools.partial(finish_kernel, [len(v) for v in (up, first, second, vectors)]),
        [
            shape(rows, joint),
            shape(rows, D - joint),
            shape(rows, D),
            shape(*low[0].shape),
            shape(*low[1].shape[::-1]),
            shape(1),
        ]
        + [shape(n) for n in sizes],
        (),
        (*up, *first, *second, *vectors, loss, *low),
    )


def both_pairs(partner):
    dp, rep = lax.axis_size("dp"), lax.axis_size("rep")
    pairs = []
    for i in range(dp):
        for j in range(rep):
            a, b = partner(i, j)
            pairs.append((i * rep + j, a * rep + b))
    return pairs


def exchange(value, partner):
    return lax.ppermute(value, ("dp", "rep"), both_pairs(partner))


def first_turn(i, j):
    return (i, j ^ 2) if j & 1 == 0 else (i ^ 1, j)


def second_turn(i, j):
    return (i ^ 1, j) if j & 1 == 0 else (i, j ^ 2)


def added(a, b):
    return (a.astype(F32) + b.astype(F32)).astype(BF)


def halved(here, got):
    half = here.shape[0] // 2
    return added(here[:half], got[:half]), added(here[half:], got[half:])


def parted(here, got, count):
    rows = here.shape[-2] // count
    parts = [slice(i * rows, (i + 1) * rows) for i in range(count)]
    return [added(here[..., p, :], got[..., p, :]) for p in parts]


def core_turn(i, j):
    return i, j ^ 1


def across(i, j):
    return i, j ^ 2


def group_round(keep, got, group):
    masks = group_masks(group)
    bits = len(group)
    parts = parted(keep, got, len(masks))
    place = [sum(((c >> n) & 1) << (bits - 1 - n) for n in range(bits)) for c in range(len(masks))]
    return [parts[0]] + [
        exchange(parts[place[c]], lambda i, j: (i ^ masks[c][0], j)) for c in range(1, len(masks))
    ]


def row_rounds(keep, got, groups):
    terms = [keep, got]
    for group in groups:
        if len(terms) > 2:
            terms = [terms[0], sum(v.astype(F32) for v in terms[1:])]
        terms = group_round(*terms, group)
    return terms


order = lax.optimization_barrier


def dp_groups():
    bits = [("dp", b) for b in range(1, lax.axis_size("dp").bit_length() - 1)]
    return [bits[i : i + 2] for i in range(0, len(bits), 2)] + [[("dp", 0)]]


def all_groups():
    bits = [("rep", b) for b in range(1, lax.axis_size("rep").bit_length() - 1)]
    groups = dp_groups()
    return groups[:-1] + [groups[-1] + bits, [("rep", 0)]]


def group_masks(group):
    out = [(0, 0)]
    for axis, bit in group:
        out += [(a | 1 << bit, b) if axis == "dp" else (a, b | 1 << bit) for a, b in out]
    return out


def gather_masks(rounds, blocks):
    bits = [0] + list(range(blocks.bit_length() - 2, 0, -1))
    masks, used = [0], 0
    for count in rounds:
        for bit in bits[used : used + count]:
            masks = masks + [m | 1 << bit for m in masks]
        used += count
    return masks


def split_round(value, wide, group):
    blocks = (value.shape[1] - D) // wide
    turns = group_masks(group)
    text = value[:, blocks * wide :]
    pieces = []
    for c, (a, b) in enumerate(turns):
        chosen = [value[:, i * wide : (i + 1) * wide] for i in range(c, blocks, len(turns))]
        piece = jnp.concatenate(chosen + [text], axis=1)
        pieces.append(piece if c == 0 else exchange(piece, lambda i, j: (i ^ a, j ^ b)))
    return pieces


def round_of(value, group):
    return [value] + [
        exchange(value, lambda i, j: (i ^ a, j ^ b)) for a, b in group_masks(group)[1:]
    ]


def relative_rows(value, blocks):
    rows = value.shape[0] // blocks
    if rows % SLOT == 0:
        return value
    bits = blocks.bit_length() - 1
    place = jnp.arange(blocks, dtype=jnp.int32)
    source = jnp.zeros_like(place)
    for bit in range(bits):
        source = source + ((place >> (bits - 1 - bit)) & 1) * (1 << bit)
    source = source ^ lax.axis_index("dp")
    return value.reshape(blocks, rows, -1)[source].reshape(value.shape)


def local(
    incoming_activations,
    caption_final_place,
    paired_picture,
    caption_weight,
    locked_picture_features,
    softmax_heat,
    premix_scaling_factor,
    premix_shift_term,
    stacked_mixing_matrix,
    asking_reading_offsets,
    mixing_result_matrix,
    mixing_result_offset,
    premlp_scaling_factor,
    premlp_shift_term,
    widening_matrix,
    widening_offset,
    narrowing_matrix,
    narrowing_offset,
    caption_mapping_matrix,
    picture_mapping_matrix,
):
    both = ("dp", "rep")
    devices = lax.axis_size(both)
    blocks = lax.axis_size("dp")
    parts = lax.axis_size("rep")
    captions = caption_final_place.shape[0]
    images = locked_picture_features.shape[0]
    groups = all_groups()
    pieces = round_of(jnp.pad(locked_picture_features, ((0, SLOT - images), (0, 0))), groups[0])
    project, normed_t = project_tokens(
        blocks,
        premix_scaling_factor,
        premix_shift_term,
        asking_reading_offsets,
        incoming_activations,
        stacked_mixing_matrix,
    )
    project, pieces = order((project, pieces))
    for group in groups[1:-1]:
        pieces = round_of(jnp.concatenate(pieces), group)
    att, context_t, middle = attend_tokens(
        blocks,
        caption_final_place,
        mixing_result_offset,
        incoming_activations,
        project,
        mixing_result_matrix,
    )
    middle, pieces = order((middle, pieces))
    own, far = round_of(jnp.concatenate(pieces), groups[-1])
    second_t, slope, box, text, factor, embed = widen_tokens(
        blocks,
        caption_final_place,
        premlp_scaling_factor,
        premlp_shift_term,
        widening_offset,
        narrowing_offset,
        middle,
        widening_matrix,
        narrowing_matrix,
        caption_mapping_matrix,
    )
    normed_t, context_t, second_t = (
        relative_rows(v, blocks) for v in (normed_t, context_t, second_t)
    )
    embed, far = order((embed, far))
    picture, score, row, inverse, stats = contrast(
        images,
        parts,
        sum(groups, []),
        softmax_heat,
        own,
        far,
        picture_mapping_matrix,
        embed,
        paired_picture,
        caption_weight,
    )
    groups = dp_groups()
    high = [[bit] for group in groups[:-1] for bit in group]
    factor_groups = groups[-1:] + high[::-1]
    stats = round_of(stats, [("rep", 0)])
    stats = round_of(merge(stats), [("rep", 1)] + groups[-1])
    for group in groups[:-1]:
        stats = round_of(merge(stats), group)
    back, away, here, pooled_back, loss, down_bias, up_bias, *pieces = head_back(
        images,
        [len(group) for group in factor_groups],
        softmax_heat,
        caption_final_place,
        stats,
        score,
        row,
        inverse,
        caption_weight,
        paired_picture,
        picture,
        text,
        factor,
        caption_mapping_matrix,
        narrowing_matrix,
        slope,
        second_t,
        box,
    )
    loss = loss / (captions * devices)
    got = exchange(away, core_turn)
    pieces = pieces[:1] + [
        exchange(piece, lambda i, j: (i ^ a, j ^ b))
        for piece, (a, b) in zip(pieces[1:], group_masks(factor_groups[0])[1:])
    ]
    total, attended, context_back, gain2, shift2, out_bias = middle_back(
        caption_final_place,
        premlp_scaling_factor,
        pooled_back,
        back,
        widening_matrix,
        middle,
        mixing_result_matrix,
    )
    context_back, got, pieces = order((context_back, got, pieces))
    up, send = halved(here, got)
    got_up = exchange(send, first_turn)
    pieces = split_round(jnp.concatenate(pieces), box.shape[2], factor_groups[1])
    project_back, joint_bias = attention_back(project, att, context_back)
    away, here = columns_gradient("left_columns", left_columns_kernel, (project_back, normed_t))
    got = exchange(away, core_turn)
    project_back, away = order((project_back, away))
    away, here2 = columns_gradient(
        "right_columns", right_columns_kernel, (project_back, attended, normed_t, context_t)
    )
    project_back, away, got, got_up = order((project_back, away, got, got_up))
    up, up_send = halved(up, got_up)
    first, send = halved(here, got)
    got = exchange(jnp.concatenate([up_send[0], send]), second_turn)
    got2 = exchange(away, core_turn)
    joint = 3 * D // parts
    token, sums = token_back(
        premix_scaling_factor,
        incoming_activations,
        total,
        project_back,
        stacked_mixing_matrix,
        (joint_bias, out_bias, gain2, shift2, up_bias, down_bias),
    )
    sums, got2 = order((sums, got2))
    lines = round_of(sums, [("rep", 0)])
    second, send2 = halved(here2, got2)
    got, send2, lines, pieces = order((got, send2, lines, pieces))
    up, got_up = group_round(up[0], got[:2], high[0])
    first, send = halved(first, got[2:])
    got2 = exchange(jnp.concatenate([send2, send]), first_turn)
    lines = round_of(sum(lines), [("rep", 1)])
    for group in factor_groups[2:]:
        pieces = split_round(jnp.concatenate(pieces), box.shape[2], group)
    got_up, got2, lines, pieces = order((got_up, got2, lines, pieces))
    second, send = halved(second, got2[:2])
    second, first, got = second[0], first[0], got2[2]
    got2 = exchange(send[0], second_turn)
    first, got = group_round(first, got, high[0])
    for group in high[1:]:
        up, got_up = group_round(up, got_up, group)
    lines = round_of(sum(lines), groups[-1])
    factors = jnp.concatenate(pieces)
    far = exchange(factors, core_turn)
    got, got2, lines, far = order((got, got2, lines, far))
    *low, other = low_rank(blocks, parts, factors, far, caption_mapping_matrix)
    other = exchange(other, across)
    for i, group in enumerate(high):
        if i:
            got_up, got2 = order((got_up, got2))
        got, got2, lines = order((got, got2, lines))
        second, got2 = group_round(second, got2, group)
        if i + 1 < len(high):
            first, got = group_round(first, got, high[i + 1])
        lines = round_of(sum(lines), group)
    first, second, up, vectors = [first, got], [second, got2], [up, got_up], lines
    joint_block, out_block, up_block, down_block, head_block, loss, *grads = finish(
        up, first, second, vectors, loss, (*low, other), joint
    )
    return (
        loss,
        token,
        grads[0],
        grads[1],
        joint_block,
        grads[2],
        out_block,
        grads[3],
        grads[4],
        grads[5],
        up_block,
        grads[6],
        down_block.T,
        grads[7],
        head_block,
    )


def solution(mesh):
    spread = P(("dp", "rep"), None)
    line = P(("dp", "rep"))
    block = P("dp", "rep")
    in_specs = (spread, line, line, line, spread) + (P(),) * 15
    out_specs = (
        P(),
        spread,
        P(),
        P(),
        block,
        P(),
        block,
        P(),
        P(),
        P(),
        block,
        P(),
        block,
        P(),
        block,
    )
    return jax.shard_map(local, mesh=mesh, in_specs=in_specs, out_specs=out_specs, check_vma=False)
```

```python
import functools

import jax
import jax.numpy as jnp
from jax import lax
from jax.experimental import pallas as pl
from jax.experimental.pallas import tpu as pltpu
from jax.sharding import PartitionSpec as P

D = 768
HEADS = 12
HEAD = 64
SEQ = 16
FF = 3072
GROUP = 128
PAIRS = HEADS // 2
SLOT = 16
BF = jnp.bfloat16
F32 = jnp.float32

epsilon = 1e-06
negative = -1e30
scale = HEAD ** (-0.5)
LIMIT = 16 * 1024 * 1024

GAIN1, SHIFT1, JOINT, OUT, GAIN2, SHIFT2, WIDE, NARROW = 0, 768, 1536, 3840, 4608, 5376, 6144, 9216
VECTORS = 9984
LINES = VECTORS // 128
ALL_LINES = LINES + -LINES % 8

vmem = pl.BlockSpec(memory_space=pltpu.VMEM)
smem = pl.BlockSpec(memory_space=pltpu.SMEM)


def dot(a, b, dims):
    return lax.dot_general(a, b, (dims, ((), ())), preferred_element_type=F32)


def nn(a, b):
    return dot(a, b, ((1,), (0,)))


def nt(a, b):
    return dot(a, b, ((1,), (1,)))


def tn(a, b):
    return dot(a, b, ((0,), (0,)))


def cost(flops):
    return pl.CostEstimate(flops=flops // 10, transcendentals=0, bytes_accessed=0)


def shape(*dims, dtype=F32):
    return jax.ShapeDtypeStruct(dims, dtype)


def kept(*dims, dtype=BF):
    return pltpu.VMEM(dims, dtype)


def near(*values):
    return [pltpu.with_memory_space_constraint(v, pltpu.VMEM) for v in values]


def kernel_call(name, body, results, small, operands, scratch=(), estimate=None, limit=LIMIT):
    return pl.pallas_call(
        body,
        out_shape=results,
        in_specs=[smem] * len(small) + [vmem] * len(operands),
        out_specs=[vmem] * len(results),
        scratch_shapes=[pltpu.VMEM(s, t) for s, t in scratch],
        compiler_params=pltpu.CompilerParams(vmem_limit_bytes=limit),
        cost_estimate=estimate,
        name=name,
    )(*small, *operands)


def iota(dims, axis):
    return lax.broadcasted_iota(jnp.int32, dims, axis)


def norm_parts(values):
    average = jnp.mean(values, axis=-1, keepdims=True)
    centred = values - average
    inverse = lax.rsqrt(jnp.mean(centred * centred, axis=-1, keepdims=True) + epsilon)
    return centred * inverse, inverse


def norm_back(unit, inverse, gain, back):
    inner = back * gain
    part = inverse * (
        inner
        - jnp.mean(inner, axis=-1, keepdims=True)
        - unit * jnp.mean(inner * unit, axis=-1, keepdims=True)
    )
    return part, jnp.sum(back * unit, axis=0, keepdims=True), jnp.sum(back, axis=0, keepdims=True)


def split(value):
    high = value.astype(BF)
    return high, (value - high.astype(F32)).astype(BF)


def two(value):
    return jnp.concatenate(split(value), axis=0)


def as_row(ref):
    return ref[...].reshape(1, ref.shape[0])


def as_column(ref):
    size = ref.shape[0]
    same = iota((size, size), 0) == iota((size, size), 1)
    row = as_row(ref)
    return jnp.sum(jnp.where(same, row, jnp.zeros_like(row)), axis=1, keepdims=True)


def token_limits(ref):
    place = as_row(ref).astype(F32)
    captions = place.shape[1]
    tokens = captions * SEQ
    owner = (iota((tokens, captions), 0) // SEQ == iota((tokens, captions), 1)).astype(F32)
    column = jnp.sum(owner * place, axis=1, keepdims=True)
    line = nt(place.astype(BF), owner.astype(BF))
    return line, column


def pool_mask(line, captions):
    dims = (captions, captions * SEQ)
    token = iota(dims, 1)
    inside = (token % SEQ).astype(F32) <= line
    return jnp.where((token // SEQ == iota(dims, 0)) & inside, 1.0, 0.0)


def spread_mask(column, captions):
    dims = (captions * SEQ, captions)
    token = iota(dims, 0)
    inside = (token % SEQ).astype(F32) <= column
    return jnp.where((token // SEQ == iota(dims, 1)) & inside, 1.0, 0.0)


def head_masks():
    lane = iota((1, 2 * HEAD), 1)
    even = (lane < HEAD).astype(F32)
    return even.astype(BF), (1.0 - even).astype(BF)


def caption_masks():
    lane = iota((SEQ, GROUP), 1) // SEQ
    return [lane == c for c in range(GROUP // SEQ)]


def compact(full, picks):
    out = full[:SEQ]
    for c in range(1, len(picks)):
        out = jnp.where(picks[c], full[c * SEQ : (c + 1) * SEQ], out)
    return out


def expand(low, lows):
    return jnp.concatenate([low * mask for mask in lows], axis=0)


def both_heads(value, masks):
    return jnp.concatenate([value * masks[0], value * masks[1]], axis=0)


def store_permuted(ref, value, dp, blocks):
    rows = value.shape[0] // blocks
    bits = blocks.bit_length() - 1
    if rows % SLOT:
        ref[...] = value
        return
    for b in range(blocks):
        k = jnp.bitwise_xor(dp, b)
        place = 0
        for bit in range(bits):
            place = place + ((k >> bit) & 1) * (1 << (bits - 1 - bit))
        ref[pl.ds(pl.multiple_of(place * rows, SLOT), rows), :] = value[b * rows : (b + 1) * rows]


def box_width(blocks):
    used = (FF + D) // blocks
    return used + -used % 128


def project_kernel(
    blocks, gain_ref, shift_ref, joint_ref, x_ref, wj_ref, project_ref, normed_ref, normed
):
    unit, _ = norm_parts(x_ref[...].astype(F32))
    normed[...] = (unit * as_row(gain_ref) + as_row(shift_ref)).astype(BF)
    joint = as_row(joint_ref)
    for i, bias in enumerate((joint[:, :D], 0.0, joint[:, D:])):
        lanes = slice(i * D, (i + 1) * D)
        project_ref[:, lanes] = (nn(normed[...], wj_ref[:, lanes]) + bias).astype(BF)
    store_permuted(normed_ref, normed[...].T, lax.axis_index("dp"), blocks)


def project_tokens(blocks, gain, shift, joint, x, wj):
    tokens = x.shape[0]
    return kernel_call(
        "project_tokens",
        functools.partial(project_kernel, blocks),
        [kept(tokens, 3 * D), kept(D, tokens)],
        (),
        (gain, shift, joint, *near(x, wj)),
        [((tokens, D), BF)],
        cost(6 * tokens * D * D),
    )


def attend_kernel(
    blocks,
    place_ref,
    out_ref,
    x_ref,
    project_ref,
    wo_ref,
    att_ref,
    context_t_ref,
    middle_ref,
    context,
):
    line, _ = token_limits(place_ref)
    masks = head_masks()
    picks = caption_masks()
    lows = [pick.astype(F32).astype(BF) for pick in picks]
    key_place = iota((SEQ, GROUP), 0).astype(F32)

    def attend(h, carry):
        at = pl.multiple_of(h * 2 * HEAD, 128)
        for g in range(x_ref.shape[0] // GROUP):
            here = slice(g * GROUP, (g + 1) * GROUP)
            query = project_ref[here, pl.ds(at, 128)]
            keys = both_heads(project_ref[here, pl.ds(pl.multiple_of(D + at, 128), 128)], masks)
            values = both_heads(
                project_ref[here, pl.ds(pl.multiple_of(2 * D + at, 128), 128)], masks
            )
            scores = nt(keys, query)
            allowed = key_place <= line[:, here]
            parts = []
            for e in range(2):
                score = compact(scores[e * GROUP : (e + 1) * GROUP], picks) * scale
                score = jnp.where(allowed, score, negative)
                score = jnp.exp(score - jnp.max(score, axis=0, keepdims=True))
                weight = score / jnp.sum(score, axis=0, keepdims=True)
                att_ref[2 * h + e, :, here] = weight
                parts.append(expand(weight.astype(BF), lows))
            context[here, pl.ds(at, 128)] = tn(jnp.concatenate(parts, axis=0), values).astype(BF)
        return carry

    lax.fori_loop(0, PAIRS, attend, 0)
    middle_ref[...] = x_ref[...].astype(F32) + (nn(context[...], wo_ref[...]) + as_row(out_ref))
    store_permuted(context_t_ref, context[...].T, lax.axis_index("dp"), blocks)


def attend_tokens(blocks, place, out, x, project, wo):
    tokens = x.shape[0]
    return kernel_call(
        "attend_tokens",
        functools.partial(attend_kernel, blocks),
        [kept(HEADS, SEQ, tokens, dtype=F32), kept(D, tokens), kept(tokens, D, dtype=F32)],
        (),
        (place, out, *near(x, project, wo)),
        [((tokens, D), BF)],
        cost(4 * tokens * D * D),
    )


def widen_kernel(
    blocks,
    place_ref,
    gain_ref,
    shift_ref,
    wide_ref,
    narrow_ref,
    middle_ref,
    wu_ref,
    wn_ref,
    wm_ref,
    second_t_ref,
    slope_ref,
    box_ref,
    text_ref,
    scale_ref,
    embed_ref,
    second,
    branch,
    wide,
    mean,
):
    captions = place_ref.shape[0]
    line, column = token_limits(place_ref)
    pool = pool_mask(line, captions)
    share = 1.0 / jnp.sum(pool, axis=1, keepdims=True)
    unit, _ = norm_parts(middle_ref[...])
    second[...] = (unit * as_row(gain_ref) + as_row(shift_ref)).astype(BF)
    store_permuted(second_t_ref, second[...].T, lax.axis_index("dp"), blocks)
    branch[...] = jnp.zeros_like(branch)
    wide[...] = as_row(wide_ref)
    pool_low = pool.astype(BF)
    c0 = 0.7978845608028654
    c1 = c0 * 0.044715
    step = 512

    def widen(i, carry):
        at = pl.multiple_of(i * step, 128)
        upper = nn(second[...], wu_ref[:, pl.ds(at, step)]) + wide[:, pl.ds(at, step)]
        square = upper * upper
        bend = jnp.tanh(upper * (c0 + c1 * square))
        half = 0.5 + 0.5 * bend
        active = upper * half
        slope_ref[:, pl.ds(at, step)] = (
            half * (1.0 + (upper - active) * (2.0 * c0 + 6.0 * c1 * square))
        ).astype(BF)
        parts = two(nn(pool_low, active.astype(BF)) * share)
        mean[:, pl.ds(at, step)] = parts[:captions]
        branch[...] += nn(parts, wn_ref[pl.ds(at, step), :])
        return carry

    lax.fori_loop(0, FF // step, widen, 0)
    inside = jnp.where((iota((captions * SEQ, 1), 0) % SEQ).astype(F32) <= column, 1.0, 0.0)
    weight = inside / (column + 1.0)
    pooled = jnp.sum((middle_ref[...] * weight).reshape(captions, SEQ, D), axis=1)
    pooled = (pooled + (branch[:captions] + branch[captions:] + as_row(narrow_ref))).astype(BF)
    hidden, part = FF // blocks, D // blocks
    for b in range(blocks):
        box_ref[b, :, :hidden] = mean[:, b * hidden : (b + 1) * hidden]
        box_ref[b, :, hidden : hidden + part] = pooled[:, b * part : (b + 1) * part]
    text = nn(pooled, wm_ref[...])
    factor = lax.rsqrt(jnp.sum(text * text, axis=1, keepdims=True) + epsilon)
    text_ref[...] = text
    scale_ref[...] = factor
    embed_ref[...] = (text * factor).astype(BF)


def widen_tokens(blocks, place, gain, shift, wide, narrow, middle, wu, wn, wm):
    tokens = middle.shape[0]
    captions = place.shape[0]
    return kernel_call(
        "widen_tokens",
        functools.partial(widen_kernel, blocks),
        [
            kept(D, tokens),
            kept(tokens, FF),
            kept(blocks, captions, box_width(blocks)),
            kept(captions, D, dtype=F32),
            kept(captions, 1, dtype=F32),
            kept(captions, D),
        ],
        (),
        (place, gain, shift, wide, narrow, *near(middle, wu, wn, wm)),
        [
            ((tokens, D), BF),
            ((2 * captions, D), F32),
            ((1, FF), F32),
            ((captions, FF), BF),
        ],
        cost(2 * tokens * D * FF),
    )


def match_of(paired, columns, images):
    column = iota((1, columns), 1)
    valid = column % SLOT < images
    name = jnp.where(valid, (column // SLOT) * images + column % SLOT, -1)
    return paired == name, valid


def contrast_kernel(
    images,
    parts,
    bits,
    heat_ref,
    own_ref,
    near_ref,
    wp_ref,
    embed_ref,
    paired_ref,
    weight_ref,
    picture_ref,
    score_ref,
    row_ref,
    inverse_ref,
    stats_ref,
    features,
):
    half = own_ref.shape[0] // SLOT
    for far, ref in enumerate((own_ref, near_ref)):

        def place(i, carry, far=far, ref=ref):
            p = i + far * half
            index = {axis: lax.axis_index(axis) for axis in ("dp", "rep")}
            for n, (axis, bit) in enumerate(bits):
                index[axis] = jnp.bitwise_xor(index[axis], ((p >> n) & 1) << bit)
            to = pl.ds(pl.multiple_of((index["dp"] * parts + index["rep"]) * SLOT, SLOT), SLOT)
            features[to, :] = ref[pl.ds(pl.multiple_of(i * SLOT, SLOT), SLOT), :]
            return carry

        lax.fori_loop(0, half, place, 0, unroll=4)
    picture = nn(features[...], wp_ref[...])
    picture = (
        picture * lax.rsqrt(jnp.sum(picture * picture, axis=1, keepdims=True) + epsilon)
    ).astype(BF)
    picture_ref[...] = picture
    score = nt(embed_ref[...], picture) / heat_ref[0]
    match, valid = match_of(as_column(paired_ref), score.shape[1], images)
    score = jnp.where(valid, score, negative)
    score_ref[...] = score
    top = jnp.max(score, axis=1, keepdims=True)
    row = jnp.log(jnp.sum(jnp.exp(score - top), axis=1, keepdims=True)) + top
    row_ref[...] = row
    positive = jnp.sum(jnp.where(match, score, 0.0), axis=1, keepdims=True)
    hits = jnp.where(match, 1.0, 0.0)
    counts = jnp.sum(hits, axis=0, keepdims=True)
    inverse = 1.0 / jnp.sum(hits * counts, axis=1, keepdims=True)
    inverse_ref[...] = inverse
    total = jnp.sum(as_column(weight_ref) * (row - positive - positive * inverse))
    best = jnp.max(score, axis=0, keepdims=True)
    mass = jnp.sum(jnp.exp(score - best), axis=0, keepdims=True)
    mass = jnp.where(iota(mass.shape, 1) == images, total, mass)
    wide = best.shape[1] // 4
    rows = [v[:, i * wide : (i + 1) * wide] for v in (best, mass) for i in range(4)]
    stats_ref[...] = jnp.concatenate(rows, axis=0)


def contrast(images, parts, bits, heat, own, far, wp, embed, paired, weight):
    captions = embed.shape[0]
    columns = 2 * own.shape[0]
    return kernel_call(
        "contrast",
        functools.partial(contrast_kernel, images, parts, bits),
        [
            kept(columns, D),
            kept(captions, columns, dtype=F32),
            kept(captions, 1, dtype=F32),
            kept(captions, 1, dtype=F32),
            shape(8, columns // 4),
        ],
        (heat,),
        (*near(own, far, wp, embed), paired, weight),
        [((columns, D), BF)],
        cost(2 * columns * D * D),
        max(LIMIT, columns * 8192),
    )


def merged(refs):
    best = functools.reduce(jnp.maximum, [ref[:4] for ref in refs])
    mass = sum(ref[4:] * jnp.exp(ref[:4] - best) for ref in refs)
    return best, mass


def merge_kernel(*refs):
    *given, out_ref = refs
    best, mass = merged(given)
    out_ref[...] = jnp.concatenate([best, mass], axis=0)


def merge(stats):
    return kernel_call("merge", merge_kernel, [shape(*stats[0].shape)], (), stats)[0]


def quarters(rep, away, flip=0):
    core = rep & 1
    out = []
    for xrel in range(2):
        for yrel in range(2):
            block = jnp.bitwise_xor(rep, 2 * xrel + away)
            x_first = 1 - core if away == flip else core
            out.append((jnp.where(x_first == 1, 2 * xrel + yrel, 2 * yrel + xrel), block, yrel))
    return out


def head_back_kernel(
    images,
    count_stats,
    rounds,
    heat_ref,
    place_ref,
    score_ref,
    row_ref,
    inverse_ref,
    weight_ref,
    paired_ref,
    picture_ref,
    text_ref,
    scale_ref,
    wm_ref,
    wn_ref,
    slope_ref,
    second_t_ref,
    box_ref,
    *refs,
):
    first = 1 << rounds[0]
    pieces = refs[len(refs) - first :]
    stats = refs[:count_stats]
    (
        back_ref,
        away_ref,
        here_ref,
        pooled_ref,
        loss_ref,
        down_bias_ref,
        up_bias_ref,
    ) = refs[count_stats : len(refs) - first]
    rep = lax.axis_index("rep")
    heat = heat_ref[0]
    captions = place_ref.shape[0]
    line, column = token_limits(place_ref)
    count = jnp.sum(pool_mask(line, captions), axis=1, keepdims=True)
    owner = spread_mask(column, captions).astype(BF)
    owner = jnp.concatenate([owner, owner], axis=1)

    score = score_ref[...]
    match, valid = match_of(as_column(paired_ref), score.shape[1], images)
    best, mass = merged(stats)
    column_log = jnp.log(mass) + best
    column_log = jnp.concatenate([column_log[i : i + 1] for i in range(4)], axis=1)
    loss_ref[...] = mass[:1, images : images + 1] + jnp.sum(
        jnp.where(valid, column_log, 0.0), axis=1, keepdims=True
    )
    weight = as_column(weight_ref)
    graded = (
        weight * jnp.exp(score - row_ref[...])
        + jnp.exp(score - column_log)
        - jnp.where(match, weight * (1.0 + inverse_ref[...]), 0.0)
    )
    graded = jnp.where(valid, graded / heat, 0.0).astype(BF)
    embed_back = nn(graded, picture_ref[...])
    text = text_ref[...]
    factor = scale_ref[...]
    text_dot = jnp.sum(text * embed_back, axis=1, keepdims=True)
    text_back = (factor * embed_back - text * (factor * factor * factor) * text_dot).astype(BF)
    blocks, _, wide = box_ref.shape
    masks = gather_masks(rounds, blocks)
    for c, piece_ref in enumerate(pieces):
        for i in range(blocks // first):
            block = jnp.bitwise_xor(lax.axis_index("dp"), masks[i * first + c])
            piece_ref[:, i * wide : (i + 1) * wide] = box_ref[block]
        piece_ref[:, (blocks // first) * wide :] = text_back
    pooled_back = nt(text_back, wm_ref[...])
    pooled_ref[...] = pooled_back
    branch = (pooled_back / count).astype(BF)
    down_bias_ref[...] = jnp.sum(branch.astype(F32) * count, axis=0, keepdims=True)
    ones = jnp.ones((SLOT, back_ref.shape[0]), BF)
    step = 512

    def widen(i, carry):
        at = pl.multiple_of(i * step, 128)
        part = nn(owner, two(nt(branch, wn_ref[pl.ds(at, step), :])))
        part = (part * slope_ref[:, pl.ds(at, step)].astype(F32)).astype(BF)
        back_ref[:, pl.ds(at, step)] = part
        up_bias_ref[:, pl.ds(at, step)] = nn(ones, part)[:1]
        return carry

    lax.fori_loop(0, FF // step, widen, 0)
    half = second_t_ref.shape[0] // 2
    wide = FF // 4
    for turn, target in enumerate((away_ref, here_ref)):
        for place, block, yrel in quarters(rep, 1 - turn):
            part = nn(
                second_t_ref[yrel * half : (yrel + 1) * half],
                back_ref[:, pl.ds(pl.multiple_of(block * wide, 128), wide)],
            )
            for h in range(2):
                target[h, place] = part[:, h * (wide // 2) : (h + 1) * (wide // 2)].astype(BF)


def head_back(images, rounds, heat, place, stats, score, row, inverse, weight, paired, picture, text,
              factor, wm, wn, slope, second_t, box):
    captions = text.shape[0]
    tokens = slope.shape[0]
    piece = (2, 4, D // 2, FF // 8)
    return kernel_call(
        "head_back",
        functools.partial(head_back_kernel, images, len(stats), rounds),
        [
            kept(tokens, FF),
            kept(*piece),
            kept(*piece),
            kept(captions, D, dtype=F32),
            shape(1, 1),
            shape(1, D),
            shape(1, FF),
        ]
        + [shape(captions, (box.shape[0] >> rounds[0]) * box.shape[2] + D, dtype=BF)] * (1 << rounds[0]),
        (heat,),
        (
            place,
            *near(score, row, inverse),
            weight,
            paired,
            *near(picture, text, factor, wm, wn, slope, second_t, box),
            *stats,
        ),
        (),
        cost(2 * tokens * D * FF),
    )


def middle_back_kernel(
    place_ref,
    gain_ref,
    pooled_ref,
    back_ref,
    wu_ref,
    middle_ref,
    wo_ref,
    total_ref,
    attended_ref,
    context_back_ref,
    gain_back_ref,
    shift_back_ref,
    bias_ref,
):
    captions = place_ref.shape[0]
    line, column = token_limits(place_ref)
    count = jnp.sum(pool_mask(line, captions), axis=1, keepdims=True)
    owner = spread_mask(column, captions).astype(BF)
    owner = jnp.concatenate([owner, owner], axis=1)
    second_back = nt(back_ref[...], wu_ref[...])
    unit, inverse = norm_parts(middle_ref[...])
    part, gain_back_ref[...], shift_back_ref[...] = norm_back(
        unit, inverse, as_row(gain_ref), second_back
    )
    total = nn(owner, two(pooled_ref[...] / count)) + part
    total_ref[...] = total
    attended = total.astype(BF)
    attended_ref[...] = attended
    bias_ref[...] = nn(jnp.ones((SLOT, attended.shape[0]), BF), attended)[:1]
    context_back_ref[...] = nt(attended, wo_ref[...]).astype(BF)


def middle_back(place, gain, pooled, back, wu, middle, wo):
    tokens = back.shape[0]
    return kernel_call(
        "middle_back",
        middle_back_kernel,
        [
            kept(tokens, D, dtype=F32),
            kept(tokens, D),
            kept(tokens, D),
            shape(1, D),
            shape(1, D),
            shape(1, D),
        ],
        (),
        (place, gain, *near(pooled, back, wu, middle, wo)),
        (),
        cost(2 * tokens * D * (FF + D)),
    )


def attention_back_kernel(project_ref, att_ref, context_back_ref, back_ref, bias_ref):
    masks = head_masks()
    picks = caption_masks()
    lows = [pick.astype(F32).astype(BF) for pick in picks]
    low_scale = jnp.asarray(scale, BF)
    first = iota((GROUP, 2 * HEAD), 1) < HEAD
    tokens = project_ref.shape[0]

    def attend(h, carry):
        at = pl.multiple_of(h * 2 * HEAD, 128)
        at_k = pl.multiple_of(D + at, 128)
        at_v = pl.multiple_of(2 * D + at, 128)
        for g in range(tokens // GROUP):
            span = slice(g * GROUP, (g + 1) * GROUP)
            query = project_ref[span, pl.ds(at, 128)]
            keys = both_heads(project_ref[span, pl.ds(at_k, 128)], masks)
            values = both_heads(project_ref[span, pl.ds(at_v, 128)], masks)
            upper = context_back_ref[span, pl.ds(at, 128)]
            full = nt(values, upper)
            weights, grads = [], []
            for e in range(2):
                weight = att_ref[2 * h + e, :, span]
                part = compact(full[e * GROUP : (e + 1) * GROUP], picks)
                grad = weight * (part - jnp.sum(weight * part, axis=0, keepdims=True))
                weights.append(expand(weight.astype(BF), lows))
                grads.append(expand(grad.astype(BF) * low_scale, lows))
            weights = jnp.concatenate(weights, axis=0)
            grads = jnp.concatenate(grads, axis=0)
            back_ref[span, pl.ds(at, 128)] = tn(grads, keys).astype(BF)
            wide = nn(grads, query)
            back_ref[span, pl.ds(at_k, 128)] = jnp.where(first, wide[:GROUP], wide[GROUP:]).astype(
                BF
            )
            wide = nn(weights, upper)
            back_ref[span, pl.ds(at_v, 128)] = jnp.where(first, wide[:GROUP], wide[GROUP:]).astype(
                BF
            )
        return carry

    lax.fori_loop(0, PAIRS, attend, 0)
    ones = jnp.ones((SLOT, tokens), BF)
    for i in range(3):
        lanes = slice(i * D, (i + 1) * D)
        bias_ref[:, lanes] = nn(ones, back_ref[:, lanes])[:1]


def attention_back(project, att, context_back):
    tokens = project.shape[0]
    return kernel_call(
        "attention_back",
        attention_back_kernel,
        [kept(tokens, 3 * D), shape(1, 3 * D)],
        (),
        near(project, att, context_back),
        (),
        cost(3 * tokens * D * D),
    )


def left_columns_kernel(back_ref, normed_t_ref, away_ref, here_ref, chosen):
    rep = lax.axis_index("rep")
    joint = 3 * D // 4
    some = chosen.shape[2]
    for r in range(4):

        @pl.when(rep == r)
        def _():
            for i, k in enumerate((1, 3, 0, 2)):
                b = r ^ k
                chosen[i] = back_ref[:, b * joint : b * joint + some]

    half = D // 2
    for turn, target in enumerate((away_ref, here_ref)):
        for i, (place, _, yrel) in enumerate(quarters(rep, 1 - turn, 1)):
            lines = slice(yrel * half, (yrel + 1) * half)
            target[place] = nn(normed_t_ref[lines], chosen[2 * turn + i // 2]).astype(BF)


def right_columns_kernel(
    back_ref, attended_ref, normed_t_ref, context_t_ref, away_ref, here_ref, chosen
):
    rep = lax.axis_index("rep")
    joint = 3 * D // 4
    out = D // 4
    some = chosen.shape[2] - out
    for r in range(4):

        @pl.when(rep == r)
        def _():
            for i, k in enumerate((1, 3, 0, 2)):
                b = r ^ k
                chosen[i, :, :some] = back_ref[:, (b + 1) * joint - some : (b + 1) * joint]
                chosen[i, :, some:] = attended_ref[:, b * out : (b + 1) * out]

    half = D // 2
    for turn, target in enumerate((away_ref, here_ref)):
        for i, (place, _, yrel) in enumerate(quarters(rep, 1 - turn)):
            block = 2 * turn + i // 2
            lines = slice(yrel * half, (yrel + 1) * half)
            target[place, :, :some] = nn(normed_t_ref[lines], chosen[block, :, :some]).astype(BF)
            target[place, :, some:] = nn(context_t_ref[lines], chosen[block, :, some:]).astype(BF)


def columns_gradient(name, body, operands):
    tokens = operands[0].shape[0]
    piece = (4, D // 2, D // 2)
    return kernel_call(
        name,
        body,
        [kept(*piece), kept(*piece)],
        (),
        near(*operands),
        [((4, tokens, D // 2), BF)],
        cost(tokens * D * FF),
    )


def token_back_kernel(
    gain_ref,
    x_ref,
    middle_ref,
    back_ref,
    wj_ref,
    joint_ref,
    out_ref,
    gain2_ref,
    shift2_ref,
    wide_ref,
    narrow_ref,
    token_ref,
    sums_ref,
):
    unit, inverse = norm_parts(x_ref[...].astype(F32))
    part, gain1, shift1 = norm_back(unit, inverse, as_row(gain_ref), nt(back_ref[...], wj_ref[...]))
    token_ref[...] = middle_ref[...] + part
    line = 0
    rest = (joint_ref, out_ref, gain2_ref, shift2_ref, wide_ref, narrow_ref)
    for value in [gain1, shift1] + [ref[...] for ref in rest]:
        for i in range(value.shape[1] // 128):
            sums_ref[line : line + 1] = value[:, i * 128 : (i + 1) * 128]
            line += 1
    sums_ref[line:] = jnp.zeros((sums_ref.shape[0] - line, 128), F32)


def token_back(gain, x, middle, back, wj, sums):
    return kernel_call(
        "token_back",
        token_back_kernel,
        [shape(x.shape[0], D), shape(ALL_LINES, 128)],
        (),
        (gain, *near(x, middle, back, wj), *sums),
        (),
        cost(6 * x.shape[0] * D * D),
    )


def low_rank_kernel(
    hidden, own_ref, near_ref, wm_ref, down_ref, head_ref, other_ref, box, back
):
    rows = own_ref.shape[0]
    box[:rows] = own_ref[...]
    box[rows:] = near_ref[...]
    part = down_ref.shape[0]
    start = box.shape[1] - D
    rep = lax.axis_index("rep")
    for r in range(D // part):

        @pl.when(rep == r)
        def _():
            for i, b in enumerate((r, r ^ 2)):
                back[i] = box[:, start + b * part : start + (b + 1) * part]

    wide = head_ref.shape[1]
    for i in range(2):
        block = jnp.bitwise_xor(rep, 2 * i)
        here = wm_ref[pl.ds(pl.multiple_of(block * part, SLOT), part), :]
        pooled = nt(box[:, start:], here).astype(BF)
        down = tn(pooled, box[:, :hidden])
        head = tn(back[i], box[:, hidden : hidden + wide])
        if i == 0:
            down_ref[...] = down
            head_ref[...] = head
        else:
            other_ref[:, :hidden] = down.astype(BF)
            other_ref[:, hidden:] = head.astype(BF)


def low_rank(blocks, parts, own, far, wm):
    rows = 2 * own.shape[0]
    hidden, wide, part = FF // blocks, D // blocks, D // parts
    return kernel_call(
        "low_rank",
        functools.partial(low_rank_kernel, hidden),
        [shape(part, hidden), shape(part, wide), shape(part, hidden + wide, dtype=BF)],
        (),
        near(own, far, wm),
        [((rows, own.shape[1]), BF), ((2, rows, part), BF)],
        cost(2 * rows * D * D),
    )


def finish_kernel(groups, *refs):
    pair, last, second, lines = (
        [refs[sum(groups[:i]) + n] for n in range(groups[i])] for i in range(4)
    )
    loss_ref, down_ref, head_ref, other_ref = refs[sum(groups) : sum(groups) + 4]
    (
        joint_ref,
        out_ref,
        up_block_ref,
        down_block_ref,
        head_block_ref,
        loss_out_ref,
        *vector_refs,
    ) = refs[sum(groups) + 4 :]

    def total(terms):
        return sum(ref[...].astype(F32) for ref in terms)

    both, two_ = total(pair), total(second)
    one = both[1]
    half = one.shape[1]
    up_block_ref[:, :half] = both[0]
    up_block_ref[:, half:] = total(last)
    some = one.shape[1]
    rest = joint_ref.shape[1] - some
    joint_ref[:, :some] = one
    joint_ref[:, some:] = two_[:, :rest]
    out_ref[...] = two_[:, rest:]
    hidden = down_ref.shape[1]
    down_block_ref[...] = down_ref[...] + other_ref[:, :hidden].astype(F32)
    head_block_ref[...] = (head_ref[...] + other_ref[:, hidden:].astype(F32)).T
    loss_out_ref[...] = loss_ref[...].reshape(1)
    vectors = total(lines)
    starts = (GAIN1, SHIFT1, JOINT, OUT, GAIN2, SHIFT2, WIDE, NARROW)
    for start, ref in zip(starts, vector_refs):
        for i in range(ref.shape[0] // 128):
            line = start // 128 + i
            if start == JOINT and i >= D // 128:
                line += D // 128
            ref[pl.ds(i * 128, 128)] = vectors[line]


def finish(pair, last, second, vectors, loss, low, joint):
    rows = last[0].shape[0]
    sizes = (D, D, 2 * D, D, D, D, FF, D)
    return kernel_call(
        "finish",
        functools.partial(finish_kernel, [len(v) for v in (pair, last, second, vectors)]),
        [
            shape(rows, joint),
            shape(rows, D - joint),
            shape(rows, D),
            shape(*low[0].shape),
            shape(*low[1].shape[::-1]),
            shape(1),
        ]
        + [shape(n) for n in sizes],
        (),
        (*pair, *last, *second, *vectors, loss, *low),
    )


def both_pairs(partner):
    dp, rep = lax.axis_size("dp"), lax.axis_size("rep")
    pairs = []
    for i in range(dp):
        for j in range(rep):
            a, b = partner(i, j)
            pairs.append((i * rep + j, a * rep + b))
    return pairs


def exchange(value, partner):
    return lax.ppermute(value, ("dp", "rep"), both_pairs(partner))


def first_turn(i, j):
    return (i, j ^ 2) if j & 1 == 0 else (i ^ 1, j)


def second_turn(i, j):
    return (i ^ 1, j) if j & 1 == 0 else (i, j ^ 2)


def added(a, b):
    return (a.astype(F32) + b.astype(F32)).astype(BF)


def halved(here, got):
    half = here.shape[0] // 2
    return added(here[:half], got[:half]), added(here[half:], got[half:])


def parted(here, got, count):
    rows = here.shape[-2] // count
    parts = [slice(i * rows, (i + 1) * rows) for i in range(count)]
    return [added(here[..., p, :], got[..., p, :]) for p in parts]


def core_turn(i, j):
    return i, j ^ 1


def across(i, j):
    return i, j ^ 2


def group_round(keep, got, group):
    masks = group_masks(group)
    bits = len(group)
    parts = parted(keep, got, len(masks))
    place = [sum(((c >> n) & 1) << (bits - 1 - n) for n in range(bits)) for c in range(len(masks))]
    return [parts[0]] + [
        exchange(parts[place[c]], lambda i, j: (i ^ masks[c][0], j)) for c in range(1, len(masks))
    ]


def flat(*values):
    return jnp.concatenate([v.reshape(-1, v.shape[-1]) for v in values])


order = lax.optimization_barrier


def dp_groups():
    bits = [("dp", b) for b in range(1, lax.axis_size("dp").bit_length() - 1)]
    return [bits[i : i + 2] for i in range(0, len(bits), 2)] + [[("dp", 0)]]


def all_groups():
    bits = [("rep", b) for b in range(1, lax.axis_size("rep").bit_length() - 1)]
    groups = dp_groups()
    return groups[:-1] + [groups[-1] + bits, [("rep", 0)]]


def group_masks(group):
    out = [(0, 0)]
    for axis, bit in group:
        out += [(a | 1 << bit, b) if axis == "dp" else (a, b | 1 << bit) for a, b in out]
    return out


def gather_masks(rounds, blocks):
    bits = [0] + list(range(blocks.bit_length() - 2, 0, -1))
    masks, used = [0], 0
    for count in rounds:
        for bit in bits[used : used + count]:
            masks = masks + [m | 1 << bit for m in masks]
        used += count
    return masks


def split_round(value, wide, group):
    blocks = (value.shape[1] - D) // wide
    turns = group_masks(group)
    text = value[:, blocks * wide :]
    pieces = []
    for c, (a, b) in enumerate(turns):
        chosen = [value[:, i * wide : (i + 1) * wide] for i in range(c, blocks, len(turns))]
        piece = jnp.concatenate(chosen + [text], axis=1)
        pieces.append(piece if c == 0 else exchange(piece, lambda i, j: (i ^ a, j ^ b)))
    return pieces


def round_of(value, group):
    return [value] + [
        exchange(value, lambda i, j: (i ^ a, j ^ b)) for a, b in group_masks(group)[1:]
    ]


def relative_rows(value, blocks):
    rows = value.shape[0] // blocks
    if rows % SLOT == 0:
        return value
    bits = blocks.bit_length() - 1
    place = jnp.arange(blocks, dtype=jnp.int32)
    source = jnp.zeros_like(place)
    for bit in range(bits):
        source = source + ((place >> (bits - 1 - bit)) & 1) * (1 << bit)
    source = source ^ lax.axis_index("dp")
    return value.reshape(blocks, rows, -1)[source].reshape(value.shape)


def local(
    incoming_activations,
    caption_final_place,
    paired_picture,
    caption_weight,
    locked_picture_features,
    softmax_heat,
    premix_scaling_factor,
    premix_shift_term,
    stacked_mixing_matrix,
    asking_reading_offsets,
    mixing_result_matrix,
    mixing_result_offset,
    premlp_scaling_factor,
    premlp_shift_term,
    widening_matrix,
    widening_offset,
    narrowing_matrix,
    narrowing_offset,
    caption_mapping_matrix,
    picture_mapping_matrix,
):
    both = ("dp", "rep")
    devices = lax.axis_size(both)
    blocks = lax.axis_size("dp")
    parts = lax.axis_size("rep")
    captions = caption_final_place.shape[0]
    images = locked_picture_features.shape[0]
    groups = all_groups()
    pieces = round_of(jnp.pad(locked_picture_features, ((0, SLOT - images), (0, 0))), groups[0])
    project, normed_t = project_tokens(
        blocks,
        premix_scaling_factor,
        premix_shift_term,
        asking_reading_offsets,
        incoming_activations,
        stacked_mixing_matrix,
    )
    project, pieces = order((project, pieces))
    for group in groups[1:-1]:
        pieces = round_of(jnp.concatenate(pieces), group)
    att, context_t, middle = attend_tokens(
        blocks,
        caption_final_place,
        mixing_result_offset,
        incoming_activations,
        project,
        mixing_result_matrix,
    )
    middle, pieces = order((middle, pieces))
    own, far = round_of(jnp.concatenate(pieces), groups[-1])
    second_t, slope, box, text, factor, embed = widen_tokens(
        blocks,
        caption_final_place,
        premlp_scaling_factor,
        premlp_shift_term,
        widening_offset,
        narrowing_offset,
        middle,
        widening_matrix,
        narrowing_matrix,
        caption_mapping_matrix,
    )
    normed_t, context_t, second_t = (
        relative_rows(v, blocks) for v in (normed_t, context_t, second_t)
    )
    embed, far = order((embed, far))
    picture, score, row, inverse, stats = contrast(
        images,
        parts,
        sum(groups, []),
        softmax_heat,
        own,
        far,
        picture_mapping_matrix,
        embed,
        paired_picture,
        caption_weight,
    )
    groups = dp_groups()
    high = [[bit] for group in groups[:-1] for bit in group]
    factor_groups = groups[-1:] + high[::-1]
    stats = round_of(stats, [("rep", 0)])
    stats = round_of(merge(stats), [("rep", 1)] + groups[-1])
    for group in groups[:-1]:
        stats = round_of(merge(stats), group)
    back, away, here, pooled_back, loss, down_bias, up_bias, *pieces = head_back(
        images,
        [len(group) for group in factor_groups],
        softmax_heat,
        caption_final_place,
        stats,
        score,
        row,
        inverse,
        caption_weight,
        paired_picture,
        picture,
        text,
        factor,
        caption_mapping_matrix,
        narrowing_matrix,
        slope,
        second_t,
        box,
    )
    loss = loss / (captions * devices)
    got = exchange(away, core_turn)
    pieces = pieces[:1] + [
        exchange(piece, lambda i, j: (i ^ a, j ^ b))
        for piece, (a, b) in zip(pieces[1:], group_masks(factor_groups[0])[1:])
    ]
    total, attended, context_back, gain2, shift2, out_bias = middle_back(
        caption_final_place,
        premlp_scaling_factor,
        pooled_back,
        back,
        widening_matrix,
        middle,
        mixing_result_matrix,
    )
    context_back, got, pieces = order((context_back, got, pieces))
    up, send = halved(here[0], got[0])
    got_up = exchange(send, first_turn)
    last, got_last = group_round(here[1], got[1], high[0])
    pieces = split_round(jnp.concatenate(pieces), box.shape[2], factor_groups[1])
    project_back, joint_bias = attention_back(project, att, context_back)
    away, here = columns_gradient("left_columns", left_columns_kernel, (project_back, normed_t))
    got = exchange(away, core_turn)
    project_back, away = order((project_back, away))
    away, here2 = columns_gradient(
        "right_columns", right_columns_kernel, (project_back, attended, normed_t, context_t)
    )
    project_back, away, got, got_up, got_last = order((project_back, away, got, got_up, got_last))
    up, send = halved(up, got_up)
    first, send1 = halved(here, got)
    got = exchange(flat(send, send1), second_turn)
    for group in high[1:]:
        last, got_last = group_round(last, got_last, group)
    got2 = exchange(away, core_turn)
    joint = 3 * D // parts
    token, sums = token_back(
        premix_scaling_factor,
        incoming_activations,
        total,
        project_back,
        stacked_mixing_matrix,
        (joint_bias, out_bias, gain2, shift2, up_bias, down_bias),
    )
    sums, got2 = order((sums, got2))
    lines = round_of(sums, [("rep", 0)])
    second, send2 = halved(here2, got2)
    got, send2, lines, pieces, got_last = order((got, send2, lines, pieces, got_last))
    here_rows = up.shape[1]
    up = added(up[0], got[:here_rows])
    first, send = halved(first, got[here_rows:].reshape(first.shape))
    last, send_last = halved(last, got_last)
    got2 = exchange(flat(send2, send, send_last), first_turn)
    lines = round_of(sum(lines), [("rep", 1)])
    for group in factor_groups[2:]:
        pieces = split_round(jnp.concatenate(pieces), box.shape[2], group)
    got2, lines, pieces = order((got2, lines, pieces))
    second, send = halved(second, got2[: 2 * here_rows].reshape(second.shape))
    first = added(first[0], got2[2 * here_rows : 3 * here_rows])
    last, send_last = halved(last, got2[3 * here_rows :].reshape(last.shape))
    got2 = exchange(flat(send, send_last), second_turn)
    pair, got_pair = jnp.stack([up, first]), None
    rows = here_rows // 2
    turn = lambda i, j: (i ^ (1 << high[0][0][1]), j)
    pair, got_pair = pair[:, :rows], exchange(pair[:, rows:], turn)
    lines = round_of(sum(lines), groups[-1])
    factors = jnp.concatenate(pieces)
    far = exchange(factors, core_turn)
    got_pair, got2, lines, far = order((got_pair, got2, lines, far))
    *low, other = low_rank(blocks, parts, factors, far, caption_mapping_matrix)
    other = exchange(other, across)
    last = [last[0], got2[here_rows:]]
    second, got2 = second[0], got2[:here_rows]
    for i, group in enumerate(high):
        got_pair, got2, lines = order((got_pair, got2, lines))
        second, got2 = group_round(second, got2, group)
        if i + 1 < len(high):
            pair, got_pair = group_round(pair, got_pair, high[i + 1])
        lines = round_of(sum(lines), group)
    pair, second, vectors = [pair, got_pair], [second, got2], lines
    joint_block, out_block, up_block, down_block, head_block, loss, *grads = finish(
        pair, last, second, vectors, loss, (*low, other), joint
    )
    return (
        loss,
        token,
        grads[0],
        grads[1],
        joint_block,
        grads[2],
        out_block,
        grads[3],
        grads[4],
        grads[5],
        up_block,
        grads[6],
        down_block.T,
        grads[7],
        head_block,
    )


def solution(mesh):
    spread = P(("dp", "rep"), None)
    line = P(("dp", "rep"))
    block = P("dp", "rep")
    in_specs = (spread, line, line, line, spread) + (P(),) * 15
    out_specs = (
        P(),
        spread,
        P(),
        P(),
        block,
        P(),
        block,
        P(),
        P(),
        P(),
        block,
        P(),
        block,
        P(),
        block,
    )
    return jax.shard_map(local, mesh=mesh, in_specs=in_specs, out_specs=out_specs, check_vma=False)
```

```python
import functools

import jax
import jax.numpy as jnp
from jax import lax
from jax.experimental import pallas as pl
from jax.experimental.pallas import tpu as pltpu
from jax.sharding import PartitionSpec as P

D = 768
HEADS = 12
HEAD = 64
SEQ = 16
FF = 3072
GROUP = 128
PAIRS = HEADS // 2
SLOT = 16
BF = jnp.bfloat16
F32 = jnp.float32

epsilon = 1e-06
negative = -1e30
scale = HEAD ** (-0.5)
LIMIT = 16 * 1024 * 1024

GAIN1, SHIFT1, JOINT, OUT, GAIN2, SHIFT2, WIDE, NARROW = 0, 768, 1536, 3840, 4608, 5376, 6144, 9216
VECTORS = 9984
LINES = VECTORS // 128
ALL_LINES = LINES + -LINES % 8

vmem = pl.BlockSpec(memory_space=pltpu.VMEM)
smem = pl.BlockSpec(memory_space=pltpu.SMEM)


def dot(a, b, dims):
    return lax.dot_general(a, b, (dims, ((), ())), preferred_element_type=F32)


def nn(a, b):
    return dot(a, b, ((1,), (0,)))


def nt(a, b):
    return dot(a, b, ((1,), (1,)))


def tn(a, b):
    return dot(a, b, ((0,), (0,)))


def cost(flops):
    return pl.CostEstimate(flops=flops // 10, transcendentals=0, bytes_accessed=0)


def shape(*dims, dtype=F32):
    return jax.ShapeDtypeStruct(dims, dtype)


def kept(*dims, dtype=BF):
    return pltpu.VMEM(dims, dtype)


def near(*values):
    return [pltpu.with_memory_space_constraint(v, pltpu.VMEM) for v in values]


def kernel_call(name, body, results, small, operands, scratch=(), estimate=None, limit=LIMIT):
    return pl.pallas_call(
        body,
        out_shape=results,
        in_specs=[smem] * len(small) + [vmem] * len(operands),
        out_specs=[vmem] * len(results),
        scratch_shapes=[pltpu.VMEM(s, t) for s, t in scratch],
        compiler_params=pltpu.CompilerParams(vmem_limit_bytes=limit),
        cost_estimate=estimate,
        name=name,
    )(*small, *operands)


def iota(dims, axis):
    return lax.broadcasted_iota(jnp.int32, dims, axis)


def norm_parts(values):
    average = jnp.mean(values, axis=-1, keepdims=True)
    centred = values - average
    inverse = lax.rsqrt(jnp.mean(centred * centred, axis=-1, keepdims=True) + epsilon)
    return centred * inverse, inverse


def norm_back(unit, inverse, gain, back):
    inner = back * gain
    part = inverse * (
        inner
        - jnp.mean(inner, axis=-1, keepdims=True)
        - unit * jnp.mean(inner * unit, axis=-1, keepdims=True)
    )
    return part, jnp.sum(back * unit, axis=0, keepdims=True), jnp.sum(back, axis=0, keepdims=True)


def split(value):
    high = value.astype(BF)
    return high, (value - high.astype(F32)).astype(BF)


def two(value):
    return jnp.concatenate(split(value), axis=0)


def as_row(ref):
    return ref[...].reshape(1, ref.shape[0])


def as_column(ref):
    size = ref.shape[0]
    same = iota((size, size), 0) == iota((size, size), 1)
    row = as_row(ref)
    return jnp.sum(jnp.where(same, row, jnp.zeros_like(row)), axis=1, keepdims=True)


def token_limits(ref):
    place = as_row(ref).astype(F32)
    captions = place.shape[1]
    tokens = captions * SEQ
    owner = (iota((tokens, captions), 0) // SEQ == iota((tokens, captions), 1)).astype(F32)
    column = jnp.sum(owner * place, axis=1, keepdims=True)
    line = nt(place.astype(BF), owner.astype(BF))
    return line, column


def pool_mask(line, captions):
    dims = (captions, captions * SEQ)
    token = iota(dims, 1)
    inside = (token % SEQ).astype(F32) <= line
    return jnp.where((token // SEQ == iota(dims, 0)) & inside, 1.0, 0.0)


def spread_mask(column, captions):
    dims = (captions * SEQ, captions)
    token = iota(dims, 0)
    inside = (token % SEQ).astype(F32) <= column
    return jnp.where((token // SEQ == iota(dims, 1)) & inside, 1.0, 0.0)


def head_masks():
    lane = iota((1, 2 * HEAD), 1)
    even = (lane < HEAD).astype(F32)
    return even.astype(BF), (1.0 - even).astype(BF)


def caption_masks():
    lane = iota((SEQ, GROUP), 1) // SEQ
    return [lane == c for c in range(GROUP // SEQ)]


def compact(full, picks):
    out = full[:SEQ]
    for c in range(1, len(picks)):
        out = jnp.where(picks[c], full[c * SEQ : (c + 1) * SEQ], out)
    return out


def expand(low, lows):
    return jnp.concatenate([low * mask for mask in lows], axis=0)


def both_heads(value, masks):
    return jnp.concatenate([value * masks[0], value * masks[1]], axis=0)


def store_permuted(ref, value, dp, blocks):
    rows = value.shape[0] // blocks
    bits = blocks.bit_length() - 1
    if rows % SLOT:
        ref[...] = value
        return
    for b in range(blocks):
        k = jnp.bitwise_xor(dp, b)
        place = 0
        for bit in range(bits):
            place = place + ((k >> bit) & 1) * (1 << (bits - 1 - bit))
        ref[pl.ds(pl.multiple_of(place * rows, SLOT), rows), :] = value[b * rows : (b + 1) * rows]


def box_width(blocks):
    used = (FF + D) // blocks
    return used + -used % 128


def project_kernel(
    blocks, gain_ref, shift_ref, joint_ref, x_ref, wj_ref, project_ref, normed_ref, normed
):
    unit, _ = norm_parts(x_ref[...].astype(F32))
    normed[...] = (unit * as_row(gain_ref) + as_row(shift_ref)).astype(BF)
    joint = as_row(joint_ref)
    for i, bias in enumerate((joint[:, :D], 0.0, joint[:, D:])):
        lanes = slice(i * D, (i + 1) * D)
        project_ref[:, lanes] = (nn(normed[...], wj_ref[:, lanes]) + bias).astype(BF)
    store_permuted(normed_ref, normed[...].T, lax.axis_index("dp"), blocks)


def project_tokens(blocks, gain, shift, joint, x, wj):
    tokens = x.shape[0]
    return kernel_call(
        "project_tokens",
        functools.partial(project_kernel, blocks),
        [kept(tokens, 3 * D), kept(D, tokens)],
        (),
        (gain, shift, joint, *near(x, wj)),
        [((tokens, D), BF)],
        cost(6 * tokens * D * D),
    )


def attend_kernel(
    blocks,
    place_ref,
    out_ref,
    x_ref,
    project_ref,
    wo_ref,
    att_ref,
    context_t_ref,
    middle_ref,
    context,
):
    line, _ = token_limits(place_ref)
    masks = head_masks()
    picks = caption_masks()
    lows = [pick.astype(F32).astype(BF) for pick in picks]
    key_place = iota((SEQ, GROUP), 0).astype(F32)

    def attend(h, carry):
        at = pl.multiple_of(h * 2 * HEAD, 128)
        for g in range(x_ref.shape[0] // GROUP):
            here = slice(g * GROUP, (g + 1) * GROUP)
            query = project_ref[here, pl.ds(at, 128)]
            keys = both_heads(project_ref[here, pl.ds(pl.multiple_of(D + at, 128), 128)], masks)
            values = both_heads(
                project_ref[here, pl.ds(pl.multiple_of(2 * D + at, 128), 128)], masks
            )
            scores = nt(keys, query)
            allowed = key_place <= line[:, here]
            parts = []
            for e in range(2):
                score = compact(scores[e * GROUP : (e + 1) * GROUP], picks) * scale
                score = jnp.where(allowed, score, negative)
                score = jnp.exp(score - jnp.max(score, axis=0, keepdims=True))
                weight = score / jnp.sum(score, axis=0, keepdims=True)
                att_ref[2 * h + e, :, here] = weight
                parts.append(expand(weight.astype(BF), lows))
            context[here, pl.ds(at, 128)] = tn(jnp.concatenate(parts, axis=0), values).astype(BF)
        return carry

    lax.fori_loop(0, PAIRS, attend, 0)
    middle_ref[...] = x_ref[...].astype(F32) + (nn(context[...], wo_ref[...]) + as_row(out_ref))
    store_permuted(context_t_ref, context[...].T, lax.axis_index("dp"), blocks)


def attend_tokens(blocks, place, out, x, project, wo):
    tokens = x.shape[0]
    return kernel_call(
        "attend_tokens",
        functools.partial(attend_kernel, blocks),
        [kept(HEADS, SEQ, tokens, dtype=F32), kept(D, tokens), kept(tokens, D, dtype=F32)],
        (),
        (place, out, *near(x, project, wo)),
        [((tokens, D), BF)],
        cost(4 * tokens * D * D),
    )


def widen_kernel(
    blocks,
    place_ref,
    gain_ref,
    shift_ref,
    wide_ref,
    narrow_ref,
    middle_ref,
    wu_ref,
    wn_ref,
    wm_ref,
    second_t_ref,
    slope_ref,
    box_ref,
    text_ref,
    scale_ref,
    embed_ref,
    second,
    branch,
    wide,
    mean,
):
    captions = place_ref.shape[0]
    line, column = token_limits(place_ref)
    pool = pool_mask(line, captions)
    share = 1.0 / jnp.sum(pool, axis=1, keepdims=True)
    unit, _ = norm_parts(middle_ref[...])
    second[...] = (unit * as_row(gain_ref) + as_row(shift_ref)).astype(BF)
    store_permuted(second_t_ref, second[...].T, lax.axis_index("dp"), blocks)
    branch[...] = jnp.zeros_like(branch)
    wide[...] = as_row(wide_ref)
    pool_low = pool.astype(BF)
    c0 = 0.7978845608028654
    c1 = c0 * 0.044715
    step = 512

    def widen(i, carry):
        at = pl.multiple_of(i * step, 128)
        upper = nn(second[...], wu_ref[:, pl.ds(at, step)]) + wide[:, pl.ds(at, step)]
        square = upper * upper
        bend = jnp.tanh(upper * (c0 + c1 * square))
        half = 0.5 + 0.5 * bend
        active = upper * half
        slope_ref[:, pl.ds(at, step)] = (
            half * (1.0 + (upper - active) * (2.0 * c0 + 6.0 * c1 * square))
        ).astype(BF)
        parts = two(nn(pool_low, active.astype(BF)) * share)
        mean[:, pl.ds(at, step)] = parts[:captions]
        branch[...] += nn(parts, wn_ref[pl.ds(at, step), :])
        return carry

    lax.fori_loop(0, FF // step, widen, 0)
    inside = jnp.where((iota((captions * SEQ, 1), 0) % SEQ).astype(F32) <= column, 1.0, 0.0)
    weight = inside / (column + 1.0)
    pooled = jnp.sum((middle_ref[...] * weight).reshape(captions, SEQ, D), axis=1)
    pooled = (pooled + (branch[:captions] + branch[captions:] + as_row(narrow_ref))).astype(BF)
    hidden, part = FF // blocks, D // blocks
    for b in range(blocks):
        box_ref[b, :, :hidden] = mean[:, b * hidden : (b + 1) * hidden]
        box_ref[b, :, hidden : hidden + part] = pooled[:, b * part : (b + 1) * part]
    text = nn(pooled, wm_ref[...])
    factor = lax.rsqrt(jnp.sum(text * text, axis=1, keepdims=True) + epsilon)
    text_ref[...] = text
    scale_ref[...] = factor
    embed_ref[...] = (text * factor).astype(BF)


def widen_tokens(blocks, place, gain, shift, wide, narrow, middle, wu, wn, wm):
    tokens = middle.shape[0]
    captions = place.shape[0]
    return kernel_call(
        "widen_tokens",
        functools.partial(widen_kernel, blocks),
        [
            kept(D, tokens),
            kept(tokens, FF),
            kept(blocks, captions, box_width(blocks)),
            kept(captions, D, dtype=F32),
            kept(captions, 1, dtype=F32),
            kept(captions, D),
        ],
        (),
        (place, gain, shift, wide, narrow, *near(middle, wu, wn, wm)),
        [
            ((tokens, D), BF),
            ((2 * captions, D), F32),
            ((1, FF), F32),
            ((captions, FF), BF),
        ],
        cost(2 * tokens * D * FF),
    )


def match_of(paired, columns, images):
    column = iota((1, columns), 1)
    valid = column % SLOT < images
    name = jnp.where(valid, (column // SLOT) * images + column % SLOT, -1)
    return paired == name, valid


def contrast_kernel(
    images,
    parts,
    bits,
    heat_ref,
    own_ref,
    near_ref,
    wp_ref,
    embed_ref,
    paired_ref,
    weight_ref,
    picture_ref,
    score_ref,
    row_ref,
    inverse_ref,
    stats_ref,
    features,
):
    half = own_ref.shape[0] // SLOT
    for far, ref in enumerate((own_ref, near_ref)):

        def place(i, carry, far=far, ref=ref):
            p = i + far * half
            index = {axis: lax.axis_index(axis) for axis in ("dp", "rep")}
            for n, (axis, bit) in enumerate(bits):
                index[axis] = jnp.bitwise_xor(index[axis], ((p >> n) & 1) << bit)
            to = pl.ds(pl.multiple_of((index["dp"] * parts + index["rep"]) * SLOT, SLOT), SLOT)
            features[to, :] = ref[pl.ds(pl.multiple_of(i * SLOT, SLOT), SLOT), :]
            return carry

        lax.fori_loop(0, half, place, 0, unroll=4)
    picture = nn(features[...], wp_ref[...])
    picture = (
        picture * lax.rsqrt(jnp.sum(picture * picture, axis=1, keepdims=True) + epsilon)
    ).astype(BF)
    picture_ref[...] = picture
    score = nt(embed_ref[...], picture) / heat_ref[0]
    match, valid = match_of(as_column(paired_ref), score.shape[1], images)
    score = jnp.where(valid, score, negative)
    score_ref[...] = score
    top = jnp.max(score, axis=1, keepdims=True)
    row = jnp.log(jnp.sum(jnp.exp(score - top), axis=1, keepdims=True)) + top
    row_ref[...] = row
    positive = jnp.sum(jnp.where(match, score, 0.0), axis=1, keepdims=True)
    hits = jnp.where(match, 1.0, 0.0)
    counts = jnp.sum(hits, axis=0, keepdims=True)
    inverse = 1.0 / jnp.sum(hits * counts, axis=1, keepdims=True)
    inverse_ref[...] = inverse
    total = jnp.sum(as_column(weight_ref) * (row - positive - positive * inverse))
    best = jnp.max(score, axis=0, keepdims=True)
    mass = jnp.sum(jnp.exp(score - best), axis=0, keepdims=True)
    mass = jnp.where(iota(mass.shape, 1) == images, total, mass)
    wide = best.shape[1] // 4
    rows = [v[:, i * wide : (i + 1) * wide] for v in (best, mass) for i in range(4)]
    stats_ref[...] = jnp.concatenate(rows, axis=0)


def contrast(images, parts, bits, heat, own, far, wp, embed, paired, weight):
    captions = embed.shape[0]
    columns = 2 * own.shape[0]
    return kernel_call(
        "contrast",
        functools.partial(contrast_kernel, images, parts, bits),
        [
            kept(columns, D),
            kept(captions, columns, dtype=F32),
            kept(captions, 1, dtype=F32),
            kept(captions, 1, dtype=F32),
            shape(8, columns // 4),
        ],
        (heat,),
        (*near(own, far, wp, embed), paired, weight),
        [((columns, D), BF)],
        cost(2 * columns * D * D),
        max(LIMIT, columns * 8192),
    )


def merged(refs):
    best = functools.reduce(jnp.maximum, [ref[:4] for ref in refs])
    mass = sum(ref[4:] * jnp.exp(ref[:4] - best) for ref in refs)
    return best, mass


def merge_kernel(*refs):
    *given, out_ref = refs
    best, mass = merged(given)
    out_ref[...] = jnp.concatenate([best, mass], axis=0)


def merge(stats):
    return kernel_call("merge", merge_kernel, [shape(*stats[0].shape)], (), stats)[0]


def quarters(rep, away):
    core = rep & 1
    out = []
    for xrel in range(2):
        for yrel in range(2):
            block = jnp.bitwise_xor(rep, 2 * xrel + away)
            x_first = 1 - core if away == 0 else core
            out.append((jnp.where(x_first == 1, 2 * xrel + yrel, 2 * yrel + xrel), block, yrel))
    return out


def head_back_kernel(
    images,
    count_stats,
    rounds,
    heat_ref,
    place_ref,
    score_ref,
    row_ref,
    inverse_ref,
    weight_ref,
    paired_ref,
    picture_ref,
    text_ref,
    scale_ref,
    wm_ref,
    wn_ref,
    slope_ref,
    second_t_ref,
    box_ref,
    *refs,
):
    first = 1 << rounds[0]
    pieces = refs[len(refs) - first :]
    stats = refs[:count_stats]
    (
        back_ref,
        away_ref,
        here_ref,
        pooled_ref,
        loss_ref,
        down_bias_ref,
        up_bias_ref,
    ) = refs[count_stats : len(refs) - first]
    rep = lax.axis_index("rep")
    heat = heat_ref[0]
    captions = place_ref.shape[0]
    line, column = token_limits(place_ref)
    count = jnp.sum(pool_mask(line, captions), axis=1, keepdims=True)
    owner = spread_mask(column, captions).astype(BF)
    owner = jnp.concatenate([owner, owner], axis=1)

    score = score_ref[...]
    match, valid = match_of(as_column(paired_ref), score.shape[1], images)
    best, mass = merged(stats)
    column_log = jnp.log(mass) + best
    column_log = jnp.concatenate([column_log[i : i + 1] for i in range(4)], axis=1)
    loss_ref[...] = mass[:1, images : images + 1] + jnp.sum(
        jnp.where(valid, column_log, 0.0), axis=1, keepdims=True
    )
    weight = as_column(weight_ref)
    graded = (
        weight * jnp.exp(score - row_ref[...])
        + jnp.exp(score - column_log)
        - jnp.where(match, weight * (1.0 + inverse_ref[...]), 0.0)
    )
    graded = jnp.where(valid, graded / heat, 0.0).astype(BF)
    embed_back = nn(graded, picture_ref[...])
    text = text_ref[...]
    factor = scale_ref[...]
    text_dot = jnp.sum(text * embed_back, axis=1, keepdims=True)
    text_back = (factor * embed_back - text * (factor * factor * factor) * text_dot).astype(BF)
    blocks, _, wide = box_ref.shape
    masks = gather_masks(rounds, blocks)
    for c, piece_ref in enumerate(pieces):
        for i in range(blocks // first):
            block = jnp.bitwise_xor(lax.axis_index("dp"), masks[i * first + c])
            piece_ref[:, i * wide : (i + 1) * wide] = box_ref[block]
        piece_ref[:, (blocks // first) * wide :] = text_back
    pooled_back = nt(text_back, wm_ref[...])
    pooled_ref[...] = pooled_back
    branch = (pooled_back / count).astype(BF)
    down_bias_ref[...] = jnp.sum(branch.astype(F32) * count, axis=0, keepdims=True)
    ones = jnp.ones((SLOT, back_ref.shape[0]), BF)
    step = 512

    def widen(i, carry):
        at = pl.multiple_of(i * step, 128)
        part = nn(owner, two(nt(branch, wn_ref[pl.ds(at, step), :])))
        part = (part * slope_ref[:, pl.ds(at, step)].astype(F32)).astype(BF)
        back_ref[:, pl.ds(at, step)] = part
        up_bias_ref[:, pl.ds(at, step)] = nn(ones, part)[:1]
        return carry

    lax.fori_loop(0, FF // step, widen, 0)
    half = second_t_ref.shape[0] // 2
    wide = FF // 4
    for turn, target in enumerate((away_ref, here_ref)):
        for place, block, yrel in quarters(rep, 1 - turn):
            part = nn(
                second_t_ref[yrel * half : (yrel + 1) * half],
                back_ref[:, pl.ds(pl.multiple_of(block * wide, 128), wide)],
            )
            for h in range(2):
                target[h, place] = part[:, h * (wide // 2) : (h + 1) * (wide // 2)].astype(BF)


def head_back(images, rounds, heat, place, stats, score, row, inverse, weight, paired, picture, text,
              factor, wm, wn, slope, second_t, box):
    captions = text.shape[0]
    tokens = slope.shape[0]
    piece = (2, 4, D // 2, FF // 8)
    return kernel_call(
        "head_back",
        functools.partial(head_back_kernel, images, len(stats), rounds),
        [
            kept(tokens, FF),
            kept(*piece),
            kept(*piece),
            kept(captions, D, dtype=F32),
            shape(1, 1),
            shape(1, D),
            shape(1, FF),
        ]
        + [shape(captions, (box.shape[0] >> rounds[0]) * box.shape[2] + D, dtype=BF)] * (1 << rounds[0]),
        (heat,),
        (
            place,
            *near(score, row, inverse),
            weight,
            paired,
            *near(picture, text, factor, wm, wn, slope, second_t, box),
            *stats,
        ),
        (),
        cost(2 * tokens * D * FF),
    )


def middle_back_kernel(
    place_ref,
    gain_ref,
    pooled_ref,
    back_ref,
    wu_ref,
    middle_ref,
    wo_ref,
    total_ref,
    attended_ref,
    context_back_ref,
    gain_back_ref,
    shift_back_ref,
    bias_ref,
):
    captions = place_ref.shape[0]
    line, column = token_limits(place_ref)
    count = jnp.sum(pool_mask(line, captions), axis=1, keepdims=True)
    owner = spread_mask(column, captions).astype(BF)
    owner = jnp.concatenate([owner, owner], axis=1)
    second_back = nt(back_ref[...], wu_ref[...])
    unit, inverse = norm_parts(middle_ref[...])
    part, gain_back_ref[...], shift_back_ref[...] = norm_back(
        unit, inverse, as_row(gain_ref), second_back
    )
    total = nn(owner, two(pooled_ref[...] / count)) + part
    total_ref[...] = total
    attended = total.astype(BF)
    attended_ref[...] = attended
    bias_ref[...] = nn(jnp.ones((SLOT, attended.shape[0]), BF), attended)[:1]
    context_back_ref[...] = nt(attended, wo_ref[...]).astype(BF)


def middle_back(place, gain, pooled, back, wu, middle, wo):
    tokens = back.shape[0]
    return kernel_call(
        "middle_back",
        middle_back_kernel,
        [
            kept(tokens, D, dtype=F32),
            kept(tokens, D),
            kept(tokens, D),
            shape(1, D),
            shape(1, D),
            shape(1, D),
        ],
        (),
        (place, gain, *near(pooled, back, wu, middle, wo)),
        (),
        cost(2 * tokens * D * (FF + D)),
    )


def attention_back_kernel(
    project_ref,
    att_ref,
    context_back_ref,
    attended_ref,
    normed_t_ref,
    context_t_ref,
    back_ref,
    bias_ref,
    away_ref,
    here_ref,
    chosen,
):
    masks = head_masks()
    picks = caption_masks()
    lows = [pick.astype(F32).astype(BF) for pick in picks]
    low_scale = jnp.asarray(scale, BF)
    first = iota((GROUP, 2 * HEAD), 1) < HEAD
    tokens = project_ref.shape[0]

    def attend(h, carry):
        at = pl.multiple_of(h * 2 * HEAD, 128)
        at_k = pl.multiple_of(D + at, 128)
        at_v = pl.multiple_of(2 * D + at, 128)
        for g in range(tokens // GROUP):
            span = slice(g * GROUP, (g + 1) * GROUP)
            query = project_ref[span, pl.ds(at, 128)]
            keys = both_heads(project_ref[span, pl.ds(at_k, 128)], masks)
            values = both_heads(project_ref[span, pl.ds(at_v, 128)], masks)
            upper = context_back_ref[span, pl.ds(at, 128)]
            full = nt(values, upper)
            weights, grads = [], []
            for e in range(2):
                weight = att_ref[2 * h + e, :, span]
                part = compact(full[e * GROUP : (e + 1) * GROUP], picks)
                grad = weight * (part - jnp.sum(weight * part, axis=0, keepdims=True))
                weights.append(expand(weight.astype(BF), lows))
                grads.append(expand(grad.astype(BF) * low_scale, lows))
            weights = jnp.concatenate(weights, axis=0)
            grads = jnp.concatenate(grads, axis=0)
            back_ref[span, pl.ds(at, 128)] = tn(grads, keys).astype(BF)
            wide = nn(grads, query)
            back_ref[span, pl.ds(at_k, 128)] = jnp.where(first, wide[:GROUP], wide[GROUP:]).astype(
                BF
            )
            wide = nn(weights, upper)
            back_ref[span, pl.ds(at_v, 128)] = jnp.where(first, wide[:GROUP], wide[GROUP:]).astype(
                BF
            )
        return carry

    lax.fori_loop(0, PAIRS, attend, 0)
    ones = jnp.ones((SLOT, tokens), BF)
    for i in range(3):
        lanes = slice(i * D, (i + 1) * D)
        bias_ref[:, lanes] = nn(ones, back_ref[:, lanes])[:1]


    rep = lax.axis_index("rep")
    joint = 3 * D // 4
    out = D // 4
    for r in range(4):

        @pl.when(rep == r)
        def _():
            for i, k in enumerate((1, 3, 0, 2)):
                b = r ^ k
                chosen[i, :, :joint] = back_ref[:, b * joint : (b + 1) * joint]
                chosen[i, :, joint:] = attended_ref[:, b * out : (b + 1) * out]

    half = D // 2
    for turn, target in enumerate((away_ref, here_ref)):
        for i, (place, _, yrel) in enumerate(quarters(rep, 1 - turn)):
            block = 2 * turn + i // 2
            rows = slice(yrel * half, (yrel + 1) * half)
            target[place, :, :joint] = nn(normed_t_ref[rows], chosen[block, :, :joint]).astype(BF)
            target[place, :, joint:] = nn(context_t_ref[rows], chosen[block, :, joint:]).astype(BF)


def attention_back(project, att, context_back, attended, normed_t, context_t):
    tokens = project.shape[0]
    piece = (4, D // 2, D)
    return kernel_call(
        "attention_back",
        attention_back_kernel,
        [kept(tokens, 3 * D), shape(1, 3 * D), kept(*piece), kept(*piece)],
        (),
        near(project, att, context_back, attended, normed_t, context_t),
        [((4, tokens, D), BF)],
        cost(4 * tokens * D * FF),
    )


def token_back_kernel(
    gain_ref,
    x_ref,
    middle_ref,
    back_ref,
    wj_ref,
    joint_ref,
    out_ref,
    gain2_ref,
    shift2_ref,
    wide_ref,
    narrow_ref,
    token_ref,
    sums_ref,
):
    unit, inverse = norm_parts(x_ref[...].astype(F32))
    part, gain1, shift1 = norm_back(unit, inverse, as_row(gain_ref), nt(back_ref[...], wj_ref[...]))
    token_ref[...] = middle_ref[...] + part
    line = 0
    rest = (joint_ref, out_ref, gain2_ref, shift2_ref, wide_ref, narrow_ref)
    for value in [gain1, shift1] + [ref[...] for ref in rest]:
        for i in range(value.shape[1] // 128):
            sums_ref[line : line + 1] = value[:, i * 128 : (i + 1) * 128]
            line += 1
    sums_ref[line:] = jnp.zeros((sums_ref.shape[0] - line, 128), F32)


def token_back(gain, x, middle, back, wj, sums):
    return kernel_call(
        "token_back",
        token_back_kernel,
        [shape(x.shape[0], D), shape(ALL_LINES, 128)],
        (),
        (gain, *near(x, middle, back, wj), *sums),
        (),
        cost(6 * x.shape[0] * D * D),
    )


def low_rank_kernel(
    hidden, own_ref, near_ref, wm_ref, down_ref, head_ref, other_ref, box, back
):
    rows = own_ref.shape[0]
    box[:rows] = own_ref[...]
    box[rows:] = near_ref[...]
    part = down_ref.shape[0]
    start = box.shape[1] - D
    rep = lax.axis_index("rep")
    for r in range(D // part):

        @pl.when(rep == r)
        def _():
            for i, b in enumerate((r, r ^ 2)):
                back[i] = box[:, start + b * part : start + (b + 1) * part]

    wide = head_ref.shape[1]
    for i in range(2):
        block = jnp.bitwise_xor(rep, 2 * i)
        here = wm_ref[pl.ds(pl.multiple_of(block * part, SLOT), part), :]
        pooled = nt(box[:, start:], here).astype(BF)
        down = tn(pooled, box[:, :hidden])
        head = tn(back[i], box[:, hidden : hidden + wide])
        if i == 0:
            down_ref[...] = down
            head_ref[...] = head
        else:
            other_ref[:, :hidden] = down.astype(BF)
            other_ref[:, hidden:] = head.astype(BF)


def low_rank(blocks, parts, own, far, wm):
    rows = 2 * own.shape[0]
    hidden, wide, part = FF // blocks, D // blocks, D // parts
    return kernel_call(
        "low_rank",
        functools.partial(low_rank_kernel, hidden),
        [shape(part, hidden), shape(part, wide), shape(part, hidden + wide, dtype=BF)],
        (),
        near(own, far, wm),
        [((rows, own.shape[1]), BF), ((2, rows, part), BF)],
        cost(2 * rows * D * D),
    )


def finish_kernel(groups, *refs):
    up, last, first, lines = (
        [refs[sum(groups[:i]) + n] for n in range(groups[i])] for i in range(4)
    )
    loss_ref, down_ref, head_ref, other_ref = refs[sum(groups) : sum(groups) + 4]
    (
        joint_ref,
        out_ref,
        up_block_ref,
        down_block_ref,
        head_block_ref,
        loss_out_ref,
        *vector_refs,
    ) = refs[sum(groups) + 4 :]

    def total(terms):
        return sum(ref[...].astype(F32) for ref in terms)

    half = up[0].shape[1]
    up_block_ref[:, :half] = total(up)
    up_block_ref[:, half:] = total(last)
    both = total(first)
    wide = joint_ref.shape[1]
    joint_ref[...] = both[:, :wide]
    out_ref[...] = both[:, wide:]
    hidden = down_ref.shape[1]
    down_block_ref[...] = down_ref[...] + other_ref[:, :hidden].astype(F32)
    head_block_ref[...] = (head_ref[...] + other_ref[:, hidden:].astype(F32)).T
    loss_out_ref[...] = loss_ref[...].reshape(1)
    vectors = total(lines)
    starts = (GAIN1, SHIFT1, JOINT, OUT, GAIN2, SHIFT2, WIDE, NARROW)
    for start, ref in zip(starts, vector_refs):
        for i in range(ref.shape[0] // 128):
            line = start // 128 + i
            if start == JOINT and i >= D // 128:
                line += D // 128
            ref[pl.ds(i * 128, 128)] = vectors[line]


def finish(up, last, first, vectors, loss, low, joint):
    rows = last[0].shape[0]
    sizes = (D, D, 2 * D, D, D, D, FF, D)
    return kernel_call(
        "finish",
        functools.partial(finish_kernel, [len(v) for v in (up, last, first, vectors)]),
        [
            shape(rows, joint),
            shape(rows, D - joint),
            shape(rows, D),
            shape(*low[0].shape),
            shape(*low[1].shape[::-1]),
            shape(1),
        ]
        + [shape(n) for n in sizes],
        (),
        (*up, *last, *first, *vectors, loss, *low),
    )


def both_pairs(partner):
    dp, rep = lax.axis_size("dp"), lax.axis_size("rep")
    pairs = []
    for i in range(dp):
        for j in range(rep):
            a, b = partner(i, j)
            pairs.append((i * rep + j, a * rep + b))
    return pairs


def exchange(value, partner):
    return lax.ppermute(value, ("dp", "rep"), both_pairs(partner))


def first_turn(i, j):
    return (i, j ^ 2) if j & 1 == 0 else (i ^ 1, j)


def second_turn(i, j):
    return (i ^ 1, j) if j & 1 == 0 else (i, j ^ 2)


def added(a, b):
    return (a.astype(F32) + b.astype(F32)).astype(BF)


def halved(here, got):
    half = here.shape[0] // 2
    return added(here[:half], got[:half]), added(here[half:], got[half:])


def parted(here, got, count):
    rows = here.shape[-2] // count
    parts = [slice(i * rows, (i + 1) * rows) for i in range(count)]
    return [added(here[..., p, :], got[..., p, :]) for p in parts]


def core_turn(i, j):
    return i, j ^ 1


def across(i, j):
    return i, j ^ 2


def group_round(keep, got, group):
    masks = group_masks(group)
    bits = len(group)
    parts = parted(keep, got, len(masks))
    place = [sum(((c >> n) & 1) << (bits - 1 - n) for n in range(bits)) for c in range(len(masks))]
    return [parts[0]] + [
        exchange(parts[place[c]], lambda i, j: (i ^ masks[c][0], j)) for c in range(1, len(masks))
    ]


order = lax.optimization_barrier


def dp_groups():
    bits = [("dp", b) for b in range(1, lax.axis_size("dp").bit_length() - 1)]
    return [bits[i : i + 2] for i in range(0, len(bits), 2)] + [[("dp", 0)]]


def all_groups():
    bits = [("rep", b) for b in range(1, lax.axis_size("rep").bit_length() - 1)]
    groups = dp_groups()
    return groups[:-1] + [groups[-1] + bits, [("rep", 0)]]


def group_masks(group):
    out = [(0, 0)]
    for axis, bit in group:
        out += [(a | 1 << bit, b) if axis == "dp" else (a, b | 1 << bit) for a, b in out]
    return out


def gather_masks(rounds, blocks):
    bits = [0] + list(range(blocks.bit_length() - 2, 0, -1))
    masks, used = [0], 0
    for count in rounds:
        for bit in bits[used : used + count]:
            masks = masks + [m | 1 << bit for m in masks]
        used += count
    return masks


def split_round(value, wide, group):
    blocks = (value.shape[1] - D) // wide
    turns = group_masks(group)
    text = value[:, blocks * wide :]
    pieces = []
    for c, (a, b) in enumerate(turns):
        chosen = [value[:, i * wide : (i + 1) * wide] for i in range(c, blocks, len(turns))]
        piece = jnp.concatenate(chosen + [text], axis=1)
        pieces.append(piece if c == 0 else exchange(piece, lambda i, j: (i ^ a, j ^ b)))
    return pieces


def round_of(value, group):
    return [value] + [
        exchange(value, lambda i, j: (i ^ a, j ^ b)) for a, b in group_masks(group)[1:]
    ]


def relative_rows(value, blocks):
    rows = value.shape[0] // blocks
    if rows % SLOT == 0:
        return value
    bits = blocks.bit_length() - 1
    place = jnp.arange(blocks, dtype=jnp.int32)
    source = jnp.zeros_like(place)
    for bit in range(bits):
        source = source + ((place >> (bits - 1 - bit)) & 1) * (1 << bit)
    source = source ^ lax.axis_index("dp")
    return value.reshape(blocks, rows, -1)[source].reshape(value.shape)


def local(
    incoming_activations,
    caption_final_place,
    paired_picture,
    caption_weight,
    locked_picture_features,
    softmax_heat,
    premix_scaling_factor,
    premix_shift_term,
    stacked_mixing_matrix,
    asking_reading_offsets,
    mixing_result_matrix,
    mixing_result_offset,
    premlp_scaling_factor,
    premlp_shift_term,
    widening_matrix,
    widening_offset,
    narrowing_matrix,
    narrowing_offset,
    caption_mapping_matrix,
    picture_mapping_matrix,
):
    both = ("dp", "rep")
    devices = lax.axis_size(both)
    blocks = lax.axis_size("dp")
    parts = lax.axis_size("rep")
    captions = caption_final_place.shape[0]
    images = locked_picture_features.shape[0]
    groups = all_groups()
    pieces = round_of(jnp.pad(locked_picture_features, ((0, SLOT - images), (0, 0))), groups[0])
    project, normed_t = project_tokens(
        blocks,
        premix_scaling_factor,
        premix_shift_term,
        asking_reading_offsets,
        incoming_activations,
        stacked_mixing_matrix,
    )
    project, pieces = order((project, pieces))
    for group in groups[1:-1]:
        pieces = round_of(jnp.concatenate(pieces), group)
    att, context_t, middle = attend_tokens(
        blocks,
        caption_final_place,
        mixing_result_offset,
        incoming_activations,
        project,
        mixing_result_matrix,
    )
    middle, pieces = order((middle, pieces))
    own, far = round_of(jnp.concatenate(pieces), groups[-1])
    second_t, slope, box, text, factor, embed = widen_tokens(
        blocks,
        caption_final_place,
        premlp_scaling_factor,
        premlp_shift_term,
        widening_offset,
        narrowing_offset,
        middle,
        widening_matrix,
        narrowing_matrix,
        caption_mapping_matrix,
    )
    normed_t, context_t, second_t = (
        relative_rows(v, blocks) for v in (normed_t, context_t, second_t)
    )
    embed, far = order((embed, far))
    picture, score, row, inverse, stats = contrast(
        images,
        parts,
        sum(groups, []),
        softmax_heat,
        own,
        far,
        picture_mapping_matrix,
        embed,
        paired_picture,
        caption_weight,
    )
    groups = dp_groups()
    high = [[bit] for group in groups[:-1] for bit in group]
    factor_groups = groups[-1:] + high[::-1]
    stats = round_of(stats, [("rep", 0)])
    stats = round_of(merge(stats), [("rep", 1)] + groups[-1])
    for group in groups[:-1]:
        stats = round_of(merge(stats), group)
    back, away, here, pooled_back, loss, down_bias, up_bias, *pieces = head_back(
        images,
        [len(group) for group in factor_groups],
        softmax_heat,
        caption_final_place,
        stats,
        score,
        row,
        inverse,
        caption_weight,
        paired_picture,
        picture,
        text,
        factor,
        caption_mapping_matrix,
        narrowing_matrix,
        slope,
        second_t,
        box,
    )
    loss = loss / (captions * devices)
    got = exchange(away, core_turn)
    pieces = pieces[:1] + [
        exchange(piece, lambda i, j: (i ^ a, j ^ b))
        for piece, (a, b) in zip(pieces[1:], group_masks(factor_groups[0])[1:])
    ]
    total, attended, context_back, gain2, shift2, out_bias = middle_back(
        caption_final_place,
        premlp_scaling_factor,
        pooled_back,
        back,
        widening_matrix,
        middle,
        mixing_result_matrix,
    )
    context_back, got, pieces = order((context_back, got, pieces))
    up, send = halved(here[0], got[0])
    got_up = exchange(send, first_turn)
    last, got_last = group_round(here[1], got[1], high[0])
    pieces = split_round(jnp.concatenate(pieces), box.shape[2], factor_groups[1])
    project_back, joint_bias, away, here = attention_back(
        project, att, context_back, attended, normed_t, context_t
    )
    project_back, away, got_up, got_last, pieces = order(
        (project_back, away, got_up, got_last, pieces)
    )
    up, send = halved(up, got_up)
    got_up = exchange(send[0], second_turn)
    got = exchange(away, core_turn)
    for group in high[1:]:
        last, got_last = group_round(last, got_last, group)
    for group in factor_groups[2:]:
        pieces = split_round(jnp.concatenate(pieces), box.shape[2], group)
    joint = 3 * D // parts
    token, sums = token_back(
        premix_scaling_factor,
        incoming_activations,
        total,
        project_back,
        stacked_mixing_matrix,
        (joint_bias, out_bias, gain2, shift2, up_bias, down_bias),
    )
    sums, got, got_up = order((sums, got, got_up))
    first, send = halved(here, got)
    got = exchange(send, first_turn)
    up = added(up[0], got_up)
    lines = round_of(sums, [("rep", 0)])
    lines = round_of(sum(lines), [("rep", 1)])
    got, lines, got_last, pieces = order((got, lines, got_last, pieces))
    first, send = halved(first, got)
    last = added(last, got_last)
    message = [send[0], jnp.concatenate([last[1], last[3]], axis=1)]
    got = exchange(jnp.concatenate(message), second_turn)
    rows = up.shape[0] // 2
    high_turn = lambda i, j: (i ^ (1 << high[0][0][1]), j)
    got_up = exchange(up[rows:], high_turn)
    up = up[:rows]
    lines = round_of(sum(lines), groups[-1])
    factors = jnp.concatenate(pieces)
    far = exchange(factors, core_turn)
    got, got_up, lines, far = order((got, got_up, lines, far))
    tall = first.shape[1]
    half = last.shape[2]
    first, got, tail = first[0], got[:tall], got[tall:]
    got_last = exchange(added(last[2], tail[:, half:]), first_turn)
    last = added(last[0], tail[:, :half])
    *low, other = low_rank(blocks, parts, factors, far, caption_mapping_matrix)
    other = exchange(other, across)
    for i, group in enumerate(high):
        if i:
            got, lines = order((got, lines))
        first, got = group_round(first, got, group)
        for later in high[i + 1 : i + 2]:
            up, got_up = group_round(up, got_up, later)
        lines = round_of(sum(lines), group)
    up, last, first, vectors = [up, got_up], [last, got_last], [first, got], lines
    joint_block, out_block, up_block, down_block, head_block, loss, *grads = finish(
        up, last, first, vectors, loss, (*low, other), joint
    )
    return (
        loss,
        token,
        grads[0],
        grads[1],
        joint_block,
        grads[2],
        out_block,
        grads[3],
        grads[4],
        grads[5],
        up_block,
        grads[6],
        down_block.T,
        grads[7],
        head_block,
    )


def solution(mesh):
    spread = P(("dp", "rep"), None)
    line = P(("dp", "rep"))
    block = P("dp", "rep")
    in_specs = (spread, line, line, line, spread) + (P(),) * 15
    out_specs = (
        P(),
        spread,
        P(),
        P(),
        block,
        P(),
        block,
        P(),
        P(),
        P(),
        block,
        P(),
        block,
        P(),
        block,
    )
    return jax.shard_map(local, mesh=mesh, in_specs=in_specs, out_specs=out_specs, check_vma=False)
```

```python
import functools

import jax
import jax.numpy as jnp
from jax import lax
from jax.experimental import pallas as pl
from jax.experimental.pallas import tpu as pltpu
from jax.sharding import PartitionSpec as P

D = 768
HEADS = 12
HEAD = 64
SEQ = 16
FF = 3072
GROUP = 128
PAIRS = HEADS // 2
SLOT = 16
BF = jnp.bfloat16
F32 = jnp.float32

epsilon = 1e-06
negative = -1e30
scale = HEAD ** (-0.5)
LIMIT = 16 * 1024 * 1024

GAIN1, SHIFT1, JOINT, OUT, GAIN2, SHIFT2, WIDE, NARROW = 0, 768, 1536, 3840, 4608, 5376, 6144, 9216
VECTORS = 9984
LINES = VECTORS // 128
ALL_LINES = LINES + -LINES % 8

vmem = pl.BlockSpec(memory_space=pltpu.VMEM)
smem = pl.BlockSpec(memory_space=pltpu.SMEM)


def dot(a, b, dims):
    return lax.dot_general(a, b, (dims, ((), ())), preferred_element_type=F32)


def nn(a, b):
    return dot(a, b, ((1,), (0,)))


def nt(a, b):
    return dot(a, b, ((1,), (1,)))


def tn(a, b):
    return dot(a, b, ((0,), (0,)))


def cost(flops):
    return pl.CostEstimate(flops=flops, transcendentals=0, bytes_accessed=0)


def shape(*dims, dtype=F32):
    return jax.ShapeDtypeStruct(dims, dtype)


def kept(*dims, dtype=BF):
    return pltpu.VMEM(dims, dtype)


def near(*values):
    return [pltpu.with_memory_space_constraint(v, pltpu.VMEM) for v in values]


def kernel_call(name, body, results, small, operands, scratch=(), estimate=None, limit=LIMIT):
    return pl.pallas_call(
        body,
        out_shape=results,
        in_specs=[smem] * len(small) + [vmem] * len(operands),
        out_specs=[vmem] * len(results),
        scratch_shapes=[pltpu.VMEM(s, t) for s, t in scratch],
        compiler_params=pltpu.CompilerParams(vmem_limit_bytes=limit),
        cost_estimate=estimate,
        name=name,
    )(*small, *operands)


def iota(dims, axis):
    return lax.broadcasted_iota(jnp.int32, dims, axis)


def norm_parts(values):
    average = jnp.mean(values, axis=-1, keepdims=True)
    centred = values - average
    inverse = lax.rsqrt(jnp.mean(centred * centred, axis=-1, keepdims=True) + epsilon)
    return centred * inverse, inverse


def norm_back(unit, inverse, gain, back):
    inner = back * gain
    part = inverse * (
        inner
        - jnp.mean(inner, axis=-1, keepdims=True)
        - unit * jnp.mean(inner * unit, axis=-1, keepdims=True)
    )
    return part, jnp.sum(back * unit, axis=0, keepdims=True), jnp.sum(back, axis=0, keepdims=True)


def split(value):
    high = value.astype(BF)
    return high, (value - high.astype(F32)).astype(BF)


def two(value):
    return jnp.concatenate(split(value), axis=0)


def as_row(ref):
    return ref[...].reshape(1, ref.shape[0])


def as_column(ref):
    size = ref.shape[0]
    same = iota((size, size), 0) == iota((size, size), 1)
    row = as_row(ref)
    return jnp.sum(jnp.where(same, row, jnp.zeros_like(row)), axis=1, keepdims=True)


def token_limits(ref):
    place = as_row(ref).astype(F32)
    captions = place.shape[1]
    tokens = captions * SEQ
    owner = (iota((tokens, captions), 0) // SEQ == iota((tokens, captions), 1)).astype(F32)
    column = jnp.sum(owner * place, axis=1, keepdims=True)
    line = nt(place.astype(BF), owner.astype(BF))
    return line, column


def pool_mask(line, captions):
    dims = (captions, captions * SEQ)
    token = iota(dims, 1)
    inside = (token % SEQ).astype(F32) <= line
    return jnp.where((token // SEQ == iota(dims, 0)) & inside, 1.0, 0.0)


def spread_mask(column, captions):
    dims = (captions * SEQ, captions)
    token = iota(dims, 0)
    inside = (token % SEQ).astype(F32) <= column
    return jnp.where((token // SEQ == iota(dims, 1)) & inside, 1.0, 0.0)


def head_masks():
    lane = iota((1, 2 * HEAD), 1)
    even = (lane < HEAD).astype(F32)
    return even.astype(BF), (1.0 - even).astype(BF)


def caption_masks():
    lane = iota((SEQ, GROUP), 1) // SEQ
    return [lane == c for c in range(GROUP // SEQ)]


def compact(full, picks):
    out = full[:SEQ]
    for c in range(1, len(picks)):
        out = jnp.where(picks[c], full[c * SEQ : (c + 1) * SEQ], out)
    return out


def expand(low, lows):
    return jnp.concatenate([low * mask for mask in lows], axis=0)


def both_heads(value, masks):
    return jnp.concatenate([value * masks[0], value * masks[1]], axis=0)


def store_permuted(ref, value, dp, blocks):
    rows = value.shape[0] // blocks
    bits = blocks.bit_length() - 1
    if rows % SLOT:
        ref[...] = value
        return
    for b in range(blocks):
        k = jnp.bitwise_xor(dp, b)
        place = 0
        for bit in range(bits):
            place = place + ((k >> bit) & 1) * (1 << (bits - 1 - bit))
        ref[pl.ds(pl.multiple_of(place * rows, SLOT), rows), :] = value[b * rows : (b + 1) * rows]


def box_width(blocks):
    used = (FF + D) // blocks
    return used + -used % 128


def norm_kernel(x_ref, unit_ref, inverse_ref):
    unit_ref[...], inverse_ref[...] = norm_parts(x_ref[...].astype(F32))


def norm_tokens(x):
    tokens = x.shape[0]
    return kernel_call(
        "norm_tokens",
        norm_kernel,
        [kept(tokens, D, dtype=F32), kept(tokens, 1, dtype=F32)],
        (),
        near(x),
        (),
        cost(16 * tokens * D),
    )


def project_kernel(gain_ref, shift_ref, joint_ref, unit_ref, wj_ref, project_ref, normed_ref):
    normed_ref[...] = (unit_ref[...] * as_row(gain_ref) + as_row(shift_ref)).astype(BF)
    joint = as_row(joint_ref)
    for i, bias in enumerate((joint[:, :D], 0.0, joint[:, D:])):
        lanes = slice(i * D, (i + 1) * D)
        project_ref[:, lanes] = (nn(normed_ref[...], wj_ref[:, lanes]) + bias).astype(BF)


def project_tokens(gain, shift, joint, unit, wj):
    tokens = unit.shape[0]
    return kernel_call(
        "project_tokens",
        project_kernel,
        [kept(tokens, 3 * D), kept(tokens, D)],
        (),
        (gain, shift, joint, *near(unit, wj)),
        (),
        cost(6 * tokens * D * D),
    )


def turn_kernel(blocks, *refs):
    dp = lax.axis_index("dp")
    count = len(refs) // 2
    for source, target in zip(refs[:count], refs[count:]):
        store_permuted(target, source[...].T, dp, blocks)


def turn_tokens(blocks, *values):
    return kernel_call(
        "turn_tokens",
        functools.partial(turn_kernel, blocks),
        [kept(*v.shape[::-1]) for v in values],
        (),
        near(*values),
        (),
        cost(32 * values[0].shape[0] * D),
    )


def attend_kernel(
    place_ref, out_ref, x_ref, project_ref, wo_ref, att_ref, context_ref, middle_ref
):
    line, _ = token_limits(place_ref)
    masks = head_masks()
    picks = caption_masks()
    lows = [pick.astype(F32).astype(BF) for pick in picks]
    key_place = iota((SEQ, GROUP), 0).astype(F32)

    def attend(h, carry):
        at = pl.multiple_of(h * 2 * HEAD, 128)
        for g in range(x_ref.shape[0] // GROUP):
            here = slice(g * GROUP, (g + 1) * GROUP)
            query = project_ref[here, pl.ds(at, 128)]
            keys = both_heads(project_ref[here, pl.ds(pl.multiple_of(D + at, 128), 128)], masks)
            values = both_heads(
                project_ref[here, pl.ds(pl.multiple_of(2 * D + at, 128), 128)], masks
            )
            scores = nt(keys, query)
            allowed = key_place <= line[:, here]
            parts = []
            for e in range(2):
                score = compact(scores[e * GROUP : (e + 1) * GROUP], picks) * scale
                score = jnp.where(allowed, score, negative)
                score = jnp.exp(score - jnp.max(score, axis=0, keepdims=True))
                weight = score / jnp.sum(score, axis=0, keepdims=True)
                att_ref[2 * h + e, :, here] = weight
                parts.append(expand(weight.astype(BF), lows))
            context_ref[here, pl.ds(at, 128)] = tn(jnp.concatenate(parts, axis=0), values).astype(BF)
        return carry

    lax.fori_loop(0, PAIRS, attend, 0)
    middle_ref[...] = x_ref[...].astype(F32) + (nn(context_ref[...], wo_ref[...]) + as_row(out_ref))


def attend_tokens(place, out, x, project, wo):
    tokens = x.shape[0]
    return kernel_call(
        "attend_tokens",
        attend_kernel,
        [kept(HEADS, SEQ, tokens, dtype=F32), kept(tokens, D), kept(tokens, D, dtype=F32)],
        (),
        (place, out, *near(x, project, wo)),
        (),
        cost(4 * tokens * D * D),
    )


def widen_kernel(
    blocks,
    place_ref,
    gain_ref,
    shift_ref,
    wide_ref,
    narrow_ref,
    middle_ref,
    wu_ref,
    wn_ref,
    wm_ref,
    second_ref,
    unit_ref,
    inverse_ref,
    slope_ref,
    box_ref,
    text_ref,
    scale_ref,
    embed_ref,
    branch,
    wide,
    mean,
):
    captions = place_ref.shape[0]
    line, column = token_limits(place_ref)
    pool = pool_mask(line, captions)
    share = 1.0 / jnp.sum(pool, axis=1, keepdims=True)
    unit, inverse_ref[...] = norm_parts(middle_ref[...])
    unit_ref[...] = unit
    second_ref[...] = (unit * as_row(gain_ref) + as_row(shift_ref)).astype(BF)
    branch[...] = jnp.zeros_like(branch)
    wide[...] = as_row(wide_ref)
    pool_low = pool.astype(BF)
    c0 = 0.7978845608028654
    c1 = c0 * 0.044715
    step = 512

    def widen(i, carry):
        at = pl.multiple_of(i * step, 128)
        upper = nn(second_ref[...], wu_ref[:, pl.ds(at, step)]) + wide[:, pl.ds(at, step)]
        square = upper * upper
        bend = jnp.tanh(upper * (c0 + c1 * square))
        half = 0.5 + 0.5 * bend
        active = upper * half
        slope_ref[:, pl.ds(at, step)] = (
            half * (1.0 + (upper - active) * (2.0 * c0 + 6.0 * c1 * square))
        ).astype(BF)
        parts = two(nn(pool_low, active.astype(BF)) * share)
        mean[:, pl.ds(at, step)] = parts[:captions]
        branch[...] += nn(parts, wn_ref[pl.ds(at, step), :])
        return carry

    lax.fori_loop(0, FF // step, widen, 0, unroll=2)
    inside = jnp.where((iota((captions * SEQ, 1), 0) % SEQ).astype(F32) <= column, 1.0, 0.0)
    weight = inside / (column + 1.0)
    pooled = jnp.sum((middle_ref[...] * weight).reshape(captions, SEQ, D), axis=1)
    pooled = (pooled + (branch[:captions] + branch[captions:] + as_row(narrow_ref))).astype(BF)
    hidden, part = FF // blocks, D // blocks
    for b in range(blocks):
        box_ref[b, :, :hidden] = mean[:, b * hidden : (b + 1) * hidden]
        box_ref[b, :, hidden : hidden + part] = pooled[:, b * part : (b + 1) * part]
    text = nn(pooled, wm_ref[...])
    factor = lax.rsqrt(jnp.sum(text * text, axis=1, keepdims=True) + epsilon)
    text_ref[...] = text
    scale_ref[...] = factor
    embed_ref[...] = (text * factor).astype(BF)


def widen_tokens(blocks, place, gain, shift, wide, narrow, middle, wu, wn, wm):
    tokens = middle.shape[0]
    captions = place.shape[0]
    return kernel_call(
        "widen_tokens",
        functools.partial(widen_kernel, blocks),
        [
            kept(tokens, D),
            kept(tokens, D, dtype=F32),
            kept(tokens, 1, dtype=F32),
            kept(tokens, FF),
            kept(blocks, captions, box_width(blocks)),
            kept(captions, D, dtype=F32),
            kept(captions, 1, dtype=F32),
            kept(captions, D),
        ],
        (),
        (place, gain, shift, wide, narrow, *near(middle, wu, wn, wm)),
        [
            ((2 * captions, D), F32),
            ((1, FF), F32),
            ((captions, FF), BF),
        ],
        cost(2 * tokens * D * FF),
    )


def match_of(paired, columns, images):
    column = iota((1, columns), 1)
    valid = column % SLOT < images
    name = jnp.where(valid, (column // SLOT) * images + column % SLOT, -1)
    return paired == name, valid


def contrast_kernel(
    images,
    parts,
    bits,
    heat_ref,
    own_ref,
    near_ref,
    wp_ref,
    embed_ref,
    paired_ref,
    weight_ref,
    picture_ref,
    score_ref,
    row_ref,
    inverse_ref,
    stats_ref,
    features,
):
    half = own_ref.shape[0] // SLOT
    for far, ref in enumerate((own_ref, near_ref)):

        def place(i, carry, far=far, ref=ref):
            p = i + far * half
            index = {axis: lax.axis_index(axis) for axis in ("dp", "rep")}
            for n, (axis, bit) in enumerate(bits):
                index[axis] = jnp.bitwise_xor(index[axis], ((p >> n) & 1) << bit)
            to = pl.ds(pl.multiple_of((index["dp"] * parts + index["rep"]) * SLOT, SLOT), SLOT)
            features[to, :] = ref[pl.ds(pl.multiple_of(i * SLOT, SLOT), SLOT), :]
            return carry

        lax.fori_loop(0, half, place, 0, unroll=4)
    picture = nn(features[...], wp_ref[...])
    picture = (
        picture * lax.rsqrt(jnp.sum(picture * picture, axis=1, keepdims=True) + epsilon)
    ).astype(BF)
    picture_ref[...] = picture
    score = nt(embed_ref[...], picture) / heat_ref[0]
    match, valid = match_of(as_column(paired_ref), score.shape[1], images)
    score = jnp.where(valid, score, negative)
    score_ref[...] = score
    top = jnp.max(score, axis=1, keepdims=True)
    row = jnp.log(jnp.sum(jnp.exp(score - top), axis=1, keepdims=True)) + top
    row_ref[...] = row
    positive = jnp.sum(jnp.where(match, score, 0.0), axis=1, keepdims=True)
    hits = jnp.where(match, 1.0, 0.0)
    counts = jnp.sum(hits, axis=0, keepdims=True)
    inverse = 1.0 / jnp.sum(hits * counts, axis=1, keepdims=True)
    inverse_ref[...] = inverse
    total = jnp.sum(as_column(weight_ref) * (row - positive - positive * inverse))
    best = jnp.max(score, axis=0, keepdims=True)
    mass = jnp.sum(jnp.exp(score - best), axis=0, keepdims=True)
    mass = jnp.where(iota(mass.shape, 1) == images, total, mass)
    wide = best.shape[1] // 4
    rows = [v[:, i * wide : (i + 1) * wide] for v in (best, mass) for i in range(4)]
    stats_ref[...] = jnp.concatenate(rows, axis=0)


def contrast(images, parts, bits, heat, own, far, wp, embed, paired, weight):
    captions = embed.shape[0]
    columns = 2 * own.shape[0]
    return kernel_call(
        "contrast",
        functools.partial(contrast_kernel, images, parts, bits),
        [
            kept(columns, D),
            kept(captions, columns, dtype=F32),
            kept(captions, 1, dtype=F32),
            kept(captions, 1, dtype=F32),
            shape(8, columns // 4),
        ],
        (heat,),
        (*near(own, far, wp, embed), paired, weight),
        [((columns, D), BF)],
        cost(2 * columns * D * D),
        max(LIMIT, columns * 8192),
    )


def merged(refs):
    best = functools.reduce(jnp.maximum, [ref[:4] for ref in refs])
    mass = sum(ref[4:] * jnp.exp(ref[:4] - best) for ref in refs)
    return best, mass


def merge_kernel(*refs):
    *given, out_ref = refs
    best, mass = merged(given)
    out_ref[...] = jnp.concatenate([best, mass], axis=0)


def merge(stats):
    return kernel_call("merge", merge_kernel, [shape(*stats[0].shape)], (), stats)[0]


def quarters(rep, away, flip=0):
    core = rep & 1
    out = []
    for xrel in range(2):
        for yrel in range(2):
            block = jnp.bitwise_xor(rep, 2 * xrel + away)
            x_first = 1 - core if away == flip else core
            out.append((jnp.where(x_first == 1, 2 * xrel + yrel, 2 * yrel + xrel), block, yrel))
    return out


def head_back_kernel(
    images,
    count_stats,
    rounds,
    heat_ref,
    place_ref,
    score_ref,
    row_ref,
    inverse_ref,
    weight_ref,
    paired_ref,
    picture_ref,
    text_ref,
    scale_ref,
    wm_ref,
    wn_ref,
    slope_ref,
    second_t_ref,
    box_ref,
    *refs,
):
    first = 1 << rounds[0]
    pieces = refs[len(refs) - first :]
    stats = refs[:count_stats]
    (
        back_ref,
        away_ref,
        here_ref,
        pooled_ref,
        loss_ref,
        down_bias_ref,
        up_bias_ref,
    ) = refs[count_stats : len(refs) - first]
    rep = lax.axis_index("rep")
    heat = heat_ref[0]
    captions = place_ref.shape[0]
    line, column = token_limits(place_ref)
    count = jnp.sum(pool_mask(line, captions), axis=1, keepdims=True)
    owner = spread_mask(column, captions).astype(BF)
    owner = jnp.concatenate([owner, owner], axis=1)

    score = score_ref[...]
    match, valid = match_of(as_column(paired_ref), score.shape[1], images)
    best, mass = merged(stats)
    column_log = jnp.log(mass) + best
    column_log = jnp.concatenate([column_log[i : i + 1] for i in range(4)], axis=1)
    loss_ref[...] = mass[:1, images : images + 1] + jnp.sum(
        jnp.where(valid, column_log, 0.0), axis=1, keepdims=True
    )
    weight = as_column(weight_ref)
    graded = (
        weight * jnp.exp(score - row_ref[...])
        + jnp.exp(score - column_log)
        - jnp.where(match, weight * (1.0 + inverse_ref[...]), 0.0)
    )
    graded = jnp.where(valid, graded / heat, 0.0).astype(BF)
    embed_back = nn(graded, picture_ref[...])
    text = text_ref[...]
    factor = scale_ref[...]
    text_dot = jnp.sum(text * embed_back, axis=1, keepdims=True)
    text_back = (factor * embed_back - text * (factor * factor * factor) * text_dot).astype(BF)
    blocks, _, wide = box_ref.shape
    masks = gather_masks(rounds, blocks)
    for c, piece_ref in enumerate(pieces):
        for i in range(blocks // first):
            block = jnp.bitwise_xor(lax.axis_index("dp"), masks[i * first + c])
            piece_ref[:, i * wide : (i + 1) * wide] = box_ref[block]
        piece_ref[:, (blocks // first) * wide :] = text_back
    pooled_back = nt(text_back, wm_ref[...])
    pooled_ref[...] = pooled_back
    branch = (pooled_back / count).astype(BF)
    down_bias_ref[...] = jnp.sum(branch.astype(F32) * count, axis=0, keepdims=True)
    ones = jnp.ones((SLOT, back_ref.shape[0]), BF)
    step = 512

    def widen(i, carry):
        at = pl.multiple_of(i * step, 128)
        part = nn(owner, two(nt(branch, wn_ref[pl.ds(at, step), :])))
        part = (part * slope_ref[:, pl.ds(at, step)].astype(F32)).astype(BF)
        back_ref[:, pl.ds(at, step)] = part
        up_bias_ref[:, pl.ds(at, step)] = nn(ones, part)[:1]
        return carry

    lax.fori_loop(0, FF // step, widen, 0, unroll=2)
    half = second_t_ref.shape[0] // 2
    wide = FF // 4
    for turn, target in enumerate((away_ref, here_ref)):
        for place, block, yrel in quarters(rep, 1 - turn):
            part = nn(
                second_t_ref[yrel * half : (yrel + 1) * half],
                back_ref[:, pl.ds(pl.multiple_of(block * wide, 128), wide)],
            )
            for h in range(2):
                target[place, h] = part[:, h * (wide // 2) : (h + 1) * (wide // 2)].astype(BF)


def head_back(images, rounds, heat, place, stats, score, row, inverse, weight, paired, picture, text,
              factor, wm, wn, slope, second_t, box):
    captions = text.shape[0]
    tokens = slope.shape[0]
    piece = (4, 2, D // 2, FF // 8)
    return kernel_call(
        "head_back",
        functools.partial(head_back_kernel, images, len(stats), rounds),
        [
            kept(tokens, FF),
            kept(*piece),
            kept(*piece),
            kept(captions, D, dtype=F32),
            shape(1, 1),
            shape(1, D),
            shape(1, FF),
        ]
        + [shape(captions, (box.shape[0] >> rounds[0]) * box.shape[2] + D, dtype=BF)] * (1 << rounds[0]),
        (heat,),
        (
            place,
            *near(score, row, inverse),
            weight,
            paired,
            *near(picture, text, factor, wm, wn, slope, second_t, box),
            *stats,
        ),
        (),
        cost(2 * tokens * D * FF),
    )


def middle_back_kernel(
    place_ref,
    gain_ref,
    pooled_ref,
    back_ref,
    wu_ref,
    unit_ref,
    inverse_ref,
    wo_ref,
    total_ref,
    attended_ref,
    context_back_ref,
    gain_back_ref,
    shift_back_ref,
    bias_ref,
):
    captions = place_ref.shape[0]
    line, column = token_limits(place_ref)
    count = jnp.sum(pool_mask(line, captions), axis=1, keepdims=True)
    owner = spread_mask(column, captions).astype(BF)
    owner = jnp.concatenate([owner, owner], axis=1)
    second_back = nt(back_ref[...], wu_ref[...])
    part, gain_back_ref[...], shift_back_ref[...] = norm_back(
        unit_ref[...], inverse_ref[...], as_row(gain_ref), second_back
    )
    total = nn(owner, two(pooled_ref[...] / count)) + part
    total_ref[...] = total
    attended = total.astype(BF)
    attended_ref[...] = attended
    bias_ref[...] = nn(jnp.ones((SLOT, attended.shape[0]), BF), attended)[:1]
    context_back_ref[...] = nt(attended, wo_ref[...]).astype(BF)


def middle_back(place, gain, pooled, back, wu, unit, inverse, wo):
    tokens = back.shape[0]
    return kernel_call(
        "middle_back",
        middle_back_kernel,
        [
            kept(tokens, D, dtype=F32),
            kept(tokens, D),
            kept(tokens, D),
            shape(1, D),
            shape(1, D),
            shape(1, D),
        ],
        (),
        (place, gain, *near(pooled, back, wu, unit, inverse, wo)),
        (),
        cost(2 * tokens * D * (FF + D)),
    )


def attention_back_kernel(project_ref, att_ref, context_back_ref, back_ref, bias_ref):
    masks = head_masks()
    picks = caption_masks()
    lows = [pick.astype(F32).astype(BF) for pick in picks]
    low_scale = jnp.asarray(scale, BF)
    first = iota((GROUP, 2 * HEAD), 1) < HEAD
    tokens = project_ref.shape[0]

    def attend(h, carry):
        at = pl.multiple_of(h * 2 * HEAD, 128)
        at_k = pl.multiple_of(D + at, 128)
        at_v = pl.multiple_of(2 * D + at, 128)
        for g in range(tokens // GROUP):
            span = slice(g * GROUP, (g + 1) * GROUP)
            query = project_ref[span, pl.ds(at, 128)]
            keys = both_heads(project_ref[span, pl.ds(at_k, 128)], masks)
            values = both_heads(project_ref[span, pl.ds(at_v, 128)], masks)
            upper = context_back_ref[span, pl.ds(at, 128)]
            full = nt(values, upper)
            weights, grads = [], []
            for e in range(2):
                weight = att_ref[2 * h + e, :, span]
                part = compact(full[e * GROUP : (e + 1) * GROUP], picks)
                grad = weight * (part - jnp.sum(weight * part, axis=0, keepdims=True))
                weights.append(expand(weight.astype(BF), lows))
                grads.append(expand(grad.astype(BF) * low_scale, lows))
            weights = jnp.concatenate(weights, axis=0)
            grads = jnp.concatenate(grads, axis=0)
            back_ref[span, pl.ds(at, 128)] = tn(grads, keys).astype(BF)
            wide = nn(grads, query)
            back_ref[span, pl.ds(at_k, 128)] = jnp.where(first, wide[:GROUP], wide[GROUP:]).astype(
                BF
            )
            wide = nn(weights, upper)
            back_ref[span, pl.ds(at_v, 128)] = jnp.where(first, wide[:GROUP], wide[GROUP:]).astype(
                BF
            )
        return carry

    lax.fori_loop(0, PAIRS, attend, 0)
    ones = jnp.ones((SLOT, tokens), BF)
    for i in range(3):
        lanes = slice(i * D, (i + 1) * D)
        bias_ref[:, lanes] = nn(ones, back_ref[:, lanes])[:1]


def attention_back(project, att, context_back):
    tokens = project.shape[0]
    return kernel_call(
        "attention_back",
        attention_back_kernel,
        [kept(tokens, 3 * D), shape(1, 3 * D)],
        (),
        near(project, att, context_back),
        (),
        cost(3 * tokens * D * D),
    )


def left_columns_kernel(back_ref, normed_t_ref, away_ref, here_ref, chosen):
    rep = lax.axis_index("rep")
    joint = 3 * D // 4
    some = chosen.shape[2]
    for r in range(4):

        @pl.when(rep == r)
        def _():
            for i, k in enumerate((1, 3, 0, 2)):
                b = r ^ k
                chosen[i] = back_ref[:, b * joint : b * joint + some]

    half = D // 2
    for turn, target in enumerate((away_ref, here_ref)):
        for i, (place, _, yrel) in enumerate(quarters(rep, 1 - turn, 1)):
            lines = slice(yrel * half, (yrel + 1) * half)
            target[place] = nn(normed_t_ref[lines], chosen[2 * turn + i // 2]).astype(BF)


def right_columns_kernel(
    back_ref, attended_ref, normed_t_ref, context_t_ref, away_ref, here_ref, chosen
):
    rep = lax.axis_index("rep")
    joint = 3 * D // 4
    out = D // 4
    some = chosen.shape[2] - out
    for r in range(4):

        @pl.when(rep == r)
        def _():
            for i, k in enumerate((1, 3, 0, 2)):
                b = r ^ k
                chosen[i, :, :some] = back_ref[:, (b + 1) * joint - some : (b + 1) * joint]
                chosen[i, :, some:] = attended_ref[:, b * out : (b + 1) * out]

    half = D // 2
    for turn, target in enumerate((away_ref, here_ref)):
        for i, (place, _, yrel) in enumerate(quarters(rep, 1 - turn)):
            block = 2 * turn + i // 2
            lines = slice(yrel * half, (yrel + 1) * half)
            target[place, :, :some] = nn(normed_t_ref[lines], chosen[block, :, :some]).astype(BF)
            target[place, :, some:] = nn(context_t_ref[lines], chosen[block, :, some:]).astype(BF)


def columns_gradient(name, body, operands):
    tokens = operands[0].shape[0]
    piece = (4, D // 2, D // 2)
    return kernel_call(
        name,
        body,
        [kept(*piece), kept(*piece)],
        (),
        near(*operands),
        [((4, tokens, D // 2), BF)],
        cost(tokens * D * FF),
    )


def token_back_kernel(
    gain_ref,
    unit_ref,
    inverse_ref,
    middle_ref,
    back_ref,
    wj_ref,
    joint_ref,
    out_ref,
    gain2_ref,
    shift2_ref,
    wide_ref,
    narrow_ref,
    token_ref,
    sums_ref,
):
    part, gain1, shift1 = norm_back(
        unit_ref[...], inverse_ref[...], as_row(gain_ref), nt(back_ref[...], wj_ref[...])
    )
    token_ref[...] = middle_ref[...] + part
    line = 0
    rest = (joint_ref, out_ref, gain2_ref, shift2_ref, wide_ref, narrow_ref)
    for value in [gain1, shift1] + [ref[...] for ref in rest]:
        for i in range(value.shape[1] // 128):
            sums_ref[line : line + 1] = value[:, i * 128 : (i + 1) * 128]
            line += 1
    sums_ref[line:] = jnp.zeros((sums_ref.shape[0] - line, 128), F32)


def token_back(gain, unit, inverse, middle, back, wj, sums):
    return kernel_call(
        "token_back",
        token_back_kernel,
        [shape(unit.shape[0], D), shape(ALL_LINES, 128)],
        (),
        (gain, *near(unit, inverse, middle, back, wj), *sums),
        (),
        cost(6 * unit.shape[0] * D * D),
    )


def low_rank_kernel(
    hidden, own_ref, near_ref, wm_ref, down_ref, head_ref, other_ref, box, back
):
    rows = own_ref.shape[0]
    box[:rows] = own_ref[...]
    box[rows:] = near_ref[...]
    part = down_ref.shape[0]
    start = box.shape[1] - D
    rep = lax.axis_index("rep")
    for r in range(D // part):

        @pl.when(rep == r)
        def _():
            for i, b in enumerate((r, r ^ 2)):
                back[i] = box[:, start + b * part : start + (b + 1) * part]

    wide = head_ref.shape[1]
    for i in range(2):
        block = jnp.bitwise_xor(rep, 2 * i)
        here = wm_ref[pl.ds(pl.multiple_of(block * part, SLOT), part), :]
        pooled = nt(box[:, start:], here).astype(BF)
        down = tn(pooled, box[:, :hidden])
        head = tn(back[i], box[:, hidden : hidden + wide])
        if i == 0:
            down_ref[...] = down
            head_ref[...] = head
        else:
            other_ref[:, :hidden] = down.astype(BF)
            other_ref[:, hidden:] = head.astype(BF)


def low_rank(blocks, parts, own, far, wm):
    rows = 2 * own.shape[0]
    hidden, wide, part = FF // blocks, D // blocks, D // parts
    return kernel_call(
        "low_rank",
        functools.partial(low_rank_kernel, hidden),
        [shape(part, hidden), shape(part, wide), shape(part, hidden + wide, dtype=BF)],
        (),
        near(own, far, wm),
        [((rows, own.shape[1]), BF), ((2, rows, part), BF)],
        cost(2 * rows * D * D),
    )


def finish_kernel(groups, *refs):
    up, first, second, lines = (
        [refs[sum(groups[:i]) + n] for n in range(groups[i])] for i in range(4)
    )
    loss_ref, down_ref, head_ref, other_ref = refs[sum(groups) : sum(groups) + 4]
    (
        joint_ref,
        out_ref,
        up_block_ref,
        down_block_ref,
        head_block_ref,
        loss_out_ref,
        *vector_refs,
    ) = refs[sum(groups) + 4 :]

    def total(terms):
        return sum(ref[...].astype(F32) for ref in terms)

    up_sum = total(up)
    for h in range(2):
        lanes = slice(h * up_sum.shape[2], (h + 1) * up_sum.shape[2])
        up_block_ref[:, lanes] = up_sum[h]
    one, two_ = total(first), total(second)
    some = one.shape[1]
    rest = joint_ref.shape[1] - some
    joint_ref[:, :some] = one
    joint_ref[:, some:] = two_[:, :rest]
    out_ref[...] = two_[:, rest:]
    hidden = down_ref.shape[1]
    down_block_ref[...] = down_ref[...] + other_ref[:, :hidden].astype(F32)
    head_block_ref[...] = (head_ref[...] + other_ref[:, hidden:].astype(F32)).T
    loss_out_ref[...] = loss_ref[...].reshape(1)
    vectors = total(lines)
    starts = (GAIN1, SHIFT1, JOINT, OUT, GAIN2, SHIFT2, WIDE, NARROW)
    for start, ref in zip(starts, vector_refs):
        for i in range(ref.shape[0] // 128):
            line = start // 128 + i
            if start == JOINT and i >= D // 128:
                line += D // 128
            ref[pl.ds(i * 128, 128)] = vectors[line]


def finish(up, first, second, vectors, loss, low, joint):
    rows = up[0].shape[1]
    sizes = (D, D, 2 * D, D, D, D, FF, D)
    return kernel_call(
        "finish",
        functools.partial(finish_kernel, [len(v) for v in (up, first, second, vectors)]),
        [
            shape(rows, joint),
            shape(rows, D - joint),
            shape(rows, D),
            shape(*low[0].shape),
            shape(*low[1].shape[::-1]),
            shape(1),
        ]
        + [shape(n) for n in sizes],
        (),
        (*up, *first, *second, *vectors, loss, *low),
    )


def both_pairs(partner):
    dp, rep = lax.axis_size("dp"), lax.axis_size("rep")
    pairs = []
    for i in range(dp):
        for j in range(rep):
            a, b = partner(i, j)
            pairs.append((i * rep + j, a * rep + b))
    return pairs


def exchange(value, partner):
    return lax.ppermute(value, ("dp", "rep"), both_pairs(partner))


def first_turn(i, j):
    return (i, j ^ 2) if j & 1 == 0 else (i ^ 1, j)


def second_turn(i, j):
    return (i ^ 1, j) if j & 1 == 0 else (i, j ^ 2)


def added(a, b):
    return (a.astype(F32) + b.astype(F32)).astype(BF)


def halved(here, got):
    half = here.shape[0] // 2
    return added(here[:half], got[:half]), added(here[half:], got[half:])


def parted(here, got, count):
    rows = here.shape[-2] // count
    parts = [slice(i * rows, (i + 1) * rows) for i in range(count)]
    return [added(here[..., p, :], got[..., p, :]) for p in parts]


def core_turn(i, j):
    return i, j ^ 1


def across(i, j):
    return i, j ^ 2


def group_round(keep, got, group):
    masks = group_masks(group)
    bits = len(group)
    parts = parted(keep, got, len(masks))
    place = [sum(((c >> n) & 1) << (bits - 1 - n) for n in range(bits)) for c in range(len(masks))]
    return [parts[0]] + [
        exchange(parts[place[c]], lambda i, j: (i ^ masks[c][0], j)) for c in range(1, len(masks))
    ]


def row_rounds(keep, got, groups):
    terms = [keep, got]
    for group in groups:
        if len(terms) > 2:
            terms = [terms[0], sum(v.astype(F32) for v in terms[1:])]
        terms = group_round(*terms, group)
    return terms


order = lax.optimization_barrier


def dp_groups():
    bits = [("dp", b) for b in range(1, lax.axis_size("dp").bit_length() - 1)]
    return [bits[i : i + 2] for i in range(0, len(bits), 2)] + [[("dp", 0)]]


def all_groups():
    bits = [("rep", b) for b in range(1, lax.axis_size("rep").bit_length() - 1)]
    groups = dp_groups()
    return groups[:-1] + [groups[-1] + bits, [("rep", 0)]]


def group_masks(group):
    out = [(0, 0)]
    for axis, bit in group:
        out += [(a | 1 << bit, b) if axis == "dp" else (a, b | 1 << bit) for a, b in out]
    return out


def gather_masks(rounds, blocks):
    bits = [0] + list(range(blocks.bit_length() - 2, 0, -1))
    masks, used = [0], 0
    for count in rounds:
        for bit in bits[used : used + count]:
            masks = masks + [m | 1 << bit for m in masks]
        used += count
    return masks


def split_round(value, wide, group):
    blocks = (value.shape[1] - D) // wide
    turns = group_masks(group)
    text = value[:, blocks * wide :]
    pieces = []
    for c, (a, b) in enumerate(turns):
        chosen = [value[:, i * wide : (i + 1) * wide] for i in range(c, blocks, len(turns))]
        piece = jnp.concatenate(chosen + [text], axis=1)
        pieces.append(piece if c == 0 else exchange(piece, lambda i, j: (i ^ a, j ^ b)))
    return pieces


def round_of(value, group):
    return [value] + [
        exchange(value, lambda i, j: (i ^ a, j ^ b)) for a, b in group_masks(group)[1:]
    ]


def relative_rows(value, blocks):
    rows = value.shape[0] // blocks
    if rows % SLOT == 0:
        return value
    bits = blocks.bit_length() - 1
    place = jnp.arange(blocks, dtype=jnp.int32)
    source = jnp.zeros_like(place)
    for bit in range(bits):
        source = source + ((place >> (bits - 1 - bit)) & 1) * (1 << bit)
    source = source ^ lax.axis_index("dp")
    return value.reshape(blocks, rows, -1)[source].reshape(value.shape)


def local(
    incoming_activations,
    caption_final_place,
    paired_picture,
    caption_weight,
    locked_picture_features,
    softmax_heat,
    premix_scaling_factor,
    premix_shift_term,
    stacked_mixing_matrix,
    asking_reading_offsets,
    mixing_result_matrix,
    mixing_result_offset,
    premlp_scaling_factor,
    premlp_shift_term,
    widening_matrix,
    widening_offset,
    narrowing_matrix,
    narrowing_offset,
    caption_mapping_matrix,
    picture_mapping_matrix,
):
    both = ("dp", "rep")
    devices = lax.axis_size(both)
    blocks = lax.axis_size("dp")
    parts = lax.axis_size("rep")
    captions = caption_final_place.shape[0]
    images = locked_picture_features.shape[0]
    groups = all_groups()
    pieces = round_of(jnp.pad(locked_picture_features, ((0, SLOT - images), (0, 0))), groups[0])
    unit1, inverse1 = norm_tokens(incoming_activations)
    project, normed = project_tokens(
        premix_scaling_factor,
        premix_shift_term,
        asking_reading_offsets,
        unit1,
        stacked_mixing_matrix,
    )
    project, pieces = order((project, pieces))
    for group in groups[1:-1]:
        pieces = round_of(jnp.concatenate(pieces), group)
    att, context, middle = attend_tokens(
        caption_final_place,
        mixing_result_offset,
        incoming_activations,
        project,
        mixing_result_matrix,
    )
    middle, pieces = order((middle, pieces))
    own, far = round_of(jnp.concatenate(pieces), groups[-1])
    second, unit2, inverse2, slope, box, text, factor, embed = widen_tokens(
        blocks,
        caption_final_place,
        premlp_scaling_factor,
        premlp_shift_term,
        widening_offset,
        narrowing_offset,
        middle,
        widening_matrix,
        narrowing_matrix,
        caption_mapping_matrix,
    )
    embed, far = order((embed, far))
    picture, score, row, inverse, stats = contrast(
        images,
        parts,
        sum(groups, []),
        softmax_heat,
        own,
        far,
        picture_mapping_matrix,
        embed,
        paired_picture,
        caption_weight,
    )
    groups = dp_groups()
    high = [[bit] for group in groups[:-1] for bit in group]
    factor_groups = groups[-1:] + high[::-1]
    stats = round_of(stats, [("rep", 0)])
    normed_t, context_t, second_t = (
        relative_rows(v, blocks) for v in turn_tokens(blocks, normed, context, second)
    )
    stats = round_of(merge(stats), [("rep", 1)] + groups[-1])
    for group in groups[:-1]:
        stats = round_of(merge(stats), group)
    back, away, here, pooled_back, loss, down_bias, up_bias, *pieces = head_back(
        images,
        [len(group) for group in factor_groups],
        softmax_heat,
        caption_final_place,
        stats,
        score,
        row,
        inverse,
        caption_weight,
        paired_picture,
        picture,
        text,
        factor,
        caption_mapping_matrix,
        narrowing_matrix,
        slope,
        second_t,
        box,
    )
    loss = loss / (captions * devices)
    got = exchange(away, core_turn)
    pieces = pieces[:1] + [
        exchange(piece, lambda i, j: (i ^ a, j ^ b))
        for piece, (a, b) in zip(pieces[1:], group_masks(factor_groups[0])[1:])
    ]
    total, attended, context_back, gain2, shift2, out_bias = middle_back(
        caption_final_place,
        premlp_scaling_factor,
        pooled_back,
        back,
        widening_matrix,
        unit2,
        inverse2,
        mixing_result_matrix,
    )
    context_back, got, pieces = order((context_back, got, pieces))
    up, send = halved(here, got)
    got_up = exchange(send, first_turn)
    pieces = split_round(jnp.concatenate(pieces), box.shape[2], factor_groups[1])
    project_back, joint_bias = attention_back(project, att, context_back)
    away, here = columns_gradient("left_columns", left_columns_kernel, (project_back, normed_t))
    got = exchange(away, core_turn)
    project_back, away = order((project_back, away))
    away, here2 = columns_gradient(
        "right_columns", right_columns_kernel, (project_back, attended, normed_t, context_t)
    )
    project_back, away, got, got_up = order((project_back, away, got, got_up))
    up, up_send = halved(up, got_up)
    first, send = halved(here, got)
    got = exchange(jnp.concatenate([up_send[0], send]), second_turn)
    got2 = exchange(away, core_turn)
    joint = 3 * D // parts
    token, sums = token_back(
        premix_scaling_factor,
        unit1,
        inverse1,
        total,
        project_back,
        stacked_mixing_matrix,
        (joint_bias, out_bias, gain2, shift2, up_bias, down_bias),
    )
    sums, got2 = order((sums, got2))
    lines = round_of(sums, [("rep", 0)])
    second, send2 = halved(here2, got2)
    got, send2, lines, pieces = order((got, send2, lines, pieces))
    up, got_up = group_round(up[0], got[:2], high[0])
    first, send = halved(first, got[2:])
    got2 = exchange(jnp.concatenate([send2, send]), first_turn)
    lines = round_of(sum(lines), [("rep", 1)])
    for group in factor_groups[2:]:
        pieces = split_round(jnp.concatenate(pieces), box.shape[2], group)
    got_up, got2, lines, pieces = order((got_up, got2, lines, pieces))
    second, send = halved(second, got2[:2])
    second, first, got = second[0], first[0], got2[2]
    got2 = exchange(send[0], second_turn)
    first, got = group_round(first, got, high[0])
    for group in high[1:]:
        up, got_up = group_round(up, got_up, group)
    lines = round_of(sum(lines), groups[-1])
    factors = jnp.concatenate(pieces)
    far = exchange(factors, core_turn)
    got, got2, lines, far = order((got, got2, lines, far))
    *low, other = low_rank(blocks, parts, factors, far, caption_mapping_matrix)
    other = exchange(other, across)
    for i, group in enumerate(high):
        if i:
            got_up, got2 = order((got_up, got2))
        got, got2, lines = order((got, got2, lines))
        second, got2 = group_round(second, got2, group)
        if i + 1 < len(high):
            first, got = group_round(first, got, high[i + 1])
        lines = round_of(sum(lines), group)
    first, second, up, vectors = [first, got], [second, got2], [up, got_up], lines
    joint_block, out_block, up_block, down_block, head_block, loss, *grads = finish(
        up, first, second, vectors, loss, (*low, other), joint
    )
    return (
        loss,
        token,
        grads[0],
        grads[1],
        joint_block,
        grads[2],
        out_block,
        grads[3],
        grads[4],
        grads[5],
        up_block,
        grads[6],
        down_block.T,
        grads[7],
        head_block,
    )


def solution(mesh):
    spread = P(("dp", "rep"), None)
    line = P(("dp", "rep"))
    block = P("dp", "rep")
    in_specs = (spread, line, line, line, spread) + (P(),) * 15
    out_specs = (
        P(),
        spread,
        P(),
        P(),
        block,
        P(),
        block,
        P(),
        P(),
        P(),
        block,
        P(),
        block,
        P(),
        block,
    )
    return jax.shard_map(local, mesh=mesh, in_specs=in_specs, out_specs=out_specs, check_vma=False)
```

```python
import functools

import jax
import jax.numpy as jnp
from jax import lax
from jax.experimental import pallas as pl
from jax.experimental.pallas import tpu as pltpu
from jax.sharding import PartitionSpec as P

D = 768
HEADS = 12
HEAD = 64
SEQ = 16
FF = 3072
GROUP = 128
PAIRS = HEADS // 2
SLOT = 16
BF = jnp.bfloat16
F32 = jnp.float32

epsilon = 1e-06
BEND = 0.7978845608028654
CUBE = BEND * 0.044715
negative = -1e30
scale = HEAD ** (-0.5)
LIMIT = 16 * 1024 * 1024

GAIN1, SHIFT1, JOINT, OUT, GAIN2, SHIFT2, WIDE, NARROW = 0, 768, 1536, 3840, 4608, 5376, 6144, 9216
VECTORS = 9984
LINES = VECTORS // 128
ALL_LINES = LINES + -LINES % 8

vmem = pl.BlockSpec(memory_space=pltpu.VMEM)
hbm = pl.BlockSpec(memory_space=pltpu.HBM)
smem = pl.BlockSpec(memory_space=pltpu.SMEM)


def dot(a, b, dims):
    return lax.dot_general(a, b, (dims, ((), ())), preferred_element_type=F32)


def nn(a, b):
    return dot(a, b, ((1,), (0,)))


def nt(a, b):
    return dot(a, b, ((1,), (1,)))


def tn(a, b):
    return dot(a, b, ((0,), (0,)))


def cost(flops):
    return pl.CostEstimate(flops=flops, transcendentals=0, bytes_accessed=0)


def shape(*dims, dtype=F32):
    return jax.ShapeDtypeStruct(dims, dtype)


def kept(*dims, dtype=BF):
    return pltpu.VMEM(dims, dtype)


def near(*values):
    return [pltpu.with_memory_space_constraint(v, pltpu.VMEM) for v in values]


def kernel_call(
    name, body, results, small, operands, scratch=(), estimate=None, limit=LIMIT, far=(), copies=0
):
    semaphores = [pltpu.SemaphoreType.DMA((copies,))] if copies else []
    return pl.pallas_call(
        body,
        out_shape=results,
        in_specs=[smem] * len(small) + [hbm] * len(far) + [vmem] * len(operands),
        out_specs=[vmem] * len(results),
        scratch_shapes=[pltpu.VMEM(s, t) for s, t in scratch] + semaphores,
        compiler_params=pltpu.CompilerParams(vmem_limit_bytes=limit),
        cost_estimate=estimate,
        name=name,
    )(*small, *[pltpu.with_memory_space_constraint(v, pltpu.HBM) for v in far], *operands)


def fetched(values):
    return [kept(*v.shape, dtype=v.dtype) for v in values]


def fetch(sources, targets, semaphores):
    copies = [
        pltpu.make_async_copy(source, target, semaphores.at[i])
        for i, (source, target) in enumerate(zip(sources, targets))
    ]
    for copy in copies:
        copy.start()
    return copies


def iota(dims, axis):
    return lax.broadcasted_iota(jnp.int32, dims, axis)


def norm_parts(values):
    average = jnp.mean(values, axis=-1, keepdims=True)
    centred = values - average
    inverse = lax.rsqrt(jnp.mean(centred * centred, axis=-1, keepdims=True) + epsilon)
    return centred * inverse, inverse


def norm_back(unit, inverse, gain, back):
    inner = back * gain
    part = inverse * (
        inner
        - jnp.mean(inner, axis=-1, keepdims=True)
        - unit * jnp.mean(inner * unit, axis=-1, keepdims=True)
    )
    return part, jnp.sum(back * unit, axis=0, keepdims=True), jnp.sum(back, axis=0, keepdims=True)


def split(value):
    high = value.astype(BF)
    return high, (value - high.astype(F32)).astype(BF)


def two(value):
    return jnp.concatenate(split(value), axis=0)


def as_row(ref):
    return ref[...].reshape(1, ref.shape[0])


def as_column(ref):
    size = ref.shape[0]
    same = iota((size, size), 0) == iota((size, size), 1)
    row = as_row(ref)
    return jnp.sum(jnp.where(same, row, jnp.zeros_like(row)), axis=1, keepdims=True)


def token_limits(ref):
    place = as_row(ref).astype(F32)
    captions = place.shape[1]
    tokens = captions * SEQ
    owner = (iota((tokens, captions), 0) // SEQ == iota((tokens, captions), 1)).astype(F32)
    column = jnp.sum(owner * place, axis=1, keepdims=True)
    line = nt(place.astype(BF), owner.astype(BF))
    return line, column


def pool_mask(line, captions):
    dims = (captions, captions * SEQ)
    token = iota(dims, 1)
    inside = (token % SEQ).astype(F32) <= line
    return jnp.where((token // SEQ == iota(dims, 0)) & inside, 1.0, 0.0)


def spread_mask(column, captions):
    dims = (captions * SEQ, captions)
    token = iota(dims, 0)
    inside = (token % SEQ).astype(F32) <= column
    return jnp.where((token // SEQ == iota(dims, 1)) & inside, 1.0, 0.0)


def head_masks():
    lane = iota((1, 2 * HEAD), 1)
    even = (lane < HEAD).astype(F32)
    return even.astype(BF), (1.0 - even).astype(BF)


def caption_masks():
    lane = iota((SEQ, GROUP), 1) // SEQ
    return [lane == c for c in range(GROUP // SEQ)]


def compact(full, picks):
    out = full[:SEQ]
    for c in range(1, len(picks)):
        out = jnp.where(picks[c], full[c * SEQ : (c + 1) * SEQ], out)
    return out


def expand(low, lows):
    return jnp.concatenate([low * mask for mask in lows], axis=0)


def both_heads(value, masks):
    return jnp.concatenate([value * masks[0], value * masks[1]], axis=0)


def store_permuted(ref, value, dp, blocks):
    rows = value.shape[0] // blocks
    bits = blocks.bit_length() - 1
    if rows % SLOT:
        ref[...] = value
        return
    for b in range(blocks):
        k = jnp.bitwise_xor(dp, b)
        place = 0
        for bit in range(bits):
            place = place + ((k >> bit) & 1) * (1 << (bits - 1 - bit))
        ref[pl.ds(pl.multiple_of(place * rows, SLOT), rows), :] = value[b * rows : (b + 1) * rows]


def box_width(blocks):
    used = (FF + D) // blocks
    return used + -used % 128


def project_kernel(*refs):
    more = (len(refs) - 5 - 4 - 5 - 1) // 2
    mine, other, refs = refs[:5], refs[5 : 5 + more], refs[5 + more :]
    project_ref, normed_ref, unit_ref, inverse_ref = refs[:4]
    targets, (x, gain, shift, joint, wj, semaphores) = refs[4 : 4 + more], refs[4 + more :]
    copies = fetch(mine + other, (x, gain, shift, joint, wj) + targets, semaphores)
    copies[0].wait()
    unit_ref[...], inverse_ref[...] = norm_parts(x[...].astype(F32))
    for copy in copies[1:5]:
        copy.wait()
    normed_ref[...] = (unit_ref[...] * as_row(gain) + as_row(shift)).astype(BF)
    bias = as_row(joint)
    for i, part in enumerate((bias[:, :D], 0.0, bias[:, D:])):
        lanes = slice(i * D, (i + 1) * D)
        project_ref[:, lanes] = (nn(normed_ref[...], wj[:, lanes]) + part).astype(BF)
    for copy in copies[5:]:
        copy.wait()


def project_tokens(x, gain, shift, joint, wj, following):
    tokens = x.shape[0]
    mine = (x, gain, shift, joint, wj)
    return kernel_call(
        "project_tokens",
        project_kernel,
        [
            kept(tokens, 3 * D),
            kept(tokens, D),
            kept(tokens, D, dtype=F32),
            kept(tokens, 1, dtype=F32),
        ]
        + fetched(following),
        (),
        (),
        [(v.shape, v.dtype) for v in mine],
        cost(6 * tokens * D * D),
        far=mine + following,
        copies=5 + len(following),
    )


def turn_kernel(blocks, *refs):
    dp = lax.axis_index("dp")
    count = len(refs) // 2
    for source, target in zip(refs[:count], refs[count:]):
        store_permuted(target, source[...].T, dp, blocks)


def turn_tokens(blocks, *values):
    return kernel_call(
        "turn_tokens",
        functools.partial(turn_kernel, blocks),
        [kept(*v.shape[::-1]) for v in values],
        (),
        near(*values),
        (),
        cost(32 * values[0].shape[0] * D),
    )


def attend_kernel(*refs):
    more = (len(refs) - 5 - 3 - 1) // 2
    far, (place_ref, out_ref, x_ref, project_ref, wo_ref) = refs[:more], refs[more : more + 5]
    att_ref, context_ref, middle_ref = refs[more + 5 : more + 8]
    copies = fetch(far, refs[more + 8 : -1], refs[-1])
    line, _ = token_limits(place_ref)
    masks = head_masks()
    picks = caption_masks()
    lows = [pick.astype(F32).astype(BF) for pick in picks]
    key_place = iota((SEQ, GROUP), 0).astype(F32)

    def attend(h, carry):
        at = pl.multiple_of(h * 2 * HEAD, 128)
        for g in range(x_ref.shape[0] // GROUP):
            here = slice(g * GROUP, (g + 1) * GROUP)
            query = project_ref[here, pl.ds(at, 128)]
            keys = both_heads(project_ref[here, pl.ds(pl.multiple_of(D + at, 128), 128)], masks)
            values = both_heads(
                project_ref[here, pl.ds(pl.multiple_of(2 * D + at, 128), 128)], masks
            )
            scores = nt(keys, query)
            allowed = key_place <= line[:, here]
            parts = []
            for e in range(2):
                score = compact(scores[e * GROUP : (e + 1) * GROUP], picks) * scale
                score = jnp.where(allowed, score, negative)
                score = jnp.exp(score - jnp.max(score, axis=0, keepdims=True))
                weight = score / jnp.sum(score, axis=0, keepdims=True)
                att_ref[2 * h + e, :, here] = weight
                parts.append(expand(weight.astype(BF), lows))
            context_ref[here, pl.ds(at, 128)] = tn(jnp.concatenate(parts, axis=0), values).astype(BF)
        return carry

    lax.fori_loop(0, PAIRS, attend, 0, unroll=2)
    middle_ref[...] = x_ref[...].astype(F32) + (nn(context_ref[...], wo_ref[...]) + as_row(out_ref))
    for copy in copies:
        copy.wait()


def attend_tokens(place, out, x, project, wo, following):
    tokens = x.shape[0]
    return kernel_call(
        "attend_tokens",
        attend_kernel,
        [kept(HEADS, SEQ, tokens, dtype=F32), kept(tokens, D), kept(tokens, D, dtype=F32)]
        + fetched(following),
        (),
        near(place, out, x, project, wo),
        (),
        cost(4 * tokens * D * D),
        far=following,
        copies=len(following),
    )


def widen_kernel(blocks, *refs):
    more = (len(refs) - 9 - 8 - 3 - 1) // 2
    far = refs[:more]
    place_ref, gain_ref, shift_ref, wide_ref, narrow_ref, middle_ref, wu_ref, wn_ref, wm_ref = refs[
        more : more + 9
    ]
    second_ref, unit_ref, inverse_ref, upper_ref, box_ref, text_ref, scale_ref, embed_ref = refs[
        more + 9 : more + 17
    ]
    branch, wide, mean, semaphores = refs[-4:]
    copies = fetch(far, refs[more + 17 : -4], semaphores)
    captions = place_ref.shape[0]
    line, column = token_limits(place_ref)
    pool = pool_mask(line, captions)
    share = 1.0 / jnp.sum(pool, axis=1, keepdims=True)
    unit, inverse_ref[...] = norm_parts(middle_ref[...])
    unit_ref[...] = unit
    second_ref[...] = (unit * as_row(gain_ref) + as_row(shift_ref)).astype(BF)
    branch[...] = jnp.zeros_like(branch)
    wide[...] = as_row(wide_ref)
    pool_low = pool.astype(BF)
    step = 512

    def widen(i, carry):
        at = pl.multiple_of(i * step, 128)
        upper = nn(second_ref[...], wu_ref[:, pl.ds(at, step)]) + wide[:, pl.ds(at, step)]
        active = upper * (0.5 + 0.5 * jnp.tanh(upper * (BEND + CUBE * (upper * upper))))
        upper_ref[:, pl.ds(at, step)] = upper
        parts = two(nn(pool_low, active.astype(BF)) * share)
        mean[:, pl.ds(at, step)] = parts[:captions]
        branch[...] += nn(parts, wn_ref[pl.ds(at, step), :])
        return carry

    lax.fori_loop(0, FF // step, widen, 0, unroll=2)
    inside = jnp.where((iota((captions * SEQ, 1), 0) % SEQ).astype(F32) <= column, 1.0, 0.0)
    weight = inside / (column + 1.0)
    pooled = jnp.sum((middle_ref[...] * weight).reshape(captions, SEQ, D), axis=1)
    pooled = (pooled + (branch[:captions] + branch[captions:] + as_row(narrow_ref))).astype(BF)
    hidden, part = FF // blocks, D // blocks
    for b in range(blocks):
        box_ref[b, :, :hidden] = mean[:, b * hidden : (b + 1) * hidden]
        box_ref[b, :, hidden : hidden + part] = pooled[:, b * part : (b + 1) * part]
    text = nn(pooled, wm_ref[...])
    factor = lax.rsqrt(jnp.sum(text * text, axis=1, keepdims=True) + epsilon)
    text_ref[...] = text
    scale_ref[...] = factor
    embed_ref[...] = (text * factor).astype(BF)
    for copy in copies:
        copy.wait()


def slope_kernel(upper_ref, slope_ref):
    step = 512

    def part(i, carry):
        at = pl.multiple_of(i * step, 128)
        upper = upper_ref[:, pl.ds(at, step)]
        square = upper * upper
        half = 0.5 + 0.5 * jnp.tanh(upper * (BEND + CUBE * square))
        slope_ref[:, pl.ds(at, step)] = (
            half * (1.0 + (upper - upper * half) * (2.0 * BEND + 6.0 * CUBE * square))
        ).astype(BF)
        return carry

    lax.fori_loop(0, FF // step, part, 0)


def slope_tokens(upper):
    return kernel_call(
        "slope_tokens", slope_kernel, [kept(*upper.shape)], (), near(upper), (), cost(upper.size)
    )[0]


def widen_tokens(blocks, place, gain, shift, wide, narrow, middle, wu, wn, wm, following):
    tokens = middle.shape[0]
    captions = place.shape[0]
    return kernel_call(
        "widen_tokens",
        functools.partial(widen_kernel, blocks),
        [
            kept(tokens, D),
            kept(tokens, D, dtype=F32),
            kept(tokens, 1, dtype=F32),
            kept(tokens, FF, dtype=F32),
            kept(blocks, captions, box_width(blocks)),
            kept(captions, D, dtype=F32),
            kept(captions, 1, dtype=F32),
            kept(captions, D),
        ]
        + fetched(following),
        (),
        near(place, gain, shift, wide, narrow, middle, wu, wn, wm),
        [
            ((2 * captions, D), F32),
            ((1, FF), F32),
            ((captions, FF), BF),
        ],
        cost(2 * tokens * D * FF),
        far=following,
        copies=len(following),
    )


def match_of(paired, columns, images):
    column = iota((1, columns), 1)
    valid = column % SLOT < images
    name = jnp.where(valid, (column // SLOT) * images + column % SLOT, -1)
    return paired == name, valid


def contrast_kernel(
    images,
    parts,
    bits,
    heat_ref,
    own_ref,
    near_ref,
    wp_ref,
    embed_ref,
    paired_ref,
    weight_ref,
    picture_ref,
    score_ref,
    row_ref,
    inverse_ref,
    stats_ref,
    features,
):
    half = own_ref.shape[0] // SLOT
    for far, ref in enumerate((own_ref, near_ref)):

        def place(i, carry, far=far, ref=ref):
            p = i + far * half
            index = {axis: lax.axis_index(axis) for axis in ("dp", "rep")}
            for n, (axis, bit) in enumerate(bits):
                index[axis] = jnp.bitwise_xor(index[axis], ((p >> n) & 1) << bit)
            to = pl.ds(pl.multiple_of((index["dp"] * parts + index["rep"]) * SLOT, SLOT), SLOT)
            features[to, :] = ref[pl.ds(pl.multiple_of(i * SLOT, SLOT), SLOT), :]
            return carry

        lax.fori_loop(0, half, place, 0, unroll=4)
    picture = nn(features[...], wp_ref[...])
    picture = (
        picture * lax.rsqrt(jnp.sum(picture * picture, axis=1, keepdims=True) + epsilon)
    ).astype(BF)
    picture_ref[...] = picture
    score = nt(embed_ref[...], picture) / heat_ref[0]
    match, valid = match_of(as_column(paired_ref), score.shape[1], images)
    score = jnp.where(valid, score, negative)
    score_ref[...] = score
    top = jnp.max(score, axis=1, keepdims=True)
    row = jnp.log(jnp.sum(jnp.exp(score - top), axis=1, keepdims=True)) + top
    row_ref[...] = row
    positive = jnp.sum(jnp.where(match, score, 0.0), axis=1, keepdims=True)
    hits = jnp.where(match, 1.0, 0.0)
    counts = jnp.sum(hits, axis=0, keepdims=True)
    inverse = 1.0 / jnp.sum(hits * counts, axis=1, keepdims=True)
    inverse_ref[...] = inverse
    total = jnp.sum(as_column(weight_ref) * (row - positive - positive * inverse))
    best = jnp.max(score, axis=0, keepdims=True)
    mass = jnp.sum(jnp.exp(score - best), axis=0, keepdims=True)
    mass = jnp.where(iota(mass.shape, 1) == images, total, mass)
    wide = best.shape[1] // 4
    rows = [v[:, i * wide : (i + 1) * wide] for v in (best, mass) for i in range(4)]
    stats_ref[...] = jnp.concatenate(rows, axis=0)


def contrast(images, parts, bits, heat, own, far, wp, embed, paired, weight):
    captions = embed.shape[0]
    columns = 2 * own.shape[0]
    return kernel_call(
        "contrast",
        functools.partial(contrast_kernel, images, parts, bits),
        [
            kept(columns, D),
            kept(captions, columns, dtype=F32),
            kept(captions, 1, dtype=F32),
            kept(captions, 1, dtype=F32),
            shape(8, columns // 4),
        ],
        (heat,),
        near(own, far, wp, embed, paired, weight),
        [((columns, D), BF)],
        cost(2 * columns * D * D),
        max(LIMIT, columns * 8192),
    )


def merged(refs):
    best = functools.reduce(jnp.maximum, [ref[:4] for ref in refs])
    mass = sum(ref[4:] * jnp.exp(ref[:4] - best) for ref in refs)
    return best, mass


def merge_kernel(*refs):
    *given, out_ref = refs
    best, mass = merged(given)
    out_ref[...] = jnp.concatenate([best, mass], axis=0)


def merge(stats):
    return kernel_call("merge", merge_kernel, [shape(*stats[0].shape)], (), stats)[0]


def quarters(rep, away, flip=0):
    core = rep & 1
    out = []
    for xrel in range(2):
        for yrel in range(2):
            block = jnp.bitwise_xor(rep, 2 * xrel + away)
            x_first = 1 - core if away == flip else core
            out.append((jnp.where(x_first == 1, 2 * xrel + yrel, 2 * yrel + xrel), block, yrel))
    return out


def head_back_kernel(
    images,
    count_stats,
    rounds,
    heat_ref,
    place_ref,
    score_ref,
    row_ref,
    inverse_ref,
    weight_ref,
    paired_ref,
    picture_ref,
    text_ref,
    scale_ref,
    wm_ref,
    wn_ref,
    slope_ref,
    second_t_ref,
    box_ref,
    *refs,
):
    first = 1 << rounds[0]
    pieces = refs[len(refs) - first :]
    stats = refs[:count_stats]
    (
        back_ref,
        away_ref,
        here_ref,
        pooled_ref,
        loss_ref,
        down_bias_ref,
        up_bias_ref,
    ) = refs[count_stats : len(refs) - first]
    rep = lax.axis_index("rep")
    heat = heat_ref[0]
    captions = place_ref.shape[0]
    line, column = token_limits(place_ref)
    count = jnp.sum(pool_mask(line, captions), axis=1, keepdims=True)
    owner = spread_mask(column, captions).astype(BF)
    owner = jnp.concatenate([owner, owner], axis=1)

    score = score_ref[...]
    match, valid = match_of(as_column(paired_ref), score.shape[1], images)
    best, mass = merged(stats)
    column_log = jnp.log(mass) + best
    column_log = jnp.concatenate([column_log[i : i + 1] for i in range(4)], axis=1)
    loss_ref[...] = mass[:1, images : images + 1] + jnp.sum(
        jnp.where(valid, column_log, 0.0), axis=1, keepdims=True
    )
    weight = as_column(weight_ref)
    graded = (
        weight * jnp.exp(score - row_ref[...])
        + jnp.exp(score - column_log)
        - jnp.where(match, weight * (1.0 + inverse_ref[...]), 0.0)
    )
    graded = jnp.where(valid, graded / heat, 0.0).astype(BF)
    embed_back = nn(graded, picture_ref[...])
    text = text_ref[...]
    factor = scale_ref[...]
    text_dot = jnp.sum(text * embed_back, axis=1, keepdims=True)
    text_back = (factor * embed_back - text * (factor * factor * factor) * text_dot).astype(BF)
    blocks, _, wide = box_ref.shape
    masks = gather_masks(rounds, blocks)
    for c, piece_ref in enumerate(pieces):
        for i in range(blocks // first):
            block = jnp.bitwise_xor(lax.axis_index("dp"), masks[i * first + c])
            piece_ref[:, i * wide : (i + 1) * wide] = box_ref[block]
        piece_ref[:, (blocks // first) * wide :] = text_back
    pooled_back = nt(text_back, wm_ref[...])
    pooled_ref[...] = pooled_back
    branch = (pooled_back / count).astype(BF)
    down_bias_ref[...] = jnp.sum(branch.astype(F32) * count, axis=0, keepdims=True)
    ones = jnp.ones((SLOT, back_ref.shape[0]), BF)
    step = 512

    def widen(i, carry):
        at = pl.multiple_of(i * step, 128)
        part = nn(owner, two(nt(branch, wn_ref[pl.ds(at, step), :])))
        part = (part * slope_ref[:, pl.ds(at, step)].astype(F32)).astype(BF)
        back_ref[:, pl.ds(at, step)] = part
        up_bias_ref[:, pl.ds(at, step)] = nn(ones, part)[:1]
        return carry

    lax.fori_loop(0, FF // step, widen, 0, unroll=2)
    half = second_t_ref.shape[0] // 2
    wide = FF // 4
    for turn, target in enumerate((away_ref, here_ref)):
        for place, block, yrel in quarters(rep, 1 - turn):
            part = nn(
                second_t_ref[yrel * half : (yrel + 1) * half],
                back_ref[:, pl.ds(pl.multiple_of(block * wide, 128), wide)],
            )
            for h in range(2):
                target[place, h] = part[:, h * (wide // 2) : (h + 1) * (wide // 2)].astype(BF)


def head_back(images, rounds, heat, place, stats, score, row, inverse, weight, paired, picture, text,
              factor, wm, wn, slope, second_t, box):
    captions = text.shape[0]
    tokens = slope.shape[0]
    piece = (4, 2, D // 2, FF // 8)
    return kernel_call(
        "head_back",
        functools.partial(head_back_kernel, images, len(stats), rounds),
        [
            kept(tokens, FF),
            kept(*piece),
            kept(*piece),
            kept(captions, D, dtype=F32),
            shape(1, 1),
            shape(1, D),
            shape(1, FF),
        ]
        + [shape(captions, (box.shape[0] >> rounds[0]) * box.shape[2] + D, dtype=BF)] * (1 << rounds[0]),
        (heat,),
        (
            *near(place, score, row, inverse, weight, paired),
            *near(picture, text, factor, wm, wn, slope, second_t, box),
            *stats,
        ),
        (),
        cost(2 * tokens * D * FF),
    )


def middle_back_kernel(
    place_ref,
    gain_ref,
    pooled_ref,
    back_ref,
    wu_ref,
    unit_ref,
    inverse_ref,
    wo_ref,
    total_ref,
    attended_ref,
    context_back_ref,
    gain_back_ref,
    shift_back_ref,
    bias_ref,
):
    captions = place_ref.shape[0]
    line, column = token_limits(place_ref)
    count = jnp.sum(pool_mask(line, captions), axis=1, keepdims=True)
    owner = spread_mask(column, captions).astype(BF)
    owner = jnp.concatenate([owner, owner], axis=1)
    second_back = nt(back_ref[...], wu_ref[...])
    part, gain_back_ref[...], shift_back_ref[...] = norm_back(
        unit_ref[...], inverse_ref[...], as_row(gain_ref), second_back
    )
    total = nn(owner, two(pooled_ref[...] / count)) + part
    total_ref[...] = total
    attended = total.astype(BF)
    attended_ref[...] = attended
    bias_ref[...] = nn(jnp.ones((SLOT, attended.shape[0]), BF), attended)[:1]
    context_back_ref[...] = nt(attended, wo_ref[...]).astype(BF)


def middle_back(place, gain, pooled, back, wu, unit, inverse, wo):
    tokens = back.shape[0]
    return kernel_call(
        "middle_back",
        middle_back_kernel,
        [
            kept(tokens, D, dtype=F32),
            kept(tokens, D),
            kept(tokens, D),
            shape(1, D),
            shape(1, D),
            shape(1, D),
        ],
        (),
        near(place, gain, pooled, back, wu, unit, inverse, wo),
        (),
        cost(2 * tokens * D * (FF + D)),
    )


def attention_back_kernel(project_ref, att_ref, context_back_ref, back_ref, bias_ref):
    masks = head_masks()
    picks = caption_masks()
    lows = [pick.astype(F32).astype(BF) for pick in picks]
    low_scale = jnp.asarray(scale, BF)
    first = iota((GROUP, 2 * HEAD), 1) < HEAD
    tokens = project_ref.shape[0]

    def attend(h, carry):
        at = pl.multiple_of(h * 2 * HEAD, 128)
        at_k = pl.multiple_of(D + at, 128)
        at_v = pl.multiple_of(2 * D + at, 128)
        for g in range(tokens // GROUP):
            span = slice(g * GROUP, (g + 1) * GROUP)
            query = project_ref[span, pl.ds(at, 128)]
            keys = both_heads(project_ref[span, pl.ds(at_k, 128)], masks)
            values = both_heads(project_ref[span, pl.ds(at_v, 128)], masks)
            upper = context_back_ref[span, pl.ds(at, 128)]
            full = nt(values, upper)
            weights, grads = [], []
            for e in range(2):
                weight = att_ref[2 * h + e, :, span]
                part = compact(full[e * GROUP : (e + 1) * GROUP], picks)
                grad = weight * (part - jnp.sum(weight * part, axis=0, keepdims=True))
                weights.append(expand(weight.astype(BF), lows))
                grads.append(expand(grad.astype(BF) * low_scale, lows))
            weights = jnp.concatenate(weights, axis=0)
            grads = jnp.concatenate(grads, axis=0)
            back_ref[span, pl.ds(at, 128)] = tn(grads, keys).astype(BF)
            wide = nn(grads, query)
            back_ref[span, pl.ds(at_k, 128)] = jnp.where(first, wide[:GROUP], wide[GROUP:]).astype(
                BF
            )
            wide = nn(weights, upper)
            back_ref[span, pl.ds(at_v, 128)] = jnp.where(first, wide[:GROUP], wide[GROUP:]).astype(
                BF
            )
        return carry

    lax.fori_loop(0, PAIRS, attend, 0, unroll=2)
    ones = jnp.ones((SLOT, tokens), BF)
    for i in range(3):
        lanes = slice(i * D, (i + 1) * D)
        bias_ref[:, lanes] = nn(ones, back_ref[:, lanes])[:1]


def attention_back(project, att, context_back):
    tokens = project.shape[0]
    return kernel_call(
        "attention_back",
        attention_back_kernel,
        [kept(tokens, 3 * D), shape(1, 3 * D)],
        (),
        near(project, att, context_back),
        (),
        cost(3 * tokens * D * D),
    )


def left_columns_kernel(back_ref, normed_t_ref, away_ref, here_ref, chosen):
    rep = lax.axis_index("rep")
    joint = 3 * D // 4
    some = chosen.shape[2]
    for r in range(4):

        @pl.when(rep == r)
        def _():
            for i, k in enumerate((1, 3, 0, 2)):
                b = r ^ k
                chosen[i] = back_ref[:, b * joint : b * joint + some]

    half = D // 2
    for turn, target in enumerate((away_ref, here_ref)):
        for i, (place, _, yrel) in enumerate(quarters(rep, 1 - turn, 1)):
            lines = slice(yrel * half, (yrel + 1) * half)
            target[place] = nn(normed_t_ref[lines], chosen[2 * turn + i // 2]).astype(BF)


def right_columns_kernel(
    back_ref, attended_ref, normed_t_ref, context_t_ref, away_ref, here_ref, chosen
):
    rep = lax.axis_index("rep")
    joint = 3 * D // 4
    out = D // 4
    some = chosen.shape[2] - out
    for r in range(4):

        @pl.when(rep == r)
        def _():
            for i, k in enumerate((1, 3, 0, 2)):
                b = r ^ k
                chosen[i, :, :some] = back_ref[:, (b + 1) * joint - some : (b + 1) * joint]
                chosen[i, :, some:] = attended_ref[:, b * out : (b + 1) * out]

    half = D // 2
    for turn, target in enumerate((away_ref, here_ref)):
        for i, (place, _, yrel) in enumerate(quarters(rep, 1 - turn)):
            block = 2 * turn + i // 2
            lines = slice(yrel * half, (yrel + 1) * half)
            target[place, :, :some] = nn(normed_t_ref[lines], chosen[block, :, :some]).astype(BF)
            target[place, :, some:] = nn(context_t_ref[lines], chosen[block, :, some:]).astype(BF)


def columns_gradient(name, body, operands):
    tokens = operands[0].shape[0]
    piece = (4, D // 2, D // 2)
    return kernel_call(
        name,
        body,
        [kept(*piece), kept(*piece)],
        (),
        near(*operands),
        [((4, tokens, D // 2), BF)],
        cost(tokens * D * FF),
    )


def token_back_kernel(
    gain_ref,
    unit_ref,
    inverse_ref,
    middle_ref,
    back_ref,
    wj_ref,
    joint_ref,
    out_ref,
    gain2_ref,
    shift2_ref,
    wide_ref,
    narrow_ref,
    token_ref,
    sums_ref,
):
    part, gain1, shift1 = norm_back(
        unit_ref[...], inverse_ref[...], as_row(gain_ref), nt(back_ref[...], wj_ref[...])
    )
    token_ref[...] = middle_ref[...] + part
    line = 0
    rest = (joint_ref, out_ref, gain2_ref, shift2_ref, wide_ref, narrow_ref)
    for value in [gain1, shift1] + [ref[...] for ref in rest]:
        for i in range(value.shape[1] // 128):
            sums_ref[line : line + 1] = value[:, i * 128 : (i + 1) * 128]
            line += 1
    sums_ref[line:] = jnp.zeros((sums_ref.shape[0] - line, 128), F32)


def token_back(gain, unit, inverse, middle, back, wj, sums):
    return kernel_call(
        "token_back",
        token_back_kernel,
        [shape(unit.shape[0], D), shape(ALL_LINES, 128)],
        (),
        (gain, *near(unit, inverse, middle, back, wj), *sums),
        (),
        cost(6 * unit.shape[0] * D * D),
    )


def low_rank_kernel(
    hidden, own_ref, near_ref, wm_ref, down_ref, head_ref, other_ref, box, back
):
    rows = own_ref.shape[0]
    box[:rows] = own_ref[...]
    box[rows:] = near_ref[...]
    part = down_ref.shape[0]
    start = box.shape[1] - D
    rep = lax.axis_index("rep")
    for r in range(D // part):

        @pl.when(rep == r)
        def _():
            for i, b in enumerate((r, r ^ 2)):
                back[i] = box[:, start + b * part : start + (b + 1) * part]

    wide = head_ref.shape[1]
    for i in range(2):
        block = jnp.bitwise_xor(rep, 2 * i)
        here = wm_ref[pl.ds(pl.multiple_of(block * part, SLOT), part), :]
        pooled = nt(box[:, start:], here).astype(BF)
        down = tn(pooled, box[:, :hidden])
        head = tn(back[i], box[:, hidden : hidden + wide])
        if i == 0:
            down_ref[...] = down
            head_ref[...] = head
        else:
            other_ref[:, :hidden] = down.astype(BF)
            other_ref[:, hidden:] = head.astype(BF)


def low_rank(blocks, parts, own, far, wm):
    rows = 2 * own.shape[0]
    hidden, wide, part = FF // blocks, D // blocks, D // parts
    return kernel_call(
        "low_rank",
        functools.partial(low_rank_kernel, hidden),
        [shape(part, hidden), shape(part, wide), shape(part, hidden + wide, dtype=BF)],
        (),
        near(own, far, wm),
        [((rows, own.shape[1]), BF), ((2, rows, part), BF)],
        cost(2 * rows * D * D),
    )


def finish_kernel(groups, *refs):
    up, first, second, lines = (
        [refs[sum(groups[:i]) + n] for n in range(groups[i])] for i in range(4)
    )
    loss_ref, down_ref, head_ref, other_ref = refs[sum(groups) : sum(groups) + 4]
    (
        joint_ref,
        out_ref,
        up_block_ref,
        down_block_ref,
        head_block_ref,
        loss_out_ref,
        *vector_refs,
    ) = refs[sum(groups) + 4 :]

    def total(terms):
        return sum(ref[...].astype(F32) for ref in terms)

    up_sum = total(up)
    for h in range(2):
        lanes = slice(h * up_sum.shape[2], (h + 1) * up_sum.shape[2])
        up_block_ref[:, lanes] = up_sum[h]
    one, two_ = total(first), total(second)
    some = one.shape[1]
    rest = joint_ref.shape[1] - some
    joint_ref[:, :some] = one
    joint_ref[:, some:] = two_[:, :rest]
    out_ref[...] = two_[:, rest:]
    hidden = down_ref.shape[1]
    down_block_ref[...] = down_ref[...] + other_ref[:, :hidden].astype(F32)
    head_block_ref[...] = (head_ref[...] + other_ref[:, hidden:].astype(F32)).T
    loss_out_ref[...] = loss_ref[...].reshape(1)
    vectors = total(lines)
    starts = (GAIN1, SHIFT1, JOINT, OUT, GAIN2, SHIFT2, WIDE, NARROW)
    for start, ref in zip(starts, vector_refs):
        for i in range(ref.shape[0] // 128):
            line = start // 128 + i
            if start == JOINT and i >= D // 128:
                line += D // 128
            ref[pl.ds(i * 128, 128)] = vectors[line]


def finish(up, first, second, vectors, loss, low, joint):
    rows = up[0].shape[1]
    sizes = (D, D, 2 * D, D, D, D, FF, D)
    return kernel_call(
        "finish",
        functools.partial(finish_kernel, [len(v) for v in (up, first, second, vectors)]),
        [
            shape(rows, joint),
            shape(rows, D - joint),
            shape(rows, D),
            shape(*low[0].shape),
            shape(*low[1].shape[::-1]),
            shape(1),
        ]
        + [shape(n) for n in sizes],
        (),
        (*up, *first, *second, *vectors, loss, *low),
    )


def both_pairs(partner):
    dp, rep = lax.axis_size("dp"), lax.axis_size("rep")
    pairs = []
    for i in range(dp):
        for j in range(rep):
            a, b = partner(i, j)
            pairs.append((i * rep + j, a * rep + b))
    return pairs


def exchange(value, partner):
    return lax.ppermute(value, ("dp", "rep"), both_pairs(partner))


def first_turn(i, j):
    return (i, j ^ 2) if j & 1 == 0 else (i ^ 1, j)


def second_turn(i, j):
    return (i ^ 1, j) if j & 1 == 0 else (i, j ^ 2)


def added(a, b):
    return (a.astype(F32) + b.astype(F32)).astype(BF)


def halved(here, got):
    half = here.shape[0] // 2
    return added(here[:half], got[:half]), added(here[half:], got[half:])


def parted(here, got, count):
    rows = here.shape[-2] // count
    parts = [slice(i * rows, (i + 1) * rows) for i in range(count)]
    return [added(here[..., p, :], got[..., p, :]) for p in parts]


def core_turn(i, j):
    return i, j ^ 1


def across(i, j):
    return i, j ^ 2


def group_round(keep, got, group):
    masks = group_masks(group)
    bits = len(group)
    parts = parted(keep, got, len(masks))
    place = [sum(((c >> n) & 1) << (bits - 1 - n) for n in range(bits)) for c in range(len(masks))]
    return [parts[0]] + [
        exchange(parts[place[c]], lambda i, j: (i ^ masks[c][0], j)) for c in range(1, len(masks))
    ]


def row_rounds(keep, got, groups):
    terms = [keep, got]
    for group in groups:
        if len(terms) > 2:
            terms = [terms[0], sum(v.astype(F32) for v in terms[1:])]
        terms = group_round(*terms, group)
    return terms


order = lax.optimization_barrier


def dp_groups():
    bits = [("dp", b) for b in range(1, lax.axis_size("dp").bit_length() - 1)]
    return [bits[i : i + 2] for i in range(0, len(bits), 2)] + [[("dp", 0)]]


def all_groups():
    bits = [("rep", b) for b in range(1, lax.axis_size("rep").bit_length() - 1)]
    groups = dp_groups()
    return groups[:-1] + [groups[-1] + bits, [("rep", 0)]]


def group_masks(group):
    out = [(0, 0)]
    for axis, bit in group:
        out += [(a | 1 << bit, b) if axis == "dp" else (a, b | 1 << bit) for a, b in out]
    return out


def gather_masks(rounds, blocks):
    bits = [0] + list(range(blocks.bit_length() - 2, 0, -1))
    masks, used = [0], 0
    for count in rounds:
        for bit in bits[used : used + count]:
            masks = masks + [m | 1 << bit for m in masks]
        used += count
    return masks


def split_round(value, wide, group):
    blocks = (value.shape[1] - D) // wide
    turns = group_masks(group)
    text = value[:, blocks * wide :]
    pieces = []
    for c, (a, b) in enumerate(turns):
        chosen = [value[:, i * wide : (i + 1) * wide] for i in range(c, blocks, len(turns))]
        piece = jnp.concatenate(chosen + [text], axis=1)
        pieces.append(piece if c == 0 else exchange(piece, lambda i, j: (i ^ a, j ^ b)))
    return pieces


def round_of(value, group):
    return [value] + [
        exchange(value, lambda i, j: (i ^ a, j ^ b)) for a, b in group_masks(group)[1:]
    ]


def relative_rows(value, blocks):
    rows = value.shape[0] // blocks
    if rows % SLOT == 0:
        return value
    bits = blocks.bit_length() - 1
    place = jnp.arange(blocks, dtype=jnp.int32)
    source = jnp.zeros_like(place)
    for bit in range(bits):
        source = source + ((place >> (bits - 1 - bit)) & 1) * (1 << bit)
    source = source ^ lax.axis_index("dp")
    return value.reshape(blocks, rows, -1)[source].reshape(value.shape)


def local(
    incoming_activations,
    caption_final_place,
    paired_picture,
    caption_weight,
    locked_picture_features,
    softmax_heat,
    premix_scaling_factor,
    premix_shift_term,
    stacked_mixing_matrix,
    asking_reading_offsets,
    mixing_result_matrix,
    mixing_result_offset,
    premlp_scaling_factor,
    premlp_shift_term,
    widening_matrix,
    widening_offset,
    narrowing_matrix,
    narrowing_offset,
    caption_mapping_matrix,
    picture_mapping_matrix,
):
    both = ("dp", "rep")
    devices = lax.axis_size(both)
    blocks = lax.axis_size("dp")
    parts = lax.axis_size("rep")
    captions = caption_final_place.shape[0]
    images = locked_picture_features.shape[0]
    groups = all_groups()
    pieces = round_of(jnp.pad(locked_picture_features, ((0, SLOT - images), (0, 0))), groups[0])
    project, normed, unit1, inverse1, place, out, x, wo = project_tokens(
        incoming_activations,
        premix_scaling_factor,
        premix_shift_term,
        asking_reading_offsets,
        stacked_mixing_matrix,
        (
            caption_final_place,
            mixing_result_offset,
            incoming_activations,
            mixing_result_matrix,
        ),
    )
    project, pieces = order((project, pieces))
    for group in groups[1:-1]:
        pieces = round_of(jnp.concatenate(pieces), group)
    att, context, middle, gain2, shift2, wide, narrow, wu, wn, wm = attend_tokens(
        place,
        out,
        x,
        project,
        wo,
        (
            premlp_scaling_factor,
            premlp_shift_term,
            widening_offset,
            narrowing_offset,
            widening_matrix,
            narrowing_matrix,
            caption_mapping_matrix,
        ),
    )
    middle, pieces = order((middle, pieces))
    own, far = round_of(jnp.concatenate(pieces), groups[-1])
    second, unit2, inverse2, upper, box, text, factor, embed, wp, paired, weight = widen_tokens(
        blocks,
        place,
        gain2,
        shift2,
        wide,
        narrow,
        middle,
        wu,
        wn,
        wm,
        (picture_mapping_matrix, paired_picture, caption_weight),
    )
    embed, far = order((embed, far))
    picture, score, row, inverse, stats = contrast(
        images,
        parts,
        sum(groups, []),
        softmax_heat,
        own,
        far,
        wp,
        embed,
        paired,
        weight,
    )
    groups = dp_groups()
    high = [[bit] for group in groups[:-1] for bit in group]
    factor_groups = groups[-1:] + high[::-1]
    stats = round_of(stats, [("rep", 0)])
    normed_t, context_t, second_t = (
        relative_rows(v, blocks) for v in turn_tokens(blocks, normed, context, second)
    )
    stats = round_of(merge(stats), [("rep", 1)] + groups[-1])
    slope = slope_tokens(upper)
    stats, slope = order((stats, slope))
    for group in groups[:-1]:
        stats = round_of(merge(stats), group)
    back, away, here, pooled_back, loss, down_bias, up_bias, *pieces = head_back(
        images,
        [len(group) for group in factor_groups],
        softmax_heat,
        place,
        stats,
        score,
        row,
        inverse,
        weight,
        paired,
        picture,
        text,
        factor,
        wm,
        wn,
        slope,
        second_t,
        box,
    )
    loss = loss / (captions * devices)
    got = exchange(away, core_turn)
    pieces = pieces[:1] + [
        exchange(piece, lambda i, j: (i ^ a, j ^ b))
        for piece, (a, b) in zip(pieces[1:], group_masks(factor_groups[0])[1:])
    ]
    total, attended, context_back, gain2, shift2, out_bias = middle_back(
        place,
        gain2,
        pooled_back,
        back,
        wu,
        unit2,
        inverse2,
        wo,
    )
    context_back, got, pieces = order((context_back, got, pieces))
    up, send = halved(here, got)
    got_up = exchange(send, first_turn)
    pieces = split_round(jnp.concatenate(pieces), box.shape[2], factor_groups[1])
    project_back, joint_bias = attention_back(project, att, context_back)
    away, here = columns_gradient("left_columns", left_columns_kernel, (project_back, normed_t))
    got = exchange(away, core_turn)
    project_back, away = order((project_back, away))
    away, here2 = columns_gradient(
        "right_columns", right_columns_kernel, (project_back, attended, normed_t, context_t)
    )
    project_back, away, got, got_up = order((project_back, away, got, got_up))
    up, up_send = halved(up, got_up)
    first, send = halved(here, got)
    got = exchange(jnp.concatenate([up_send[0], send]), second_turn)
    got2 = exchange(away, core_turn)
    joint = 3 * D // parts
    token, sums = token_back(
        premix_scaling_factor,
        unit1,
        inverse1,
        total,
        project_back,
        stacked_mixing_matrix,
        (joint_bias, out_bias, gain2, shift2, up_bias, down_bias),
    )
    sums, got2 = order((sums, got2))
    lines = round_of(sums, [("rep", 0)])
    second, send2 = halved(here2, got2)
    got, send2, lines, pieces = order((got, send2, lines, pieces))
    up, got_up = group_round(up[0], got[:2], high[0])
    first, send = halved(first, got[2:])
    got2 = exchange(jnp.concatenate([send2, send]), first_turn)
    lines = round_of(sum(lines), [("rep", 1)])
    for group in factor_groups[2:]:
        pieces = split_round(jnp.concatenate(pieces), box.shape[2], group)
    got_up, got2, lines, pieces = order((got_up, got2, lines, pieces))
    second, send = halved(second, got2[:2])
    second, first, got = second[0], first[0], got2[2]
    got2 = exchange(send[0], second_turn)
    first, got = group_round(first, got, high[0])
    for group in high[1:]:
        up, got_up = group_round(up, got_up, group)
    lines = round_of(sum(lines), groups[-1])
    factors = jnp.concatenate(pieces)
    far = exchange(factors, core_turn)
    got, got2, lines, far = order((got, got2, lines, far))
    *low, other = low_rank(blocks, parts, factors, far, wm)
    other = exchange(other, across)
    for i, group in enumerate(high):
        if i:
            got_up, got2 = order((got_up, got2))
        got, got2, lines = order((got, got2, lines))
        second, got2 = group_round(second, got2, group)
        if i + 1 < len(high):
            first, got = group_round(first, got, high[i + 1])
        lines = round_of(sum(lines), group)
    first, second, up, vectors = [first, got], [second, got2], [up, got_up], lines
    joint_block, out_block, up_block, down_block, head_block, loss, *grads = finish(
        up, first, second, vectors, loss, (*low, other), joint
    )
    return (
        loss,
        token,
        grads[0],
        grads[1],
        joint_block,
        grads[2],
        out_block,
        grads[3],
        grads[4],
        grads[5],
        up_block,
        grads[6],
        down_block.T,
        grads[7],
        head_block,
    )


def solution(mesh):
    spread = P(("dp", "rep"), None)
    line = P(("dp", "rep"))
    block = P("dp", "rep")
    in_specs = (spread, line, line, line, spread) + (P(),) * 15
    out_specs = (
        P(),
        spread,
        P(),
        P(),
        block,
        P(),
        block,
        P(),
        P(),
        P(),
        block,
        P(),
        block,
        P(),
        block,
    )
    return jax.shard_map(local, mesh=mesh, in_specs=in_specs, out_specs=out_specs, check_vma=False)
```

```python
import functools

import jax
import jax.numpy as jnp
from jax import lax
from jax.experimental import pallas as pl
from jax.experimental.pallas import tpu as pltpu
from jax.sharding import PartitionSpec as P

D = 768
HEADS = 12
HEAD = 64
SEQ = 16
FF = 3072
GROUP = 128
PAIRS = HEADS // 2
SLOT = 16
BF = jnp.bfloat16
F32 = jnp.float32

epsilon = 1e-06
BEND = 0.7978845608028654
CUBE = BEND * 0.044715
negative = -1e30
scale = HEAD ** (-0.5)
LIMIT = 20 * 1024 * 1024

GAIN1, SHIFT1, JOINT, OUT, GAIN2, SHIFT2, WIDE, NARROW = 0, 768, 1536, 3840, 4608, 5376, 6144, 9216
VECTORS = 9984
LINES = VECTORS // 128
ALL_LINES = LINES + -LINES % 8

vmem = pl.BlockSpec(memory_space=pltpu.VMEM)
hbm = pl.BlockSpec(memory_space=pltpu.HBM)
smem = pl.BlockSpec(memory_space=pltpu.SMEM)


def dot(a, b, dims):
    return lax.dot_general(a, b, (dims, ((), ())), preferred_element_type=F32)


def nn(a, b):
    return dot(a, b, ((1,), (0,)))


def nt(a, b):
    return dot(a, b, ((1,), (1,)))


def tn(a, b):
    return dot(a, b, ((0,), (0,)))


def cost(flops):
    return pl.CostEstimate(flops=flops, transcendentals=0, bytes_accessed=0)


def shape(*dims, dtype=F32):
    return jax.ShapeDtypeStruct(dims, dtype)


def kept(*dims, dtype=BF):
    return pltpu.VMEM(dims, dtype)


def near(*values):
    return [pltpu.with_memory_space_constraint(v, pltpu.VMEM) for v in values]


def kernel_call(
    name, body, results, small, operands, scratch=(), estimate=None, limit=LIMIT, far=(), copies=0
):
    semaphores = [pltpu.SemaphoreType.DMA((copies,))] if copies else []
    return pl.pallas_call(
        body,
        out_shape=results,
        in_specs=[smem] * len(small) + [hbm] * len(far) + [vmem] * len(operands),
        out_specs=[vmem] * len(results),
        scratch_shapes=[pltpu.VMEM(s, t) for s, t in scratch] + semaphores,
        compiler_params=pltpu.CompilerParams(vmem_limit_bytes=limit),
        cost_estimate=estimate,
        name=name,
    )(*small, *[pltpu.with_memory_space_constraint(v, pltpu.HBM) for v in far], *operands)


def fetched(values):
    return [kept(*v.shape, dtype=v.dtype) for v in values]


def fetch(sources, targets, semaphores):
    copies = [
        pltpu.make_async_copy(source, target, semaphores.at[i])
        for i, (source, target) in enumerate(zip(sources, targets))
    ]
    for copy in copies:
        copy.start()
    return copies


def iota(dims, axis):
    return lax.broadcasted_iota(jnp.int32, dims, axis)


def norm_parts(values):
    average = jnp.mean(values, axis=-1, keepdims=True)
    centred = values - average
    inverse = lax.rsqrt(jnp.mean(centred * centred, axis=-1, keepdims=True) + epsilon)
    return centred * inverse, inverse


def norm_back(unit, inverse, gain, back):
    inner = back * gain
    part = inverse * (
        inner
        - jnp.mean(inner, axis=-1, keepdims=True)
        - unit * jnp.mean(inner * unit, axis=-1, keepdims=True)
    )
    return part, jnp.sum(back * unit, axis=0, keepdims=True), jnp.sum(back, axis=0, keepdims=True)


def split(value):
    high = value.astype(BF)
    return high, (value - high.astype(F32)).astype(BF)


def two(value):
    return jnp.concatenate(split(value), axis=0)


def as_row(ref):
    return ref[...].reshape(1, ref.shape[0])


def as_column(ref):
    size = ref.shape[0]
    same = iota((size, size), 0) == iota((size, size), 1)
    row = as_row(ref)
    return jnp.sum(jnp.where(same, row, jnp.zeros_like(row)), axis=1, keepdims=True)


def token_limits(ref):
    place = as_row(ref).astype(F32)
    captions = place.shape[1]
    tokens = captions * SEQ
    owner = (iota((tokens, captions), 0) // SEQ == iota((tokens, captions), 1)).astype(F32)
    column = jnp.sum(owner * place, axis=1, keepdims=True)
    line = nt(place.astype(BF), owner.astype(BF))
    return line, column


def pool_mask(line, captions):
    dims = (captions, captions * SEQ)
    token = iota(dims, 1)
    inside = (token % SEQ).astype(F32) <= line
    return jnp.where((token // SEQ == iota(dims, 0)) & inside, 1.0, 0.0)


def spread_mask(column, captions):
    dims = (captions * SEQ, captions)
    token = iota(dims, 0)
    inside = (token % SEQ).astype(F32) <= column
    return jnp.where((token // SEQ == iota(dims, 1)) & inside, 1.0, 0.0)


def head_masks():
    lane = iota((1, 2 * HEAD), 1)
    even = (lane < HEAD).astype(F32)
    return even.astype(BF), (1.0 - even).astype(BF)


def caption_masks():
    lane = iota((SEQ, GROUP), 1) // SEQ
    return [lane == c for c in range(GROUP // SEQ)]


def compact(full, picks):
    out = full[:SEQ]
    for c in range(1, len(picks)):
        out = jnp.where(picks[c], full[c * SEQ : (c + 1) * SEQ], out)
    return out


def expand(low, lows):
    return jnp.concatenate([low * mask for mask in lows], axis=0)


def both_heads(value, masks):
    return jnp.concatenate([value * masks[0], value * masks[1]], axis=0)


def store_permuted(ref, value, dp, blocks):
    rows = value.shape[0] // blocks
    bits = blocks.bit_length() - 1
    if rows % SLOT:
        ref[...] = value
        return
    for b in range(blocks):
        k = jnp.bitwise_xor(dp, b)
        place = 0
        for bit in range(bits):
            place = place + ((k >> bit) & 1) * (1 << (bits - 1 - bit))
        ref[pl.ds(pl.multiple_of(place * rows, SLOT), rows), :] = value[b * rows : (b + 1) * rows]


def box_width(blocks):
    used = (FF + D) // blocks
    return used + -used % 128


def project_kernel(*refs):
    more = (len(refs) - 5 - 4 - 5 - 1) // 2
    mine, other, refs = refs[:5], refs[5 : 5 + more], refs[5 + more :]
    project_ref, normed_ref, unit_ref, inverse_ref = refs[:4]
    targets, (x, gain, shift, joint, wj, semaphores) = refs[4 : 4 + more], refs[4 + more :]
    copies = fetch(mine + other, (x, gain, shift, joint, wj) + targets, semaphores)
    copies[0].wait()
    unit_ref[...], inverse_ref[...] = norm_parts(x[...].astype(F32))
    for copy in copies[1:5]:
        copy.wait()
    normed_ref[...] = (unit_ref[...] * as_row(gain) + as_row(shift)).astype(BF)
    bias = as_row(joint)
    for i, part in enumerate((bias[:, :D], 0.0, bias[:, D:])):
        lanes = slice(i * D, (i + 1) * D)
        project_ref[:, lanes] = (nn(normed_ref[...], wj[:, lanes]) + part).astype(BF)
    for copy in copies[5:]:
        copy.wait()


def project_tokens(x, gain, shift, joint, wj, following):
    tokens = x.shape[0]
    mine = (x, gain, shift, joint, wj)
    return kernel_call(
        "project_tokens",
        project_kernel,
        [
            kept(tokens, 3 * D),
            kept(tokens, D),
            kept(tokens, D, dtype=F32),
            kept(tokens, 1, dtype=F32),
        ]
        + fetched(following),
        (),
        (),
        [(v.shape, v.dtype) for v in mine],
        cost(6 * tokens * D * D),
        far=mine + following,
        copies=5 + len(following),
    )


def turn_kernel(blocks, *refs):
    dp = lax.axis_index("dp")
    count = len(refs) // 2
    for source, target in zip(refs[:count], refs[count:]):
        store_permuted(target, source[...].T, dp, blocks)


def turn_tokens(blocks, *values):
    return kernel_call(
        "turn_tokens",
        functools.partial(turn_kernel, blocks),
        [kept(*v.shape[::-1]) for v in values],
        (),
        near(*values),
        (),
        cost(32 * values[0].shape[0] * D),
    )


def attend_kernel(*refs):
    more = (len(refs) - 5 - 3 - 1) // 2
    far, (place_ref, out_ref, x_ref, project_ref, wo_ref) = refs[:more], refs[more : more + 5]
    att_ref, context_ref, middle_ref = refs[more + 5 : more + 8]
    copies = fetch(far, refs[more + 8 : -1], refs[-1])
    line, _ = token_limits(place_ref)
    masks = head_masks()
    picks = caption_masks()
    lows = [pick.astype(F32).astype(BF) for pick in picks]
    key_place = iota((SEQ, GROUP), 0).astype(F32)

    def attend(h, carry):
        at = pl.multiple_of(h * 2 * HEAD, 128)
        for g in range(x_ref.shape[0] // GROUP):
            here = slice(g * GROUP, (g + 1) * GROUP)
            query = project_ref[here, pl.ds(at, 128)]
            keys = both_heads(project_ref[here, pl.ds(pl.multiple_of(D + at, 128), 128)], masks)
            values = both_heads(
                project_ref[here, pl.ds(pl.multiple_of(2 * D + at, 128), 128)], masks
            )
            scores = nt(keys, query)
            allowed = key_place <= line[:, here]
            parts = []
            for e in range(2):
                score = compact(scores[e * GROUP : (e + 1) * GROUP], picks) * scale
                score = jnp.where(allowed, score, negative)
                score = jnp.exp(score - jnp.max(score, axis=0, keepdims=True))
                weight = score / jnp.sum(score, axis=0, keepdims=True)
                att_ref[2 * h + e, :, here] = weight
                parts.append(expand(weight.astype(BF), lows))
            context_ref[here, pl.ds(at, 128)] = tn(jnp.concatenate(parts, axis=0), values).astype(BF)
        return carry

    lax.fori_loop(0, PAIRS, attend, 0, unroll=3)
    middle_ref[...] = x_ref[...].astype(F32) + (nn(context_ref[...], wo_ref[...]) + as_row(out_ref))
    for copy in copies:
        copy.wait()


def attend_tokens(place, out, x, project, wo, following):
    tokens = x.shape[0]
    return kernel_call(
        "attend_tokens",
        attend_kernel,
        [kept(HEADS, SEQ, tokens, dtype=F32), kept(tokens, D), kept(tokens, D, dtype=F32)]
        + fetched(following),
        (),
        near(place, out, x, project, wo),
        (),
        cost(4 * tokens * D * D),
        far=following,
        copies=len(following),
    )


def widen_kernel(blocks, *refs):
    more = (len(refs) - 9 - 8 - 3 - 1) // 2
    far = refs[:more]
    place_ref, gain_ref, shift_ref, wide_ref, narrow_ref, middle_ref, wu_ref, wn_ref, wm_ref = refs[
        more : more + 9
    ]
    second_ref, unit_ref, inverse_ref, upper_ref, box_ref, text_ref, scale_ref, embed_ref = refs[
        more + 9 : more + 17
    ]
    branch, wide, mean, semaphores = refs[-4:]
    copies = fetch(far, refs[more + 17 : -4], semaphores)
    captions = place_ref.shape[0]
    line, column = token_limits(place_ref)
    pool = pool_mask(line, captions)
    share = 1.0 / jnp.sum(pool, axis=1, keepdims=True)
    unit, inverse_ref[...] = norm_parts(middle_ref[...])
    unit_ref[...] = unit
    second_ref[...] = (unit * as_row(gain_ref) + as_row(shift_ref)).astype(BF)
    branch[...] = jnp.zeros_like(branch)
    wide[...] = as_row(wide_ref)
    pool_low = pool.astype(BF)
    step = 512

    def widen(i, carry):
        at = pl.multiple_of(i * step, 128)
        upper = nn(second_ref[...], wu_ref[:, pl.ds(at, step)]) + wide[:, pl.ds(at, step)]
        active = upper * (0.5 + 0.5 * jnp.tanh(upper * (BEND + CUBE * (upper * upper))))
        upper_ref[:, pl.ds(at, step)] = upper
        parts = two(nn(pool_low, active.astype(BF)) * share)
        mean[:, pl.ds(at, step)] = parts[:captions]
        branch[...] += nn(parts, wn_ref[pl.ds(at, step), :])
        return carry

    lax.fori_loop(0, FF // step, widen, 0, unroll=3)
    inside = jnp.where((iota((captions * SEQ, 1), 0) % SEQ).astype(F32) <= column, 1.0, 0.0)
    weight = inside / (column + 1.0)
    pooled = jnp.sum((middle_ref[...] * weight).reshape(captions, SEQ, D), axis=1)
    pooled = (pooled + (branch[:captions] + branch[captions:] + as_row(narrow_ref))).astype(BF)
    hidden, part = FF // blocks, D // blocks
    for b in range(blocks):
        box_ref[b, :, :hidden] = mean[:, b * hidden : (b + 1) * hidden]
        box_ref[b, :, hidden : hidden + part] = pooled[:, b * part : (b + 1) * part]
    text = nn(pooled, wm_ref[...])
    factor = lax.rsqrt(jnp.sum(text * text, axis=1, keepdims=True) + epsilon)
    text_ref[...] = text
    scale_ref[...] = factor
    embed_ref[...] = (text * factor).astype(BF)
    for copy in copies:
        copy.wait()


def slope_kernel(upper_ref, slope_ref):
    step = 512

    def part(i, carry):
        at = pl.multiple_of(i * step, 128)
        upper = upper_ref[:, pl.ds(at, step)]
        square = upper * upper
        half = 0.5 + 0.5 * jnp.tanh(upper * (BEND + CUBE * square))
        slope_ref[:, pl.ds(at, step)] = (
            half * (1.0 + (upper - upper * half) * (2.0 * BEND + 6.0 * CUBE * square))
        ).astype(BF)
        return carry

    lax.fori_loop(0, FF // step, part, 0)


def slope_tokens(upper):
    return kernel_call(
        "slope_tokens", slope_kernel, [kept(*upper.shape)], (), near(upper), (), cost(upper.size)
    )[0]


def widen_tokens(blocks, place, gain, shift, wide, narrow, middle, wu, wn, wm, following):
    tokens = middle.shape[0]
    captions = place.shape[0]
    return kernel_call(
        "widen_tokens",
        functools.partial(widen_kernel, blocks),
        [
            kept(tokens, D),
            kept(tokens, D, dtype=F32),
            kept(tokens, 1, dtype=F32),
            kept(tokens, FF, dtype=F32),
            kept(blocks, captions, box_width(blocks)),
            kept(captions, D, dtype=F32),
            kept(captions, 1, dtype=F32),
            kept(captions, D),
        ]
        + fetched(following),
        (),
        near(place, gain, shift, wide, narrow, middle, wu, wn, wm),
        [
            ((2 * captions, D), F32),
            ((1, FF), F32),
            ((captions, FF), BF),
        ],
        cost(2 * tokens * D * FF),
        far=following,
        copies=len(following),
    )


def match_of(paired, columns, images):
    column = iota((1, columns), 1)
    valid = column % SLOT < images
    name = jnp.where(valid, (column // SLOT) * images + column % SLOT, -1)
    return paired == name, valid


def contrast_kernel(
    images,
    parts,
    bits,
    heat_ref,
    own_ref,
    near_ref,
    wp_ref,
    embed_ref,
    paired_ref,
    weight_ref,
    picture_ref,
    score_ref,
    row_ref,
    inverse_ref,
    stats_ref,
    features,
):
    half = own_ref.shape[0] // SLOT
    for far, ref in enumerate((own_ref, near_ref)):

        def place(i, carry, far=far, ref=ref):
            p = i + far * half
            index = {axis: lax.axis_index(axis) for axis in ("dp", "rep")}
            for n, (axis, bit) in enumerate(bits):
                index[axis] = jnp.bitwise_xor(index[axis], ((p >> n) & 1) << bit)
            to = pl.ds(pl.multiple_of((index["dp"] * parts + index["rep"]) * SLOT, SLOT), SLOT)
            features[to, :] = ref[pl.ds(pl.multiple_of(i * SLOT, SLOT), SLOT), :]
            return carry

        lax.fori_loop(0, half, place, 0, unroll=4)
    picture = nn(features[...], wp_ref[...])
    picture = (
        picture * lax.rsqrt(jnp.sum(picture * picture, axis=1, keepdims=True) + epsilon)
    ).astype(BF)
    picture_ref[...] = picture
    score = nt(embed_ref[...], picture) / heat_ref[0]
    match, valid = match_of(as_column(paired_ref), score.shape[1], images)
    score = jnp.where(valid, score, negative)
    score_ref[...] = score
    top = jnp.max(score, axis=1, keepdims=True)
    row = jnp.log(jnp.sum(jnp.exp(score - top), axis=1, keepdims=True)) + top
    row_ref[...] = row
    positive = jnp.sum(jnp.where(match, score, 0.0), axis=1, keepdims=True)
    hits = jnp.where(match, 1.0, 0.0)
    counts = jnp.sum(hits, axis=0, keepdims=True)
    inverse = 1.0 / jnp.sum(hits * counts, axis=1, keepdims=True)
    inverse_ref[...] = inverse
    total = jnp.sum(as_column(weight_ref) * (row - positive - positive * inverse))
    best = jnp.max(score, axis=0, keepdims=True)
    mass = jnp.sum(jnp.exp(score - best), axis=0, keepdims=True)
    mass = jnp.where(iota(mass.shape, 1) == images, total, mass)
    wide = best.shape[1] // 4
    rows = [v[:, i * wide : (i + 1) * wide] for v in (best, mass) for i in range(4)]
    stats_ref[...] = jnp.concatenate(rows, axis=0)


def contrast(images, parts, bits, heat, own, far, wp, embed, paired, weight):
    captions = embed.shape[0]
    columns = 2 * own.shape[0]
    return kernel_call(
        "contrast",
        functools.partial(contrast_kernel, images, parts, bits),
        [
            kept(columns, D),
            kept(captions, columns, dtype=F32),
            kept(captions, 1, dtype=F32),
            kept(captions, 1, dtype=F32),
            shape(8, columns // 4),
        ],
        (heat,),
        near(own, far, wp, embed, paired, weight),
        [((columns, D), BF)],
        cost(2 * columns * D * D),
        max(LIMIT, columns * 8192),
    )


def merged(refs):
    best = functools.reduce(jnp.maximum, [ref[:4] for ref in refs])
    mass = sum(ref[4:] * jnp.exp(ref[:4] - best) for ref in refs)
    return best, mass


def merge_kernel(*refs):
    *given, out_ref = refs
    best, mass = merged(given)
    out_ref[...] = jnp.concatenate([best, mass], axis=0)


def merge(stats):
    return kernel_call("merge", merge_kernel, [shape(*stats[0].shape)], (), stats)[0]


def quarters(rep, away, flip=0):
    core = rep & 1
    out = []
    for xrel in range(2):
        for yrel in range(2):
            block = jnp.bitwise_xor(rep, 2 * xrel + away)
            x_first = 1 - core if away == flip else core
            out.append((jnp.where(x_first == 1, 2 * xrel + yrel, 2 * yrel + xrel), block, yrel))
    return out


def head_back_kernel(
    images,
    count_stats,
    rounds,
    heat_ref,
    place_ref,
    score_ref,
    row_ref,
    inverse_ref,
    weight_ref,
    paired_ref,
    picture_ref,
    text_ref,
    scale_ref,
    wm_ref,
    wn_ref,
    slope_ref,
    second_t_ref,
    box_ref,
    *refs,
):
    first = 1 << rounds[0]
    pieces = refs[len(refs) - first :]
    stats = refs[:count_stats]
    (
        back_ref,
        away_ref,
        here_ref,
        pooled_ref,
        loss_ref,
        down_bias_ref,
        up_bias_ref,
    ) = refs[count_stats : len(refs) - first]
    rep = lax.axis_index("rep")
    heat = heat_ref[0]
    captions = place_ref.shape[0]
    line, column = token_limits(place_ref)
    count = jnp.sum(pool_mask(line, captions), axis=1, keepdims=True)
    owner = spread_mask(column, captions).astype(BF)
    owner = jnp.concatenate([owner, owner], axis=1)

    score = score_ref[...]
    match, valid = match_of(as_column(paired_ref), score.shape[1], images)
    best, mass = merged(stats)
    column_log = jnp.log(mass) + best
    column_log = jnp.concatenate([column_log[i : i + 1] for i in range(4)], axis=1)
    loss_ref[...] = mass[:1, images : images + 1] + jnp.sum(
        jnp.where(valid, column_log, 0.0), axis=1, keepdims=True
    )
    weight = as_column(weight_ref)
    graded = (
        weight * jnp.exp(score - row_ref[...])
        + jnp.exp(score - column_log)
        - jnp.where(match, weight * (1.0 + inverse_ref[...]), 0.0)
    )
    graded = jnp.where(valid, graded / heat, 0.0).astype(BF)
    embed_back = nn(graded, picture_ref[...])
    text = text_ref[...]
    factor = scale_ref[...]
    text_dot = jnp.sum(text * embed_back, axis=1, keepdims=True)
    text_back = (factor * embed_back - text * (factor * factor * factor) * text_dot).astype(BF)
    blocks, _, wide = box_ref.shape
    masks = gather_masks(rounds, blocks)
    for c, piece_ref in enumerate(pieces):
        for i in range(blocks // first):
            block = jnp.bitwise_xor(lax.axis_index("dp"), masks[i * first + c])
            piece_ref[:, i * wide : (i + 1) * wide] = box_ref[block]
        piece_ref[:, (blocks // first) * wide :] = text_back
    pooled_back = nt(text_back, wm_ref[...])
    pooled_ref[...] = pooled_back
    branch = (pooled_back / count).astype(BF)
    down_bias_ref[...] = jnp.sum(branch.astype(F32) * count, axis=0, keepdims=True)
    ones = jnp.ones((SLOT, back_ref.shape[0]), BF)
    step = 512

    def widen(i, carry):
        at = pl.multiple_of(i * step, 128)
        part = nn(owner, two(nt(branch, wn_ref[pl.ds(at, step), :])))
        part = (part * slope_ref[:, pl.ds(at, step)].astype(F32)).astype(BF)
        back_ref[:, pl.ds(at, step)] = part
        up_bias_ref[:, pl.ds(at, step)] = nn(ones, part)[:1]
        return carry

    lax.fori_loop(0, FF // step, widen, 0, unroll=3)
    half = second_t_ref.shape[0] // 2
    wide = FF // 4
    for turn, target in enumerate((away_ref, here_ref)):
        for place, block, yrel in quarters(rep, 1 - turn):
            part = nn(
                second_t_ref[yrel * half : (yrel + 1) * half],
                back_ref[:, pl.ds(pl.multiple_of(block * wide, 128), wide)],
            )
            for h in range(2):
                target[place, h] = part[:, h * (wide // 2) : (h + 1) * (wide // 2)].astype(BF)


def head_back(images, rounds, heat, place, stats, score, row, inverse, weight, paired, picture, text,
              factor, wm, wn, slope, second_t, box):
    captions = text.shape[0]
    tokens = slope.shape[0]
    piece = (4, 2, D // 2, FF // 8)
    return kernel_call(
        "head_back",
        functools.partial(head_back_kernel, images, len(stats), rounds),
        [
            kept(tokens, FF),
            kept(*piece),
            kept(*piece),
            kept(captions, D, dtype=F32),
            shape(1, 1),
            shape(1, D),
            shape(1, FF),
        ]
        + [shape(captions, (box.shape[0] >> rounds[0]) * box.shape[2] + D, dtype=BF)] * (1 << rounds[0]),
        (heat,),
        (
            *near(place, score, row, inverse, weight, paired),
            *near(picture, text, factor, wm, wn, slope, second_t, box),
            *stats,
        ),
        (),
        cost(2 * tokens * D * FF),
    )


def middle_back_kernel(
    place_ref,
    gain_ref,
    pooled_ref,
    back_ref,
    wu_ref,
    unit_ref,
    inverse_ref,
    wo_ref,
    total_ref,
    attended_ref,
    context_back_ref,
    gain_back_ref,
    shift_back_ref,
    bias_ref,
):
    captions = place_ref.shape[0]
    line, column = token_limits(place_ref)
    count = jnp.sum(pool_mask(line, captions), axis=1, keepdims=True)
    owner = spread_mask(column, captions).astype(BF)
    owner = jnp.concatenate([owner, owner], axis=1)
    second_back = nt(back_ref[...], wu_ref[...])
    part, gain_back_ref[...], shift_back_ref[...] = norm_back(
        unit_ref[...], inverse_ref[...], as_row(gain_ref), second_back
    )
    total = nn(owner, two(pooled_ref[...] / count)) + part
    total_ref[...] = total
    attended = total.astype(BF)
    attended_ref[...] = attended
    bias_ref[...] = nn(jnp.ones((SLOT, attended.shape[0]), BF), attended)[:1]
    context_back_ref[...] = nt(attended, wo_ref[...]).astype(BF)


def middle_back(place, gain, pooled, back, wu, unit, inverse, wo):
    tokens = back.shape[0]
    return kernel_call(
        "middle_back",
        middle_back_kernel,
        [
            kept(tokens, D, dtype=F32),
            kept(tokens, D),
            kept(tokens, D),
            shape(1, D),
            shape(1, D),
            shape(1, D),
        ],
        (),
        near(place, gain, pooled, back, wu, unit, inverse, wo),
        (),
        cost(2 * tokens * D * (FF + D)),
    )


def attention_back_kernel(project_ref, att_ref, context_back_ref, back_ref, bias_ref):
    masks = head_masks()
    picks = caption_masks()
    lows = [pick.astype(F32).astype(BF) for pick in picks]
    low_scale = jnp.asarray(scale, BF)
    first = iota((GROUP, 2 * HEAD), 1) < HEAD
    tokens = project_ref.shape[0]

    def attend(h, carry):
        at = pl.multiple_of(h * 2 * HEAD, 128)
        at_k = pl.multiple_of(D + at, 128)
        at_v = pl.multiple_of(2 * D + at, 128)
        for g in range(tokens // GROUP):
            span = slice(g * GROUP, (g + 1) * GROUP)
            query = project_ref[span, pl.ds(at, 128)]
            keys = both_heads(project_ref[span, pl.ds(at_k, 128)], masks)
            values = both_heads(project_ref[span, pl.ds(at_v, 128)], masks)
            upper = context_back_ref[span, pl.ds(at, 128)]
            full = nt(values, upper)
            weights, grads = [], []
            for e in range(2):
                weight = att_ref[2 * h + e, :, span]
                part = compact(full[e * GROUP : (e + 1) * GROUP], picks)
                grad = weight * (part - jnp.sum(weight * part, axis=0, keepdims=True))
                weights.append(expand(weight.astype(BF), lows))
                grads.append(expand(grad.astype(BF) * low_scale, lows))
            weights = jnp.concatenate(weights, axis=0)
            grads = jnp.concatenate(grads, axis=0)
            back_ref[span, pl.ds(at, 128)] = tn(grads, keys).astype(BF)
            wide = nn(grads, query)
            back_ref[span, pl.ds(at_k, 128)] = jnp.where(first, wide[:GROUP], wide[GROUP:]).astype(
                BF
            )
            wide = nn(weights, upper)
            back_ref[span, pl.ds(at_v, 128)] = jnp.where(first, wide[:GROUP], wide[GROUP:]).astype(
                BF
            )
        return carry

    lax.fori_loop(0, PAIRS, attend, 0, unroll=3)
    ones = jnp.ones((SLOT, tokens), BF)
    for i in range(3):
        lanes = slice(i * D, (i + 1) * D)
        bias_ref[:, lanes] = nn(ones, back_ref[:, lanes])[:1]


def attention_back(project, att, context_back):
    tokens = project.shape[0]
    return kernel_call(
        "attention_back",
        attention_back_kernel,
        [kept(tokens, 3 * D), shape(1, 3 * D)],
        (),
        near(project, att, context_back),
        (),
        cost(3 * tokens * D * D),
    )


def left_columns_kernel(back_ref, normed_t_ref, away_ref, here_ref, chosen):
    rep = lax.axis_index("rep")
    joint = 3 * D // 4
    some = chosen.shape[2]
    for r in range(4):

        @pl.when(rep == r)
        def _():
            for i, k in enumerate((1, 3, 0, 2)):
                b = r ^ k
                chosen[i] = back_ref[:, b * joint : b * joint + some]

    half = D // 2
    for turn, target in enumerate((away_ref, here_ref)):
        for i, (place, _, yrel) in enumerate(quarters(rep, 1 - turn, 1)):
            lines = slice(yrel * half, (yrel + 1) * half)
            target[place] = nn(normed_t_ref[lines], chosen[2 * turn + i // 2]).astype(BF)


def right_columns_kernel(
    back_ref, attended_ref, normed_t_ref, context_t_ref, away_ref, here_ref, chosen
):
    rep = lax.axis_index("rep")
    joint = 3 * D // 4
    out = D // 4
    some = chosen.shape[2] - out
    for r in range(4):

        @pl.when(rep == r)
        def _():
            for i, k in enumerate((1, 3, 0, 2)):
                b = r ^ k
                chosen[i, :, :some] = back_ref[:, (b + 1) * joint - some : (b + 1) * joint]
                chosen[i, :, some:] = attended_ref[:, b * out : (b + 1) * out]

    half = D // 2
    for turn, target in enumerate((away_ref, here_ref)):
        for i, (place, _, yrel) in enumerate(quarters(rep, 1 - turn)):
            block = 2 * turn + i // 2
            lines = slice(yrel * half, (yrel + 1) * half)
            target[place, :, :some] = nn(normed_t_ref[lines], chosen[block, :, :some]).astype(BF)
            target[place, :, some:] = nn(context_t_ref[lines], chosen[block, :, some:]).astype(BF)


def columns_gradient(name, body, operands):
    tokens = operands[0].shape[0]
    piece = (4, D // 2, D // 2)
    return kernel_call(
        name,
        body,
        [kept(*piece), kept(*piece)],
        (),
        near(*operands),
        [((4, tokens, D // 2), BF)],
        cost(tokens * D * FF),
    )


def token_back_kernel(
    gain_ref,
    unit_ref,
    inverse_ref,
    middle_ref,
    back_ref,
    wj_ref,
    joint_ref,
    out_ref,
    gain2_ref,
    shift2_ref,
    wide_ref,
    narrow_ref,
    token_ref,
    sums_ref,
):
    part, gain1, shift1 = norm_back(
        unit_ref[...], inverse_ref[...], as_row(gain_ref), nt(back_ref[...], wj_ref[...])
    )
    token_ref[...] = middle_ref[...] + part
    line = 0
    rest = (joint_ref, out_ref, gain2_ref, shift2_ref, wide_ref, narrow_ref)
    for value in [gain1, shift1] + [ref[...] for ref in rest]:
        for i in range(value.shape[1] // 128):
            sums_ref[line : line + 1] = value[:, i * 128 : (i + 1) * 128]
            line += 1
    sums_ref[line:] = jnp.zeros((sums_ref.shape[0] - line, 128), F32)


def token_back(gain, unit, inverse, middle, back, wj, sums):
    return kernel_call(
        "token_back",
        token_back_kernel,
        [shape(unit.shape[0], D), shape(ALL_LINES, 128)],
        (),
        (gain, *near(unit, inverse, middle, back, wj), *sums),
        (),
        cost(6 * unit.shape[0] * D * D),
    )


def low_rank_kernel(
    hidden, own_ref, near_ref, wm_ref, down_ref, head_ref, other_ref, box, back
):
    rows = own_ref.shape[0]
    box[:rows] = own_ref[...]
    box[rows:] = near_ref[...]
    part = down_ref.shape[0]
    start = box.shape[1] - D
    rep = lax.axis_index("rep")
    for r in range(D // part):

        @pl.when(rep == r)
        def _():
            for i, b in enumerate((r, r ^ 2)):
                back[i] = box[:, start + b * part : start + (b + 1) * part]

    wide = head_ref.shape[1]
    for i in range(2):
        block = jnp.bitwise_xor(rep, 2 * i)
        here = wm_ref[pl.ds(pl.multiple_of(block * part, SLOT), part), :]
        pooled = nt(box[:, start:], here).astype(BF)
        down = tn(pooled, box[:, :hidden])
        head = tn(back[i], box[:, hidden : hidden + wide])
        if i == 0:
            down_ref[...] = down
            head_ref[...] = head
        else:
            other_ref[:, :hidden] = down.astype(BF)
            other_ref[:, hidden:] = head.astype(BF)


def low_rank(blocks, parts, own, far, wm):
    rows = 2 * own.shape[0]
    hidden, wide, part = FF // blocks, D // blocks, D // parts
    return kernel_call(
        "low_rank",
        functools.partial(low_rank_kernel, hidden),
        [shape(part, hidden), shape(part, wide), shape(part, hidden + wide, dtype=BF)],
        (),
        near(own, far, wm),
        [((rows, own.shape[1]), BF), ((2, rows, part), BF)],
        cost(2 * rows * D * D),
    )


def finish_kernel(groups, *refs):
    up, first, second, lines = (
        [refs[sum(groups[:i]) + n] for n in range(groups[i])] for i in range(4)
    )
    loss_ref, down_ref, head_ref, other_ref = refs[sum(groups) : sum(groups) + 4]
    (
        joint_ref,
        out_ref,
        up_block_ref,
        down_block_ref,
        head_block_ref,
        loss_out_ref,
        *vector_refs,
    ) = refs[sum(groups) + 4 :]

    def total(terms):
        return sum(ref[...].astype(F32) for ref in terms)

    up_sum = total(up)
    for h in range(2):
        lanes = slice(h * up_sum.shape[2], (h + 1) * up_sum.shape[2])
        up_block_ref[:, lanes] = up_sum[h]
    one, two_ = total(first), total(second)
    some = one.shape[1]
    rest = joint_ref.shape[1] - some
    joint_ref[:, :some] = one
    joint_ref[:, some:] = two_[:, :rest]
    out_ref[...] = two_[:, rest:]
    hidden = down_ref.shape[1]
    down_block_ref[...] = down_ref[...] + other_ref[:, :hidden].astype(F32)
    head_block_ref[...] = (head_ref[...] + other_ref[:, hidden:].astype(F32)).T
    loss_out_ref[...] = loss_ref[...].reshape(1)
    vectors = total(lines)
    starts = (GAIN1, SHIFT1, JOINT, OUT, GAIN2, SHIFT2, WIDE, NARROW)
    for start, ref in zip(starts, vector_refs):
        for i in range(ref.shape[0] // 128):
            line = start // 128 + i
            if start == JOINT and i >= D // 128:
                line += D // 128
            ref[pl.ds(i * 128, 128)] = vectors[line]


def finish(up, first, second, vectors, loss, low, joint):
    rows = up[0].shape[1]
    sizes = (D, D, 2 * D, D, D, D, FF, D)
    return kernel_call(
        "finish",
        functools.partial(finish_kernel, [len(v) for v in (up, first, second, vectors)]),
        [
            shape(rows, joint),
            shape(rows, D - joint),
            shape(rows, D),
            shape(*low[0].shape),
            shape(*low[1].shape[::-1]),
            shape(1),
        ]
        + [shape(n) for n in sizes],
        (),
        (*up, *first, *second, *vectors, loss, *low),
    )


def both_pairs(partner):
    dp, rep = lax.axis_size("dp"), lax.axis_size("rep")
    pairs = []
    for i in range(dp):
        for j in range(rep):
            a, b = partner(i, j)
            pairs.append((i * rep + j, a * rep + b))
    return pairs


def exchange(value, partner):
    return lax.ppermute(value, ("dp", "rep"), both_pairs(partner))


def first_turn(i, j):
    return (i, j ^ 2) if j & 1 == 0 else (i ^ 1, j)


def second_turn(i, j):
    return (i ^ 1, j) if j & 1 == 0 else (i, j ^ 2)


def added(a, b):
    return (a.astype(F32) + b.astype(F32)).astype(BF)


def halved(here, got):
    half = here.shape[0] // 2
    return added(here[:half], got[:half]), added(here[half:], got[half:])


def parted(here, got, count):
    rows = here.shape[-2] // count
    parts = [slice(i * rows, (i + 1) * rows) for i in range(count)]
    return [added(here[..., p, :], got[..., p, :]) for p in parts]


def core_turn(i, j):
    return i, j ^ 1


def across(i, j):
    return i, j ^ 2


def group_round(keep, got, group):
    masks = group_masks(group)
    bits = len(group)
    parts = parted(keep, got, len(masks))
    place = [sum(((c >> n) & 1) << (bits - 1 - n) for n in range(bits)) for c in range(len(masks))]
    return [parts[0]] + [
        exchange(parts[place[c]], lambda i, j: (i ^ masks[c][0], j)) for c in range(1, len(masks))
    ]


def row_rounds(keep, got, groups):
    terms = [keep, got]
    for group in groups:
        if len(terms) > 2:
            terms = [terms[0], sum(v.astype(F32) for v in terms[1:])]
        terms = group_round(*terms, group)
    return terms


order = lax.optimization_barrier


def dp_groups():
    bits = [("dp", b) for b in range(1, lax.axis_size("dp").bit_length() - 1)]
    return [bits[i : i + 2] for i in range(0, len(bits), 2)] + [[("dp", 0)]]


def all_groups():
    bits = [("rep", b) for b in range(1, lax.axis_size("rep").bit_length() - 1)]
    groups = dp_groups()
    return groups[:-1] + [groups[-1] + bits, [("rep", 0)]]


def group_masks(group):
    out = [(0, 0)]
    for axis, bit in group:
        out += [(a | 1 << bit, b) if axis == "dp" else (a, b | 1 << bit) for a, b in out]
    return out


def gather_masks(rounds, blocks):
    bits = [0] + list(range(blocks.bit_length() - 2, 0, -1))
    masks, used = [0], 0
    for count in rounds:
        for bit in bits[used : used + count]:
            masks = masks + [m | 1 << bit for m in masks]
        used += count
    return masks


def split_round(value, wide, group):
    blocks = (value.shape[1] - D) // wide
    turns = group_masks(group)
    text = value[:, blocks * wide :]
    pieces = []
    for c, (a, b) in enumerate(turns):
        chosen = [value[:, i * wide : (i + 1) * wide] for i in range(c, blocks, len(turns))]
        piece = jnp.concatenate(chosen + [text], axis=1)
        pieces.append(piece if c == 0 else exchange(piece, lambda i, j: (i ^ a, j ^ b)))
    return pieces


def round_of(value, group):
    return [value] + [
        exchange(value, lambda i, j: (i ^ a, j ^ b)) for a, b in group_masks(group)[1:]
    ]


def relative_rows(value, blocks):
    rows = value.shape[0] // blocks
    if rows % SLOT == 0:
        return value
    bits = blocks.bit_length() - 1
    place = jnp.arange(blocks, dtype=jnp.int32)
    source = jnp.zeros_like(place)
    for bit in range(bits):
        source = source + ((place >> (bits - 1 - bit)) & 1) * (1 << bit)
    source = source ^ lax.axis_index("dp")
    return value.reshape(blocks, rows, -1)[source].reshape(value.shape)


def local(
    incoming_activations,
    caption_final_place,
    paired_picture,
    caption_weight,
    locked_picture_features,
    softmax_heat,
    premix_scaling_factor,
    premix_shift_term,
    stacked_mixing_matrix,
    asking_reading_offsets,
    mixing_result_matrix,
    mixing_result_offset,
    premlp_scaling_factor,
    premlp_shift_term,
    widening_matrix,
    widening_offset,
    narrowing_matrix,
    narrowing_offset,
    caption_mapping_matrix,
    picture_mapping_matrix,
):
    both = ("dp", "rep")
    devices = lax.axis_size(both)
    blocks = lax.axis_size("dp")
    parts = lax.axis_size("rep")
    captions = caption_final_place.shape[0]
    images = locked_picture_features.shape[0]
    groups = all_groups()
    pieces = round_of(jnp.pad(locked_picture_features, ((0, SLOT - images), (0, 0))), groups[0])
    project, normed, unit1, inverse1, place, out, x, wo = project_tokens(
        incoming_activations,
        premix_scaling_factor,
        premix_shift_term,
        asking_reading_offsets,
        stacked_mixing_matrix,
        (
            caption_final_place,
            mixing_result_offset,
            incoming_activations,
            mixing_result_matrix,
        ),
    )
    project, pieces = order((project, pieces))
    for group in groups[1:-1]:
        pieces = round_of(jnp.concatenate(pieces), group)
    att, context, middle, gain2, shift2, wide, narrow, wu, wn, wm = attend_tokens(
        place,
        out,
        x,
        project,
        wo,
        (
            premlp_scaling_factor,
            premlp_shift_term,
            widening_offset,
            narrowing_offset,
            widening_matrix,
            narrowing_matrix,
            caption_mapping_matrix,
        ),
    )
    middle, pieces = order((middle, pieces))
    own, far = round_of(jnp.concatenate(pieces), groups[-1])
    second, unit2, inverse2, upper, box, text, factor, embed, wp, paired, weight = widen_tokens(
        blocks,
        place,
        gain2,
        shift2,
        wide,
        narrow,
        middle,
        wu,
        wn,
        wm,
        (picture_mapping_matrix, paired_picture, caption_weight),
    )
    embed, far = order((embed, far))
    picture, score, row, inverse, stats = contrast(
        images,
        parts,
        sum(groups, []),
        softmax_heat,
        own,
        far,
        wp,
        embed,
        paired,
        weight,
    )
    groups = dp_groups()
    high = [[bit] for group in groups[:-1] for bit in group]
    factor_groups = groups[-1:] + high[::-1]
    stats = round_of(stats, [("rep", 0)])
    normed_t, context_t, second_t = (
        relative_rows(v, blocks) for v in turn_tokens(blocks, normed, context, second)
    )
    stats = round_of(merge(stats), [("rep", 1)] + groups[-1])
    slope = slope_tokens(upper)
    stats, slope = order((stats, slope))
    for group in groups[:-1]:
        stats = round_of(merge(stats), group)
    back, away, here, pooled_back, loss, down_bias, up_bias, *pieces = head_back(
        images,
        [len(group) for group in factor_groups],
        softmax_heat,
        place,
        stats,
        score,
        row,
        inverse,
        weight,
        paired,
        picture,
        text,
        factor,
        wm,
        wn,
        slope,
        second_t,
        box,
    )
    loss = loss / (captions * devices)
    got = exchange(away, core_turn)
    pieces = pieces[:1] + [
        exchange(piece, lambda i, j: (i ^ a, j ^ b))
        for piece, (a, b) in zip(pieces[1:], group_masks(factor_groups[0])[1:])
    ]
    total, attended, context_back, gain2, shift2, out_bias = middle_back(
        place,
        gain2,
        pooled_back,
        back,
        wu,
        unit2,
        inverse2,
        wo,
    )
    context_back, got, pieces = order((context_back, got, pieces))
    up, send = halved(here, got)
    got_up = exchange(send, first_turn)
    pieces = split_round(jnp.concatenate(pieces), box.shape[2], factor_groups[1])
    project_back, joint_bias = attention_back(project, att, context_back)
    away, here = columns_gradient("left_columns", left_columns_kernel, (project_back, normed_t))
    got = exchange(away, core_turn)
    project_back, away = order((project_back, away))
    away, here2 = columns_gradient(
        "right_columns", right_columns_kernel, (project_back, attended, normed_t, context_t)
    )
    project_back, away, got, got_up = order((project_back, away, got, got_up))
    up, up_send = halved(up, got_up)
    first, send = halved(here, got)
    got = exchange(jnp.concatenate([up_send[0], send]), second_turn)
    got2 = exchange(away, core_turn)
    joint = 3 * D // parts
    token, sums = token_back(
        premix_scaling_factor,
        unit1,
        inverse1,
        total,
        project_back,
        stacked_mixing_matrix,
        (joint_bias, out_bias, gain2, shift2, up_bias, down_bias),
    )
    sums, got2 = order((sums, got2))
    lines = round_of(sums, [("rep", 0)])
    lines = round_of(sum(lines), [("rep", 1)])
    second, send2 = halved(here2, got2)
    got, send2, lines, pieces = order((got, send2, lines, pieces))
    up, got_up = group_round(up[0], got[:2], high[0])
    first, send = halved(first, got[2:])
    got2 = exchange(jnp.concatenate([send2, send]), first_turn)
    lines = round_of(sum(lines), groups[-1])
    for group in factor_groups[2:]:
        pieces = split_round(jnp.concatenate(pieces), box.shape[2], group)
    got_up, got2, lines, pieces = order((got_up, got2, lines, pieces))
    second, send = halved(second, got2[:2])
    second, first, got = second[0], first[0], got2[2]
    got2 = exchange(send[0], second_turn)
    first, got = group_round(first, got, high[0])
    for group in high[1:]:
        up, got_up = group_round(up, got_up, group)
    lines = round_of(sum(lines), high[0])
    factors = jnp.concatenate(pieces)
    far = exchange(factors, core_turn)
    got, got2, lines, far = order((got, got2, lines, far))
    second = [second, got2]
    for group in groups[:-1]:
        if len(second) > 2:
            second = [second[0], sum(v.astype(F32) for v in second[1:])]
        second = group_round(*second, group)
    for group in high[1:]:
        first, got = group_round(first, got, group)
        lines = round_of(sum(lines), group)
    *low, other = low_rank(blocks, parts, factors, far, wm)
    other = exchange(other, across)
    first, up, vectors = [first, got], [up, got_up], lines
    joint_block, out_block, up_block, down_block, head_block, loss, *grads = finish(
        up, first, second, vectors, loss, (*low, other), joint
    )
    return (
        loss,
        token,
        grads[0],
        grads[1],
        joint_block,
        grads[2],
        out_block,
        grads[3],
        grads[4],
        grads[5],
        up_block,
        grads[6],
        down_block.T,
        grads[7],
        head_block,
    )


def solution(mesh):
    spread = P(("dp", "rep"), None)
    line = P(("dp", "rep"))
    block = P("dp", "rep")
    in_specs = (spread, line, line, line, spread) + (P(),) * 15
    out_specs = (
        P(),
        spread,
        P(),
        P(),
        block,
        P(),
        block,
        P(),
        P(),
        P(),
        block,
        P(),
        block,
        P(),
        block,
    )
    return jax.shard_map(local, mesh=mesh, in_specs=in_specs, out_specs=out_specs, check_vma=False)
```

```python
import functools

import jax
import jax.numpy as jnp
from jax import lax
from jax.experimental import pallas as pl
from jax.experimental.pallas import tpu as pltpu
from jax.sharding import PartitionSpec as P

D = 768
HEADS = 12
HEAD = 64
SEQ = 16
FF = 3072
GROUP = 128
PAIRS = HEADS // 2
SLOT = 16
BF = jnp.bfloat16
F32 = jnp.float32

epsilon = 1e-06
BEND = 0.7978845608028654
CUBE = BEND * 0.044715
negative = -1e30
scale = HEAD ** (-0.5)
LIMIT = 20 * 1024 * 1024

GAIN1, SHIFT1, JOINT, OUT, GAIN2, SHIFT2, WIDE, NARROW = 0, 768, 1536, 3840, 4608, 5376, 6144, 9216
VECTORS = 9984
LINES = VECTORS // 128
ALL_LINES = LINES + -LINES % 8

vmem = pl.BlockSpec(memory_space=pltpu.VMEM)
hbm = pl.BlockSpec(memory_space=pltpu.HBM)
smem = pl.BlockSpec(memory_space=pltpu.SMEM)


def dot(a, b, dims):
    return lax.dot_general(a, b, (dims, ((), ())), preferred_element_type=F32)


def nn(a, b):
    return dot(a, b, ((1,), (0,)))


def nt(a, b):
    return dot(a, b, ((1,), (1,)))


def tn(a, b):
    return dot(a, b, ((0,), (0,)))


def cost(flops):
    return pl.CostEstimate(flops=flops, transcendentals=0, bytes_accessed=0)


def shape(*dims, dtype=F32):
    return jax.ShapeDtypeStruct(dims, dtype)


def kept(*dims, dtype=BF):
    return pltpu.VMEM(dims, dtype)


def near(*values):
    return [pltpu.with_memory_space_constraint(v, pltpu.VMEM) for v in values]


def kernel_call(
    name, body, results, small, operands, scratch=(), estimate=None, limit=LIMIT, far=(), copies=0
):
    semaphores = [pltpu.SemaphoreType.DMA((copies,))] if copies else []
    return pl.pallas_call(
        body,
        out_shape=results,
        in_specs=[smem] * len(small) + [hbm] * len(far) + [vmem] * len(operands),
        out_specs=[vmem] * len(results),
        scratch_shapes=[pltpu.VMEM(s, t) for s, t in scratch] + semaphores,
        compiler_params=pltpu.CompilerParams(vmem_limit_bytes=limit),
        cost_estimate=estimate,
        name=name,
    )(*small, *[pltpu.with_memory_space_constraint(v, pltpu.HBM) for v in far], *operands)


def fetched(values):
    return [kept(*v.shape, dtype=v.dtype) for v in values]


def fetch(sources, targets, semaphores):
    copies = [
        pltpu.make_async_copy(source, target, semaphores.at[i])
        for i, (source, target) in enumerate(zip(sources, targets))
    ]
    for copy in copies:
        copy.start()
    return copies


def iota(dims, axis):
    return lax.broadcasted_iota(jnp.int32, dims, axis)


def norm_parts(values):
    average = jnp.mean(values, axis=-1, keepdims=True)
    centred = values - average
    inverse = lax.rsqrt(jnp.mean(centred * centred, axis=-1, keepdims=True) + epsilon)
    return centred * inverse, inverse


def norm_back(unit, inverse, gain, back):
    inner = back * gain
    part = inverse * (
        inner
        - jnp.mean(inner, axis=-1, keepdims=True)
        - unit * jnp.mean(inner * unit, axis=-1, keepdims=True)
    )
    return part, jnp.sum(back * unit, axis=0, keepdims=True), jnp.sum(back, axis=0, keepdims=True)


def split(value):
    high = value.astype(BF)
    return high, (value - high.astype(F32)).astype(BF)


def two(value):
    return jnp.concatenate(split(value), axis=0)


def as_row(ref):
    return ref[...].reshape(1, ref.shape[0])


def as_column(ref):
    size = ref.shape[0]
    same = iota((size, size), 0) == iota((size, size), 1)
    row = as_row(ref)
    return jnp.sum(jnp.where(same, row, jnp.zeros_like(row)), axis=1, keepdims=True)


def token_limits(ref):
    place = as_row(ref).astype(F32)
    captions = place.shape[1]
    tokens = captions * SEQ
    owner = (iota((tokens, captions), 0) // SEQ == iota((tokens, captions), 1)).astype(F32)
    column = jnp.sum(owner * place, axis=1, keepdims=True)
    line = nt(place.astype(BF), owner.astype(BF))
    return line, column


def pool_mask(line, captions):
    dims = (captions, captions * SEQ)
    token = iota(dims, 1)
    inside = (token % SEQ).astype(F32) <= line
    return jnp.where((token // SEQ == iota(dims, 0)) & inside, 1.0, 0.0)


def spread_mask(column, captions):
    dims = (captions * SEQ, captions)
    token = iota(dims, 0)
    inside = (token % SEQ).astype(F32) <= column
    return jnp.where((token // SEQ == iota(dims, 1)) & inside, 1.0, 0.0)


def head_masks():
    lane = iota((1, 2 * HEAD), 1)
    even = (lane < HEAD).astype(F32)
    return even.astype(BF), (1.0 - even).astype(BF)


def caption_masks():
    lane = iota((SEQ, GROUP), 1) // SEQ
    return [lane == c for c in range(GROUP // SEQ)]


def compact(full, picks):
    out = full[:SEQ]
    for c in range(1, len(picks)):
        out = jnp.where(picks[c], full[c * SEQ : (c + 1) * SEQ], out)
    return out


def expand(low, lows):
    return jnp.concatenate([low * mask for mask in lows], axis=0)


def both_heads(value, masks):
    return jnp.concatenate([value * masks[0], value * masks[1]], axis=0)


def store_permuted(ref, value, dp, blocks):
    rows = value.shape[0] // blocks
    bits = blocks.bit_length() - 1
    if rows % SLOT:
        ref[...] = value
        return
    for b in range(blocks):
        k = jnp.bitwise_xor(dp, b)
        place = 0
        for bit in range(bits):
            place = place + ((k >> bit) & 1) * (1 << (bits - 1 - bit))
        ref[pl.ds(pl.multiple_of(place * rows, SLOT), rows), :] = value[b * rows : (b + 1) * rows]


def box_width(blocks):
    used = (FF + D) // blocks
    return used + -used % 128


def project_kernel(*refs):
    more = (len(refs) - 5 - 4 - 5 - 1) // 2
    mine, other, refs = refs[:5], refs[5 : 5 + more], refs[5 + more :]
    project_ref, normed_ref, unit_ref, inverse_ref = refs[:4]
    targets, (x, gain, shift, joint, wj, semaphores) = refs[4 : 4 + more], refs[4 + more :]
    copies = fetch(mine + other, (x, gain, shift, joint, wj) + targets, semaphores)
    copies[0].wait()
    unit_ref[...], inverse_ref[...] = norm_parts(x[...].astype(F32))
    for copy in copies[1:5]:
        copy.wait()
    normed_ref[...] = (unit_ref[...] * as_row(gain) + as_row(shift)).astype(BF)
    bias = as_row(joint)
    for i, part in enumerate((bias[:, :D], 0.0, bias[:, D:])):
        lanes = slice(i * D, (i + 1) * D)
        project_ref[:, lanes] = (nn(normed_ref[...], wj[:, lanes]) + part).astype(BF)
    for copy in copies[5:]:
        copy.wait()


def project_tokens(x, gain, shift, joint, wj, following):
    tokens = x.shape[0]
    mine = (x, gain, shift, joint, wj)
    return kernel_call(
        "project_tokens",
        project_kernel,
        [
            kept(tokens, 3 * D),
            kept(tokens, D),
            kept(tokens, D, dtype=F32),
            kept(tokens, 1, dtype=F32),
        ]
        + fetched(following),
        (),
        (),
        [(v.shape, v.dtype) for v in mine],
        cost(6 * tokens * D * D),
        far=mine + following,
        copies=5 + len(following),
    )


def turn_kernel(blocks, *refs):
    dp = lax.axis_index("dp")
    count = len(refs) // 2
    for source, target in zip(refs[:count], refs[count:]):
        store_permuted(target, source[...].T, dp, blocks)


def turn_tokens(blocks, *values):
    return kernel_call(
        "turn_tokens",
        functools.partial(turn_kernel, blocks),
        [kept(*v.shape[::-1]) for v in values],
        (),
        near(*values),
        (),
        cost(32 * values[0].shape[0] * D),
    )


def attend_kernel(*refs):
    more = (len(refs) - 5 - 3 - 1) // 2
    far, (place_ref, out_ref, x_ref, project_ref, wo_ref) = refs[:more], refs[more : more + 5]
    att_ref, context_ref, middle_ref = refs[more + 5 : more + 8]
    copies = fetch(far, refs[more + 8 : -1], refs[-1])
    line, _ = token_limits(place_ref)
    masks = head_masks()
    picks = caption_masks()
    lows = [pick.astype(F32).astype(BF) for pick in picks]
    key_place = iota((SEQ, GROUP), 0).astype(F32)

    def attend(h, carry):
        at = pl.multiple_of(h * 2 * HEAD, 128)
        for g in range(x_ref.shape[0] // GROUP):
            here = slice(g * GROUP, (g + 1) * GROUP)
            query = project_ref[here, pl.ds(at, 128)]
            keys = both_heads(project_ref[here, pl.ds(pl.multiple_of(D + at, 128), 128)], masks)
            values = both_heads(
                project_ref[here, pl.ds(pl.multiple_of(2 * D + at, 128), 128)], masks
            )
            scores = nt(keys, query)
            allowed = key_place <= line[:, here]
            parts = []
            for e in range(2):
                score = compact(scores[e * GROUP : (e + 1) * GROUP], picks) * scale
                score = jnp.where(allowed, score, negative)
                score = jnp.exp(score - jnp.max(score, axis=0, keepdims=True))
                weight = score / jnp.sum(score, axis=0, keepdims=True)
                att_ref[2 * h + e, :, here] = weight
                parts.append(expand(weight.astype(BF), lows))
            context_ref[here, pl.ds(at, 128)] = tn(jnp.concatenate(parts, axis=0), values).astype(BF)
        return carry

    lax.fori_loop(0, PAIRS, attend, 0, unroll=3)
    middle_ref[...] = x_ref[...].astype(F32) + (nn(context_ref[...], wo_ref[...]) + as_row(out_ref))
    for copy in copies:
        copy.wait()


def attend_tokens(place, out, x, project, wo, following):
    tokens = x.shape[0]
    return kernel_call(
        "attend_tokens",
        attend_kernel,
        [kept(HEADS, SEQ, tokens, dtype=F32), kept(tokens, D), kept(tokens, D, dtype=F32)]
        + fetched(following),
        (),
        near(place, out, x, project, wo),
        (),
        cost(4 * tokens * D * D),
        far=following,
        copies=len(following),
    )


def widen_kernel(blocks, *refs):
    more = (len(refs) - 9 - 8 - 3 - 1) // 2
    far = refs[:more]
    place_ref, gain_ref, shift_ref, wide_ref, narrow_ref, middle_ref, wu_ref, wn_ref, wm_ref = refs[
        more : more + 9
    ]
    second_ref, unit_ref, inverse_ref, upper_ref, box_ref, text_ref, scale_ref, embed_ref = refs[
        more + 9 : more + 17
    ]
    branch, wide, mean, semaphores = refs[-4:]
    copies = fetch(far, refs[more + 17 : -4], semaphores)
    captions = place_ref.shape[0]
    line, column = token_limits(place_ref)
    pool = pool_mask(line, captions)
    share = 1.0 / jnp.sum(pool, axis=1, keepdims=True)
    unit, inverse_ref[...] = norm_parts(middle_ref[...])
    unit_ref[...] = unit
    second_ref[...] = (unit * as_row(gain_ref) + as_row(shift_ref)).astype(BF)
    branch[...] = jnp.zeros_like(branch)
    wide[...] = as_row(wide_ref)
    pool_low = pool.astype(BF)
    step = 512

    def widen(i, carry):
        at = pl.multiple_of(i * step, 128)
        upper = nn(second_ref[...], wu_ref[:, pl.ds(at, step)]) + wide[:, pl.ds(at, step)]
        active = upper * (0.5 + 0.5 * jnp.tanh(upper * (BEND + CUBE * (upper * upper))))
        upper_ref[:, pl.ds(at, step)] = upper
        parts = two(nn(pool_low, active.astype(BF)) * share)
        mean[:, pl.ds(at, step)] = parts[:captions]
        branch[...] += nn(parts, wn_ref[pl.ds(at, step), :])
        return carry

    lax.fori_loop(0, FF // step, widen, 0, unroll=3)
    inside = jnp.where((iota((captions * SEQ, 1), 0) % SEQ).astype(F32) <= column, 1.0, 0.0)
    weight = inside / (column + 1.0)
    pooled = jnp.sum((middle_ref[...] * weight).reshape(captions, SEQ, D), axis=1)
    pooled = (pooled + (branch[:captions] + branch[captions:] + as_row(narrow_ref))).astype(BF)
    hidden, part = FF // blocks, D // blocks
    for b in range(blocks):
        box_ref[b, :, :hidden] = mean[:, b * hidden : (b + 1) * hidden]
        box_ref[b, :, hidden : hidden + part] = pooled[:, b * part : (b + 1) * part]
    text = nn(pooled, wm_ref[...])
    factor = lax.rsqrt(jnp.sum(text * text, axis=1, keepdims=True) + epsilon)
    text_ref[...] = text
    scale_ref[...] = factor
    embed_ref[...] = (text * factor).astype(BF)
    for copy in copies:
        copy.wait()


def slope_kernel(upper_ref, slope_ref):
    step = 512

    def part(i, carry):
        at = pl.multiple_of(i * step, 128)
        upper = upper_ref[:, pl.ds(at, step)]
        square = upper * upper
        half = 0.5 + 0.5 * jnp.tanh(upper * (BEND + CUBE * square))
        slope_ref[:, pl.ds(at, step)] = (
            half * (1.0 + (upper - upper * half) * (2.0 * BEND + 6.0 * CUBE * square))
        ).astype(BF)
        return carry

    lax.fori_loop(0, FF // step, part, 0)


def slope_tokens(upper):
    return kernel_call(
        "slope_tokens", slope_kernel, [kept(*upper.shape)], (), near(upper), (), cost(upper.size)
    )[0]


def widen_tokens(blocks, place, gain, shift, wide, narrow, middle, wu, wn, wm, following):
    tokens = middle.shape[0]
    captions = place.shape[0]
    return kernel_call(
        "widen_tokens",
        functools.partial(widen_kernel, blocks),
        [
            kept(tokens, D),
            kept(tokens, D, dtype=F32),
            kept(tokens, 1, dtype=F32),
            kept(tokens, FF, dtype=F32),
            kept(blocks, captions, box_width(blocks)),
            kept(captions, D, dtype=F32),
            kept(captions, 1, dtype=F32),
            kept(captions, D),
        ]
        + fetched(following),
        (),
        near(place, gain, shift, wide, narrow, middle, wu, wn, wm),
        [
            ((2 * captions, D), F32),
            ((1, FF), F32),
            ((captions, FF), BF),
        ],
        cost(2 * tokens * D * FF),
        far=following,
        copies=len(following),
    )


def match_of(paired, columns, images):
    column = iota((1, columns), 1)
    valid = column % SLOT < images
    name = jnp.where(valid, (column // SLOT) * images + column % SLOT, -1)
    return paired == name, valid


def contrast_kernel(
    images,
    parts,
    bits,
    heat_ref,
    own_ref,
    near_ref,
    wp_ref,
    embed_ref,
    paired_ref,
    weight_ref,
    picture_ref,
    score_ref,
    row_ref,
    inverse_ref,
    stats_ref,
    features,
):
    half = own_ref.shape[0] // SLOT
    for far, ref in enumerate((own_ref, near_ref)):

        def place(i, carry, far=far, ref=ref):
            p = i + far * half
            index = {axis: lax.axis_index(axis) for axis in ("dp", "rep")}
            for n, (axis, bit) in enumerate(bits):
                index[axis] = jnp.bitwise_xor(index[axis], ((p >> n) & 1) << bit)
            to = pl.ds(pl.multiple_of((index["dp"] * parts + index["rep"]) * SLOT, SLOT), SLOT)
            features[to, :] = ref[pl.ds(pl.multiple_of(i * SLOT, SLOT), SLOT), :]
            return carry

        lax.fori_loop(0, half, place, 0, unroll=4)
    picture = nn(features[...], wp_ref[...])
    picture = (
        picture * lax.rsqrt(jnp.sum(picture * picture, axis=1, keepdims=True) + epsilon)
    ).astype(BF)
    picture_ref[...] = picture
    score = nt(embed_ref[...], picture) / heat_ref[0]
    match, valid = match_of(as_column(paired_ref), score.shape[1], images)
    score = jnp.where(valid, score, negative)
    score_ref[...] = score
    top = jnp.max(score, axis=1, keepdims=True)
    row = jnp.log(jnp.sum(jnp.exp(score - top), axis=1, keepdims=True)) + top
    row_ref[...] = row
    positive = jnp.sum(jnp.where(match, score, 0.0), axis=1, keepdims=True)
    hits = jnp.where(match, 1.0, 0.0)
    counts = jnp.sum(hits, axis=0, keepdims=True)
    inverse = 1.0 / jnp.sum(hits * counts, axis=1, keepdims=True)
    inverse_ref[...] = inverse
    total = jnp.sum(as_column(weight_ref) * (row - positive - positive * inverse))
    best = jnp.max(score, axis=0, keepdims=True)
    mass = jnp.sum(jnp.exp(score - best), axis=0, keepdims=True)
    mass = jnp.where(iota(mass.shape, 1) == images, total, mass)
    wide = best.shape[1] // 4
    rows = [v[:, i * wide : (i + 1) * wide] for v in (best, mass) for i in range(4)]
    stats_ref[...] = jnp.concatenate(rows, axis=0)


def contrast(images, parts, bits, heat, own, far, wp, embed, paired, weight):
    captions = embed.shape[0]
    columns = 2 * own.shape[0]
    return kernel_call(
        "contrast",
        functools.partial(contrast_kernel, images, parts, bits),
        [
            kept(columns, D),
            kept(captions, columns, dtype=F32),
            kept(captions, 1, dtype=F32),
            kept(captions, 1, dtype=F32),
            shape(8, columns // 4),
        ],
        (heat,),
        near(own, far, wp, embed, paired, weight),
        [((columns, D), BF)],
        cost(2 * columns * D * D),
        max(LIMIT, columns * 8192),
    )


def merged(refs):
    best = functools.reduce(jnp.maximum, [ref[:4] for ref in refs])
    mass = sum(ref[4:] * jnp.exp(ref[:4] - best) for ref in refs)
    return best, mass


def merge_kernel(*refs):
    *given, out_ref = refs
    best, mass = merged(given)
    out_ref[...] = jnp.concatenate([best, mass], axis=0)


def merge(stats):
    return kernel_call("merge", merge_kernel, [shape(*stats[0].shape)], (), stats)[0]


def quarters(rep, away, flip=0):
    core = rep & 1
    out = []
    for xrel in range(2):
        for yrel in range(2):
            block = jnp.bitwise_xor(rep, 2 * xrel + away)
            x_first = 1 - core if away == flip else core
            out.append((jnp.where(x_first == 1, 2 * xrel + yrel, 2 * yrel + xrel), block, yrel))
    return out


def head_back_kernel(
    images,
    count_stats,
    rounds,
    heat_ref,
    place_ref,
    score_ref,
    row_ref,
    inverse_ref,
    weight_ref,
    paired_ref,
    picture_ref,
    text_ref,
    scale_ref,
    wm_ref,
    wn_ref,
    slope_ref,
    second_t_ref,
    box_ref,
    *refs,
):
    first = 1 << rounds[0]
    pieces = refs[len(refs) - first :]
    stats = refs[:count_stats]
    (
        back_ref,
        away_ref,
        here_ref,
        pooled_ref,
        loss_ref,
        down_bias_ref,
        up_bias_ref,
    ) = refs[count_stats : len(refs) - first]
    rep = lax.axis_index("rep")
    heat = heat_ref[0]
    captions = place_ref.shape[0]
    line, column = token_limits(place_ref)
    count = jnp.sum(pool_mask(line, captions), axis=1, keepdims=True)
    owner = spread_mask(column, captions).astype(BF)
    owner = jnp.concatenate([owner, owner], axis=1)

    score = score_ref[...]
    match, valid = match_of(as_column(paired_ref), score.shape[1], images)
    best, mass = merged(stats)
    column_log = jnp.log(mass) + best
    column_log = jnp.concatenate([column_log[i : i + 1] for i in range(4)], axis=1)
    loss_ref[...] = mass[:1, images : images + 1] + jnp.sum(
        jnp.where(valid, column_log, 0.0), axis=1, keepdims=True
    )
    weight = as_column(weight_ref)
    graded = (
        weight * jnp.exp(score - row_ref[...])
        + jnp.exp(score - column_log)
        - jnp.where(match, weight * (1.0 + inverse_ref[...]), 0.0)
    )
    graded = jnp.where(valid, graded / heat, 0.0).astype(BF)
    embed_back = nn(graded, picture_ref[...])
    text = text_ref[...]
    factor = scale_ref[...]
    text_dot = jnp.sum(text * embed_back, axis=1, keepdims=True)
    text_back = (factor * embed_back - text * (factor * factor * factor) * text_dot).astype(BF)
    blocks, _, wide = box_ref.shape
    masks = gather_masks(rounds, blocks)
    for c, piece_ref in enumerate(pieces):
        for i in range(blocks // first):
            block = jnp.bitwise_xor(lax.axis_index("dp"), masks[i * first + c])
            piece_ref[:, i * wide : (i + 1) * wide] = box_ref[block]
        piece_ref[:, (blocks // first) * wide :] = text_back
    pooled_back = nt(text_back, wm_ref[...])
    pooled_ref[...] = pooled_back
    branch = (pooled_back / count).astype(BF)
    down_bias_ref[...] = jnp.sum(branch.astype(F32) * count, axis=0, keepdims=True)
    ones = jnp.ones((SLOT, back_ref.shape[0]), BF)
    step = 512

    def widen(i, carry):
        at = pl.multiple_of(i * step, 128)
        part = nn(owner, two(nt(branch, wn_ref[pl.ds(at, step), :])))
        part = (part * slope_ref[:, pl.ds(at, step)].astype(F32)).astype(BF)
        back_ref[:, pl.ds(at, step)] = part
        up_bias_ref[:, pl.ds(at, step)] = nn(ones, part)[:1]
        return carry

    lax.fori_loop(0, FF // step, widen, 0, unroll=3)
    half = second_t_ref.shape[0] // 2
    wide = FF // 4
    for turn, target in enumerate((away_ref, here_ref)):
        for place, block, yrel in quarters(rep, 1 - turn):
            part = nn(
                second_t_ref[yrel * half : (yrel + 1) * half],
                back_ref[:, pl.ds(pl.multiple_of(block * wide, 128), wide)],
            )
            for h in range(2):
                target[place, h] = part[:, h * (wide // 2) : (h + 1) * (wide // 2)].astype(BF)


def head_back(images, rounds, heat, place, stats, score, row, inverse, weight, paired, picture, text,
              factor, wm, wn, slope, second_t, box):
    captions = text.shape[0]
    tokens = slope.shape[0]
    piece = (4, 2, D // 2, FF // 8)
    return kernel_call(
        "head_back",
        functools.partial(head_back_kernel, images, len(stats), rounds),
        [
            kept(tokens, FF),
            kept(*piece),
            kept(*piece),
            kept(captions, D, dtype=F32),
            shape(1, 1),
            shape(1, D),
            shape(1, FF),
        ]
        + [shape(captions, (box.shape[0] >> rounds[0]) * box.shape[2] + D, dtype=BF)] * (1 << rounds[0]),
        (heat,),
        (
            *near(place, score, row, inverse, weight, paired),
            *near(picture, text, factor, wm, wn, slope, second_t, box),
            *stats,
        ),
        (),
        cost(2 * tokens * D * FF),
    )


def middle_back_kernel(
    place_ref,
    gain_ref,
    pooled_ref,
    back_ref,
    wu_ref,
    unit_ref,
    inverse_ref,
    wo_ref,
    total_ref,
    attended_ref,
    context_back_ref,
    gain_back_ref,
    shift_back_ref,
    bias_ref,
):
    captions = place_ref.shape[0]
    line, column = token_limits(place_ref)
    count = jnp.sum(pool_mask(line, captions), axis=1, keepdims=True)
    owner = spread_mask(column, captions).astype(BF)
    owner = jnp.concatenate([owner, owner], axis=1)
    second_back = nt(back_ref[...], wu_ref[...])
    part, gain_back_ref[...], shift_back_ref[...] = norm_back(
        unit_ref[...], inverse_ref[...], as_row(gain_ref), second_back
    )
    total = nn(owner, two(pooled_ref[...] / count)) + part
    total_ref[...] = total
    attended = total.astype(BF)
    attended_ref[...] = attended
    bias_ref[...] = nn(jnp.ones((SLOT, attended.shape[0]), BF), attended)[:1]
    context_back_ref[...] = nt(attended, wo_ref[...]).astype(BF)


def middle_back(place, gain, pooled, back, wu, unit, inverse, wo):
    tokens = back.shape[0]
    return kernel_call(
        "middle_back",
        middle_back_kernel,
        [
            kept(tokens, D, dtype=F32),
            kept(tokens, D),
            kept(tokens, D),
            shape(1, D),
            shape(1, D),
            shape(1, D),
        ],
        (),
        near(place, gain, pooled, back, wu, unit, inverse, wo),
        (),
        cost(2 * tokens * D * (FF + D)),
    )


def attention_back_kernel(project_ref, att_ref, context_back_ref, back_ref, bias_ref):
    masks = head_masks()
    picks = caption_masks()
    lows = [pick.astype(F32).astype(BF) for pick in picks]
    low_scale = jnp.asarray(scale, BF)
    first = iota((GROUP, 2 * HEAD), 1) < HEAD
    tokens = project_ref.shape[0]

    def attend(h, carry):
        at = pl.multiple_of(h * 2 * HEAD, 128)
        at_k = pl.multiple_of(D + at, 128)
        at_v = pl.multiple_of(2 * D + at, 128)
        for g in range(tokens // GROUP):
            span = slice(g * GROUP, (g + 1) * GROUP)
            query = project_ref[span, pl.ds(at, 128)]
            keys = both_heads(project_ref[span, pl.ds(at_k, 128)], masks)
            values = both_heads(project_ref[span, pl.ds(at_v, 128)], masks)
            upper = context_back_ref[span, pl.ds(at, 128)]
            full = nt(values, upper)
            weights, grads = [], []
            for e in range(2):
                weight = att_ref[2 * h + e, :, span]
                part = compact(full[e * GROUP : (e + 1) * GROUP], picks)
                grad = weight * (part - jnp.sum(weight * part, axis=0, keepdims=True))
                weights.append(expand(weight.astype(BF), lows))
                grads.append(expand(grad.astype(BF) * low_scale, lows))
            weights = jnp.concatenate(weights, axis=0)
            grads = jnp.concatenate(grads, axis=0)
            back_ref[span, pl.ds(at, 128)] = tn(grads, keys).astype(BF)
            wide = nn(grads, query)
            back_ref[span, pl.ds(at_k, 128)] = jnp.where(first, wide[:GROUP], wide[GROUP:]).astype(
                BF
            )
            wide = nn(weights, upper)
            back_ref[span, pl.ds(at_v, 128)] = jnp.where(first, wide[:GROUP], wide[GROUP:]).astype(
                BF
            )
        return carry

    lax.fori_loop(0, PAIRS, attend, 0, unroll=3)
    ones = jnp.ones((SLOT, tokens), BF)
    for i in range(3):
        lanes = slice(i * D, (i + 1) * D)
        bias_ref[:, lanes] = nn(ones, back_ref[:, lanes])[:1]


def attention_back(project, att, context_back):
    tokens = project.shape[0]
    return kernel_call(
        "attention_back",
        attention_back_kernel,
        [kept(tokens, 3 * D), shape(1, 3 * D)],
        (),
        near(project, att, context_back),
        (),
        cost(3 * tokens * D * D),
    )


def left_columns_kernel(back_ref, normed_t_ref, away_ref, here_ref, chosen):
    rep = lax.axis_index("rep")
    joint = 3 * D // 4
    some = chosen.shape[2]
    for r in range(4):

        @pl.when(rep == r)
        def _():
            for i, k in enumerate((1, 3, 0, 2)):
                b = r ^ k
                chosen[i] = back_ref[:, b * joint : b * joint + some]

    half = D // 2
    for turn, target in enumerate((away_ref, here_ref)):
        for i, (place, _, yrel) in enumerate(quarters(rep, 1 - turn, 1)):
            lines = slice(yrel * half, (yrel + 1) * half)
            target[place] = nn(normed_t_ref[lines], chosen[2 * turn + i // 2]).astype(BF)


def right_columns_kernel(
    back_ref, attended_ref, normed_t_ref, context_t_ref, away_ref, here_ref, chosen
):
    rep = lax.axis_index("rep")
    joint = 3 * D // 4
    out = D // 4
    some = chosen.shape[2] - out
    for r in range(4):

        @pl.when(rep == r)
        def _():
            for i, k in enumerate((1, 3, 0, 2)):
                b = r ^ k
                chosen[i, :, :some] = back_ref[:, (b + 1) * joint - some : (b + 1) * joint]
                chosen[i, :, some:] = attended_ref[:, b * out : (b + 1) * out]

    half = D // 2
    for turn, target in enumerate((away_ref, here_ref)):
        for i, (place, _, yrel) in enumerate(quarters(rep, 1 - turn)):
            block = 2 * turn + i // 2
            lines = slice(yrel * half, (yrel + 1) * half)
            target[place, :, :some] = nn(normed_t_ref[lines], chosen[block, :, :some]).astype(BF)
            target[place, :, some:] = nn(context_t_ref[lines], chosen[block, :, some:]).astype(BF)


def columns_gradient(name, body, operands):
    tokens = operands[0].shape[0]
    piece = (4, D // 2, D // 2)
    return kernel_call(
        name,
        body,
        [kept(*piece), kept(*piece)],
        (),
        near(*operands),
        [((4, tokens, D // 2), BF)],
        cost(tokens * D * FF),
    )


def token_back_kernel(
    gain_ref,
    unit_ref,
    inverse_ref,
    middle_ref,
    back_ref,
    wj_ref,
    joint_ref,
    out_ref,
    gain2_ref,
    shift2_ref,
    wide_ref,
    narrow_ref,
    token_ref,
    sums_ref,
):
    part, gain1, shift1 = norm_back(
        unit_ref[...], inverse_ref[...], as_row(gain_ref), nt(back_ref[...], wj_ref[...])
    )
    token_ref[...] = middle_ref[...] + part
    line = 0
    rest = (joint_ref, out_ref, gain2_ref, shift2_ref, wide_ref, narrow_ref)
    for value in [gain1, shift1] + [ref[...] for ref in rest]:
        for i in range(value.shape[1] // 128):
            sums_ref[line : line + 1] = value[:, i * 128 : (i + 1) * 128]
            line += 1
    sums_ref[line:] = jnp.zeros((sums_ref.shape[0] - line, 128), F32)


def token_back(gain, unit, inverse, middle, back, wj, sums):
    return kernel_call(
        "token_back",
        token_back_kernel,
        [shape(unit.shape[0], D), shape(ALL_LINES, 128)],
        (),
        (gain, *near(unit, inverse, middle, back, wj), *sums),
        (),
        cost(6 * unit.shape[0] * D * D),
    )


def low_rank_kernel(
    hidden, own_ref, near_ref, wm_ref, down_ref, head_ref, other_ref, box, back
):
    rows = own_ref.shape[0]
    box[:rows] = own_ref[...]
    box[rows:] = near_ref[...]
    part = down_ref.shape[0]
    start = box.shape[1] - D
    rep = lax.axis_index("rep")
    for r in range(D // part):

        @pl.when(rep == r)
        def _():
            for i, b in enumerate((r, r ^ 2)):
                back[i] = box[:, start + b * part : start + (b + 1) * part]

    wide = head_ref.shape[1]
    for i in range(2):
        block = jnp.bitwise_xor(rep, 2 * i)
        here = wm_ref[pl.ds(pl.multiple_of(block * part, SLOT), part), :]
        pooled = nt(box[:, start:], here).astype(BF)
        down = tn(pooled, box[:, :hidden])
        head = tn(back[i], box[:, hidden : hidden + wide])
        if i == 0:
            down_ref[...] = down
            head_ref[...] = head
        else:
            other_ref[:, :hidden] = down.astype(BF)
            other_ref[:, hidden:] = head.astype(BF)


def low_rank(blocks, parts, own, far, wm):
    rows = 2 * own.shape[0]
    hidden, wide, part = FF // blocks, D // blocks, D // parts
    return kernel_call(
        "low_rank",
        functools.partial(low_rank_kernel, hidden),
        [shape(part, hidden), shape(part, wide), shape(part, hidden + wide, dtype=BF)],
        (),
        near(own, far, wm),
        [((rows, own.shape[1]), BF), ((2, rows, part), BF)],
        cost(2 * rows * D * D),
    )


def finish_kernel(groups, *refs):
    up, first, second, lines = (
        [refs[sum(groups[:i]) + n] for n in range(groups[i])] for i in range(4)
    )
    loss_ref, down_ref, head_ref, other_ref = refs[sum(groups) : sum(groups) + 4]
    (
        joint_ref,
        out_ref,
        up_block_ref,
        down_block_ref,
        head_block_ref,
        loss_out_ref,
        *vector_refs,
    ) = refs[sum(groups) + 4 :]

    def total(terms):
        return sum(ref[...].astype(F32) for ref in terms)

    up_sum = total(up)
    for h in range(2):
        lanes = slice(h * up_sum.shape[2], (h + 1) * up_sum.shape[2])
        up_block_ref[:, lanes] = up_sum[h]
    one, two_ = total(first), total(second)
    some = one.shape[1]
    rest = joint_ref.shape[1] - some
    joint_ref[:, :some] = one
    joint_ref[:, some:] = two_[:, :rest]
    out_ref[...] = two_[:, rest:]
    hidden = down_ref.shape[1]
    down_block_ref[...] = down_ref[...] + other_ref[:, :hidden].astype(F32)
    head_block_ref[...] = (head_ref[...] + other_ref[:, hidden:].astype(F32)).T
    loss_out_ref[...] = loss_ref[...].reshape(1)
    vectors = total(lines)
    starts = (GAIN1, SHIFT1, JOINT, OUT, GAIN2, SHIFT2, WIDE, NARROW)
    for start, ref in zip(starts, vector_refs):
        for i in range(ref.shape[0] // 128):
            line = start // 128 + i
            if start == JOINT and i >= D // 128:
                line += D // 128
            ref[pl.ds(i * 128, 128)] = vectors[line]


def finish(up, first, second, vectors, loss, low, joint):
    rows = up[0].shape[1]
    sizes = (D, D, 2 * D, D, D, D, FF, D)
    return kernel_call(
        "finish",
        functools.partial(finish_kernel, [len(v) for v in (up, first, second, vectors)]),
        [
            shape(rows, joint),
            shape(rows, D - joint),
            shape(rows, D),
            shape(*low[0].shape),
            shape(*low[1].shape[::-1]),
            shape(1),
        ]
        + [shape(n) for n in sizes],
        (),
        (*up, *first, *second, *vectors, loss, *low),
    )


def both_pairs(partner):
    dp, rep = lax.axis_size("dp"), lax.axis_size("rep")
    pairs = []
    for i in range(dp):
        for j in range(rep):
            a, b = partner(i, j)
            pairs.append((i * rep + j, a * rep + b))
    return pairs


def exchange(value, partner):
    return lax.ppermute(value, ("dp", "rep"), both_pairs(partner))


def first_turn(i, j):
    return (i, j ^ 2) if j & 1 == 0 else (i ^ 1, j)


def second_turn(i, j):
    return (i ^ 1, j) if j & 1 == 0 else (i, j ^ 2)


def added(a, b):
    return (a.astype(F32) + b.astype(F32)).astype(BF)


def halved(here, got):
    half = here.shape[0] // 2
    return added(here[:half], got[:half]), added(here[half:], got[half:])


def parted(here, got, count):
    rows = here.shape[-2] // count
    parts = [slice(i * rows, (i + 1) * rows) for i in range(count)]
    return [added(here[..., p, :], got[..., p, :]) for p in parts]


def core_turn(i, j):
    return i, j ^ 1


def across(i, j):
    return i, j ^ 2


def group_round(keep, got, group):
    masks = group_masks(group)
    bits = len(group)
    parts = parted(keep, got, len(masks))
    place = [sum(((c >> n) & 1) << (bits - 1 - n) for n in range(bits)) for c in range(len(masks))]
    return [parts[0]] + [
        exchange(parts[place[c]], lambda i, j: (i ^ masks[c][0], j)) for c in range(1, len(masks))
    ]


def row_rounds(keep, got, groups):
    terms = [keep, got]
    for group in groups:
        if len(terms) > 2:
            terms = [terms[0], sum(v.astype(F32) for v in terms[1:])]
        terms = group_round(*terms, group)
    return terms


order = lax.optimization_barrier


def dp_groups():
    bits = [("dp", b) for b in range(1, lax.axis_size("dp").bit_length() - 1)]
    return [bits[i : i + 2] for i in range(0, len(bits), 2)] + [[("dp", 0)]]


def all_groups():
    bits = [("rep", b) for b in range(1, lax.axis_size("rep").bit_length() - 1)]
    groups = dp_groups()
    return groups[:-1] + [groups[-1] + bits, [("rep", 0)]]


def group_masks(group):
    out = [(0, 0)]
    for axis, bit in group:
        out += [(a | 1 << bit, b) if axis == "dp" else (a, b | 1 << bit) for a, b in out]
    return out


def gather_masks(rounds, blocks):
    bits = [0] + list(range(blocks.bit_length() - 2, 0, -1))
    masks, used = [0], 0
    for count in rounds:
        for bit in bits[used : used + count]:
            masks = masks + [m | 1 << bit for m in masks]
        used += count
    return masks


def split_round(value, wide, group):
    blocks = (value.shape[1] - D) // wide
    turns = group_masks(group)
    text = value[:, blocks * wide :]
    pieces = []
    for c, (a, b) in enumerate(turns):
        chosen = [value[:, i * wide : (i + 1) * wide] for i in range(c, blocks, len(turns))]
        piece = jnp.concatenate(chosen + [text], axis=1)
        pieces.append(piece if c == 0 else exchange(piece, lambda i, j: (i ^ a, j ^ b)))
    return pieces


def round_of(value, group):
    return [value] + [
        exchange(value, lambda i, j: (i ^ a, j ^ b)) for a, b in group_masks(group)[1:]
    ]


def relative_rows(value, blocks):
    rows = value.shape[0] // blocks
    if rows % SLOT == 0:
        return value
    bits = blocks.bit_length() - 1
    place = jnp.arange(blocks, dtype=jnp.int32)
    source = jnp.zeros_like(place)
    for bit in range(bits):
        source = source + ((place >> (bits - 1 - bit)) & 1) * (1 << bit)
    source = source ^ lax.axis_index("dp")
    return value.reshape(blocks, rows, -1)[source].reshape(value.shape)


def local(
    incoming_activations,
    caption_final_place,
    paired_picture,
    caption_weight,
    locked_picture_features,
    softmax_heat,
    premix_scaling_factor,
    premix_shift_term,
    stacked_mixing_matrix,
    asking_reading_offsets,
    mixing_result_matrix,
    mixing_result_offset,
    premlp_scaling_factor,
    premlp_shift_term,
    widening_matrix,
    widening_offset,
    narrowing_matrix,
    narrowing_offset,
    caption_mapping_matrix,
    picture_mapping_matrix,
):
    both = ("dp", "rep")
    devices = lax.axis_size(both)
    blocks = lax.axis_size("dp")
    parts = lax.axis_size("rep")
    captions = caption_final_place.shape[0]
    images = locked_picture_features.shape[0]
    groups = all_groups()
    pieces = round_of(jnp.pad(locked_picture_features, ((0, SLOT - images), (0, 0))), groups[0])
    project, normed, unit1, inverse1, place, out, x, wo = project_tokens(
        incoming_activations,
        premix_scaling_factor,
        premix_shift_term,
        asking_reading_offsets,
        stacked_mixing_matrix,
        (
            caption_final_place,
            mixing_result_offset,
            incoming_activations,
            mixing_result_matrix,
        ),
    )
    project, pieces = order((project, pieces))
    for group in groups[1:-1]:
        pieces = round_of(jnp.concatenate(pieces), group)
    att, context, middle, gain2, shift2, wide, narrow, wu, wn, wm = attend_tokens(
        place,
        out,
        x,
        project,
        wo,
        (
            premlp_scaling_factor,
            premlp_shift_term,
            widening_offset,
            narrowing_offset,
            widening_matrix,
            narrowing_matrix,
            caption_mapping_matrix,
        ),
    )
    middle, pieces = order((middle, pieces))
    own, far = round_of(jnp.concatenate(pieces), groups[-1])
    second, unit2, inverse2, upper, box, text, factor, embed, wp, paired, weight = widen_tokens(
        blocks,
        place,
        gain2,
        shift2,
        wide,
        narrow,
        middle,
        wu,
        wn,
        wm,
        (picture_mapping_matrix, paired_picture, caption_weight),
    )
    embed, far = order((embed, far))
    picture, score, row, inverse, stats = contrast(
        images,
        parts,
        sum(groups, []),
        softmax_heat,
        own,
        far,
        wp,
        embed,
        paired,
        weight,
    )
    groups = dp_groups()
    high = [[bit] for group in groups[:-1] for bit in group]
    factor_groups = groups[-1:] + high[::-1]
    stats = round_of(stats, [("rep", 0)])
    normed_t, context_t, second_t = (
        relative_rows(v, blocks) for v in turn_tokens(blocks, normed, context, second)
    )
    stats = round_of(merge(stats), [("rep", 1)] + groups[-1])
    slope = slope_tokens(upper)
    stats, slope = order((stats, slope))
    for group in groups[:-1]:
        stats = round_of(merge(stats), group)
    back, away, here, pooled_back, loss, down_bias, up_bias, *pieces = head_back(
        images,
        [len(group) for group in factor_groups],
        softmax_heat,
        place,
        stats,
        score,
        row,
        inverse,
        weight,
        paired,
        picture,
        text,
        factor,
        wm,
        wn,
        slope,
        second_t,
        box,
    )
    loss = loss / (captions * devices)
    got = exchange(away, core_turn)
    pieces = pieces[:1] + [
        exchange(piece, lambda i, j: (i ^ a, j ^ b))
        for piece, (a, b) in zip(pieces[1:], group_masks(factor_groups[0])[1:])
    ]
    total, attended, context_back, gain2, shift2, out_bias = middle_back(
        place,
        gain2,
        pooled_back,
        back,
        wu,
        unit2,
        inverse2,
        wo,
    )
    context_back, got, pieces = order((context_back, got, pieces))
    up, send = halved(here, got)
    got_up = exchange(send, first_turn)
    pieces = split_round(jnp.concatenate(pieces), box.shape[2], factor_groups[1])
    project_back, joint_bias = attention_back(project, att, context_back)
    project_back, pieces = order((project_back, pieces))
    for group in factor_groups[2:]:
        pieces = split_round(jnp.concatenate(pieces), box.shape[2], group)
    away, here = columns_gradient("left_columns", left_columns_kernel, (project_back, normed_t))
    got = exchange(away, core_turn)
    project_back, away = order((project_back, away))
    away, here2 = columns_gradient(
        "right_columns", right_columns_kernel, (project_back, attended, normed_t, context_t)
    )
    project_back, away, got, got_up = order((project_back, away, got, got_up))
    up, up_send = halved(up, got_up)
    first, send = halved(here, got)
    got = exchange(jnp.concatenate([up_send[0], send]), second_turn)
    got2 = exchange(away, core_turn)
    joint = 3 * D // parts
    token, sums = token_back(
        premix_scaling_factor,
        unit1,
        inverse1,
        total,
        project_back,
        stacked_mixing_matrix,
        (joint_bias, out_bias, gain2, shift2, up_bias, down_bias),
    )
    sums, got2, pieces = order((sums, got2, pieces))
    factors = jnp.concatenate(pieces)
    far = exchange(factors, core_turn)
    lines = round_of(sums, [("rep", 0)])
    lines = round_of(sum(lines), [("rep", 1)])
    second, send2 = halved(here2, got2)
    got, send2, lines, far = order((got, send2, lines, far))
    up, got_up = group_round(up[0], got[:2], high[0])
    first, send = halved(first, got[2:])
    got2 = exchange(jnp.concatenate([send2, send]), first_turn)
    lines = round_of(sum(lines), groups[-1])
    *low, other = low_rank(blocks, parts, factors, far, wm)
    got_up, lines, other = order((got_up, lines, other))
    for group in high[1:]:
        up, got_up = group_round(up, got_up, group)
    lines = round_of(sum(lines), high[0])
    got2, got_up, lines, other = order((got2, got_up, lines, other))
    second, send = halved(second, got2[:2])
    second, first, got = second[0], first[0], got2[2]
    got2 = exchange(send[0], second_turn)
    first, got = group_round(first, got, high[0])
    for group in high[1:]:
        lines = round_of(sum(lines), group)
    other = exchange(other, across)
    for i, group in enumerate(high):
        second, got2 = group_round(second, got2, group)
        if i + 1 < len(high):
            got, second, lines = order((got, second, lines))
            first, got = group_round(first, got, high[i + 1])
    first, second, up, vectors = [first, got], [second, got2], [up, got_up], lines
    joint_block, out_block, up_block, down_block, head_block, loss, *grads = finish(
        up, first, second, vectors, loss, (*low, other), joint
    )
    return (
        loss,
        token,
        grads[0],
        grads[1],
        joint_block,
        grads[2],
        out_block,
        grads[3],
        grads[4],
        grads[5],
        up_block,
        grads[6],
        down_block.T,
        grads[7],
        head_block,
    )


def solution(mesh):
    spread = P(("dp", "rep"), None)
    line = P(("dp", "rep"))
    block = P("dp", "rep")
    in_specs = (spread, line, line, line, spread) + (P(),) * 15
    out_specs = (
        P(),
        spread,
        P(),
        P(),
        block,
        P(),
        block,
        P(),
        P(),
        P(),
        block,
        P(),
        block,
        P(),
        block,
    )
    return jax.shard_map(local, mesh=mesh, in_specs=in_specs, out_specs=out_specs, check_vma=False)
```

```python
import functools

import jax
import jax.numpy as jnp
from jax import lax
from jax.experimental import pallas as pl
from jax.experimental.pallas import tpu as pltpu
from jax.sharding import PartitionSpec as P

D = 768
HEADS = 12
HEAD = 64
SEQ = 16
FF = 3072
GROUP = 128
PAIRS = HEADS // 2
SLOT = 16
BF = jnp.bfloat16
F32 = jnp.float32

epsilon = 1e-06
BEND = 0.7978845608028654
CUBE = BEND * 0.044715
negative = -1e30
scale = HEAD ** (-0.5)
LIMIT = 20 * 1024 * 1024

GAIN1, SHIFT1, JOINT, OUT, GAIN2, SHIFT2, WIDE, NARROW = 0, 768, 1536, 3840, 4608, 5376, 6144, 9216
VECTORS = 9984
LINES = VECTORS // 128
ALL_LINES = LINES + -LINES % 8

vmem = pl.BlockSpec(memory_space=pltpu.VMEM)
hbm = pl.BlockSpec(memory_space=pltpu.HBM)
smem = pl.BlockSpec(memory_space=pltpu.SMEM)


def dot(a, b, dims):
    return lax.dot_general(a, b, (dims, ((), ())), preferred_element_type=F32)


def nn(a, b):
    return dot(a, b, ((1,), (0,)))


def nt(a, b):
    return dot(a, b, ((1,), (1,)))


def tn(a, b):
    return dot(a, b, ((0,), (0,)))


def cost(flops):
    return pl.CostEstimate(flops=flops, transcendentals=0, bytes_accessed=0)


def shape(*dims, dtype=F32):
    return jax.ShapeDtypeStruct(dims, dtype)


def kept(*dims, dtype=BF):
    return pltpu.VMEM(dims, dtype)


def near(*values):
    return [pltpu.with_memory_space_constraint(v, pltpu.VMEM) for v in values]


def kernel_call(
    name, body, results, small, operands, scratch=(), estimate=None, limit=LIMIT, far=(), copies=0
):
    semaphores = [pltpu.SemaphoreType.DMA((copies,))] if copies else []
    return pl.pallas_call(
        body,
        out_shape=results,
        in_specs=[smem] * len(small) + [hbm] * len(far) + [vmem] * len(operands),
        out_specs=[vmem] * len(results),
        scratch_shapes=[pltpu.VMEM(s, t) for s, t in scratch] + semaphores,
        compiler_params=pltpu.CompilerParams(vmem_limit_bytes=limit),
        cost_estimate=estimate,
        name=name,
    )(*small, *[pltpu.with_memory_space_constraint(v, pltpu.HBM) for v in far], *operands)


def fetched(values):
    return [kept(*v.shape, dtype=v.dtype) for v in values]


def fetch(sources, targets, semaphores):
    copies = [
        pltpu.make_async_copy(source, target, semaphores.at[i])
        for i, (source, target) in enumerate(zip(sources, targets))
    ]
    for copy in copies:
        copy.start()
    return copies


def iota(dims, axis):
    return lax.broadcasted_iota(jnp.int32, dims, axis)


def norm_parts(values):
    average = jnp.mean(values, axis=-1, keepdims=True)
    centred = values - average
    inverse = lax.rsqrt(jnp.mean(centred * centred, axis=-1, keepdims=True) + epsilon)
    return centred * inverse, inverse


def norm_back(unit, inverse, gain, back):
    inner = back * gain
    part = inverse * (
        inner
        - jnp.mean(inner, axis=-1, keepdims=True)
        - unit * jnp.mean(inner * unit, axis=-1, keepdims=True)
    )
    return part, jnp.sum(back * unit, axis=0, keepdims=True), jnp.sum(back, axis=0, keepdims=True)


def split(value):
    high = value.astype(BF)
    return high, (value - high.astype(F32)).astype(BF)


def two(value):
    return jnp.concatenate(split(value), axis=0)


def as_row(ref):
    return ref[...].reshape(1, ref.shape[0])


def as_column(ref):
    size = ref.shape[0]
    same = iota((size, size), 0) == iota((size, size), 1)
    row = as_row(ref)
    return jnp.sum(jnp.where(same, row, jnp.zeros_like(row)), axis=1, keepdims=True)


def token_limits(ref):
    place = as_row(ref).astype(F32)
    captions = place.shape[1]
    tokens = captions * SEQ
    owner = (iota((tokens, captions), 0) // SEQ == iota((tokens, captions), 1)).astype(F32)
    column = jnp.sum(owner * place, axis=1, keepdims=True)
    line = nt(place.astype(BF), owner.astype(BF))
    return line, column


def pool_mask(line, captions):
    dims = (captions, captions * SEQ)
    token = iota(dims, 1)
    inside = (token % SEQ).astype(F32) <= line
    return jnp.where((token // SEQ == iota(dims, 0)) & inside, 1.0, 0.0)


def spread_mask(column, captions):
    dims = (captions * SEQ, captions)
    token = iota(dims, 0)
    inside = (token % SEQ).astype(F32) <= column
    return jnp.where((token // SEQ == iota(dims, 1)) & inside, 1.0, 0.0)


def head_masks():
    lane = iota((1, 2 * HEAD), 1)
    even = (lane < HEAD).astype(F32)
    return even.astype(BF), (1.0 - even).astype(BF)


def caption_masks():
    lane = iota((SEQ, GROUP), 1) // SEQ
    return [lane == c for c in range(GROUP // SEQ)]


def compact(full, picks):
    out = full[:SEQ]
    for c in range(1, len(picks)):
        out = jnp.where(picks[c], full[c * SEQ : (c + 1) * SEQ], out)
    return out


def expand(low, lows):
    return jnp.concatenate([low * mask for mask in lows], axis=0)


def both_heads(value, masks):
    return jnp.concatenate([value * masks[0], value * masks[1]], axis=0)


def store_permuted(ref, value, dp, blocks):
    rows = value.shape[0] // blocks
    bits = blocks.bit_length() - 1
    if rows % SLOT:
        ref[...] = value
        return
    for b in range(blocks):
        k = jnp.bitwise_xor(dp, b)
        place = 0
        for bit in range(bits):
            place = place + ((k >> bit) & 1) * (1 << (bits - 1 - bit))
        ref[pl.ds(pl.multiple_of(place * rows, SLOT), rows), :] = value[b * rows : (b + 1) * rows]


def box_width(blocks):
    used = (FF + D) // blocks
    return used + -used % 128


def project_kernel(*refs):
    more = (len(refs) - 5 - 4 - 5 - 1) // 2
    mine, other, refs = refs[:5], refs[5 : 5 + more], refs[5 + more :]
    project_ref, normed_ref, unit_ref, inverse_ref = refs[:4]
    targets, (x, gain, shift, joint, wj, semaphores) = refs[4 : 4 + more], refs[4 + more :]
    copies = fetch(mine + other, (x, gain, shift, joint, wj) + targets, semaphores)
    copies[0].wait()
    unit_ref[...], inverse_ref[...] = norm_parts(x[...].astype(F32))
    for copy in copies[1:5]:
        copy.wait()
    normed_ref[...] = (unit_ref[...] * as_row(gain) + as_row(shift)).astype(BF)
    bias = as_row(joint)
    for i, part in enumerate((bias[:, :D], 0.0, bias[:, D:])):
        lanes = slice(i * D, (i + 1) * D)
        project_ref[:, lanes] = (nn(normed_ref[...], wj[:, lanes]) + part).astype(BF)
    for copy in copies[5:]:
        copy.wait()


def project_tokens(x, gain, shift, joint, wj, following):
    tokens = x.shape[0]
    mine = (x, gain, shift, joint, wj)
    return kernel_call(
        "project_tokens",
        project_kernel,
        [
            kept(tokens, 3 * D),
            kept(tokens, D),
            kept(tokens, D, dtype=F32),
            kept(tokens, 1, dtype=F32),
        ]
        + fetched(following),
        (),
        (),
        [(v.shape, v.dtype) for v in mine],
        cost(6 * tokens * D * D),
        far=mine + following,
        copies=5 + len(following),
    )


def turn_kernel(blocks, *refs):
    dp = lax.axis_index("dp")
    count = len(refs) // 2
    for source, target in zip(refs[:count], refs[count:]):
        store_permuted(target, source[...].T, dp, blocks)


def turn_tokens(blocks, *values):
    return kernel_call(
        "turn_tokens",
        functools.partial(turn_kernel, blocks),
        [kept(*v.shape[::-1]) for v in values],
        (),
        near(*values),
        (),
        cost(32 * values[0].shape[0] * D),
    )


def attend_kernel(*refs):
    more = (len(refs) - 5 - 3 - 1) // 2
    far, (place_ref, out_ref, x_ref, project_ref, wo_ref) = refs[:more], refs[more : more + 5]
    att_ref, context_ref, middle_ref = refs[more + 5 : more + 8]
    copies = fetch(far, refs[more + 8 : -1], refs[-1])
    line, _ = token_limits(place_ref)
    masks = head_masks()
    picks = caption_masks()
    lows = [pick.astype(F32).astype(BF) for pick in picks]
    key_place = iota((SEQ, GROUP), 0).astype(F32)

    def attend(h, carry):
        at = pl.multiple_of(h * 2 * HEAD, 128)
        for g in range(x_ref.shape[0] // GROUP):
            here = slice(g * GROUP, (g + 1) * GROUP)
            query = project_ref[here, pl.ds(at, 128)]
            keys = both_heads(project_ref[here, pl.ds(pl.multiple_of(D + at, 128), 128)], masks)
            values = both_heads(
                project_ref[here, pl.ds(pl.multiple_of(2 * D + at, 128), 128)], masks
            )
            scores = nt(keys, query)
            allowed = key_place <= line[:, here]
            parts = []
            for e in range(2):
                score = compact(scores[e * GROUP : (e + 1) * GROUP], picks) * scale
                score = jnp.where(allowed, score, negative)
                score = jnp.exp(score - jnp.max(score, axis=0, keepdims=True))
                weight = score / jnp.sum(score, axis=0, keepdims=True)
                att_ref[2 * h + e, :, here] = weight
                parts.append(expand(weight.astype(BF), lows))
            context_ref[here, pl.ds(at, 128)] = tn(jnp.concatenate(parts, axis=0), values).astype(BF)
        return carry

    lax.fori_loop(0, PAIRS, attend, 0, unroll=3)
    middle_ref[...] = x_ref[...].astype(F32) + (nn(context_ref[...], wo_ref[...]) + as_row(out_ref))
    for copy in copies:
        copy.wait()


def attend_tokens(place, out, x, project, wo, following):
    tokens = x.shape[0]
    return kernel_call(
        "attend_tokens",
        attend_kernel,
        [kept(HEADS, SEQ, tokens, dtype=F32), kept(tokens, D), kept(tokens, D, dtype=F32)]
        + fetched(following),
        (),
        near(place, out, x, project, wo),
        (),
        cost(4 * tokens * D * D),
        far=following,
        copies=len(following),
    )


def widen_kernel(blocks, *refs):
    more = (len(refs) - 9 - 8 - 3 - 1) // 2
    far = refs[:more]
    place_ref, gain_ref, shift_ref, wide_ref, narrow_ref, middle_ref, wu_ref, wn_ref, wm_ref = refs[
        more : more + 9
    ]
    second_ref, unit_ref, inverse_ref, upper_ref, box_ref, text_ref, scale_ref, embed_ref = refs[
        more + 9 : more + 17
    ]
    branch, wide, mean, semaphores = refs[-4:]
    copies = fetch(far, refs[more + 17 : -4], semaphores)
    captions = place_ref.shape[0]
    line, column = token_limits(place_ref)
    pool = pool_mask(line, captions)
    share = 1.0 / jnp.sum(pool, axis=1, keepdims=True)
    unit, inverse_ref[...] = norm_parts(middle_ref[...])
    unit_ref[...] = unit
    second_ref[...] = (unit * as_row(gain_ref) + as_row(shift_ref)).astype(BF)
    branch[...] = jnp.zeros_like(branch)
    wide[...] = as_row(wide_ref)
    pool_low = pool.astype(BF)
    step = 512

    def widen(i, carry):
        at = pl.multiple_of(i * step, 128)
        upper = nn(second_ref[...], wu_ref[:, pl.ds(at, step)]) + wide[:, pl.ds(at, step)]
        active = upper * (0.5 + 0.5 * jnp.tanh(upper * (BEND + CUBE * (upper * upper))))
        upper_ref[:, pl.ds(at, step)] = upper
        parts = two(nn(pool_low, active.astype(BF)) * share)
        mean[:, pl.ds(at, step)] = parts[:captions]
        branch[...] += nn(parts, wn_ref[pl.ds(at, step), :])
        return carry

    lax.fori_loop(0, FF // step, widen, 0, unroll=3)
    inside = jnp.where((iota((captions * SEQ, 1), 0) % SEQ).astype(F32) <= column, 1.0, 0.0)
    weight = inside / (column + 1.0)
    pooled = jnp.sum((middle_ref[...] * weight).reshape(captions, SEQ, D), axis=1)
    pooled = (pooled + (branch[:captions] + branch[captions:] + as_row(narrow_ref))).astype(BF)
    hidden, part = FF // blocks, D // blocks
    for b in range(blocks):
        box_ref[b, :, :hidden] = mean[:, b * hidden : (b + 1) * hidden]
        box_ref[b, :, hidden : hidden + part] = pooled[:, b * part : (b + 1) * part]
    text = nn(pooled, wm_ref[...])
    factor = lax.rsqrt(jnp.sum(text * text, axis=1, keepdims=True) + epsilon)
    text_ref[...] = text
    scale_ref[...] = factor
    embed_ref[...] = (text * factor).astype(BF)
    for copy in copies:
        copy.wait()


def slope_kernel(upper_ref, slope_ref):
    step = 512

    def part(i, carry):
        at = pl.multiple_of(i * step, 128)
        upper = upper_ref[:, pl.ds(at, step)]
        square = upper * upper
        half = 0.5 + 0.5 * jnp.tanh(upper * (BEND + CUBE * square))
        slope_ref[:, pl.ds(at, step)] = (
            half * (1.0 + (upper - upper * half) * (2.0 * BEND + 6.0 * CUBE * square))
        ).astype(BF)
        return carry

    lax.fori_loop(0, FF // step, part, 0)


def slope_tokens(upper):
    return kernel_call(
        "slope_tokens", slope_kernel, [kept(*upper.shape)], (), near(upper), (), cost(upper.size)
    )[0]


def widen_tokens(blocks, place, gain, shift, wide, narrow, middle, wu, wn, wm, following):
    tokens = middle.shape[0]
    captions = place.shape[0]
    return kernel_call(
        "widen_tokens",
        functools.partial(widen_kernel, blocks),
        [
            kept(tokens, D),
            kept(tokens, D, dtype=F32),
            kept(tokens, 1, dtype=F32),
            kept(tokens, FF, dtype=F32),
            kept(blocks, captions, box_width(blocks)),
            kept(captions, D, dtype=F32),
            kept(captions, 1, dtype=F32),
            kept(captions, D),
        ]
        + fetched(following),
        (),
        near(place, gain, shift, wide, narrow, middle, wu, wn, wm),
        [
            ((2 * captions, D), F32),
            ((1, FF), F32),
            ((captions, FF), BF),
        ],
        cost(2 * tokens * D * FF),
        far=following,
        copies=len(following),
    )


def match_of(paired, columns, images):
    column = iota((1, columns), 1)
    valid = column % SLOT < images
    name = jnp.where(valid, (column // SLOT) * images + column % SLOT, -1)
    return paired == name, valid


def contrast_kernel(
    images,
    parts,
    bits,
    heat_ref,
    own_ref,
    near_ref,
    wp_ref,
    embed_ref,
    paired_ref,
    weight_ref,
    picture_ref,
    score_ref,
    row_ref,
    inverse_ref,
    stats_ref,
    features,
):
    half = own_ref.shape[0] // SLOT
    for far, ref in enumerate((own_ref, near_ref)):

        def place(i, carry, far=far, ref=ref):
            p = i + far * half
            index = {axis: lax.axis_index(axis) for axis in ("dp", "rep")}
            for n, (axis, bit) in enumerate(bits):
                index[axis] = jnp.bitwise_xor(index[axis], ((p >> n) & 1) << bit)
            to = pl.ds(pl.multiple_of((index["dp"] * parts + index["rep"]) * SLOT, SLOT), SLOT)
            features[to, :] = ref[pl.ds(pl.multiple_of(i * SLOT, SLOT), SLOT), :]
            return carry

        lax.fori_loop(0, half, place, 0, unroll=4)
    picture = nn(features[...], wp_ref[...])
    picture = (
        picture * lax.rsqrt(jnp.sum(picture * picture, axis=1, keepdims=True) + epsilon)
    ).astype(BF)
    picture_ref[...] = picture
    score = nt(embed_ref[...], picture) / heat_ref[0]
    match, valid = match_of(as_column(paired_ref), score.shape[1], images)
    score = jnp.where(valid, score, negative)
    score_ref[...] = score
    top = jnp.max(score, axis=1, keepdims=True)
    row = jnp.log(jnp.sum(jnp.exp(score - top), axis=1, keepdims=True)) + top
    row_ref[...] = row
    positive = jnp.sum(jnp.where(match, score, 0.0), axis=1, keepdims=True)
    hits = jnp.where(match, 1.0, 0.0)
    counts = jnp.sum(hits, axis=0, keepdims=True)
    inverse = 1.0 / jnp.sum(hits * counts, axis=1, keepdims=True)
    inverse_ref[...] = inverse
    total = jnp.sum(as_column(weight_ref) * (row - positive - positive * inverse))
    best = jnp.max(score, axis=0, keepdims=True)
    mass = jnp.sum(jnp.exp(score - best), axis=0, keepdims=True)
    mass = jnp.where(iota(mass.shape, 1) == images, total, mass)
    wide = best.shape[1] // 4
    rows = [v[:, i * wide : (i + 1) * wide] for v in (best, mass) for i in range(4)]
    stats_ref[...] = jnp.concatenate(rows, axis=0)


def contrast(images, parts, bits, heat, own, far, wp, embed, paired, weight):
    captions = embed.shape[0]
    columns = 2 * own.shape[0]
    return kernel_call(
        "contrast",
        functools.partial(contrast_kernel, images, parts, bits),
        [
            kept(columns, D),
            kept(captions, columns, dtype=F32),
            kept(captions, 1, dtype=F32),
            kept(captions, 1, dtype=F32),
            shape(8, columns // 4),
        ],
        (heat,),
        near(own, far, wp, embed, paired, weight),
        [((columns, D), BF)],
        cost(2 * columns * D * D),
        max(LIMIT, columns * 8192),
    )


def merged(refs):
    best = functools.reduce(jnp.maximum, [ref[:4] for ref in refs])
    mass = sum(ref[4:] * jnp.exp(ref[:4] - best) for ref in refs)
    return best, mass


def merge_kernel(*refs):
    *given, out_ref = refs
    best, mass = merged(given)
    out_ref[...] = jnp.concatenate([best, mass], axis=0)


def merge(stats):
    return kernel_call("merge", merge_kernel, [shape(*stats[0].shape)], (), stats)[0]


def quarters(rep, away, flip=0):
    core = rep & 1
    out = []
    for xrel in range(2):
        for yrel in range(2):
            block = jnp.bitwise_xor(rep, 2 * xrel + away)
            x_first = 1 - core if away == flip else core
            out.append((jnp.where(x_first == 1, 2 * xrel + yrel, 2 * yrel + xrel), block, yrel))
    return out


def head_back_kernel(
    images,
    count_stats,
    rounds,
    heat_ref,
    place_ref,
    score_ref,
    row_ref,
    inverse_ref,
    weight_ref,
    paired_ref,
    picture_ref,
    text_ref,
    scale_ref,
    wm_ref,
    wn_ref,
    slope_ref,
    second_t_ref,
    box_ref,
    *refs,
):
    first = 1 << rounds[0]
    pieces = refs[len(refs) - first :]
    stats = refs[:count_stats]
    (
        back_ref,
        away_ref,
        here_ref,
        pooled_ref,
        loss_ref,
        down_bias_ref,
        up_bias_ref,
    ) = refs[count_stats : len(refs) - first]
    rep = lax.axis_index("rep")
    heat = heat_ref[0]
    captions = place_ref.shape[0]
    line, column = token_limits(place_ref)
    count = jnp.sum(pool_mask(line, captions), axis=1, keepdims=True)
    owner = spread_mask(column, captions).astype(BF)
    owner = jnp.concatenate([owner, owner], axis=1)

    score = score_ref[...]
    match, valid = match_of(as_column(paired_ref), score.shape[1], images)
    best, mass = merged(stats)
    column_log = jnp.log(mass) + best
    column_log = jnp.concatenate([column_log[i : i + 1] for i in range(4)], axis=1)
    loss_ref[...] = mass[:1, images : images + 1] + jnp.sum(
        jnp.where(valid, column_log, 0.0), axis=1, keepdims=True
    )
    weight = as_column(weight_ref)
    graded = (
        weight * jnp.exp(score - row_ref[...])
        + jnp.exp(score - column_log)
        - jnp.where(match, weight * (1.0 + inverse_ref[...]), 0.0)
    )
    graded = jnp.where(valid, graded / heat, 0.0).astype(BF)
    embed_back = nn(graded, picture_ref[...])
    text = text_ref[...]
    factor = scale_ref[...]
    text_dot = jnp.sum(text * embed_back, axis=1, keepdims=True)
    text_back = (factor * embed_back - text * (factor * factor * factor) * text_dot).astype(BF)
    blocks, _, wide = box_ref.shape
    masks = gather_masks(rounds, blocks)
    for c, piece_ref in enumerate(pieces):
        for i in range(blocks // first):
            block = jnp.bitwise_xor(lax.axis_index("dp"), masks[i * first + c])
            piece_ref[:, i * wide : (i + 1) * wide] = box_ref[block]
        piece_ref[:, (blocks // first) * wide :] = text_back
    pooled_back = nt(text_back, wm_ref[...])
    pooled_ref[...] = pooled_back
    branch = (pooled_back / count).astype(BF)
    down_bias_ref[...] = jnp.sum(branch.astype(F32) * count, axis=0, keepdims=True)
    ones = jnp.ones((SLOT, back_ref.shape[0]), BF)
    step = 512

    def widen(i, carry):
        at = pl.multiple_of(i * step, 128)
        part = nn(owner, two(nt(branch, wn_ref[pl.ds(at, step), :])))
        part = (part * slope_ref[:, pl.ds(at, step)].astype(F32)).astype(BF)
        back_ref[:, pl.ds(at, step)] = part
        up_bias_ref[:, pl.ds(at, step)] = nn(ones, part)[:1]
        return carry

    lax.fori_loop(0, FF // step, widen, 0, unroll=3)
    half = second_t_ref.shape[0] // 2
    wide = FF // 4
    for turn, target in enumerate((away_ref, here_ref)):
        for place, block, yrel in quarters(rep, 1 - turn):
            part = nn(
                second_t_ref[yrel * half : (yrel + 1) * half],
                back_ref[:, pl.ds(pl.multiple_of(block * wide, 128), wide)],
            )
            for h in range(2):
                target[place, h] = part[:, h * (wide // 2) : (h + 1) * (wide // 2)].astype(BF)


def head_back(images, rounds, heat, place, stats, score, row, inverse, weight, paired, picture, text,
              factor, wm, wn, slope, second_t, box):
    captions = text.shape[0]
    tokens = slope.shape[0]
    piece = (4, 2, D // 2, FF // 8)
    return kernel_call(
        "head_back",
        functools.partial(head_back_kernel, images, len(stats), rounds),
        [
            kept(tokens, FF),
            kept(*piece),
            kept(*piece),
            kept(captions, D, dtype=F32),
            shape(1, 1),
            shape(1, D),
            shape(1, FF),
        ]
        + [shape(captions, (box.shape[0] >> rounds[0]) * box.shape[2] + D, dtype=BF)] * (1 << rounds[0]),
        (heat,),
        (
            *near(place, score, row, inverse, weight, paired),
            *near(picture, text, factor, wm, wn, slope, second_t, box),
            *stats,
        ),
        (),
        cost(2 * tokens * D * FF),
    )


def middle_back_kernel(
    place_ref,
    gain_ref,
    pooled_ref,
    back_ref,
    wu_ref,
    unit_ref,
    inverse_ref,
    wo_ref,
    total_ref,
    attended_ref,
    context_back_ref,
    gain_back_ref,
    shift_back_ref,
    bias_ref,
):
    captions = place_ref.shape[0]
    line, column = token_limits(place_ref)
    count = jnp.sum(pool_mask(line, captions), axis=1, keepdims=True)
    owner = spread_mask(column, captions).astype(BF)
    owner = jnp.concatenate([owner, owner], axis=1)
    second_back = nt(back_ref[...], wu_ref[...])
    part, gain_back_ref[...], shift_back_ref[...] = norm_back(
        unit_ref[...], inverse_ref[...], as_row(gain_ref), second_back
    )
    total = nn(owner, two(pooled_ref[...] / count)) + part
    total_ref[...] = total
    attended = total.astype(BF)
    attended_ref[...] = attended
    bias_ref[...] = nn(jnp.ones((SLOT, attended.shape[0]), BF), attended)[:1]
    context_back_ref[...] = nt(attended, wo_ref[...]).astype(BF)


def middle_back(place, gain, pooled, back, wu, unit, inverse, wo):
    tokens = back.shape[0]
    return kernel_call(
        "middle_back",
        middle_back_kernel,
        [
            kept(tokens, D, dtype=F32),
            kept(tokens, D),
            kept(tokens, D),
            shape(1, D),
            shape(1, D),
            shape(1, D),
        ],
        (),
        near(place, gain, pooled, back, wu, unit, inverse, wo),
        (),
        cost(2 * tokens * D * (FF + D)),
    )


def attention_back_kernel(project_ref, att_ref, context_back_ref, back_ref, bias_ref):
    masks = head_masks()
    picks = caption_masks()
    lows = [pick.astype(F32).astype(BF) for pick in picks]
    low_scale = jnp.asarray(scale, BF)
    first = iota((GROUP, 2 * HEAD), 1) < HEAD
    tokens = project_ref.shape[0]

    def attend(h, carry):
        at = pl.multiple_of(h * 2 * HEAD, 128)
        at_k = pl.multiple_of(D + at, 128)
        at_v = pl.multiple_of(2 * D + at, 128)
        for g in range(tokens // GROUP):
            span = slice(g * GROUP, (g + 1) * GROUP)
            query = project_ref[span, pl.ds(at, 128)]
            keys = both_heads(project_ref[span, pl.ds(at_k, 128)], masks)
            values = both_heads(project_ref[span, pl.ds(at_v, 128)], masks)
            upper = context_back_ref[span, pl.ds(at, 128)]
            full = nt(values, upper)
            weights, grads = [], []
            for e in range(2):
                weight = att_ref[2 * h + e, :, span]
                part = compact(full[e * GROUP : (e + 1) * GROUP], picks)
                grad = weight * (part - jnp.sum(weight * part, axis=0, keepdims=True))
                weights.append(expand(weight.astype(BF), lows))
                grads.append(expand(grad.astype(BF) * low_scale, lows))
            weights = jnp.concatenate(weights, axis=0)
            grads = jnp.concatenate(grads, axis=0)
            back_ref[span, pl.ds(at, 128)] = tn(grads, keys).astype(BF)
            wide = nn(grads, query)
            back_ref[span, pl.ds(at_k, 128)] = jnp.where(first, wide[:GROUP], wide[GROUP:]).astype(
                BF
            )
            wide = nn(weights, upper)
            back_ref[span, pl.ds(at_v, 128)] = jnp.where(first, wide[:GROUP], wide[GROUP:]).astype(
                BF
            )
        return carry

    lax.fori_loop(0, PAIRS, attend, 0, unroll=3)
    ones = jnp.ones((SLOT, tokens), BF)
    for i in range(3):
        lanes = slice(i * D, (i + 1) * D)
        bias_ref[:, lanes] = nn(ones, back_ref[:, lanes])[:1]


def attention_back(project, att, context_back):
    tokens = project.shape[0]
    return kernel_call(
        "attention_back",
        attention_back_kernel,
        [kept(tokens, 3 * D), shape(1, 3 * D)],
        (),
        near(project, att, context_back),
        (),
        cost(3 * tokens * D * D),
    )


def left_columns_kernel(back_ref, normed_t_ref, away_ref, here_ref, chosen):
    rep = lax.axis_index("rep")
    joint = 3 * D // 4
    some = chosen.shape[2]
    for r in range(4):

        @pl.when(rep == r)
        def _():
            for i, k in enumerate((1, 3, 0, 2)):
                b = r ^ k
                chosen[i] = back_ref[:, b * joint : b * joint + some]

    half = D // 2
    for turn, target in enumerate((away_ref, here_ref)):
        for i, (place, _, yrel) in enumerate(quarters(rep, 1 - turn, 1)):
            lines = slice(yrel * half, (yrel + 1) * half)
            target[place] = nn(normed_t_ref[lines], chosen[2 * turn + i // 2]).astype(BF)


def right_columns_kernel(
    back_ref, attended_ref, normed_t_ref, context_t_ref, away_ref, here_ref, chosen
):
    rep = lax.axis_index("rep")
    joint = 3 * D // 4
    out = D // 4
    some = chosen.shape[2] - out
    for r in range(4):

        @pl.when(rep == r)
        def _():
            for i, k in enumerate((1, 3, 0, 2)):
                b = r ^ k
                chosen[i, :, :some] = back_ref[:, (b + 1) * joint - some : (b + 1) * joint]
                chosen[i, :, some:] = attended_ref[:, b * out : (b + 1) * out]

    half = D // 2
    for turn, target in enumerate((away_ref, here_ref)):
        for i, (place, _, yrel) in enumerate(quarters(rep, 1 - turn)):
            block = 2 * turn + i // 2
            lines = slice(yrel * half, (yrel + 1) * half)
            target[place, :, :some] = nn(normed_t_ref[lines], chosen[block, :, :some]).astype(BF)
            target[place, :, some:] = nn(context_t_ref[lines], chosen[block, :, some:]).astype(BF)


def columns_gradient(name, body, operands):
    tokens = operands[0].shape[0]
    piece = (4, D // 2, D // 2)
    return kernel_call(
        name,
        body,
        [kept(*piece), kept(*piece)],
        (),
        near(*operands),
        [((4, tokens, D // 2), BF)],
        cost(tokens * D * FF),
    )


def token_back_kernel(
    gain_ref,
    unit_ref,
    inverse_ref,
    middle_ref,
    back_ref,
    wj_ref,
    joint_ref,
    out_ref,
    gain2_ref,
    shift2_ref,
    wide_ref,
    narrow_ref,
    token_ref,
    sums_ref,
):
    part, gain1, shift1 = norm_back(
        unit_ref[...], inverse_ref[...], as_row(gain_ref), nt(back_ref[...], wj_ref[...])
    )
    token_ref[...] = middle_ref[...] + part
    line = 0
    rest = (joint_ref, out_ref, gain2_ref, shift2_ref, wide_ref, narrow_ref)
    for value in [gain1, shift1] + [ref[...] for ref in rest]:
        for i in range(value.shape[1] // 128):
            sums_ref[line : line + 1] = value[:, i * 128 : (i + 1) * 128]
            line += 1
    sums_ref[line:] = jnp.zeros((sums_ref.shape[0] - line, 128), F32)


def token_back(gain, unit, inverse, middle, back, wj, sums):
    return kernel_call(
        "token_back",
        token_back_kernel,
        [shape(unit.shape[0], D), shape(ALL_LINES, 128)],
        (),
        (gain, *near(unit, inverse, middle, back, wj), *sums),
        (),
        cost(6 * unit.shape[0] * D * D),
    )


def low_rank_kernel(
    hidden, own_ref, near_ref, wm_ref, down_ref, head_ref, other_ref, box, back
):
    rows = own_ref.shape[0]
    box[:rows] = own_ref[...]
    box[rows:] = near_ref[...]
    part = down_ref.shape[0]
    start = box.shape[1] - D
    rep = lax.axis_index("rep")
    for r in range(D // part):

        @pl.when(rep == r)
        def _():
            for i, b in enumerate((r, r ^ 2)):
                back[i] = box[:, start + b * part : start + (b + 1) * part]

    wide = head_ref.shape[1]
    for i in range(2):
        block = jnp.bitwise_xor(rep, 2 * i)
        here = wm_ref[pl.ds(pl.multiple_of(block * part, SLOT), part), :]
        pooled = nt(box[:, start:], here).astype(BF)
        down = tn(pooled, box[:, :hidden])
        head = tn(back[i], box[:, hidden : hidden + wide])
        if i == 0:
            down_ref[...] = down
            head_ref[...] = head
        else:
            other_ref[:, :hidden] = down.astype(BF)
            other_ref[:, hidden:] = head.astype(BF)


def low_rank(blocks, parts, own, far, wm):
    rows = 2 * own.shape[0]
    hidden, wide, part = FF // blocks, D // blocks, D // parts
    return kernel_call(
        "low_rank",
        functools.partial(low_rank_kernel, hidden),
        [shape(part, hidden), shape(part, wide), shape(part, hidden + wide, dtype=BF)],
        (),
        near(own, far, wm),
        [((rows, own.shape[1]), BF), ((2, rows, part), BF)],
        cost(2 * rows * D * D),
    )


def finish_kernel(groups, *refs):
    up, first, second, lines = (
        [refs[sum(groups[:i]) + n] for n in range(groups[i])] for i in range(4)
    )
    loss_ref, down_ref, head_ref, other_ref = refs[sum(groups) : sum(groups) + 4]
    (
        joint_ref,
        out_ref,
        up_block_ref,
        down_block_ref,
        head_block_ref,
        loss_out_ref,
        *vector_refs,
    ) = refs[sum(groups) + 4 :]

    def total(terms):
        return sum(ref[...].astype(F32) for ref in terms)

    up_sum = total(up)
    for h in range(2):
        lanes = slice(h * up_sum.shape[2], (h + 1) * up_sum.shape[2])
        up_block_ref[:, lanes] = up_sum[h]
    one, two_ = total(first), total(second)
    some = one.shape[1]
    rest = joint_ref.shape[1] - some
    joint_ref[:, :some] = one
    joint_ref[:, some:] = two_[:, :rest]
    out_ref[...] = two_[:, rest:]
    hidden = down_ref.shape[1]
    down_block_ref[...] = down_ref[...] + other_ref[:, :hidden].astype(F32)
    head_block_ref[...] = (head_ref[...] + other_ref[:, hidden:].astype(F32)).T
    loss_out_ref[...] = loss_ref[...].reshape(1)
    vectors = total(lines)
    starts = (GAIN1, SHIFT1, JOINT, OUT, GAIN2, SHIFT2, WIDE, NARROW)
    for start, ref in zip(starts, vector_refs):
        for i in range(ref.shape[0] // 128):
            line = start // 128 + i
            if start == JOINT and i >= D // 128:
                line += D // 128
            ref[pl.ds(i * 128, 128)] = vectors[line]


def finish(up, first, second, vectors, loss, low, joint):
    rows = up[0].shape[1]
    sizes = (D, D, 2 * D, D, D, D, FF, D)
    return kernel_call(
        "finish",
        functools.partial(finish_kernel, [len(v) for v in (up, first, second, vectors)]),
        [
            shape(rows, joint),
            shape(rows, D - joint),
            shape(rows, D),
            shape(*low[0].shape),
            shape(*low[1].shape[::-1]),
            shape(1),
        ]
        + [shape(n) for n in sizes],
        (),
        (*up, *first, *second, *vectors, loss, *low),
    )


def both_pairs(partner):
    dp, rep = lax.axis_size("dp"), lax.axis_size("rep")
    pairs = []
    for i in range(dp):
        for j in range(rep):
            a, b = partner(i, j)
            pairs.append((i * rep + j, a * rep + b))
    return pairs


def exchange(value, partner):
    return lax.ppermute(value, ("dp", "rep"), both_pairs(partner))


def first_turn(i, j):
    return (i, j ^ 2) if j & 1 == 0 else (i ^ 1, j)


def second_turn(i, j):
    return (i ^ 1, j) if j & 1 == 0 else (i, j ^ 2)


def added(a, b):
    return (a.astype(F32) + b.astype(F32)).astype(BF)


def halved(here, got):
    half = here.shape[0] // 2
    return added(here[:half], got[:half]), added(here[half:], got[half:])


def parted(here, got, count):
    rows = here.shape[-2] // count
    parts = [slice(i * rows, (i + 1) * rows) for i in range(count)]
    return [added(here[..., p, :], got[..., p, :]) for p in parts]


def core_turn(i, j):
    return i, j ^ 1


def across(i, j):
    return i, j ^ 2


def group_round(keep, got, group):
    masks = group_masks(group)
    bits = len(group)
    parts = parted(keep, got, len(masks))
    place = [sum(((c >> n) & 1) << (bits - 1 - n) for n in range(bits)) for c in range(len(masks))]
    return [parts[0]] + [
        exchange(parts[place[c]], lambda i, j: (i ^ masks[c][0], j)) for c in range(1, len(masks))
    ]


def row_rounds(keep, got, groups):
    terms = [keep, got]
    for group in groups:
        if len(terms) > 2:
            terms = [terms[0], sum(v.astype(F32) for v in terms[1:])]
        terms = group_round(*terms, group)
    return terms


order = lax.optimization_barrier


def dp_groups():
    bits = [("dp", b) for b in range(1, lax.axis_size("dp").bit_length() - 1)]
    return [bits[i : i + 2] for i in range(0, len(bits), 2)] + [[("dp", 0)]]


def all_groups():
    bits = [("rep", b) for b in range(1, lax.axis_size("rep").bit_length() - 1)]
    groups = dp_groups()
    return groups[:-1] + [groups[-1] + bits, [("rep", 0)]]


def group_masks(group):
    out = [(0, 0)]
    for axis, bit in group:
        out += [(a | 1 << bit, b) if axis == "dp" else (a, b | 1 << bit) for a, b in out]
    return out


def gather_masks(rounds, blocks):
    bits = [0] + list(range(blocks.bit_length() - 2, 0, -1))
    masks, used = [0], 0
    for count in rounds:
        for bit in bits[used : used + count]:
            masks = masks + [m | 1 << bit for m in masks]
        used += count
    return masks


def split_round(value, wide, group):
    blocks = (value.shape[1] - D) // wide
    turns = group_masks(group)
    text = value[:, blocks * wide :]
    pieces = []
    for c, (a, b) in enumerate(turns):
        chosen = [value[:, i * wide : (i + 1) * wide] for i in range(c, blocks, len(turns))]
        piece = jnp.concatenate(chosen + [text], axis=1)
        pieces.append(piece if c == 0 else exchange(piece, lambda i, j: (i ^ a, j ^ b)))
    return pieces


def round_of(value, group):
    return [value] + [
        exchange(value, lambda i, j: (i ^ a, j ^ b)) for a, b in group_masks(group)[1:]
    ]


def relative_rows(value, blocks):
    rows = value.shape[0] // blocks
    if rows % SLOT == 0:
        return value
    bits = blocks.bit_length() - 1
    place = jnp.arange(blocks, dtype=jnp.int32)
    source = jnp.zeros_like(place)
    for bit in range(bits):
        source = source + ((place >> (bits - 1 - bit)) & 1) * (1 << bit)
    source = source ^ lax.axis_index("dp")
    return value.reshape(blocks, rows, -1)[source].reshape(value.shape)


def local(
    incoming_activations,
    caption_final_place,
    paired_picture,
    caption_weight,
    locked_picture_features,
    softmax_heat,
    premix_scaling_factor,
    premix_shift_term,
    stacked_mixing_matrix,
    asking_reading_offsets,
    mixing_result_matrix,
    mixing_result_offset,
    premlp_scaling_factor,
    premlp_shift_term,
    widening_matrix,
    widening_offset,
    narrowing_matrix,
    narrowing_offset,
    caption_mapping_matrix,
    picture_mapping_matrix,
):
    both = ("dp", "rep")
    devices = lax.axis_size(both)
    blocks = lax.axis_size("dp")
    parts = lax.axis_size("rep")
    captions = caption_final_place.shape[0]
    images = locked_picture_features.shape[0]
    groups = all_groups()
    pieces = round_of(jnp.pad(locked_picture_features, ((0, SLOT - images), (0, 0))), groups[0])
    project, normed, unit1, inverse1, place, out, x, wo = project_tokens(
        incoming_activations,
        premix_scaling_factor,
        premix_shift_term,
        asking_reading_offsets,
        stacked_mixing_matrix,
        (
            caption_final_place,
            mixing_result_offset,
            incoming_activations,
            mixing_result_matrix,
        ),
    )
    project, pieces = order((project, pieces))
    for group in groups[1:-1]:
        pieces = round_of(jnp.concatenate(pieces), group)
    att, context, middle, gain2, shift2, wide, narrow, wu, wn, wm = attend_tokens(
        place,
        out,
        x,
        project,
        wo,
        (
            premlp_scaling_factor,
            premlp_shift_term,
            widening_offset,
            narrowing_offset,
            widening_matrix,
            narrowing_matrix,
            caption_mapping_matrix,
        ),
    )
    middle, pieces = order((middle, pieces))
    own, far = round_of(jnp.concatenate(pieces), groups[-1])
    second, unit2, inverse2, upper, box, text, factor, embed, wp, paired, weight = widen_tokens(
        blocks,
        place,
        gain2,
        shift2,
        wide,
        narrow,
        middle,
        wu,
        wn,
        wm,
        (picture_mapping_matrix, paired_picture, caption_weight),
    )
    embed, far = order((embed, far))
    picture, score, row, inverse, stats = contrast(
        images,
        parts,
        sum(groups, []),
        softmax_heat,
        own,
        far,
        wp,
        embed,
        paired,
        weight,
    )
    groups = dp_groups()
    high = [[bit] for group in groups[:-1] for bit in group]
    factor_groups = groups[-1:] + high[::-1]
    stats = round_of(stats, [("rep", 0)])
    normed_t, context_t, second_t = (
        relative_rows(v, blocks) for v in turn_tokens(blocks, normed, context, second)
    )
    stats = round_of(merge(stats), [("rep", 1)] + groups[-1])
    slope = slope_tokens(upper)
    stats, slope = order((stats, slope))
    for group in groups[:-1]:
        stats = round_of(merge(stats), group)
    back, away, here, pooled_back, loss, down_bias, up_bias, *pieces = head_back(
        images,
        [len(group) for group in factor_groups],
        softmax_heat,
        place,
        stats,
        score,
        row,
        inverse,
        weight,
        paired,
        picture,
        text,
        factor,
        wm,
        wn,
        slope,
        second_t,
        box,
    )
    loss = loss / (captions * devices)
    got = exchange(away, core_turn)
    pieces = pieces[:1] + [
        exchange(piece, lambda i, j: (i ^ a, j ^ b))
        for piece, (a, b) in zip(pieces[1:], group_masks(factor_groups[0])[1:])
    ]
    total, attended, context_back, gain2, shift2, out_bias = middle_back(
        place,
        gain2,
        pooled_back,
        back,
        wu,
        unit2,
        inverse2,
        wo,
    )
    context_back, got, pieces = order((context_back, got, pieces))
    up, send = halved(here, got)
    got_up = exchange(send, first_turn)
    pieces = split_round(jnp.concatenate(pieces), box.shape[2], factor_groups[1])
    project_back, joint_bias = attention_back(project, att, context_back)
    away, here = columns_gradient("left_columns", left_columns_kernel, (project_back, normed_t))
    got = exchange(away, core_turn)
    project_back, away = order((project_back, away))
    away, here2 = columns_gradient(
        "right_columns", right_columns_kernel, (project_back, attended, normed_t, context_t)
    )
    project_back, away, got, got_up = order((project_back, away, got, got_up))
    up, up_send = halved(up, got_up)
    first, send = halved(here, got)
    got = exchange(jnp.concatenate([up_send[0], send]), second_turn)
    got2 = exchange(away, core_turn)
    joint = 3 * D // parts
    token, sums = token_back(
        premix_scaling_factor,
        unit1,
        inverse1,
        total,
        project_back,
        stacked_mixing_matrix,
        (joint_bias, out_bias, gain2, shift2, up_bias, down_bias),
    )
    sums, got2 = order((sums, got2))
    lines = round_of(sums, [("rep", 0)])
    lines = round_of(sum(lines), [("rep", 1)])
    second, send2 = halved(here2, got2)
    got, send2, lines, pieces = order((got, send2, lines, pieces))
    up, got_up = group_round(up[0], got[:2], high[0])
    first, send = halved(first, got[2:])
    got2 = exchange(jnp.concatenate([send2, send]), first_turn)
    lines = round_of(sum(lines), groups[-1])
    for group in factor_groups[2:]:
        pieces = split_round(jnp.concatenate(pieces), box.shape[2], group)
    got_up, got2, lines, pieces = order((got_up, got2, lines, pieces))
    second, send = halved(second, got2[:2])
    second, first, got = second[0], first[0], got2[2]
    got2 = exchange(send[0], second_turn)
    first, got = group_round(first, got, high[0])
    for group in high[1:]:
        up, got_up = group_round(up, got_up, group)
    lines = round_of(sum(lines), high[0])
    factors = jnp.concatenate(pieces)
    far = exchange(factors, core_turn)
    got, got2, lines, far = order((got, got2, lines, far))
    *low, other = low_rank(blocks, parts, factors, far, wm)
    other = exchange(other, across)
    for i, group in enumerate(high):
        if i:
            got2, lines = order((got2, lines))
        second, got2 = group_round(second, got2, group)
        if i + 1 < len(high):
            first, got = group_round(first, got, high[i + 1])
            lines = round_of(sum(lines), high[i + 1])
    first, second, up, vectors = [first, got], [second, got2], [up, got_up], lines
    joint_block, out_block, up_block, down_block, head_block, loss, *grads = finish(
        up, first, second, vectors, loss, (*low, other), joint
    )
    return (
        loss,
        token,
        grads[0],
        grads[1],
        joint_block,
        grads[2],
        out_block,
        grads[3],
        grads[4],
        grads[5],
        up_block,
        grads[6],
        down_block.T,
        grads[7],
        head_block,
    )


def solution(mesh):
    spread = P(("dp", "rep"), None)
    line = P(("dp", "rep"))
    block = P("dp", "rep")
    in_specs = (spread, line, line, line, spread) + (P(),) * 15
    out_specs = (
        P(),
        spread,
        P(),
        P(),
        block,
        P(),
        block,
        P(),
        P(),
        P(),
        block,
        P(),
        block,
        P(),
        block,
    )
    return jax.shard_map(local, mesh=mesh, in_specs=in_specs, out_specs=out_specs, check_vma=False)
```

```python
import functools

import jax
import jax.numpy as jnp
from jax import lax
from jax.experimental import pallas as pl
from jax.experimental.pallas import tpu as pltpu
from jax.sharding import PartitionSpec as P

D = 768
HEADS = 12
HEAD = 64
SEQ = 16
FF = 3072
GROUP = 128
PAIRS = HEADS // 2
SLOT = 16
BF = jnp.bfloat16
F32 = jnp.float32

epsilon = 1e-06
BEND = 0.7978845608028654
CUBE = BEND * 0.044715
negative = -1e30
scale = HEAD ** (-0.5)
LIMIT = 20 * 1024 * 1024

GAIN1, SHIFT1, JOINT, OUT, GAIN2, SHIFT2, WIDE, NARROW = 0, 768, 1536, 3840, 4608, 5376, 6144, 9216
VECTORS = 9984
LINES = VECTORS // 128
ALL_LINES = LINES + -LINES % 8

vmem = pl.BlockSpec(memory_space=pltpu.VMEM)
hbm = pl.BlockSpec(memory_space=pltpu.HBM)
smem = pl.BlockSpec(memory_space=pltpu.SMEM)


def dot(a, b, dims):
    return lax.dot_general(a, b, (dims, ((), ())), preferred_element_type=F32)


def nn(a, b):
    return dot(a, b, ((1,), (0,)))


def nt(a, b):
    return dot(a, b, ((1,), (1,)))


def tn(a, b):
    return dot(a, b, ((0,), (0,)))


def cost(flops):
    return pl.CostEstimate(flops=flops, transcendentals=0, bytes_accessed=0)


def shape(*dims, dtype=F32):
    return jax.ShapeDtypeStruct(dims, dtype)


def kept(*dims, dtype=BF):
    return pltpu.VMEM(dims, dtype)


def near(*values):
    return [pltpu.with_memory_space_constraint(v, pltpu.VMEM) for v in values]


def kernel_call(
    name, body, results, small, operands, scratch=(), estimate=None, limit=LIMIT, far=(), copies=0
):
    semaphores = [pltpu.SemaphoreType.DMA((copies,))] if copies else []
    return pl.pallas_call(
        body,
        out_shape=results,
        in_specs=[smem] * len(small) + [hbm] * len(far) + [vmem] * len(operands),
        out_specs=[vmem] * len(results),
        scratch_shapes=[pltpu.VMEM(s, t) for s, t in scratch] + semaphores,
        compiler_params=pltpu.CompilerParams(vmem_limit_bytes=limit),
        cost_estimate=estimate,
        name=name,
    )(*small, *[pltpu.with_memory_space_constraint(v, pltpu.HBM) for v in far], *operands)


def fetched(values):
    return [kept(*v.shape, dtype=v.dtype) for v in values]


def fetch(sources, targets, semaphores):
    copies = [
        pltpu.make_async_copy(source, target, semaphores.at[i])
        for i, (source, target) in enumerate(zip(sources, targets))
    ]
    for copy in copies:
        copy.start()
    return copies


def iota(dims, axis):
    return lax.broadcasted_iota(jnp.int32, dims, axis)


def norm_parts(values):
    average = jnp.mean(values, axis=-1, keepdims=True)
    centred = values - average
    inverse = lax.rsqrt(jnp.mean(centred * centred, axis=-1, keepdims=True) + epsilon)
    return centred * inverse, inverse


def norm_back(unit, inverse, gain, back):
    inner = back * gain
    part = inverse * (
        inner
        - jnp.mean(inner, axis=-1, keepdims=True)
        - unit * jnp.mean(inner * unit, axis=-1, keepdims=True)
    )
    return part, jnp.sum(back * unit, axis=0, keepdims=True), jnp.sum(back, axis=0, keepdims=True)


def split(value):
    high = value.astype(BF)
    return high, (value - high.astype(F32)).astype(BF)


def two(value):
    return jnp.concatenate(split(value), axis=0)


def as_row(ref):
    return ref[...].reshape(1, ref.shape[0])


def as_column(ref):
    size = ref.shape[0]
    same = iota((size, size), 0) == iota((size, size), 1)
    row = as_row(ref)
    return jnp.sum(jnp.where(same, row, jnp.zeros_like(row)), axis=1, keepdims=True)


def token_limits(ref):
    place = as_row(ref).astype(F32)
    captions = place.shape[1]
    tokens = captions * SEQ
    owner = (iota((tokens, captions), 0) // SEQ == iota((tokens, captions), 1)).astype(F32)
    column = jnp.sum(owner * place, axis=1, keepdims=True)
    line = nt(place.astype(BF), owner.astype(BF))
    return line, column


def pool_mask(line, captions):
    dims = (captions, captions * SEQ)
    token = iota(dims, 1)
    inside = (token % SEQ).astype(F32) <= line
    return jnp.where((token // SEQ == iota(dims, 0)) & inside, 1.0, 0.0)


def spread_mask(column, captions):
    dims = (captions * SEQ, captions)
    token = iota(dims, 0)
    inside = (token % SEQ).astype(F32) <= column
    return jnp.where((token // SEQ == iota(dims, 1)) & inside, 1.0, 0.0)


def head_masks():
    lane = iota((1, 2 * HEAD), 1)
    even = (lane < HEAD).astype(F32)
    return even.astype(BF), (1.0 - even).astype(BF)


def caption_masks():
    lane = iota((SEQ, GROUP), 1) // SEQ
    return [lane == c for c in range(GROUP // SEQ)]


def compact(full, picks):
    out = full[:SEQ]
    for c in range(1, len(picks)):
        out = jnp.where(picks[c], full[c * SEQ : (c + 1) * SEQ], out)
    return out


def expand(low, lows):
    return jnp.concatenate([low * mask for mask in lows], axis=0)


def both_heads(value, masks):
    return jnp.concatenate([value * masks[0], value * masks[1]], axis=0)


def store_permuted(ref, value, dp, blocks):
    rows = value.shape[0] // blocks
    bits = blocks.bit_length() - 1
    if rows % SLOT:
        ref[...] = value
        return
    for b in range(blocks):
        k = jnp.bitwise_xor(dp, b)
        place = 0
        for bit in range(bits):
            place = place + ((k >> bit) & 1) * (1 << (bits - 1 - bit))
        ref[pl.ds(pl.multiple_of(place * rows, SLOT), rows), :] = value[b * rows : (b + 1) * rows]


def box_width(blocks):
    used = (FF + D) // blocks
    return used + -used % 128


def project_kernel(*refs):
    more = (len(refs) - 5 - 4 - 5 - 1) // 2
    mine, other, refs = refs[:5], refs[5 : 5 + more], refs[5 + more :]
    project_ref, normed_ref, unit_ref, inverse_ref = refs[:4]
    targets, (x, gain, shift, joint, wj, semaphores) = refs[4 : 4 + more], refs[4 + more :]
    copies = fetch(mine + other, (x, gain, shift, joint, wj) + targets, semaphores)
    copies[0].wait()
    unit_ref[...], inverse_ref[...] = norm_parts(x[...].astype(F32))
    for copy in copies[1:5]:
        copy.wait()
    normed_ref[...] = (unit_ref[...] * as_row(gain) + as_row(shift)).astype(BF)
    bias = as_row(joint)
    for i, part in enumerate((bias[:, :D], 0.0, bias[:, D:])):
        lanes = slice(i * D, (i + 1) * D)
        project_ref[:, lanes] = (nn(normed_ref[...], wj[:, lanes]) + part).astype(BF)
    for copy in copies[5:]:
        copy.wait()


def project_tokens(x, gain, shift, joint, wj, following):
    tokens = x.shape[0]
    mine = (x, gain, shift, joint, wj)
    return kernel_call(
        "project_tokens",
        project_kernel,
        [
            kept(tokens, 3 * D),
            kept(tokens, D),
            kept(tokens, D, dtype=F32),
            kept(tokens, 1, dtype=F32),
        ]
        + fetched(following),
        (),
        (),
        [(v.shape, v.dtype) for v in mine],
        cost(6 * tokens * D * D),
        far=mine + following,
        copies=5 + len(following),
    )


def turn_kernel(blocks, *refs):
    dp = lax.axis_index("dp")
    count = len(refs) // 2
    for source, target in zip(refs[:count], refs[count:]):
        store_permuted(target, source[...].T, dp, blocks)


def turn_tokens(blocks, *values):
    return kernel_call(
        "turn_tokens",
        functools.partial(turn_kernel, blocks),
        [kept(*v.shape[::-1]) for v in values],
        (),
        near(*values),
        (),
        cost(32 * values[0].shape[0] * D),
    )


def attend_kernel(*refs):
    more = (len(refs) - 5 - 3 - 1) // 2
    far, (place_ref, out_ref, x_ref, project_ref, wo_ref) = refs[:more], refs[more : more + 5]
    att_ref, context_ref, middle_ref = refs[more + 5 : more + 8]
    copies = fetch(far, refs[more + 8 : -1], refs[-1])
    line, _ = token_limits(place_ref)
    masks = head_masks()
    picks = caption_masks()
    lows = [pick.astype(F32).astype(BF) for pick in picks]
    key_place = iota((SEQ, GROUP), 0).astype(F32)

    def attend(h, carry):
        at = pl.multiple_of(h * 2 * HEAD, 128)
        for g in range(x_ref.shape[0] // GROUP):
            here = slice(g * GROUP, (g + 1) * GROUP)
            query = project_ref[here, pl.ds(at, 128)]
            keys = both_heads(project_ref[here, pl.ds(pl.multiple_of(D + at, 128), 128)], masks)
            values = both_heads(
                project_ref[here, pl.ds(pl.multiple_of(2 * D + at, 128), 128)], masks
            )
            scores = nt(keys, query)
            allowed = key_place <= line[:, here]
            parts = []
            for e in range(2):
                score = compact(scores[e * GROUP : (e + 1) * GROUP], picks) * scale
                score = jnp.where(allowed, score, negative)
                score = jnp.exp(score - jnp.max(score, axis=0, keepdims=True))
                weight = score / jnp.sum(score, axis=0, keepdims=True)
                att_ref[2 * h + e, :, here] = weight
                parts.append(expand(weight.astype(BF), lows))
            context_ref[here, pl.ds(at, 128)] = tn(jnp.concatenate(parts, axis=0), values).astype(BF)
        return carry

    lax.fori_loop(0, PAIRS, attend, 0, unroll=3)
    middle_ref[...] = x_ref[...].astype(F32) + (nn(context_ref[...], wo_ref[...]) + as_row(out_ref))
    for copy in copies:
        copy.wait()


def attend_tokens(place, out, x, project, wo, following):
    tokens = x.shape[0]
    return kernel_call(
        "attend_tokens",
        attend_kernel,
        [kept(HEADS, SEQ, tokens, dtype=F32), kept(tokens, D), kept(tokens, D, dtype=F32)]
        + fetched(following),
        (),
        near(place, out, x, project, wo),
        (),
        cost(4 * tokens * D * D),
        far=following,
        copies=len(following),
    )


def widen_kernel(blocks, *refs):
    more = (len(refs) - 9 - 8 - 3 - 1) // 2
    far = refs[:more]
    place_ref, gain_ref, shift_ref, wide_ref, narrow_ref, middle_ref, wu_ref, wn_ref, wm_ref = refs[
        more : more + 9
    ]
    second_ref, unit_ref, inverse_ref, upper_ref, box_ref, text_ref, scale_ref, embed_ref = refs[
        more + 9 : more + 17
    ]
    branch, wide, mean, semaphores = refs[-4:]
    copies = fetch(far, refs[more + 17 : -4], semaphores)
    captions = place_ref.shape[0]
    line, column = token_limits(place_ref)
    pool = pool_mask(line, captions)
    share = 1.0 / jnp.sum(pool, axis=1, keepdims=True)
    unit, inverse_ref[...] = norm_parts(middle_ref[...])
    unit_ref[...] = unit
    second_ref[...] = (unit * as_row(gain_ref) + as_row(shift_ref)).astype(BF)
    branch[...] = jnp.zeros_like(branch)
    wide[...] = as_row(wide_ref)
    pool_low = pool.astype(BF)
    step = 512

    def widen(i, carry):
        at = pl.multiple_of(i * step, 128)
        upper = nn(second_ref[...], wu_ref[:, pl.ds(at, step)]) + wide[:, pl.ds(at, step)]
        active = upper * (0.5 + 0.5 * jnp.tanh(upper * (BEND + CUBE * (upper * upper))))
        upper_ref[:, pl.ds(at, step)] = upper
        parts = two(nn(pool_low, active.astype(BF)) * share)
        mean[:, pl.ds(at, step)] = parts[:captions]
        branch[...] += nn(parts, wn_ref[pl.ds(at, step), :])
        return carry

    lax.fori_loop(0, FF // step, widen, 0, unroll=3)
    inside = jnp.where((iota((captions * SEQ, 1), 0) % SEQ).astype(F32) <= column, 1.0, 0.0)
    weight = inside / (column + 1.0)
    pooled = jnp.sum((middle_ref[...] * weight).reshape(captions, SEQ, D), axis=1)
    pooled = (pooled + (branch[:captions] + branch[captions:] + as_row(narrow_ref))).astype(BF)
    hidden, part = FF // blocks, D // blocks
    for b in range(blocks):
        box_ref[b, :, :hidden] = mean[:, b * hidden : (b + 1) * hidden]
        box_ref[b, :, hidden : hidden + part] = pooled[:, b * part : (b + 1) * part]
    text = nn(pooled, wm_ref[...])
    factor = lax.rsqrt(jnp.sum(text * text, axis=1, keepdims=True) + epsilon)
    text_ref[...] = text
    scale_ref[...] = factor
    embed_ref[...] = (text * factor).astype(BF)
    for copy in copies:
        copy.wait()


def slope_kernel(upper_ref, slope_ref):
    step = 512

    def part(i, carry):
        at = pl.multiple_of(i * step, 128)
        upper = upper_ref[:, pl.ds(at, step)]
        square = upper * upper
        half = 0.5 + 0.5 * jnp.tanh(upper * (BEND + CUBE * square))
        slope_ref[:, pl.ds(at, step)] = (
            half * (1.0 + (upper - upper * half) * (2.0 * BEND + 6.0 * CUBE * square))
        ).astype(BF)
        return carry

    lax.fori_loop(0, FF // step, part, 0)


def slope_tokens(upper):
    return kernel_call(
        "slope_tokens", slope_kernel, [kept(*upper.shape)], (), near(upper), (), cost(upper.size)
    )[0]


def widen_tokens(blocks, place, gain, shift, wide, narrow, middle, wu, wn, wm, following):
    tokens = middle.shape[0]
    captions = place.shape[0]
    return kernel_call(
        "widen_tokens",
        functools.partial(widen_kernel, blocks),
        [
            kept(tokens, D),
            kept(tokens, D, dtype=F32),
            kept(tokens, 1, dtype=F32),
            kept(tokens, FF, dtype=F32),
            kept(blocks, captions, box_width(blocks)),
            kept(captions, D, dtype=F32),
            kept(captions, 1, dtype=F32),
            kept(captions, D),
        ]
        + fetched(following),
        (),
        near(place, gain, shift, wide, narrow, middle, wu, wn, wm),
        [
            ((2 * captions, D), F32),
            ((1, FF), F32),
            ((captions, FF), BF),
        ],
        cost(2 * tokens * D * FF),
        far=following,
        copies=len(following),
    )


def match_of(paired, columns, images):
    column = iota((1, columns), 1)
    valid = column % SLOT < images
    name = jnp.where(valid, (column // SLOT) * images + column % SLOT, -1)
    return paired == name, valid


def contrast_kernel(
    images,
    parts,
    bits,
    heat_ref,
    own_ref,
    near_ref,
    wp_ref,
    embed_ref,
    paired_ref,
    weight_ref,
    picture_ref,
    score_ref,
    row_ref,
    inverse_ref,
    stats_ref,
    features,
):
    half = own_ref.shape[0] // SLOT
    for far, ref in enumerate((own_ref, near_ref)):

        def place(i, carry, far=far, ref=ref):
            p = i + far * half
            index = {axis: lax.axis_index(axis) for axis in ("dp", "rep")}
            for n, (axis, bit) in enumerate(bits):
                index[axis] = jnp.bitwise_xor(index[axis], ((p >> n) & 1) << bit)
            to = pl.ds(pl.multiple_of((index["dp"] * parts + index["rep"]) * SLOT, SLOT), SLOT)
            features[to, :] = ref[pl.ds(pl.multiple_of(i * SLOT, SLOT), SLOT), :]
            return carry

        lax.fori_loop(0, half, place, 0, unroll=4)
    picture = nn(features[...], wp_ref[...])
    picture = (
        picture * lax.rsqrt(jnp.sum(picture * picture, axis=1, keepdims=True) + epsilon)
    ).astype(BF)
    picture_ref[...] = picture
    score = nt(embed_ref[...], picture) / heat_ref[0]
    match, valid = match_of(as_column(paired_ref), score.shape[1], images)
    score = jnp.where(valid, score, negative)
    score_ref[...] = score
    top = jnp.max(score, axis=1, keepdims=True)
    row = jnp.log(jnp.sum(jnp.exp(score - top), axis=1, keepdims=True)) + top
    row_ref[...] = row
    positive = jnp.sum(jnp.where(match, score, 0.0), axis=1, keepdims=True)
    hits = jnp.where(match, 1.0, 0.0)
    counts = jnp.sum(hits, axis=0, keepdims=True)
    inverse = 1.0 / jnp.sum(hits * counts, axis=1, keepdims=True)
    inverse_ref[...] = inverse
    total = jnp.sum(as_column(weight_ref) * (row - positive - positive * inverse))
    best = jnp.max(score, axis=0, keepdims=True)
    mass = jnp.sum(jnp.exp(score - best), axis=0, keepdims=True)
    mass = jnp.where(iota(mass.shape, 1) == images, total, mass)
    wide = best.shape[1] // 4
    rows = [v[:, i * wide : (i + 1) * wide] for v in (best, mass) for i in range(4)]
    stats_ref[...] = jnp.concatenate(rows, axis=0)


def contrast(images, parts, bits, heat, own, far, wp, embed, paired, weight):
    captions = embed.shape[0]
    columns = 2 * own.shape[0]
    return kernel_call(
        "contrast",
        functools.partial(contrast_kernel, images, parts, bits),
        [
            kept(columns, D),
            kept(captions, columns, dtype=F32),
            kept(captions, 1, dtype=F32),
            kept(captions, 1, dtype=F32),
            shape(8, columns // 4),
        ],
        (heat,),
        near(own, far, wp, embed, paired, weight),
        [((columns, D), BF)],
        cost(2 * columns * D * D),
        max(LIMIT, columns * 8192),
    )


def merged(refs):
    best = functools.reduce(jnp.maximum, [ref[:4] for ref in refs])
    mass = sum(ref[4:] * jnp.exp(ref[:4] - best) for ref in refs)
    return best, mass


def merge_kernel(*refs):
    *given, out_ref = refs
    best, mass = merged(given)
    out_ref[...] = jnp.concatenate([best, mass], axis=0)


def merge(stats):
    return kernel_call("merge", merge_kernel, [shape(*stats[0].shape)], (), stats)[0]


def quarters(rep, away, flip=0):
    core = rep & 1
    out = []
    for xrel in range(2):
        for yrel in range(2):
            block = jnp.bitwise_xor(rep, 2 * xrel + away)
            x_first = 1 - core if away == flip else core
            out.append((jnp.where(x_first == 1, 2 * xrel + yrel, 2 * yrel + xrel), block, yrel))
    return out


def head_back_kernel(
    images,
    count_stats,
    rounds,
    heat_ref,
    place_ref,
    score_ref,
    row_ref,
    inverse_ref,
    weight_ref,
    paired_ref,
    picture_ref,
    text_ref,
    scale_ref,
    wm_ref,
    wn_ref,
    slope_ref,
    second_t_ref,
    box_ref,
    *refs,
):
    first = 1 << rounds[0]
    pieces = refs[len(refs) - first :]
    stats = refs[:count_stats]
    (
        back_ref,
        away_ref,
        here_ref,
        pooled_ref,
        loss_ref,
        down_bias_ref,
        up_bias_ref,
    ) = refs[count_stats : len(refs) - first]
    rep = lax.axis_index("rep")
    heat = heat_ref[0]
    captions = place_ref.shape[0]
    line, column = token_limits(place_ref)
    count = jnp.sum(pool_mask(line, captions), axis=1, keepdims=True)
    owner = spread_mask(column, captions).astype(BF)
    owner = jnp.concatenate([owner, owner], axis=1)

    score = score_ref[...]
    match, valid = match_of(as_column(paired_ref), score.shape[1], images)
    best, mass = merged(stats)
    column_log = jnp.log(mass) + best
    column_log = jnp.concatenate([column_log[i : i + 1] for i in range(4)], axis=1)
    loss_ref[...] = mass[:1, images : images + 1] + jnp.sum(
        jnp.where(valid, column_log, 0.0), axis=1, keepdims=True
    )
    weight = as_column(weight_ref)
    graded = (
        weight * jnp.exp(score - row_ref[...])
        + jnp.exp(score - column_log)
        - jnp.where(match, weight * (1.0 + inverse_ref[...]), 0.0)
    )
    graded = jnp.where(valid, graded / heat, 0.0).astype(BF)
    embed_back = nn(graded, picture_ref[...])
    text = text_ref[...]
    factor = scale_ref[...]
    text_dot = jnp.sum(text * embed_back, axis=1, keepdims=True)
    text_back = (factor * embed_back - text * (factor * factor * factor) * text_dot).astype(BF)
    blocks, _, wide = box_ref.shape
    masks = gather_masks(rounds, blocks)
    for c, piece_ref in enumerate(pieces):
        for i in range(blocks // first):
            block = jnp.bitwise_xor(lax.axis_index("dp"), masks[i * first + c])
            piece_ref[:, i * wide : (i + 1) * wide] = box_ref[block]
        piece_ref[:, (blocks // first) * wide :] = text_back
    pooled_back = nt(text_back, wm_ref[...])
    pooled_ref[...] = pooled_back
    branch = (pooled_back / count).astype(BF)
    down_bias_ref[...] = jnp.sum(branch.astype(F32) * count, axis=0, keepdims=True)
    ones = jnp.ones((SLOT, back_ref.shape[0]), BF)
    step = 512

    def widen(i, carry):
        at = pl.multiple_of(i * step, 128)
        part = nn(owner, two(nt(branch, wn_ref[pl.ds(at, step), :])))
        part = (part * slope_ref[:, pl.ds(at, step)].astype(F32)).astype(BF)
        back_ref[:, pl.ds(at, step)] = part
        up_bias_ref[:, pl.ds(at, step)] = nn(ones, part)[:1]
        return carry

    lax.fori_loop(0, FF // step, widen, 0, unroll=3)
    half = second_t_ref.shape[0] // 2
    wide = FF // 4
    for turn, target in enumerate((away_ref, here_ref)):
        for place, block, yrel in quarters(rep, 1 - turn):
            part = nn(
                second_t_ref[yrel * half : (yrel + 1) * half],
                back_ref[:, pl.ds(pl.multiple_of(block * wide, 128), wide)],
            )
            for h in range(2):
                target[place, h] = part[:, h * (wide // 2) : (h + 1) * (wide // 2)].astype(BF)


def head_back(images, rounds, heat, place, stats, score, row, inverse, weight, paired, picture, text,
              factor, wm, wn, slope, second_t, box):
    captions = text.shape[0]
    tokens = slope.shape[0]
    piece = (4, 2, D // 2, FF // 8)
    return kernel_call(
        "head_back",
        functools.partial(head_back_kernel, images, len(stats), rounds),
        [
            kept(tokens, FF),
            kept(*piece),
            kept(*piece),
            kept(captions, D, dtype=F32),
            shape(1, 1),
            shape(1, D),
            shape(1, FF),
        ]
        + [shape(captions, (box.shape[0] >> rounds[0]) * box.shape[2] + D, dtype=BF)] * (1 << rounds[0]),
        (heat,),
        (
            *near(place, score, row, inverse, weight, paired),
            *near(picture, text, factor, wm, wn, slope, second_t, box),
            *stats,
        ),
        (),
        cost(2 * tokens * D * FF),
    )


def middle_back_kernel(
    place_ref,
    gain_ref,
    pooled_ref,
    back_ref,
    wu_ref,
    unit_ref,
    inverse_ref,
    wo_ref,
    total_ref,
    attended_ref,
    context_back_ref,
    gain_back_ref,
    shift_back_ref,
    bias_ref,
):
    captions = place_ref.shape[0]
    line, column = token_limits(place_ref)
    count = jnp.sum(pool_mask(line, captions), axis=1, keepdims=True)
    owner = spread_mask(column, captions).astype(BF)
    owner = jnp.concatenate([owner, owner], axis=1)
    second_back = nt(back_ref[...], wu_ref[...])
    part, gain_back_ref[...], shift_back_ref[...] = norm_back(
        unit_ref[...], inverse_ref[...], as_row(gain_ref), second_back
    )
    total = nn(owner, two(pooled_ref[...] / count)) + part
    total_ref[...] = total
    attended = total.astype(BF)
    attended_ref[...] = attended
    bias_ref[...] = nn(jnp.ones((SLOT, attended.shape[0]), BF), attended)[:1]
    context_back_ref[...] = nt(attended, wo_ref[...]).astype(BF)


def middle_back(place, gain, pooled, back, wu, unit, inverse, wo):
    tokens = back.shape[0]
    return kernel_call(
        "middle_back",
        middle_back_kernel,
        [
            kept(tokens, D, dtype=F32),
            kept(tokens, D),
            kept(tokens, D),
            shape(1, D),
            shape(1, D),
            shape(1, D),
        ],
        (),
        near(place, gain, pooled, back, wu, unit, inverse, wo),
        (),
        cost(2 * tokens * D * (FF + D)),
    )


def attention_back_kernel(project_ref, att_ref, context_back_ref, back_ref, bias_ref):
    masks = head_masks()
    picks = caption_masks()
    lows = [pick.astype(F32).astype(BF) for pick in picks]
    low_scale = jnp.asarray(scale, BF)
    first = iota((GROUP, 2 * HEAD), 1) < HEAD
    tokens = project_ref.shape[0]

    def attend(h, carry):
        at = pl.multiple_of(h * 2 * HEAD, 128)
        at_k = pl.multiple_of(D + at, 128)
        at_v = pl.multiple_of(2 * D + at, 128)
        for g in range(tokens // GROUP):
            span = slice(g * GROUP, (g + 1) * GROUP)
            query = project_ref[span, pl.ds(at, 128)]
            keys = both_heads(project_ref[span, pl.ds(at_k, 128)], masks)
            values = both_heads(project_ref[span, pl.ds(at_v, 128)], masks)
            upper = context_back_ref[span, pl.ds(at, 128)]
            full = nt(values, upper)
            weights, grads = [], []
            for e in range(2):
                weight = att_ref[2 * h + e, :, span]
                part = compact(full[e * GROUP : (e + 1) * GROUP], picks)
                grad = weight * (part - jnp.sum(weight * part, axis=0, keepdims=True))
                weights.append(expand(weight.astype(BF), lows))
                grads.append(expand(grad.astype(BF) * low_scale, lows))
            weights = jnp.concatenate(weights, axis=0)
            grads = jnp.concatenate(grads, axis=0)
            back_ref[span, pl.ds(at, 128)] = tn(grads, keys).astype(BF)
            wide = nn(grads, query)
            back_ref[span, pl.ds(at_k, 128)] = jnp.where(first, wide[:GROUP], wide[GROUP:]).astype(
                BF
            )
            wide = nn(weights, upper)
            back_ref[span, pl.ds(at_v, 128)] = jnp.where(first, wide[:GROUP], wide[GROUP:]).astype(
                BF
            )
        return carry

    lax.fori_loop(0, PAIRS, attend, 0, unroll=3)
    ones = jnp.ones((SLOT, tokens), BF)
    for i in range(3):
        lanes = slice(i * D, (i + 1) * D)
        bias_ref[:, lanes] = nn(ones, back_ref[:, lanes])[:1]


def attention_back(project, att, context_back):
    tokens = project.shape[0]
    return kernel_call(
        "attention_back",
        attention_back_kernel,
        [kept(tokens, 3 * D), shape(1, 3 * D)],
        (),
        near(project, att, context_back),
        (),
        cost(3 * tokens * D * D),
    )


def left_columns_kernel(back_ref, normed_t_ref, away_ref, here_ref, chosen):
    rep = lax.axis_index("rep")
    joint = 3 * D // 4
    some = chosen.shape[2]
    for r in range(4):

        @pl.when(rep == r)
        def _():
            for i, k in enumerate((1, 3, 0, 2)):
                b = r ^ k
                chosen[i] = back_ref[:, b * joint : b * joint + some]

    half = D // 2
    for turn, target in enumerate((away_ref, here_ref)):
        for i, (place, _, yrel) in enumerate(quarters(rep, 1 - turn, 1)):
            lines = slice(yrel * half, (yrel + 1) * half)
            target[place] = nn(normed_t_ref[lines], chosen[2 * turn + i // 2]).astype(BF)


def right_columns_kernel(
    back_ref, attended_ref, normed_t_ref, context_t_ref, away_ref, here_ref, chosen
):
    rep = lax.axis_index("rep")
    joint = 3 * D // 4
    out = D // 4
    some = chosen.shape[2] - out
    for r in range(4):

        @pl.when(rep == r)
        def _():
            for i, k in enumerate((1, 3, 0, 2)):
                b = r ^ k
                chosen[i, :, :some] = back_ref[:, (b + 1) * joint - some : (b + 1) * joint]
                chosen[i, :, some:] = attended_ref[:, b * out : (b + 1) * out]

    half = D // 2
    for turn, target in enumerate((away_ref, here_ref)):
        for i, (place, _, yrel) in enumerate(quarters(rep, 1 - turn)):
            block = 2 * turn + i // 2
            lines = slice(yrel * half, (yrel + 1) * half)
            target[place, :, :some] = nn(normed_t_ref[lines], chosen[block, :, :some]).astype(BF)
            target[place, :, some:] = nn(context_t_ref[lines], chosen[block, :, some:]).astype(BF)


def columns_gradient(name, body, operands):
    tokens = operands[0].shape[0]
    piece = (4, D // 2, D // 2)
    return kernel_call(
        name,
        body,
        [kept(*piece), kept(*piece)],
        (),
        near(*operands),
        [((4, tokens, D // 2), BF)],
        cost(tokens * D * FF),
    )


def token_back_kernel(
    gain_ref,
    unit_ref,
    inverse_ref,
    middle_ref,
    back_ref,
    wj_ref,
    joint_ref,
    out_ref,
    gain2_ref,
    shift2_ref,
    wide_ref,
    narrow_ref,
    token_ref,
    sums_ref,
):
    part, gain1, shift1 = norm_back(
        unit_ref[...], inverse_ref[...], as_row(gain_ref), nt(back_ref[...], wj_ref[...])
    )
    token_ref[...] = middle_ref[...] + part
    line = 0
    rest = (joint_ref, out_ref, gain2_ref, shift2_ref, wide_ref, narrow_ref)
    for value in [gain1, shift1] + [ref[...] for ref in rest]:
        for i in range(value.shape[1] // 128):
            sums_ref[line : line + 1] = value[:, i * 128 : (i + 1) * 128]
            line += 1
    sums_ref[line:] = jnp.zeros((sums_ref.shape[0] - line, 128), F32)


def token_back(gain, unit, inverse, middle, back, wj, sums):
    return kernel_call(
        "token_back",
        token_back_kernel,
        [shape(unit.shape[0], D), shape(ALL_LINES, 128)],
        (),
        (gain, *near(unit, inverse, middle, back, wj), *sums),
        (),
        cost(6 * unit.shape[0] * D * D),
    )


def low_rank_kernel(
    hidden, own_ref, near_ref, wm_ref, down_ref, head_ref, other_ref, box, back
):
    rows = own_ref.shape[0]
    box[:rows] = own_ref[...]
    box[rows:] = near_ref[...]
    part = down_ref.shape[0]
    start = box.shape[1] - D
    rep = lax.axis_index("rep")
    for r in range(D // part):

        @pl.when(rep == r)
        def _():
            for i, b in enumerate((r, r ^ 2)):
                back[i] = box[:, start + b * part : start + (b + 1) * part]

    wide = head_ref.shape[1]
    for i in range(2):
        block = jnp.bitwise_xor(rep, 2 * i)
        here = wm_ref[pl.ds(pl.multiple_of(block * part, SLOT), part), :]
        pooled = nt(box[:, start:], here).astype(BF)
        down = tn(pooled, box[:, :hidden])
        head = tn(back[i], box[:, hidden : hidden + wide])
        if i == 0:
            down_ref[...] = down
            head_ref[...] = head
        else:
            other_ref[:, :hidden] = down.astype(BF)
            other_ref[:, hidden:] = head.astype(BF)


def low_rank(blocks, parts, own, far, wm):
    rows = 2 * own.shape[0]
    hidden, wide, part = FF // blocks, D // blocks, D // parts
    return kernel_call(
        "low_rank",
        functools.partial(low_rank_kernel, hidden),
        [shape(part, hidden), shape(part, wide), shape(part, hidden + wide, dtype=BF)],
        (),
        near(own, far, wm),
        [((rows, own.shape[1]), BF), ((2, rows, part), BF)],
        cost(2 * rows * D * D),
    )


def finish_kernel(groups, *refs):
    up, first, second, lines = (
        [refs[sum(groups[:i]) + n] for n in range(groups[i])] for i in range(4)
    )
    loss_ref, down_ref, head_ref, other_ref = refs[sum(groups) : sum(groups) + 4]
    (
        joint_ref,
        out_ref,
        up_block_ref,
        down_block_ref,
        head_block_ref,
        loss_out_ref,
        *vector_refs,
    ) = refs[sum(groups) + 4 :]

    def total(terms):
        return sum(ref[...].astype(F32) for ref in terms)

    up_sum = total(up)
    for h in range(2):
        lanes = slice(h * up_sum.shape[2], (h + 1) * up_sum.shape[2])
        up_block_ref[:, lanes] = up_sum[h]
    one, two_ = total(first), total(second)
    some = one.shape[1]
    rest = joint_ref.shape[1] - some
    joint_ref[:, :some] = one
    joint_ref[:, some:] = two_[:, :rest]
    out_ref[...] = two_[:, rest:]
    hidden = down_ref.shape[1]
    down_block_ref[...] = down_ref[...] + other_ref[:, :hidden].astype(F32)
    head_block_ref[...] = (head_ref[...] + other_ref[:, hidden:].astype(F32)).T
    loss_out_ref[...] = loss_ref[...].reshape(1)
    vectors = total(lines)
    starts = (GAIN1, SHIFT1, JOINT, OUT, GAIN2, SHIFT2, WIDE, NARROW)
    for start, ref in zip(starts, vector_refs):
        for i in range(ref.shape[0] // 128):
            line = start // 128 + i
            if start == JOINT and i >= D // 128:
                line += D // 128
            ref[pl.ds(i * 128, 128)] = vectors[line]


def finish(up, first, second, vectors, loss, low, joint):
    rows = up[0].shape[1]
    sizes = (D, D, 2 * D, D, D, D, FF, D)
    return kernel_call(
        "finish",
        functools.partial(finish_kernel, [len(v) for v in (up, first, second, vectors)]),
        [
            shape(rows, joint),
            shape(rows, D - joint),
            shape(rows, D),
            shape(*low[0].shape),
            shape(*low[1].shape[::-1]),
            shape(1),
        ]
        + [shape(n) for n in sizes],
        (),
        (*up, *first, *second, *vectors, loss, *low),
    )


def both_pairs(partner):
    dp, rep = lax.axis_size("dp"), lax.axis_size("rep")
    pairs = []
    for i in range(dp):
        for j in range(rep):
            a, b = partner(i, j)
            pairs.append((i * rep + j, a * rep + b))
    return pairs


def exchange(value, partner):
    return lax.ppermute(value, ("dp", "rep"), both_pairs(partner))


def first_turn(i, j):
    return (i, j ^ 2) if j & 1 == 0 else (i ^ 1, j)


def second_turn(i, j):
    return (i ^ 1, j) if j & 1 == 0 else (i, j ^ 2)


def added(a, b):
    return (a.astype(F32) + b.astype(F32)).astype(BF)


def halved(here, got):
    half = here.shape[0] // 2
    return added(here[:half], got[:half]), added(here[half:], got[half:])


def parted(here, got, count):
    rows = here.shape[-2] // count
    parts = [slice(i * rows, (i + 1) * rows) for i in range(count)]
    return [added(here[..., p, :], got[..., p, :]) for p in parts]


def core_turn(i, j):
    return i, j ^ 1


def across(i, j):
    return i, j ^ 2


def group_round(keep, got, group):
    masks = group_masks(group)
    bits = len(group)
    parts = parted(keep, got, len(masks))
    place = [sum(((c >> n) & 1) << (bits - 1 - n) for n in range(bits)) for c in range(len(masks))]
    return [parts[0]] + [
        exchange(parts[place[c]], lambda i, j: (i ^ masks[c][0], j)) for c in range(1, len(masks))
    ]


def row_rounds(keep, got, groups):
    terms = [keep, got]
    for group in groups:
        if len(terms) > 2:
            terms = [terms[0], sum(v.astype(F32) for v in terms[1:])]
        terms = group_round(*terms, group)
    return terms


order = lax.optimization_barrier


def dp_groups():
    bits = [("dp", b) for b in range(1, lax.axis_size("dp").bit_length() - 1)]
    return [bits[i : i + 2] for i in range(0, len(bits), 2)] + [[("dp", 0)]]


def all_groups():
    bits = [("rep", b) for b in range(1, lax.axis_size("rep").bit_length() - 1)]
    groups = dp_groups()
    return groups[:-1] + [groups[-1] + bits, [("rep", 0)]]


def group_masks(group):
    out = [(0, 0)]
    for axis, bit in group:
        out += [(a | 1 << bit, b) if axis == "dp" else (a, b | 1 << bit) for a, b in out]
    return out


def gather_masks(rounds, blocks):
    bits = [0] + list(range(blocks.bit_length() - 2, 0, -1))
    masks, used = [0], 0
    for count in rounds:
        for bit in bits[used : used + count]:
            masks = masks + [m | 1 << bit for m in masks]
        used += count
    return masks


def split_round(value, wide, group):
    blocks = (value.shape[1] - D) // wide
    turns = group_masks(group)
    text = value[:, blocks * wide :]
    pieces = []
    for c, (a, b) in enumerate(turns):
        chosen = [value[:, i * wide : (i + 1) * wide] for i in range(c, blocks, len(turns))]
        piece = jnp.concatenate(chosen + [text], axis=1)
        pieces.append(piece if c == 0 else exchange(piece, lambda i, j: (i ^ a, j ^ b)))
    return pieces


def round_of(value, group):
    return [value] + [
        exchange(value, lambda i, j: (i ^ a, j ^ b)) for a, b in group_masks(group)[1:]
    ]


def relative_rows(value, blocks):
    rows = value.shape[0] // blocks
    if rows % SLOT == 0:
        return value
    bits = blocks.bit_length() - 1
    place = jnp.arange(blocks, dtype=jnp.int32)
    source = jnp.zeros_like(place)
    for bit in range(bits):
        source = source + ((place >> (bits - 1 - bit)) & 1) * (1 << bit)
    source = source ^ lax.axis_index("dp")
    return value.reshape(blocks, rows, -1)[source].reshape(value.shape)


def local(
    incoming_activations,
    caption_final_place,
    paired_picture,
    caption_weight,
    locked_picture_features,
    softmax_heat,
    premix_scaling_factor,
    premix_shift_term,
    stacked_mixing_matrix,
    asking_reading_offsets,
    mixing_result_matrix,
    mixing_result_offset,
    premlp_scaling_factor,
    premlp_shift_term,
    widening_matrix,
    widening_offset,
    narrowing_matrix,
    narrowing_offset,
    caption_mapping_matrix,
    picture_mapping_matrix,
):
    both = ("dp", "rep")
    devices = lax.axis_size(both)
    blocks = lax.axis_size("dp")
    parts = lax.axis_size("rep")
    captions = caption_final_place.shape[0]
    images = locked_picture_features.shape[0]
    groups = all_groups()
    pieces = round_of(jnp.pad(locked_picture_features, ((0, SLOT - images), (0, 0))), groups[0])
    project, normed, unit1, inverse1, place, out, x, wo = project_tokens(
        incoming_activations,
        premix_scaling_factor,
        premix_shift_term,
        asking_reading_offsets,
        stacked_mixing_matrix,
        (
            caption_final_place,
            mixing_result_offset,
            incoming_activations,
            mixing_result_matrix,
        ),
    )
    project, pieces = order((project, pieces))
    for group in groups[1:-1]:
        pieces = round_of(jnp.concatenate(pieces), group)
    att, context, middle, gain2, shift2, wide, narrow, wu, wn, wm = attend_tokens(
        place,
        out,
        x,
        project,
        wo,
        (
            premlp_scaling_factor,
            premlp_shift_term,
            widening_offset,
            narrowing_offset,
            widening_matrix,
            narrowing_matrix,
            caption_mapping_matrix,
        ),
    )
    middle, pieces = order((middle, pieces))
    own, far = round_of(jnp.concatenate(pieces), groups[-1])
    second, unit2, inverse2, upper, box, text, factor, embed, wp, paired, weight = widen_tokens(
        blocks,
        place,
        gain2,
        shift2,
        wide,
        narrow,
        middle,
        wu,
        wn,
        wm,
        (picture_mapping_matrix, paired_picture, caption_weight),
    )
    embed, far = order((embed, far))
    picture, score, row, inverse, stats = contrast(
        images,
        parts,
        sum(groups, []),
        softmax_heat,
        own,
        far,
        wp,
        embed,
        paired,
        weight,
    )
    groups = dp_groups()
    high = [[bit] for group in groups[:-1] for bit in group]
    factor_groups = groups[-1:] + high[::-1]
    stats = round_of(stats, [("rep", 0)])
    normed_t, context_t, second_t = (
        relative_rows(v, blocks) for v in turn_tokens(blocks, normed, context, second)
    )
    stats = round_of(merge(stats), [("rep", 1)] + groups[-1])
    slope = slope_tokens(upper)
    stats, slope = order((stats, slope))
    for group in groups[:-1]:
        stats = round_of(merge(stats), group)
    back, away, here, pooled_back, loss, down_bias, up_bias, *pieces = head_back(
        images,
        [len(group) for group in factor_groups],
        softmax_heat,
        place,
        stats,
        score,
        row,
        inverse,
        weight,
        paired,
        picture,
        text,
        factor,
        wm,
        wn,
        slope,
        second_t,
        box,
    )
    loss = loss / (captions * devices)
    got = exchange(away, core_turn)
    pieces = pieces[:1] + [
        exchange(piece, lambda i, j: (i ^ a, j ^ b))
        for piece, (a, b) in zip(pieces[1:], group_masks(factor_groups[0])[1:])
    ]
    total, attended, context_back, gain2, shift2, out_bias = middle_back(
        place,
        gain2,
        pooled_back,
        back,
        wu,
        unit2,
        inverse2,
        wo,
    )
    context_back, got, pieces = order((context_back, got, pieces))
    up, send = halved(here, got)
    got_up = exchange(send, first_turn)
    pieces = split_round(jnp.concatenate(pieces), box.shape[2], factor_groups[1])
    project_back, joint_bias = attention_back(project, att, context_back)
    project_back, pieces = order((project_back, pieces))
    for group in factor_groups[2:]:
        pieces = split_round(jnp.concatenate(pieces), box.shape[2], group)
    away, here = columns_gradient("left_columns", left_columns_kernel, (project_back, normed_t))
    got = exchange(away, core_turn)
    project_back, away = order((project_back, away))
    away, here2 = columns_gradient(
        "right_columns", right_columns_kernel, (project_back, attended, normed_t, context_t)
    )
    project_back, away, got, got_up = order((project_back, away, got, got_up))
    up, up_send = halved(up, got_up)
    first, send = halved(here, got)
    got = exchange(jnp.concatenate([up_send[0], send]), second_turn)
    got2 = exchange(away, core_turn)
    joint = 3 * D // parts
    token, sums = token_back(
        premix_scaling_factor,
        unit1,
        inverse1,
        total,
        project_back,
        stacked_mixing_matrix,
        (joint_bias, out_bias, gain2, shift2, up_bias, down_bias),
    )
    sums, got2, pieces = order((sums, got2, pieces))
    factors = jnp.concatenate(pieces)
    far = exchange(factors, core_turn)
    lines = round_of(sums, [("rep", 0)])
    lines = round_of(sum(lines), [("rep", 1)])
    second, send2 = halved(here2, got2)
    got, send2, lines, far = order((got, send2, lines, far))
    up, got_up = group_round(up[0], got[:2], high[0])
    first, send = halved(first, got[2:])
    got2 = exchange(jnp.concatenate([send2, send]), first_turn)
    lines = round_of(sum(lines), groups[-1])
    *low, other = low_rank(blocks, parts, factors, far, wm)
    got_up, lines, other = order((got_up, lines, other))
    lines = round_of(sum(lines), high[0])
    got2, lines, other = order((got2, lines, other))
    second, send = halved(second, got2[:2])
    second, first, got = second[0], first[0], got2[2]
    got2 = exchange(send[0], second_turn)
    first, got = group_round(first, got, high[0])
    for group in high[1:]:
        lines = round_of(sum(lines), group)
    for group in high[1:]:
        up, got_up = group_round(up, got_up, group)
    other = exchange(other, across)
    for i, group in enumerate(high):
        if i == 0:
            got, got2, lines = order((got, got2, lines))
        second, got2 = group_round(second, got2, group)
        if i + 1 < len(high):
            first, got = group_round(first, got, high[i + 1])
    first, second, up, vectors = [first, got], [second, got2], [up, got_up], lines
    joint_block, out_block, up_block, down_block, head_block, loss, *grads = finish(
        up, first, second, vectors, loss, (*low, other), joint
    )
    return (
        loss,
        token,
        grads[0],
        grads[1],
        joint_block,
        grads[2],
        out_block,
        grads[3],
        grads[4],
        grads[5],
        up_block,
        grads[6],
        down_block.T,
        grads[7],
        head_block,
    )


def solution(mesh):
    spread = P(("dp", "rep"), None)
    line = P(("dp", "rep"))
    block = P("dp", "rep")
    in_specs = (spread, line, line, line, spread) + (P(),) * 15
    out_specs = (
        P(),
        spread,
        P(),
        P(),
        block,
        P(),
        block,
        P(),
        P(),
        P(),
        block,
        P(),
        block,
        P(),
        block,
    )
    return jax.shard_map(local, mesh=mesh, in_specs=in_specs, out_specs=out_specs, check_vma=False)
```

```python
import functools

import jax
import jax.numpy as jnp
from jax import lax
from jax.experimental import pallas as pl
from jax.experimental.pallas import tpu as pltpu
from jax.sharding import PartitionSpec as P

D = 768
HEADS = 12
HEAD = 64
SEQ = 16
FF = 3072
GROUP = 128
PAIRS = HEADS // 2
SLOT = 16
BF = jnp.bfloat16
F32 = jnp.float32

epsilon = 1e-06
BEND = 0.7978845608028654
CUBE = BEND * 0.044715
negative = -1e30
scale = HEAD ** (-0.5)
LIMIT = 20 * 1024 * 1024

GAIN1, SHIFT1, JOINT, OUT, GAIN2, SHIFT2, WIDE, NARROW = 0, 768, 1536, 3840, 4608, 5376, 6144, 9216
VECTORS = 9984
LINES = VECTORS // 128
ALL_LINES = LINES + -LINES % 8

vmem = pl.BlockSpec(memory_space=pltpu.VMEM)
hbm = pl.BlockSpec(memory_space=pltpu.HBM)
smem = pl.BlockSpec(memory_space=pltpu.SMEM)


def dot(a, b, dims):
    return lax.dot_general(a, b, (dims, ((), ())), preferred_element_type=F32)


def nn(a, b):
    return dot(a, b, ((1,), (0,)))


def nt(a, b):
    return dot(a, b, ((1,), (1,)))


def tn(a, b):
    return dot(a, b, ((0,), (0,)))


def cost(flops):
    return pl.CostEstimate(flops=flops, transcendentals=0, bytes_accessed=0)


def shape(*dims, dtype=F32):
    return jax.ShapeDtypeStruct(dims, dtype)


def kept(*dims, dtype=BF):
    return pltpu.VMEM(dims, dtype)


def near(*values):
    return [pltpu.with_memory_space_constraint(v, pltpu.VMEM) for v in values]


def kernel_call(
    name, body, results, small, operands, scratch=(), estimate=None, limit=LIMIT, far=(), copies=0
):
    semaphores = [pltpu.SemaphoreType.DMA((copies,))] if copies else []
    return pl.pallas_call(
        body,
        out_shape=results,
        in_specs=[smem] * len(small) + [hbm] * len(far) + [vmem] * len(operands),
        out_specs=[vmem] * len(results),
        scratch_shapes=[pltpu.VMEM(s, t) for s, t in scratch] + semaphores,
        compiler_params=pltpu.CompilerParams(vmem_limit_bytes=limit),
        cost_estimate=estimate,
        name=name,
    )(*small, *[pltpu.with_memory_space_constraint(v, pltpu.HBM) for v in far], *operands)


def fetched(values):
    return [kept(*v.shape, dtype=v.dtype) for v in values]


def fetch(sources, targets, semaphores):
    copies = [
        pltpu.make_async_copy(source, target, semaphores.at[i])
        for i, (source, target) in enumerate(zip(sources, targets))
    ]
    for copy in copies:
        copy.start()
    return copies


def iota(dims, axis):
    return lax.broadcasted_iota(jnp.int32, dims, axis)


def norm_parts(values):
    average = jnp.mean(values, axis=-1, keepdims=True)
    centred = values - average
    inverse = lax.rsqrt(jnp.mean(centred * centred, axis=-1, keepdims=True) + epsilon)
    return centred * inverse, inverse


def norm_back(unit, inverse, gain, back):
    inner = back * gain
    part = inverse * (
        inner
        - jnp.mean(inner, axis=-1, keepdims=True)
        - unit * jnp.mean(inner * unit, axis=-1, keepdims=True)
    )
    return part, jnp.sum(back * unit, axis=0, keepdims=True), jnp.sum(back, axis=0, keepdims=True)


def split(value):
    high = value.astype(BF)
    return high, (value - high.astype(F32)).astype(BF)


def two(value):
    return jnp.concatenate(split(value), axis=0)


def as_row(ref):
    return ref[...].reshape(1, ref.shape[0])


def as_column(ref):
    size = ref.shape[0]
    same = iota((size, size), 0) == iota((size, size), 1)
    row = as_row(ref)
    return jnp.sum(jnp.where(same, row, jnp.zeros_like(row)), axis=1, keepdims=True)


def token_limits(ref):
    place = as_row(ref).astype(F32)
    captions = place.shape[1]
    tokens = captions * SEQ
    owner = (iota((tokens, captions), 0) // SEQ == iota((tokens, captions), 1)).astype(F32)
    column = jnp.sum(owner * place, axis=1, keepdims=True)
    line = nt(place.astype(BF), owner.astype(BF))
    return line, column


def pool_mask(line, captions):
    dims = (captions, captions * SEQ)
    token = iota(dims, 1)
    inside = (token % SEQ).astype(F32) <= line
    return jnp.where((token // SEQ == iota(dims, 0)) & inside, 1.0, 0.0)


def spread_mask(column, captions):
    dims = (captions * SEQ, captions)
    token = iota(dims, 0)
    inside = (token % SEQ).astype(F32) <= column
    return jnp.where((token // SEQ == iota(dims, 1)) & inside, 1.0, 0.0)


def head_masks():
    lane = iota((1, 2 * HEAD), 1)
    even = (lane < HEAD).astype(F32)
    return even.astype(BF), (1.0 - even).astype(BF)


def caption_masks():
    lane = iota((SEQ, GROUP), 1) // SEQ
    return [lane == c for c in range(GROUP // SEQ)]


def compact(full, picks):
    out = full[:SEQ]
    for c in range(1, len(picks)):
        out = jnp.where(picks[c], full[c * SEQ : (c + 1) * SEQ], out)
    return out


def expand(low, lows):
    return jnp.concatenate([low * mask for mask in lows], axis=0)


def both_heads(value, masks):
    return jnp.concatenate([value * masks[0], value * masks[1]], axis=0)


def store_permuted(ref, value, dp, blocks):
    rows = value.shape[0] // blocks
    bits = blocks.bit_length() - 1
    if rows % SLOT:
        ref[...] = value
        return
    for b in range(blocks):
        k = jnp.bitwise_xor(dp, b)
        place = 0
        for bit in range(bits):
            place = place + ((k >> bit) & 1) * (1 << (bits - 1 - bit))
        ref[pl.ds(pl.multiple_of(place * rows, SLOT), rows), :] = value[b * rows : (b + 1) * rows]


def box_width(blocks):
    used = (FF + D) // blocks
    return used + -used % 128


def project_kernel(*refs):
    more = (len(refs) - 5 - 4 - 5 - 1) // 2
    mine, other, refs = refs[:5], refs[5 : 5 + more], refs[5 + more :]
    project_ref, normed_ref, unit_ref, inverse_ref = refs[:4]
    targets, (x, gain, shift, joint, wj, semaphores) = refs[4 : 4 + more], refs[4 + more :]
    copies = fetch(mine + other, (x, gain, shift, joint, wj) + targets, semaphores)
    copies[0].wait()
    unit_ref[...], inverse_ref[...] = norm_parts(x[...].astype(F32))
    for copy in copies[1:5]:
        copy.wait()
    normed_ref[...] = (unit_ref[...] * as_row(gain) + as_row(shift)).astype(BF)
    bias = as_row(joint)
    for i, part in enumerate((bias[:, :D], 0.0, bias[:, D:])):
        lanes = slice(i * D, (i + 1) * D)
        project_ref[:, lanes] = (nn(normed_ref[...], wj[:, lanes]) + part).astype(BF)
    for copy in copies[5:]:
        copy.wait()


def project_tokens(x, gain, shift, joint, wj, following):
    tokens = x.shape[0]
    mine = (x, gain, shift, joint, wj)
    return kernel_call(
        "project_tokens",
        project_kernel,
        [
            kept(tokens, 3 * D),
            kept(tokens, D),
            kept(tokens, D, dtype=F32),
            kept(tokens, 1, dtype=F32),
        ]
        + fetched(following),
        (),
        (),
        [(v.shape, v.dtype) for v in mine],
        cost(6 * tokens * D * D),
        far=mine + following,
        copies=5 + len(following),
    )


def turn_kernel(blocks, *refs):
    dp = lax.axis_index("dp")
    count = len(refs) // 2
    for source, target in zip(refs[:count], refs[count:]):
        store_permuted(target, source[...].T, dp, blocks)


def turn_tokens(blocks, *values):
    return kernel_call(
        "turn_tokens",
        functools.partial(turn_kernel, blocks),
        [kept(*v.shape[::-1]) for v in values],
        (),
        near(*values),
        (),
        cost(32 * values[0].shape[0] * D),
    )


def attend_kernel(*refs):
    more = (len(refs) - 5 - 3 - 1) // 2
    far, (place_ref, out_ref, x_ref, project_ref, wo_ref) = refs[:more], refs[more : more + 5]
    att_ref, context_ref, middle_ref = refs[more + 5 : more + 8]
    copies = fetch(far, refs[more + 8 : -1], refs[-1])
    line, _ = token_limits(place_ref)
    masks = head_masks()
    picks = caption_masks()
    lows = [pick.astype(F32).astype(BF) for pick in picks]
    key_place = iota((SEQ, GROUP), 0).astype(F32)

    def attend(h, carry):
        at = pl.multiple_of(h * 2 * HEAD, 128)
        for g in range(x_ref.shape[0] // GROUP):
            here = slice(g * GROUP, (g + 1) * GROUP)
            query = project_ref[here, pl.ds(at, 128)]
            keys = both_heads(project_ref[here, pl.ds(pl.multiple_of(D + at, 128), 128)], masks)
            values = both_heads(
                project_ref[here, pl.ds(pl.multiple_of(2 * D + at, 128), 128)], masks
            )
            scores = nt(keys, query)
            allowed = key_place <= line[:, here]
            parts = []
            for e in range(2):
                score = compact(scores[e * GROUP : (e + 1) * GROUP], picks) * scale
                score = jnp.where(allowed, score, negative)
                score = jnp.exp(score - jnp.max(score, axis=0, keepdims=True))
                weight = score / jnp.sum(score, axis=0, keepdims=True)
                att_ref[2 * h + e, :, here] = weight
                parts.append(expand(weight.astype(BF), lows))
            context_ref[here, pl.ds(at, 128)] = tn(jnp.concatenate(parts, axis=0), values).astype(BF)
        return carry

    lax.fori_loop(0, PAIRS, attend, 0, unroll=3)
    middle_ref[...] = x_ref[...].astype(F32) + (nn(context_ref[...], wo_ref[...]) + as_row(out_ref))
    for copy in copies:
        copy.wait()


def attend_tokens(place, out, x, project, wo, following):
    tokens = x.shape[0]
    return kernel_call(
        "attend_tokens",
        attend_kernel,
        [kept(HEADS, SEQ, tokens, dtype=F32), kept(tokens, D), kept(tokens, D, dtype=F32)]
        + fetched(following),
        (),
        near(place, out, x, project, wo),
        (),
        cost(4 * tokens * D * D),
        far=following,
        copies=len(following),
    )


def widen_kernel(blocks, *refs):
    more = (len(refs) - 9 - 8 - 3 - 1) // 2
    far = refs[:more]
    place_ref, gain_ref, shift_ref, wide_ref, narrow_ref, middle_ref, wu_ref, wn_ref, wm_ref = refs[
        more : more + 9
    ]
    second_ref, unit_ref, inverse_ref, upper_ref, box_ref, text_ref, scale_ref, embed_ref = refs[
        more + 9 : more + 17
    ]
    branch, wide, mean, semaphores = refs[-4:]
    copies = fetch(far, refs[more + 17 : -4], semaphores)
    captions = place_ref.shape[0]
    line, column = token_limits(place_ref)
    pool = pool_mask(line, captions)
    share = 1.0 / jnp.sum(pool, axis=1, keepdims=True)
    unit, inverse_ref[...] = norm_parts(middle_ref[...])
    unit_ref[...] = unit
    second_ref[...] = (unit * as_row(gain_ref) + as_row(shift_ref)).astype(BF)
    branch[...] = jnp.zeros_like(branch)
    wide[...] = as_row(wide_ref)
    pool_low = pool.astype(BF)
    step = 512

    def widen(i, carry):
        at = pl.multiple_of(i * step, 128)
        upper = nn(second_ref[...], wu_ref[:, pl.ds(at, step)]) + wide[:, pl.ds(at, step)]
        active = upper * (0.5 + 0.5 * jnp.tanh(upper * (BEND + CUBE * (upper * upper))))
        upper_ref[:, pl.ds(at, step)] = upper
        parts = two(nn(pool_low, active.astype(BF)) * share)
        mean[:, pl.ds(at, step)] = parts[:captions]
        branch[...] += nn(parts, wn_ref[pl.ds(at, step), :])
        return carry

    lax.fori_loop(0, FF // step, widen, 0, unroll=3)
    inside = jnp.where((iota((captions * SEQ, 1), 0) % SEQ).astype(F32) <= column, 1.0, 0.0)
    weight = inside / (column + 1.0)
    pooled = jnp.sum((middle_ref[...] * weight).reshape(captions, SEQ, D), axis=1)
    pooled = (pooled + (branch[:captions] + branch[captions:] + as_row(narrow_ref))).astype(BF)
    hidden, part = FF // blocks, D // blocks
    for b in range(blocks):
        box_ref[b, :, :hidden] = mean[:, b * hidden : (b + 1) * hidden]
        box_ref[b, :, hidden : hidden + part] = pooled[:, b * part : (b + 1) * part]
    text = nn(pooled, wm_ref[...])
    factor = lax.rsqrt(jnp.sum(text * text, axis=1, keepdims=True) + epsilon)
    text_ref[...] = text
    scale_ref[...] = factor
    embed_ref[...] = (text * factor).astype(BF)
    for copy in copies:
        copy.wait()


def slope_kernel(upper_ref, slope_ref):
    step = 512

    def part(i, carry):
        at = pl.multiple_of(i * step, 128)
        upper = upper_ref[:, pl.ds(at, step)]
        square = upper * upper
        half = 0.5 + 0.5 * jnp.tanh(upper * (BEND + CUBE * square))
        slope_ref[:, pl.ds(at, step)] = (
            half * (1.0 + (upper - upper * half) * (2.0 * BEND + 6.0 * CUBE * square))
        ).astype(BF)
        return carry

    lax.fori_loop(0, FF // step, part, 0)


def slope_tokens(upper):
    return kernel_call(
        "slope_tokens", slope_kernel, [kept(*upper.shape)], (), near(upper), (), cost(upper.size)
    )[0]


def widen_tokens(blocks, place, gain, shift, wide, narrow, middle, wu, wn, wm, following):
    tokens = middle.shape[0]
    captions = place.shape[0]
    return kernel_call(
        "widen_tokens",
        functools.partial(widen_kernel, blocks),
        [
            kept(tokens, D),
            kept(tokens, D, dtype=F32),
            kept(tokens, 1, dtype=F32),
            kept(tokens, FF, dtype=F32),
            kept(blocks, captions, box_width(blocks)),
            kept(captions, D, dtype=F32),
            kept(captions, 1, dtype=F32),
            kept(captions, D),
        ]
        + fetched(following),
        (),
        near(place, gain, shift, wide, narrow, middle, wu, wn, wm),
        [
            ((2 * captions, D), F32),
            ((1, FF), F32),
            ((captions, FF), BF),
        ],
        cost(2 * tokens * D * FF),
        far=following,
        copies=len(following),
    )


def match_of(paired, columns, images):
    column = iota((1, columns), 1)
    valid = column % SLOT < images
    name = jnp.where(valid, (column // SLOT) * images + column % SLOT, -1)
    return paired == name, valid


def contrast_kernel(
    images,
    parts,
    bits,
    heat_ref,
    own_ref,
    near_ref,
    wp_ref,
    embed_ref,
    paired_ref,
    weight_ref,
    picture_ref,
    score_ref,
    row_ref,
    inverse_ref,
    stats_ref,
    features,
):
    half = own_ref.shape[0] // SLOT
    for far, ref in enumerate((own_ref, near_ref)):

        def place(i, carry, far=far, ref=ref):
            p = i + far * half
            index = {axis: lax.axis_index(axis) for axis in ("dp", "rep")}
            for n, (axis, bit) in enumerate(bits):
                index[axis] = jnp.bitwise_xor(index[axis], ((p >> n) & 1) << bit)
            to = pl.ds(pl.multiple_of((index["dp"] * parts + index["rep"]) * SLOT, SLOT), SLOT)
            features[to, :] = ref[pl.ds(pl.multiple_of(i * SLOT, SLOT), SLOT), :]
            return carry

        lax.fori_loop(0, half, place, 0, unroll=4)
    picture = nn(features[...], wp_ref[...])
    picture = (
        picture * lax.rsqrt(jnp.sum(picture * picture, axis=1, keepdims=True) + epsilon)
    ).astype(BF)
    picture_ref[...] = picture
    score = nt(embed_ref[...], picture) / heat_ref[0]
    match, valid = match_of(as_column(paired_ref), score.shape[1], images)
    score = jnp.where(valid, score, negative)
    score_ref[...] = score
    top = jnp.max(score, axis=1, keepdims=True)
    row = jnp.log(jnp.sum(jnp.exp(score - top), axis=1, keepdims=True)) + top
    row_ref[...] = row
    positive = jnp.sum(jnp.where(match, score, 0.0), axis=1, keepdims=True)
    hits = jnp.where(match, 1.0, 0.0)
    counts = jnp.sum(hits, axis=0, keepdims=True)
    inverse = 1.0 / jnp.sum(hits * counts, axis=1, keepdims=True)
    inverse_ref[...] = inverse
    total = jnp.sum(as_column(weight_ref) * (row - positive - positive * inverse))
    best = jnp.max(score, axis=0, keepdims=True)
    mass = jnp.sum(jnp.exp(score - best), axis=0, keepdims=True)
    mass = jnp.where(iota(mass.shape, 1) == images, total, mass)
    wide = best.shape[1] // 4
    rows = [v[:, i * wide : (i + 1) * wide] for v in (best, mass) for i in range(4)]
    stats_ref[...] = jnp.concatenate(rows, axis=0)


def contrast(images, parts, bits, heat, own, far, wp, embed, paired, weight):
    captions = embed.shape[0]
    columns = 2 * own.shape[0]
    return kernel_call(
        "contrast",
        functools.partial(contrast_kernel, images, parts, bits),
        [
            kept(columns, D),
            kept(captions, columns, dtype=F32),
            kept(captions, 1, dtype=F32),
            kept(captions, 1, dtype=F32),
            shape(8, columns // 4),
        ],
        (heat,),
        near(own, far, wp, embed, paired, weight),
        [((columns, D), BF)],
        cost(2 * columns * D * D),
        max(LIMIT, columns * 8192),
    )


def merged(refs):
    best = functools.reduce(jnp.maximum, [ref[:4] for ref in refs])
    mass = sum(ref[4:] * jnp.exp(ref[:4] - best) for ref in refs)
    return best, mass


def merge_kernel(*refs):
    *given, out_ref = refs
    best, mass = merged(given)
    out_ref[...] = jnp.concatenate([best, mass], axis=0)


def merge(stats):
    return kernel_call("merge", merge_kernel, [shape(*stats[0].shape)], (), stats)[0]


def quarters(rep, away, flip=0):
    core = rep & 1
    out = []
    for xrel in range(2):
        for yrel in range(2):
            block = jnp.bitwise_xor(rep, 2 * xrel + away)
            x_first = 1 - core if away == flip else core
            out.append((jnp.where(x_first == 1, 2 * xrel + yrel, 2 * yrel + xrel), block, yrel))
    return out


def head_back_kernel(
    images,
    count_stats,
    rounds,
    heat_ref,
    place_ref,
    score_ref,
    row_ref,
    inverse_ref,
    weight_ref,
    paired_ref,
    picture_ref,
    text_ref,
    scale_ref,
    wm_ref,
    wn_ref,
    slope_ref,
    second_t_ref,
    box_ref,
    *refs,
):
    first = 1 << rounds[0]
    pieces = refs[len(refs) - first :]
    stats = refs[:count_stats]
    (
        back_ref,
        away_ref,
        here_ref,
        pooled_ref,
        loss_ref,
        down_bias_ref,
        up_bias_ref,
    ) = refs[count_stats : len(refs) - first]
    rep = lax.axis_index("rep")
    heat = heat_ref[0]
    captions = place_ref.shape[0]
    line, column = token_limits(place_ref)
    count = jnp.sum(pool_mask(line, captions), axis=1, keepdims=True)
    owner = spread_mask(column, captions).astype(BF)
    owner = jnp.concatenate([owner, owner], axis=1)

    score = score_ref[...]
    match, valid = match_of(as_column(paired_ref), score.shape[1], images)
    best, mass = merged(stats)
    column_log = jnp.log(mass) + best
    column_log = jnp.concatenate([column_log[i : i + 1] for i in range(4)], axis=1)
    loss_ref[...] = mass[:1, images : images + 1] + jnp.sum(
        jnp.where(valid, column_log, 0.0), axis=1, keepdims=True
    )
    weight = as_column(weight_ref)
    graded = (
        weight * jnp.exp(score - row_ref[...])
        + jnp.exp(score - column_log)
        - jnp.where(match, weight * (1.0 + inverse_ref[...]), 0.0)
    )
    graded = jnp.where(valid, graded / heat, 0.0).astype(BF)
    embed_back = nn(graded, picture_ref[...])
    text = text_ref[...]
    factor = scale_ref[...]
    text_dot = jnp.sum(text * embed_back, axis=1, keepdims=True)
    text_back = (factor * embed_back - text * (factor * factor * factor) * text_dot).astype(BF)
    blocks, _, wide = box_ref.shape
    masks = gather_masks(rounds, blocks)
    for c, piece_ref in enumerate(pieces):
        for i in range(blocks // first):
            block = jnp.bitwise_xor(lax.axis_index("dp"), masks[i * first + c])
            piece_ref[:, i * wide : (i + 1) * wide] = box_ref[block]
        piece_ref[:, (blocks // first) * wide :] = text_back
    pooled_back = nt(text_back, wm_ref[...])
    pooled_ref[...] = pooled_back
    branch = (pooled_back / count).astype(BF)
    down_bias_ref[...] = jnp.sum(branch.astype(F32) * count, axis=0, keepdims=True)
    ones = jnp.ones((SLOT, back_ref.shape[0]), BF)
    step = 512

    def widen(i, carry):
        at = pl.multiple_of(i * step, 128)
        part = nn(owner, two(nt(branch, wn_ref[pl.ds(at, step), :])))
        part = (part * slope_ref[:, pl.ds(at, step)].astype(F32)).astype(BF)
        back_ref[:, pl.ds(at, step)] = part
        up_bias_ref[:, pl.ds(at, step)] = nn(ones, part)[:1]
        return carry

    lax.fori_loop(0, FF // step, widen, 0, unroll=3)
    half = second_t_ref.shape[0] // 2
    wide = FF // 4
    for turn, target in enumerate((away_ref, here_ref)):
        for place, block, yrel in quarters(rep, 1 - turn):
            part = nn(
                second_t_ref[yrel * half : (yrel + 1) * half],
                back_ref[:, pl.ds(pl.multiple_of(block * wide, 128), wide)],
            )
            for h in range(2):
                target[place, h] = part[:, h * (wide // 2) : (h + 1) * (wide // 2)].astype(BF)


def head_back(images, rounds, heat, place, stats, score, row, inverse, weight, paired, picture, text,
              factor, wm, wn, slope, second_t, box):
    captions = text.shape[0]
    tokens = slope.shape[0]
    piece = (4, 2, D // 2, FF // 8)
    return kernel_call(
        "head_back",
        functools.partial(head_back_kernel, images, len(stats), rounds),
        [
            kept(tokens, FF),
            kept(*piece),
            kept(*piece),
            kept(captions, D, dtype=F32),
            shape(1, 1),
            shape(1, D),
            shape(1, FF),
        ]
        + [shape(captions, (box.shape[0] >> rounds[0]) * box.shape[2] + D, dtype=BF)] * (1 << rounds[0]),
        (heat,),
        (
            *near(place, score, row, inverse, weight, paired),
            *near(picture, text, factor, wm, wn, slope, second_t, box),
            *stats,
        ),
        (),
        cost(2 * tokens * D * FF),
    )


def middle_back_kernel(
    place_ref,
    gain_ref,
    pooled_ref,
    back_ref,
    wu_ref,
    unit_ref,
    inverse_ref,
    wo_ref,
    total_ref,
    attended_ref,
    context_back_ref,
    gain_back_ref,
    shift_back_ref,
    bias_ref,
):
    captions = place_ref.shape[0]
    line, column = token_limits(place_ref)
    count = jnp.sum(pool_mask(line, captions), axis=1, keepdims=True)
    owner = spread_mask(column, captions).astype(BF)
    owner = jnp.concatenate([owner, owner], axis=1)
    second_back = nt(back_ref[...], wu_ref[...])
    part, gain_back_ref[...], shift_back_ref[...] = norm_back(
        unit_ref[...], inverse_ref[...], as_row(gain_ref), second_back
    )
    total = nn(owner, two(pooled_ref[...] / count)) + part
    total_ref[...] = total
    attended = total.astype(BF)
    attended_ref[...] = attended
    bias_ref[...] = nn(jnp.ones((SLOT, attended.shape[0]), BF), attended)[:1]
    context_back_ref[...] = nt(attended, wo_ref[...]).astype(BF)


def middle_back(place, gain, pooled, back, wu, unit, inverse, wo):
    tokens = back.shape[0]
    return kernel_call(
        "middle_back",
        middle_back_kernel,
        [
            kept(tokens, D, dtype=F32),
            kept(tokens, D),
            kept(tokens, D),
            shape(1, D),
            shape(1, D),
            shape(1, D),
        ],
        (),
        near(place, gain, pooled, back, wu, unit, inverse, wo),
        (),
        cost(2 * tokens * D * (FF + D)),
    )


def attention_back_kernel(project_ref, att_ref, context_back_ref, back_ref, bias_ref):
    masks = head_masks()
    picks = caption_masks()
    lows = [pick.astype(F32).astype(BF) for pick in picks]
    low_scale = jnp.asarray(scale, BF)
    first = iota((GROUP, 2 * HEAD), 1) < HEAD
    tokens = project_ref.shape[0]

    def attend(h, carry):
        at = pl.multiple_of(h * 2 * HEAD, 128)
        at_k = pl.multiple_of(D + at, 128)
        at_v = pl.multiple_of(2 * D + at, 128)
        for g in range(tokens // GROUP):
            span = slice(g * GROUP, (g + 1) * GROUP)
            query = project_ref[span, pl.ds(at, 128)]
            keys = both_heads(project_ref[span, pl.ds(at_k, 128)], masks)
            values = both_heads(project_ref[span, pl.ds(at_v, 128)], masks)
            upper = context_back_ref[span, pl.ds(at, 128)]
            full = nt(values, upper)
            weights, grads = [], []
            for e in range(2):
                weight = att_ref[2 * h + e, :, span]
                part = compact(full[e * GROUP : (e + 1) * GROUP], picks)
                grad = weight * (part - jnp.sum(weight * part, axis=0, keepdims=True))
                weights.append(expand(weight.astype(BF), lows))
                grads.append(expand(grad.astype(BF) * low_scale, lows))
            weights = jnp.concatenate(weights, axis=0)
            grads = jnp.concatenate(grads, axis=0)
            back_ref[span, pl.ds(at, 128)] = tn(grads, keys).astype(BF)
            wide = nn(grads, query)
            back_ref[span, pl.ds(at_k, 128)] = jnp.where(first, wide[:GROUP], wide[GROUP:]).astype(
                BF
            )
            wide = nn(weights, upper)
            back_ref[span, pl.ds(at_v, 128)] = jnp.where(first, wide[:GROUP], wide[GROUP:]).astype(
                BF
            )
        return carry

    lax.fori_loop(0, PAIRS, attend, 0, unroll=3)
    ones = jnp.ones((SLOT, tokens), BF)
    for i in range(3):
        lanes = slice(i * D, (i + 1) * D)
        bias_ref[:, lanes] = nn(ones, back_ref[:, lanes])[:1]


def attention_back(project, att, context_back):
    tokens = project.shape[0]
    return kernel_call(
        "attention_back",
        attention_back_kernel,
        [kept(tokens, 3 * D), shape(1, 3 * D)],
        (),
        near(project, att, context_back),
        (),
        cost(3 * tokens * D * D),
    )


def left_columns_kernel(back_ref, normed_t_ref, away_ref, here_ref, chosen):
    rep = lax.axis_index("rep")
    joint = 3 * D // 4
    some = chosen.shape[2]
    for r in range(4):

        @pl.when(rep == r)
        def _():
            for i, k in enumerate((1, 3, 0, 2)):
                b = r ^ k
                chosen[i] = back_ref[:, b * joint : b * joint + some]

    half = D // 2
    for turn, target in enumerate((away_ref, here_ref)):
        for i, (place, _, yrel) in enumerate(quarters(rep, 1 - turn, 1)):
            lines = slice(yrel * half, (yrel + 1) * half)
            target[place] = nn(normed_t_ref[lines], chosen[2 * turn + i // 2]).astype(BF)


def right_columns_kernel(
    back_ref, attended_ref, normed_t_ref, context_t_ref, away_ref, here_ref, chosen
):
    rep = lax.axis_index("rep")
    joint = 3 * D // 4
    out = D // 4
    some = chosen.shape[2] - out
    for r in range(4):

        @pl.when(rep == r)
        def _():
            for i, k in enumerate((1, 3, 0, 2)):
                b = r ^ k
                chosen[i, :, :some] = back_ref[:, (b + 1) * joint - some : (b + 1) * joint]
                chosen[i, :, some:] = attended_ref[:, b * out : (b + 1) * out]

    half = D // 2
    for turn, target in enumerate((away_ref, here_ref)):
        for i, (place, _, yrel) in enumerate(quarters(rep, 1 - turn)):
            block = 2 * turn + i // 2
            lines = slice(yrel * half, (yrel + 1) * half)
            target[place, :, :some] = nn(normed_t_ref[lines], chosen[block, :, :some]).astype(BF)
            target[place, :, some:] = nn(context_t_ref[lines], chosen[block, :, some:]).astype(BF)


def columns_gradient(name, body, operands):
    tokens = operands[0].shape[0]
    piece = (4, D // 2, D // 2)
    return kernel_call(
        name,
        body,
        [kept(*piece), kept(*piece)],
        (),
        near(*operands),
        [((4, tokens, D // 2), BF)],
        cost(tokens * D * FF),
    )


def token_back_kernel(
    gain_ref,
    unit_ref,
    inverse_ref,
    middle_ref,
    back_ref,
    wj_ref,
    joint_ref,
    out_ref,
    gain2_ref,
    shift2_ref,
    wide_ref,
    narrow_ref,
    token_ref,
    sums_ref,
):
    part, gain1, shift1 = norm_back(
        unit_ref[...], inverse_ref[...], as_row(gain_ref), nt(back_ref[...], wj_ref[...])
    )
    token_ref[...] = middle_ref[...] + part
    line = 0
    rest = (joint_ref, out_ref, gain2_ref, shift2_ref, wide_ref, narrow_ref)
    for value in [gain1, shift1] + [ref[...] for ref in rest]:
        for i in range(value.shape[1] // 128):
            sums_ref[line : line + 1] = value[:, i * 128 : (i + 1) * 128]
            line += 1
    sums_ref[line:] = jnp.zeros((sums_ref.shape[0] - line, 128), F32)


def token_back(gain, unit, inverse, middle, back, wj, sums):
    return kernel_call(
        "token_back",
        token_back_kernel,
        [shape(unit.shape[0], D), shape(ALL_LINES, 128)],
        (),
        (gain, *near(unit, inverse, middle, back, wj), *sums),
        (),
        cost(6 * unit.shape[0] * D * D),
    )


def low_rank_kernel(
    hidden, own_ref, near_ref, wm_ref, down_ref, head_ref, other_ref, box, back
):
    rows = own_ref.shape[0]
    box[:rows] = own_ref[...]
    box[rows:] = near_ref[...]
    part = down_ref.shape[0]
    start = box.shape[1] - D
    rep = lax.axis_index("rep")
    for r in range(D // part):

        @pl.when(rep == r)
        def _():
            for i, b in enumerate((r, r ^ 2)):
                back[i] = box[:, start + b * part : start + (b + 1) * part]

    wide = head_ref.shape[1]
    for i in range(2):
        block = jnp.bitwise_xor(rep, 2 * i)
        here = wm_ref[pl.ds(pl.multiple_of(block * part, SLOT), part), :]
        pooled = nt(box[:, start:], here).astype(BF)
        down = tn(pooled, box[:, :hidden])
        head = tn(back[i], box[:, hidden : hidden + wide])
        if i == 0:
            down_ref[...] = down
            head_ref[...] = head
        else:
            other_ref[:, :hidden] = down.astype(BF)
            other_ref[:, hidden:] = head.astype(BF)


def low_rank(blocks, parts, own, far, wm):
    rows = 2 * own.shape[0]
    hidden, wide, part = FF // blocks, D // blocks, D // parts
    return kernel_call(
        "low_rank",
        functools.partial(low_rank_kernel, hidden),
        [shape(part, hidden), shape(part, wide), shape(part, hidden + wide, dtype=BF)],
        (),
        near(own, far, wm),
        [((rows, own.shape[1]), BF), ((2, rows, part), BF)],
        cost(2 * rows * D * D),
    )


def finish_kernel(groups, *refs):
    up, first, second, lines = (
        [refs[sum(groups[:i]) + n] for n in range(groups[i])] for i in range(4)
    )
    loss_ref, down_ref, head_ref, other_ref = refs[sum(groups) : sum(groups) + 4]
    (
        joint_ref,
        out_ref,
        up_block_ref,
        down_block_ref,
        head_block_ref,
        loss_out_ref,
        *vector_refs,
    ) = refs[sum(groups) + 4 :]

    def total(terms):
        return sum(ref[...].astype(F32) for ref in terms)

    up_sum = total(up)
    for h in range(2):
        lanes = slice(h * up_sum.shape[2], (h + 1) * up_sum.shape[2])
        up_block_ref[:, lanes] = up_sum[h]
    one, two_ = total(first), total(second)
    some = one.shape[1]
    rest = joint_ref.shape[1] - some
    joint_ref[:, :some] = one
    joint_ref[:, some:] = two_[:, :rest]
    out_ref[...] = two_[:, rest:]
    hidden = down_ref.shape[1]
    down_block_ref[...] = down_ref[...] + other_ref[:, :hidden].astype(F32)
    head_block_ref[...] = (head_ref[...] + other_ref[:, hidden:].astype(F32)).T
    loss_out_ref[...] = loss_ref[...].reshape(1)
    vectors = total(lines)
    starts = (GAIN1, SHIFT1, JOINT, OUT, GAIN2, SHIFT2, WIDE, NARROW)
    for start, ref in zip(starts, vector_refs):
        for i in range(ref.shape[0] // 128):
            line = start // 128 + i
            if start == JOINT and i >= D // 128:
                line += D // 128
            ref[pl.ds(i * 128, 128)] = vectors[line]


def finish(up, first, second, vectors, loss, low, joint):
    rows = up[0].shape[1]
    sizes = (D, D, 2 * D, D, D, D, FF, D)
    return kernel_call(
        "finish",
        functools.partial(finish_kernel, [len(v) for v in (up, first, second, vectors)]),
        [
            shape(rows, joint),
            shape(rows, D - joint),
            shape(rows, D),
            shape(*low[0].shape),
            shape(*low[1].shape[::-1]),
            shape(1),
        ]
        + [shape(n) for n in sizes],
        (),
        (*up, *first, *second, *vectors, loss, *low),
    )


def both_pairs(partner):
    dp, rep = lax.axis_size("dp"), lax.axis_size("rep")
    pairs = []
    for i in range(dp):
        for j in range(rep):
            a, b = partner(i, j)
            pairs.append((i * rep + j, a * rep + b))
    return pairs


def exchange(value, partner):
    return lax.ppermute(value, ("dp", "rep"), both_pairs(partner))


def first_turn(i, j):
    return (i, j ^ 2) if j & 1 == 0 else (i ^ 1, j)


def second_turn(i, j):
    return (i ^ 1, j) if j & 1 == 0 else (i, j ^ 2)


def added(a, b):
    return (a.astype(F32) + b.astype(F32)).astype(BF)


def halved(here, got):
    half = here.shape[0] // 2
    return added(here[:half], got[:half]), added(here[half:], got[half:])


def parted(here, got, count):
    rows = here.shape[-2] // count
    parts = [slice(i * rows, (i + 1) * rows) for i in range(count)]
    return [added(here[..., p, :], got[..., p, :]) for p in parts]


def core_turn(i, j):
    return i, j ^ 1


def across(i, j):
    return i, j ^ 2


def group_round(keep, got, group):
    masks = group_masks(group)
    bits = len(group)
    parts = parted(keep, got, len(masks))
    place = [sum(((c >> n) & 1) << (bits - 1 - n) for n in range(bits)) for c in range(len(masks))]
    return [parts[0]] + [
        exchange(parts[place[c]], lambda i, j: (i ^ masks[c][0], j)) for c in range(1, len(masks))
    ]


def row_rounds(keep, got, groups):
    terms = [keep, got]
    for group in groups:
        if len(terms) > 2:
            terms = [terms[0], sum(v.astype(F32) for v in terms[1:])]
        terms = group_round(*terms, group)
    return terms


order = lax.optimization_barrier


def dp_groups():
    bits = [("dp", b) for b in range(1, lax.axis_size("dp").bit_length() - 1)]
    return [bits[i : i + 2] for i in range(0, len(bits), 2)] + [[("dp", 0)]]


def all_groups():
    bits = [("rep", b) for b in range(1, lax.axis_size("rep").bit_length() - 1)]
    groups = dp_groups()
    return groups[:-1] + [groups[-1] + bits, [("rep", 0)]]


def group_masks(group):
    out = [(0, 0)]
    for axis, bit in group:
        out += [(a | 1 << bit, b) if axis == "dp" else (a, b | 1 << bit) for a, b in out]
    return out


def gather_masks(rounds, blocks):
    bits = [0] + list(range(blocks.bit_length() - 2, 0, -1))
    masks, used = [0], 0
    for count in rounds:
        for bit in bits[used : used + count]:
            masks = masks + [m | 1 << bit for m in masks]
        used += count
    return masks


def split_round(value, wide, group):
    blocks = (value.shape[1] - D) // wide
    turns = group_masks(group)
    text = value[:, blocks * wide :]
    pieces = []
    for c, (a, b) in enumerate(turns):
        chosen = [value[:, i * wide : (i + 1) * wide] for i in range(c, blocks, len(turns))]
        piece = jnp.concatenate(chosen + [text], axis=1)
        pieces.append(piece if c == 0 else exchange(piece, lambda i, j: (i ^ a, j ^ b)))
    return pieces


def round_of(value, group):
    return [value] + [
        exchange(value, lambda i, j: (i ^ a, j ^ b)) for a, b in group_masks(group)[1:]
    ]


def relative_rows(value, blocks):
    rows = value.shape[0] // blocks
    if rows % SLOT == 0:
        return value
    bits = blocks.bit_length() - 1
    place = jnp.arange(blocks, dtype=jnp.int32)
    source = jnp.zeros_like(place)
    for bit in range(bits):
        source = source + ((place >> (bits - 1 - bit)) & 1) * (1 << bit)
    source = source ^ lax.axis_index("dp")
    return value.reshape(blocks, rows, -1)[source].reshape(value.shape)


def local(
    incoming_activations,
    caption_final_place,
    paired_picture,
    caption_weight,
    locked_picture_features,
    softmax_heat,
    premix_scaling_factor,
    premix_shift_term,
    stacked_mixing_matrix,
    asking_reading_offsets,
    mixing_result_matrix,
    mixing_result_offset,
    premlp_scaling_factor,
    premlp_shift_term,
    widening_matrix,
    widening_offset,
    narrowing_matrix,
    narrowing_offset,
    caption_mapping_matrix,
    picture_mapping_matrix,
):
    both = ("dp", "rep")
    devices = lax.axis_size(both)
    blocks = lax.axis_size("dp")
    parts = lax.axis_size("rep")
    captions = caption_final_place.shape[0]
    images = locked_picture_features.shape[0]
    groups = all_groups()
    pieces = round_of(jnp.pad(locked_picture_features, ((0, SLOT - images), (0, 0))), groups[0])
    project, normed, unit1, inverse1, place, out, x, wo = project_tokens(
        incoming_activations,
        premix_scaling_factor,
        premix_shift_term,
        asking_reading_offsets,
        stacked_mixing_matrix,
        (
            caption_final_place,
            mixing_result_offset,
            incoming_activations,
            mixing_result_matrix,
        ),
    )
    project, pieces = order((project, pieces))
    for group in groups[1:-1]:
        pieces = round_of(jnp.concatenate(pieces), group)
    att, context, middle, gain2, shift2, wide, narrow, wu, wn, wm = attend_tokens(
        place,
        out,
        x,
        project,
        wo,
        (
            premlp_scaling_factor,
            premlp_shift_term,
            widening_offset,
            narrowing_offset,
            widening_matrix,
            narrowing_matrix,
            caption_mapping_matrix,
        ),
    )
    middle, pieces = order((middle, pieces))
    own, far = round_of(jnp.concatenate(pieces), groups[-1])
    second, unit2, inverse2, upper, box, text, factor, embed, wp, paired, weight = widen_tokens(
        blocks,
        place,
        gain2,
        shift2,
        wide,
        narrow,
        middle,
        wu,
        wn,
        wm,
        (picture_mapping_matrix, paired_picture, caption_weight),
    )
    embed, far = order((embed, far))
    picture, score, row, inverse, stats = contrast(
        images,
        parts,
        sum(groups, []),
        softmax_heat,
        own,
        far,
        wp,
        embed,
        paired,
        weight,
    )
    groups = dp_groups()
    high = [[bit] for group in groups[:-1] for bit in group]
    factor_groups = groups[-1:] + high[::-1]
    stats = round_of(stats, [("rep", 0)])
    normed_t, context_t, second_t = (
        relative_rows(v, blocks) for v in turn_tokens(blocks, normed, context, second)
    )
    stats = round_of(merge(stats), [("rep", 1)] + groups[-1])
    slope = slope_tokens(upper)
    stats, slope = order((stats, slope))
    for group in groups[:-1]:
        stats = round_of(merge(stats), group)
    back, away, here, pooled_back, loss, down_bias, up_bias, *pieces = head_back(
        images,
        [len(group) for group in factor_groups],
        softmax_heat,
        place,
        stats,
        score,
        row,
        inverse,
        weight,
        paired,
        picture,
        text,
        factor,
        wm,
        wn,
        slope,
        second_t,
        box,
    )
    loss = loss / (captions * devices)
    got = exchange(away, core_turn)
    pieces = pieces[:1] + [
        exchange(piece, lambda i, j: (i ^ a, j ^ b))
        for piece, (a, b) in zip(pieces[1:], group_masks(factor_groups[0])[1:])
    ]
    total, attended, context_back, gain2, shift2, out_bias = middle_back(
        place,
        gain2,
        pooled_back,
        back,
        wu,
        unit2,
        inverse2,
        wo,
    )
    context_back, got, pieces = order((context_back, got, pieces))
    up, send = halved(here, got)
    got_up = exchange(send, first_turn)
    pieces = split_round(jnp.concatenate(pieces), box.shape[2], factor_groups[1])
    project_back, joint_bias = attention_back(project, att, context_back)
    project_back, pieces = order((project_back, pieces))
    for group in factor_groups[2:]:
        pieces = split_round(jnp.concatenate(pieces), box.shape[2], group)
    away, here = columns_gradient("left_columns", left_columns_kernel, (project_back, normed_t))
    got = exchange(away, core_turn)
    project_back, away = order((project_back, away))
    away, here2 = columns_gradient(
        "right_columns", right_columns_kernel, (project_back, attended, normed_t, context_t)
    )
    project_back, away, got, got_up = order((project_back, away, got, got_up))
    up, up_send = halved(up, got_up)
    first, send = halved(here, got)
    got = exchange(jnp.concatenate([up_send[0], send]), second_turn)
    got2 = exchange(away, core_turn)
    joint = 3 * D // parts
    token, sums = token_back(
        premix_scaling_factor,
        unit1,
        inverse1,
        total,
        project_back,
        stacked_mixing_matrix,
        (joint_bias, out_bias, gain2, shift2, up_bias, down_bias),
    )
    sums, got2, pieces = order((sums, got2, pieces))
    factors = jnp.concatenate(pieces)
    far = exchange(factors, core_turn)
    lines = round_of(sums, [("rep", 0)])
    lines = round_of(sum(lines), [("rep", 1)])
    second, send2 = halved(here2, got2)
    got, send2, lines, far = order((got, send2, lines, far))
    up, got_up = group_round(up[0], got[:2], high[0])
    first, send = halved(first, got[2:])
    got2 = exchange(jnp.concatenate([send2, send]), first_turn)
    lines = round_of(sum(lines), groups[-1])
    *low, other = low_rank(blocks, parts, factors, far, wm)
    got_up, lines, other = order((got_up, lines, other))
    lines = round_of(sum(lines), high[0])
    got2, lines, other = order((got2, lines, other))
    second, send = halved(second, got2[:2])
    second, first, got = second[0], first[0], got2[2]
    got2 = exchange(send[0], second_turn)
    first, got = group_round(first, got, high[0])
    for group in high[1:]:
        lines = round_of(sum(lines), group)
    for group in high[1:]:
        up, got_up = group_round(up, got_up, group)
    other = exchange(other, across)
    got, got2, lines = order((got, got2, lines))
    second, got2 = group_round(second, got2, high[0])
    got, got2, got_up, other = order((got, got2, got_up, other))
    for ((_, bit),) in high[1:]:
        one, two_ = parted(first, got, 2), parted(second, got2, 2)
        rows = one[1].shape[0]
        got = exchange(jnp.concatenate([one[1], two_[1]]), lambda i, j: (i ^ (1 << bit), j))
        first, second, got, got2 = one[0], two_[0], got[:rows], got[rows:]
    first, second, up, vectors = [first, got], [second, got2], [up, got_up], lines
    joint_block, out_block, up_block, down_block, head_block, loss, *grads = finish(
        up, first, second, vectors, loss, (*low, other), joint
    )
    return (
        loss,
        token,
        grads[0],
        grads[1],
        joint_block,
        grads[2],
        out_block,
        grads[3],
        grads[4],
        grads[5],
        up_block,
        grads[6],
        down_block.T,
        grads[7],
        head_block,
    )


def solution(mesh):
    spread = P(("dp", "rep"), None)
    line = P(("dp", "rep"))
    block = P("dp", "rep")
    in_specs = (spread, line, line, line, spread) + (P(),) * 15
    out_specs = (
        P(),
        spread,
        P(),
        P(),
        block,
        P(),
        block,
        P(),
        P(),
        P(),
        block,
        P(),
        block,
        P(),
        block,
    )
    return jax.shard_map(local, mesh=mesh, in_specs=in_specs, out_specs=out_specs, check_vma=False)
```

```python
import functools

import jax
import jax.numpy as jnp
from jax import lax
from jax.experimental import pallas as pl
from jax.experimental.pallas import tpu as pltpu
from jax.sharding import PartitionSpec as P

D = 768
HEADS = 12
HEAD = 64
SEQ = 16
FF = 3072
GROUP = 128
PAIRS = HEADS // 2
SLOT = 16
BF = jnp.bfloat16
F32 = jnp.float32

epsilon = 1e-06
BEND = 0.7978845608028654
CUBE = BEND * 0.044715
negative = -1e30
scale = HEAD ** (-0.5)
LIMIT = 20 * 1024 * 1024

GAIN1, SHIFT1, JOINT, OUT, GAIN2, SHIFT2, WIDE, NARROW = 0, 768, 1536, 3840, 4608, 5376, 6144, 9216
VECTORS = 9984
LINES = VECTORS // 128
ALL_LINES = LINES + -LINES % 8

vmem = pl.BlockSpec(memory_space=pltpu.VMEM)
hbm = pl.BlockSpec(memory_space=pltpu.HBM)
smem = pl.BlockSpec(memory_space=pltpu.SMEM)


def dot(a, b, dims):
    return lax.dot_general(a, b, (dims, ((), ())), preferred_element_type=F32)


def nn(a, b):
    return dot(a, b, ((1,), (0,)))


def nt(a, b):
    return dot(a, b, ((1,), (1,)))


def tn(a, b):
    return dot(a, b, ((0,), (0,)))


def cost(flops):
    return pl.CostEstimate(flops=flops, transcendentals=0, bytes_accessed=0)


def shape(*dims, dtype=F32):
    return jax.ShapeDtypeStruct(dims, dtype)


def kept(*dims, dtype=BF):
    return pltpu.VMEM(dims, dtype)


def near(*values):
    return [pltpu.with_memory_space_constraint(v, pltpu.VMEM) for v in values]


def kernel_call(
    name, body, results, small, operands, scratch=(), estimate=None, limit=LIMIT, far=(), copies=0
):
    semaphores = [pltpu.SemaphoreType.DMA((copies,))] if copies else []
    return pl.pallas_call(
        body,
        out_shape=results,
        in_specs=[smem] * len(small) + [hbm] * len(far) + [vmem] * len(operands),
        out_specs=[vmem] * len(results),
        scratch_shapes=[pltpu.VMEM(s, t) for s, t in scratch] + semaphores,
        compiler_params=pltpu.CompilerParams(vmem_limit_bytes=limit),
        cost_estimate=estimate,
        name=name,
    )(*small, *[pltpu.with_memory_space_constraint(v, pltpu.HBM) for v in far], *operands)


def fetched(values):
    return [kept(*v.shape, dtype=v.dtype) for v in values]


def fetch(sources, targets, semaphores):
    copies = [
        pltpu.make_async_copy(source, target, semaphores.at[i])
        for i, (source, target) in enumerate(zip(sources, targets))
    ]
    for copy in copies:
        copy.start()
    return copies


def iota(dims, axis):
    return lax.broadcasted_iota(jnp.int32, dims, axis)


def norm_parts(values):
    average = jnp.mean(values, axis=-1, keepdims=True)
    centred = values - average
    inverse = lax.rsqrt(jnp.mean(centred * centred, axis=-1, keepdims=True) + epsilon)
    return centred * inverse, inverse


def norm_back(unit, inverse, gain, back):
    inner = back * gain
    part = inverse * (
        inner
        - jnp.mean(inner, axis=-1, keepdims=True)
        - unit * jnp.mean(inner * unit, axis=-1, keepdims=True)
    )
    return part, jnp.sum(back * unit, axis=0, keepdims=True), jnp.sum(back, axis=0, keepdims=True)


def split(value):
    high = value.astype(BF)
    return high, (value - high.astype(F32)).astype(BF)


def two(value):
    return jnp.concatenate(split(value), axis=0)


def as_row(ref):
    return ref[...].reshape(1, ref.shape[0])


def as_column(ref):
    size = ref.shape[0]
    same = iota((size, size), 0) == iota((size, size), 1)
    row = as_row(ref)
    return jnp.sum(jnp.where(same, row, jnp.zeros_like(row)), axis=1, keepdims=True)


def token_limits(ref):
    place = as_row(ref).astype(F32)
    captions = place.shape[1]
    tokens = captions * SEQ
    owner = (iota((tokens, captions), 0) // SEQ == iota((tokens, captions), 1)).astype(F32)
    column = jnp.sum(owner * place, axis=1, keepdims=True)
    line = nt(place.astype(BF), owner.astype(BF))
    return line, column


def pool_mask(line, captions):
    dims = (captions, captions * SEQ)
    token = iota(dims, 1)
    inside = (token % SEQ).astype(F32) <= line
    return jnp.where((token // SEQ == iota(dims, 0)) & inside, 1.0, 0.0)


def spread_mask(column, captions):
    dims = (captions * SEQ, captions)
    token = iota(dims, 0)
    inside = (token % SEQ).astype(F32) <= column
    return jnp.where((token // SEQ == iota(dims, 1)) & inside, 1.0, 0.0)


def head_masks():
    lane = iota((1, 2 * HEAD), 1)
    even = (lane < HEAD).astype(F32)
    return even.astype(BF), (1.0 - even).astype(BF)


def caption_masks():
    lane = iota((SEQ, GROUP), 1) // SEQ
    return [lane == c for c in range(GROUP // SEQ)]


def compact(full, picks):
    out = full[:SEQ]
    for c in range(1, len(picks)):
        out = jnp.where(picks[c], full[c * SEQ : (c + 1) * SEQ], out)
    return out


def expand(low, lows):
    return jnp.concatenate([low * mask for mask in lows], axis=0)


def both_heads(value, masks):
    return jnp.concatenate([value * masks[0], value * masks[1]], axis=0)


def store_permuted(ref, value, dp, blocks):
    rows = value.shape[0] // blocks
    bits = blocks.bit_length() - 1
    if rows % SLOT:
        ref[...] = value
        return
    for b in range(blocks):
        k = jnp.bitwise_xor(dp, b)
        place = 0
        for bit in range(bits):
            place = place + ((k >> bit) & 1) * (1 << (bits - 1 - bit))
        ref[pl.ds(pl.multiple_of(place * rows, SLOT), rows), :] = value[b * rows : (b + 1) * rows]


def box_width(blocks):
    used = (FF + D) // blocks
    return used + -used % 128


def project_kernel(*refs):
    more = (len(refs) - 5 - 4 - 5 - 1) // 2
    mine, other, refs = refs[:5], refs[5 : 5 + more], refs[5 + more :]
    project_ref, normed_ref, unit_ref, inverse_ref = refs[:4]
    targets, (x, gain, shift, joint, wj, semaphores) = refs[4 : 4 + more], refs[4 + more :]
    copies = fetch(mine + other, (x, gain, shift, joint, wj) + targets, semaphores)
    copies[0].wait()
    unit_ref[...], inverse_ref[...] = norm_parts(x[...].astype(F32))
    for copy in copies[1:5]:
        copy.wait()
    normed_ref[...] = (unit_ref[...] * as_row(gain) + as_row(shift)).astype(BF)
    bias = as_row(joint)
    for i, part in enumerate((bias[:, :D], 0.0, bias[:, D:])):
        lanes = slice(i * D, (i + 1) * D)
        project_ref[:, lanes] = (nn(normed_ref[...], wj[:, lanes]) + part).astype(BF)
    for copy in copies[5:]:
        copy.wait()


def project_tokens(x, gain, shift, joint, wj, following):
    tokens = x.shape[0]
    mine = (x, gain, shift, joint, wj)
    return kernel_call(
        "project_tokens",
        project_kernel,
        [
            kept(tokens, 3 * D),
            kept(tokens, D),
            kept(tokens, D, dtype=F32),
            kept(tokens, 1, dtype=F32),
        ]
        + fetched(following),
        (),
        (),
        [(v.shape, v.dtype) for v in mine],
        cost(6 * tokens * D * D),
        far=mine + following,
        copies=5 + len(following),
    )


def turn_kernel(blocks, *refs):
    dp = lax.axis_index("dp")
    count = len(refs) // 2
    for source, target in zip(refs[:count], refs[count:]):
        store_permuted(target, source[...].T, dp, blocks)


def turn_tokens(blocks, *values):
    return kernel_call(
        "turn_tokens",
        functools.partial(turn_kernel, blocks),
        [kept(*v.shape[::-1]) for v in values],
        (),
        near(*values),
        (),
        cost(32 * values[0].shape[0] * D),
    )


def attend_kernel(*refs):
    more = (len(refs) - 5 - 3 - 1) // 2
    far, (place_ref, out_ref, x_ref, project_ref, wo_ref) = refs[:more], refs[more : more + 5]
    att_ref, context_ref, middle_ref = refs[more + 5 : more + 8]
    copies = fetch(far, refs[more + 8 : -1], refs[-1])
    line, _ = token_limits(place_ref)
    masks = head_masks()
    picks = caption_masks()
    lows = [pick.astype(F32).astype(BF) for pick in picks]
    key_place = iota((SEQ, GROUP), 0).astype(F32)

    def attend(h, carry):
        at = pl.multiple_of(h * 2 * HEAD, 128)
        for g in range(x_ref.shape[0] // GROUP):
            here = slice(g * GROUP, (g + 1) * GROUP)
            query = project_ref[here, pl.ds(at, 128)]
            keys = both_heads(project_ref[here, pl.ds(pl.multiple_of(D + at, 128), 128)], masks)
            values = both_heads(
                project_ref[here, pl.ds(pl.multiple_of(2 * D + at, 128), 128)], masks
            )
            scores = nt(keys, query)
            allowed = key_place <= line[:, here]
            parts = []
            for e in range(2):
                score = compact(scores[e * GROUP : (e + 1) * GROUP], picks) * scale
                score = jnp.where(allowed, score, negative)
                score = jnp.exp(score - jnp.max(score, axis=0, keepdims=True))
                weight = score / jnp.sum(score, axis=0, keepdims=True)
                att_ref[2 * h + e, :, here] = weight
                parts.append(expand(weight.astype(BF), lows))
            context_ref[here, pl.ds(at, 128)] = tn(jnp.concatenate(parts, axis=0), values).astype(BF)
        return carry

    lax.fori_loop(0, PAIRS, attend, 0, unroll=3)
    middle_ref[...] = x_ref[...].astype(F32) + (nn(context_ref[...], wo_ref[...]) + as_row(out_ref))
    for copy in copies:
        copy.wait()


def attend_tokens(place, out, x, project, wo, following):
    tokens = x.shape[0]
    return kernel_call(
        "attend_tokens",
        attend_kernel,
        [kept(HEADS, SEQ, tokens, dtype=F32), kept(tokens, D), kept(tokens, D, dtype=F32)]
        + fetched(following),
        (),
        near(place, out, x, project, wo),
        (),
        cost(4 * tokens * D * D),
        far=following,
        copies=len(following),
    )


def widen_kernel(blocks, *refs):
    more = (len(refs) - 9 - 8 - 3 - 1) // 2
    far = refs[:more]
    place_ref, gain_ref, shift_ref, wide_ref, narrow_ref, middle_ref, wu_ref, wn_ref, wm_ref = refs[
        more : more + 9
    ]
    second_ref, unit_ref, inverse_ref, upper_ref, box_ref, text_ref, scale_ref, embed_ref = refs[
        more + 9 : more + 17
    ]
    branch, wide, mean, semaphores = refs[-4:]
    copies = fetch(far, refs[more + 17 : -4], semaphores)
    captions = place_ref.shape[0]
    line, column = token_limits(place_ref)
    pool = pool_mask(line, captions)
    share = 1.0 / jnp.sum(pool, axis=1, keepdims=True)
    unit, inverse_ref[...] = norm_parts(middle_ref[...])
    unit_ref[...] = unit
    second_ref[...] = (unit * as_row(gain_ref) + as_row(shift_ref)).astype(BF)
    branch[...] = jnp.zeros_like(branch)
    wide[...] = as_row(wide_ref)
    pool_low = pool.astype(BF)
    step = 512

    def widen(i, carry):
        at = pl.multiple_of(i * step, 128)
        upper = nn(second_ref[...], wu_ref[:, pl.ds(at, step)]) + wide[:, pl.ds(at, step)]
        active = upper * (0.5 + 0.5 * jnp.tanh(upper * (BEND + CUBE * (upper * upper))))
        upper_ref[:, pl.ds(at, step)] = upper
        parts = two(nn(pool_low, active.astype(BF)) * share)
        mean[:, pl.ds(at, step)] = parts[:captions]
        branch[...] += nn(parts, wn_ref[pl.ds(at, step), :])
        return carry

    lax.fori_loop(0, FF // step, widen, 0, unroll=3)
    inside = jnp.where((iota((captions * SEQ, 1), 0) % SEQ).astype(F32) <= column, 1.0, 0.0)
    weight = inside / (column + 1.0)
    pooled = jnp.sum((middle_ref[...] * weight).reshape(captions, SEQ, D), axis=1)
    pooled = (pooled + (branch[:captions] + branch[captions:] + as_row(narrow_ref))).astype(BF)
    hidden, part = FF // blocks, D // blocks
    for b in range(blocks):
        box_ref[b, :, :hidden] = mean[:, b * hidden : (b + 1) * hidden]
        box_ref[b, :, hidden : hidden + part] = pooled[:, b * part : (b + 1) * part]
    text = nn(pooled, wm_ref[...])
    factor = lax.rsqrt(jnp.sum(text * text, axis=1, keepdims=True) + epsilon)
    text_ref[...] = text
    scale_ref[...] = factor
    embed_ref[...] = (text * factor).astype(BF)
    for copy in copies:
        copy.wait()


def slope_kernel(upper_ref, slope_ref):
    step = 512

    def part(i, carry):
        at = pl.multiple_of(i * step, 128)
        upper = upper_ref[:, pl.ds(at, step)]
        square = upper * upper
        half = 0.5 + 0.5 * jnp.tanh(upper * (BEND + CUBE * square))
        slope_ref[:, pl.ds(at, step)] = (
            half * (1.0 + (upper - upper * half) * (2.0 * BEND + 6.0 * CUBE * square))
        ).astype(BF)
        return carry

    lax.fori_loop(0, FF // step, part, 0)


def slope_tokens(upper):
    return kernel_call(
        "slope_tokens", slope_kernel, [kept(*upper.shape)], (), near(upper), (), cost(upper.size)
    )[0]


def widen_tokens(blocks, place, gain, shift, wide, narrow, middle, wu, wn, wm, following):
    tokens = middle.shape[0]
    captions = place.shape[0]
    return kernel_call(
        "widen_tokens",
        functools.partial(widen_kernel, blocks),
        [
            kept(tokens, D),
            kept(tokens, D, dtype=F32),
            kept(tokens, 1, dtype=F32),
            kept(tokens, FF, dtype=F32),
            kept(blocks, captions, box_width(blocks)),
            kept(captions, D, dtype=F32),
            kept(captions, 1, dtype=F32),
            kept(captions, D),
        ]
        + fetched(following),
        (),
        near(place, gain, shift, wide, narrow, middle, wu, wn, wm),
        [
            ((2 * captions, D), F32),
            ((1, FF), F32),
            ((captions, FF), BF),
        ],
        cost(2 * tokens * D * FF),
        far=following,
        copies=len(following),
    )


def match_of(paired, columns, images):
    column = iota((1, columns), 1)
    valid = column % SLOT < images
    name = jnp.where(valid, (column // SLOT) * images + column % SLOT, -1)
    return paired == name, valid


def contrast_kernel(
    images,
    parts,
    bits,
    heat_ref,
    own_ref,
    near_ref,
    wp_ref,
    embed_ref,
    paired_ref,
    weight_ref,
    picture_ref,
    score_ref,
    row_ref,
    inverse_ref,
    stats_ref,
    features,
):
    half = own_ref.shape[0] // SLOT
    for far, ref in enumerate((own_ref, near_ref)):

        def place(i, carry, far=far, ref=ref):
            p = i + far * half
            index = {axis: lax.axis_index(axis) for axis in ("dp", "rep")}
            for n, (axis, bit) in enumerate(bits):
                index[axis] = jnp.bitwise_xor(index[axis], ((p >> n) & 1) << bit)
            to = pl.ds(pl.multiple_of((index["dp"] * parts + index["rep"]) * SLOT, SLOT), SLOT)
            features[to, :] = ref[pl.ds(pl.multiple_of(i * SLOT, SLOT), SLOT), :]
            return carry

        lax.fori_loop(0, half, place, 0, unroll=4)
    picture = nn(features[...], wp_ref[...])
    picture = (
        picture * lax.rsqrt(jnp.sum(picture * picture, axis=1, keepdims=True) + epsilon)
    ).astype(BF)
    picture_ref[...] = picture
    score = nt(embed_ref[...], picture) / heat_ref[0]
    match, valid = match_of(as_column(paired_ref), score.shape[1], images)
    score = jnp.where(valid, score, negative)
    score_ref[...] = score
    top = jnp.max(score, axis=1, keepdims=True)
    row = jnp.log(jnp.sum(jnp.exp(score - top), axis=1, keepdims=True)) + top
    row_ref[...] = row
    positive = jnp.sum(jnp.where(match, score, 0.0), axis=1, keepdims=True)
    hits = jnp.where(match, 1.0, 0.0)
    counts = jnp.sum(hits, axis=0, keepdims=True)
    inverse = 1.0 / jnp.sum(hits * counts, axis=1, keepdims=True)
    inverse_ref[...] = inverse
    total = jnp.sum(as_column(weight_ref) * (row - positive - positive * inverse))
    best = jnp.max(score, axis=0, keepdims=True)
    mass = jnp.sum(jnp.exp(score - best), axis=0, keepdims=True)
    mass = jnp.where(iota(mass.shape, 1) == images, total, mass)
    wide = best.shape[1] // 4
    rows = [v[:, i * wide : (i + 1) * wide] for v in (best, mass) for i in range(4)]
    stats_ref[...] = jnp.concatenate(rows, axis=0)


def contrast(images, parts, bits, heat, own, far, wp, embed, paired, weight):
    captions = embed.shape[0]
    columns = 2 * own.shape[0]
    return kernel_call(
        "contrast",
        functools.partial(contrast_kernel, images, parts, bits),
        [
            kept(columns, D),
            kept(captions, columns, dtype=F32),
            kept(captions, 1, dtype=F32),
            kept(captions, 1, dtype=F32),
            shape(8, columns // 4),
        ],
        (heat,),
        near(own, far, wp, embed, paired, weight),
        [((columns, D), BF)],
        cost(2 * columns * D * D),
        max(LIMIT, columns * 8192),
    )


def merged(refs):
    best = functools.reduce(jnp.maximum, [ref[:4] for ref in refs])
    mass = sum(ref[4:] * jnp.exp(ref[:4] - best) for ref in refs)
    return best, mass


def merge_kernel(*refs):
    *given, out_ref = refs
    best, mass = merged(given)
    out_ref[...] = jnp.concatenate([best, mass], axis=0)


def merge(stats):
    return kernel_call("merge", merge_kernel, [shape(*stats[0].shape)], (), stats)[0]


def quarters(rep, away, flip=0):
    core = rep & 1
    out = []
    for xrel in range(2):
        for yrel in range(2):
            block = jnp.bitwise_xor(rep, 2 * xrel + away)
            x_first = 1 - core if away == flip else core
            out.append((jnp.where(x_first == 1, 2 * xrel + yrel, 2 * yrel + xrel), block, yrel))
    return out


def head_back_kernel(
    images,
    count_stats,
    rounds,
    heat_ref,
    place_ref,
    score_ref,
    row_ref,
    inverse_ref,
    weight_ref,
    paired_ref,
    picture_ref,
    text_ref,
    scale_ref,
    wm_ref,
    wn_ref,
    slope_ref,
    second_t_ref,
    box_ref,
    *refs,
):
    first = 1 << rounds[0]
    pieces = refs[len(refs) - first :]
    stats = refs[:count_stats]
    (
        back_ref,
        away_ref,
        here_ref,
        pooled_ref,
        loss_ref,
        down_bias_ref,
        up_bias_ref,
    ) = refs[count_stats : len(refs) - first]
    rep = lax.axis_index("rep")
    heat = heat_ref[0]
    captions = place_ref.shape[0]
    line, column = token_limits(place_ref)
    count = jnp.sum(pool_mask(line, captions), axis=1, keepdims=True)
    owner = spread_mask(column, captions).astype(BF)
    owner = jnp.concatenate([owner, owner], axis=1)

    score = score_ref[...]
    match, valid = match_of(as_column(paired_ref), score.shape[1], images)
    best, mass = merged(stats)
    column_log = jnp.log(mass) + best
    column_log = jnp.concatenate([column_log[i : i + 1] for i in range(4)], axis=1)
    loss_ref[...] = mass[:1, images : images + 1] + jnp.sum(
        jnp.where(valid, column_log, 0.0), axis=1, keepdims=True
    )
    weight = as_column(weight_ref)
    graded = (
        weight * jnp.exp(score - row_ref[...])
        + jnp.exp(score - column_log)
        - jnp.where(match, weight * (1.0 + inverse_ref[...]), 0.0)
    )
    graded = jnp.where(valid, graded / heat, 0.0).astype(BF)
    embed_back = nn(graded, picture_ref[...])
    text = text_ref[...]
    factor = scale_ref[...]
    text_dot = jnp.sum(text * embed_back, axis=1, keepdims=True)
    text_back = (factor * embed_back - text * (factor * factor * factor) * text_dot).astype(BF)
    blocks, _, wide = box_ref.shape
    masks = gather_masks(rounds, blocks)
    for c, piece_ref in enumerate(pieces):
        for i in range(blocks // first):
            block = jnp.bitwise_xor(lax.axis_index("dp"), masks[i * first + c])
            piece_ref[:, i * wide : (i + 1) * wide] = box_ref[block]
        piece_ref[:, (blocks // first) * wide :] = text_back
    pooled_back = nt(text_back, wm_ref[...])
    pooled_ref[...] = pooled_back
    branch = (pooled_back / count).astype(BF)
    down_bias_ref[...] = jnp.sum(branch.astype(F32) * count, axis=0, keepdims=True)
    ones = jnp.ones((SLOT, back_ref.shape[0]), BF)
    step = 512

    def widen(i, carry):
        at = pl.multiple_of(i * step, 128)
        part = nn(owner, two(nt(branch, wn_ref[pl.ds(at, step), :])))
        part = (part * slope_ref[:, pl.ds(at, step)].astype(F32)).astype(BF)
        back_ref[:, pl.ds(at, step)] = part
        up_bias_ref[:, pl.ds(at, step)] = nn(ones, part)[:1]
        return carry

    lax.fori_loop(0, FF // step, widen, 0, unroll=3)
    half = second_t_ref.shape[0] // 2
    wide = FF // 4
    for turn, target in enumerate((away_ref, here_ref)):
        for place, block, yrel in quarters(rep, 1 - turn):
            part = nn(
                second_t_ref[yrel * half : (yrel + 1) * half],
                back_ref[:, pl.ds(pl.multiple_of(block * wide, 128), wide)],
            )
            for h in range(2):
                target[place, h] = part[:, h * (wide // 2) : (h + 1) * (wide // 2)].astype(BF)


def head_back(images, rounds, heat, place, stats, score, row, inverse, weight, paired, picture, text,
              factor, wm, wn, slope, second_t, box):
    captions = text.shape[0]
    tokens = slope.shape[0]
    piece = (4, 2, D // 2, FF // 8)
    return kernel_call(
        "head_back",
        functools.partial(head_back_kernel, images, len(stats), rounds),
        [
            kept(tokens, FF),
            kept(*piece),
            kept(*piece),
            kept(captions, D, dtype=F32),
            shape(1, 1),
            shape(1, D),
            shape(1, FF),
        ]
        + [shape(captions, (box.shape[0] >> rounds[0]) * box.shape[2] + D, dtype=BF)] * (1 << rounds[0]),
        (heat,),
        (
            *near(place, score, row, inverse, weight, paired),
            *near(picture, text, factor, wm, wn, slope, second_t, box),
            *stats,
        ),
        (),
        cost(2 * tokens * D * FF),
    )


def middle_back_kernel(
    place_ref,
    gain_ref,
    pooled_ref,
    back_ref,
    wu_ref,
    unit_ref,
    inverse_ref,
    wo_ref,
    total_ref,
    attended_ref,
    context_back_ref,
    gain_back_ref,
    shift_back_ref,
    bias_ref,
):
    captions = place_ref.shape[0]
    line, column = token_limits(place_ref)
    count = jnp.sum(pool_mask(line, captions), axis=1, keepdims=True)
    owner = spread_mask(column, captions).astype(BF)
    owner = jnp.concatenate([owner, owner], axis=1)
    second_back = nt(back_ref[...], wu_ref[...])
    part, gain_back_ref[...], shift_back_ref[...] = norm_back(
        unit_ref[...], inverse_ref[...], as_row(gain_ref), second_back
    )
    total = nn(owner, two(pooled_ref[...] / count)) + part
    total_ref[...] = total
    attended = total.astype(BF)
    attended_ref[...] = attended
    bias_ref[...] = nn(jnp.ones((SLOT, attended.shape[0]), BF), attended)[:1]
    context_back_ref[...] = nt(attended, wo_ref[...]).astype(BF)


def middle_back(place, gain, pooled, back, wu, unit, inverse, wo):
    tokens = back.shape[0]
    return kernel_call(
        "middle_back",
        middle_back_kernel,
        [
            kept(tokens, D, dtype=F32),
            kept(tokens, D),
            kept(tokens, D),
            shape(1, D),
            shape(1, D),
            shape(1, D),
        ],
        (),
        near(place, gain, pooled, back, wu, unit, inverse, wo),
        (),
        cost(2 * tokens * D * (FF + D)),
    )


def attention_back_kernel(project_ref, att_ref, context_back_ref, back_ref, bias_ref):
    masks = head_masks()
    picks = caption_masks()
    lows = [pick.astype(F32).astype(BF) for pick in picks]
    low_scale = jnp.asarray(scale, BF)
    first = iota((GROUP, 2 * HEAD), 1) < HEAD
    tokens = project_ref.shape[0]

    def attend(h, carry):
        at = pl.multiple_of(h * 2 * HEAD, 128)
        at_k = pl.multiple_of(D + at, 128)
        at_v = pl.multiple_of(2 * D + at, 128)
        for g in range(tokens // GROUP):
            span = slice(g * GROUP, (g + 1) * GROUP)
            query = project_ref[span, pl.ds(at, 128)]
            keys = both_heads(project_ref[span, pl.ds(at_k, 128)], masks)
            values = both_heads(project_ref[span, pl.ds(at_v, 128)], masks)
            upper = context_back_ref[span, pl.ds(at, 128)]
            full = nt(values, upper)
            weights, grads = [], []
            for e in range(2):
                weight = att_ref[2 * h + e, :, span]
                part = compact(full[e * GROUP : (e + 1) * GROUP], picks)
                grad = weight * (part - jnp.sum(weight * part, axis=0, keepdims=True))
                weights.append(expand(weight.astype(BF), lows))
                grads.append(expand(grad.astype(BF) * low_scale, lows))
            weights = jnp.concatenate(weights, axis=0)
            grads = jnp.concatenate(grads, axis=0)
            back_ref[span, pl.ds(at, 128)] = tn(grads, keys).astype(BF)
            wide = nn(grads, query)
            back_ref[span, pl.ds(at_k, 128)] = jnp.where(first, wide[:GROUP], wide[GROUP:]).astype(
                BF
            )
            wide = nn(weights, upper)
            back_ref[span, pl.ds(at_v, 128)] = jnp.where(first, wide[:GROUP], wide[GROUP:]).astype(
                BF
            )
        return carry

    lax.fori_loop(0, PAIRS, attend, 0, unroll=3)
    ones = jnp.ones((SLOT, tokens), BF)
    for i in range(3):
        lanes = slice(i * D, (i + 1) * D)
        bias_ref[:, lanes] = nn(ones, back_ref[:, lanes])[:1]


def attention_back(project, att, context_back):
    tokens = project.shape[0]
    return kernel_call(
        "attention_back",
        attention_back_kernel,
        [kept(tokens, 3 * D), shape(1, 3 * D)],
        (),
        near(project, att, context_back),
        (),
        cost(3 * tokens * D * D),
    )


def left_columns_kernel(back_ref, normed_t_ref, away_ref, here_ref, chosen):
    rep = lax.axis_index("rep")
    joint = 3 * D // 4
    some = chosen.shape[2]
    for r in range(4):

        @pl.when(rep == r)
        def _():
            for i, k in enumerate((1, 3, 0, 2)):
                b = r ^ k
                chosen[i] = back_ref[:, b * joint : b * joint + some]

    half = D // 2
    for turn, target in enumerate((away_ref, here_ref)):
        for i, (place, _, yrel) in enumerate(quarters(rep, 1 - turn, 1)):
            lines = slice(yrel * half, (yrel + 1) * half)
            target[place] = nn(normed_t_ref[lines], chosen[2 * turn + i // 2]).astype(BF)


def right_columns_kernel(
    back_ref, attended_ref, normed_t_ref, context_t_ref, away_ref, here_ref, chosen
):
    rep = lax.axis_index("rep")
    joint = 3 * D // 4
    out = D // 4
    some = chosen.shape[2] - out
    for r in range(4):

        @pl.when(rep == r)
        def _():
            for i, k in enumerate((1, 3, 0, 2)):
                b = r ^ k
                chosen[i, :, :some] = back_ref[:, (b + 1) * joint - some : (b + 1) * joint]
                chosen[i, :, some:] = attended_ref[:, b * out : (b + 1) * out]

    half = D // 2
    for turn, target in enumerate((away_ref, here_ref)):
        for i, (place, _, yrel) in enumerate(quarters(rep, 1 - turn)):
            block = 2 * turn + i // 2
            lines = slice(yrel * half, (yrel + 1) * half)
            target[place, :, :some] = nn(normed_t_ref[lines], chosen[block, :, :some]).astype(BF)
            target[place, :, some:] = nn(context_t_ref[lines], chosen[block, :, some:]).astype(BF)


def columns_gradient(name, body, operands):
    tokens = operands[0].shape[0]
    piece = (4, D // 2, D // 2)
    return kernel_call(
        name,
        body,
        [kept(*piece), kept(*piece)],
        (),
        near(*operands),
        [((4, tokens, D // 2), BF)],
        cost(tokens * D * FF),
    )


def token_back_kernel(
    gain_ref,
    unit_ref,
    inverse_ref,
    middle_ref,
    back_ref,
    wj_ref,
    joint_ref,
    out_ref,
    gain2_ref,
    shift2_ref,
    wide_ref,
    narrow_ref,
    token_ref,
    sums_ref,
):
    part, gain1, shift1 = norm_back(
        unit_ref[...], inverse_ref[...], as_row(gain_ref), nt(back_ref[...], wj_ref[...])
    )
    token_ref[...] = middle_ref[...] + part
    line = 0
    rest = (joint_ref, out_ref, gain2_ref, shift2_ref, wide_ref, narrow_ref)
    for value in [gain1, shift1] + [ref[...] for ref in rest]:
        for i in range(value.shape[1] // 128):
            sums_ref[line : line + 1] = value[:, i * 128 : (i + 1) * 128]
            line += 1
    sums_ref[line:] = jnp.zeros((sums_ref.shape[0] - line, 128), F32)


def token_back(gain, unit, inverse, middle, back, wj, sums):
    return kernel_call(
        "token_back",
        token_back_kernel,
        [shape(unit.shape[0], D), shape(ALL_LINES, 128)],
        (),
        (gain, *near(unit, inverse, middle, back, wj), *sums),
        (),
        cost(6 * unit.shape[0] * D * D),
    )


def low_rank_kernel(
    hidden, own_ref, near_ref, wm_ref, down_ref, head_ref, other_ref, box, back
):
    rows = own_ref.shape[0]
    box[:rows] = own_ref[...]
    box[rows:] = near_ref[...]
    part = down_ref.shape[0]
    start = box.shape[1] - D
    rep = lax.axis_index("rep")
    for r in range(D // part):

        @pl.when(rep == r)
        def _():
            for i, b in enumerate((r, r ^ 2)):
                back[i] = box[:, start + b * part : start + (b + 1) * part]

    wide = head_ref.shape[1]
    for i in range(2):
        block = jnp.bitwise_xor(rep, 2 * i)
        here = wm_ref[pl.ds(pl.multiple_of(block * part, SLOT), part), :]
        pooled = nt(box[:, start:], here).astype(BF)
        down = tn(pooled, box[:, :hidden])
        head = tn(back[i], box[:, hidden : hidden + wide])
        if i == 0:
            down_ref[...] = down
            head_ref[...] = head
        else:
            other_ref[:, :hidden] = down.astype(BF)
            other_ref[:, hidden:] = head.astype(BF)


def low_rank(blocks, parts, own, far, wm):
    rows = 2 * own.shape[0]
    hidden, wide, part = FF // blocks, D // blocks, D // parts
    return kernel_call(
        "low_rank",
        functools.partial(low_rank_kernel, hidden),
        [shape(part, hidden), shape(part, wide), shape(part, hidden + wide, dtype=BF)],
        (),
        near(own, far, wm),
        [((rows, own.shape[1]), BF), ((2, rows, part), BF)],
        cost(2 * rows * D * D),
    )


def finish_kernel(groups, *refs):
    up, first, second, lines = (
        [refs[sum(groups[:i]) + n] for n in range(groups[i])] for i in range(4)
    )
    loss_ref, down_ref, head_ref, other_ref = refs[sum(groups) : sum(groups) + 4]
    (
        joint_ref,
        out_ref,
        up_block_ref,
        down_block_ref,
        head_block_ref,
        loss_out_ref,
        *vector_refs,
    ) = refs[sum(groups) + 4 :]

    def total(terms):
        return sum(ref[...].astype(F32) for ref in terms)

    up_sum = total(up)
    for h in range(2):
        lanes = slice(h * up_sum.shape[2], (h + 1) * up_sum.shape[2])
        up_block_ref[:, lanes] = up_sum[h]
    one, two_ = total(first), total(second)
    some = one.shape[1]
    rest = joint_ref.shape[1] - some
    joint_ref[:, :some] = one
    joint_ref[:, some:] = two_[:, :rest]
    out_ref[...] = two_[:, rest:]
    hidden = down_ref.shape[1]
    down_block_ref[...] = down_ref[...] + other_ref[:, :hidden].astype(F32)
    head_block_ref[...] = (head_ref[...] + other_ref[:, hidden:].astype(F32)).T
    loss_out_ref[...] = loss_ref[...].reshape(1)
    vectors = total(lines)
    starts = (GAIN1, SHIFT1, JOINT, OUT, GAIN2, SHIFT2, WIDE, NARROW)
    for start, ref in zip(starts, vector_refs):
        for i in range(ref.shape[0] // 128):
            line = start // 128 + i
            if start == JOINT and i >= D // 128:
                line += D // 128
            ref[pl.ds(i * 128, 128)] = vectors[line]


def finish(up, first, second, vectors, loss, low, joint):
    rows = up[0].shape[1]
    sizes = (D, D, 2 * D, D, D, D, FF, D)
    return kernel_call(
        "finish",
        functools.partial(finish_kernel, [len(v) for v in (up, first, second, vectors)]),
        [
            shape(rows, joint),
            shape(rows, D - joint),
            shape(rows, D),
            shape(*low[0].shape),
            shape(*low[1].shape[::-1]),
            shape(1),
        ]
        + [shape(n) for n in sizes],
        (),
        (*up, *first, *second, *vectors, loss, *low),
    )


def both_pairs(partner):
    dp, rep = lax.axis_size("dp"), lax.axis_size("rep")
    pairs = []
    for i in range(dp):
        for j in range(rep):
            a, b = partner(i, j)
            pairs.append((i * rep + j, a * rep + b))
    return pairs


def exchange(value, partner):
    return lax.ppermute(value, ("dp", "rep"), both_pairs(partner))


def first_turn(i, j):
    return (i, j ^ 2) if j & 1 == 0 else (i ^ 1, j)


def second_turn(i, j):
    return (i ^ 1, j) if j & 1 == 0 else (i, j ^ 2)


def added(a, b):
    return (a.astype(F32) + b.astype(F32)).astype(BF)


def halved(here, got):
    half = here.shape[0] // 2
    return added(here[:half], got[:half]), added(here[half:], got[half:])


def parted(here, got, count):
    rows = here.shape[-2] // count
    parts = [slice(i * rows, (i + 1) * rows) for i in range(count)]
    return [added(here[..., p, :], got[..., p, :]) for p in parts]


def core_turn(i, j):
    return i, j ^ 1


def across(i, j):
    return i, j ^ 2


def group_round(keep, got, group):
    masks = group_masks(group)
    bits = len(group)
    parts = parted(keep, got, len(masks))
    place = [sum(((c >> n) & 1) << (bits - 1 - n) for n in range(bits)) for c in range(len(masks))]
    return [parts[0]] + [
        exchange(parts[place[c]], lambda i, j: (i ^ masks[c][0], j)) for c in range(1, len(masks))
    ]


def row_rounds(keep, got, groups):
    terms = [keep, got]
    for group in groups:
        if len(terms) > 2:
            terms = [terms[0], sum(v.astype(F32) for v in terms[1:])]
        terms = group_round(*terms, group)
    return terms


order = lax.optimization_barrier


def dp_groups():
    bits = [("dp", b) for b in range(1, lax.axis_size("dp").bit_length() - 1)]
    return [bits[i : i + 2] for i in range(0, len(bits), 2)] + [[("dp", 0)]]


def all_groups():
    bits = [("rep", b) for b in range(1, lax.axis_size("rep").bit_length() - 1)]
    groups = dp_groups()
    return groups[:-1] + [groups[-1] + bits, [("rep", 0)]]


def group_masks(group):
    out = [(0, 0)]
    for axis, bit in group:
        out += [(a | 1 << bit, b) if axis == "dp" else (a, b | 1 << bit) for a, b in out]
    return out


def gather_masks(rounds, blocks):
    bits = [0] + list(range(blocks.bit_length() - 2, 0, -1))
    masks, used = [0], 0
    for count in rounds:
        for bit in bits[used : used + count]:
            masks = masks + [m | 1 << bit for m in masks]
        used += count
    return masks


def split_round(value, wide, group):
    blocks = (value.shape[1] - D) // wide
    turns = group_masks(group)
    text = value[:, blocks * wide :]
    pieces = []
    for c, (a, b) in enumerate(turns):
        chosen = [value[:, i * wide : (i + 1) * wide] for i in range(c, blocks, len(turns))]
        piece = jnp.concatenate(chosen + [text], axis=1)
        pieces.append(piece if c == 0 else exchange(piece, lambda i, j: (i ^ a, j ^ b)))
    return pieces


def round_of(value, group):
    return [value] + [
        exchange(value, lambda i, j: (i ^ a, j ^ b)) for a, b in group_masks(group)[1:]
    ]


def relative_rows(value, blocks):
    rows = value.shape[0] // blocks
    if rows % SLOT == 0:
        return value
    bits = blocks.bit_length() - 1
    place = jnp.arange(blocks, dtype=jnp.int32)
    source = jnp.zeros_like(place)
    for bit in range(bits):
        source = source + ((place >> (bits - 1 - bit)) & 1) * (1 << bit)
    source = source ^ lax.axis_index("dp")
    return value.reshape(blocks, rows, -1)[source].reshape(value.shape)


def local(
    incoming_activations,
    caption_final_place,
    paired_picture,
    caption_weight,
    locked_picture_features,
    softmax_heat,
    premix_scaling_factor,
    premix_shift_term,
    stacked_mixing_matrix,
    asking_reading_offsets,
    mixing_result_matrix,
    mixing_result_offset,
    premlp_scaling_factor,
    premlp_shift_term,
    widening_matrix,
    widening_offset,
    narrowing_matrix,
    narrowing_offset,
    caption_mapping_matrix,
    picture_mapping_matrix,
):
    both = ("dp", "rep")
    devices = lax.axis_size(both)
    blocks = lax.axis_size("dp")
    parts = lax.axis_size("rep")
    captions = caption_final_place.shape[0]
    images = locked_picture_features.shape[0]
    groups = all_groups()
    pieces = round_of(jnp.pad(locked_picture_features, ((0, SLOT - images), (0, 0))), groups[0])
    project, normed, unit1, inverse1, place, out, x, wo = project_tokens(
        incoming_activations,
        premix_scaling_factor,
        premix_shift_term,
        asking_reading_offsets,
        stacked_mixing_matrix,
        (
            caption_final_place,
            mixing_result_offset,
            incoming_activations,
            mixing_result_matrix,
        ),
    )
    project, pieces = order((project, pieces))
    for group in groups[1:-1]:
        pieces = round_of(jnp.concatenate(pieces), group)
    att, context, middle, gain2, shift2, wide, narrow, wu, wn, wm = attend_tokens(
        place,
        out,
        x,
        project,
        wo,
        (
            premlp_scaling_factor,
            premlp_shift_term,
            widening_offset,
            narrowing_offset,
            widening_matrix,
            narrowing_matrix,
            caption_mapping_matrix,
        ),
    )
    middle, pieces = order((middle, pieces))
    own, far = round_of(jnp.concatenate(pieces), groups[-1])
    second, unit2, inverse2, upper, box, text, factor, embed, wp, paired, weight = widen_tokens(
        blocks,
        place,
        gain2,
        shift2,
        wide,
        narrow,
        middle,
        wu,
        wn,
        wm,
        (picture_mapping_matrix, paired_picture, caption_weight),
    )
    embed, far = order((embed, far))
    picture, score, row, inverse, stats = contrast(
        images,
        parts,
        sum(groups, []),
        softmax_heat,
        own,
        far,
        wp,
        embed,
        paired,
        weight,
    )
    groups = dp_groups()
    high = [[bit] for group in groups[:-1] for bit in group]
    factor_groups = groups[-1:] + high[::-1]
    stats = round_of(stats, [("rep", 0)])
    normed_t, context_t, second_t = (
        relative_rows(v, blocks) for v in turn_tokens(blocks, normed, context, second)
    )
    stats = round_of(merge(stats), [("rep", 1)] + groups[-1])
    slope = slope_tokens(upper)
    stats, slope = order((stats, slope))
    for group in groups[:-1]:
        stats = round_of(merge(stats), group)
    back, away, here, pooled_back, loss, down_bias, up_bias, *pieces = head_back(
        images,
        [len(group) for group in factor_groups],
        softmax_heat,
        place,
        stats,
        score,
        row,
        inverse,
        weight,
        paired,
        picture,
        text,
        factor,
        wm,
        wn,
        slope,
        second_t,
        box,
    )
    loss = loss / (captions * devices)
    got = exchange(away, core_turn)
    pieces = pieces[:1] + [
        exchange(piece, lambda i, j: (i ^ a, j ^ b))
        for piece, (a, b) in zip(pieces[1:], group_masks(factor_groups[0])[1:])
    ]
    total, attended, context_back, gain2, shift2, out_bias = middle_back(
        place,
        gain2,
        pooled_back,
        back,
        wu,
        unit2,
        inverse2,
        wo,
    )
    context_back, got, pieces = order((context_back, got, pieces))
    up, send = halved(here, got)
    got_up = exchange(send, first_turn)
    pieces = split_round(jnp.concatenate(pieces), box.shape[2], factor_groups[1])
    project_back, joint_bias = attention_back(project, att, context_back)
    project_back, pieces = order((project_back, pieces))
    for group in factor_groups[2:]:
        pieces = split_round(jnp.concatenate(pieces), box.shape[2], group)
    away, here = columns_gradient("left_columns", left_columns_kernel, (project_back, normed_t))
    got = exchange(away, core_turn)
    project_back, away = order((project_back, away))
    away, here2 = columns_gradient(
        "right_columns", right_columns_kernel, (project_back, attended, normed_t, context_t)
    )
    project_back, away, got, got_up = order((project_back, away, got, got_up))
    up, up_send = halved(up, got_up)
    first, send = halved(here, got)
    got = exchange(jnp.concatenate([up_send[0], send]), second_turn)
    got2 = exchange(away, core_turn)
    joint = 3 * D // parts
    token, sums = token_back(
        premix_scaling_factor,
        unit1,
        inverse1,
        total,
        project_back,
        stacked_mixing_matrix,
        (joint_bias, out_bias, gain2, shift2, up_bias, down_bias),
    )
    sums, got2, pieces = order((sums, got2, pieces))
    factors = jnp.concatenate(pieces)
    far = exchange(factors, core_turn)
    lines = round_of(sums, [("rep", 0)])
    lines = round_of(sum(lines), [("rep", 1)])
    second, send2 = halved(here2, got2)
    got, send2, lines, far = order((got, send2, lines, far))
    up, got_up = group_round(up[0], got[:2], high[0])
    first, send = halved(first, got[2:])
    got2 = exchange(jnp.concatenate([send2, send]), first_turn)
    lines = round_of(sum(lines), groups[-1])
    *low, other = low_rank(blocks, parts, factors, far, wm)
    got_up, lines, other = order((got_up, lines, other))
    lines = round_of(sum(lines), high[0])
    got2, lines, other = order((got2, lines, other))
    second, send = halved(second, got2[:2])
    second, first, got = second[0], first[0], got2[2]
    got2 = exchange(send[0], second_turn)
    first, got = group_round(first, got, high[0])
    for group in high[1:]:
        lines = round_of(sum(lines), group)
    for group in high[1:]:
        up, got_up = group_round(up, got_up, group)
    other = exchange(other, across)
    got, got2, lines = order((got, got2, lines))
    for group in high:
        second, got2 = group_round(second, got2, group)
    got, second = order((got, second))
    for group in high[1:]:
        first, got = group_round(first, got, group)
    first, second, up, vectors = [first, got], [second, got2], [up, got_up], lines
    joint_block, out_block, up_block, down_block, head_block, loss, *grads = finish(
        up, first, second, vectors, loss, (*low, other), joint
    )
    return (
        loss,
        token,
        grads[0],
        grads[1],
        joint_block,
        grads[2],
        out_block,
        grads[3],
        grads[4],
        grads[5],
        up_block,
        grads[6],
        down_block.T,
        grads[7],
        head_block,
    )


def solution(mesh):
    spread = P(("dp", "rep"), None)
    line = P(("dp", "rep"))
    block = P("dp", "rep")
    in_specs = (spread, line, line, line, spread) + (P(),) * 15
    out_specs = (
        P(),
        spread,
        P(),
        P(),
        block,
        P(),
        block,
        P(),
        P(),
        P(),
        block,
        P(),
        block,
        P(),
        block,
    )
    return jax.shard_map(local, mesh=mesh, in_specs=in_specs, out_specs=out_specs, check_vma=False)
```
